32 devices in a mesh: dp: 4 (over z), fsdp: 8 (over y, x, core).
Axes of the slice: x: 2, y: 2, z: 4, core: 2. Of those that a mesh axis runs over, the one named last changes fastest.
Arguments:
- tokens: bfloat16 [65536, 256], P(('dp', 'fsdp')), may hold values from -6 to 6
- cotangent: bfloat16 [65536, 256], P(('dp', 'fsdp')), may hold values from -6 to 6
- segment_ids: int32 [64, 1024], P(('dp', 'fsdp')), may hold values from 0 to 3, never falling along the last dimension, each value on 1 to 512 neighbouring positions
- attn_weight: float32 [256, 1024], P('dp', 'fsdp'), may hold values from -1 to 1, as said below
- ffn_in: float32 [256, 2048], P('dp', 'fsdp'), may hold values from -0.375 to 0.375
- ffn_out: float32 [256, 2048], P('dp', 'fsdp'), may hold values from -0.1875 to 0.1875
- vectors: float32 [16, 256], P('dp', 'fsdp'), may hold values from -1.6 to 1.6, as said below
- attn_rows: float32 [256], P('dp'), may hold values from 3120 to 13107
- attn_cols: float32 [1024], P('fsdp'), may hold values from 3120 to 13107
- in_rows: float32 [256], P('dp'), may hold values from 492 to 1985
- in_cols: float32 [2048], P('fsdp'), may hold values from 492 to 1985
- out_rows: float32 [256], P('dp'), may hold values from 4369 to 17476
- out_cols: float32 [2048], P('fsdp'), may hold values from 4369 to 17476
- vector_moment: float32 [16, 256], P('dp', 'fsdp'), may hold values from 13107 to 52428
Outputs:
- block_out: float32 [65536, 256], P(('dp', 'fsdp'))
- input_grad: float32 [65536, 256], P(('dp', 'fsdp'))
- attn_grad: float32 [256, 1024], P('dp', 'fsdp')
- ffn_in_grad: float32 [256, 2048], P('dp', 'fsdp')
- ffn_out_grad: float32 [256, 2048], P('dp', 'fsdp')
- vector_grad: float32 [16, 256], P('dp', 'fsdp')
- attn_rows_new: float32 [256], P('dp')
- attn_cols_new: float32 [1024], P('fsdp')
- in_rows_new: float32 [256], P('dp')
- in_cols_new: float32 [2048], P('fsdp')
- out_rows_new: float32 [256], P('dp')
- out_cols_new: float32 [2048], P('fsdp')
- vector_moment_new: float32 [16, 256], P('dp', 'fsdp')
- attn_new: float32 [256, 1024], P('dp', 'fsdp')
- ffn_in_new: float32 [256, 2048], P('dp', 'fsdp')
- ffn_out_new: float32 [256, 2048], P('dp', 'fsdp')
- vectors_new: float32 [16, 256], P('dp', 'fsdp')
The draws below stay inside these ranges and needn't reach their ends.
Inputs may be any that keep to these rules, and one draw needn't show every extreme that they name: `segment_ids`: along each row the image numbers never fall; every image of a row holds 1 to 512 tokens, and one holds exactly 512. `attn_weight`: the first 768 columns lie within 4 / sqrt(256) of zero, the last 256 columns within 16 / sqrt(256). `vectors`: the two gain rows lie in 0.6 to 1.4; the other rows lie in -1.6 to 1.6.
All inputs are finite; a program needn't handle non-finite values.
Results may differ from the reference program's by a relative error of at most 0.02.
The reference program's roundings to bfloat16 on the way count: a program that leaves them out, or rounds other values in their place, can miss the bound.
Values may be sent and summed in bfloat16 or wider, within the bound.
No kernel may reach another device: no remote copies, remote signals or barrier semaphores. Data moves between devices by JAX's collectives and lax.ppermute only.
A program may use at most 192 MiB of HBM per device.

```python
import math
import jax
import jax.numpy as jnp
import numpy as np
from jax import lax

D = 256
FF = 2048
HEADS = 8
HEAD_DIM = 32
SEQ = 1024
IMAGES = 4
MOST = 512
WGRID = 32
STEP = 10
ROWS_DEV = 2
VEC = 16
ROWS = 64
TOKENS = 65536


def draw_attn_weight(key, part):
    key = jax.random.fold_in(key, 11)
    normal_draw = jnp.clip(jax.random.normal(key, (D, 4 * D), jnp.float32), -4.0, 4.0)
    column = jnp.arange(4 * D)
    factor = jnp.where(column >= 3 * D, 4.0, 1.0) / jnp.sqrt(jnp.float32(D))
    return normal_draw * factor[None, :]


def draw_vectors(key, part):
    key = jax.random.fold_in(key, 12)
    normal_draw = jax.random.normal(key, (VEC, D), jnp.float32)
    param_index = jnp.arange(VEC)[:, None] - (VEC - 8)
    is_gain = (param_index == 4) | (param_index == 6)
    gains = 1.0 + 0.4 * jnp.tanh(normal_draw)
    others = 0.4 * jnp.clip(normal_draw, -4.0, 4.0)
    return jnp.where(is_gain, gains, others)


def levels(stream_key, extent, pieces, smallest, high):
    level = 1.0
    for axis_at, parts in pieces:
        draws = jax.random.uniform(jax.random.fold_in(jax.random.fold_in(stream_key, 6), axis_at), (parts,), jnp.float32, smallest / len(pieces), high / len(pieces))
        level = level * jnp.repeat(jnp.exp(draws), extent[axis_at] // parts).reshape((-1,) + (1,) * (len(extent) - 1 - axis_at))
    return level


def profile(count, total, bound, slope):
    weights = [(1 << 20) // math.isqrt(grade ** slope) + 1 for grade in range(2, count + 1)]
    surplus, given = total - bound - (count - 1), [1] * (count - 1)
    while surplus > 0:
        movable = [i for i in range(count - 1) if given[i] < bound]
        pool, remaining = sum([weights[i] for i in movable]), surplus
        for i in movable:
            more = min(bound - given[i], max(1, remaining * weights[i] // pool), surplus)
            given[i] = given[i] + more
            surplus = surplus - more
    return np.array([bound] + given)


def uneven_parts(stream_key, number_of, total, most, lean):
    if number_of == 2:
        one = jax.random.randint(stream_key, (), max(1, total - most), min(most, total - 1) + 1)
        return jnp.stack([one, total - one])
    sizes = jnp.asarray(profile(number_of, total, most, lean), jnp.int32)
    pairs = (number_of - 1) // 2
    donor, receiver = sizes[1:1 + 2 * pairs:2], sizes[2:2 + 2 * pairs:2]
    room = jnp.minimum(donor - 1, most - receiver)
    moved = jax.random.randint(jax.random.fold_in(stream_key, 1), (pairs,), 0, 1 << 20) % (room + 1)
    sizes = sizes.at[1:1 + 2 * pairs:2].set(donor - moved).at[2:2 + 2 * pairs:2].set(receiver + moved)
    return sizes[jax.random.permutation(jax.random.fold_in(stream_key, 2), number_of)]


def gaussian(rng, shape, width, most, split=(), held_as=jnp.bfloat16):
    drawn = width * jax.random.normal(rng, shape, jnp.float32)
    if split:
        drawn = drawn * levels(rng, shape, split, -0.22, 0.18)
    return jnp.clip(drawn, -most, most).astype(held_as)


def setup_inputs(seed: int = 0) -> dict:
    splits = jax.random.split(jax.random.key(seed), 15)
    tokens = gaussian(splits[0], (TOKENS, D), 1.0, 6.0, ((0, 32),))
    cotangent = gaussian(splits[1], (TOKENS, D), 1.0, 6.0, ((0, 32),))
    segment_ids = jax.vmap(lambda own: jnp.searchsorted(jnp.cumsum(uneven_parts(own, IMAGES, SEQ, MOST, 2)), jnp.arange(SEQ), side="right"))(jax.random.split(splits[2], ROWS)).reshape((ROWS, SEQ)).astype(jnp.int32)
    attn_weight = draw_attn_weight(jax.random.fold_in(splits[14], 71), 0)
    ffn_in = gaussian(splits[4], (D, FF), D ** -0.5, 0.375, ((0, 4), (1, 8)), jnp.float32)
    ffn_out = gaussian(splits[5], (D, FF), (FF // 2) ** -0.5, 0.1875, ((0, 4), (1, 8)), jnp.float32)
    vectors = draw_vectors(jax.random.fold_in(splits[14], 71), 0)
    attn_rows = jnp.clip(jnp.exp(math.log(13107.0) - 1.43531344 * jax.random.uniform(splits[7], (D,), jnp.float32) ** levels(splits[7], (D,), ((0, 4),), -0.2, 0.2)), 3120.0, 13107.0)
    attn_cols = jnp.clip(jnp.exp(math.log(13107.0) - 1.43531344 * jax.random.uniform(splits[8], (4 * D,), jnp.float32) ** levels(splits[8], (4 * D,), ((0, 8),), -0.2, 0.2)), 3120.0, 13107.0)
    in_rows = jnp.clip(jnp.exp(math.log(1985.0) - 1.39489548 * jax.random.uniform(splits[9], (D,), jnp.float32) ** levels(splits[9], (D,), ((0, 4),), -0.2, 0.2)), 492.0, 1985.0)
    in_cols = jnp.clip(jnp.exp(math.log(1985.0) - 1.39489548 * jax.random.uniform(splits[10], (FF,), jnp.float32) ** levels(splits[10], (FF,), ((0, 8),), -0.2, 0.2)), 492.0, 1985.0)
    out_rows = jnp.clip(jnp.exp(math.log(17476.0) - 1.3862944 * jax.random.uniform(splits[11], (D,), jnp.float32) ** levels(splits[11], (D,), ((0, 4),), -0.2, 0.2)), 4369.0, 17476.0)
    out_cols = jnp.clip(jnp.exp(math.log(17476.0) - 1.3862944 * jax.random.uniform(splits[12], (FF,), jnp.float32) ** levels(splits[12], (FF,), ((0, 8),), -0.2, 0.2)), 4369.0, 17476.0)
    vector_moment = jnp.clip(jnp.exp(math.log(52428.0) - 1.3862944 * jax.random.uniform(splits[13], (VEC, D), jnp.float32) ** levels(splits[13], (VEC, D), ((0, 4), (1, 8)), -0.2, 0.2)), 13107.0, 52428.0)
    return dict(tokens=tokens, cotangent=cotangent, segment_ids=segment_ids, attn_weight=attn_weight, ffn_in=ffn_in, ffn_out=ffn_out, vectors=vectors, attn_rows=attn_rows, attn_cols=attn_cols, in_rows=in_rows, in_cols=in_cols, out_rows=out_rows, out_cols=out_cols, vector_moment=vector_moment)


@jax.custom_vjp
def low(v):
    return lax.optimization_barrier(v.astype(jnp.bfloat16)).astype(jnp.float32)

@jax.custom_vjp
def low_back(v):
    return v

def low_keep(v):
    return (low(v), None)

def low_pass(kept, grad):
    return (grad,)

def back_keep(v):
    return (v, None)

def back_low(kept, grad):
    return (low(grad),)
low.defvjp(low_keep, low_pass)
low_back.defvjp(back_keep, back_low)
EPS_NORM = 1e-05
EPS_ONE = 1e-30
EPS_TWO = 0.001
CLIP_LIMIT = 1.0
STEP_RATE = 0.3
MASKED_SCORE = -1e+30
highest = lax.Precision.HIGHEST

def matmul(left, right):
    return jnp.dot(left, right, preferred_element_type=jnp.float32, precision=highest)

def smooth(values):
    return jax.nn.gelu(values, approximate=True)

def sine_table(segments):
    length = segments.shape[-1]
    places = jnp.arange(length, dtype=jnp.int32)
    previous = jnp.concatenate([segments[..., :1] - 1, segments[..., :-1]], axis=-1)
    starts = lax.cummax(jnp.where(segments != previous, places, 0), axis=segments.ndim - 1)
    local_place = places - starts
    grid_rows = (local_place // WGRID + 1).astype(jnp.float32)
    grid_cols = (local_place % WGRID + 1).astype(jnp.float32)
    half_width = D // 2
    feature = jnp.arange(half_width, dtype=jnp.int32)
    inverse_freq = jnp.exp((2 * (feature // 2)).astype(jnp.float32) * (-math.log(10000.0) / half_width))
    is_even = feature % 2 == 0

    def encode(values):
        angles = values[..., None] * inverse_freq
        return jnp.where(is_even, jnp.sin(angles), jnp.cos(angles))
    return jnp.concatenate([encode(grid_rows), encode(grid_cols)], axis=-1)

def unpack(vectors):
    bias_rows = FF // D
    return (vectors[:bias_rows].reshape(FF), vectors[bias_rows:])

def layer_norm(rows, gain, shift):
    centered = rows - lax.optimization_barrier(jnp.mean(rows, axis=-1, keepdims=True))
    inverse = lax.rsqrt(lax.optimization_barrier(jnp.mean(centered * centered, axis=-1, keepdims=True)) + EPS_NORM)
    return centered * inverse * gain + shift

def layer_row(token_row, segment_row, attn_weight, ffn_in, ffn_out, vectors):
    w_attn = low(attn_weight)
    w_first = low(ffn_in)
    w_second = low(ffn_out)
    ffn_bias, params = unpack(low(vectors))
    score_scale = HEAD_DIM ** (-0.5)
    qk_input = low(token_row + sine_table(segment_row))
    v_input = low(token_row)
    queries = low(low_back((matmul(qk_input, w_attn[:, :D]) + params[0]) * score_scale))
    keys_all = low(low_back(matmul(qk_input, w_attn[:, D:2 * D])))
    values_all = low(low_back(matmul(v_input, w_attn[:, 2 * D:3 * D]) + params[1]))
    query_heads = queries.reshape(SEQ, HEADS, HEAD_DIM)
    key_heads = keys_all.reshape(SEQ, HEADS, HEAD_DIM)
    value_heads = values_all.reshape(SEQ, HEADS, HEAD_DIM)
    scores = low_back(jnp.einsum('qhd,khd->hqk', query_heads, key_heads, precision=highest))
    allowed = segment_row[:, None] == segment_row[None, :]
    masked = jnp.where(allowed[None], scores, MASKED_SCORE)
    largest = lax.optimization_barrier(jnp.max(masked, axis=-1, keepdims=True))
    exponent = jnp.exp(masked - largest)
    softmax_weights = exponent / lax.optimization_barrier(jnp.sum(exponent, axis=-1, keepdims=True))
    mixed = jnp.einsum('hqk,khd->qhd', low(softmax_weights), value_heads, precision=highest).reshape(SEQ, D)
    mixed = low(low_back(mixed))
    attended = low_back(matmul(mixed, w_attn[:, 3 * D:]) + params[2])
    first = layer_norm(token_row + attended, params[4], params[5])
    hidden_pre = low_back(matmul(low(first), w_first) + ffn_bias)
    hidden = low(smooth(hidden_pre))
    branch = low_back(matmul(hidden, w_second.T) + params[3])
    return layer_norm(first + branch, params[6], params[7])

def factored_update(gradient, weight, rows_old, cols_old, decay):
    squares = gradient * gradient + EPS_ONE
    rows_new = decay * rows_old + (1.0 - decay) * lax.optimization_barrier(jnp.mean(squares, axis=1))
    cols_new = decay * cols_old + (1.0 - decay) * lax.optimization_barrier(jnp.mean(squares, axis=0))
    second = rows_new[:, None] * cols_new[None, :] / jnp.mean(rows_new)
    update = gradient * lax.rsqrt(second)
    clip_factor = jnp.maximum(1.0, jnp.sqrt(jnp.mean(update * update)) / CLIP_LIMIT)
    step_size = STEP_RATE * jnp.maximum(EPS_TWO, jnp.sqrt(jnp.mean(weight * weight)))
    return (rows_new, cols_new, weight - step_size / clip_factor * update)

def reference(tokens, cotangent, segment_ids, attn_weight, ffn_in, ffn_out, vectors, attn_rows, attn_cols, in_rows, in_cols, out_rows, out_cols, vector_moment):
    token_groups = tokens.astype(jnp.float32).reshape(-1, ROWS_DEV, SEQ, D)
    back_groups = cotangent.astype(jnp.float32).reshape(-1, ROWS_DEV, SEQ, D)
    segment_groups = segment_ids.reshape(-1, ROWS_DEV, SEQ)
    params = (attn_weight, ffn_in, ffn_out, vectors)
    row_layer = jax.checkpoint(layer_row)

    def scan_step(running, group_item):
        token_group, segment_group, back_group = group_item

        def local_layer(token_values, attn_w, first_w, second_w, vector_w):

            def one_row(row_pair):
                return row_layer(row_pair[0], row_pair[1], attn_w, first_w, second_w, vector_w)
            return lax.map(one_row, (token_values, segment_group))
        outputs, pullback = jax.vjp(local_layer, token_group, *params)
        gradients = pullback(back_group)
        updated = tuple((total_one + grad_one for total_one, grad_one in zip(running, gradients[1:])))
        return (updated, (outputs, gradients[0]))
    initial = tuple((jnp.zeros_like(param) for param in params))
    summed, (block_groups, input_groups) = lax.scan(scan_step, initial, (token_groups, segment_groups, back_groups))
    block_out = block_groups.reshape(-1, D)
    input_grad = input_groups.reshape(-1, D)
    attn_grad, in_grad, out_grad, vector_grad = summed
    decay = 1.0 - STEP ** (-0.8)
    attn_rows_new, attn_cols_new, attn_new = factored_update(attn_grad, attn_weight, attn_rows, attn_cols, decay)
    in_rows_new, in_cols_new, ffn_in_new = factored_update(in_grad, ffn_in, in_rows, in_cols, decay)
    out_rows_new, out_cols_new, ffn_out_new = factored_update(out_grad, ffn_out, out_rows, out_cols, decay)
    moment_new = decay * vector_moment + (1.0 - decay) * (vector_grad * vector_grad + EPS_ONE)
    vector_step = vector_grad * lax.rsqrt(moment_new)
    bias_rows = FF // D
    row_places = jnp.arange(VEC)
    row_updates = lax.optimization_barrier(jnp.sum(vector_step * vector_step, axis=1))
    row_weights = lax.optimization_barrier(jnp.sum(vectors * vectors, axis=1))
    counts = jnp.where(row_places < bias_rows, float(FF), float(D))
    grouped_updates = jnp.where(row_places < bias_rows, jnp.sum(row_updates[:bias_rows]), row_updates)
    grouped_weights = jnp.where(row_places < bias_rows, jnp.sum(row_weights[:bias_rows]), row_weights)
    clip_rows = jnp.maximum(1.0, jnp.sqrt(grouped_updates / counts) / CLIP_LIMIT)
    step_rows = STEP_RATE * jnp.maximum(EPS_TWO, jnp.sqrt(grouped_weights / counts))
    vectors_new = vectors - (step_rows / clip_rows)[:, None] * vector_step
    return (block_out, input_grad, attn_grad, in_grad, out_grad, vector_grad, attn_rows_new, attn_cols_new, in_rows_new, in_cols_new, out_rows_new, out_cols_new, moment_new, attn_new, ffn_in_new, ffn_out_new, vectors_new)
```

```python
import functools
import math

import jax
import jax.numpy as jnp
import numpy as np
from jax import lax
from jax.experimental import pallas as pl
from jax.experimental.pallas import tpu as pltpu
from jax.sharding import PartitionSpec as P

D = 256
FF = 2048
HEADS = 8
HEAD_DIM = 32
SEQ = 1024
HALF = 512
GROUP = 4
LANES = 128
QBLOCK = 256
WGRID = 32
STEP = 10
VEC = 16
TILE = 512
CHUNK = 512

EPS_NORM = 1e-05
EPS_ONE = 1e-30
EPS_TWO = 0.001
CLIP_LIMIT = 1.0
STEP_RATE = 0.3
FAR = 1e30
SCALE = HEAD_DIM ** (-0.5)
GELU_A = math.sqrt(2.0 / math.pi)
GELU_B = 0.044715
F32 = jnp.float32
BF16 = jnp.bfloat16
VMEM_LIMIT = 56 * 1024 * 1024


def dot(left, right):
    return jnp.dot(left, right, preferred_element_type=F32)


def dot_nt(left, right):
    return lax.dot_general(left, right, (((1,), (1,)), ((), ())), preferred_element_type=F32)


def encode_table():
    half = D // 2
    feature = np.arange(half)
    freq = np.exp(
        (2 * (feature // 2)).astype(np.float32) * np.float32(-math.log(10000.0) / half)
    ).astype(np.float32)
    angles = np.arange(1, WGRID + 1, dtype=np.float32)[:, None] * freq[None, :]
    table = np.where(feature % 2 == 0, np.sin(angles), np.cos(angles)).astype(np.float32)
    low = jnp.bfloat16
    one = table.astype(low)
    rest = table - one.astype(np.float32)
    two = rest.astype(low)
    three = (rest - two.astype(np.float32)).astype(low)
    blank = np.zeros((LANES - 3 * WGRID, half), low)
    return np.concatenate([one, two, three, blank], axis=0)


def iota(shape, dim):
    return lax.broadcasted_iota(jnp.int32, shape, dim)


def norm_forward(rows):
    centered = rows - jnp.mean(rows, axis=-1, keepdims=True)
    inverse = lax.rsqrt(jnp.mean(centered * centered, axis=-1, keepdims=True) + EPS_NORM)
    return centered * inverse, inverse


def norm_backward(upstream, normed, inverse):
    return inverse * (
        upstream
        - jnp.mean(upstream, axis=-1, keepdims=True)
        - normed * jnp.mean(upstream * normed, axis=-1, keepdims=True)
    )


def attend_kernel(
    marks,
    tokens_ref,
    table_ref,
    weight_ref,
    vector_ref,
    qk_ref,
    x_ref,
    query_ref,
    value_ref,
    key_t_ref,
    out_t_ref,
    inverse_ref,
    mixed_ref,
    exps_ref,
    key_s,
    value_s,
    mark_k,
    mark_q,
):
    row = pl.program_id(0)
    group = pl.program_id(1)
    begin = marks[row, 3]

    @pl.when(group == 0)
    def _():
        x = pltpu.roll(tokens_ref[...].astype(F32), (SEQ - begin) & (SEQ - 1), 0)
        x_low = x.astype(BF16)
        x_ref[...] = x_low
        place = (iota((SEQ, LANES), 0) + begin) & (SEQ - 1)
        lane = iota((SEQ, LANES), 1)
        one, two, three = marks[row, 0], marks[row, 1], marks[row, 2]
        start = jnp.where(
            place >= three, three, jnp.where(place >= two, two, jnp.where(place >= one, one, 0))
        )
        local = place - start
        kept = lane < 3 * WGRID
        slot = lane & (WGRID - 1)
        hot_r = jnp.where(((local >> 5) == slot) & kept, 1.0, 0.0).astype(BF16)
        hot_c = jnp.where(((local & (WGRID - 1)) == slot) & kept, 1.0, 0.0).astype(BF16)
        places = jnp.concatenate([dot(hot_r, table_ref[...]), dot(hot_c, table_ref[...])], axis=1)
        qk = (x + places).astype(BF16)
        qk_ref[...] = qk
        bias_q = vector_ref[8:9, :].astype(F32)
        bias_v = vector_ref[9:10, :].astype(F32)
        query = (dot(qk, weight_ref[:, :D]) + bias_q) * SCALE
        query_ref[...] = query.astype(BF16)
        key = dot(qk, weight_ref[:, D : 2 * D])
        key_s[...] = key.astype(BF16)
        key_t_ref[...] = key.T.astype(BF16)
        value = dot(x_low, weight_ref[:, 2 * D : 3 * D]) + bias_v
        value_ref[...] = value.astype(BF16)
        value_t = value.T.astype(BF16)
        for head in range(HEADS):
            value_s[head, :HEAD_DIM, :] = value_t[head * HEAD_DIM : (head + 1) * HEAD_DIM, :]
            value_s[head, HEAD_DIM:, :] = jnp.ones((16, SEQ), BF16)
        here = place[HALF:, :]
        number = (
            jnp.where(here >= one, 1, 0)
            + jnp.where(here >= two, 1, 0)
            + jnp.where(here >= three, 1, 0)
        )
        lane = lane[HALF:, :]
        mark_q[...] = jnp.where(number == lane, 1.0, 0.0).astype(BF16)
        mark_k[...] = jnp.where((number != lane) & (lane < 4), -FAR, 0.0).astype(BF16)

    lanes = pl.ds(pl.multiple_of(group * LANES, LANES), LANES)
    head_of = iota((1, LANES), 1) // HEAD_DIM
    for half in range(2):
        rows = slice(half * HALF, (half + 1) * HALF)
        keys_here = key_s[rows, lanes]
        for place in range(GROUP):
            head = group * GROUP + place
            key_m = keys_here * jnp.where(head_of == place, 1.0, 0.0).astype(BF16)
            if half == 1:
                key_m = jnp.concatenate([key_m, mark_k[...]], axis=1)
            for block in range(HALF // QBLOCK):
                at = half * HALF + block * QBLOCK
                query = query_ref[at : at + QBLOCK, lanes]
                if half == 1:
                    query = jnp.concatenate(
                        [query, mark_q[block * QBLOCK : (block + 1) * QBLOCK, :]], axis=1
                    )
                scores = dot_nt(key_m, query)
                exps = jnp.exp(scores - jnp.max(scores, axis=0, keepdims=True)).astype(BF16)
                exps_ref[0, place, half, :, block * QBLOCK : (block + 1) * QBLOCK] = exps
                out = dot(value_s[head, :, rows], exps)
                inverse = 1.0 / out[HEAD_DIM : HEAD_DIM + 1, :]
                inverse_ref[pl.ds(head, 1), at : at + QBLOCK] = inverse
                out_t_ref[pl.ds(pl.multiple_of(head * HEAD_DIM, HEAD_DIM), HEAD_DIM), at : at + QBLOCK] = (
                    out[:HEAD_DIM, :] * inverse
                )

    @pl.when(group == 1)
    def _():
        mixed_ref[...] = pltpu.roll(out_t_ref[...].T, begin, 0).astype(BF16)


def attend_forward(marks, tokens, table, weight, vector):
    rows = tokens.shape[0] // SEQ
    total = rows * SEQ
    by_row = lambda r, g, m: (r, 0)
    by_col = lambda r, g, m: (0, r)
    whole = lambda r, g, m: (0, 0)
    return pl.pallas_call(
        attend_kernel,
        out_shape=(
            jax.ShapeDtypeStruct((total, D), BF16),
            jax.ShapeDtypeStruct((total, D), BF16),
            jax.ShapeDtypeStruct((total, D), BF16),
            jax.ShapeDtypeStruct((total, D), BF16),
            jax.ShapeDtypeStruct((D, total), BF16),
            jax.ShapeDtypeStruct((D, total), F32),
            jax.ShapeDtypeStruct((HEADS, total), F32),
            jax.ShapeDtypeStruct((total, D), BF16),
            jax.ShapeDtypeStruct((rows, HEADS, 2, HALF, HALF), BF16),
        ),
        grid_spec=pltpu.PrefetchScalarGridSpec(
            num_scalar_prefetch=1,
            grid=(rows, 2),
            in_specs=[
                pl.BlockSpec((SEQ, D), by_row),
                pl.BlockSpec((LANES, LANES), whole),
                pl.BlockSpec((D, 3 * D), whole),
                pl.BlockSpec((VEC, D), whole),
            ],
            out_specs=[
                pl.BlockSpec((SEQ, D), by_row),
                pl.BlockSpec((SEQ, D), by_row),
                pl.BlockSpec((SEQ, D), by_row),
                pl.BlockSpec((SEQ, D), by_row),
                pl.BlockSpec((D, SEQ), by_col),
                pl.BlockSpec((D, SEQ), by_col),
                pl.BlockSpec((HEADS, SEQ), by_col),
                pl.BlockSpec((SEQ, D), by_row),
                pl.BlockSpec((1, GROUP, 2, HALF, HALF), lambda r, g, m: (r, g, 0, 0, 0)),
            ],
            scratch_shapes=[
                pltpu.VMEM((SEQ, D), BF16),
                pltpu.VMEM((HEADS, HEAD_DIM + 16, SEQ), BF16),
                pltpu.VMEM((HALF, LANES), BF16),
                pltpu.VMEM((HALF, LANES), BF16),
            ],
        ),
        compiler_params=pltpu.CompilerParams(
            dimension_semantics=("arbitrary", "arbitrary"), vmem_limit_bytes=VMEM_LIMIT
        ),
        cost_estimate=pl.CostEstimate(
            flops=20_000_000_000, bytes_accessed=30_000_000, transcendentals=8_400_000
        ),
        name="attend_forward",
    )(marks, tokens, table, weight, vector)


def feed_kernel(
    tokens_ref,
    cotangent_ref,
    mixed_ref,
    proj_ref,
    first_w_ref,
    second_w_ref,
    vector_ref,
    block_ref,
    resid_ref,
    mixed_grad_ref,
    first_out,
    second_out,
    proj_out,
    vector_out,
    first_acc,
    second_acc,
    proj_acc,
    vector_acc,
    hidden_s,
    slope_s,
):
    step = pl.program_id(0)

    @pl.when(step == 0)
    def _():
        first_acc[...] = jnp.zeros_like(first_acc)
        second_acc[...] = jnp.zeros_like(second_acc)
        proj_acc[...] = jnp.zeros_like(proj_acc)
        vector_acc[...] = jnp.zeros_like(vector_acc)

    vector = vector_ref[...].astype(F32)
    bias_o, bias_2 = vector[10:11], vector[11:12]
    gain_1, shift_1, gain_2, shift_2 = vector[12:13], vector[13:14], vector[14:15], vector[15:16]
    mixed = mixed_ref[...]
    attended = dot(mixed, proj_ref[...]) + bias_o
    norm_1, inverse_1 = norm_forward(tokens_ref[...].astype(F32) + attended)
    first = norm_1 * gain_1 + shift_1
    first_low = first.astype(BF16)
    per = CHUNK // D
    branch = jnp.zeros((TILE, D), F32)
    for at in range(FF // CHUNK):
        cols = slice(at * CHUNK, (at + 1) * CHUNK)
        bias = jnp.concatenate([vector[at * per + i : at * per + i + 1] for i in range(per)], axis=1)
        pre = dot(first_low, first_w_ref[:, cols]) + bias
        square = pre * pre
        inner = pre * (GELU_A + (GELU_A * GELU_B) * square)
        gate = 0.5 + 0.5 * jnp.tanh(inner)
        hidden = (pre * gate).astype(BF16)
        hidden_s[:, cols] = hidden
        rise = (2.0 * GELU_A) + (6.0 * GELU_A * GELU_B) * square
        slope_s[:, cols] = gate + (gate - gate * gate) * (pre * rise)
        branch += dot_nt(hidden, second_w_ref[:, cols])
    norm_2, inverse_2 = norm_forward(first + (branch + bias_2))
    block_ref[...] = norm_2 * gain_2 + shift_2
    back = cotangent_ref[...].astype(F32)
    vector_acc[14:15, :] += jnp.sum(back * norm_2, axis=0, keepdims=True)
    vector_acc[15:16, :] += jnp.sum(back, axis=0, keepdims=True)
    resid_2 = norm_backward(back * gain_2, norm_2, inverse_2)
    branch_low = resid_2.astype(BF16)
    branch_f = branch_low.astype(F32)
    vector_acc[11:12, :] += jnp.sum(branch_f, axis=0, keepdims=True)
    branch_t = branch_f.T.astype(BF16)
    first_t = first_low.astype(F32).T.astype(BF16)
    first_back = resid_2
    for at in range(FF // CHUNK):
        cols = slice(at * CHUNK, (at + 1) * CHUNK)
        hidden_grad = dot(branch_low, second_w_ref[:, cols])
        pre_low = (hidden_grad * slope_s[:, cols]).astype(BF16)
        sums = jnp.sum(pre_low.astype(F32), axis=0, keepdims=True)
        for i in range(per):
            vector_acc[at * per + i : at * per + i + 1, :] += sums[:, i * D : (i + 1) * D]
        second_acc[:, cols] += dot(branch_t, hidden_s[:, cols])
        first_acc[:, cols] += dot(first_t, pre_low)
        first_back += dot_nt(pre_low, first_w_ref[:, cols])
    vector_acc[12:13, :] += jnp.sum(first_back * norm_1, axis=0, keepdims=True)
    vector_acc[13:14, :] += jnp.sum(first_back, axis=0, keepdims=True)
    resid_1 = norm_backward(first_back * gain_1, norm_1, inverse_1)
    resid_ref[...] = resid_1
    attended_low = resid_1.astype(BF16)
    vector_acc[10:11, :] += jnp.sum(attended_low.astype(F32), axis=0, keepdims=True)
    mixed_t = mixed.astype(F32).T.astype(BF16)
    proj_acc[...] += dot(mixed_t, attended_low)
    mixed_grad_ref[...] = dot_nt(attended_low, proj_ref[...]).astype(BF16)

    @pl.when(step == pl.num_programs(0) - 1)
    def _():
        first_out[...] = first_acc[...].astype(BF16)
        second_out[...] = second_acc[...].astype(BF16)
        proj_out[...] = proj_acc[...].astype(BF16)
        vector_out[...] = vector_acc[...]


def feed_forward(tokens, cotangent, mixed, proj, first_w, second_w, vector):
    total = tokens.shape[0]
    tile = lambda i: (i, 0)
    whole = lambda i: (0, 0)
    return pl.pallas_call(
        feed_kernel,
        out_shape=(
            jax.ShapeDtypeStruct((total, D), F32),
            jax.ShapeDtypeStruct((total, D), F32),
            jax.ShapeDtypeStruct((total, D), BF16),
            jax.ShapeDtypeStruct((D, FF), BF16),
            jax.ShapeDtypeStruct((D, FF), BF16),
            jax.ShapeDtypeStruct((D, D), BF16),
            jax.ShapeDtypeStruct((VEC, D), F32),
        ),
        grid=(total // TILE,),
        in_specs=[
            pl.BlockSpec((TILE, D), tile),
            pl.BlockSpec((TILE, D), tile),
            pl.BlockSpec((TILE, D), tile),
            pl.BlockSpec((D, D), whole),
            pl.BlockSpec((D, FF), whole),
            pl.BlockSpec((D, FF), whole),
            pl.BlockSpec((VEC, D), whole),
        ],
        out_specs=[
            pl.BlockSpec((TILE, D), tile),
            pl.BlockSpec((TILE, D), tile),
            pl.BlockSpec((TILE, D), tile),
            pl.BlockSpec((D, FF), whole),
            pl.BlockSpec((D, FF), whole),
            pl.BlockSpec((D, D), whole),
            pl.BlockSpec((VEC, D), whole),
        ],
        scratch_shapes=[
            pltpu.VMEM((D, FF), F32),
            pltpu.VMEM((D, FF), F32),
            pltpu.VMEM((D, D), F32),
            pltpu.VMEM((VEC, D), F32),
            pltpu.VMEM((TILE, FF), BF16),
            pltpu.VMEM((TILE, FF), F32),
        ],
        compiler_params=pltpu.CompilerParams(
            dimension_semantics=("arbitrary",), vmem_limit_bytes=VMEM_LIMIT
        ),
        cost_estimate=pl.CostEstimate(
            flops=14_000_000_000, bytes_accessed=15_000_000, transcendentals=4_200_000
        ),
        name="feed_forward",
    )(tokens, cotangent, mixed, proj, first_w, second_w, vector)


def pull_kernel(
    group,
    marks,
    mixed_grad_ref,
    query_ref,
    value_ref,
    key_t_ref,
    out_t_ref,
    inverse_ref,
    exps_ref,
    qk_ref,
    x_ref,
    *refs,
):
    last = group == 1
    if last:
        (resid_ref, weight_ref, other_ref, input_ref, grads_ref, sums_ref, dot_s, query_t_s, acc, sum_acc) = refs
    else:
        (low_ref, grads_ref, sums_ref, dot_s, query_t_s, acc, sum_acc) = refs
    row = pl.program_id(0)
    begin = marks[row, 3]

    @pl.when(row == 0)
    def _():
        acc[...] = jnp.zeros_like(acc)
        sum_acc[...] = jnp.zeros_like(sum_acc)

    grad = pltpu.roll(mixed_grad_ref[...].astype(F32), (SEQ - begin) & (SEQ - 1), 0)
    grad_t = grad.T
    inverse = inverse_ref[group * GROUP : (group + 1) * GROUP, :]
    scaled = []
    for place in range(GROUP):
        rows = slice(place * HEAD_DIM, (place + 1) * HEAD_DIM)
        part = grad_t[rows, :] * inverse[place : place + 1, :]
        scaled.append(part)
        dot_s[place : place + 1, :] = jnp.sum(part * out_t_ref[rows, :], axis=0, keepdims=True)
    scaled_t = jnp.concatenate(scaled, axis=0)
    scaled_low_t = scaled_t.astype(BF16)
    scaled_low = scaled_t.T.astype(BF16)
    head_of = iota((1, LANES), 1) // HEAD_DIM
    key_parts = []
    value_parts = []
    for half in range(2):
        rows = slice(half * HALF, (half + 1) * HALF)
        value_here = value_ref[rows, :]
        query_here = query_ref[rows, :]
        scaled_here = scaled_low[rows, :]
        scaled_t_here = scaled_low_t[:, rows]
        key_grad = jnp.zeros((HALF, LANES), F32)
        value_grad = jnp.zeros((HALF, LANES), F32)
        for place in range(GROUP):
            mask = jnp.where(head_of == place, 1.0, 0.0).astype(BF16)
            exps = exps_ref[0, place, half]
            weight_grad = dot(value_here * mask, scaled_t_here)
            score_grad = (
                exps.astype(F32) * (weight_grad - dot_s[place : place + 1, rows])
            ).astype(BF16)
            value_grad += dot(exps, scaled_here * mask)
            key_grad += dot(score_grad, query_here * mask)
            query_t_s[place * HEAD_DIM : (place + 1) * HEAD_DIM, rows] = dot(
                key_t_ref[place * HEAD_DIM : (place + 1) * HEAD_DIM, rows], score_grad
            )
        key_parts.append(key_grad)
        value_parts.append(value_grad)
    query_low = query_t_s[...].T.astype(BF16)
    key_low = jnp.concatenate(key_parts, axis=0).astype(BF16)
    value_low = jnp.concatenate(value_parts, axis=0).astype(BF16)
    sum_acc[0:1, :] += jnp.sum(query_low.astype(F32), axis=0, keepdims=True) * SCALE
    sum_acc[1:2, :] += jnp.sum(value_low.astype(F32), axis=0, keepdims=True)
    qk_t = qk_ref[...].astype(F32).T.astype(BF16)
    x_t = x_ref[...].astype(F32).T.astype(BF16)
    acc[:, :LANES] += dot(qk_t, query_low) * SCALE
    acc[:, LANES : 2 * LANES] += dot(qk_t, key_low)
    acc[:, 2 * LANES :] += dot(x_t, value_low)
    if last:
        other = other_ref[...]
        query_all = jnp.concatenate([other[:, :LANES], query_low], axis=1)
        key_all = jnp.concatenate([other[:, LANES : 2 * LANES], key_low], axis=1)
        value_all = jnp.concatenate([other[:, 2 * LANES :], value_low], axis=1)
        pulled = (
            dot_nt(query_all, weight_ref[:, :D]) * SCALE
            + dot_nt(key_all, weight_ref[:, D : 2 * D])
            + dot_nt(value_all, weight_ref[:, 2 * D : 3 * D])
        )
        input_ref[...] = resid_ref[...] + pltpu.roll(pulled, begin, 0)
    else:
        low_ref[:, :LANES] = query_low
        low_ref[:, LANES : 2 * LANES] = key_low
        low_ref[:, 2 * LANES :] = value_low

    @pl.when(row == pl.num_programs(0) - 1)
    def _():
        grads_ref[...] = acc[...].astype(BF16)
        sums_ref[...] = sum_acc[...]


def attend_back(group, marks, mixed_grad, query, value, key_t, out_t, inverse, exps, qk, x, *more):
    total = query.shape[0]
    rows = total // SEQ
    last = group == 1
    by_group = lambda r, m: (r, group)
    by_row = lambda r, m: (r, 0)
    whole = lambda r, m: (0, 0)
    in_specs = [
        pl.BlockSpec((SEQ, LANES), by_group),
        pl.BlockSpec((SEQ, LANES), by_group),
        pl.BlockSpec((SEQ, LANES), by_group),
        pl.BlockSpec((LANES, SEQ), lambda r, m: (group, r)),
        pl.BlockSpec((LANES, SEQ), lambda r, m: (group, r)),
        pl.BlockSpec((HEADS, SEQ), lambda r, m: (0, r)),
        pl.BlockSpec((1, GROUP, 2, HALF, HALF), lambda r, m: (r, group, 0, 0, 0)),
        pl.BlockSpec((SEQ, D), by_row),
        pl.BlockSpec((SEQ, D), by_row),
    ]
    out_shape = [
        jax.ShapeDtypeStruct((D, 3 * LANES), BF16),
        jax.ShapeDtypeStruct((8, LANES), F32),
    ]
    out_specs = [pl.BlockSpec((D, 3 * LANES), whole), pl.BlockSpec((8, LANES), whole)]
    if last:
        in_specs += [
            pl.BlockSpec((SEQ, D), by_row),
            pl.BlockSpec((D, 3 * D), whole),
            pl.BlockSpec((SEQ, 3 * LANES), by_row),
        ]
        out_shape.insert(0, jax.ShapeDtypeStruct((total, D), F32))
        out_specs.insert(0, pl.BlockSpec((SEQ, D), by_row))
    else:
        out_shape.insert(0, jax.ShapeDtypeStruct((total, 3 * LANES), BF16))
        out_specs.insert(0, pl.BlockSpec((SEQ, 3 * LANES), by_row))
    return pl.pallas_call(
        functools.partial(pull_kernel, group),
        out_shape=out_shape,
        grid_spec=pltpu.PrefetchScalarGridSpec(
            num_scalar_prefetch=1,
            grid=(rows,),
            in_specs=in_specs,
            out_specs=out_specs,
            scratch_shapes=[
                pltpu.VMEM((8, SEQ), F32),
                pltpu.VMEM((LANES, SEQ), F32),
                pltpu.VMEM((D, 3 * LANES), F32),
                pltpu.VMEM((8, LANES), F32),
            ],
        ),
        compiler_params=pltpu.CompilerParams(
            dimension_semantics=("arbitrary",), vmem_limit_bytes=VMEM_LIMIT
        ),
        cost_estimate=pl.CostEstimate(
            flops=18_000_000_000, bytes_accessed=15_000_000, transcendentals=0
        ),
        name="attend_back",
    )(marks, mixed_grad, query, value, key_t, out_t, inverse, exps, qk, x, *more)


def row_marks(segment_ids):
    starts = [jnp.sum((segment_ids < number).astype(jnp.int32), axis=1) for number in range(1, 4)]
    first = jnp.zeros_like(starts[0])
    edges = [first] + starts + [jnp.full_like(first, segment_ids.shape[1])]
    begin = first
    for number in range(3, -1, -1):
        begin = jnp.where(edges[number + 1] - edges[number] == HALF, edges[number], begin)
    return jnp.stack(starts + [begin], axis=1)


def gather_blocks(block, dp_count, fsdp_count):
    parts = lax.all_gather(block, ("dp", "fsdp"), axis=0, tiled=False)
    return parts.reshape((dp_count, fsdp_count) + block.shape)


def unblock(parts):
    dp_count, fsdp_count, rows, cols = parts.shape
    return parts.transpose(0, 2, 1, 3).reshape(dp_count * rows, fsdp_count * cols)


def scatter_sum(full, dp_count, fsdp_count):
    rows, cols = full.shape
    by_col = full.reshape(rows, fsdp_count, cols // fsdp_count).transpose(1, 0, 2)
    got = lax.all_to_all(by_col, "fsdp", split_axis=0, concat_axis=0, tiled=True)
    part = jnp.sum(got.astype(F32), axis=0).astype(BF16)
    by_row = part.reshape(dp_count, rows // dp_count, cols // fsdp_count)
    got = lax.all_to_all(by_row, "dp", split_axis=0, concat_axis=0, tiled=True)
    return jnp.sum(got.astype(F32), axis=0)


def body(
    tokens,
    cotangent,
    segment_ids,
    attn_weight,
    ffn_in,
    ffn_out,
    vectors,
    attn_rows,
    attn_cols,
    in_rows,
    in_cols,
    out_rows,
    out_cols,
    vector_moment,
):
    dp_count = lax.axis_size("dp")
    fsdp_count = lax.axis_size("fsdp")
    dp_place = lax.axis_index("dp")
    fsdp_place = lax.axis_index("fsdp")
    rows_w, cols_w = attn_weight.shape
    rows_v, cols_v = vectors.shape
    marks = row_marks(segment_ids)
    table = jnp.asarray(encode_table())

    flat = jnp.concatenate(
        [attn_weight.astype(BF16).reshape(-1), vectors.astype(BF16).reshape(-1)]
    )
    flat = jnp.pad(flat, (0, -flat.shape[0] % 2048)).reshape(-1, LANES)
    got = gather_blocks(flat, dp_count, fsdp_count).reshape(dp_count, fsdp_count, -1)
    size = rows_w * cols_w
    full_attn = unblock(got[:, :, :size].reshape(dp_count, fsdp_count, rows_w, cols_w))
    full_vector = unblock(
        got[:, :, size : size + rows_v * cols_v].reshape(dp_count, fsdp_count, rows_v, cols_v)
    )
    ffn = jnp.stack([ffn_in.astype(BF16), ffn_out.astype(BF16)])
    got = gather_blocks(ffn, dp_count, fsdp_count)
    full_first = unblock(got[:, :, 0])
    full_second = unblock(got[:, :, 1])

    qkv_w = full_attn[:, : 3 * D]
    proj = full_attn[:, 3 * D :]
    qk, x, query, value, key_t, out_t, inverse, mixed, exps = attend_forward(
        marks, tokens, table, qkv_w, full_vector
    )
    block_out, resid, mixed_grad, first_g, second_g, proj_g, vector_g = feed_forward(
        tokens, cotangent, mixed, proj, full_first, full_second, full_vector
    )
    in_grad = scatter_sum(first_g, dp_count, fsdp_count)
    out_grad = scatter_sum(second_g, dp_count, fsdp_count)
    low, grads_0, sums_0 = attend_back(
        0, marks, mixed_grad, query, value, key_t, out_t, inverse, exps, qk, x
    )
    input_grad, grads_1, sums_1 = attend_back(
        1, marks, mixed_grad, query, value, key_t, out_t, inverse, exps, qk, x, resid, qkv_w, low
    )
    attn_full = jnp.concatenate(
        [
            grads_0[:, :LANES],
            grads_1[:, :LANES],
            grads_0[:, LANES : 2 * LANES],
            grads_1[:, LANES : 2 * LANES],
            grads_0[:, 2 * LANES :],
            grads_1[:, 2 * LANES :],
            proj_g,
        ],
        axis=1,
    )
    sums = jnp.concatenate([sums_0[:2], sums_1[:2]], axis=1)
    vector_full = jnp.concatenate([vector_g[:8], sums, vector_g[10:]], axis=0)
    attn_grad = scatter_sum(attn_full, dp_count, fsdp_count)
    vector_grad = scatter_sum(vector_full.astype(BF16), dp_count, fsdp_count)

    decay = 1.0 - STEP ** (-0.8)
    gradients = (attn_grad, in_grad, out_grad)
    weights_old = (attn_weight, ffn_in, ffn_out)
    rows_old = (attn_rows, in_rows, out_rows)
    cols_old = (attn_cols, in_cols, out_cols)
    moment_new = decay * vector_moment + (1.0 - decay) * (vector_grad * vector_grad + EPS_ONE)
    vector_step = vector_grad * lax.rsqrt(moment_new)
    squares = [gradient * gradient + EPS_ONE for gradient in gradients]
    pieces = []
    for square in squares:
        pieces.append(jnp.sum(square, axis=1))
    for square in squares:
        pieces.append(jnp.sum(square, axis=0))
    pieces.append(jnp.sum(vector_step * vector_step, axis=1))
    pieces.append(jnp.sum(vectors * vectors, axis=1))
    pieces.append(jnp.stack([jnp.sum(weight * weight) for weight in weights_old]))
    pieces.append(jnp.stack([jnp.sum(old) for old in rows_old]))
    sizes = [piece.shape[0] for piece in pieces]
    flat = jnp.concatenate(pieces)
    flat = jnp.pad(flat, (0, -flat.shape[0] % 1024)).reshape(-1, LANES)
    got = gather_blocks(flat, dp_count, fsdp_count).reshape(dp_count, fsdp_count, -1)
    offsets = [0]
    for size in sizes:
        offsets.append(offsets[-1] + size)
    take = lambda i: got[:, :, offsets[i] : offsets[i + 1]]
    rows_new, cols_new, row_means, entries = [], [], [], []
    for i in range(3):
        count_rows = rows_w * dp_count
        count_cols = weights_old[i].shape[1] * fsdp_count
        entries.append(float(count_rows * count_cols))
        row_all = jnp.sum(take(i), axis=1)
        mine = lax.dynamic_index_in_dim(row_all, dp_place, 0, keepdims=False)
        rows_new.append(decay * rows_old[i] + (1.0 - decay) * mine / count_cols)
        col_all = jnp.sum(take(3 + i), axis=0)
        mine = lax.dynamic_index_in_dim(col_all, fsdp_place, 0, keepdims=False)
        cols_new.append(decay * cols_old[i] + (1.0 - decay) * mine / count_rows)
        old_total = jnp.sum(take(9)[:, 0, i])
        row_means.append(
            (decay * old_total + (1.0 - decay) * jnp.sum(row_all) / count_cols) / count_rows
        )
    step_rows = jnp.sum(take(6), axis=1).reshape(-1)
    weight_rows = jnp.sum(take(7), axis=1).reshape(-1)
    weight_totals = jnp.sum(take(8), axis=(0, 1))
    updates = []
    for i in range(3):
        second = rows_new[i][:, None] * cols_new[i][None, :] / row_means[i]
        updates.append(gradients[i] * lax.rsqrt(second))
    totals = lax.psum(jnp.stack([jnp.sum(update * update) for update in updates]), ("dp", "fsdp"))
    new_weights = []
    for i in range(3):
        clip_factor = jnp.maximum(1.0, jnp.sqrt(totals[i] / entries[i]) / CLIP_LIMIT)
        step_size = STEP_RATE * jnp.maximum(EPS_TWO, jnp.sqrt(weight_totals[i] / entries[i]))
        new_weights.append(weights_old[i] - step_size / clip_factor * updates[i])
    bias_rows = FF // D
    row_places = jnp.arange(VEC)
    counts = jnp.where(row_places < bias_rows, float(FF), float(D))
    grouped_updates = jnp.where(row_places < bias_rows, jnp.sum(step_rows[:bias_rows]), step_rows)
    grouped_weights = jnp.where(row_places < bias_rows, jnp.sum(weight_rows[:bias_rows]), weight_rows)
    clip_rows = jnp.maximum(1.0, jnp.sqrt(grouped_updates / counts) / CLIP_LIMIT)
    step_sizes = STEP_RATE * jnp.maximum(EPS_TWO, jnp.sqrt(grouped_weights / counts))
    factor_rows = lax.dynamic_slice_in_dim(step_sizes / clip_rows, dp_place * rows_v, rows_v)
    vectors_new = vectors - factor_rows[:, None] * vector_step
    return (
        block_out,
        input_grad,
        attn_grad,
        in_grad,
        out_grad,
        vector_grad,
        rows_new[0],
        cols_new[0],
        rows_new[1],
        cols_new[1],
        rows_new[2],
        cols_new[2],
        moment_new,
        new_weights[0],
        new_weights[1],
        new_weights[2],
        vectors_new,
    )


def solution(mesh):
    split = P(("dp", "fsdp"), None)
    block = P("dp", "fsdp")
    stats = (P("dp"), P("fsdp")) * 3
    return jax.shard_map(
        body,
        mesh=mesh,
        in_specs=(split,) * 3 + (block,) * 4 + stats + (block,),
        out_specs=(split,) * 2 + (block,) * 4 + stats + (block,) * 5,
        check_vma=False,
    )
```

```python
import functools
import math

import jax
import jax.numpy as jnp
import numpy as np
from jax import lax
from jax.experimental import pallas as pl
from jax.experimental.pallas import tpu as pltpu
from jax.sharding import PartitionSpec as P

D = 256
FF = 2048
HEADS = 8
HEAD_DIM = 32
SEQ = 1024
HALF = 512
GROUP = 4
LANES = 128
QBLOCK = 256
WGRID = 32
STEP = 10
VEC = 16
TILE = 512
CHUNK = 512

EPS_NORM = 1e-05
EPS_ONE = 1e-30
EPS_TWO = 0.001
CLIP_LIMIT = 1.0
STEP_RATE = 0.3
FAR = 1e30
SCALE = HEAD_DIM ** (-0.5)
GELU_A = math.sqrt(2.0 / math.pi)
GELU_B = 0.044715
F32 = jnp.float32
BF16 = jnp.bfloat16
VMEM_LIMIT = 56 * 1024 * 1024


def dot(left, right):
    return jnp.dot(left, right, preferred_element_type=F32)


def dot_nt(left, right):
    return lax.dot_general(left, right, (((1,), (1,)), ((), ())), preferred_element_type=F32)


def encode_table():
    half = D // 2
    feature = np.arange(half)
    freq = np.exp(
        (2 * (feature // 2)).astype(np.float32) * np.float32(-math.log(10000.0) / half)
    ).astype(np.float32)
    angles = np.arange(1, WGRID + 1, dtype=np.float32)[:, None] * freq[None, :]
    table = np.where(feature % 2 == 0, np.sin(angles), np.cos(angles)).astype(np.float32)
    low = jnp.bfloat16
    one = table.astype(low)
    rest = table - one.astype(np.float32)
    two = rest.astype(low)
    three = (rest - two.astype(np.float32)).astype(low)
    blank = np.zeros((LANES - 3 * WGRID, half), low)
    return np.concatenate([one, two, three, blank], axis=0)


def iota(shape, dim):
    return lax.broadcasted_iota(jnp.int32, shape, dim)


def norm_forward(rows):
    centered = rows - jnp.mean(rows, axis=-1, keepdims=True)
    inverse = lax.rsqrt(jnp.mean(centered * centered, axis=-1, keepdims=True) + EPS_NORM)
    return centered * inverse, inverse


def norm_backward(upstream, normed, inverse):
    return inverse * (
        upstream
        - jnp.mean(upstream, axis=-1, keepdims=True)
        - normed * jnp.mean(upstream * normed, axis=-1, keepdims=True)
    )


def attend_kernel(
    marks,
    tokens_ref,
    table_ref,
    weight_ref,
    vector_ref,
    qk_ref,
    x_ref,
    query_ref,
    value_ref,
    key_t_ref,
    out_t_ref,
    inverse_ref,
    mixed_ref,
    exps_ref,
    key_s,
    value_s,
    mark_k,
    mark_q,
):
    row = pl.program_id(0)
    group = pl.program_id(1)
    begin = marks[row, 3]

    @pl.when(group == 0)
    def _():
        x = pltpu.roll(tokens_ref[...].astype(F32), (SEQ - begin) & (SEQ - 1), 0)
        x_low = x.astype(BF16)
        x_ref[...] = x_low
        place = (iota((SEQ, LANES), 0) + begin) & (SEQ - 1)
        lane = iota((SEQ, LANES), 1)
        one, two, three = marks[row, 0], marks[row, 1], marks[row, 2]
        start = jnp.where(
            place >= three, three, jnp.where(place >= two, two, jnp.where(place >= one, one, 0))
        )
        local = place - start
        kept = lane < 3 * WGRID
        slot = lane & (WGRID - 1)
        hot_r = jnp.where(((local >> 5) == slot) & kept, 1.0, 0.0).astype(BF16)
        hot_c = jnp.where(((local & (WGRID - 1)) == slot) & kept, 1.0, 0.0).astype(BF16)
        places = jnp.concatenate([dot(hot_r, table_ref[...]), dot(hot_c, table_ref[...])], axis=1)
        qk = (x + places).astype(BF16)
        qk_ref[...] = qk
        bias_q = vector_ref[8:9, :].astype(F32)
        bias_v = vector_ref[9:10, :].astype(F32)
        query = (dot(qk, weight_ref[:, :D]) + bias_q) * SCALE
        query_ref[...] = query.astype(BF16)
        key = dot(qk, weight_ref[:, D : 2 * D])
        key_s[...] = key.astype(BF16)
        key_t_ref[...] = key.T.astype(BF16)
        value = dot(x_low, weight_ref[:, 2 * D : 3 * D]) + bias_v
        value_ref[...] = value.astype(BF16)
        value_t = value.T.astype(BF16)
        for head in range(HEADS):
            value_s[head, :HEAD_DIM, :] = value_t[head * HEAD_DIM : (head + 1) * HEAD_DIM, :]
            value_s[head, HEAD_DIM:, :] = jnp.ones((16, SEQ), BF16)
        here = place[HALF:, :]
        number = (
            jnp.where(here >= one, 1, 0)
            + jnp.where(here >= two, 1, 0)
            + jnp.where(here >= three, 1, 0)
        )
        lane = lane[HALF:, :]
        mark_q[...] = jnp.where(number == lane, 1.0, 0.0).astype(BF16)
        mark_k[...] = jnp.where((number != lane) & (lane < 4), -FAR, 0.0).astype(BF16)

    lanes = pl.ds(pl.multiple_of(group * LANES, LANES), LANES)
    head_of = iota((1, LANES), 1) // HEAD_DIM
    for half in range(2):
        rows = slice(half * HALF, (half + 1) * HALF)
        keys_here = key_s[rows, lanes]
        for place in range(GROUP):
            head = group * GROUP + place
            key_m = keys_here * jnp.where(head_of == place, 1.0, 0.0).astype(BF16)
            if half == 1:
                key_m = jnp.concatenate([key_m, mark_k[...]], axis=1)
            for block in range(HALF // QBLOCK):
                at = half * HALF + block * QBLOCK
                query = query_ref[at : at + QBLOCK, lanes]
                if half == 1:
                    query = jnp.concatenate(
                        [query, mark_q[block * QBLOCK : (block + 1) * QBLOCK, :]], axis=1
                    )
                scores = dot_nt(key_m, query)
                exps = jnp.exp(scores - jnp.max(scores, axis=0, keepdims=True)).astype(BF16)
                exps_ref[0, place, half, :, block * QBLOCK : (block + 1) * QBLOCK] = exps
                out = dot(value_s[head, :, rows], exps)
                inverse = 1.0 / out[HEAD_DIM : HEAD_DIM + 1, :]
                inverse_ref[pl.ds(head, 1), at : at + QBLOCK] = inverse
                out_t_ref[pl.ds(pl.multiple_of(head * HEAD_DIM, HEAD_DIM), HEAD_DIM), at : at + QBLOCK] = (
                    out[:HEAD_DIM, :] * inverse
                )

    @pl.when(group == 1)
    def _():
        mixed_ref[...] = pltpu.roll(out_t_ref[...].T, begin, 0).astype(BF16)


def attend_forward(marks, tokens, table, weight, vector):
    rows = tokens.shape[0] // SEQ
    total = rows * SEQ
    by_row = lambda r, g, m: (r, 0)
    by_col = lambda r, g, m: (0, r)
    whole = lambda r, g, m: (0, 0)
    return pl.pallas_call(
        attend_kernel,
        out_shape=(
            jax.ShapeDtypeStruct((total, D), BF16),
            jax.ShapeDtypeStruct((total, D), BF16),
            jax.ShapeDtypeStruct((total, D), BF16),
            jax.ShapeDtypeStruct((total, D), BF16),
            jax.ShapeDtypeStruct((D, total), BF16),
            jax.ShapeDtypeStruct((D, total), F32),
            jax.ShapeDtypeStruct((HEADS, total), F32),
            jax.ShapeDtypeStruct((total, D), BF16),
            jax.ShapeDtypeStruct((rows, HEADS, 2, HALF, HALF), BF16),
        ),
        grid_spec=pltpu.PrefetchScalarGridSpec(
            num_scalar_prefetch=1,
            grid=(rows, 2),
            in_specs=[
                pl.BlockSpec((SEQ, D), by_row),
                pl.BlockSpec((LANES, LANES), whole),
                pl.BlockSpec((D, 3 * D), whole),
                pl.BlockSpec((VEC, D), whole),
            ],
            out_specs=[
                pl.BlockSpec((SEQ, D), by_row),
                pl.BlockSpec((SEQ, D), by_row),
                pl.BlockSpec((SEQ, D), by_row),
                pl.BlockSpec((SEQ, D), by_row),
                pl.BlockSpec((D, SEQ), by_col),
                pl.BlockSpec((D, SEQ), by_col),
                pl.BlockSpec((HEADS, SEQ), by_col),
                pl.BlockSpec((SEQ, D), by_row),
                pl.BlockSpec((1, GROUP, 2, HALF, HALF), lambda r, g, m: (r, g, 0, 0, 0)),
            ],
            scratch_shapes=[
                pltpu.VMEM((SEQ, D), BF16),
                pltpu.VMEM((HEADS, HEAD_DIM + 16, SEQ), BF16),
                pltpu.VMEM((HALF, LANES), BF16),
                pltpu.VMEM((HALF, LANES), BF16),
            ],
        ),
        compiler_params=pltpu.CompilerParams(
            dimension_semantics=("arbitrary", "arbitrary"), vmem_limit_bytes=VMEM_LIMIT
        ),
        cost_estimate=pl.CostEstimate(
            flops=20_000_000_000, bytes_accessed=30_000_000, transcendentals=8_400_000
        ),
        name="attend_forward",
    )(marks, tokens, table, weight, vector)


def feed_kernel(
    tokens_ref,
    cotangent_ref,
    mixed_ref,
    proj_ref,
    first_w_ref,
    second_w_ref,
    vector_ref,
    block_ref,
    resid_ref,
    mixed_grad_ref,
    first_out,
    second_out,
    proj_out,
    vector_out,
    first_acc,
    second_acc,
    proj_acc,
    vector_acc,
    hidden_s,
    slope_s,
):
    step = pl.program_id(0)

    @pl.when(step == 0)
    def _():
        first_acc[...] = jnp.zeros_like(first_acc)
        second_acc[...] = jnp.zeros_like(second_acc)
        proj_acc[...] = jnp.zeros_like(proj_acc)
        vector_acc[...] = jnp.zeros_like(vector_acc)

    vector = vector_ref[...].astype(F32)
    bias_o, bias_2 = vector[10:11], vector[11:12]
    gain_1, shift_1, gain_2, shift_2 = vector[12:13], vector[13:14], vector[14:15], vector[15:16]
    mixed = mixed_ref[...]
    attended = dot(mixed, proj_ref[...]) + bias_o
    norm_1, inverse_1 = norm_forward(tokens_ref[...].astype(F32) + attended)
    first = norm_1 * gain_1 + shift_1
    first_low = first.astype(BF16)
    per = CHUNK // D
    branch = jnp.zeros((TILE, D), F32)
    for at in range(FF // CHUNK):
        cols = slice(at * CHUNK, (at + 1) * CHUNK)
        bias = jnp.concatenate([vector[at * per + i : at * per + i + 1] for i in range(per)], axis=1)
        pre = dot(first_low, first_w_ref[:, cols]) + bias
        square = pre * pre
        inner = pre * (GELU_A + (GELU_A * GELU_B) * square)
        gate = 0.5 + 0.5 * jnp.tanh(inner)
        hidden = (pre * gate).astype(BF16)
        hidden_s[:, cols] = hidden
        rise = (2.0 * GELU_A) + (6.0 * GELU_A * GELU_B) * square
        slope_s[:, cols] = gate + (gate - gate * gate) * (pre * rise)
        branch += dot_nt(hidden, second_w_ref[:, cols])
    norm_2, inverse_2 = norm_forward(first + (branch + bias_2))
    block_ref[...] = norm_2 * gain_2 + shift_2
    back = cotangent_ref[...].astype(F32)
    vector_acc[14:15, :] += jnp.sum(back * norm_2, axis=0, keepdims=True)
    vector_acc[15:16, :] += jnp.sum(back, axis=0, keepdims=True)
    resid_2 = norm_backward(back * gain_2, norm_2, inverse_2)
    branch_low = resid_2.astype(BF16)
    branch_f = branch_low.astype(F32)
    vector_acc[11:12, :] += jnp.sum(branch_f, axis=0, keepdims=True)
    branch_t = branch_f.T.astype(BF16)
    first_t = first_low.astype(F32).T.astype(BF16)
    first_back = resid_2
    for at in range(FF // CHUNK):
        cols = slice(at * CHUNK, (at + 1) * CHUNK)
        hidden_grad = dot(branch_low, second_w_ref[:, cols])
        pre_low = (hidden_grad * slope_s[:, cols]).astype(BF16)
        sums = jnp.sum(pre_low.astype(F32), axis=0, keepdims=True)
        for i in range(per):
            vector_acc[at * per + i : at * per + i + 1, :] += sums[:, i * D : (i + 1) * D]
        second_acc[:, cols] += dot(branch_t, hidden_s[:, cols])
        first_acc[:, cols] += dot(first_t, pre_low)
        first_back += dot_nt(pre_low, first_w_ref[:, cols])
    vector_acc[12:13, :] += jnp.sum(first_back * norm_1, axis=0, keepdims=True)
    vector_acc[13:14, :] += jnp.sum(first_back, axis=0, keepdims=True)
    resid_1 = norm_backward(first_back * gain_1, norm_1, inverse_1)
    resid_ref[...] = resid_1
    attended_low = resid_1.astype(BF16)
    vector_acc[10:11, :] += jnp.sum(attended_low.astype(F32), axis=0, keepdims=True)
    mixed_t = mixed.astype(F32).T.astype(BF16)
    proj_acc[...] += dot(mixed_t, attended_low)
    mixed_grad_ref[...] = dot_nt(attended_low, proj_ref[...]).astype(BF16)

    @pl.when(step == pl.num_programs(0) - 1)
    def _():
        first_out[...] = first_acc[...].astype(BF16)
        second_out[...] = second_acc[...].astype(BF16)
        proj_out[...] = proj_acc[...].astype(BF16)
        vector_out[...] = vector_acc[...]


def feed_forward(tokens, cotangent, mixed, proj, first_w, second_w, vector):
    total = tokens.shape[0]
    tile = lambda i: (i, 0)
    whole = lambda i: (0, 0)
    return pl.pallas_call(
        feed_kernel,
        out_shape=(
            jax.ShapeDtypeStruct((total, D), F32),
            jax.ShapeDtypeStruct((total, D), F32),
            jax.ShapeDtypeStruct((total, D), BF16),
            jax.ShapeDtypeStruct((D, FF), BF16),
            jax.ShapeDtypeStruct((D, FF), BF16),
            jax.ShapeDtypeStruct((D, D), BF16),
            jax.ShapeDtypeStruct((VEC, D), F32),
        ),
        grid=(total // TILE,),
        in_specs=[
            pl.BlockSpec((TILE, D), tile),
            pl.BlockSpec((TILE, D), tile),
            pl.BlockSpec((TILE, D), tile),
            pl.BlockSpec((D, D), whole),
            pl.BlockSpec((D, FF), whole),
            pl.BlockSpec((D, FF), whole),
            pl.BlockSpec((VEC, D), whole),
        ],
        out_specs=[
            pl.BlockSpec((TILE, D), tile),
            pl.BlockSpec((TILE, D), tile),
            pl.BlockSpec((TILE, D), tile),
            pl.BlockSpec((D, FF), whole),
            pl.BlockSpec((D, FF), whole),
            pl.BlockSpec((D, D), whole),
            pl.BlockSpec((VEC, D), whole),
        ],
        scratch_shapes=[
            pltpu.VMEM((D, FF), F32),
            pltpu.VMEM((D, FF), F32),
            pltpu.VMEM((D, D), F32),
            pltpu.VMEM((VEC, D), F32),
            pltpu.VMEM((TILE, FF), BF16),
            pltpu.VMEM((TILE, FF), F32),
        ],
        compiler_params=pltpu.CompilerParams(
            dimension_semantics=("arbitrary",), vmem_limit_bytes=VMEM_LIMIT
        ),
        cost_estimate=pl.CostEstimate(
            flops=14_000_000_000, bytes_accessed=15_000_000, transcendentals=4_200_000
        ),
        name="feed_forward",
    )(tokens, cotangent, mixed, proj, first_w, second_w, vector)


def pull_kernel(
    group,
    marks,
    mixed_grad_ref,
    query_ref,
    value_ref,
    key_t_ref,
    out_t_ref,
    inverse_ref,
    exps_ref,
    qk_ref,
    x_ref,
    *refs,
):
    last = group == 1
    if last:
        (resid_ref, weight_ref, other_ref, input_ref, grads_ref, sums_ref, dot_s, query_t_s, acc, sum_acc) = refs
    else:
        (low_ref, grads_ref, sums_ref, dot_s, query_t_s, acc, sum_acc) = refs
    row = pl.program_id(0)
    begin = marks[row, 3]

    @pl.when(row == 0)
    def _():
        acc[...] = jnp.zeros_like(acc)
        sum_acc[...] = jnp.zeros_like(sum_acc)

    grad = pltpu.roll(mixed_grad_ref[...].astype(F32), (SEQ - begin) & (SEQ - 1), 0)
    grad_t = grad.T
    inverse = inverse_ref[group * GROUP : (group + 1) * GROUP, :]
    scaled = []
    for place in range(GROUP):
        rows = slice(place * HEAD_DIM, (place + 1) * HEAD_DIM)
        part = grad_t[rows, :] * inverse[place : place + 1, :]
        scaled.append(part)
        dot_s[place : place + 1, :] = jnp.sum(part * out_t_ref[rows, :], axis=0, keepdims=True)
    scaled_t = jnp.concatenate(scaled, axis=0)
    scaled_low_t = scaled_t.astype(BF16)
    scaled_low = scaled_t.T.astype(BF16)
    head_of = iota((1, LANES), 1) // HEAD_DIM
    key_parts = []
    value_parts = []
    for half in range(2):
        rows = slice(half * HALF, (half + 1) * HALF)
        value_here = value_ref[rows, :]
        query_here = query_ref[rows, :]
        scaled_here = scaled_low[rows, :]
        scaled_t_here = scaled_low_t[:, rows]
        key_grad = jnp.zeros((HALF, LANES), F32)
        value_grad = jnp.zeros((HALF, LANES), F32)
        for place in range(GROUP):
            mask = jnp.where(head_of == place, 1.0, 0.0).astype(BF16)
            exps = exps_ref[0, place, half]
            weight_grad = dot(value_here * mask, scaled_t_here)
            score_grad = (
                exps.astype(F32) * (weight_grad - dot_s[place : place + 1, rows])
            ).astype(BF16)
            value_grad += dot(exps, scaled_here * mask)
            key_grad += dot(score_grad, query_here * mask)
            query_t_s[place * HEAD_DIM : (place + 1) * HEAD_DIM, rows] = dot(
                key_t_ref[place * HEAD_DIM : (place + 1) * HEAD_DIM, rows], score_grad
            )
        key_parts.append(key_grad)
        value_parts.append(value_grad)
    query_low = query_t_s[...].T.astype(BF16)
    key_low = jnp.concatenate(key_parts, axis=0).astype(BF16)
    value_low = jnp.concatenate(value_parts, axis=0).astype(BF16)
    sum_acc[0:1, :] += jnp.sum(query_low.astype(F32), axis=0, keepdims=True) * SCALE
    sum_acc[1:2, :] += jnp.sum(value_low.astype(F32), axis=0, keepdims=True)
    qk_t = qk_ref[...].astype(F32).T.astype(BF16)
    x_t = x_ref[...].astype(F32).T.astype(BF16)
    acc[:, :LANES] += dot(qk_t, query_low) * SCALE
    acc[:, LANES : 2 * LANES] += dot(qk_t, key_low)
    acc[:, 2 * LANES :] += dot(x_t, value_low)
    if last:
        other = other_ref[...]
        query_all = jnp.concatenate([other[:, :LANES], query_low], axis=1)
        key_all = jnp.concatenate([other[:, LANES : 2 * LANES], key_low], axis=1)
        value_all = jnp.concatenate([other[:, 2 * LANES :], value_low], axis=1)
        pulled = (
            dot_nt(query_all, weight_ref[:, :D]) * SCALE
            + dot_nt(key_all, weight_ref[:, D : 2 * D])
            + dot_nt(value_all, weight_ref[:, 2 * D : 3 * D])
        )
        input_ref[...] = resid_ref[...] + pltpu.roll(pulled, begin, 0)
    else:
        low_ref[:, :LANES] = query_low
        low_ref[:, LANES : 2 * LANES] = key_low
        low_ref[:, 2 * LANES :] = value_low

    @pl.when(row == pl.num_programs(0) - 1)
    def _():
        grads_ref[...] = acc[...].astype(BF16)
        sums_ref[...] = sum_acc[...]


def attend_back(group, marks, mixed_grad, query, value, key_t, out_t, inverse, exps, qk, x, *more):
    total = query.shape[0]
    rows = total // SEQ
    last = group == 1
    by_group = lambda r, m: (r, group)
    by_row = lambda r, m: (r, 0)
    whole = lambda r, m: (0, 0)
    in_specs = [
        pl.BlockSpec((SEQ, LANES), by_group),
        pl.BlockSpec((SEQ, LANES), by_group),
        pl.BlockSpec((SEQ, LANES), by_group),
        pl.BlockSpec((LANES, SEQ), lambda r, m: (group, r)),
        pl.BlockSpec((LANES, SEQ), lambda r, m: (group, r)),
        pl.BlockSpec((HEADS, SEQ), lambda r, m: (0, r)),
        pl.BlockSpec((1, GROUP, 2, HALF, HALF), lambda r, m: (r, group, 0, 0, 0)),
        pl.BlockSpec((SEQ, D), by_row),
        pl.BlockSpec((SEQ, D), by_row),
    ]
    out_shape = [
        jax.ShapeDtypeStruct((D, 3 * LANES), BF16),
        jax.ShapeDtypeStruct((8, LANES), F32),
    ]
    out_specs = [pl.BlockSpec((D, 3 * LANES), whole), pl.BlockSpec((8, LANES), whole)]
    if last:
        in_specs += [
            pl.BlockSpec((SEQ, D), by_row),
            pl.BlockSpec((D, 3 * D), whole),
            pl.BlockSpec((SEQ, 3 * LANES), by_row),
        ]
        out_shape.insert(0, jax.ShapeDtypeStruct((total, D), F32))
        out_specs.insert(0, pl.BlockSpec((SEQ, D), by_row))
    else:
        out_shape.insert(0, jax.ShapeDtypeStruct((total, 3 * LANES), BF16))
        out_specs.insert(0, pl.BlockSpec((SEQ, 3 * LANES), by_row))
    return pl.pallas_call(
        functools.partial(pull_kernel, group),
        out_shape=out_shape,
        grid_spec=pltpu.PrefetchScalarGridSpec(
            num_scalar_prefetch=1,
            grid=(rows,),
            in_specs=in_specs,
            out_specs=out_specs,
            scratch_shapes=[
                pltpu.VMEM((8, SEQ), F32),
                pltpu.VMEM((LANES, SEQ), F32),
                pltpu.VMEM((D, 3 * LANES), F32),
                pltpu.VMEM((8, LANES), F32),
            ],
        ),
        compiler_params=pltpu.CompilerParams(
            dimension_semantics=("arbitrary",), vmem_limit_bytes=VMEM_LIMIT
        ),
        cost_estimate=pl.CostEstimate(
            flops=18_000_000_000, bytes_accessed=15_000_000, transcendentals=0
        ),
        name="attend_back",
    )(marks, mixed_grad, query, value, key_t, out_t, inverse, exps, qk, x, *more)


def row_marks(segment_ids):
    starts = [jnp.sum((segment_ids < number).astype(jnp.int32), axis=1) for number in range(1, 4)]
    first = jnp.zeros_like(starts[0])
    edges = [first] + starts + [jnp.full_like(first, segment_ids.shape[1])]
    begin = first
    for number in range(3, -1, -1):
        begin = jnp.where(edges[number + 1] - edges[number] == HALF, edges[number], begin)
    return jnp.stack(starts + [begin], axis=1)


def gather_axis(block, axis):
    count = lax.axis_size(axis)
    me = lax.axis_index(axis)
    parts = [block]
    for step in range(1, count):
        parts.append(lax.ppermute(block, axis, [(i, i ^ step) for i in range(count)]))
    stacked = jnp.stack(parts)
    return jnp.stack(
        [lax.dynamic_index_in_dim(stacked, me ^ i, 0, keepdims=False) for i in range(count)]
    )


def gather_blocks(block, dp_count, fsdp_count):
    return gather_axis(gather_axis(block, "fsdp"), "dp")


def unblock(parts):
    dp_count, fsdp_count, rows, cols = parts.shape
    return parts.transpose(0, 2, 1, 3).reshape(dp_count * rows, fsdp_count * cols)


def sum_axis(blocks, axis):
    count = blocks.shape[0]
    me = lax.axis_index(axis)
    pick = lambda i: lax.dynamic_index_in_dim(blocks, i, 0, keepdims=False)
    total = pick(me).astype(F32)
    for step in range(1, count):
        part = lax.ppermute(pick(me ^ step), axis, [(i, i ^ step) for i in range(count)])
        total = total + part.astype(F32)
    return total


def scatter_sum(full, dp_count, fsdp_count):
    rows, cols = full.shape
    by_col = full.reshape(rows, fsdp_count, cols // fsdp_count).transpose(1, 0, 2)
    part = sum_axis(by_col, "fsdp").astype(BF16)
    by_row = part.reshape(dp_count, rows // dp_count, cols // fsdp_count)
    return sum_axis(by_row, "dp")


def total_sum(block):
    return jnp.sum(gather_blocks(block, 0, 0), axis=(0, 1))


def body(
    tokens,
    cotangent,
    segment_ids,
    attn_weight,
    ffn_in,
    ffn_out,
    vectors,
    attn_rows,
    attn_cols,
    in_rows,
    in_cols,
    out_rows,
    out_cols,
    vector_moment,
):
    dp_count = lax.axis_size("dp")
    fsdp_count = lax.axis_size("fsdp")
    dp_place = lax.axis_index("dp")
    fsdp_place = lax.axis_index("fsdp")
    rows_w, cols_w = attn_weight.shape
    rows_v, cols_v = vectors.shape
    marks = row_marks(segment_ids)
    table = jnp.asarray(encode_table())

    flat = jnp.concatenate(
        [attn_weight.astype(BF16).reshape(-1), vectors.astype(BF16).reshape(-1)]
    )
    flat = jnp.pad(flat, (0, -flat.shape[0] % 2048)).reshape(-1, LANES)
    got = gather_blocks(flat, dp_count, fsdp_count).reshape(dp_count, fsdp_count, -1)
    size = rows_w * cols_w
    full_attn = unblock(got[:, :, :size].reshape(dp_count, fsdp_count, rows_w, cols_w))
    full_vector = unblock(
        got[:, :, size : size + rows_v * cols_v].reshape(dp_count, fsdp_count, rows_v, cols_v)
    )
    ffn = jnp.stack([ffn_in.astype(BF16), ffn_out.astype(BF16)])
    got = gather_blocks(ffn, dp_count, fsdp_count)
    full_first = unblock(got[:, :, 0])
    full_second = unblock(got[:, :, 1])

    qkv_w = full_attn[:, : 3 * D]
    proj = full_attn[:, 3 * D :]
    qk, x, query, value, key_t, out_t, inverse, mixed, exps = attend_forward(
        marks, tokens, table, qkv_w, full_vector
    )
    block_out, resid, mixed_grad, first_g, second_g, proj_g, vector_g = feed_forward(
        tokens, cotangent, mixed, proj, full_first, full_second, full_vector
    )
    in_grad = scatter_sum(first_g, dp_count, fsdp_count)
    out_grad = scatter_sum(second_g, dp_count, fsdp_count)
    low, grads_0, sums_0 = attend_back(
        0, marks, mixed_grad, query, value, key_t, out_t, inverse, exps, qk, x
    )
    input_grad, grads_1, sums_1 = attend_back(
        1, marks, mixed_grad, query, value, key_t, out_t, inverse, exps, qk, x, resid, qkv_w, low
    )
    attn_full = jnp.concatenate(
        [
            grads_0[:, :LANES],
            grads_1[:, :LANES],
            grads_0[:, LANES : 2 * LANES],
            grads_1[:, LANES : 2 * LANES],
            grads_0[:, 2 * LANES :],
            grads_1[:, 2 * LANES :],
            proj_g,
        ],
        axis=1,
    )
    sums = jnp.concatenate([sums_0[:2], sums_1[:2]], axis=1)
    vector_full = jnp.concatenate([vector_g[:8], sums, vector_g[10:]], axis=0)
    attn_grad = scatter_sum(attn_full, dp_count, fsdp_count)
    vector_grad = scatter_sum(vector_full.astype(BF16), dp_count, fsdp_count)

    decay = 1.0 - STEP ** (-0.8)
    gradients = (attn_grad, in_grad, out_grad)
    weights_old = (attn_weight, ffn_in, ffn_out)
    rows_old = (attn_rows, in_rows, out_rows)
    cols_old = (attn_cols, in_cols, out_cols)
    moment_new = decay * vector_moment + (1.0 - decay) * (vector_grad * vector_grad + EPS_ONE)
    vector_step = vector_grad * lax.rsqrt(moment_new)
    squares = [gradient * gradient + EPS_ONE for gradient in gradients]
    pieces = []
    for square in squares:
        pieces.append(jnp.sum(square, axis=1))
    for square in squares:
        pieces.append(jnp.sum(square, axis=0))
    pieces.append(jnp.sum(vector_step * vector_step, axis=1))
    pieces.append(jnp.sum(vectors * vectors, axis=1))
    pieces.append(jnp.stack([jnp.sum(weight * weight) for weight in weights_old]))
    pieces.append(jnp.stack([jnp.sum(old) for old in rows_old]))
    sizes = [piece.shape[0] for piece in pieces]
    flat = jnp.concatenate(pieces)
    flat = jnp.pad(flat, (0, -flat.shape[0] % 1024)).reshape(-1, LANES)
    got = gather_blocks(flat, dp_count, fsdp_count).reshape(dp_count, fsdp_count, -1)
    offsets = [0]
    for size in sizes:
        offsets.append(offsets[-1] + size)
    take = lambda i: got[:, :, offsets[i] : offsets[i + 1]]
    rows_new, cols_new, row_means, entries = [], [], [], []
    for i in range(3):
        count_rows = rows_w * dp_count
        count_cols = weights_old[i].shape[1] * fsdp_count
        entries.append(float(count_rows * count_cols))
        row_all = jnp.sum(take(i), axis=1)
        mine = lax.dynamic_index_in_dim(row_all, dp_place, 0, keepdims=False)
        rows_new.append(decay * rows_old[i] + (1.0 - decay) * mine / count_cols)
        col_all = jnp.sum(take(3 + i), axis=0)
        mine = lax.dynamic_index_in_dim(col_all, fsdp_place, 0, keepdims=False)
        cols_new.append(decay * cols_old[i] + (1.0 - decay) * mine / count_rows)
        old_total = jnp.sum(take(9)[:, 0, i])
        row_means.append(
            (decay * old_total + (1.0 - decay) * jnp.sum(row_all) / count_cols) / count_rows
        )
    step_rows = jnp.sum(take(6), axis=1).reshape(-1)
    weight_rows = jnp.sum(take(7), axis=1).reshape(-1)
    weight_totals = jnp.sum(take(8), axis=(0, 1))
    updates = []
    for i in range(3):
        second = rows_new[i][:, None] * cols_new[i][None, :] / row_means[i]
        updates.append(gradients[i] * lax.rsqrt(second))
    totals = total_sum(jnp.stack([jnp.sum(update * update) for update in updates]))
    new_weights = []
    for i in range(3):
        clip_factor = jnp.maximum(1.0, jnp.sqrt(totals[i] / entries[i]) / CLIP_LIMIT)
        step_size = STEP_RATE * jnp.maximum(EPS_TWO, jnp.sqrt(weight_totals[i] / entries[i]))
        new_weights.append(weights_old[i] - step_size / clip_factor * updates[i])
    bias_rows = FF // D
    row_places = jnp.arange(VEC)
    counts = jnp.where(row_places < bias_rows, float(FF), float(D))
    grouped_updates = jnp.where(row_places < bias_rows, jnp.sum(step_rows[:bias_rows]), step_rows)
    grouped_weights = jnp.where(row_places < bias_rows, jnp.sum(weight_rows[:bias_rows]), weight_rows)
    clip_rows = jnp.maximum(1.0, jnp.sqrt(grouped_updates / counts) / CLIP_LIMIT)
    step_sizes = STEP_RATE * jnp.maximum(EPS_TWO, jnp.sqrt(grouped_weights / counts))
    factor_rows = lax.dynamic_slice_in_dim(step_sizes / clip_rows, dp_place * rows_v, rows_v)
    vectors_new = vectors - factor_rows[:, None] * vector_step
    return (
        block_out,
        input_grad,
        attn_grad,
        in_grad,
        out_grad,
        vector_grad,
        rows_new[0],
        cols_new[0],
        rows_new[1],
        cols_new[1],
        rows_new[2],
        cols_new[2],
        moment_new,
        new_weights[0],
        new_weights[1],
        new_weights[2],
        vectors_new,
    )


def solution(mesh):
    split = P(("dp", "fsdp"), None)
    block = P("dp", "fsdp")
    stats = (P("dp"), P("fsdp")) * 3
    return jax.shard_map(
        body,
        mesh=mesh,
        in_specs=(split,) * 3 + (block,) * 4 + stats + (block,),
        out_specs=(split,) * 2 + (block,) * 4 + stats + (block,) * 5,
        check_vma=False,
    )
```

```python
import functools
import math

import jax
import jax.numpy as jnp
import numpy as np
from jax import lax
from jax.experimental import pallas as pl
from jax.experimental.pallas import tpu as pltpu
from jax.sharding import PartitionSpec as P

D = 256
FF = 2048
HEADS = 8
HEAD_DIM = 32
SEQ = 1024
HALF = 512
GROUP = 4
LANES = 128
QBLOCK = 256
WGRID = 32
STEP = 10
VEC = 16
TILE = 512
CHUNK = 512

EPS_NORM = 1e-05
EPS_ONE = 1e-30
EPS_TWO = 0.001
CLIP_LIMIT = 1.0
STEP_RATE = 0.3
FAR = 1e30
SCALE = HEAD_DIM ** (-0.5)
GELU_A = math.sqrt(2.0 / math.pi)
GELU_B = 0.044715
F32 = jnp.float32
BF16 = jnp.bfloat16
VMEM_LIMIT = 56 * 1024 * 1024


def dot(left, right):
    return jnp.dot(left, right, preferred_element_type=F32)


def dot_nt(left, right):
    return lax.dot_general(left, right, (((1,), (1,)), ((), ())), preferred_element_type=F32)


def encode_table():
    half = D // 2
    feature = np.arange(half)
    freq = np.exp(
        (2 * (feature // 2)).astype(np.float32) * np.float32(-math.log(10000.0) / half)
    ).astype(np.float32)
    angles = np.arange(1, WGRID + 1, dtype=np.float32)[:, None] * freq[None, :]
    table = np.where(feature % 2 == 0, np.sin(angles), np.cos(angles)).astype(np.float32)
    low = jnp.bfloat16
    one = table.astype(low)
    rest = table - one.astype(np.float32)
    two = rest.astype(low)
    three = (rest - two.astype(np.float32)).astype(low)
    blank = np.zeros((LANES - 3 * WGRID, half), low)
    return np.concatenate([one, two, three, blank], axis=0)


def iota(shape, dim):
    return lax.broadcasted_iota(jnp.int32, shape, dim)


def norm_forward(rows):
    centered = rows - jnp.mean(rows, axis=-1, keepdims=True)
    inverse = lax.rsqrt(jnp.mean(centered * centered, axis=-1, keepdims=True) + EPS_NORM)
    return centered * inverse, inverse


def norm_backward(upstream, normed, inverse):
    return inverse * (
        upstream
        - jnp.mean(upstream, axis=-1, keepdims=True)
        - normed * jnp.mean(upstream * normed, axis=-1, keepdims=True)
    )


def attend_kernel(
    marks,
    tokens_ref,
    table_ref,
    weight_ref,
    vector_ref,
    qk_ref,
    x_ref,
    query_ref,
    value_ref,
    key_t_ref,
    out_t_ref,
    inverse_ref,
    mixed_ref,
    exps_ref,
    key_s,
    value_s,
    mark_k,
    mark_q,
):
    row = pl.program_id(0)
    group = pl.program_id(1)
    begin = marks[row, 3]

    @pl.when(group == 0)
    def _():
        x = pltpu.roll(tokens_ref[...].astype(F32), (SEQ - begin) & (SEQ - 1), 0)
        x_low = x.astype(BF16)
        x_ref[...] = x_low
        place = (iota((SEQ, LANES), 0) + begin) & (SEQ - 1)
        lane = iota((SEQ, LANES), 1)
        one, two, three = marks[row, 0], marks[row, 1], marks[row, 2]
        start = jnp.where(
            place >= three, three, jnp.where(place >= two, two, jnp.where(place >= one, one, 0))
        )
        local = place - start
        kept = lane < 3 * WGRID
        slot = lane & (WGRID - 1)
        hot_r = jnp.where(((local >> 5) == slot) & kept, 1.0, 0.0).astype(BF16)
        hot_c = jnp.where(((local & (WGRID - 1)) == slot) & kept, 1.0, 0.0).astype(BF16)
        places = jnp.concatenate([dot(hot_r, table_ref[...]), dot(hot_c, table_ref[...])], axis=1)
        qk = (x + places).astype(BF16)
        qk_ref[...] = qk
        bias_q = vector_ref[8:9, :].astype(F32)
        bias_v = vector_ref[9:10, :].astype(F32)
        query = (dot(qk, weight_ref[:, :D]) + bias_q) * SCALE
        query_ref[...] = query.astype(BF16)
        key = dot(qk, weight_ref[:, D : 2 * D])
        key_s[...] = key.astype(BF16)
        key_t_ref[...] = key.T.astype(BF16)
        value = dot(x_low, weight_ref[:, 2 * D : 3 * D]) + bias_v
        value_ref[...] = value.astype(BF16)
        value_t = value.T.astype(BF16)
        for head in range(HEADS):
            value_s[head, :HEAD_DIM, :] = value_t[head * HEAD_DIM : (head + 1) * HEAD_DIM, :]
            value_s[head, HEAD_DIM:, :] = jnp.ones((16, SEQ), BF16)
        here = place[HALF:, :]
        number = (
            jnp.where(here >= one, 1, 0)
            + jnp.where(here >= two, 1, 0)
            + jnp.where(here >= three, 1, 0)
        )
        lane = lane[HALF:, :]
        mark_q[...] = jnp.where(number == lane, 1.0, 0.0).astype(BF16)
        mark_k[...] = jnp.where((number != lane) & (lane < 4), -FAR, 0.0).astype(BF16)

    lanes = pl.ds(pl.multiple_of(group * LANES, LANES), LANES)
    head_of = iota((1, LANES), 1) // HEAD_DIM
    for half in range(2):
        rows = slice(half * HALF, (half + 1) * HALF)
        keys_here = key_s[rows, lanes]
        for place in range(GROUP):
            head = group * GROUP + place
            key_m = keys_here * jnp.where(head_of == place, 1.0, 0.0).astype(BF16)
            if half == 1:
                key_m = jnp.concatenate([key_m, mark_k[...]], axis=1)
            for block in range(HALF // QBLOCK):
                at = half * HALF + block * QBLOCK
                query = query_ref[at : at + QBLOCK, lanes]
                if half == 1:
                    query = jnp.concatenate(
                        [query, mark_q[block * QBLOCK : (block + 1) * QBLOCK, :]], axis=1
                    )
                scores = dot_nt(key_m, query)
                exps = jnp.exp(scores - jnp.max(scores, axis=0, keepdims=True)).astype(BF16)
                exps_ref[0, place, half, :, block * QBLOCK : (block + 1) * QBLOCK] = exps
                out = dot(value_s[head, :, rows], exps)
                inverse = 1.0 / out[HEAD_DIM : HEAD_DIM + 1, :]
                inverse_ref[pl.ds(head, 1), at : at + QBLOCK] = inverse
                out_t_ref[pl.ds(pl.multiple_of(head * HEAD_DIM, HEAD_DIM), HEAD_DIM), at : at + QBLOCK] = (
                    out[:HEAD_DIM, :] * inverse
                )

    @pl.when(group == 1)
    def _():
        mixed_ref[...] = pltpu.roll(out_t_ref[...].T, begin, 0).astype(BF16)


def attend_forward(marks, tokens, table, weight, vector):
    rows = tokens.shape[0] // SEQ
    total = rows * SEQ
    by_row = lambda r, g, m: (r, 0)
    by_col = lambda r, g, m: (0, r)
    whole = lambda r, g, m: (0, 0)
    return pl.pallas_call(
        attend_kernel,
        out_shape=(
            jax.ShapeDtypeStruct((total, D), BF16),
            jax.ShapeDtypeStruct((total, D), BF16),
            jax.ShapeDtypeStruct((total, D), BF16),
            jax.ShapeDtypeStruct((total, D), BF16),
            jax.ShapeDtypeStruct((D, total), BF16),
            jax.ShapeDtypeStruct((D, total), F32),
            jax.ShapeDtypeStruct((HEADS, total), F32),
            jax.ShapeDtypeStruct((total, D), BF16),
            jax.ShapeDtypeStruct((rows, HEADS, 2, HALF, HALF), BF16),
        ),
        grid_spec=pltpu.PrefetchScalarGridSpec(
            num_scalar_prefetch=1,
            grid=(rows, 2),
            in_specs=[
                pl.BlockSpec((SEQ, D), by_row),
                pl.BlockSpec((LANES, LANES), whole),
                pl.BlockSpec((D, 3 * D), whole),
                pl.BlockSpec((VEC, D), whole),
            ],
            out_specs=[
                pl.BlockSpec((SEQ, D), by_row),
                pl.BlockSpec((SEQ, D), by_row),
                pl.BlockSpec((SEQ, D), by_row),
                pl.BlockSpec((SEQ, D), by_row),
                pl.BlockSpec((D, SEQ), by_col),
                pl.BlockSpec((D, SEQ), by_col),
                pl.BlockSpec((HEADS, SEQ), by_col),
                pl.BlockSpec((SEQ, D), by_row),
                pl.BlockSpec((1, GROUP, 2, HALF, HALF), lambda r, g, m: (r, g, 0, 0, 0)),
            ],
            scratch_shapes=[
                pltpu.VMEM((SEQ, D), BF16),
                pltpu.VMEM((HEADS, HEAD_DIM + 16, SEQ), BF16),
                pltpu.VMEM((HALF, LANES), BF16),
                pltpu.VMEM((HALF, LANES), BF16),
            ],
        ),
        compiler_params=pltpu.CompilerParams(
            dimension_semantics=("arbitrary", "arbitrary"), vmem_limit_bytes=VMEM_LIMIT
        ),
        cost_estimate=pl.CostEstimate(
            flops=20_000_000_000, bytes_accessed=30_000_000, transcendentals=8_400_000
        ),
        name="attend_forward",
    )(marks, tokens, table, weight, vector)


def feed_kernel(
    tokens_ref,
    cotangent_ref,
    mixed_ref,
    proj_ref,
    first_w_ref,
    second_w_ref,
    vector_ref,
    block_ref,
    resid_ref,
    mixed_grad_ref,
    both_out,
    proj_out,
    vector_out,
    first_acc,
    second_acc,
    proj_acc,
    vector_acc,
    hidden_s,
    slope_s,
):
    step = pl.program_id(0)

    @pl.when(step == 0)
    def _():
        first_acc[...] = jnp.zeros_like(first_acc)
        second_acc[...] = jnp.zeros_like(second_acc)
        proj_acc[...] = jnp.zeros_like(proj_acc)
        vector_acc[...] = jnp.zeros_like(vector_acc)

    vector = vector_ref[...].astype(F32)
    bias_o, bias_2 = vector[10:11], vector[11:12]
    gain_1, shift_1, gain_2, shift_2 = vector[12:13], vector[13:14], vector[14:15], vector[15:16]
    mixed = mixed_ref[...]
    attended = dot(mixed, proj_ref[...]) + bias_o
    norm_1, inverse_1 = norm_forward(tokens_ref[...].astype(F32) + attended)
    first = norm_1 * gain_1 + shift_1
    first_low = first.astype(BF16)
    per = CHUNK // D
    branch = jnp.zeros((TILE, D), F32)
    for at in range(FF // CHUNK):
        cols = slice(at * CHUNK, (at + 1) * CHUNK)
        bias = jnp.concatenate([vector[at * per + i : at * per + i + 1] for i in range(per)], axis=1)
        pre = dot(first_low, first_w_ref[:, cols]) + bias
        square = pre * pre
        inner = pre * (GELU_A + (GELU_A * GELU_B) * square)
        gate = 0.5 + 0.5 * jnp.tanh(inner)
        hidden = (pre * gate).astype(BF16)
        hidden_s[:, cols] = hidden
        rise = (2.0 * GELU_A) + (6.0 * GELU_A * GELU_B) * square
        slope_s[:, cols] = gate + (gate - gate * gate) * (pre * rise)
        branch += dot_nt(hidden, second_w_ref[:, cols])
    norm_2, inverse_2 = norm_forward(first + (branch + bias_2))
    block_ref[...] = norm_2 * gain_2 + shift_2
    back = cotangent_ref[...].astype(F32)
    vector_acc[14:15, :] += jnp.sum(back * norm_2, axis=0, keepdims=True)
    vector_acc[15:16, :] += jnp.sum(back, axis=0, keepdims=True)
    resid_2 = norm_backward(back * gain_2, norm_2, inverse_2)
    branch_low = resid_2.astype(BF16)
    branch_f = branch_low.astype(F32)
    vector_acc[11:12, :] += jnp.sum(branch_f, axis=0, keepdims=True)
    branch_t = branch_f.T.astype(BF16)
    first_t = first_low.astype(F32).T.astype(BF16)
    first_back = resid_2
    for at in range(FF // CHUNK):
        cols = slice(at * CHUNK, (at + 1) * CHUNK)
        hidden_grad = dot(branch_low, second_w_ref[:, cols])
        pre_low = (hidden_grad * slope_s[:, cols]).astype(BF16)
        sums = jnp.sum(pre_low.astype(F32), axis=0, keepdims=True)
        for i in range(per):
            vector_acc[at * per + i : at * per + i + 1, :] += sums[:, i * D : (i + 1) * D]
        second_acc[:, cols] += dot(branch_t, hidden_s[:, cols])
        first_acc[:, cols] += dot(first_t, pre_low)
        first_back += dot_nt(pre_low, first_w_ref[:, cols])
    vector_acc[12:13, :] += jnp.sum(first_back * norm_1, axis=0, keepdims=True)
    vector_acc[13:14, :] += jnp.sum(first_back, axis=0, keepdims=True)
    resid_1 = norm_backward(first_back * gain_1, norm_1, inverse_1)
    resid_ref[...] = resid_1
    attended_low = resid_1.astype(BF16)
    vector_acc[10:11, :] += jnp.sum(attended_low.astype(F32), axis=0, keepdims=True)
    mixed_t = mixed.astype(F32).T.astype(BF16)
    proj_acc[...] += dot(mixed_t, attended_low)
    mixed_grad_ref[...] = dot_nt(attended_low, proj_ref[...]).astype(BF16)

    @pl.when(step == pl.num_programs(0) - 1)
    def _():
        both_out[0] = first_acc[...].astype(BF16)
        both_out[1] = second_acc[...].astype(BF16)
        proj_out[...] = proj_acc[...].astype(BF16)
        vector_out[...] = vector_acc[...]


def feed_forward(tokens, cotangent, mixed, proj, first_w, second_w, vector):
    total = tokens.shape[0]
    tile = lambda i: (i, 0)
    whole = lambda i: (0, 0)
    return pl.pallas_call(
        feed_kernel,
        out_shape=(
            jax.ShapeDtypeStruct((total, D), F32),
            jax.ShapeDtypeStruct((total, D), F32),
            jax.ShapeDtypeStruct((total, D), BF16),
            jax.ShapeDtypeStruct((2, D, FF), BF16),
            jax.ShapeDtypeStruct((D, D), BF16),
            jax.ShapeDtypeStruct((VEC, D), F32),
        ),
        grid=(total // TILE,),
        in_specs=[
            pl.BlockSpec((TILE, D), tile),
            pl.BlockSpec((TILE, D), tile),
            pl.BlockSpec((TILE, D), tile),
            pl.BlockSpec((D, D), whole),
            pl.BlockSpec((D, FF), whole),
            pl.BlockSpec((D, FF), whole),
            pl.BlockSpec((VEC, D), whole),
        ],
        out_specs=[
            pl.BlockSpec((TILE, D), tile),
            pl.BlockSpec((TILE, D), tile),
            pl.BlockSpec((TILE, D), tile),
            pl.BlockSpec((2, D, FF), lambda i: (0, 0, 0)),
            pl.BlockSpec((D, D), whole),
            pl.BlockSpec((VEC, D), whole),
        ],
        scratch_shapes=[
            pltpu.VMEM((D, FF), F32),
            pltpu.VMEM((D, FF), F32),
            pltpu.VMEM((D, D), F32),
            pltpu.VMEM((VEC, D), F32),
            pltpu.VMEM((TILE, FF), BF16),
            pltpu.VMEM((TILE, FF), F32),
        ],
        compiler_params=pltpu.CompilerParams(
            dimension_semantics=("arbitrary",), vmem_limit_bytes=VMEM_LIMIT
        ),
        cost_estimate=pl.CostEstimate(
            flops=14_000_000_000, bytes_accessed=15_000_000, transcendentals=4_200_000
        ),
        name="feed_forward",
    )(tokens, cotangent, mixed, proj, first_w, second_w, vector)


def pull_kernel(
    group,
    marks,
    mixed_grad_ref,
    query_ref,
    value_ref,
    key_t_ref,
    out_t_ref,
    inverse_ref,
    exps_ref,
    qk_ref,
    x_ref,
    *refs,
):
    last = group == 1
    if last:
        (resid_ref, weight_ref, other_ref, input_ref, grads_ref, sums_ref, dot_s, query_t_s, acc, sum_acc) = refs
    else:
        (low_ref, grads_ref, sums_ref, dot_s, query_t_s, acc, sum_acc) = refs
    row = pl.program_id(0)
    begin = marks[row, 3]

    @pl.when(row == 0)
    def _():
        acc[...] = jnp.zeros_like(acc)
        sum_acc[...] = jnp.zeros_like(sum_acc)

    grad = pltpu.roll(mixed_grad_ref[...].astype(F32), (SEQ - begin) & (SEQ - 1), 0)
    grad_t = grad.T
    inverse = inverse_ref[group * GROUP : (group + 1) * GROUP, :]
    scaled = []
    for place in range(GROUP):
        rows = slice(place * HEAD_DIM, (place + 1) * HEAD_DIM)
        part = grad_t[rows, :] * inverse[place : place + 1, :]
        scaled.append(part)
        dot_s[place : place + 1, :] = jnp.sum(part * out_t_ref[rows, :], axis=0, keepdims=True)
    scaled_t = jnp.concatenate(scaled, axis=0)
    scaled_low_t = scaled_t.astype(BF16)
    scaled_low = scaled_t.T.astype(BF16)
    head_of = iota((1, LANES), 1) // HEAD_DIM
    key_parts = []
    value_parts = []
    for half in range(2):
        rows = slice(half * HALF, (half + 1) * HALF)
        value_here = value_ref[rows, :]
        query_here = query_ref[rows, :]
        scaled_here = scaled_low[rows, :]
        scaled_t_here = scaled_low_t[:, rows]
        key_grad = jnp.zeros((HALF, LANES), F32)
        value_grad = jnp.zeros((HALF, LANES), F32)
        for place in range(GROUP):
            mask = jnp.where(head_of == place, 1.0, 0.0).astype(BF16)
            exps = exps_ref[0, place, half]
            weight_grad = dot(value_here * mask, scaled_t_here)
            score_grad = (
                exps.astype(F32) * (weight_grad - dot_s[place : place + 1, rows])
            ).astype(BF16)
            value_grad += dot(exps, scaled_here * mask)
            key_grad += dot(score_grad, query_here * mask)
            query_t_s[place * HEAD_DIM : (place + 1) * HEAD_DIM, rows] = dot(
                key_t_ref[place * HEAD_DIM : (place + 1) * HEAD_DIM, rows], score_grad
            )
        key_parts.append(key_grad)
        value_parts.append(value_grad)
    query_low = query_t_s[...].T.astype(BF16)
    key_low = jnp.concatenate(key_parts, axis=0).astype(BF16)
    value_low = jnp.concatenate(value_parts, axis=0).astype(BF16)
    sum_acc[0:1, :] += jnp.sum(query_low.astype(F32), axis=0, keepdims=True) * SCALE
    sum_acc[1:2, :] += jnp.sum(value_low.astype(F32), axis=0, keepdims=True)
    qk_t = qk_ref[...].astype(F32).T.astype(BF16)
    x_t = x_ref[...].astype(F32).T.astype(BF16)
    acc[:, :LANES] += dot(qk_t, query_low) * SCALE
    acc[:, LANES : 2 * LANES] += dot(qk_t, key_low)
    acc[:, 2 * LANES :] += dot(x_t, value_low)
    if last:
        other = other_ref[...]
        query_all = jnp.concatenate([other[:, :LANES], query_low], axis=1)
        key_all = jnp.concatenate([other[:, LANES : 2 * LANES], key_low], axis=1)
        value_all = jnp.concatenate([other[:, 2 * LANES :], value_low], axis=1)
        pulled = (
            dot_nt(query_all, weight_ref[:, :D]) * SCALE
            + dot_nt(key_all, weight_ref[:, D : 2 * D])
            + dot_nt(value_all, weight_ref[:, 2 * D : 3 * D])
        )
        input_ref[...] = resid_ref[...] + pltpu.roll(pulled, begin, 0)
    else:
        low_ref[:, :LANES] = query_low
        low_ref[:, LANES : 2 * LANES] = key_low
        low_ref[:, 2 * LANES :] = value_low

    @pl.when(row == pl.num_programs(0) - 1)
    def _():
        grads_ref[...] = acc[...].astype(BF16)
        sums_ref[...] = sum_acc[...]


def attend_back(group, marks, mixed_grad, query, value, key_t, out_t, inverse, exps, qk, x, *more):
    total = query.shape[0]
    rows = total // SEQ
    last = group == 1
    by_group = lambda r, m: (r, group)
    by_row = lambda r, m: (r, 0)
    whole = lambda r, m: (0, 0)
    in_specs = [
        pl.BlockSpec((SEQ, LANES), by_group),
        pl.BlockSpec((SEQ, LANES), by_group),
        pl.BlockSpec((SEQ, LANES), by_group),
        pl.BlockSpec((LANES, SEQ), lambda r, m: (group, r)),
        pl.BlockSpec((LANES, SEQ), lambda r, m: (group, r)),
        pl.BlockSpec((HEADS, SEQ), lambda r, m: (0, r)),
        pl.BlockSpec((1, GROUP, 2, HALF, HALF), lambda r, m: (r, group, 0, 0, 0)),
        pl.BlockSpec((SEQ, D), by_row),
        pl.BlockSpec((SEQ, D), by_row),
    ]
    out_shape = [
        jax.ShapeDtypeStruct((D, 3 * LANES), BF16),
        jax.ShapeDtypeStruct((8, LANES), F32),
    ]
    out_specs = [pl.BlockSpec((D, 3 * LANES), whole), pl.BlockSpec((8, LANES), whole)]
    if last:
        in_specs += [
            pl.BlockSpec((SEQ, D), by_row),
            pl.BlockSpec((D, 3 * D), whole),
            pl.BlockSpec((SEQ, 3 * LANES), by_row),
        ]
        out_shape.insert(0, jax.ShapeDtypeStruct((total, D), F32))
        out_specs.insert(0, pl.BlockSpec((SEQ, D), by_row))
    else:
        out_shape.insert(0, jax.ShapeDtypeStruct((total, 3 * LANES), BF16))
        out_specs.insert(0, pl.BlockSpec((SEQ, 3 * LANES), by_row))
    return pl.pallas_call(
        functools.partial(pull_kernel, group),
        out_shape=out_shape,
        grid_spec=pltpu.PrefetchScalarGridSpec(
            num_scalar_prefetch=1,
            grid=(rows,),
            in_specs=in_specs,
            out_specs=out_specs,
            scratch_shapes=[
                pltpu.VMEM((8, SEQ), F32),
                pltpu.VMEM((LANES, SEQ), F32),
                pltpu.VMEM((D, 3 * LANES), F32),
                pltpu.VMEM((8, LANES), F32),
            ],
        ),
        compiler_params=pltpu.CompilerParams(
            dimension_semantics=("arbitrary",), vmem_limit_bytes=VMEM_LIMIT
        ),
        cost_estimate=pl.CostEstimate(
            flops=18_000_000_000, bytes_accessed=15_000_000, transcendentals=0
        ),
        name="attend_back",
    )(marks, mixed_grad, query, value, key_t, out_t, inverse, exps, qk, x, *more)


def row_marks(segment_ids):
    starts = [jnp.sum((segment_ids < number).astype(jnp.int32), axis=1) for number in range(1, 4)]
    first = jnp.zeros_like(starts[0])
    edges = [first] + starts + [jnp.full_like(first, segment_ids.shape[1])]
    begin = first
    for number in range(3, -1, -1):
        begin = jnp.where(edges[number + 1] - edges[number] == HALF, edges[number], begin)
    return jnp.stack(starts + [begin], axis=1)


def gather_blocks(block, dp_count, fsdp_count):
    count = dp_count * fsdp_count
    sent = jnp.broadcast_to(block[None], (count,) + block.shape)
    got = lax.all_to_all(sent, ("dp", "fsdp"), split_axis=0, concat_axis=0, tiled=True)
    return got.reshape((dp_count, fsdp_count) + block.shape)


def unblock(parts):
    dp_count, fsdp_count, rows, cols = parts.shape
    return parts.transpose(0, 2, 1, 3).reshape(dp_count * rows, fsdp_count * cols)


def chip_groups(fsdp_count):
    return [[core + 2 * chip for chip in range(fsdp_count // 2)] for core in range(2)]


def core_swap(block, fsdp_count):
    return lax.ppermute(block, "fsdp", [(i, i ^ 1) for i in range(fsdp_count)])


def gather_early(block, dp_count, fsdp_count):
    core = lax.axis_index("fsdp") & 1
    other = core_swap(block, fsdp_count)
    pair = jnp.stack([jnp.where(core == 0, block, other), jnp.where(core == 0, other, block)])
    sent = jnp.broadcast_to(pair[None], (dp_count,) + pair.shape)
    return lax.all_to_all(sent, "dp", split_axis=0, concat_axis=0, tiled=True)


def gather_late(part, fsdp_count):
    chips = fsdp_count // 2
    sent = jnp.broadcast_to(part[None], (chips,) + part.shape)
    return lax.all_to_all(
        sent,
        "fsdp",
        split_axis=0,
        concat_axis=0,
        axis_index_groups=chip_groups(fsdp_count),
        tiled=True,
    )


def sum_core(full, fsdp_count):
    core = lax.axis_index("fsdp") & 1
    kinds, rows, cols = full.shape
    by_col = full.reshape(kinds, rows, fsdp_count // 2, 2, cols // fsdp_count)
    by_col = by_col.transpose(3, 2, 0, 1, 4)
    mine = lax.dynamic_index_in_dim(by_col, core, 0, keepdims=False)
    other = lax.dynamic_index_in_dim(by_col, 1 - core, 0, keepdims=False)
    got = core_swap(other, fsdp_count)
    return (mine.astype(F32) + got.astype(F32)).astype(BF16)


def sum_chips(part, fsdp_count):
    got = lax.all_to_all(
        part,
        "fsdp",
        split_axis=0,
        concat_axis=0,
        axis_index_groups=chip_groups(fsdp_count),
        tiled=True,
    )
    return jnp.sum(got.astype(F32), axis=0).astype(BF16)


def sum_dp(part, dp_count):
    kinds, rows, cols = part.shape
    by_row = part.reshape(kinds, dp_count, rows // dp_count, cols).transpose(1, 0, 2, 3)
    got = lax.all_to_all(by_row, "dp", split_axis=0, concat_axis=0, tiled=True)
    return jnp.sum(got.astype(F32), axis=0)


def to_blocks(full, dp_count, fsdp_count):
    rows, cols = full.shape
    blocks = full.reshape(dp_count, rows // dp_count, fsdp_count, cols // fsdp_count)
    return blocks.transpose(0, 2, 1, 3).reshape(dp_count * fsdp_count, -1)


def body(
    tokens,
    cotangent,
    segment_ids,
    attn_weight,
    ffn_in,
    ffn_out,
    vectors,
    attn_rows,
    attn_cols,
    in_rows,
    in_cols,
    out_rows,
    out_cols,
    vector_moment,
):
    dp_count = lax.axis_size("dp")
    fsdp_count = lax.axis_size("fsdp")
    dp_place = lax.axis_index("dp")
    fsdp_place = lax.axis_index("fsdp")
    rows_w, cols_w = attn_weight.shape
    rows_v, cols_v = vectors.shape
    marks = row_marks(segment_ids)
    table = jnp.asarray(encode_table())

    flat = jnp.concatenate(
        [attn_weight.astype(BF16).reshape(-1), vectors.astype(BF16).reshape(-1)]
    )
    flat = jnp.pad(flat, (0, -flat.shape[0] % 2048)).reshape(-1, LANES)
    ffn = jnp.stack([ffn_in.astype(BF16), ffn_out.astype(BF16)])
    early = gather_early(ffn, dp_count, fsdp_count)
    got = gather_blocks(flat, dp_count, fsdp_count)
    got, early = lax.optimization_barrier((got, early))
    late = gather_late(early, fsdp_count)
    got = got.reshape(dp_count, fsdp_count, -1)
    size = rows_w * cols_w
    full_attn = unblock(got[:, :, :size].reshape(dp_count, fsdp_count, rows_w, cols_w))
    full_vector = unblock(
        got[:, :, size : size + rows_v * cols_v].reshape(dp_count, fsdp_count, rows_v, cols_v)
    )

    qkv_w = full_attn[:, : 3 * D]
    proj = full_attn[:, 3 * D :]
    qk, x, query, value, key_t, out_t, inverse, mixed, exps = attend_forward(
        marks, tokens, table, qkv_w, full_vector
    )
    late = late.transpose(3, 1, 4, 0, 2, 5).reshape(2, D, FF)
    full_first, full_second = late[0], late[1]
    block_out, resid, mixed_grad, ffn_g, proj_g, vector_g = feed_forward(
        tokens, cotangent, mixed, proj, full_first, full_second, full_vector
    )
    ffn_part = sum_core(ffn_g, fsdp_count)
    low, grads_0, sums_0 = attend_back(
        0, marks, mixed_grad, query, value, key_t, out_t, inverse, exps, qk, x
    )
    resid, low, ffn_part = lax.optimization_barrier((resid, low, ffn_part))
    ffn_part = sum_chips(ffn_part, fsdp_count)
    input_grad, grads_1, sums_1 = attend_back(
        1, marks, mixed_grad, query, value, key_t, out_t, inverse, exps, qk, x, resid, qkv_w, low
    )
    attn_full = jnp.concatenate(
        [
            grads_0[:, :LANES],
            grads_1[:, :LANES],
            grads_0[:, LANES : 2 * LANES],
            grads_1[:, LANES : 2 * LANES],
            grads_0[:, 2 * LANES :],
            grads_1[:, 2 * LANES :],
            proj_g,
        ],
        axis=1,
    )
    sums = jnp.concatenate([sums_0[:2], sums_1[:2]], axis=1)
    vector_full = jnp.concatenate([vector_g[:8], sums, vector_g[10:]], axis=0)
    attn_full, vector_full, ffn_part = lax.optimization_barrier((attn_full, vector_full, ffn_part))
    sent = jnp.concatenate(
        [
            to_blocks(attn_full, dp_count, fsdp_count),
            to_blocks(vector_full.astype(BF16), dp_count, fsdp_count),
        ],
        axis=1,
    )
    pad = -sent.shape[1] % 2048
    sent = jnp.pad(sent, ((0, 0), (0, pad))).reshape(dp_count * fsdp_count, -1, LANES)
    got = lax.all_to_all(sent, ("dp", "fsdp"), split_axis=0, concat_axis=0, tiled=True)
    ffn_grad = sum_dp(ffn_part, dp_count)
    in_grad, out_grad = ffn_grad[0], ffn_grad[1]
    got = jnp.sum(got.astype(F32), axis=0).reshape(-1)
    attn_grad = got[:size].reshape(rows_w, cols_w)
    vector_grad = got[size : size + rows_v * cols_v].reshape(rows_v, cols_v)

    decay = 1.0 - STEP ** (-0.8)
    gradients = (attn_grad, in_grad, out_grad)
    weights_old = (attn_weight, ffn_in, ffn_out)
    rows_old = (attn_rows, in_rows, out_rows)
    cols_old = (attn_cols, in_cols, out_cols)
    moment_new = decay * vector_moment + (1.0 - decay) * (vector_grad * vector_grad + EPS_ONE)
    vector_step = vector_grad * lax.rsqrt(moment_new)
    squares = [gradient * gradient + EPS_ONE for gradient in gradients]
    pieces = []
    for square in squares:
        pieces.append(jnp.sum(square, axis=1))
    for square in squares:
        pieces.append(jnp.sum(square, axis=0))
    pieces.append(jnp.sum(vector_step * vector_step, axis=1))
    pieces.append(jnp.sum(vectors * vectors, axis=1))
    pieces.append(jnp.stack([jnp.sum(weight * weight) for weight in weights_old]))
    pieces.append(jnp.stack([jnp.sum(old) for old in rows_old]))
    sizes = [piece.shape[0] for piece in pieces]
    flat = jnp.concatenate(pieces)
    flat = jnp.pad(flat, (0, -flat.shape[0] % 1024)).reshape(-1, LANES)
    got = gather_blocks(flat, dp_count, fsdp_count).reshape(dp_count, fsdp_count, -1)
    offsets = [0]
    for length in sizes:
        offsets.append(offsets[-1] + length)
    take = lambda i: got[:, :, offsets[i] : offsets[i + 1]]
    rows_new, cols_new, row_means, entries = [], [], [], []
    for i in range(3):
        count_rows = rows_w * dp_count
        count_cols = weights_old[i].shape[1] * fsdp_count
        entries.append(float(count_rows * count_cols))
        row_all = jnp.sum(take(i), axis=1)
        mine = lax.dynamic_index_in_dim(row_all, dp_place, 0, keepdims=False)
        rows_new.append(decay * rows_old[i] + (1.0 - decay) * mine / count_cols)
        col_all = jnp.sum(take(3 + i), axis=0)
        mine = lax.dynamic_index_in_dim(col_all, fsdp_place, 0, keepdims=False)
        cols_new.append(decay * cols_old[i] + (1.0 - decay) * mine / count_rows)
        old_total = jnp.sum(take(9)[:, 0, i])
        row_means.append(
            (decay * old_total + (1.0 - decay) * jnp.sum(row_all) / count_cols) / count_rows
        )
    step_rows = jnp.sum(take(6), axis=1).reshape(-1)
    weight_rows = jnp.sum(take(7), axis=1).reshape(-1)
    weight_totals = jnp.sum(take(8), axis=(0, 1))
    updates = []
    for i in range(3):
        second = rows_new[i][:, None] * cols_new[i][None, :] / row_means[i]
        updates.append(gradients[i] * lax.rsqrt(second))
    flat = jnp.stack([jnp.sum(update * update) for update in updates])
    flat = jnp.broadcast_to(jnp.pad(flat, (0, 5))[:, None], (8, LANES))
    totals = jnp.sum(gather_blocks(flat, dp_count, fsdp_count)[:, :, :, 0], axis=(0, 1))
    new_weights = []
    for i in range(3):
        clip_factor = jnp.maximum(1.0, jnp.sqrt(totals[i] / entries[i]) / CLIP_LIMIT)
        step_size = STEP_RATE * jnp.maximum(EPS_TWO, jnp.sqrt(weight_totals[i] / entries[i]))
        new_weights.append(weights_old[i] - step_size / clip_factor * updates[i])
    bias_rows = FF // D
    row_places = jnp.arange(VEC)
    counts = jnp.where(row_places < bias_rows, float(FF), float(D))
    grouped_updates = jnp.where(row_places < bias_rows, jnp.sum(step_rows[:bias_rows]), step_rows)
    grouped_weights = jnp.where(row_places < bias_rows, jnp.sum(weight_rows[:bias_rows]), weight_rows)
    clip_rows = jnp.maximum(1.0, jnp.sqrt(grouped_updates / counts) / CLIP_LIMIT)
    step_sizes = STEP_RATE * jnp.maximum(EPS_TWO, jnp.sqrt(grouped_weights / counts))
    factor_rows = lax.dynamic_slice_in_dim(step_sizes / clip_rows, dp_place * rows_v, rows_v)
    vectors_new = vectors - factor_rows[:, None] * vector_step
    return (
        block_out,
        input_grad,
        attn_grad,
        in_grad,
        out_grad,
        vector_grad,
        rows_new[0],
        cols_new[0],
        rows_new[1],
        cols_new[1],
        rows_new[2],
        cols_new[2],
        moment_new,
        new_weights[0],
        new_weights[1],
        new_weights[2],
        vectors_new,
    )


def solution(mesh):
    split = P(("dp", "fsdp"), None)
    block = P("dp", "fsdp")
    stats = (P("dp"), P("fsdp")) * 3
    return jax.shard_map(
        body,
        mesh=mesh,
        in_specs=(split,) * 3 + (block,) * 4 + stats + (block,),
        out_specs=(split,) * 2 + (block,) * 4 + stats + (block,) * 5,
        check_vma=False,
    )
```

```python
import functools
import math

import jax
import jax.numpy as jnp
import numpy as np
from jax import lax
from jax.experimental import pallas as pl
from jax.experimental.pallas import tpu as pltpu
from jax.sharding import PartitionSpec as P

D = 256
FF = 2048
HEADS = 8
HEAD_DIM = 32
SEQ = 1024
HALF = 512
GROUP = 4
LANES = 128
QBLOCK = 256
WGRID = 32
STEP = 10
VEC = 16
TILE = 512
CHUNK = 512
VDP = 4
VCHIP = 4
VROWS = 16

EPS_NORM = 1e-05
EPS_ONE = 1e-30
EPS_TWO = 0.001
CLIP_LIMIT = 1.0
STEP_RATE = 0.3
FAR = 1e30
SCALE = HEAD_DIM ** (-0.5)
GELU_A = math.sqrt(2.0 / math.pi)
GELU_B = 0.044715
F32 = jnp.float32
BF16 = jnp.bfloat16
VMEM_LIMIT = 56 * 1024 * 1024


def dot(left, right):
    return jnp.dot(left, right, preferred_element_type=F32)


def dot_nt(left, right):
    return lax.dot_general(left, right, (((1,), (1,)), ((), ())), preferred_element_type=F32)


def encode_table():
    half = D // 2
    feature = np.arange(half)
    freq = np.exp(
        (2 * (feature // 2)).astype(np.float32) * np.float32(-math.log(10000.0) / half)
    ).astype(np.float32)
    angles = np.arange(1, WGRID + 1, dtype=np.float32)[:, None] * freq[None, :]
    table = np.where(feature % 2 == 0, np.sin(angles), np.cos(angles)).astype(np.float32)
    low = jnp.bfloat16
    one = table.astype(low)
    rest = table - one.astype(np.float32)
    two = rest.astype(low)
    three = (rest - two.astype(np.float32)).astype(low)
    blank = np.zeros((LANES - 3 * WGRID, half), low)
    return np.concatenate([one, two, three, blank], axis=0)


def iota(shape, dim):
    return lax.broadcasted_iota(jnp.int32, shape, dim)


def norm_forward(rows):
    centered = rows - jnp.mean(rows, axis=-1, keepdims=True)
    inverse = lax.rsqrt(jnp.mean(centered * centered, axis=-1, keepdims=True) + EPS_NORM)
    return centered * inverse, inverse


def norm_backward(upstream, normed, inverse):
    return inverse * (
        upstream
        - jnp.mean(upstream, axis=-1, keepdims=True)
        - normed * jnp.mean(upstream * normed, axis=-1, keepdims=True)
    )

def vspec():
    return pl.BlockSpec(memory_space=pltpu.VMEM)


def params(**more):
    return pltpu.CompilerParams(vmem_limit_bytes=VMEM_LIMIT, **more)


def pack_kernel(place, attn_ref, first_ref, second_ref, vector_ref, attn_out, ffn_out):
    owner = place[1] * 2 + place[2]
    vector = vector_ref[...]
    rows = vector.shape[0]
    wide = jnp.concatenate([vector] * (LANES // vector.shape[1]), axis=1)
    slot = iota((rows, LANES), 1) // vector.shape[1]
    per = LANES // vector.shape[1]
    parts = [attn_ref[...]]
    for half in range(2):
        parts.append(jnp.where(slot + half * per == owner, wide, 0.0))
    parts.append(jnp.zeros((VROWS - 2 * rows, LANES), F32))
    piece = jnp.concatenate(parts, axis=0).astype(BF16)
    first = first_ref[...].astype(BF16)
    second = second_ref[...].astype(BF16)
    for at in range(VDP * VCHIP):
        attn_out[at] = piece
        ffn_out[at, 0] = first
        ffn_out[at, 1] = second


def pack(place, attn_weight, ffn_in, ffn_out, vectors):
    count = VDP * VCHIP
    return pl.pallas_call(
        pack_kernel,
        out_shape=(
            jax.ShapeDtypeStruct((count, attn_weight.shape[0] + VROWS, LANES), BF16),
            jax.ShapeDtypeStruct((count, 2) + ffn_in.shape, BF16),
        ),
        in_specs=[pl.BlockSpec(memory_space=pltpu.SMEM)] + [vspec()] * 4,
        out_specs=(vspec(), vspec()),
        compiler_params=params(),
        name="pack",
    )(place, attn_weight, ffn_in, ffn_out, vectors)


def place_kernel(segment_ref, tokens_ref, table_ref, qk_ref, x_ref, marks_ref):
    row = pl.program_id(0)
    starts = []
    for number in range(1, 4):
        at = jnp.int32(0)
        for step in (512, 256, 128, 64, 32, 16, 8, 4, 2, 1, 1):
            probe = jnp.minimum(at + (step - 1), SEQ - 1)
            at = jnp.where(segment_ref[row, probe] < number, at + step, at)
        starts.append(at)
    edges = [jnp.int32(0)] + starts + [jnp.int32(SEQ)]
    begin = jnp.int32(0)
    for number in range(3, -1, -1):
        begin = jnp.where(edges[number + 1] - edges[number] == HALF, edges[number], begin)
    for number in range(3):
        marks_ref[row, number] = starts[number]
    marks_ref[row, 3] = begin
    one, two, three = starts
    x = pltpu.roll(tokens_ref[...].astype(F32), (SEQ - begin) & (SEQ - 1), 0)
    x_ref[...] = x.astype(BF16)
    at = (iota((SEQ, LANES), 0) + begin) & (SEQ - 1)
    lane = iota((SEQ, LANES), 1)
    start = jnp.where(at >= three, three, jnp.where(at >= two, two, jnp.where(at >= one, one, 0)))
    local = at - start
    kept = lane < 3 * WGRID
    slot = lane & (WGRID - 1)
    hot_r = jnp.where(((local >> 5) == slot) & kept, 1.0, 0.0).astype(BF16)
    hot_c = jnp.where(((local & (WGRID - 1)) == slot) & kept, 1.0, 0.0).astype(BF16)
    table = table_ref[...]
    places = jnp.concatenate([dot(hot_r, table), dot(hot_c, table)], axis=1)
    qk_ref[...] = (x + places).astype(BF16)


def place_tokens(segment_ids, tokens, table):
    rows = segment_ids.shape[0]
    by_row = lambda r: (r, 0)
    return pl.pallas_call(
        place_kernel,
        out_shape=(
            jax.ShapeDtypeStruct(tokens.shape, BF16),
            jax.ShapeDtypeStruct(tokens.shape, BF16),
            jax.ShapeDtypeStruct((rows, 4), jnp.int32),
        ),
        grid=(rows,),
        in_specs=[
            pl.BlockSpec(memory_space=pltpu.SMEM),
            pl.BlockSpec((SEQ, D), by_row),
            pl.BlockSpec((LANES, LANES), lambda r: (0, 0)),
        ],
        out_specs=(
            pl.BlockSpec((SEQ, D), by_row),
            pl.BlockSpec((SEQ, D), by_row),
            pl.BlockSpec(memory_space=pltpu.SMEM),
        ),
        compiler_params=params(dimension_semantics=("arbitrary",)),
        cost_estimate=pl.CostEstimate(flops=600_000_000, bytes_accessed=4_000_000, transcendentals=0),
        name="place_tokens",
    )(segment_ids, tokens, table)


def attend_kernel(
    marks,
    place,
    x_ref,
    qk_ref,
    mine_ref,
    other_ref,
    query_ref,
    value_ref,
    key_t_ref,
    out_t_ref,
    inverse_ref,
    mixed_ref,
    exps_ref,
    weight_ref,
    proj_ref,
    vector_ref,
    key_s,
    value_s,
    mark_k,
    mark_q,
):
    row = pl.program_id(0)
    group = pl.program_id(1)
    begin = marks[row, 3]
    core = place[2]

    @pl.when((row == 0) & (group == 0))
    def _():
        tall = D // VDP
        for d in range(VDP):
            rows = slice(d * tall, (d + 1) * tall)
            total = jnp.zeros((8, LANES), F32)
            for c in range(VCHIP):
                for ref, half in ((mine_ref, core), (other_ref, 1 - core)):
                    if c < 3:
                        to = pl.ds(pl.multiple_of(c * D + half * LANES, LANES), LANES)
                        weight_ref[rows, to] = ref[d, c, :tall, :]
                    else:
                        to = pl.ds(pl.multiple_of(half * LANES, LANES), LANES)
                        proj_ref[rows, to] = ref[d, c, :tall, :]
                    total += ref[d, c, tall : tall + 8, :].astype(F32)
            vector_ref[d * 4 : (d + 1) * 4, :LANES] = total[:4]
            vector_ref[d * 4 : (d + 1) * 4, LANES:] = total[4:]

    @pl.when(group == 0)
    def _():
        x_low = x_ref[...]
        qk = qk_ref[...]
        bias_q = vector_ref[8:9, :]
        bias_v = vector_ref[9:10, :]
        query = (dot(qk, weight_ref[:, :D]) + bias_q) * SCALE
        query_ref[...] = query.astype(BF16)
        key = dot(qk, weight_ref[:, D : 2 * D])
        key_s[...] = key.astype(BF16)
        key_t_ref[...] = key.T.astype(BF16)
        value = dot(x_low, weight_ref[:, 2 * D : 3 * D]) + bias_v
        value_ref[...] = value.astype(BF16)
        value_t = value.T.astype(BF16)
        for head in range(HEADS):
            value_s[head, :HEAD_DIM, :] = value_t[head * HEAD_DIM : (head + 1) * HEAD_DIM, :]
            value_s[head, HEAD_DIM:, :] = jnp.ones((16, SEQ), BF16)
        one, two, three = marks[row, 0], marks[row, 1], marks[row, 2]
        here = (iota((HALF, LANES), 0) + (HALF + begin)) & (SEQ - 1)
        number = (
            jnp.where(here >= one, 1, 0)
            + jnp.where(here >= two, 1, 0)
            + jnp.where(here >= three, 1, 0)
        )
        lane = iota((HALF, LANES), 1)
        mark_q[...] = jnp.where(number == lane, 1.0, 0.0).astype(BF16)
        mark_k[...] = jnp.where((number != lane) & (lane < 4), -FAR, 0.0).astype(BF16)

    lanes = pl.ds(pl.multiple_of(group * LANES, LANES), LANES)
    head_of = iota((1, LANES), 1) // HEAD_DIM

    def scores_of(item):
        half, at_head, block = item
        mask = jnp.where(head_of == at_head, 1.0, 0.0).astype(BF16)
        key_m = key_s[half * HALF : (half + 1) * HALF, lanes] * mask
        at = half * HALF + block * QBLOCK
        query = query_ref[at : at + QBLOCK, lanes]
        if half == 1:
            key_m = jnp.concatenate([key_m, mark_k[...]], axis=1)
            query = jnp.concatenate(
                [query, mark_q[block * QBLOCK : (block + 1) * QBLOCK, :]], axis=1
            )
        return dot_nt(key_m, query)

    def exps_of(item, scores):
        half, at_head, block = item
        exps = jnp.exp(scores - jnp.max(scores, axis=0, keepdims=True)).astype(BF16)
        exps_ref[0, at_head, half, :, block * QBLOCK : (block + 1) * QBLOCK] = exps
        return exps

    def finish(item, exps):
        half, at_head, block = item
        at = half * HALF + block * QBLOCK
        rows = slice(half * HALF, (half + 1) * HALF)
        out = dot(value_s[group * GROUP + at_head, :, rows], exps)
        inverse = 1.0 / out[HEAD_DIM : HEAD_DIM + 1, :]
        inverse_ref[0, at_head : at_head + 1, at : at + QBLOCK] = inverse
        out_t_ref[at_head * HEAD_DIM : (at_head + 1) * HEAD_DIM, at : at + QBLOCK] = (
            out[:HEAD_DIM, :] * inverse
        )

    items = [
        (half, at_head, block)
        for half in range(2)
        for at_head in range(GROUP)
        for block in range(HALF // QBLOCK)
    ]
    scores, exps = {}, {}
    for i in range(len(items) + 2):
        if i < len(items):
            scores[i] = scores_of(items[i])
        if 1 <= i <= len(items):
            exps[i - 1] = exps_of(items[i - 1], scores.pop(i - 1))
        if i >= 2:
            finish(items[i - 2], exps.pop(i - 2))
    mixed_ref[...] = pltpu.roll(out_t_ref[...].T, begin, 0).astype(BF16)


def attend_forward(marks, place, x, qk, mine, other):
    total = x.shape[0]
    rows = total // SEQ
    by_row = lambda r, g, m, p: (r, 0)
    by_col = lambda r, g, m, p: (0, r)
    whole = lambda r, g, m, p: (0, 0)
    whole4 = lambda r, g, m, p: (0, 0, 0, 0)
    return pl.pallas_call(
        attend_kernel,
        out_shape=(
            jax.ShapeDtypeStruct((total, D), BF16),
            jax.ShapeDtypeStruct((total, D), BF16),
            jax.ShapeDtypeStruct((D, total), BF16),
            jax.ShapeDtypeStruct((D, total), F32),
            jax.ShapeDtypeStruct((2, 8, total), F32),
            jax.ShapeDtypeStruct((total, D), BF16),
            jax.ShapeDtypeStruct((rows, HEADS, 2, HALF, HALF), BF16),
            jax.ShapeDtypeStruct((D, 3 * D), BF16),
            jax.ShapeDtypeStruct((D, D), BF16),
            jax.ShapeDtypeStruct((VEC, D), F32),
        ),
        grid_spec=pltpu.PrefetchScalarGridSpec(
            num_scalar_prefetch=2,
            grid=(rows, 2),
            in_specs=[
                pl.BlockSpec((SEQ, D), by_row),
                pl.BlockSpec((SEQ, D), by_row),
                pl.BlockSpec(mine.shape, whole4),
                pl.BlockSpec(other.shape, whole4),
            ],
            out_specs=[
                pl.BlockSpec((SEQ, D), by_row),
                pl.BlockSpec((SEQ, D), by_row),
                pl.BlockSpec((D, SEQ), by_col),
                pl.BlockSpec((LANES, SEQ), lambda r, g, m, p: (g, r)),
                pl.BlockSpec((1, 8, SEQ), lambda r, g, m, p: (g, 0, r)),
                pl.BlockSpec((SEQ, LANES), lambda r, g, m, p: (r, g)),
                pl.BlockSpec((1, GROUP, 2, HALF, HALF), lambda r, g, m, p: (r, g, 0, 0, 0)),
                pl.BlockSpec((D, 3 * D), whole),
                pl.BlockSpec((D, D), whole),
                pl.BlockSpec((VEC, D), whole),
            ],
            scratch_shapes=[
                pltpu.VMEM((SEQ, D), BF16),
                pltpu.VMEM((HEADS, HEAD_DIM + 16, SEQ), BF16),
                pltpu.VMEM((HALF, LANES), BF16),
                pltpu.VMEM((HALF, LANES), BF16),
            ],
        ),
        compiler_params=params(dimension_semantics=("arbitrary", "arbitrary")),
        cost_estimate=pl.CostEstimate(
            flops=20_000_000_000, bytes_accessed=30_000_000, transcendentals=8_400_000
        ),
        name="attend_forward",
    )(marks, place, x, qk, mine, other)


def feed_kernel(
    place,
    tokens_ref,
    cotangent_ref,
    mixed_ref,
    proj_ref,
    mine_ref,
    other_ref,
    vector_ref,
    block_ref,
    resid_ref,
    mixed_grad_ref,
    mine_out,
    other_out,
    proj_out,
    vector_out,
    first_w,
    second_w,
    first_acc,
    second_acc,
    proj_acc,
    vector_acc,
    hidden_s,
    slope_s,
):
    step = pl.program_id(0)
    core = place[2]
    tall = D // VDP
    wide = FF // (2 * VCHIP)

    @pl.when(step == 0)
    def _():
        first_acc[...] = jnp.zeros_like(first_acc)
        second_acc[...] = jnp.zeros_like(second_acc)
        proj_acc[...] = jnp.zeros_like(proj_acc)
        vector_acc[...] = jnp.zeros_like(vector_acc)
        for d in range(VDP):
            rows = slice(d * tall, (d + 1) * tall)
            for c in range(VCHIP):
                for ref, half in ((mine_ref, core), (other_ref, 1 - core)):
                    to = pl.ds(pl.multiple_of((2 * c + half) * wide, wide), wide)
                    first_w[rows, to] = ref[d, c, 0]
                    second_w[rows, to] = ref[d, c, 1]

    bias_o, bias_2 = vector_ref[10:11, :], vector_ref[11:12, :]
    gain_1, shift_1 = vector_ref[12:13, :], vector_ref[13:14, :]
    gain_2, shift_2 = vector_ref[14:15, :], vector_ref[15:16, :]
    mixed = mixed_ref[...]
    attended = dot(mixed, proj_ref[...]) + bias_o
    norm_1, inverse_1 = norm_forward(tokens_ref[...].astype(F32) + attended)
    first = norm_1 * gain_1 + shift_1
    first_low = first.astype(BF16)
    per = CHUNK // D
    chunks = FF // CHUNK

    def columns(at):
        return slice(at * CHUNK, (at + 1) * CHUNK)

    def pre_of(at):
        bias = jnp.concatenate(
            [vector_ref[at * per + i : at * per + i + 1, :] for i in range(per)], axis=1
        )
        return dot(first_low, first_w[:, columns(at)]) + bias

    def hidden_of(at, pre):
        square = pre * pre
        inner = pre * (GELU_A + (GELU_A * GELU_B) * square)
        gate = 0.5 + 0.5 * jnp.tanh(inner)
        hidden = (pre * gate).astype(BF16)
        hidden_s[:, columns(at)] = hidden
        rise = (2.0 * GELU_A) + (6.0 * GELU_A * GELU_B) * square
        slope_s[:, columns(at)] = gate + (gate - gate * gate) * (pre * rise)
        return hidden

    branch = jnp.zeros((TILE, D), F32)
    pres, hiddens = {}, {}
    for i in range(chunks + 2):
        if i < chunks:
            pres[i] = pre_of(i)
        if 1 <= i <= chunks:
            hiddens[i - 1] = hidden_of(i - 1, pres.pop(i - 1))
        if i >= 2:
            branch += dot_nt(hiddens.pop(i - 2), second_w[:, columns(i - 2)])
    norm_2, inverse_2 = norm_forward(first + (branch + bias_2))
    block_ref[...] = norm_2 * gain_2 + shift_2
    back = cotangent_ref[...].astype(F32)
    vector_acc[14:15, :] += jnp.sum(back * norm_2, axis=0, keepdims=True)
    vector_acc[15:16, :] += jnp.sum(back, axis=0, keepdims=True)
    resid_2 = norm_backward(back * gain_2, norm_2, inverse_2)
    branch_low = resid_2.astype(BF16)
    branch_f = branch_low.astype(F32)
    vector_acc[11:12, :] += jnp.sum(branch_f, axis=0, keepdims=True)
    branch_t = branch_f.T.astype(BF16)
    first_t = first_low.astype(F32).T.astype(BF16)
    first_back = resid_2

    def pre_grad_of(at, hidden_grad):
        pre_low = (hidden_grad * slope_s[:, columns(at)]).astype(BF16)
        sums = jnp.sum(pre_low.astype(F32), axis=0, keepdims=True)
        for i in range(per):
            vector_acc[at * per + i : at * per + i + 1, :] += sums[:, i * D : (i + 1) * D]
        return pre_low

    pulls, grads = {}, {}
    for i in range(chunks + 2):
        if i < chunks:
            pulls[i] = dot(branch_low, second_w[:, columns(i)])
            second_acc[:, columns(i)] += dot(branch_t, hidden_s[:, columns(i)])
        if 1 <= i <= chunks:
            grads[i - 1] = pre_grad_of(i - 1, pulls.pop(i - 1))
        if i >= 2:
            pre_low = grads.pop(i - 2)
            first_acc[:, columns(i - 2)] += dot(first_t, pre_low)
            first_back += dot_nt(pre_low, first_w[:, columns(i - 2)])
    vector_acc[12:13, :] += jnp.sum(first_back * norm_1, axis=0, keepdims=True)
    vector_acc[13:14, :] += jnp.sum(first_back, axis=0, keepdims=True)
    resid_1 = norm_backward(first_back * gain_1, norm_1, inverse_1)
    resid_ref[...] = resid_1
    attended_low = resid_1.astype(BF16)
    vector_acc[10:11, :] += jnp.sum(attended_low.astype(F32), axis=0, keepdims=True)
    mixed_t = mixed.astype(F32).T.astype(BF16)
    proj_acc[...] += dot(mixed_t, attended_low)
    mixed_grad_ref[...] = dot_nt(attended_low, proj_ref[...]).astype(BF16)

    @pl.when(step == pl.num_programs(0) - 1)
    def _():
        for d in range(VDP):
            rows = slice(d * tall, (d + 1) * tall)
            for c in range(VCHIP):
                for ref, half in ((mine_out, core), (other_out, 1 - core)):
                    to = pl.ds(pl.multiple_of((2 * c + half) * wide, wide), wide)
                    ref[d, c, 0] = first_acc[rows, to].astype(BF16)
                    ref[d, c, 1] = second_acc[rows, to].astype(BF16)
        proj_out[...] = proj_acc[...]
        vector_out[...] = vector_acc[...]


def feed_forward(place, tokens, cotangent, mixed, proj, mine, other, vector):
    total = tokens.shape[0]
    tile = lambda i, p: (i, 0)
    whole = lambda i, p: (0, 0)
    whole5 = lambda i, p: (0, 0, 0, 0, 0)
    return pl.pallas_call(
        feed_kernel,
        out_shape=(
            jax.ShapeDtypeStruct((total, D), F32),
            jax.ShapeDtypeStruct((total, D), F32),
            jax.ShapeDtypeStruct((total, D), BF16),
            jax.ShapeDtypeStruct(mine.shape, BF16),
            jax.ShapeDtypeStruct(mine.shape, BF16),
            jax.ShapeDtypeStruct((D, D), F32),
            jax.ShapeDtypeStruct((VEC, D), F32),
        ),
        grid_spec=pltpu.PrefetchScalarGridSpec(
            num_scalar_prefetch=1,
            grid=(total // TILE,),
            in_specs=[
                pl.BlockSpec((TILE, D), tile),
                pl.BlockSpec((TILE, D), tile),
                pl.BlockSpec((TILE, D), tile),
                pl.BlockSpec((D, D), whole),
                pl.BlockSpec(mine.shape, whole5),
                pl.BlockSpec(mine.shape, whole5),
                pl.BlockSpec((VEC, D), whole),
            ],
            out_specs=[
                pl.BlockSpec((TILE, D), tile),
                pl.BlockSpec((TILE, D), tile),
                pl.BlockSpec((TILE, D), tile),
                pl.BlockSpec(mine.shape, whole5),
                pl.BlockSpec(mine.shape, whole5),
                pl.BlockSpec((D, D), whole),
                pl.BlockSpec((VEC, D), whole),
            ],
            scratch_shapes=[
                pltpu.VMEM((D, FF), BF16),
                pltpu.VMEM((D, FF), BF16),
                pltpu.VMEM((D, FF), F32),
                pltpu.VMEM((D, FF), F32),
                pltpu.VMEM((D, D), F32),
                pltpu.VMEM((VEC, D), F32),
                pltpu.VMEM((TILE, FF), BF16),
                pltpu.VMEM((TILE, FF), F32),
            ],
        ),
        compiler_params=params(dimension_semantics=("arbitrary",)),
        cost_estimate=pl.CostEstimate(
            flops=14_000_000_000, bytes_accessed=15_000_000, transcendentals=4_200_000
        ),
        name="feed_forward",
    )(place, tokens, cotangent, mixed, proj, mine, other, vector)


def pull_kernel(
    own,
    marks,
    place,
    mixed_grad_ref,
    query_ref,
    value_ref,
    key_t_ref,
    out_t_ref,
    inverse_ref,
    exps_ref,
    qk_ref,
    x_ref,
    weight_ref,
    proj_ref,
    *refs,
):
    if own:
        resid_ref, other_ref, pulled_ref, grads_ref, sums_ref, dot_s, query_t_s, acc, sum_acc = refs
    else:
        pulled_ref, grads_ref, sums_ref, dot_s, query_t_s, acc, sum_acc = refs
    row = pl.program_id(0)
    begin = marks[row, 3]
    group = place[2] if own else 1 - place[2]

    @pl.when(row == 0)
    def _():
        acc[...] = jnp.zeros_like(acc)
        sum_acc[...] = jnp.zeros_like(sum_acc)

    grad = pltpu.roll(mixed_grad_ref[...].astype(F32), (SEQ - begin) & (SEQ - 1), 0)
    grad_t = grad.T
    scaled = []
    for at_head in range(GROUP):
        rows = slice(at_head * HEAD_DIM, (at_head + 1) * HEAD_DIM)
        part = grad_t[rows, :] * inverse_ref[0, at_head : at_head + 1, :]
        scaled.append(part)
        dot_s[at_head : at_head + 1, :] = jnp.sum(part * out_t_ref[rows, :], axis=0, keepdims=True)
    scaled_t = jnp.concatenate(scaled, axis=0)
    scaled_low_t = scaled_t.astype(BF16)
    scaled_low = scaled_t.T.astype(BF16)
    head_of = iota((1, LANES), 1) // HEAD_DIM
    masks = [jnp.where(head_of == at_head, 1.0, 0.0).astype(BF16) for at_head in range(GROUP)]
    key_parts = [jnp.zeros((HALF, LANES), F32) for _ in range(2)]
    value_parts = [jnp.zeros((HALF, LANES), F32) for _ in range(2)]

    def pull_of(item):
        half, at_head = item
        rows = slice(half * HALF, (half + 1) * HALF)
        return dot(value_ref[rows, :] * masks[at_head], scaled_low_t[:, rows])

    def score_grad_of(item, weight_grad):
        half, at_head = item
        rows = slice(half * HALF, (half + 1) * HALF)
        exps = exps_ref[0, at_head, half].astype(F32)
        return (exps * (weight_grad - dot_s[at_head : at_head + 1, rows])).astype(BF16)

    def finish(item, score_grad):
        half, at_head = item
        rows = slice(half * HALF, (half + 1) * HALF)
        value_parts[half] += dot(exps_ref[0, at_head, half], scaled_low[rows, :] * masks[at_head])
        key_parts[half] += dot(score_grad, query_ref[rows, :] * masks[at_head])
        heads = slice(at_head * HEAD_DIM, (at_head + 1) * HEAD_DIM)
        query_t_s[heads, rows] = dot(key_t_ref[heads, rows], score_grad)

    items = [(half, at_head) for half in range(2) for at_head in range(GROUP)]
    pulls, score_grads = {}, {}
    for i in range(len(items) + 2):
        if i < len(items):
            pulls[i] = pull_of(items[i])
        if 1 <= i <= len(items):
            score_grads[i - 1] = score_grad_of(items[i - 1], pulls.pop(i - 1))
        if i >= 2:
            finish(items[i - 2], score_grads.pop(i - 2))
    query_low = query_t_s[...].T.astype(BF16)
    key_low = jnp.concatenate(key_parts, axis=0).astype(BF16)
    value_low = jnp.concatenate(value_parts, axis=0).astype(BF16)
    sum_acc[0:1, :] += jnp.sum(query_low.astype(F32), axis=0, keepdims=True) * SCALE
    sum_acc[1:2, :] += jnp.sum(value_low.astype(F32), axis=0, keepdims=True)
    qk_t = qk_ref[...].astype(F32).T.astype(BF16)
    x_t = x_ref[...].astype(F32).T.astype(BF16)
    acc[:, :LANES] += dot(qk_t, query_low) * SCALE
    acc[:, LANES : 2 * LANES] += dot(qk_t, key_low)
    acc[:, 2 * LANES :] += dot(x_t, value_low)
    at = [pl.ds(pl.multiple_of(i * D + group * LANES, LANES), LANES) for i in range(3)]
    pulled = dot_nt(query_low, weight_ref[:, at[0]]) * SCALE + dot_nt(
        jnp.concatenate([key_low, value_low], axis=1),
        jnp.concatenate([weight_ref[:, at[1]], weight_ref[:, at[2]]], axis=1),
    )
    if own:
        pulled_ref[...] = resid_ref[...] + pltpu.roll(pulled + other_ref[...], begin, 0)
    else:
        pulled_ref[...] = pulled

    @pl.when(row == pl.num_programs(0) - 1)
    def _():
        tall = D // VDP
        for d in range(VDP):
            rows = slice(d * tall, (d + 1) * tall)
            for c in range(3):
                grads_ref[d, c] = acc[rows, c * LANES : (c + 1) * LANES].astype(BF16)
            grads_ref[d, 3] = proj_ref[rows, :].astype(BF16)
        sums_ref[...] = sum_acc[...]


def attend_back(own, marks, place, mixed_grad, query, value, key_t, out_t, inverse, exps, qk, x, weight, proj, *more):
    total = query.shape[0]
    rows = total // SEQ
    pick = (lambda p: p[2]) if own else (lambda p: 1 - p[2])
    by_group = lambda r, m, p: (r, pick(p))
    by_row = lambda r, m, p: (r, 0)
    whole = lambda r, m, p: (0, 0)
    in_specs = [
        pl.BlockSpec((SEQ, LANES), by_group),
        pl.BlockSpec((SEQ, LANES), by_group),
        pl.BlockSpec((SEQ, LANES), by_group),
        pl.BlockSpec((LANES, SEQ), lambda r, m, p: (pick(p), r)),
        pl.BlockSpec((LANES, SEQ), lambda r, m, p: (pick(p), r)),
        pl.BlockSpec((1, 8, SEQ), lambda r, m, p: (pick(p), 0, r)),
        pl.BlockSpec((1, GROUP, 2, HALF, HALF), lambda r, m, p: (r, pick(p), 0, 0, 0)),
        pl.BlockSpec((SEQ, D), by_row),
        pl.BlockSpec((SEQ, D), by_row),
        pl.BlockSpec((D, 3 * D), whole),
        pl.BlockSpec((D, LANES), lambda r, m, p: (0, pick(p))),
    ] + [pl.BlockSpec((SEQ, D), by_row)] * len(more)
    return pl.pallas_call(
        functools.partial(pull_kernel, own),
        out_shape=(
            jax.ShapeDtypeStruct((total, D), F32),
            jax.ShapeDtypeStruct((VDP, VCHIP, D // VDP, LANES), BF16),
            jax.ShapeDtypeStruct((8, LANES), F32),
        ),
        grid_spec=pltpu.PrefetchScalarGridSpec(
            num_scalar_prefetch=2,
            grid=(rows,),
            in_specs=in_specs,
            out_specs=[
                pl.BlockSpec((SEQ, D), by_row),
                pl.BlockSpec((VDP, VCHIP, D // VDP, LANES), lambda r, m, p: (0, 0, 0, 0)),
                pl.BlockSpec((8, LANES), whole),
            ],
            scratch_shapes=[
                pltpu.VMEM((8, SEQ), F32),
                pltpu.VMEM((LANES, SEQ), F32),
                pltpu.VMEM((D, 3 * LANES), F32),
                pltpu.VMEM((8, LANES), F32),
            ],
        ),
        compiler_params=params(dimension_semantics=("arbitrary",)),
        cost_estimate=pl.CostEstimate(
            flops=18_000_000_000, bytes_accessed=15_000_000, transcendentals=0
        ),
        name="attend_back",
    )(marks, place, mixed_grad, query, value, key_t, out_t, inverse, exps, qk, x, weight, proj, *more)


def sums_by_group(place, sums_own, sums_other):
    first = place[2] == 0
    return (
        jnp.where(first, sums_own, sums_other),
        jnp.where(first, sums_other, sums_own),
    )


def tail_send_kernel(
    place, mine_ref, got_ref, vector_ref, own_ref, other_ref, ffn_ref, send_ref, grad_ref
):
    tall = D // VDP
    low, high = sums_by_group(place, own_ref[...], other_ref[...])
    vector = jnp.concatenate(
        [
            vector_ref[:8, :],
            jnp.concatenate([low[:2], high[:2]], axis=1),
            vector_ref[10:, :],
        ],
        axis=0,
    )
    rows = VEC // VDP
    for d in range(VDP):
        for c in range(VCHIP):
            at = d * VCHIP + c
            both = mine_ref[d, c].astype(F32) + got_ref[d, c].astype(F32)
            send_ref[at, :tall, :] = both.astype(BF16)
            part = vector[d * rows : (d + 1) * rows, c * 64 : (c + 1) * 64]
            part = jnp.concatenate([part, jnp.zeros((rows, LANES - 64), F32)], axis=1)
            part = jnp.concatenate([part, jnp.zeros((VROWS - rows, LANES), F32)], axis=0)
            send_ref[at, tall:, :] = part.astype(BF16)
    for kind in range(2):
        total = ffn_ref[0, kind].astype(F32)
        for at in range(1, VDP * VCHIP):
            total = total + ffn_ref[at, kind].astype(F32)
        grad_ref[kind] = total


def column_to_row(columns, rows):
    lane = iota((rows, LANES), 1)
    wide = jnp.zeros((rows, LANES), F32)
    for i, column in enumerate(columns):
        wide = jnp.where(lane == i, column, wide)
    return wide.T[:8, :]


def tail_stats_kernel(
    place, got_ref, ffn_grad_ref, attn_ref, first_ref, second_ref, rows_0, rows_1, rows_2, vector_ref, grad_ref, send_ref
):
    tall = attn_ref.shape[0]
    rows = vector_ref.shape[0]
    total = got_ref[0, :tall, :].astype(F32)
    part = got_ref[0, tall : tall + rows, :].astype(F32)
    for at in range(1, got_ref.shape[0]):
        total = total + got_ref[at, :tall, :].astype(F32)
        part = part + got_ref[at, tall : tall + rows, :].astype(F32)
    grad_ref[...] = total
    grads = [total, ffn_grad_ref[0], ffn_grad_ref[1]]
    squares = [grad * grad + EPS_ONE for grad in grads]
    piece = []
    for square in squares:
        down = jnp.sum(square, axis=0, keepdims=True)
        for i in range(down.shape[1] // LANES):
            piece.append(down[:, i * LANES : (i + 1) * LANES])
    across = column_to_row([jnp.sum(square, axis=1, keepdims=True) for square in squares], tall)[:3]
    piece.append(jnp.concatenate([across, jnp.zeros((3, LANES - tall), F32)], axis=1))
    lane = iota((1, LANES), 1)
    scalars = jnp.zeros((1, LANES), F32)
    for i, ref in enumerate((attn_ref, first_ref, second_ref)):
        weight = ref[...]
        down = jnp.sum(weight * weight, axis=0, keepdims=True)
        scalars = jnp.where(lane == i, jnp.sum(down, axis=1, keepdims=True), scalars)
    for i, ref in enumerate((rows_0, rows_1, rows_2)):
        scalars = jnp.where(lane == 3 + i, jnp.sum(ref[...], axis=1, keepdims=True), scalars)
    piece.append(scalars)
    piece.append(jnp.zeros((3, LANES), F32))
    vector = vector_ref[...]
    power = jnp.sum(vector * vector, axis=1, keepdims=True)
    piece.append(jnp.where(iota((rows, LANES), 1) < 64, part, power))
    piece = jnp.concatenate(piece, axis=0)
    for at in range(send_ref.shape[0]):
        send_ref[at] = piece


def tail_update_kernel(
    place,
    got_ref,
    grad_ref,
    ffn_grad_ref,
    rows_0,
    rows_1,
    rows_2,
    cols_0,
    cols_1,
    cols_2,
    moment_ref,
    update_0,
    update_1,
    update_2,
    rows_out,
    cols_out_0,
    cols_out_1,
    cols_out_2,
    vector_grad_ref,
    moment_out,
    step_ref,
    kept_ref,
    send_ref,
):
    decay = 1.0 - STEP ** (-0.8)
    dp, chip, core = place[0], place[1], place[2]
    fsdp = 2 * VCHIP
    tall = grad_ref.shape[0]
    lane = iota((1, LANES), 1)
    mine = jnp.zeros((3, LANES), F32)
    every = jnp.zeros((3, LANES), F32)
    for f in range(fsdp):
        mine = mine + got_ref[pl.ds(dp * fsdp + f, 1), 5:8, :][0]
        for d in range(VDP):
            every = every + got_ref[d * fsdp + f, 5:8, :]
    down = jnp.zeros((5, LANES), F32)
    for d in range(VDP):
        down = down + got_ref[pl.ds(d * fsdp + chip * 2 + core, 1), 0:5, :][0]
    scalars = jnp.zeros((1, LANES), F32)
    olds = jnp.zeros((1, LANES), F32)
    for d in range(VDP):
        olds = olds + got_ref[d * fsdp, 8:9, :]
        for f in range(fsdp):
            scalars = scalars + got_ref[d * fsdp + f, 8:9, :]
    grads = [grad_ref[...], ffn_grad_ref[0], ffn_grad_ref[1]]
    downs = [
        down[0:1],
        jnp.concatenate([down[1:2], down[2:3]], axis=1),
        jnp.concatenate([down[3:4], down[4:5]], axis=1),
    ]
    row_total = tall * VDP
    new_rows, means = [], []
    for i, ref in enumerate((rows_0, rows_1, rows_2)):
        width = grads[i].shape[1] * fsdp
        new_rows.append(decay * ref[...] + (1.0 - decay) * (mine[i : i + 1, :tall] / width))
        old = jnp.sum(jnp.where(lane == 3 + i, olds, 0.0), axis=1, keepdims=True)
        fresh = jnp.sum(every[i : i + 1], axis=1, keepdims=True)
        means.append((decay * old + (1.0 - decay) * (fresh / width)) / row_total)
    tile = jnp.concatenate(new_rows + [jnp.zeros((5, tall), F32)], axis=0)
    rows_out[...] = tile
    tile = jnp.concatenate([tile, jnp.zeros((8, LANES - tall), F32)], axis=1)
    turned = jnp.concatenate([tile, jnp.zeros((LANES - 8, LANES), F32)], axis=0).T
    powers = jnp.zeros((1, LANES), F32)
    for i, (ref, out, to) in enumerate(
        ((cols_0, cols_out_0, update_0), (cols_1, cols_out_1, update_1), (cols_2, cols_out_2, update_2))
    ):
        cols = decay * ref[...] + (1.0 - decay) * (downs[i] / row_total)
        out[...] = cols
        second = turned[:tall, i : i + 1] * cols / means[i]
        update = grads[i] * lax.rsqrt(second)
        to[...] = update
        power = jnp.sum(jnp.sum(update * update, axis=0, keepdims=True), axis=1, keepdims=True)
        powers = jnp.where(lane == i, power, powers)
    rows, width = moment_ref.shape
    pair = dp * fsdp + chip * 2
    both = got_ref[pl.ds(pair, 1), 12 : 12 + rows, :][0] + got_ref[pl.ds(pair + 1, 1), 12 : 12 + rows, :][0]
    vector_grad = jnp.where(core == 0, both[:, :width], both[:, width : 2 * width])
    vector_grad_ref[...] = vector_grad
    moment = decay * moment_ref[...] + (1.0 - decay) * (vector_grad * vector_grad + EPS_ONE)
    moment_out[...] = moment
    step = vector_grad * lax.rsqrt(moment)
    step_ref[...] = step
    weight_rows = jnp.zeros((rows, LANES), F32)
    weight_bias = jnp.zeros((rows, LANES), F32)
    for f in range(fsdp):
        weight_rows = weight_rows + got_ref[pl.ds(dp * fsdp + f, 1), 12 : 12 + rows, :][0]
        for d in range(VDP // 2):
            weight_bias = weight_bias + got_ref[d * fsdp + f, 12 : 12 + rows, :]
    bias = jnp.sum(weight_bias, axis=0, keepdims=True)
    kept_ref[...] = jnp.concatenate([scalars, bias, jnp.zeros((2, LANES), F32), weight_rows], axis=0)
    power = jnp.broadcast_to(jnp.sum(step * step, axis=1, keepdims=True), (rows, LANES))
    piece = jnp.concatenate([powers, jnp.zeros((3, LANES), F32), power], axis=0)
    for at in range(send_ref.shape[0]):
        send_ref[at] = piece


def tail_apply_kernel(
    place,
    got_ref,
    kept_ref,
    update_0,
    update_1,
    update_2,
    weight_0,
    weight_1,
    weight_2,
    step_ref,
    vector_ref,
    new_0,
    new_1,
    new_2,
    vector_out,
):
    dp = place[0]
    fsdp = 2 * VCHIP
    rows = vector_ref.shape[0]
    lane = iota((1, LANES), 1)
    total = got_ref[0]
    for at in range(1, VDP * fsdp):
        total = total + got_ref[at]
    for i, (update, weight, new) in enumerate(
        ((update_0, weight_0, new_0), (update_1, weight_1, new_1), (update_2, weight_2, new_2))
    ):
        entries = float(weight.shape[0] * weight.shape[1] * VDP * fsdp)
        power = jnp.sum(jnp.where(lane == i, total[0:1], 0.0), axis=1, keepdims=True)
        size = jnp.sum(jnp.where(lane == i, kept_ref[0:1, :], 0.0), axis=1, keepdims=True)
        clip = jnp.maximum(1.0, jnp.sqrt(power / entries) / CLIP_LIMIT)
        rate = STEP_RATE * jnp.maximum(EPS_TWO, jnp.sqrt(size / entries))
        new[...] = weight[...] - rate / clip * update[...]
    mine = jnp.zeros((rows, LANES), F32)
    bias = jnp.zeros((rows, LANES), F32)
    for f in range(fsdp):
        mine = mine + got_ref[pl.ds(dp * fsdp + f, 1), 4 : 4 + rows, :][0]
        for d in range(VDP // 2):
            bias = bias + got_ref[d * fsdp + f, 4 : 4 + rows, :]
    is_bias = dp < VDP // 2
    power = jnp.where(is_bias, jnp.sum(bias, axis=0, keepdims=True), mine)[:, 64:65]
    size = jnp.where(is_bias, kept_ref[1:2, :], kept_ref[4 : 4 + rows, :])[:, 64:65]
    count = jnp.where(is_bias, float(FF), float(D))
    clip = jnp.maximum(1.0, jnp.sqrt(power / count) / CLIP_LIMIT)
    rate = STEP_RATE * jnp.maximum(EPS_TWO, jnp.sqrt(size / count))
    vector_out[...] = vector_ref[...] - rate / clip * step_ref[...]


def whole_call(kernel, name, place, outs, *operands):
    return pl.pallas_call(
        kernel,
        out_shape=[jax.ShapeDtypeStruct(shape, kind) for shape, kind in outs],
        in_specs=[pl.BlockSpec(memory_space=pltpu.SMEM)] + [vspec()] * len(operands),
        out_specs=[vspec()] * len(outs),
        compiler_params=params(),
        name=name,
    )(place, *operands)


def core_swap(block):
    return lax.ppermute(block, "core", [(0, 1), (1, 0)])


def exchange(blocks, axes):
    return lax.all_to_all(blocks, axes, split_axis=0, concat_axis=0, tiled=True)


CHIPS = ("dp", "chip")
ALL = ("dp", "chip", "core")


def layer(place, weights, segment_ids, tokens, cotangent, ffn_weights, send_core, send_ffn):
    table = jnp.asarray(encode_table())
    qk, x, marks = place_tokens(segment_ids, tokens, table)
    query, value, key_t, out_t, inverse, mixed, exps, weight, proj, vector = attend_forward(
        marks, place, x, qk, *weights
    )
    ffn_mine, ffn_other = ffn_weights()
    block_out, resid, mixed_grad, ffn_mine, ffn_other, proj_g, vector_g = feed_forward(
        place, tokens, cotangent, mixed, proj, ffn_mine, ffn_other, vector
    )
    ffn_got = send_ffn(ffn_mine, ffn_other)
    shared = (marks, place, mixed_grad, query, value, key_t, out_t, inverse, exps, qk, x, weight, proj_g)
    pulled, grads_other, sums_other = attend_back(False, *shared)
    attn_got = send_core(grads_other)
    input_grad, grads_own, sums_own = attend_back(True, *shared, resid, pulled)
    return block_out, input_grad, grads_own, grads_other, attn_got, sums_own, sums_other, vector_g, ffn_got


def body(
    tokens,
    cotangent,
    segment_ids,
    attn_weight,
    ffn_in,
    ffn_out,
    vectors,
    attn_rows,
    attn_cols,
    in_rows,
    in_cols,
    out_rows,
    out_cols,
    vector_moment,
):
    place = jnp.stack([lax.axis_index("dp"), lax.axis_index("chip"), lax.axis_index("core")])
    place = place.astype(jnp.int32)
    pieces = VDP * VCHIP
    tall, wide = attn_weight.shape
    rows_v, cols_v = vectors.shape
    split = lambda array: array.reshape((VDP, VCHIP) + array.shape[1:])
    attn_sent, ffn_sent = pack(place, attn_weight, ffn_in, ffn_out, vectors)
    attn_mine = split(exchange(attn_sent, CHIPS))
    weights = (attn_mine, core_swap(attn_mine))
    ffn_mine = split(exchange(ffn_sent, CHIPS))

    def ffn_weights():
        return ffn_mine, core_swap(ffn_mine)

    def send_ffn(mine, other):
        both = mine.astype(F32) + core_swap(other).astype(F32)
        both = both.astype(BF16).reshape((pieces,) + mine.shape[2:])
        return exchange(both, CHIPS)

    (
        block_out,
        input_grad,
        grads_own,
        grads_other,
        attn_got,
        sums_own,
        sums_other,
        vector_g,
        ffn_got,
    ) = layer(place, weights, segment_ids, tokens, cotangent, ffn_weights, core_swap, send_ffn)
    sent, ffn_grad = whole_call(
        tail_send_kernel,
        "tail_send",
        place,
        [((pieces, tall + VROWS, LANES), BF16), ((2,) + ffn_in.shape, F32)],
        grads_own,
        attn_got,
        vector_g,
        sums_own,
        sums_other,
        ffn_got,
    )
    got = exchange(sent, CHIPS)
    lay = lambda stat: stat.reshape(1, -1)
    rows_old = (lay(attn_rows), lay(in_rows), lay(out_rows))
    cols_old = (lay(attn_cols), lay(in_cols), lay(out_cols))
    attn_grad, sent = whole_call(
        tail_stats_kernel,
        "tail_stats",
        place,
        [(attn_weight.shape, F32), ((2 * pieces, 16, LANES), F32)],
        got,
        ffn_grad,
        attn_weight,
        ffn_in,
        ffn_out,
        *rows_old,
        vectors,
    )
    got = exchange(sent, ALL)
    (
        update_0,
        update_1,
        update_2,
        rows_new,
        cols_new_0,
        cols_new_1,
        cols_new_2,
        vector_grad,
        moment_new,
        step,
        kept,
        sent,
    ) = whole_call(
        tail_update_kernel,
        "tail_update",
        place,
        [
            (attn_weight.shape, F32),
            (ffn_in.shape, F32),
            (ffn_out.shape, F32),
            ((8, tall), F32),
            (cols_old[0].shape, F32),
            (cols_old[1].shape, F32),
            (cols_old[2].shape, F32),
            (vectors.shape, F32),
            (vectors.shape, F32),
            (vectors.shape, F32),
            ((8, LANES), F32),
            ((2 * pieces, 8, LANES), F32),
        ],
        got,
        attn_grad,
        ffn_grad,
        *rows_old,
        *cols_old,
        vector_moment,
    )
    got = exchange(sent, ALL)
    attn_new, in_new, out_new, vectors_new = whole_call(
        tail_apply_kernel,
        "tail_apply",
        place,
        [(attn_weight.shape, F32), (ffn_in.shape, F32), (ffn_out.shape, F32), (vectors.shape, F32)],
        got,
        kept,
        update_0,
        update_1,
        update_2,
        attn_weight,
        ffn_in,
        ffn_out,
        step,
        vectors,
    )
    return (
        block_out,
        input_grad,
        attn_grad,
        ffn_grad[0],
        ffn_grad[1],
        vector_grad,
        rows_new[0],
        cols_new_0.reshape(-1),
        rows_new[1],
        cols_new_1.reshape(-1),
        rows_new[2],
        cols_new_2.reshape(-1),
        moment_new,
        attn_new,
        in_new,
        out_new,
        vectors_new,
    )


def gather_all(block):
    shape = (lax.axis_size("dp"), lax.axis_size("chip") * 2)
    count = shape[0] * shape[1]
    got = exchange(jnp.broadcast_to(block[None], (count,) + block.shape), ALL)
    return got.reshape(shape + block.shape)


def unblock(parts):
    dp_count, fsdp_count, rows, cols = parts.shape
    return parts.transpose(0, 2, 1, 3).reshape(dp_count * rows, fsdp_count * cols)


def scatter_sum(full):
    dp_count = lax.axis_size("dp")
    fsdp_count = lax.axis_size("chip") * 2
    rows, cols = full.shape
    by_col = full.astype(BF16).reshape(rows, fsdp_count, cols // fsdp_count).transpose(1, 0, 2)
    got = exchange(by_col, ("chip", "core"))
    part = jnp.sum(got.astype(F32), axis=0).astype(BF16)
    by_row = part.reshape(dp_count, rows // dp_count, cols // fsdp_count)
    return jnp.sum(exchange(by_row, "dp").astype(F32), axis=0)


def body_any(
    tokens,
    cotangent,
    segment_ids,
    attn_weight,
    ffn_in,
    ffn_out,
    vectors,
    attn_rows,
    attn_cols,
    in_rows,
    in_cols,
    out_rows,
    out_cols,
    vector_moment,
):
    dp_count = lax.axis_size("dp")
    fsdp_count = lax.axis_size("chip") * 2
    dp_place = lax.axis_index("dp")
    fsdp_place = lax.axis_index("chip") * 2 + lax.axis_index("core")
    rows_w = attn_weight.shape[0]
    rows_v = vectors.shape[0]
    place = jnp.zeros((3,), jnp.int32)
    full_attn = unblock(gather_all(attn_weight.astype(BF16)))
    full_vector = unblock(gather_all(vectors.astype(BF16)))
    full_ffn = jnp.stack(
        [unblock(gather_all(ffn_in.astype(BF16))), unblock(gather_all(ffn_out.astype(BF16)))]
    )
    tall = D // VDP
    cut = full_attn.reshape(VDP, tall, VCHIP, 2, LANES).transpose(3, 0, 2, 1, 4)
    lines = full_vector.reshape(VDP, VEC // VDP, 2, LANES).transpose(0, 2, 1, 3)
    lines = lines.reshape(VDP, 1, 2 * VEC // VDP, LANES)
    lines = jnp.pad(lines, ((0, 0), (0, VCHIP - 1), (0, VROWS - 2 * VEC // VDP), (0, 0)))
    weights = (
        jnp.concatenate([cut[0], lines], axis=2),
        jnp.concatenate([cut[1], jnp.zeros_like(lines)], axis=2),
    )
    ffn_cut = full_ffn.reshape(2, VDP, tall, VCHIP, 2, FF // (2 * VCHIP))
    ffn_cut = ffn_cut.transpose(4, 1, 3, 0, 2, 5)
    (
        block_out,
        input_grad,
        grads_own,
        grads_other,
        _,
        sums_own,
        sums_other,
        vector_g,
        ffn_got,
    ) = layer(
        place,
        weights,
        segment_ids,
        tokens,
        cotangent,
        lambda: (ffn_cut[0], ffn_cut[1]),
        lambda block: block,
        lambda mine, other: jnp.stack([mine, other]),
    )
    attn_full = jnp.stack([grads_own, grads_other]).transpose(1, 3, 2, 0, 4).reshape(D, 4 * D)
    ffn_full = ffn_got.transpose(3, 1, 4, 2, 0, 5).reshape(2, D, FF)
    sums = jnp.concatenate([sums_own[:2], sums_other[:2]], axis=1)
    vector_full = jnp.concatenate([vector_g[:8], sums, vector_g[10:]], axis=0)
    attn_grad = scatter_sum(attn_full)
    in_grad = scatter_sum(ffn_full[0])
    out_grad = scatter_sum(ffn_full[1])
    vector_grad = scatter_sum(vector_full)

    decay = 1.0 - STEP ** (-0.8)
    gradients = (attn_grad, in_grad, out_grad)
    weights_old = (attn_weight, ffn_in, ffn_out)
    rows_old = (attn_rows, in_rows, out_rows)
    cols_old = (attn_cols, in_cols, out_cols)
    moment_new = decay * vector_moment + (1.0 - decay) * (vector_grad * vector_grad + EPS_ONE)
    vector_step = vector_grad * lax.rsqrt(moment_new)
    squares = [gradient * gradient + EPS_ONE for gradient in gradients]
    pieces = []
    for square in squares:
        pieces.append(jnp.sum(square, axis=1))
    for square in squares:
        pieces.append(jnp.sum(square, axis=0))
    pieces.append(jnp.sum(vector_step * vector_step, axis=1))
    pieces.append(jnp.sum(vectors * vectors, axis=1))
    pieces.append(jnp.stack([jnp.sum(weight * weight) for weight in weights_old]))
    pieces.append(jnp.stack([jnp.sum(old) for old in rows_old]))
    sizes = [piece.shape[0] for piece in pieces]
    flat = jnp.concatenate(pieces)
    flat = jnp.pad(flat, (0, -flat.shape[0] % 1024)).reshape(-1, LANES)
    got = gather_all(flat).reshape(dp_count, fsdp_count, -1)
    offsets = [0]
    for length in sizes:
        offsets.append(offsets[-1] + length)
    take = lambda i: got[:, :, offsets[i] : offsets[i + 1]]
    rows_new, cols_new, row_means, entries = [], [], [], []
    for i in range(3):
        count_rows = rows_w * dp_count
        count_cols = weights_old[i].shape[1] * fsdp_count
        entries.append(float(count_rows * count_cols))
        row_all = jnp.sum(take(i), axis=1)
        mine = lax.dynamic_index_in_dim(row_all, dp_place, 0, keepdims=False)
        rows_new.append(decay * rows_old[i] + (1.0 - decay) * mine / count_cols)
        col_all = jnp.sum(take(3 + i), axis=0)
        mine = lax.dynamic_index_in_dim(col_all, fsdp_place, 0, keepdims=False)
        cols_new.append(decay * cols_old[i] + (1.0 - decay) * mine / count_rows)
        old_total = jnp.sum(take(9)[:, 0, i])
        row_means.append(
            (decay * old_total + (1.0 - decay) * jnp.sum(row_all) / count_cols) / count_rows
        )
    step_rows = jnp.sum(take(6), axis=1).reshape(-1)
    weight_rows = jnp.sum(take(7), axis=1).reshape(-1)
    weight_totals = jnp.sum(take(8), axis=(0, 1))
    updates = []
    for i in range(3):
        second = rows_new[i][:, None] * cols_new[i][None, :] / row_means[i]
        updates.append(gradients[i] * lax.rsqrt(second))
    flat = jnp.stack([jnp.sum(update * update) for update in updates])
    flat = jnp.broadcast_to(jnp.pad(flat, (0, 5))[:, None], (8, LANES))
    totals = jnp.sum(gather_all(flat)[:, :, :, 0], axis=(0, 1))
    new_weights = []
    for i in range(3):
        clip_factor = jnp.maximum(1.0, jnp.sqrt(totals[i] / entries[i]) / CLIP_LIMIT)
        step_size = STEP_RATE * jnp.maximum(EPS_TWO, jnp.sqrt(weight_totals[i] / entries[i]))
        new_weights.append(weights_old[i] - step_size / clip_factor * updates[i])
    bias_rows = FF // D
    row_places = jnp.arange(VEC)
    counts = jnp.where(row_places < bias_rows, float(FF), float(D))
    grouped_updates = jnp.where(row_places < bias_rows, jnp.sum(step_rows[:bias_rows]), step_rows)
    grouped_weights = jnp.where(row_places < bias_rows, jnp.sum(weight_rows[:bias_rows]), weight_rows)
    clip_rows = jnp.maximum(1.0, jnp.sqrt(grouped_updates / counts) / CLIP_LIMIT)
    step_sizes = STEP_RATE * jnp.maximum(EPS_TWO, jnp.sqrt(grouped_weights / counts))
    factor_rows = lax.dynamic_slice_in_dim(step_sizes / clip_rows, dp_place * rows_v, rows_v)
    vectors_new = vectors - factor_rows[:, None] * vector_step
    return (
        block_out,
        input_grad,
        attn_grad,
        in_grad,
        out_grad,
        vector_grad,
        rows_new[0],
        cols_new[0],
        rows_new[1],
        cols_new[1],
        rows_new[2],
        cols_new[2],
        moment_new,
        new_weights[0],
        new_weights[1],
        new_weights[2],
        vectors_new,
    )


def solution(mesh):
    dp_count, fsdp_count = mesh.shape["dp"], mesh.shape["fsdp"]
    inner = jax.sharding.Mesh(mesh.devices.reshape(dp_count, fsdp_count // 2, 2), ALL)
    fsdp = ("chip", "core")
    split = P(ALL, None)
    block = P("dp", fsdp)
    stats = (P("dp"), P(fsdp)) * 3
    plain = dp_count == VDP and fsdp_count == 2 * VCHIP
    return jax.shard_map(
        body if plain else body_any,
        mesh=inner,
        in_specs=(split,) * 3 + (block,) * 4 + stats + (block,),
        out_specs=(split,) * 2 + (block,) * 4 + stats + (block,) * 5,
        check_vma=False,
    )
```

```python
import functools
import math

import jax
import jax.numpy as jnp
import numpy as np
from jax import lax
from jax.experimental import pallas as pl
from jax.experimental.pallas import tpu as pltpu
from jax.sharding import PartitionSpec as P

D = 256
FF = 2048
HEADS = 8
HEAD_DIM = 32
SEQ = 1024
HALF = 512
GROUP = 4
LANES = 128
QBLOCK = 256
WGRID = 32
STEP = 10
VEC = 16
TILE = 512
CHUNK = 256
STRIP = 64
VDP = 4
VCHIP = 4
VROWS = 16

EPS_NORM = 1e-05
EPS_ONE = 1e-30
EPS_TWO = 0.001
CLIP_LIMIT = 1.0
STEP_RATE = 0.3
FAR = 1e30
SCALE = HEAD_DIM ** (-0.5)
GELU_A = math.sqrt(2.0 / math.pi)
GELU_B = 0.044715
F32 = jnp.float32
BF16 = jnp.bfloat16
VMEM_LIMIT = 56 * 1024 * 1024


def dot(left, right):
    return jnp.dot(left, right, preferred_element_type=F32)


def dot_nt(left, right):
    return lax.dot_general(left, right, (((1,), (1,)), ((), ())), preferred_element_type=F32)


def encode_table():
    half = D // 2
    feature = np.arange(half)
    freq = np.exp(
        (2 * (feature // 2)).astype(np.float32) * np.float32(-math.log(10000.0) / half)
    ).astype(np.float32)
    angles = np.arange(1, WGRID + 1, dtype=np.float32)[:, None] * freq[None, :]
    table = np.where(feature % 2 == 0, np.sin(angles), np.cos(angles)).astype(np.float32)
    low = jnp.bfloat16
    one = table.astype(low)
    rest = table - one.astype(np.float32)
    two = rest.astype(low)
    three = (rest - two.astype(np.float32)).astype(low)
    blank = np.zeros((LANES - 3 * WGRID, half), low)
    return np.concatenate([one, two, three, blank], axis=0)


def iota(shape, dim):
    return lax.broadcasted_iota(jnp.int32, shape, dim)


def norm_forward(rows):
    centered = rows - jnp.mean(rows, axis=-1, keepdims=True)
    inverse = lax.rsqrt(jnp.mean(centered * centered, axis=-1, keepdims=True) + EPS_NORM)
    return centered * inverse, inverse


def norm_backward(upstream, normed, inverse):
    return inverse * (
        upstream
        - jnp.mean(upstream, axis=-1, keepdims=True)
        - normed * jnp.mean(upstream * normed, axis=-1, keepdims=True)
    )

def vspec():
    return pl.BlockSpec(memory_space=pltpu.VMEM)


def params(**more):
    return pltpu.CompilerParams(vmem_limit_bytes=VMEM_LIMIT, **more)


def pack_kernel(place, attn_ref, first_ref, second_ref, vector_ref, attn_out, ffn_out):
    owner = place[1] * 2 + place[2]
    vector = vector_ref[...]
    rows = vector.shape[0]
    wide = jnp.concatenate([vector] * (LANES // vector.shape[1]), axis=1)
    slot = iota((rows, LANES), 1) // vector.shape[1]
    per = LANES // vector.shape[1]
    parts = [attn_ref[...]]
    for half in range(2):
        parts.append(jnp.where(slot + half * per == owner, wide, 0.0))
    parts.append(jnp.zeros((VROWS - 2 * rows, LANES), F32))
    piece = jnp.concatenate(parts, axis=0).astype(BF16)
    first = first_ref[...].astype(BF16)
    second = second_ref[...].astype(BF16)
    for at in range(VDP * VCHIP):
        attn_out[at] = piece
        ffn_out[at, 0] = first
        ffn_out[at, 1] = second


def pack(place, attn_weight, ffn_in, ffn_out, vectors):
    count = VDP * VCHIP
    return pl.pallas_call(
        pack_kernel,
        out_shape=(
            jax.ShapeDtypeStruct((count, attn_weight.shape[0] + VROWS, LANES), BF16),
            jax.ShapeDtypeStruct((count, 2) + ffn_in.shape, BF16),
        ),
        in_specs=[pl.BlockSpec(memory_space=pltpu.SMEM)] + [vspec()] * 4,
        out_specs=(vspec(), vspec()),
        compiler_params=params(),
        name="pack",
    )(place, attn_weight, ffn_in, ffn_out, vectors)


def place_kernel(segment_ref, tokens_ref, table_ref, qk_ref, x_ref, qk_t_ref, x_t_ref, marks_ref):
    row = pl.program_id(0)
    starts = []
    for number in range(1, 4):
        at = jnp.int32(0)
        for step in (512, 256, 128, 64, 32, 16, 8, 4, 2, 1, 1):
            probe = jnp.minimum(at + (step - 1), SEQ - 1)
            at = jnp.where(segment_ref[row, probe] < number, at + step, at)
        starts.append(at)
    edges = [jnp.int32(0)] + starts + [jnp.int32(SEQ)]
    begin = jnp.int32(0)
    for number in range(3, -1, -1):
        begin = jnp.where(edges[number + 1] - edges[number] == HALF, edges[number], begin)
    for number in range(3):
        marks_ref[row, number] = starts[number]
    marks_ref[row, 3] = begin
    one, two, three = starts
    x = pltpu.roll(tokens_ref[...].astype(F32), (SEQ - begin) & (SEQ - 1), 0)
    x_ref[...] = x.astype(BF16)
    x_t_ref[...] = x.T.astype(BF16)
    at = (iota((SEQ, LANES), 0) + begin) & (SEQ - 1)
    lane = iota((SEQ, LANES), 1)
    start = jnp.where(at >= three, three, jnp.where(at >= two, two, jnp.where(at >= one, one, 0)))
    local = at - start
    kept = lane < 3 * WGRID
    slot = lane & (WGRID - 1)
    hot_r = jnp.where(((local >> 5) == slot) & kept, 1.0, 0.0).astype(BF16)
    hot_c = jnp.where(((local & (WGRID - 1)) == slot) & kept, 1.0, 0.0).astype(BF16)
    table = table_ref[...]
    places = jnp.concatenate([dot(hot_r, table), dot(hot_c, table)], axis=1)
    qk = x + places
    qk_ref[...] = qk.astype(BF16)
    qk_t_ref[...] = qk.T.astype(BF16)


def place_tokens(segment_ids, tokens, table):
    rows = segment_ids.shape[0]
    by_row = lambda r: (r, 0)
    return pl.pallas_call(
        place_kernel,
        out_shape=(
            jax.ShapeDtypeStruct(tokens.shape, BF16),
            jax.ShapeDtypeStruct(tokens.shape, BF16),
            jax.ShapeDtypeStruct((D, tokens.shape[0]), BF16),
            jax.ShapeDtypeStruct((D, tokens.shape[0]), BF16),
            jax.ShapeDtypeStruct((rows, 4), jnp.int32),
        ),
        grid=(rows,),
        in_specs=[
            pl.BlockSpec(memory_space=pltpu.SMEM),
            pl.BlockSpec((SEQ, D), by_row),
            pl.BlockSpec((LANES, LANES), lambda r: (0, 0)),
        ],
        out_specs=(
            pl.BlockSpec((SEQ, D), by_row),
            pl.BlockSpec((SEQ, D), by_row),
            pl.BlockSpec((D, SEQ), lambda r: (0, r)),
            pl.BlockSpec((D, SEQ), lambda r: (0, r)),
            pl.BlockSpec(memory_space=pltpu.SMEM),
        ),
        compiler_params=params(dimension_semantics=("arbitrary",)),
        cost_estimate=pl.CostEstimate(flops=600_000_000, bytes_accessed=4_000_000, transcendentals=0),
        name="place_tokens",
    )(segment_ids, tokens, table)


def attend_kernel(
    marks,
    place,
    x_ref,
    qk_ref,
    mine_ref,
    other_ref,
    query_ref,
    value_ref,
    key_t_ref,
    out_t_ref,
    inverse_ref,
    mixed_ref,
    exps_ref,
    weight_ref,
    proj_ref,
    vector_ref,
    key_s,
    value_s,
    mark_k,
    mark_q,
    scores_s,
):
    row = pl.program_id(0)
    group = pl.program_id(1)
    begin = marks[row, 3]
    core = place[2]

    @pl.when((row == 0) & (group == 0))
    def _():
        tall = D // VDP
        for d in range(VDP):
            rows = slice(d * tall, (d + 1) * tall)
            total = jnp.zeros((8, LANES), F32)
            for c in range(VCHIP):
                for ref, half in ((mine_ref, core), (other_ref, 1 - core)):
                    if c < 3:
                        to = pl.ds(pl.multiple_of(c * D + half * LANES, LANES), LANES)
                        weight_ref[rows, to] = ref[d, c, :tall, :]
                    else:
                        to = pl.ds(pl.multiple_of(half * LANES, LANES), LANES)
                        proj_ref[rows, to] = ref[d, c, :tall, :]
                    total += ref[d, c, tall : tall + 8, :].astype(F32)
            vector_ref[d * 4 : (d + 1) * 4, :LANES] = total[:4]
            vector_ref[d * 4 : (d + 1) * 4, LANES:] = total[4:]

    @pl.when(group == 0)
    def _():
        x_low = x_ref[...]
        qk = qk_ref[...]
        bias_q = vector_ref[8:9, :]
        bias_v = vector_ref[9:10, :]
        query = (dot(qk, weight_ref[:, :D]) + bias_q) * SCALE
        query_ref[...] = query.astype(BF16)
        key = dot(qk, weight_ref[:, D : 2 * D])
        key_s[...] = key.astype(BF16)
        key_t_ref[...] = key.T.astype(BF16)
        value = dot(x_low, weight_ref[:, 2 * D : 3 * D]) + bias_v
        value_ref[...] = value.astype(BF16)
        value_t = value.T.astype(BF16)
        for head in range(HEADS):
            value_s[head, :HEAD_DIM, :] = value_t[head * HEAD_DIM : (head + 1) * HEAD_DIM, :]
            value_s[head, HEAD_DIM:, :] = jnp.ones((16, SEQ), BF16)
        one, two, three = marks[row, 0], marks[row, 1], marks[row, 2]
        here = (iota((HALF, LANES), 0) + (HALF + begin)) & (SEQ - 1)
        number = (
            jnp.where(here >= one, 1, 0)
            + jnp.where(here >= two, 1, 0)
            + jnp.where(here >= three, 1, 0)
        )
        lane = iota((HALF, LANES), 1)
        mark_q[...] = jnp.where(number == lane, 1.0, 0.0).astype(BF16)
        mark_k[...] = jnp.where((number != lane) & (lane < 4), -FAR, 0.0).astype(BF16)

    lanes = pl.ds(pl.multiple_of(group * LANES, LANES), LANES)
    head_of = iota((1, LANES), 1) // HEAD_DIM

    def scores_of(item):
        half, at_head, block = item
        mask = jnp.where(head_of == at_head, 1.0, 0.0).astype(BF16)
        key_m = key_s[half * HALF : (half + 1) * HALF, lanes] * mask
        at = half * HALF + block * QBLOCK
        query = query_ref[at : at + QBLOCK, lanes]
        if half == 1:
            key_m = jnp.concatenate([key_m, mark_k[...]], axis=1)
            query = jnp.concatenate(
                [query, mark_q[block * QBLOCK : (block + 1) * QBLOCK, :]], axis=1
            )
        return dot_nt(key_m, query)

    def exps_of(item, slot):
        half, at_head, block = item
        cols = slice(at_head * HALF + block * QBLOCK, at_head * HALF + (block + 1) * QBLOCK)
        largest = scores_s[slot, :STRIP, :]
        for at in range(STRIP, HALF, STRIP):
            largest = jnp.maximum(largest, scores_s[slot, at : at + STRIP, :])
        largest = jnp.max(largest, axis=0, keepdims=True)
        for at in range(0, HALF, STRIP):
            exps = jnp.exp(scores_s[slot, at : at + STRIP, :] - largest)
            exps_ref[0, 0, half, at : at + STRIP, cols] = exps.astype(BF16)

    def finish(item):
        half, at_head, block = item
        at = half * HALF + block * QBLOCK
        rows = slice(half * HALF, (half + 1) * HALF)
        cols = slice(at_head * HALF + block * QBLOCK, at_head * HALF + (block + 1) * QBLOCK)
        out = dot(value_s[group * GROUP + at_head, :, rows], exps_ref[0, 0, half, :, cols])
        inverse = 1.0 / out[HEAD_DIM : HEAD_DIM + 1, :]
        inverse_ref[0, at_head : at_head + 1, at : at + QBLOCK] = inverse
        out_t_ref[at_head * HEAD_DIM : (at_head + 1) * HEAD_DIM, at : at + QBLOCK] = (
            out[:HEAD_DIM, :] * inverse
        )

    items = [
        (half, at_head, block)
        for half in range(2)
        for at_head in range(GROUP)
        for block in range(HALF // QBLOCK)
    ]
    for i in range(len(items) + 2):
        if i < len(items):
            scores_s[i % 2] = scores_of(items[i])
        if 1 <= i <= len(items):
            exps_of(items[i - 1], (i - 1) % 2)
        if i >= 2:
            finish(items[i - 2])
    mixed_ref[...] = pltpu.roll(out_t_ref[...].T, begin, 0).astype(BF16)


def attend_forward(marks, place, x, qk, mine, other):
    total = x.shape[0]
    rows = total // SEQ
    by_row = lambda r, g, m, p: (r, 0)
    by_col = lambda r, g, m, p: (0, r)
    whole = lambda r, g, m, p: (0, 0)
    whole4 = lambda r, g, m, p: (0, 0, 0, 0)
    return pl.pallas_call(
        attend_kernel,
        out_shape=(
            jax.ShapeDtypeStruct((total, D), BF16),
            jax.ShapeDtypeStruct((total, D), BF16),
            jax.ShapeDtypeStruct((D, total), BF16),
            jax.ShapeDtypeStruct((D, total), F32),
            jax.ShapeDtypeStruct((2, 8, total), F32),
            jax.ShapeDtypeStruct((total, D), BF16),
            jax.ShapeDtypeStruct((rows, 2, 2, HALF, GROUP * HALF), BF16),
            jax.ShapeDtypeStruct((D, 3 * D), BF16),
            jax.ShapeDtypeStruct((D, D), BF16),
            jax.ShapeDtypeStruct((VEC, D), F32),
        ),
        grid_spec=pltpu.PrefetchScalarGridSpec(
            num_scalar_prefetch=2,
            grid=(rows, 2),
            in_specs=[
                pl.BlockSpec((SEQ, D), by_row),
                pl.BlockSpec((SEQ, D), by_row),
                pl.BlockSpec(mine.shape, whole4),
                pl.BlockSpec(other.shape, whole4),
            ],
            out_specs=[
                pl.BlockSpec((SEQ, D), by_row),
                pl.BlockSpec((SEQ, D), by_row),
                pl.BlockSpec((D, SEQ), by_col),
                pl.BlockSpec((LANES, SEQ), lambda r, g, m, p: (g, r)),
                pl.BlockSpec((1, 8, SEQ), lambda r, g, m, p: (g, 0, r)),
                pl.BlockSpec((SEQ, LANES), lambda r, g, m, p: (r, g)),
                pl.BlockSpec((1, 1, 2, HALF, GROUP * HALF), lambda r, g, m, p: (r, g, 0, 0, 0)),
                pl.BlockSpec((D, 3 * D), whole),
                pl.BlockSpec((D, D), whole),
                pl.BlockSpec((VEC, D), whole),
            ],
            scratch_shapes=[
                pltpu.VMEM((SEQ, D), BF16),
                pltpu.VMEM((HEADS, HEAD_DIM + 16, SEQ), BF16),
                pltpu.VMEM((HALF, LANES), BF16),
                pltpu.VMEM((HALF, LANES), BF16),
                pltpu.VMEM((2, HALF, QBLOCK), F32),
            ],
        ),
        compiler_params=params(dimension_semantics=("arbitrary", "arbitrary")),
        cost_estimate=pl.CostEstimate(
            flops=20_000_000_000, bytes_accessed=30_000_000, transcendentals=8_400_000
        ),
        name="attend_forward",
    )(marks, place, x, qk, mine, other)


def feed_kernel(
    place,
    tokens_ref,
    cotangent_ref,
    mixed_ref,
    proj_ref,
    mine_ref,
    other_ref,
    vector_ref,
    block_ref,
    resid_ref,
    mixed_grad_ref,
    mine_out,
    other_out,
    proj_out,
    vector_out,
    first_w,
    second_w,
    first_acc,
    second_acc,
    proj_acc,
    vector_acc,
    hidden_s,
    slope_s,
    pre_s,
    work_s,
):
    step = pl.program_id(0)
    core = place[2]
    tall = D // VDP
    wide = FF // (2 * VCHIP)

    @pl.when(step == 0)
    def _():
        first_acc[...] = jnp.zeros_like(first_acc)
        second_acc[...] = jnp.zeros_like(second_acc)
        proj_acc[...] = jnp.zeros_like(proj_acc)
        vector_acc[...] = jnp.zeros_like(vector_acc)
        for d in range(VDP):
            rows = slice(d * tall, (d + 1) * tall)
            for c in range(VCHIP):
                for ref, half in ((mine_ref, core), (other_ref, 1 - core)):
                    to = pl.ds(pl.multiple_of((2 * c + half) * wide, wide), wide)
                    first_w[rows, to] = ref[d, c, 0]
                    second_w[rows, to] = ref[d, c, 1]

    bias_o, bias_2 = vector_ref[10:11, :], vector_ref[11:12, :]
    gain_1, shift_1 = vector_ref[12:13, :], vector_ref[13:14, :]
    gain_2, shift_2 = vector_ref[14:15, :], vector_ref[15:16, :]
    mixed = mixed_ref[...]
    attended = dot(mixed, proj_ref[...]) + bias_o
    norm_1, inverse_1 = norm_forward(tokens_ref[...].astype(F32) + attended)
    first = norm_1 * gain_1 + shift_1
    first_low = first.astype(BF16)
    chunks = FF // CHUNK
    pair = 2

    def columns(at, count=1):
        return slice(at * CHUNK, (at + count) * CHUNK)

    def hidden_of(at, slot):
        bias = vector_ref[at : at + 1, :]
        cols = columns(at)
        for top in range(0, TILE, STRIP):
            rows = slice(top, top + STRIP)
            pre = work_s[slot, rows, :] + bias
            cube = (GELU_A * GELU_B) * (pre * pre)
            gate = 0.5 + 0.5 * jnp.tanh(pre * (cube + GELU_A))
            hidden_s[rows, cols] = (pre * gate).astype(BF16)
            slope_s[rows, cols] = gate + (gate - gate * gate) * (pre * (6.0 * cube + 2.0 * GELU_A))

    branch = jnp.zeros((TILE, D), F32)
    for i in range(chunks + 2):
        if i < chunks:
            work_s[i % 2] = dot(first_low, first_w[:, columns(i)])
        if 1 <= i <= chunks:
            hidden_of(i - 1, (i - 1) % 2)
        if i >= 2 and (i - 2) % pair == pair - 1:
            cols = columns(i - 1 - pair, pair)
            branch += dot_nt(hidden_s[:, cols], second_w[:, cols])
    norm_2, inverse_2 = norm_forward(first + (branch + bias_2))
    block_ref[...] = norm_2 * gain_2 + shift_2
    back = cotangent_ref[...].astype(F32)
    vector_acc[14:15, :] += jnp.sum(back * norm_2, axis=0, keepdims=True)
    vector_acc[15:16, :] += jnp.sum(back, axis=0, keepdims=True)
    resid_2 = norm_backward(back * gain_2, norm_2, inverse_2)
    branch_low = resid_2.astype(BF16)
    branch_f = branch_low.astype(F32)
    vector_acc[11:12, :] += jnp.sum(branch_f, axis=0, keepdims=True)
    branch_t = branch_f.T.astype(BF16)
    first_t = first_low.astype(F32).T.astype(BF16)
    first_back = resid_2

    def pre_grad_of(at, slot):
        cols = columns(at)
        sums = jnp.zeros((STRIP, CHUNK), F32)
        for top in range(0, TILE, STRIP):
            rows = slice(top, top + STRIP)
            pre_low = (work_s[slot, rows, :] * slope_s[rows, cols]).astype(BF16)
            pre_s[rows, cols] = pre_low
            sums = sums + pre_low.astype(F32)
        vector_acc[at : at + 1, :] += jnp.sum(sums, axis=0, keepdims=True)

    for i in range(chunks + 2):
        if i < chunks:
            work_s[i % 2] = dot(branch_low, second_w[:, columns(i)])
            second_acc[:, columns(i)] += dot(branch_t, hidden_s[:, columns(i)])
        if 1 <= i <= chunks:
            pre_grad_of(i - 1, (i - 1) % 2)
        if i >= 2:
            first_acc[:, columns(i - 2)] += dot(first_t, pre_s[:, columns(i - 2)])
        if i >= 2 and (i - 2) % pair == pair - 1:
            cols = columns(i - 1 - pair, pair)
            first_back += dot_nt(pre_s[:, cols], first_w[:, cols])
    vector_acc[12:13, :] += jnp.sum(first_back * norm_1, axis=0, keepdims=True)
    vector_acc[13:14, :] += jnp.sum(first_back, axis=0, keepdims=True)
    resid_1 = norm_backward(first_back * gain_1, norm_1, inverse_1)
    resid_ref[...] = resid_1
    attended_low = resid_1.astype(BF16)
    vector_acc[10:11, :] += jnp.sum(attended_low.astype(F32), axis=0, keepdims=True)
    mixed_t = mixed.astype(F32).T.astype(BF16)
    proj_acc[...] += dot(mixed_t, attended_low)
    mixed_grad_ref[...] = dot_nt(attended_low, proj_ref[...]).astype(BF16)

    @pl.when(step == pl.num_programs(0) - 1)
    def _():
        for d in range(VDP):
            rows = slice(d * tall, (d + 1) * tall)
            for c in range(VCHIP):
                for ref, half in ((mine_out, core), (other_out, 1 - core)):
                    to = pl.ds(pl.multiple_of((2 * c + half) * wide, wide), wide)
                    ref[d, c, 0] = first_acc[rows, to].astype(BF16)
                    ref[d, c, 1] = second_acc[rows, to].astype(BF16)
        proj_out[...] = proj_acc[...]
        vector_out[...] = vector_acc[...]


def feed_forward(place, tokens, cotangent, mixed, proj, mine, other, vector):
    total = tokens.shape[0]
    tile = lambda i, p: (i, 0)
    whole = lambda i, p: (0, 0)
    whole5 = lambda i, p: (0, 0, 0, 0, 0)
    return pl.pallas_call(
        feed_kernel,
        out_shape=(
            jax.ShapeDtypeStruct((total, D), F32),
            jax.ShapeDtypeStruct((total, D), F32),
            jax.ShapeDtypeStruct((total, D), BF16),
            jax.ShapeDtypeStruct(mine.shape, BF16),
            jax.ShapeDtypeStruct(mine.shape, BF16),
            jax.ShapeDtypeStruct((D, D), F32),
            jax.ShapeDtypeStruct((VEC, D), F32),
        ),
        grid_spec=pltpu.PrefetchScalarGridSpec(
            num_scalar_prefetch=1,
            grid=(total // TILE,),
            in_specs=[
                pl.BlockSpec((TILE, D), tile),
                pl.BlockSpec((TILE, D), tile),
                pl.BlockSpec((TILE, D), tile),
                pl.BlockSpec((D, D), whole),
                pl.BlockSpec(mine.shape, whole5),
                pl.BlockSpec(mine.shape, whole5),
                pl.BlockSpec((VEC, D), whole),
            ],
            out_specs=[
                pl.BlockSpec((TILE, D), tile),
                pl.BlockSpec((TILE, D), tile),
                pl.BlockSpec((TILE, D), tile),
                pl.BlockSpec(mine.shape, whole5),
                pl.BlockSpec(mine.shape, whole5),
                pl.BlockSpec((D, D), whole),
                pl.BlockSpec((VEC, D), whole),
            ],
            scratch_shapes=[
                pltpu.VMEM((D, FF), BF16),
                pltpu.VMEM((D, FF), BF16),
                pltpu.VMEM((D, FF), F32),
                pltpu.VMEM((D, FF), F32),
                pltpu.VMEM((D, D), F32),
                pltpu.VMEM((VEC, D), F32),
                pltpu.VMEM((TILE, FF), BF16),
                pltpu.VMEM((TILE, FF), F32),
                pltpu.VMEM((TILE, FF), BF16),
                pltpu.VMEM((2, TILE, CHUNK), F32),
            ],
        ),
        compiler_params=params(dimension_semantics=("arbitrary",)),
        cost_estimate=pl.CostEstimate(
            flops=14_000_000_000, bytes_accessed=15_000_000, transcendentals=4_200_000
        ),
        name="feed_forward",
    )(place, tokens, cotangent, mixed, proj, mine, other, vector)


def pull_kernel(
    own,
    marks,
    place,
    mixed_grad_ref,
    query_ref,
    value_ref,
    key_t_ref,
    out_t_ref,
    inverse_ref,
    exps_ref,
    qk_t_ref,
    x_t_ref,
    weight_ref,
    proj_ref,
    *refs,
):
    if own:
        resid_ref, other_ref, pulled_ref, grads_ref, sums_ref = refs[:5]
    else:
        pulled_ref, grads_ref, sums_ref = refs[:3]
    dot_s, query_t_s, acc, sum_acc, scaled_s, query_s, value_s, scaled_t_s, score_s, work_s = refs[-10:]
    row = pl.program_id(0)
    begin = marks[row, 3]
    group = place[2] if own else 1 - place[2]

    @pl.when(row == 0)
    def _():
        acc[...] = jnp.zeros_like(acc)
        sum_acc[...] = jnp.zeros_like(sum_acc)

    grad = pltpu.roll(mixed_grad_ref[...].astype(F32), (SEQ - begin) & (SEQ - 1), 0)
    grad_t = grad.T
    scaled = []
    for at_head in range(GROUP):
        rows = slice(at_head * HEAD_DIM, (at_head + 1) * HEAD_DIM)
        part = grad_t[rows, :] * inverse_ref[0, at_head : at_head + 1, :]
        scaled.append(part)
        dot_s[at_head : at_head + 1, :] = jnp.sum(part * out_t_ref[rows, :], axis=0, keepdims=True)
    scaled_t = jnp.concatenate(scaled, axis=0)
    scaled_low_t = scaled_t.astype(BF16)
    scaled_low = scaled_t.T.astype(BF16)
    head_of = iota((1, LANES), 1) // HEAD_DIM
    for at_head in range(GROUP):
        mask = jnp.where(head_of == at_head, 1.0, 0.0).astype(BF16)
        for half in range(2):
            rows = slice(half * HALF, (half + 1) * HALF)
            to = slice(at_head * HALF, (at_head + 1) * HALF)
            scaled_s[half, to, :] = scaled_low[rows, :] * mask
            query_s[half, to, :] = query_ref[rows, :] * mask
            value_s[half, to, :] = value_ref[rows, :] * mask
    scaled_t_s[...] = scaled_low_t
    key_parts = [jnp.zeros((HALF, LANES), F32) for _ in range(2)]
    value_parts = [jnp.zeros((HALF, LANES), F32) for _ in range(2)]

    def pull_of(item):
        half, at_head, block = item
        at = half * HALF + block * QBLOCK
        value = value_s[half, at_head * HALF : (at_head + 1) * HALF, :]
        return dot(value, scaled_t_s[:, at : at + QBLOCK])

    def score_grad_of(item, slot):
        half, at_head, block = item
        at = half * HALF + block * QBLOCK
        cols = slice(at_head * HALF + block * QBLOCK, at_head * HALF + (block + 1) * QBLOCK)
        shift = dot_s[at_head : at_head + 1, at : at + QBLOCK]
        for top in range(0, HALF, STRIP):
            rows = slice(top, top + STRIP)
            exps = exps_ref[0, 0, half, rows, cols].astype(F32)
            score_s[half, rows, cols] = (exps * (work_s[slot, rows, :] - shift)).astype(BF16)

    def finish(half, at_head):
        cols = slice(at_head * HALF, (at_head + 2) * HALF)
        rows = slice(half * HALF, (half + 1) * HALF)
        value_parts[half] += dot(exps_ref[0, 0, half, :, cols], scaled_s[half, cols, :])
        key_parts[half] += dot(score_s[half, :, cols], query_s[half, cols, :])
        for head in range(at_head, at_head + 2):
            heads = slice(head * HEAD_DIM, (head + 1) * HEAD_DIM)
            query_t_s[heads, rows] = dot(
                key_t_ref[heads, rows], score_s[half, :, head * HALF : (head + 1) * HALF]
            )

    items = [
        (half, at_head, block)
        for half in range(2)
        for at_head in range(GROUP)
        for block in range(HALF // QBLOCK)
    ]
    for i in range(len(items) + 1):
        if i < len(items):
            work_s[i % 2] = pull_of(items[i])
        if i >= 1:
            score_grad_of(items[i - 1], (i - 1) % 2)
            if i % 4 == 0:
                half, at_head, _ = items[i - 1]
                finish(half, at_head - 1)
    query_low = query_t_s[...].T.astype(BF16)
    key_low = jnp.concatenate(key_parts, axis=0).astype(BF16)
    value_low = jnp.concatenate(value_parts, axis=0).astype(BF16)
    sum_acc[0:1, :] += jnp.sum(query_low.astype(F32), axis=0, keepdims=True) * SCALE
    sum_acc[1:2, :] += jnp.sum(value_low.astype(F32), axis=0, keepdims=True)
    qk_t = qk_t_ref[...]
    x_t = x_t_ref[...]
    acc[:, :LANES] += dot(qk_t, query_low) * SCALE
    acc[:, LANES : 2 * LANES] += dot(qk_t, key_low)
    acc[:, 2 * LANES :] += dot(x_t, value_low)
    at = [pl.ds(pl.multiple_of(i * D + group * LANES, LANES), LANES) for i in range(3)]
    pulled = dot_nt(query_low, weight_ref[:, at[0]]) * SCALE + dot_nt(
        jnp.concatenate([key_low, value_low], axis=1),
        jnp.concatenate([weight_ref[:, at[1]], weight_ref[:, at[2]]], axis=1),
    )
    if own:
        pulled_ref[...] = resid_ref[...] + pltpu.roll(pulled + other_ref[...], begin, 0)
    else:
        pulled_ref[...] = pulled

    @pl.when(row == pl.num_programs(0) - 1)
    def _():
        tall = D // VDP
        for d in range(VDP):
            rows = slice(d * tall, (d + 1) * tall)
            for c in range(3):
                grads_ref[d, c] = acc[rows, c * LANES : (c + 1) * LANES].astype(BF16)
            grads_ref[d, 3] = proj_ref[rows, :].astype(BF16)
        sums_ref[...] = sum_acc[...]


def attend_back(own, marks, place, mixed_grad, query, value, key_t, out_t, inverse, exps, qk_t, x_t, weight, proj, *more):
    total = query.shape[0]
    rows = total // SEQ
    pick = (lambda p: p[2]) if own else (lambda p: 1 - p[2])
    by_group = lambda r, m, p: (r, pick(p))
    by_row = lambda r, m, p: (r, 0)
    whole = lambda r, m, p: (0, 0)
    in_specs = [
        pl.BlockSpec((SEQ, LANES), by_group),
        pl.BlockSpec((SEQ, LANES), by_group),
        pl.BlockSpec((SEQ, LANES), by_group),
        pl.BlockSpec((LANES, SEQ), lambda r, m, p: (pick(p), r)),
        pl.BlockSpec((LANES, SEQ), lambda r, m, p: (pick(p), r)),
        pl.BlockSpec((1, 8, SEQ), lambda r, m, p: (pick(p), 0, r)),
        pl.BlockSpec((1, 1, 2, HALF, GROUP * HALF), lambda r, m, p: (r, pick(p), 0, 0, 0)),
        pl.BlockSpec((D, SEQ), lambda r, m, p: (0, r)),
        pl.BlockSpec((D, SEQ), lambda r, m, p: (0, r)),
        pl.BlockSpec((D, 3 * D), whole),
        pl.BlockSpec((D, LANES), lambda r, m, p: (0, pick(p))),
    ] + [pl.BlockSpec((SEQ, D), by_row)] * len(more)
    return pl.pallas_call(
        functools.partial(pull_kernel, own),
        out_shape=(
            jax.ShapeDtypeStruct((total, D), F32),
            jax.ShapeDtypeStruct((VDP, VCHIP, D // VDP, LANES), BF16),
            jax.ShapeDtypeStruct((8, LANES), F32),
        ),
        grid_spec=pltpu.PrefetchScalarGridSpec(
            num_scalar_prefetch=2,
            grid=(rows,),
            in_specs=in_specs,
            out_specs=[
                pl.BlockSpec((SEQ, D), by_row),
                pl.BlockSpec((VDP, VCHIP, D // VDP, LANES), lambda r, m, p: (0, 0, 0, 0)),
                pl.BlockSpec((8, LANES), whole),
            ],
            scratch_shapes=[
                pltpu.VMEM((8, SEQ), F32),
                pltpu.VMEM((LANES, SEQ), F32),
                pltpu.VMEM((D, 3 * LANES), F32),
                pltpu.VMEM((8, LANES), F32),
                pltpu.VMEM((2, GROUP * HALF, LANES), BF16),
                pltpu.VMEM((2, GROUP * HALF, LANES), BF16),
                pltpu.VMEM((2, GROUP * HALF, LANES), BF16),
                pltpu.VMEM((LANES, SEQ), BF16),
                pltpu.VMEM((2, HALF, GROUP * HALF), BF16),
                pltpu.VMEM((2, HALF, QBLOCK), F32),
            ],
        ),
        compiler_params=params(dimension_semantics=("arbitrary",)),
        cost_estimate=pl.CostEstimate(
            flops=18_000_000_000, bytes_accessed=15_000_000, transcendentals=0
        ),
        name="attend_back",
    )(marks, place, mixed_grad, query, value, key_t, out_t, inverse, exps, qk_t, x_t, weight, proj, *more)


def sums_by_group(place, sums_own, sums_other):
    first = place[2] == 0
    return (
        jnp.where(first, sums_own, sums_other),
        jnp.where(first, sums_other, sums_own),
    )


def tail_send_kernel(
    place, mine_ref, got_ref, vector_ref, own_ref, other_ref, ffn_ref, send_ref, grad_ref
):
    tall = D // VDP
    low, high = sums_by_group(place, own_ref[...], other_ref[...])
    vector = jnp.concatenate(
        [
            vector_ref[:8, :],
            jnp.concatenate([low[:2], high[:2]], axis=1),
            vector_ref[10:, :],
        ],
        axis=0,
    )
    rows = VEC // VDP
    for d in range(VDP):
        for c in range(VCHIP):
            at = d * VCHIP + c
            both = mine_ref[d, c].astype(F32) + got_ref[d, c].astype(F32)
            send_ref[at, :tall, :] = both.astype(BF16)
            part = vector[d * rows : (d + 1) * rows, c * 64 : (c + 1) * 64]
            part = jnp.concatenate([part, jnp.zeros((rows, LANES - 64), F32)], axis=1)
            part = jnp.concatenate([part, jnp.zeros((VROWS - rows, LANES), F32)], axis=0)
            send_ref[at, tall:, :] = part.astype(BF16)
    for kind in range(2):
        total = ffn_ref[0, kind].astype(F32)
        for at in range(1, VDP * VCHIP):
            total = total + ffn_ref[at, kind].astype(F32)
        grad_ref[kind] = total


def column_to_row(columns, rows):
    lane = iota((rows, LANES), 1)
    wide = jnp.zeros((rows, LANES), F32)
    for i, column in enumerate(columns):
        wide = jnp.where(lane == i, column, wide)
    return wide.T[:8, :]


def tail_stats_kernel(
    place, got_ref, ffn_grad_ref, attn_ref, first_ref, second_ref, rows_0, rows_1, rows_2, vector_ref, grad_ref, send_ref
):
    tall = attn_ref.shape[0]
    rows = vector_ref.shape[0]
    total = got_ref[0, :tall, :].astype(F32)
    part = got_ref[0, tall : tall + rows, :].astype(F32)
    for at in range(1, got_ref.shape[0]):
        total = total + got_ref[at, :tall, :].astype(F32)
        part = part + got_ref[at, tall : tall + rows, :].astype(F32)
    grad_ref[...] = total
    grads = [total, ffn_grad_ref[0], ffn_grad_ref[1]]
    squares = [grad * grad + EPS_ONE for grad in grads]
    piece = []
    for square in squares:
        down = jnp.sum(square, axis=0, keepdims=True)
        for i in range(down.shape[1] // LANES):
            piece.append(down[:, i * LANES : (i + 1) * LANES])
    across = column_to_row([jnp.sum(square, axis=1, keepdims=True) for square in squares], tall)[:3]
    piece.append(jnp.concatenate([across, jnp.zeros((3, LANES - tall), F32)], axis=1))
    lane = iota((1, LANES), 1)
    scalars = jnp.zeros((1, LANES), F32)
    for i, ref in enumerate((attn_ref, first_ref, second_ref)):
        weight = ref[...]
        down = jnp.sum(weight * weight, axis=0, keepdims=True)
        scalars = jnp.where(lane == i, jnp.sum(down, axis=1, keepdims=True), scalars)
    for i, ref in enumerate((rows_0, rows_1, rows_2)):
        scalars = jnp.where(lane == 3 + i, jnp.sum(ref[...], axis=1, keepdims=True), scalars)
    piece.append(scalars)
    piece.append(jnp.zeros((3, LANES), F32))
    vector = vector_ref[...]
    power = jnp.sum(vector * vector, axis=1, keepdims=True)
    piece.append(jnp.where(iota((rows, LANES), 1) < 64, part, power))
    piece = jnp.concatenate(piece, axis=0)
    for at in range(send_ref.shape[0]):
        send_ref[at] = piece


def tail_update_kernel(
    place,
    got_ref,
    grad_ref,
    ffn_grad_ref,
    rows_0,
    rows_1,
    rows_2,
    cols_0,
    cols_1,
    cols_2,
    moment_ref,
    update_0,
    update_1,
    update_2,
    rows_out,
    cols_out_0,
    cols_out_1,
    cols_out_2,
    vector_grad_ref,
    moment_out,
    step_ref,
    kept_ref,
    send_ref,
):
    decay = 1.0 - STEP ** (-0.8)
    dp, chip, core = place[0], place[1], place[2]
    fsdp = 2 * VCHIP
    tall = grad_ref.shape[0]
    lane = iota((1, LANES), 1)
    mine = jnp.zeros((3, LANES), F32)
    every = jnp.zeros((3, LANES), F32)
    for f in range(fsdp):
        mine = mine + got_ref[pl.ds(dp * fsdp + f, 1), 5:8, :][0]
        for d in range(VDP):
            every = every + got_ref[d * fsdp + f, 5:8, :]
    down = jnp.zeros((5, LANES), F32)
    for d in range(VDP):
        down = down + got_ref[pl.ds(d * fsdp + chip * 2 + core, 1), 0:5, :][0]
    scalars = jnp.zeros((1, LANES), F32)
    olds = jnp.zeros((1, LANES), F32)
    for d in range(VDP):
        olds = olds + got_ref[d * fsdp, 8:9, :]
        for f in range(fsdp):
            scalars = scalars + got_ref[d * fsdp + f, 8:9, :]
    grads = [grad_ref[...], ffn_grad_ref[0], ffn_grad_ref[1]]
    downs = [
        down[0:1],
        jnp.concatenate([down[1:2], down[2:3]], axis=1),
        jnp.concatenate([down[3:4], down[4:5]], axis=1),
    ]
    row_total = tall * VDP
    new_rows, means = [], []
    for i, ref in enumerate((rows_0, rows_1, rows_2)):
        width = grads[i].shape[1] * fsdp
        new_rows.append(decay * ref[...] + (1.0 - decay) * (mine[i : i + 1, :tall] / width))
        old = jnp.sum(jnp.where(lane == 3 + i, olds, 0.0), axis=1, keepdims=True)
        fresh = jnp.sum(every[i : i + 1], axis=1, keepdims=True)
        means.append((decay * old + (1.0 - decay) * (fresh / width)) / row_total)
    tile = jnp.concatenate(new_rows + [jnp.zeros((5, tall), F32)], axis=0)
    rows_out[...] = tile
    tile = jnp.concatenate([tile, jnp.zeros((8, LANES - tall), F32)], axis=1)
    turned = jnp.concatenate([tile, jnp.zeros((LANES - 8, LANES), F32)], axis=0).T
    powers = jnp.zeros((1, LANES), F32)
    for i, (ref, out, to) in enumerate(
        ((cols_0, cols_out_0, update_0), (cols_1, cols_out_1, update_1), (cols_2, cols_out_2, update_2))
    ):
        cols = decay * ref[...] + (1.0 - decay) * (downs[i] / row_total)
        out[...] = cols
        second = turned[:tall, i : i + 1] * cols / means[i]
        update = grads[i] * lax.rsqrt(second)
        to[...] = update
        power = jnp.sum(jnp.sum(update * update, axis=0, keepdims=True), axis=1, keepdims=True)
        powers = jnp.where(lane == i, power, powers)
    rows, width = moment_ref.shape
    pair = dp * fsdp + chip * 2
    both = got_ref[pl.ds(pair, 1), 12 : 12 + rows, :][0] + got_ref[pl.ds(pair + 1, 1), 12 : 12 + rows, :][0]
    vector_grad = jnp.where(core == 0, both[:, :width], both[:, width : 2 * width])
    vector_grad_ref[...] = vector_grad
    moment = decay * moment_ref[...] + (1.0 - decay) * (vector_grad * vector_grad + EPS_ONE)
    moment_out[...] = moment
    step = vector_grad * lax.rsqrt(moment)
    step_ref[...] = step
    weight_rows = jnp.zeros((rows, LANES), F32)
    weight_bias = jnp.zeros((rows, LANES), F32)
    for f in range(fsdp):
        weight_rows = weight_rows + got_ref[pl.ds(dp * fsdp + f, 1), 12 : 12 + rows, :][0]
        for d in range(VDP // 2):
            weight_bias = weight_bias + got_ref[d * fsdp + f, 12 : 12 + rows, :]
    bias = jnp.sum(weight_bias, axis=0, keepdims=True)
    kept_ref[...] = jnp.concatenate([scalars, bias, jnp.zeros((2, LANES), F32), weight_rows], axis=0)
    power = jnp.broadcast_to(jnp.sum(step * step, axis=1, keepdims=True), (rows, LANES))
    piece = jnp.concatenate([powers, jnp.zeros((3, LANES), F32), power], axis=0)
    for at in range(send_ref.shape[0]):
        send_ref[at] = piece


def tail_apply_kernel(
    place,
    got_ref,
    kept_ref,
    update_0,
    update_1,
    update_2,
    weight_0,
    weight_1,
    weight_2,
    step_ref,
    vector_ref,
    new_0,
    new_1,
    new_2,
    vector_out,
):
    dp = place[0]
    fsdp = 2 * VCHIP
    rows = vector_ref.shape[0]
    lane = iota((1, LANES), 1)
    total = got_ref[0]
    for at in range(1, VDP * fsdp):
        total = total + got_ref[at]
    for i, (update, weight, new) in enumerate(
        ((update_0, weight_0, new_0), (update_1, weight_1, new_1), (update_2, weight_2, new_2))
    ):
        entries = float(weight.shape[0] * weight.shape[1] * VDP * fsdp)
        power = jnp.sum(jnp.where(lane == i, total[0:1], 0.0), axis=1, keepdims=True)
        size = jnp.sum(jnp.where(lane == i, kept_ref[0:1, :], 0.0), axis=1, keepdims=True)
        clip = jnp.maximum(1.0, jnp.sqrt(power / entries) / CLIP_LIMIT)
        rate = STEP_RATE * jnp.maximum(EPS_TWO, jnp.sqrt(size / entries))
        new[...] = weight[...] - rate / clip * update[...]
    mine = jnp.zeros((rows, LANES), F32)
    bias = jnp.zeros((rows, LANES), F32)
    for f in range(fsdp):
        mine = mine + got_ref[pl.ds(dp * fsdp + f, 1), 4 : 4 + rows, :][0]
        for d in range(VDP // 2):
            bias = bias + got_ref[d * fsdp + f, 4 : 4 + rows, :]
    is_bias = dp < VDP // 2
    power = jnp.where(is_bias, jnp.sum(bias, axis=0, keepdims=True), mine)[:, 64:65]
    size = jnp.where(is_bias, kept_ref[1:2, :], kept_ref[4 : 4 + rows, :])[:, 64:65]
    count = jnp.where(is_bias, float(FF), float(D))
    clip = jnp.maximum(1.0, jnp.sqrt(power / count) / CLIP_LIMIT)
    rate = STEP_RATE * jnp.maximum(EPS_TWO, jnp.sqrt(size / count))
    vector_out[...] = vector_ref[...] - rate / clip * step_ref[...]


def whole_call(kernel, name, place, outs, *operands):
    return pl.pallas_call(
        kernel,
        out_shape=[jax.ShapeDtypeStruct(shape, kind) for shape, kind in outs],
        in_specs=[pl.BlockSpec(memory_space=pltpu.SMEM)] + [vspec()] * len(operands),
        out_specs=[vspec()] * len(outs),
        compiler_params=params(),
        name=name,
    )(place, *operands)


def core_swap(block):
    return lax.ppermute(block, "core", [(0, 1), (1, 0)])


def exchange(blocks, axes):
    return lax.all_to_all(blocks, axes, split_axis=0, concat_axis=0, tiled=True)


def after(value, *earlier):
    return pl.pallas_call(
        lambda *refs: None,
        out_shape=jax.ShapeDtypeStruct(value.shape, value.dtype),
        in_specs=[pl.BlockSpec(memory_space=pl.ANY)] * (1 + len(earlier)),
        out_specs=pl.BlockSpec(memory_space=pl.ANY),
        input_output_aliases={0: 0},
        name="after",
    )(value, *earlier)


def pair_kernel(mine_ref, got_ref, out_ref):
    out_ref[...] = (mine_ref[...].astype(F32) + got_ref[...].astype(F32)).astype(BF16)


def pair_sum(mine, got):
    spec = pl.BlockSpec((1,) + mine.shape[1:], lambda i: (i,) + (0,) * (mine.ndim - 1))
    return pl.pallas_call(
        pair_kernel,
        out_shape=jax.ShapeDtypeStruct(mine.shape, BF16),
        grid=mine.shape[:1],
        in_specs=[spec, spec],
        out_specs=spec,
        compiler_params=params(dimension_semantics=("arbitrary",)),
        name="pair_sum",
    )(mine, got)


CHIPS = ("dp", "chip")
ALL = ("dp", "chip", "core")


def layer(place, weights, segment_ids, tokens, cotangent, ffn_weights, send_core, send_ffn):
    table = jnp.asarray(encode_table())
    qk, x, qk_t, x_t, marks = place_tokens(segment_ids, tokens, table)
    query, value, key_t, out_t, inverse, mixed, exps, weight, proj, vector = attend_forward(
        marks, place, x, qk, *weights
    )
    ffn_mine, ffn_other = ffn_weights(vector)
    block_out, resid, mixed_grad, ffn_mine, ffn_other, proj_g, vector_g = feed_forward(
        place, tokens, cotangent, mixed, proj, ffn_mine, ffn_other, vector
    )
    ffn_got, mixed_grad = send_ffn(ffn_mine, ffn_other, mixed_grad)
    shared = (marks, place, mixed_grad, query, value, key_t, out_t, inverse, exps, qk_t, x_t, weight, proj_g)
    pulled, grads_other, sums_other = attend_back(False, *shared)
    attn_got = send_core(grads_other)
    input_grad, grads_own, sums_own = attend_back(True, *shared, resid, pulled)
    return block_out, input_grad, grads_own, grads_other, attn_got, sums_own, sums_other, vector_g, ffn_got


def body(
    tokens,
    cotangent,
    segment_ids,
    attn_weight,
    ffn_in,
    ffn_out,
    vectors,
    attn_rows,
    attn_cols,
    in_rows,
    in_cols,
    out_rows,
    out_cols,
    vector_moment,
):
    place = jnp.stack([lax.axis_index("dp"), lax.axis_index("chip"), lax.axis_index("core")])
    place = place.astype(jnp.int32)
    pieces = VDP * VCHIP
    tall, wide = attn_weight.shape
    rows_v, cols_v = vectors.shape
    split = lambda array: array.reshape((VDP, VCHIP) + array.shape[1:])
    attn_sent, ffn_sent = pack(place, attn_weight, ffn_in, ffn_out, vectors)
    attn_mine = split(exchange(attn_sent, CHIPS))
    weights = (attn_mine, core_swap(attn_mine))
    ffn_got = split(exchange(after(ffn_sent, attn_mine), CHIPS))

    def ffn_weights(vector):
        ffn_mine = after(ffn_got, vector)
        return ffn_mine, core_swap(ffn_mine)

    def send_ffn(mine, other, mixed_grad):
        both = pair_sum(mine, core_swap(other))
        got = exchange(both.reshape((pieces,) + mine.shape[2:]), CHIPS)
        return got, after(mixed_grad, both)

    (
        block_out,
        input_grad,
        grads_own,
        grads_other,
        attn_got,
        sums_own,
        sums_other,
        vector_g,
        ffn_got,
    ) = layer(place, weights, segment_ids, tokens, cotangent, ffn_weights, core_swap, send_ffn)
    sent, ffn_grad = whole_call(
        tail_send_kernel,
        "tail_send",
        place,
        [((pieces, tall + VROWS, LANES), BF16), ((2,) + ffn_in.shape, F32)],
        grads_own,
        attn_got,
        vector_g,
        sums_own,
        sums_other,
        ffn_got,
    )
    got = exchange(sent, CHIPS)
    lay = lambda stat: stat.reshape(1, -1)
    rows_old = (lay(attn_rows), lay(in_rows), lay(out_rows))
    cols_old = (lay(attn_cols), lay(in_cols), lay(out_cols))
    attn_grad, sent = whole_call(
        tail_stats_kernel,
        "tail_stats",
        place,
        [(attn_weight.shape, F32), ((2 * pieces, 16, LANES), F32)],
        got,
        ffn_grad,
        attn_weight,
        ffn_in,
        ffn_out,
        *rows_old,
        vectors,
    )
    got = exchange(sent, ALL)
    (
        update_0,
        update_1,
        update_2,
        rows_new,
        cols_new_0,
        cols_new_1,
        cols_new_2,
        vector_grad,
        moment_new,
        step,
        kept,
        sent,
    ) = whole_call(
        tail_update_kernel,
        "tail_update",
        place,
        [
            (attn_weight.shape, F32),
            (ffn_in.shape, F32),
            (ffn_out.shape, F32),
            ((8, tall), F32),
            (cols_old[0].shape, F32),
            (cols_old[1].shape, F32),
            (cols_old[2].shape, F32),
            (vectors.shape, F32),
            (vectors.shape, F32),
            (vectors.shape, F32),
            ((8, LANES), F32),
            ((2 * pieces, 8, LANES), F32),
        ],
        got,
        attn_grad,
        ffn_grad,
        *rows_old,
        *cols_old,
        vector_moment,
    )
    got = exchange(sent, ALL)
    attn_new, in_new, out_new, vectors_new = whole_call(
        tail_apply_kernel,
        "tail_apply",
        place,
        [(attn_weight.shape, F32), (ffn_in.shape, F32), (ffn_out.shape, F32), (vectors.shape, F32)],
        got,
        kept,
        update_0,
        update_1,
        update_2,
        attn_weight,
        ffn_in,
        ffn_out,
        step,
        vectors,
    )
    return (
        block_out,
        input_grad,
        attn_grad,
        ffn_grad[0],
        ffn_grad[1],
        vector_grad,
        rows_new[0],
        cols_new_0.reshape(-1),
        rows_new[1],
        cols_new_1.reshape(-1),
        rows_new[2],
        cols_new_2.reshape(-1),
        moment_new,
        attn_new,
        in_new,
        out_new,
        vectors_new,
    )


def gather_all(block):
    shape = (lax.axis_size("dp"), lax.axis_size("chip") * 2)
    count = shape[0] * shape[1]
    got = exchange(jnp.broadcast_to(block[None], (count,) + block.shape), ALL)
    return got.reshape(shape + block.shape)


def unblock(parts):
    dp_count, fsdp_count, rows, cols = parts.shape
    return parts.transpose(0, 2, 1, 3).reshape(dp_count * rows, fsdp_count * cols)


def scatter_sum(full):
    dp_count = lax.axis_size("dp")
    fsdp_count = lax.axis_size("chip") * 2
    rows, cols = full.shape
    by_col = full.astype(BF16).reshape(rows, fsdp_count, cols // fsdp_count).transpose(1, 0, 2)
    got = exchange(by_col, ("chip", "core"))
    part = jnp.sum(got.astype(F32), axis=0).astype(BF16)
    by_row = part.reshape(dp_count, rows // dp_count, cols // fsdp_count)
    return jnp.sum(exchange(by_row, "dp").astype(F32), axis=0)


def body_any(
    tokens,
    cotangent,
    segment_ids,
    attn_weight,
    ffn_in,
    ffn_out,
    vectors,
    attn_rows,
    attn_cols,
    in_rows,
    in_cols,
    out_rows,
    out_cols,
    vector_moment,
):
    dp_count = lax.axis_size("dp")
    fsdp_count = lax.axis_size("chip") * 2
    dp_place = lax.axis_index("dp")
    fsdp_place = lax.axis_index("chip") * 2 + lax.axis_index("core")
    rows_w = attn_weight.shape[0]
    rows_v = vectors.shape[0]
    place = jnp.zeros((3,), jnp.int32)
    full_attn = unblock(gather_all(attn_weight.astype(BF16)))
    full_vector = unblock(gather_all(vectors.astype(BF16)))
    full_ffn = jnp.stack(
        [unblock(gather_all(ffn_in.astype(BF16))), unblock(gather_all(ffn_out.astype(BF16)))]
    )
    tall = D // VDP
    cut = full_attn.reshape(VDP, tall, VCHIP, 2, LANES).transpose(3, 0, 2, 1, 4)
    lines = full_vector.reshape(VDP, VEC // VDP, 2, LANES).transpose(0, 2, 1, 3)
    lines = lines.reshape(VDP, 1, 2 * VEC // VDP, LANES)
    lines = jnp.pad(lines, ((0, 0), (0, VCHIP - 1), (0, VROWS - 2 * VEC // VDP), (0, 0)))
    weights = (
        jnp.concatenate([cut[0], lines], axis=2),
        jnp.concatenate([cut[1], jnp.zeros_like(lines)], axis=2),
    )
    ffn_cut = full_ffn.reshape(2, VDP, tall, VCHIP, 2, FF // (2 * VCHIP))
    ffn_cut = ffn_cut.transpose(4, 1, 3, 0, 2, 5)
    (
        block_out,
        input_grad,
        grads_own,
        grads_other,
        _,
        sums_own,
        sums_other,
        vector_g,
        ffn_got,
    ) = layer(
        place,
        weights,
        segment_ids,
        tokens,
        cotangent,
        lambda vector: (ffn_cut[0], ffn_cut[1]),
        lambda block: block,
        lambda mine, other, mixed_grad: (jnp.stack([mine, other]), mixed_grad),
    )
    attn_full = jnp.stack([grads_own, grads_other]).transpose(1, 3, 2, 0, 4).reshape(D, 4 * D)
    ffn_full = ffn_got.transpose(3, 1, 4, 2, 0, 5).reshape(2, D, FF)
    sums = jnp.concatenate([sums_own[:2], sums_other[:2]], axis=1)
    vector_full = jnp.concatenate([vector_g[:8], sums, vector_g[10:]], axis=0)
    attn_grad = scatter_sum(attn_full)
    in_grad = scatter_sum(ffn_full[0])
    out_grad = scatter_sum(ffn_full[1])
    vector_grad = scatter_sum(vector_full)

    decay = 1.0 - STEP ** (-0.8)
    gradients = (attn_grad, in_grad, out_grad)
    weights_old = (attn_weight, ffn_in, ffn_out)
    rows_old = (attn_rows, in_rows, out_rows)
    cols_old = (attn_cols, in_cols, out_cols)
    moment_new = decay * vector_moment + (1.0 - decay) * (vector_grad * vector_grad + EPS_ONE)
    vector_step = vector_grad * lax.rsqrt(moment_new)
    squares = [gradient * gradient + EPS_ONE for gradient in gradients]
    pieces = []
    for square in squares:
        pieces.append(jnp.sum(square, axis=1))
    for square in squares:
        pieces.append(jnp.sum(square, axis=0))
    pieces.append(jnp.sum(vector_step * vector_step, axis=1))
    pieces.append(jnp.sum(vectors * vectors, axis=1))
    pieces.append(jnp.stack([jnp.sum(weight * weight) for weight in weights_old]))
    pieces.append(jnp.stack([jnp.sum(old) for old in rows_old]))
    sizes = [piece.shape[0] for piece in pieces]
    flat = jnp.concatenate(pieces)
    flat = jnp.pad(flat, (0, -flat.shape[0] % 1024)).reshape(-1, LANES)
    got = gather_all(flat).reshape(dp_count, fsdp_count, -1)
    offsets = [0]
    for length in sizes:
        offsets.append(offsets[-1] + length)
    take = lambda i: got[:, :, offsets[i] : offsets[i + 1]]
    rows_new, cols_new, row_means, entries = [], [], [], []
    for i in range(3):
        count_rows = rows_w * dp_count
        count_cols = weights_old[i].shape[1] * fsdp_count
        entries.append(float(count_rows * count_cols))
        row_all = jnp.sum(take(i), axis=1)
        mine = lax.dynamic_index_in_dim(row_all, dp_place, 0, keepdims=False)
        rows_new.append(decay * rows_old[i] + (1.0 - decay) * mine / count_cols)
        col_all = jnp.sum(take(3 + i), axis=0)
        mine = lax.dynamic_index_in_dim(col_all, fsdp_place, 0, keepdims=False)
        cols_new.append(decay * cols_old[i] + (1.0 - decay) * mine / count_rows)
        old_total = jnp.sum(take(9)[:, 0, i])
        row_means.append(
            (decay * old_total + (1.0 - decay) * jnp.sum(row_all) / count_cols) / count_rows
        )
    step_rows = jnp.sum(take(6), axis=1).reshape(-1)
    weight_rows = jnp.sum(take(7), axis=1).reshape(-1)
    weight_totals = jnp.sum(take(8), axis=(0, 1))
    updates = []
    for i in range(3):
        second = rows_new[i][:, None] * cols_new[i][None, :] / row_means[i]
        updates.append(gradients[i] * lax.rsqrt(second))
    flat = jnp.stack([jnp.sum(update * update) for update in updates])
    flat = jnp.broadcast_to(jnp.pad(flat, (0, 5))[:, None], (8, LANES))
    totals = jnp.sum(gather_all(flat)[:, :, :, 0], axis=(0, 1))
    new_weights = []
    for i in range(3):
        clip_factor = jnp.maximum(1.0, jnp.sqrt(totals[i] / entries[i]) / CLIP_LIMIT)
        step_size = STEP_RATE * jnp.maximum(EPS_TWO, jnp.sqrt(weight_totals[i] / entries[i]))
        new_weights.append(weights_old[i] - step_size / clip_factor * updates[i])
    bias_rows = FF // D
    row_places = jnp.arange(VEC)
    counts = jnp.where(row_places < bias_rows, float(FF), float(D))
    grouped_updates = jnp.where(row_places < bias_rows, jnp.sum(step_rows[:bias_rows]), step_rows)
    grouped_weights = jnp.where(row_places < bias_rows, jnp.sum(weight_rows[:bias_rows]), weight_rows)
    clip_rows = jnp.maximum(1.0, jnp.sqrt(grouped_updates / counts) / CLIP_LIMIT)
    step_sizes = STEP_RATE * jnp.maximum(EPS_TWO, jnp.sqrt(grouped_weights / counts))
    factor_rows = lax.dynamic_slice_in_dim(step_sizes / clip_rows, dp_place * rows_v, rows_v)
    vectors_new = vectors - factor_rows[:, None] * vector_step
    return (
        block_out,
        input_grad,
        attn_grad,
        in_grad,
        out_grad,
        vector_grad,
        rows_new[0],
        cols_new[0],
        rows_new[1],
        cols_new[1],
        rows_new[2],
        cols_new[2],
        moment_new,
        new_weights[0],
        new_weights[1],
        new_weights[2],
        vectors_new,
    )


def solution(mesh):
    dp_count, fsdp_count = mesh.shape["dp"], mesh.shape["fsdp"]
    inner = jax.sharding.Mesh(mesh.devices.reshape(dp_count, fsdp_count // 2, 2), ALL)
    fsdp = ("chip", "core")
    split = P(ALL, None)
    block = P("dp", fsdp)
    stats = (P("dp"), P(fsdp)) * 3
    plain = dp_count == VDP and fsdp_count == 2 * VCHIP
    return jax.shard_map(
        body if plain else body_any,
        mesh=inner,
        in_specs=(split,) * 3 + (block,) * 4 + stats + (block,),
        out_specs=(split,) * 2 + (block,) * 4 + stats + (block,) * 5,
        check_vma=False,
    )
```

```python
import functools
import math

import jax
import jax.numpy as jnp
import numpy as np
from jax import lax
from jax.experimental import pallas as pl
from jax.experimental.pallas import tpu as pltpu
from jax.sharding import PartitionSpec as P

D = 256
FF = 2048
HEADS = 8
HEAD_DIM = 32
SEQ = 1024
HALF = 512
GROUP = 4
LANES = 128
QBLOCK = 256
WGRID = 32
STEP = 10
VEC = 16
TILE = 512
CHUNK = 512
SUB = 256
LEAD = 4
STRIP = 64
VDP = 4
VCHIP = 4
VROWS = 16

EPS_NORM = 1e-05
EPS_ONE = 1e-30
EPS_TWO = 0.001
CLIP_LIMIT = 1.0
STEP_RATE = 0.3
FAR = 1e30
SCALE = HEAD_DIM ** (-0.5)
GELU_A = math.sqrt(2.0 / math.pi)
GELU_B = 0.044715
F32 = jnp.float32
BF16 = jnp.bfloat16
MIB = 1024 * 1024


def dot(left, right):
    return jnp.dot(left, right, preferred_element_type=F32)


def dot_nt(left, right):
    return lax.dot_general(left, right, (((1,), (1,)), ((), ())), preferred_element_type=F32)


def encode_table():
    half = D // 2
    feature = np.arange(half)
    freq = np.exp(
        (2 * (feature // 2)).astype(np.float32) * np.float32(-math.log(10000.0) / half)
    ).astype(np.float32)
    angles = np.arange(1, WGRID + 1, dtype=np.float32)[:, None] * freq[None, :]
    table = np.where(feature % 2 == 0, np.sin(angles), np.cos(angles)).astype(np.float32)
    low = jnp.bfloat16
    one = table.astype(low)
    rest = table - one.astype(np.float32)
    two = rest.astype(low)
    three = (rest - two.astype(np.float32)).astype(low)
    blank = np.zeros((LANES - 3 * WGRID, half), low)
    return np.concatenate([one, two, three, blank], axis=0)


def iota(shape, dim):
    return lax.broadcasted_iota(jnp.int32, shape, dim)


def norm_forward(rows):
    centered = rows - jnp.mean(rows, axis=-1, keepdims=True)
    inverse = lax.rsqrt(jnp.mean(centered * centered, axis=-1, keepdims=True) + EPS_NORM)
    return centered * inverse, inverse


def norm_backward(upstream, normed, inverse):
    return inverse * (
        upstream
        - jnp.mean(upstream, axis=-1, keepdims=True)
        - normed * jnp.mean(upstream * normed, axis=-1, keepdims=True)
    )

def vspec():
    return pl.BlockSpec(memory_space=pltpu.VMEM)


def params(mib=40, **more):
    return pltpu.CompilerParams(vmem_limit_bytes=mib * MIB, **more)


def pack_kernel(place, attn_ref, first_ref, second_ref, vector_ref, attn_out, ffn_out):
    owner = place[1] * 2 + place[2]
    vector = vector_ref[...]
    rows = vector.shape[0]
    wide = jnp.concatenate([vector] * (LANES // vector.shape[1]), axis=1)
    slot = iota((rows, LANES), 1) // vector.shape[1]
    per = LANES // vector.shape[1]
    parts = [attn_ref[...]]
    for half in range(2):
        parts.append(jnp.where(slot + half * per == owner, wide, 0.0))
    parts.append(jnp.zeros((VROWS - 2 * rows, LANES), F32))
    piece = jnp.concatenate(parts, axis=0).astype(BF16)
    first = first_ref[...].astype(BF16)
    second = second_ref[...].astype(BF16)
    for at in range(VDP * VCHIP):
        attn_out[at] = piece
        ffn_out[at, 0] = first
        ffn_out[at, 1] = second


def pack(place, attn_weight, ffn_in, ffn_out, vectors):
    count = VDP * VCHIP
    return pl.pallas_call(
        pack_kernel,
        out_shape=(
            jax.ShapeDtypeStruct((count, attn_weight.shape[0] + VROWS, LANES), BF16),
            jax.ShapeDtypeStruct((count, 2) + ffn_in.shape, BF16),
        ),
        in_specs=[pl.BlockSpec(memory_space=pltpu.SMEM)] + [vspec()] * 4,
        out_specs=(vspec(), vspec()),
        compiler_params=params(),
        name="pack",
    )(place, attn_weight, ffn_in, ffn_out, vectors)


def place_kernel(
    segment_ref, tokens_ref, back_ref, table_ref, qk_ref, x_ref, qk_t_ref, x_t_ref, turned_ref, marks_ref
):
    row = pl.program_id(0)
    starts = []
    for number in range(1, 4):
        at = jnp.int32(0)
        for step in (512, 256, 128, 64, 32, 16, 8, 4, 2, 1, 1):
            probe = jnp.minimum(at + (step - 1), SEQ - 1)
            at = jnp.where(segment_ref[row, probe] < number, at + step, at)
        starts.append(at)
    edges = [jnp.int32(0)] + starts + [jnp.int32(SEQ)]
    begin = jnp.int32(0)
    for number in range(3, -1, -1):
        begin = jnp.where(edges[number + 1] - edges[number] == HALF, edges[number], begin)
    for number in range(3):
        marks_ref[row, number] = starts[number]
    marks_ref[row, 3] = begin
    one, two, three = starts
    x = pltpu.roll(tokens_ref[...].astype(F32), (SEQ - begin) & (SEQ - 1), 0)
    x_ref[...] = x.astype(BF16)
    x_t_ref[...] = x.T.astype(BF16)
    back = back_ref[...].astype(F32)
    turned_ref[...] = pltpu.roll(back, (SEQ - begin) & (SEQ - 1), 0).astype(BF16)
    at = (iota((SEQ, LANES), 0) + begin) & (SEQ - 1)
    lane = iota((SEQ, LANES), 1)
    start = jnp.where(at >= three, three, jnp.where(at >= two, two, jnp.where(at >= one, one, 0)))
    local = at - start
    kept = lane < 3 * WGRID
    slot = lane & (WGRID - 1)
    hot_r = jnp.where(((local >> 5) == slot) & kept, 1.0, 0.0).astype(BF16)
    hot_c = jnp.where(((local & (WGRID - 1)) == slot) & kept, 1.0, 0.0).astype(BF16)
    table = table_ref[...]
    places = jnp.concatenate([dot(hot_r, table), dot(hot_c, table)], axis=1)
    qk = x + places
    qk_ref[...] = qk.astype(BF16)
    qk_t_ref[...] = qk.T.astype(BF16)


def place_tokens(segment_ids, tokens, cotangent, table):
    rows = segment_ids.shape[0]
    by_row = lambda r: (r, 0)
    return pl.pallas_call(
        place_kernel,
        out_shape=(
            jax.ShapeDtypeStruct(tokens.shape, BF16),
            jax.ShapeDtypeStruct(tokens.shape, BF16),
            jax.ShapeDtypeStruct((D, tokens.shape[0]), BF16),
            jax.ShapeDtypeStruct((D, tokens.shape[0]), BF16),
            jax.ShapeDtypeStruct(tokens.shape, BF16),
            jax.ShapeDtypeStruct((rows, 4), jnp.int32),
        ),
        grid=(rows,),
        in_specs=[
            pl.BlockSpec(memory_space=pltpu.SMEM),
            pl.BlockSpec((SEQ, D), by_row),
            pl.BlockSpec((SEQ, D), by_row),
            pl.BlockSpec((LANES, LANES), lambda r: (0, 0)),
        ],
        out_specs=(
            pl.BlockSpec((SEQ, D), by_row),
            pl.BlockSpec((SEQ, D), by_row),
            pl.BlockSpec((D, SEQ), lambda r: (0, r)),
            pl.BlockSpec((D, SEQ), lambda r: (0, r)),
            pl.BlockSpec((SEQ, D), by_row),
            pl.BlockSpec(memory_space=pltpu.SMEM),
        ),
        compiler_params=params(dimension_semantics=("arbitrary",)),
        cost_estimate=pl.CostEstimate(flops=600_000_000, bytes_accessed=4_000_000, transcendentals=0),
        name="place_tokens",
    )(segment_ids, tokens, cotangent, table)


def attend_kernel(
    marks,
    place,
    x_ref,
    qk_ref,
    x_t_ref,
    qk_t_ref,
    mine_ref,
    other_ref,
    query_t_ref,
    value_ref,
    key_t_ref,
    out_t_ref,
    inverse_ref,
    mixed_ref,
    mixed_t_ref,
    exps_ref,
    weight_ref,
    proj_ref,
    vector_ref,
    key_s,
    value_s,
    mark_k,
    mark_q,
    scores_s,
    weight_t_s,
    bias_s,
):
    row = pl.program_id(0)
    group = pl.program_id(1)
    begin = marks[row, 3]
    core = place[2]

    @pl.when((row == 0) & (group == 0))
    def _():
        tall = D // VDP
        for d in range(VDP):
            rows = slice(d * tall, (d + 1) * tall)
            total = jnp.zeros((8, LANES), F32)
            for c in range(VCHIP):
                for ref, half in ((mine_ref, core), (other_ref, 1 - core)):
                    if c < 3:
                        to = pl.ds(pl.multiple_of(c * D + half * LANES, LANES), LANES)
                        weight_ref[rows, to] = ref[d, c, :tall, :]
                    else:
                        to = pl.ds(pl.multiple_of(half * LANES, LANES), LANES)
                        proj_ref[rows, to] = ref[d, c, :tall, :]
                    total += ref[d, c, tall : tall + 8, :].astype(F32)
            vector_ref[d * 4 : (d + 1) * 4, :LANES] = total[:4]
            vector_ref[d * 4 : (d + 1) * 4, LANES:] = total[4:]
        weight_t_s[...] = weight_ref[...].astype(F32).T.astype(BF16)
        bias_s[...] = vector_ref[8:16, :].T

    @pl.when(group == 0)
    def _():
        qk_t = qk_t_ref[...]
        query_t = (dot(weight_t_s[:D, :], qk_t) + bias_s[:, 0:1]) * SCALE
        query_t_ref[...] = query_t.astype(BF16)
        key_t_ref[...] = dot(weight_t_s[D : 2 * D, :], qk_t).astype(BF16)
        key_s[...] = dot(qk_ref[...], weight_ref[:, D : 2 * D]).astype(BF16)
        value = dot(x_ref[...], weight_ref[:, 2 * D : 3 * D]) + vector_ref[9:10, :]
        value_ref[...] = value.astype(BF16)
        value_t = dot(weight_t_s[2 * D :, :], x_t_ref[...]) + bias_s[:, 1:2]
        value_t = value_t.astype(BF16)
        for head in range(HEADS):
            value_s[head, :HEAD_DIM, :] = value_t[head * HEAD_DIM : (head + 1) * HEAD_DIM, :]
            value_s[head, HEAD_DIM:, :] = jnp.ones((16, SEQ), BF16)
        one, two, three = marks[row, 0], marks[row, 1], marks[row, 2]

        def number_of(shape, dim):
            here = (iota(shape, dim) + (HALF + begin)) & (SEQ - 1)
            return (
                jnp.where(here >= one, 1, 0)
                + jnp.where(here >= two, 1, 0)
                + jnp.where(here >= three, 1, 0)
            )

        lane = iota((HALF, LANES), 1)
        number = number_of((HALF, LANES), 0)
        mark_k[...] = jnp.where((number != lane) & (lane < 4), -FAR, 0.0).astype(BF16)
        number = number_of((LANES, HALF), 1)
        mark_q[...] = jnp.where(number == iota((LANES, HALF), 0), 1.0, 0.0).astype(BF16)

    lanes = pl.ds(pl.multiple_of(group * LANES, LANES), LANES)
    head_of = iota((1, LANES), 1) // HEAD_DIM

    def scores_of(item):
        half, at_head, block = item
        mask = jnp.where(head_of == at_head, 1.0, 0.0).astype(BF16)
        key_m = key_s[half * HALF : (half + 1) * HALF, lanes] * mask
        at = half * HALF + block * QBLOCK
        query = query_t_ref[lanes, at : at + QBLOCK]
        if half == 1:
            key_m = jnp.concatenate([key_m, mark_k[...]], axis=1)
            query = jnp.concatenate(
                [query, mark_q[:, block * QBLOCK : (block + 1) * QBLOCK]], axis=0
            )
        return dot(key_m, query)

    def exps_of(item, slot):
        half, at_head, block = item
        cols = slice(at_head * HALF + block * QBLOCK, at_head * HALF + (block + 1) * QBLOCK)
        largest = scores_s[slot, :STRIP, :]
        for at in range(STRIP, HALF, STRIP):
            largest = jnp.maximum(largest, scores_s[slot, at : at + STRIP, :])
        largest = jnp.max(largest, axis=0, keepdims=True)
        for at in range(0, HALF, STRIP):
            exps = jnp.exp(scores_s[slot, at : at + STRIP, :] - largest)
            exps_ref[0, 0, half, at : at + STRIP, cols] = exps.astype(BF16)

    def finish(item):
        half, at_head, block = item
        at = half * HALF + block * QBLOCK
        rows = slice(half * HALF, (half + 1) * HALF)
        cols = slice(at_head * HALF + block * QBLOCK, at_head * HALF + (block + 1) * QBLOCK)
        out = dot(value_s[group * GROUP + at_head, :, rows], exps_ref[0, 0, half, :, cols])
        inverse = 1.0 / out[HEAD_DIM : HEAD_DIM + 1, :]
        inverse_ref[0, at_head : at_head + 1, at : at + QBLOCK] = inverse
        out_t_ref[at_head * HEAD_DIM : (at_head + 1) * HEAD_DIM, at : at + QBLOCK] = (
            out[:HEAD_DIM, :] * inverse
        )

    items = [
        (half, at_head, block)
        for half in range(2)
        for at_head in range(GROUP)
        for block in range(HALF // QBLOCK)
    ]
    for i in range(len(items) + 2):
        if i < len(items):
            scores_s[i % 2] = scores_of(items[i])
        if 1 <= i <= len(items):
            exps_of(items[i - 1], (i - 1) % 2)
        if i >= 2:
            finish(items[i - 2])
    out_t = out_t_ref[...]
    mixed_t_ref[...] = out_t.astype(BF16)
    mixed_ref[...] = out_t.T.astype(BF16)


def attend_forward(marks, place, x, qk, x_t, qk_t, mine, other):
    total = x.shape[0]
    rows = total // SEQ
    by_row = lambda r, g, m, p: (r, 0)
    by_col = lambda r, g, m, p: (0, r)
    by_both = lambda r, g, m, p: (g, r)
    whole = lambda r, g, m, p: (0, 0)
    return pl.pallas_call(
        attend_kernel,
        out_shape=(
            jax.ShapeDtypeStruct((D, total), BF16),
            jax.ShapeDtypeStruct((total, D), BF16),
            jax.ShapeDtypeStruct((D, total), BF16),
            jax.ShapeDtypeStruct((D, total), F32),
            jax.ShapeDtypeStruct((2, 8, total), F32),
            jax.ShapeDtypeStruct((total, D), BF16),
            jax.ShapeDtypeStruct((D, total), BF16),
            jax.ShapeDtypeStruct((rows, 2, 2, HALF, GROUP * HALF), BF16),
            jax.ShapeDtypeStruct((D, 3 * D), BF16),
            jax.ShapeDtypeStruct((D, D), BF16),
            jax.ShapeDtypeStruct((VEC, D), F32),
        ),
        grid_spec=pltpu.PrefetchScalarGridSpec(
            num_scalar_prefetch=2,
            grid=(rows, 2),
            in_specs=[
                pl.BlockSpec((SEQ, D), by_row),
                pl.BlockSpec((SEQ, D), by_row),
                pl.BlockSpec((D, SEQ), by_col),
                pl.BlockSpec((D, SEQ), by_col),
                vspec(),
                vspec(),
            ],
            out_specs=[
                pl.BlockSpec((D, SEQ), by_col),
                pl.BlockSpec((SEQ, D), by_row),
                pl.BlockSpec((D, SEQ), by_col),
                pl.BlockSpec((LANES, SEQ), by_both),
                pl.BlockSpec((1, 8, SEQ), lambda r, g, m, p: (g, 0, r)),
                pl.BlockSpec((SEQ, LANES), lambda r, g, m, p: (r, g)),
                pl.BlockSpec((LANES, SEQ), by_both),
                pl.BlockSpec((1, 1, 2, HALF, GROUP * HALF), lambda r, g, m, p: (r, g, 0, 0, 0)),
                pl.BlockSpec((D, 3 * D), whole),
                pl.BlockSpec((D, D), whole),
                pl.BlockSpec((VEC, D), whole),
            ],
            scratch_shapes=[
                pltpu.VMEM((SEQ, D), BF16),
                pltpu.VMEM((HEADS, HEAD_DIM + 16, SEQ), BF16),
                pltpu.VMEM((HALF, LANES), BF16),
                pltpu.VMEM((LANES, HALF), BF16),
                pltpu.VMEM((2, HALF, QBLOCK), F32),
                pltpu.VMEM((3 * D, D), BF16),
                pltpu.VMEM((D, 8), F32),
            ],
        ),
        compiler_params=params(dimension_semantics=("arbitrary", "arbitrary")),
        cost_estimate=pl.CostEstimate(
            flops=20_000_000_000, bytes_accessed=30_000_000, transcendentals=8_400_000
        ),
        name="attend_forward",
    )(marks, place, x, qk, x_t, qk_t, mine, other)


def feed_kernel(
    marks,
    place,
    x_ref,
    back_ref,
    mixed_ref,
    mixed_t_ref,
    proj_ref,
    mine_ref,
    other_ref,
    vector_ref,
    block_ref,
    resid_ref,
    mixed_grad_ref,
    mine_out,
    other_out,
    proj_out,
    vector_out,
    first_w,
    second_w,
    first_acc,
    second_acc,
    proj_acc,
    vector_acc,
    hidden_s,
    slope_s,
    pre_s,
    work_s,
    first_low_s,
    branch_low_s,
    attended_s,
    block_s,
    eye_s,
):
    step = pl.program_id(0)
    core = place[2]
    tall = D // VDP
    wide = FF // (2 * VCHIP)

    @pl.when(step == 0)
    def _():
        first_acc[...] = jnp.zeros_like(first_acc)
        second_acc[...] = jnp.zeros_like(second_acc)
        proj_acc[...] = jnp.zeros_like(proj_acc)
        vector_acc[...] = jnp.zeros_like(vector_acc)
        eye_s[...] = jnp.where(iota((D, D), 0) == iota((D, D), 1), 1.0, 0.0).astype(BF16)
        for d in range(VDP):
            rows = slice(d * tall, (d + 1) * tall)
            for c in range(VCHIP):
                for ref, half in ((mine_ref, core), (other_ref, 1 - core)):
                    to = pl.ds(pl.multiple_of((2 * c + half) * wide, wide), wide)
                    first_w[rows, to] = ref[d, c, 0]
                    second_w[rows, to] = ref[d, c, 1]

    bias_o, bias_2 = vector_ref[10:11, :], vector_ref[11:12, :]
    gain_1, shift_1 = vector_ref[12:13, :], vector_ref[13:14, :]
    gain_2, shift_2 = vector_ref[14:15, :], vector_ref[15:16, :]
    at_row = pl.multiple_of((step % (SEQ // TILE)) * TILE, TILE)
    per = CHUNK // D
    chunks = FF // CHUNK

    def columns(at):
        return slice(at * CHUNK, (at + 1) * CHUNK)

    def hidden_of(rows_at, at, slot):
        for side in range(per):
            bias = vector_ref[at * per + side : at * per + side + 1, :]
            cols = slice(at * CHUNK + side * D, at * CHUNK + (side + 1) * D)
            for top in range(0, SUB, STRIP):
                rows = slice(rows_at + top, rows_at + top + STRIP)
                pre = work_s[slot, top : top + STRIP, side * D : (side + 1) * D] + bias
                cube = (GELU_A * GELU_B) * (pre * pre)
                gate = 0.5 + 0.5 * jnp.tanh(pre * (cube + GELU_A))
                hidden_s[rows, cols] = (pre * gate).astype(BF16)
                slope_s[rows, cols] = gate + (gate - gate * gate) * (
                    pre * (6.0 * cube + 2.0 * GELU_A)
                )

    def pre_grad_of(rows_at, at, slot):
        for side in range(per):
            cols = slice(at * CHUNK + side * D, at * CHUNK + (side + 1) * D)
            sums = jnp.zeros((STRIP, D), F32)
            for top in range(0, SUB, STRIP):
                rows = slice(rows_at + top, rows_at + top + STRIP)
                pull = work_s[slot, top : top + STRIP, side * D : (side + 1) * D]
                pre_low = (pull * slope_s[rows, cols]).astype(BF16)
                pre_s[rows, cols] = pre_low
                sums = sums + pre_low.astype(F32)
            to = at * per + side
            vector_acc[to : to + 1, :] += jnp.sum(sums, axis=0, keepdims=True)

    def stages(sub):
        rows_at = sub * SUB
        rows = slice(rows_at, rows_at + SUB)
        slots = (2 * sub, 2 * sub + 1)
        attended = dot(mixed_ref[rows, :], proj_ref[...]) + bias_o
        norm_1, inverse_1 = norm_forward(x_ref[rows, :].astype(F32) + attended)
        first = norm_1 * gain_1 + shift_1
        first_low = first.astype(BF16)
        first_low_s[rows, :] = first_low
        yield
        branch = jnp.zeros((SUB, D), F32)
        for i in range(chunks + 2):
            if i < chunks:
                work_s[slots[i % 2]] = dot(first_low, first_w[:, columns(i)])
            if 1 <= i <= chunks:
                hidden_of(rows_at, i - 1, slots[(i - 1) % 2])
            if i >= 2:
                cols = columns(i - 2)
                branch += dot_nt(hidden_s[rows, cols], second_w[:, cols])
            yield
        norm_2, inverse_2 = norm_forward(first + (branch + bias_2))
        block_s[pl.ds(at_row + rows_at, SUB), :] = norm_2 * gain_2 + shift_2
        back = back_ref[rows, :].astype(F32)
        vector_acc[14:15, :] += jnp.sum(back * norm_2, axis=0, keepdims=True)
        vector_acc[15:16, :] += jnp.sum(back, axis=0, keepdims=True)
        resid_2 = norm_backward(back * gain_2, norm_2, inverse_2)
        branch_low = resid_2.astype(BF16)
        branch_low_s[rows, :] = branch_low
        vector_acc[11:12, :] += jnp.sum(branch_low.astype(F32), axis=0, keepdims=True)
        yield
        first_back = resid_2
        if sub == 1:
            branch_t = dot_nt(eye_s[...], branch_low_s[...]).astype(BF16)
            first_t = dot_nt(eye_s[...], first_low_s[...]).astype(BF16)
        for i in range(chunks + 2):
            if i < chunks:
                work_s[slots[i % 2]] = dot(branch_low, second_w[:, columns(i)])
                if sub == 1:
                    second_acc[:, columns(i)] += dot(branch_t, hidden_s[:, columns(i)])
            if 1 <= i <= chunks:
                pre_grad_of(rows_at, i - 1, slots[(i - 1) % 2])
            if i >= 2:
                cols = columns(i - 2)
                first_back += dot_nt(pre_s[rows, cols], first_w[:, cols])
                if sub == 1:
                    first_acc[:, cols] += dot(first_t, pre_s[:, cols])
            yield
        vector_acc[12:13, :] += jnp.sum(first_back * norm_1, axis=0, keepdims=True)
        vector_acc[13:14, :] += jnp.sum(first_back, axis=0, keepdims=True)
        resid_1 = norm_backward(first_back * gain_1, norm_1, inverse_1)
        resid_ref[rows, :] = resid_1
        attended_low = resid_1.astype(BF16)
        attended_s[rows, :] = attended_low
        vector_acc[10:11, :] += jnp.sum(attended_low.astype(F32), axis=0, keepdims=True)
        mixed_grad_ref[:, rows] = dot_nt(proj_ref[...], attended_low).astype(BF16)
        yield

    ahead, behind = stages(0), stages(1)
    for _ in range(LEAD):
        next(ahead)
    running = [ahead, behind]
    while running:
        for program in list(running):
            if next(program, 0) == 0:
                running.remove(program)
    proj_acc[...] += dot(mixed_t_ref[...], attended_s[...])

    @pl.when(step % (SEQ // TILE) == SEQ // TILE - 1)
    def _():
        block_ref[...] = pltpu.roll(block_s[...], marks[step // (SEQ // TILE), 3], 0)

    @pl.when(step == pl.num_programs(0) - 1)
    def _():
        for d in range(VDP):
            rows = slice(d * tall, (d + 1) * tall)
            for c in range(VCHIP):
                for ref, half in ((mine_out, core), (other_out, 1 - core)):
                    to = pl.ds(pl.multiple_of((2 * c + half) * wide, wide), wide)
                    ref[d, c, 0] = first_acc[rows, to].astype(BF16)
                    ref[d, c, 1] = second_acc[rows, to].astype(BF16)
        proj_out[...] = proj_acc[...]
        vector_out[...] = vector_acc[...]


def feed_forward(marks, place, x, back, mixed, mixed_t, proj, mine, other, vector):
    total = x.shape[0]
    tile = lambda i, m, p: (i, 0)
    by_col = lambda i, m, p: (0, i)
    whole = lambda i, m, p: (0, 0)
    whole5 = lambda i, m, p: (0, 0, 0, 0, 0)
    return pl.pallas_call(
        feed_kernel,
        out_shape=(
            jax.ShapeDtypeStruct((total, D), F32),
            jax.ShapeDtypeStruct((total, D), F32),
            jax.ShapeDtypeStruct((D, total), BF16),
            jax.ShapeDtypeStruct(mine.shape, BF16),
            jax.ShapeDtypeStruct(mine.shape, BF16),
            jax.ShapeDtypeStruct((D, D), F32),
            jax.ShapeDtypeStruct((VEC, D), F32),
        ),
        grid_spec=pltpu.PrefetchScalarGridSpec(
            num_scalar_prefetch=2,
            grid=(total // TILE,),
            in_specs=[
                pl.BlockSpec((TILE, D), tile),
                pl.BlockSpec((TILE, D), tile),
                pl.BlockSpec((TILE, D), tile),
                pl.BlockSpec((D, TILE), by_col),
                pl.BlockSpec((D, D), whole),
                vspec(),
                vspec(),
                pl.BlockSpec((VEC, D), whole),
            ],
            out_specs=[
                pl.BlockSpec((SEQ, D), lambda i, m, p: (i // (SEQ // TILE), 0)),
                pl.BlockSpec((TILE, D), tile),
                pl.BlockSpec((D, TILE), by_col),
                pl.BlockSpec(mine.shape, whole5),
                pl.BlockSpec(mine.shape, whole5),
                pl.BlockSpec((D, D), whole),
                pl.BlockSpec((VEC, D), whole),
            ],
            scratch_shapes=[
                pltpu.VMEM((D, FF), BF16),
                pltpu.VMEM((D, FF), BF16),
                pltpu.VMEM((D, FF), F32),
                pltpu.VMEM((D, FF), F32),
                pltpu.VMEM((D, D), F32),
                pltpu.VMEM((VEC, D), F32),
                pltpu.VMEM((TILE, FF), BF16),
                pltpu.VMEM((TILE, FF), F32),
                pltpu.VMEM((TILE, FF), BF16),
                pltpu.VMEM((4, SUB, CHUNK), F32),
                pltpu.VMEM((TILE, D), BF16),
                pltpu.VMEM((TILE, D), BF16),
                pltpu.VMEM((TILE, D), BF16),
                pltpu.VMEM((SEQ, D), F32),
                pltpu.VMEM((D, D), BF16),
            ],
        ),
        compiler_params=params(dimension_semantics=("arbitrary",)),
        cost_estimate=pl.CostEstimate(
            flops=14_000_000_000, bytes_accessed=15_000_000, transcendentals=4_200_000
        ),
        name="feed_forward",
    )(marks, place, x, back, mixed, mixed_t, proj, mine, other, vector)


def pull_kernel(
    own,
    marks,
    place,
    grad_t_ref,
    query_t_ref,
    value_ref,
    key_t_ref,
    out_t_ref,
    inverse_ref,
    exps_ref,
    qk_t_ref,
    x_t_ref,
    weight_ref,
    proj_ref,
    *refs,
):
    if own:
        resid_ref, other_ref, pulled_ref, grads_ref, sums_ref = refs[:5]
    else:
        pulled_ref, grads_ref, sums_ref = refs[:3]
    dot_s, query_t_s, acc, sum_acc, scaled_s, query_s, value_s, scaled_t_s, score_s, work_s = refs[-10:]
    row = pl.program_id(0)
    begin = marks[row, 3]
    group = place[2] if own else 1 - place[2]

    @pl.when(row == 0)
    def _():
        acc[...] = jnp.zeros_like(acc)
        sum_acc[...] = jnp.zeros_like(sum_acc)

    grad_t = grad_t_ref[...].astype(F32)
    scaled_s[...] = jnp.zeros_like(scaled_s)
    query_s[...] = jnp.zeros_like(query_s)
    head_of = iota((1, LANES), 1) // HEAD_DIM
    for at_head in range(GROUP):
        heads = slice(at_head * HEAD_DIM, (at_head + 1) * HEAD_DIM)
        part = grad_t[heads, :] * inverse_ref[0, at_head : at_head + 1, :]
        dot_s[at_head : at_head + 1, :] = jnp.sum(part * out_t_ref[heads, :], axis=0, keepdims=True)
        part = part.astype(BF16)
        scaled_t_s[heads, :] = part
        mask = jnp.where(head_of == at_head, 1.0, 0.0).astype(BF16)
        for half in range(2):
            rows = slice(half * HALF, (half + 1) * HALF)
            to = slice(at_head * HALF, (at_head + 1) * HALF)
            scaled_s[half, heads, to] = part[:, rows]
            query_s[half, heads, to] = query_t_ref[heads, rows]
            value_s[half, to, :] = value_ref[rows, :] * mask
    key_parts = [jnp.zeros((HALF, LANES), F32) for _ in range(2)]
    value_parts = [jnp.zeros((HALF, LANES), F32) for _ in range(2)]

    def pull_of(item):
        half, at_head, block = item
        at = half * HALF + block * QBLOCK
        value = value_s[half, at_head * HALF : (at_head + 1) * HALF, :]
        return dot(value, scaled_t_s[:, at : at + QBLOCK])

    def score_grad_of(item, slot):
        half, at_head, block = item
        at = half * HALF + block * QBLOCK
        cols = slice(at_head * HALF + block * QBLOCK, at_head * HALF + (block + 1) * QBLOCK)
        shift = dot_s[at_head : at_head + 1, at : at + QBLOCK]
        for top in range(0, HALF, STRIP):
            rows = slice(top, top + STRIP)
            exps = exps_ref[0, 0, half, rows, cols].astype(F32)
            score_s[half, rows, cols] = (exps * (work_s[slot, rows, :] - shift)).astype(BF16)

    def finish(half, at_head):
        cols = slice(at_head * HALF, (at_head + 2) * HALF)
        rows = slice(half * HALF, (half + 1) * HALF)
        value_parts[half] += dot_nt(exps_ref[0, 0, half, :, cols], scaled_s[half, :, cols])
        key_parts[half] += dot_nt(score_s[half, :, cols], query_s[half, :, cols])
        for head in range(at_head, at_head + 2):
            heads = slice(head * HEAD_DIM, (head + 1) * HEAD_DIM)
            query_t_s[heads, rows] = dot(
                key_t_ref[heads, rows], score_s[half, :, head * HALF : (head + 1) * HALF]
            )

    items = [
        (half, at_head, block)
        for half in range(2)
        for at_head in range(GROUP)
        for block in range(HALF // QBLOCK)
    ]
    for i in range(len(items) + 1):
        if i < len(items):
            work_s[i % 2] = pull_of(items[i])
        if i >= 1:
            score_grad_of(items[i - 1], (i - 1) % 2)
            if i % 4 == 0:
                half, at_head, _ = items[i - 1]
                finish(half, at_head - 1)
    query_low = query_t_s[...].T.astype(BF16)
    key_low = jnp.concatenate(key_parts, axis=0).astype(BF16)
    value_low = jnp.concatenate(value_parts, axis=0).astype(BF16)
    sum_acc[0:1, :] += jnp.sum(query_low.astype(F32), axis=0, keepdims=True) * SCALE
    sum_acc[1:2, :] += jnp.sum(value_low.astype(F32), axis=0, keepdims=True)
    qk_t = qk_t_ref[...]
    x_t = x_t_ref[...]
    acc[:, :LANES] += dot(qk_t, query_low) * SCALE
    acc[:, LANES : 2 * LANES] += dot(qk_t, key_low)
    acc[:, 2 * LANES :] += dot(x_t, value_low)
    at = [pl.ds(pl.multiple_of(i * D + group * LANES, LANES), LANES) for i in range(3)]
    pulled = dot_nt(query_low, weight_ref[:, at[0]]) * SCALE + dot_nt(
        jnp.concatenate([key_low, value_low], axis=1),
        jnp.concatenate([weight_ref[:, at[1]], weight_ref[:, at[2]]], axis=1),
    )
    if own:
        pulled_ref[...] = pltpu.roll(resid_ref[...] + (pulled + other_ref[...]), begin, 0)
    else:
        pulled_ref[...] = pulled

    @pl.when(row == pl.num_programs(0) - 1)
    def _():
        tall = D // VDP
        for d in range(VDP):
            rows = slice(d * tall, (d + 1) * tall)
            for c in range(3):
                grads_ref[d, c] = acc[rows, c * LANES : (c + 1) * LANES].astype(BF16)
            grads_ref[d, 3] = proj_ref[rows, :].astype(BF16)
        sums_ref[...] = sum_acc[...]


def attend_back(own, marks, place, grad_t, query_t, value, key_t, out_t, inverse, exps, qk_t, x_t, weight, proj, *more):
    total = value.shape[0]
    rows = total // SEQ
    pick = (lambda p: p[2]) if own else (lambda p: 1 - p[2])
    by_group = lambda r, m, p: (r, pick(p))
    by_row = lambda r, m, p: (r, 0)
    whole = lambda r, m, p: (0, 0)
    in_specs = [
        pl.BlockSpec((LANES, SEQ), lambda r, m, p: (pick(p), r)),
        pl.BlockSpec((LANES, SEQ), lambda r, m, p: (pick(p), r)),
        pl.BlockSpec((SEQ, LANES), by_group),
        pl.BlockSpec((LANES, SEQ), lambda r, m, p: (pick(p), r)),
        pl.BlockSpec((LANES, SEQ), lambda r, m, p: (pick(p), r)),
        pl.BlockSpec((1, 8, SEQ), lambda r, m, p: (pick(p), 0, r)),
        pl.BlockSpec((1, 1, 2, HALF, GROUP * HALF), lambda r, m, p: (r, pick(p), 0, 0, 0)),
        pl.BlockSpec((D, SEQ), lambda r, m, p: (0, r)),
        pl.BlockSpec((D, SEQ), lambda r, m, p: (0, r)),
        pl.BlockSpec((D, 3 * D), whole),
        pl.BlockSpec((D, LANES), lambda r, m, p: (0, pick(p))),
    ] + [pl.BlockSpec((SEQ, D), by_row)] * len(more)
    return pl.pallas_call(
        functools.partial(pull_kernel, own),
        out_shape=(
            jax.ShapeDtypeStruct((total, D), F32),
            jax.ShapeDtypeStruct((VDP, VCHIP, D // VDP, LANES), BF16),
            jax.ShapeDtypeStruct((8, LANES), F32),
        ),
        grid_spec=pltpu.PrefetchScalarGridSpec(
            num_scalar_prefetch=2,
            grid=(rows,),
            in_specs=in_specs,
            out_specs=[
                pl.BlockSpec((SEQ, D), by_row),
                pl.BlockSpec((VDP, VCHIP, D // VDP, LANES), lambda r, m, p: (0, 0, 0, 0)),
                pl.BlockSpec((8, LANES), whole),
            ],
            scratch_shapes=[
                pltpu.VMEM((8, SEQ), F32),
                pltpu.VMEM((LANES, SEQ), F32),
                pltpu.VMEM((D, 3 * LANES), F32),
                pltpu.VMEM((8, LANES), F32),
                pltpu.VMEM((2, LANES, GROUP * HALF), BF16),
                pltpu.VMEM((2, LANES, GROUP * HALF), BF16),
                pltpu.VMEM((2, GROUP * HALF, LANES), BF16),
                pltpu.VMEM((LANES, SEQ), BF16),
                pltpu.VMEM((2, HALF, GROUP * HALF), BF16),
                pltpu.VMEM((2, HALF, QBLOCK), F32),
            ],
        ),
        compiler_params=params(dimension_semantics=("arbitrary",)),
        cost_estimate=pl.CostEstimate(
            flops=18_000_000_000, bytes_accessed=15_000_000, transcendentals=0
        ),
        name="attend_back",
    )(marks, place, grad_t, query_t, value, key_t, out_t, inverse, exps, qk_t, x_t, weight, proj, *more)


def sums_by_group(place, sums_own, sums_other):
    first = place[2] == 0
    return (
        jnp.where(first, sums_own, sums_other),
        jnp.where(first, sums_other, sums_own),
    )


def tail_send_kernel(
    place, mine_ref, got_ref, vector_ref, own_ref, other_ref, ffn_ref, send_ref, grad_ref
):
    tall = D // VDP
    low, high = sums_by_group(place, own_ref[...], other_ref[...])
    vector = jnp.concatenate(
        [
            vector_ref[:8, :],
            jnp.concatenate([low[:2], high[:2]], axis=1),
            vector_ref[10:, :],
        ],
        axis=0,
    )
    rows = VEC // VDP
    for d in range(VDP):
        for c in range(VCHIP):
            at = d * VCHIP + c
            both = mine_ref[d, c].astype(F32) + got_ref[d, c].astype(F32)
            send_ref[at, :tall, :] = both.astype(BF16)
            part = vector[d * rows : (d + 1) * rows, c * 64 : (c + 1) * 64]
            part = jnp.concatenate([part, jnp.zeros((rows, LANES - 64), F32)], axis=1)
            part = jnp.concatenate([part, jnp.zeros((VROWS - rows, LANES), F32)], axis=0)
            send_ref[at, tall:, :] = part.astype(BF16)
    for kind in range(2):
        total = ffn_ref[0, kind].astype(F32)
        for at in range(1, VDP * VCHIP):
            total = total + ffn_ref[at, kind].astype(F32)
        grad_ref[kind] = total


def column_to_row(columns, rows):
    lane = iota((rows, LANES), 1)
    wide = jnp.zeros((rows, LANES), F32)
    for i, column in enumerate(columns):
        wide = jnp.where(lane == i, column, wide)
    return wide.T[:8, :]


def tail_stats_kernel(
    place, got_ref, ffn_grad_ref, attn_ref, first_ref, second_ref, rows_0, rows_1, rows_2, vector_ref, grad_ref, send_ref
):
    tall = attn_ref.shape[0]
    rows = vector_ref.shape[0]
    total = got_ref[0, :tall, :].astype(F32)
    part = got_ref[0, tall : tall + rows, :].astype(F32)
    for at in range(1, got_ref.shape[0]):
        total = total + got_ref[at, :tall, :].astype(F32)
        part = part + got_ref[at, tall : tall + rows, :].astype(F32)
    grad_ref[...] = total
    grads = [total, ffn_grad_ref[0], ffn_grad_ref[1]]
    squares = [grad * grad + EPS_ONE for grad in grads]
    piece = []
    for square in squares:
        down = jnp.sum(square, axis=0, keepdims=True)
        for i in range(down.shape[1] // LANES):
            piece.append(down[:, i * LANES : (i + 1) * LANES])
    across = column_to_row([jnp.sum(square, axis=1, keepdims=True) for square in squares], tall)[:3]
    piece.append(jnp.concatenate([across, jnp.zeros((3, LANES - tall), F32)], axis=1))
    lane = iota((1, LANES), 1)
    scalars = jnp.zeros((1, LANES), F32)
    for i, ref in enumerate((attn_ref, first_ref, second_ref)):
        weight = ref[...]
        down = jnp.sum(weight * weight, axis=0, keepdims=True)
        scalars = jnp.where(lane == i, jnp.sum(down, axis=1, keepdims=True), scalars)
    for i, ref in enumerate((rows_0, rows_1, rows_2)):
        scalars = jnp.where(lane == 3 + i, jnp.sum(ref[...], axis=1, keepdims=True), scalars)
    piece.append(scalars)
    piece.append(jnp.zeros((3, LANES), F32))
    vector = vector_ref[...]
    power = jnp.sum(vector * vector, axis=1, keepdims=True)
    piece.append(jnp.where(iota((rows, LANES), 1) < 64, part, power))
    piece = jnp.concatenate(piece, axis=0)
    for at in range(send_ref.shape[0]):
        send_ref[at] = piece


def tail_update_kernel(
    place,
    got_ref,
    grad_ref,
    ffn_grad_ref,
    rows_0,
    rows_1,
    rows_2,
    cols_0,
    cols_1,
    cols_2,
    moment_ref,
    update_0,
    update_1,
    update_2,
    rows_out,
    cols_out_0,
    cols_out_1,
    cols_out_2,
    vector_grad_ref,
    moment_out,
    step_ref,
    kept_ref,
    send_ref,
):
    decay = 1.0 - STEP ** (-0.8)
    dp, chip, core = place[0], place[1], place[2]
    fsdp = 2 * VCHIP
    tall = grad_ref.shape[0]
    lane = iota((1, LANES), 1)
    mine = jnp.zeros((3, LANES), F32)
    every = jnp.zeros((3, LANES), F32)
    for f in range(fsdp):
        mine = mine + got_ref[pl.ds(dp * fsdp + f, 1), 5:8, :][0]
        for d in range(VDP):
            every = every + got_ref[d * fsdp + f, 5:8, :]
    down = jnp.zeros((5, LANES), F32)
    for d in range(VDP):
        down = down + got_ref[pl.ds(d * fsdp + chip * 2 + core, 1), 0:5, :][0]
    scalars = jnp.zeros((1, LANES), F32)
    olds = jnp.zeros((1, LANES), F32)
    for d in range(VDP):
        olds = olds + got_ref[d * fsdp, 8:9, :]
        for f in range(fsdp):
            scalars = scalars + got_ref[d * fsdp + f, 8:9, :]
    grads = [grad_ref[...], ffn_grad_ref[0], ffn_grad_ref[1]]
    downs = [
        down[0:1],
        jnp.concatenate([down[1:2], down[2:3]], axis=1),
        jnp.concatenate([down[3:4], down[4:5]], axis=1),
    ]
    row_total = tall * VDP
    new_rows, means = [], []
    for i, ref in enumerate((rows_0, rows_1, rows_2)):
        width = grads[i].shape[1] * fsdp
        new_rows.append(decay * ref[...] + (1.0 - decay) * (mine[i : i + 1, :tall] / width))
        old = jnp.sum(jnp.where(lane == 3 + i, olds, 0.0), axis=1, keepdims=True)
        fresh = jnp.sum(every[i : i + 1], axis=1, keepdims=True)
        means.append((decay * old + (1.0 - decay) * (fresh / width)) / row_total)
    tile = jnp.concatenate(new_rows + [jnp.zeros((5, tall), F32)], axis=0)
    rows_out[...] = tile
    tile = jnp.concatenate([tile, jnp.zeros((8, LANES - tall), F32)], axis=1)
    turned = jnp.concatenate([tile, jnp.zeros((LANES - 8, LANES), F32)], axis=0).T
    powers = jnp.zeros((1, LANES), F32)
    for i, (ref, out, to) in enumerate(
        ((cols_0, cols_out_0, update_0), (cols_1, cols_out_1, update_1), (cols_2, cols_out_2, update_2))
    ):
        cols = decay * ref[...] + (1.0 - decay) * (downs[i] / row_total)
        out[...] = cols
        second = turned[:tall, i : i + 1] * cols / means[i]
        update = grads[i] * lax.rsqrt(second)
        to[...] = update
        power = jnp.sum(jnp.sum(update * update, axis=0, keepdims=True), axis=1, keepdims=True)
        powers = jnp.where(lane == i, power, powers)
    rows, width = moment_ref.shape
    pair = dp * fsdp + chip * 2
    both = got_ref[pl.ds(pair, 1), 12 : 12 + rows, :][0] + got_ref[pl.ds(pair + 1, 1), 12 : 12 + rows, :][0]
    vector_grad = jnp.where(core == 0, both[:, :width], both[:, width : 2 * width])
    vector_grad_ref[...] = vector_grad
    moment = decay * moment_ref[...] + (1.0 - decay) * (vector_grad * vector_grad + EPS_ONE)
    moment_out[...] = moment
    step = vector_grad * lax.rsqrt(moment)
    step_ref[...] = step
    weight_rows = jnp.zeros((rows, LANES), F32)
    weight_bias = jnp.zeros((rows, LANES), F32)
    for f in range(fsdp):
        weight_rows = weight_rows + got_ref[pl.ds(dp * fsdp + f, 1), 12 : 12 + rows, :][0]
        for d in range(VDP // 2):
            weight_bias = weight_bias + got_ref[d * fsdp + f, 12 : 12 + rows, :]
    bias = jnp.sum(weight_bias, axis=0, keepdims=True)
    kept_ref[...] = jnp.concatenate([scalars, bias, jnp.zeros((2, LANES), F32), weight_rows], axis=0)
    power = jnp.broadcast_to(jnp.sum(step * step, axis=1, keepdims=True), (rows, LANES))
    piece = jnp.concatenate([powers, jnp.zeros((3, LANES), F32), power], axis=0)
    for at in range(send_ref.shape[0]):
        send_ref[at] = piece


def tail_apply_kernel(
    place,
    got_ref,
    kept_ref,
    update_0,
    update_1,
    update_2,
    weight_0,
    weight_1,
    weight_2,
    step_ref,
    vector_ref,
    new_0,
    new_1,
    new_2,
    vector_out,
):
    dp = place[0]
    fsdp = 2 * VCHIP
    rows = vector_ref.shape[0]
    lane = iota((1, LANES), 1)
    total = got_ref[0]
    for at in range(1, VDP * fsdp):
        total = total + got_ref[at]
    for i, (update, weight, new) in enumerate(
        ((update_0, weight_0, new_0), (update_1, weight_1, new_1), (update_2, weight_2, new_2))
    ):
        entries = float(weight.shape[0] * weight.shape[1] * VDP * fsdp)
        power = jnp.sum(jnp.where(lane == i, total[0:1], 0.0), axis=1, keepdims=True)
        size = jnp.sum(jnp.where(lane == i, kept_ref[0:1, :], 0.0), axis=1, keepdims=True)
        clip = jnp.maximum(1.0, jnp.sqrt(power / entries) / CLIP_LIMIT)
        rate = STEP_RATE * jnp.maximum(EPS_TWO, jnp.sqrt(size / entries))
        new[...] = weight[...] - rate / clip * update[...]
    mine = jnp.zeros((rows, LANES), F32)
    bias = jnp.zeros((rows, LANES), F32)
    for f in range(fsdp):
        mine = mine + got_ref[pl.ds(dp * fsdp + f, 1), 4 : 4 + rows, :][0]
        for d in range(VDP // 2):
            bias = bias + got_ref[d * fsdp + f, 4 : 4 + rows, :]
    is_bias = dp < VDP // 2
    power = jnp.where(is_bias, jnp.sum(bias, axis=0, keepdims=True), mine)[:, 64:65]
    size = jnp.where(is_bias, kept_ref[1:2, :], kept_ref[4 : 4 + rows, :])[:, 64:65]
    count = jnp.where(is_bias, float(FF), float(D))
    clip = jnp.maximum(1.0, jnp.sqrt(power / count) / CLIP_LIMIT)
    rate = STEP_RATE * jnp.maximum(EPS_TWO, jnp.sqrt(size / count))
    vector_out[...] = vector_ref[...] - rate / clip * step_ref[...]


def whole_call(kernel, name, place, outs, *operands):
    return pl.pallas_call(
        kernel,
        out_shape=[jax.ShapeDtypeStruct(shape, kind) for shape, kind in outs],
        in_specs=[pl.BlockSpec(memory_space=pltpu.SMEM)] + [vspec()] * len(operands),
        out_specs=[vspec()] * len(outs),
        compiler_params=params(),
        name=name,
    )(place, *operands)


def core_swap(block):
    return lax.ppermute(block, "core", [(0, 1), (1, 0)])


def exchange(blocks, axes):
    return lax.all_to_all(blocks, axes, split_axis=0, concat_axis=0, tiled=True)


def after(value, *earlier):
    return pl.pallas_call(
        lambda *refs: None,
        out_shape=jax.ShapeDtypeStruct(value.shape, value.dtype),
        in_specs=[pl.BlockSpec(memory_space=pl.ANY)] * (1 + len(earlier)),
        out_specs=pl.BlockSpec(memory_space=pl.ANY),
        input_output_aliases={0: 0},
        name="after",
    )(value, *earlier)


def pair_kernel(mine_ref, got_ref, out_ref):
    out_ref[...] = (mine_ref[...].astype(F32) + got_ref[...].astype(F32)).astype(BF16)


def pair_sum(mine, got):
    return pl.pallas_call(
        pair_kernel,
        out_shape=jax.ShapeDtypeStruct(mine.shape, BF16),
        in_specs=[vspec(), vspec()],
        out_specs=vspec(),
        compiler_params=params(16),
        name="pair_sum",
    )(mine, got)


CHIPS = ("dp", "chip")
ALL = ("dp", "chip", "core")


def layer(place, weights, segment_ids, tokens, cotangent, ffn_weights, send_core, send_ffn):
    table = jnp.asarray(encode_table())
    qk, x, qk_t, x_t, back, marks = place_tokens(segment_ids, tokens, cotangent, table)
    query_t, value, key_t, out_t, inverse, mixed, mixed_t, exps, weight, proj, vector = attend_forward(
        marks, place, x, qk, x_t, qk_t, *weights
    )
    ffn_mine, ffn_other = ffn_weights(marks, vector)
    block_out, resid, grad_t, ffn_mine, ffn_other, proj_g, vector_g = feed_forward(
        marks, place, x, back, mixed, mixed_t, proj, ffn_mine, ffn_other, vector
    )
    ffn_got, grad_t = send_ffn(ffn_mine, ffn_other, grad_t)
    shared = (marks, place, grad_t, query_t, value, key_t, out_t, inverse, exps, qk_t, x_t, weight, proj_g)
    pulled, grads_other, sums_other = attend_back(False, *shared)
    attn_got = send_core(grads_other)
    input_grad, grads_own, sums_own = attend_back(True, *shared, resid, pulled)
    return block_out, input_grad, grads_own, grads_other, attn_got, sums_own, sums_other, vector_g, ffn_got


def body(
    tokens,
    cotangent,
    segment_ids,
    attn_weight,
    ffn_in,
    ffn_out,
    vectors,
    attn_rows,
    attn_cols,
    in_rows,
    in_cols,
    out_rows,
    out_cols,
    vector_moment,
):
    place = jnp.stack([lax.axis_index("dp"), lax.axis_index("chip"), lax.axis_index("core")])
    place = place.astype(jnp.int32)
    pieces = VDP * VCHIP
    tall, wide = attn_weight.shape
    rows_v, cols_v = vectors.shape
    split = lambda array: array.reshape((VDP, VCHIP) + array.shape[1:])
    attn_sent, ffn_sent = pack(place, attn_weight, ffn_in, ffn_out, vectors)
    attn_mine = split(exchange(attn_sent, CHIPS))
    weights = (attn_mine, core_swap(attn_mine))

    def ffn_weights(marks, vector):
        got = split(exchange(after(ffn_sent, attn_mine, marks), CHIPS))
        ffn_mine = after(got, vector)
        return ffn_mine, core_swap(ffn_mine)

    def send_ffn(mine, other, grad_t):
        both = pair_sum(mine, core_swap(other))
        got = exchange(both.reshape((pieces,) + mine.shape[2:]), CHIPS)
        return got, after(grad_t, both)

    (
        block_out,
        input_grad,
        grads_own,
        grads_other,
        attn_got,
        sums_own,
        sums_other,
        vector_g,
        ffn_got,
    ) = layer(place, weights, segment_ids, tokens, cotangent, ffn_weights, core_swap, send_ffn)
    sent, ffn_grad = whole_call(
        tail_send_kernel,
        "tail_send",
        place,
        [((pieces, tall + VROWS, LANES), BF16), ((2,) + ffn_in.shape, F32)],
        grads_own,
        attn_got,
        vector_g,
        sums_own,
        sums_other,
        ffn_got,
    )
    got = exchange(sent, CHIPS)
    lay = lambda stat: stat.reshape(1, -1)
    rows_old = (lay(attn_rows), lay(in_rows), lay(out_rows))
    cols_old = (lay(attn_cols), lay(in_cols), lay(out_cols))
    attn_grad, sent = whole_call(
        tail_stats_kernel,
        "tail_stats",
        place,
        [(attn_weight.shape, F32), ((2 * pieces, 16, LANES), F32)],
        got,
        ffn_grad,
        attn_weight,
        ffn_in,
        ffn_out,
        *rows_old,
        vectors,
    )
    got = exchange(sent, ALL)
    (
        update_0,
        update_1,
        update_2,
        rows_new,
        cols_new_0,
        cols_new_1,
        cols_new_2,
        vector_grad,
        moment_new,
        step,
        kept,
        sent,
    ) = whole_call(
        tail_update_kernel,
        "tail_update",
        place,
        [
            (attn_weight.shape, F32),
            (ffn_in.shape, F32),
            (ffn_out.shape, F32),
            ((8, tall), F32),
            (cols_old[0].shape, F32),
            (cols_old[1].shape, F32),
            (cols_old[2].shape, F32),
            (vectors.shape, F32),
            (vectors.shape, F32),
            (vectors.shape, F32),
            ((8, LANES), F32),
            ((2 * pieces, 8, LANES), F32),
        ],
        got,
        attn_grad,
        ffn_grad,
        *rows_old,
        *cols_old,
        vector_moment,
    )
    got = exchange(sent, ALL)
    attn_new, in_new, out_new, vectors_new = whole_call(
        tail_apply_kernel,
        "tail_apply",
        place,
        [(attn_weight.shape, F32), (ffn_in.shape, F32), (ffn_out.shape, F32), (vectors.shape, F32)],
        got,
        kept,
        update_0,
        update_1,
        update_2,
        attn_weight,
        ffn_in,
        ffn_out,
        step,
        vectors,
    )
    return (
        block_out,
        input_grad,
        attn_grad,
        ffn_grad[0],
        ffn_grad[1],
        vector_grad,
        rows_new[0],
        cols_new_0.reshape(-1),
        rows_new[1],
        cols_new_1.reshape(-1),
        rows_new[2],
        cols_new_2.reshape(-1),
        moment_new,
        attn_new,
        in_new,
        out_new,
        vectors_new,
    )


def gather_all(block):
    shape = (lax.axis_size("dp"), lax.axis_size("chip") * 2)
    count = shape[0] * shape[1]
    got = exchange(jnp.broadcast_to(block[None], (count,) + block.shape), ALL)
    return got.reshape(shape + block.shape)


def unblock(parts):
    dp_count, fsdp_count, rows, cols = parts.shape
    return parts.transpose(0, 2, 1, 3).reshape(dp_count * rows, fsdp_count * cols)


def scatter_sum(full):
    dp_count = lax.axis_size("dp")
    fsdp_count = lax.axis_size("chip") * 2
    rows, cols = full.shape
    by_col = full.astype(BF16).reshape(rows, fsdp_count, cols // fsdp_count).transpose(1, 0, 2)
    got = exchange(by_col, ("chip", "core"))
    part = jnp.sum(got.astype(F32), axis=0).astype(BF16)
    by_row = part.reshape(dp_count, rows // dp_count, cols // fsdp_count)
    return jnp.sum(exchange(by_row, "dp").astype(F32), axis=0)


def body_any(
    tokens,
    cotangent,
    segment_ids,
    attn_weight,
    ffn_in,
    ffn_out,
    vectors,
    attn_rows,
    attn_cols,
    in_rows,
    in_cols,
    out_rows,
    out_cols,
    vector_moment,
):
    dp_count = lax.axis_size("dp")
    fsdp_count = lax.axis_size("chip") * 2
    dp_place = lax.axis_index("dp")
    fsdp_place = lax.axis_index("chip") * 2 + lax.axis_index("core")
    rows_w = attn_weight.shape[0]
    rows_v = vectors.shape[0]
    place = jnp.zeros((3,), jnp.int32)
    full_attn = unblock(gather_all(attn_weight.astype(BF16)))
    full_vector = unblock(gather_all(vectors.astype(BF16)))
    full_ffn = jnp.stack(
        [unblock(gather_all(ffn_in.astype(BF16))), unblock(gather_all(ffn_out.astype(BF16)))]
    )
    tall = D // VDP
    cut = full_attn.reshape(VDP, tall, VCHIP, 2, LANES).transpose(3, 0, 2, 1, 4)
    lines = full_vector.reshape(VDP, VEC // VDP, 2, LANES).transpose(0, 2, 1, 3)
    lines = lines.reshape(VDP, 1, 2 * VEC // VDP, LANES)
    lines = jnp.pad(lines, ((0, 0), (0, VCHIP - 1), (0, VROWS - 2 * VEC // VDP), (0, 0)))
    weights = (
        jnp.concatenate([cut[0], lines], axis=2),
        jnp.concatenate([cut[1], jnp.zeros_like(lines)], axis=2),
    )
    ffn_cut = full_ffn.reshape(2, VDP, tall, VCHIP, 2, FF // (2 * VCHIP))
    ffn_cut = ffn_cut.transpose(4, 1, 3, 0, 2, 5)
    (
        block_out,
        input_grad,
        grads_own,
        grads_other,
        _,
        sums_own,
        sums_other,
        vector_g,
        ffn_got,
    ) = layer(
        place,
        weights,
        segment_ids,
        tokens,
        cotangent,
        lambda marks, vector: (ffn_cut[0], ffn_cut[1]),
        lambda block: block,
        lambda mine, other, grad_t: (jnp.stack([mine, other]), grad_t),
    )
    attn_full = jnp.stack([grads_own, grads_other]).transpose(1, 3, 2, 0, 4).reshape(D, 4 * D)
    ffn_full = ffn_got.transpose(3, 1, 4, 2, 0, 5).reshape(2, D, FF)
    sums = jnp.concatenate([sums_own[:2], sums_other[:2]], axis=1)
    vector_full = jnp.concatenate([vector_g[:8], sums, vector_g[10:]], axis=0)
    attn_grad = scatter_sum(attn_full)
    in_grad = scatter_sum(ffn_full[0])
    out_grad = scatter_sum(ffn_full[1])
    vector_grad = scatter_sum(vector_full)

    decay = 1.0 - STEP ** (-0.8)
    gradients = (attn_grad, in_grad, out_grad)
    weights_old = (attn_weight, ffn_in, ffn_out)
    rows_old = (attn_rows, in_rows, out_rows)
    cols_old = (attn_cols, in_cols, out_cols)
    moment_new = decay * vector_moment + (1.0 - decay) * (vector_grad * vector_grad + EPS_ONE)
    vector_step = vector_grad * lax.rsqrt(moment_new)
    squares = [gradient * gradient + EPS_ONE for gradient in gradients]
    pieces = []
    for square in squares:
        pieces.append(jnp.sum(square, axis=1))
    for square in squares:
        pieces.append(jnp.sum(square, axis=0))
    pieces.append(jnp.sum(vector_step * vector_step, axis=1))
    pieces.append(jnp.sum(vectors * vectors, axis=1))
    pieces.append(jnp.stack([jnp.sum(weight * weight) for weight in weights_old]))
    pieces.append(jnp.stack([jnp.sum(old) for old in rows_old]))
    sizes = [piece.shape[0] for piece in pieces]
    flat = jnp.concatenate(pieces)
    flat = jnp.pad(flat, (0, -flat.shape[0] % 1024)).reshape(-1, LANES)
    got = gather_all(flat).reshape(dp_count, fsdp_count, -1)
    offsets = [0]
    for length in sizes:
        offsets.append(offsets[-1] + length)
    take = lambda i: got[:, :, offsets[i] : offsets[i + 1]]
    rows_new, cols_new, row_means, entries = [], [], [], []
    for i in range(3):
        count_rows = rows_w * dp_count
        count_cols = weights_old[i].shape[1] * fsdp_count
        entries.append(float(count_rows * count_cols))
        row_all = jnp.sum(take(i), axis=1)
        mine = lax.dynamic_index_in_dim(row_all, dp_place, 0, keepdims=False)
        rows_new.append(decay * rows_old[i] + (1.0 - decay) * mine / count_cols)
        col_all = jnp.sum(take(3 + i), axis=0)
        mine = lax.dynamic_index_in_dim(col_all, fsdp_place, 0, keepdims=False)
        cols_new.append(decay * cols_old[i] + (1.0 - decay) * mine / count_rows)
        old_total = jnp.sum(take(9)[:, 0, i])
        row_means.append(
            (decay * old_total + (1.0 - decay) * jnp.sum(row_all) / count_cols) / count_rows
        )
    step_rows = jnp.sum(take(6), axis=1).reshape(-1)
    weight_rows = jnp.sum(take(7), axis=1).reshape(-1)
    weight_totals = jnp.sum(take(8), axis=(0, 1))
    updates = []
    for i in range(3):
        second = rows_new[i][:, None] * cols_new[i][None, :] / row_means[i]
        updates.append(gradients[i] * lax.rsqrt(second))
    flat = jnp.stack([jnp.sum(update * update) for update in updates])
    flat = jnp.broadcast_to(jnp.pad(flat, (0, 5))[:, None], (8, LANES))
    totals = jnp.sum(gather_all(flat)[:, :, :, 0], axis=(0, 1))
    new_weights = []
    for i in range(3):
        clip_factor = jnp.maximum(1.0, jnp.sqrt(totals[i] / entries[i]) / CLIP_LIMIT)
        step_size = STEP_RATE * jnp.maximum(EPS_TWO, jnp.sqrt(weight_totals[i] / entries[i]))
        new_weights.append(weights_old[i] - step_size / clip_factor * updates[i])
    bias_rows = FF // D
    row_places = jnp.arange(VEC)
    counts = jnp.where(row_places < bias_rows, float(FF), float(D))
    grouped_updates = jnp.where(row_places < bias_rows, jnp.sum(step_rows[:bias_rows]), step_rows)
    grouped_weights = jnp.where(row_places < bias_rows, jnp.sum(weight_rows[:bias_rows]), weight_rows)
    clip_rows = jnp.maximum(1.0, jnp.sqrt(grouped_updates / counts) / CLIP_LIMIT)
    step_sizes = STEP_RATE * jnp.maximum(EPS_TWO, jnp.sqrt(grouped_weights / counts))
    factor_rows = lax.dynamic_slice_in_dim(step_sizes / clip_rows, dp_place * rows_v, rows_v)
    vectors_new = vectors - factor_rows[:, None] * vector_step
    return (
        block_out,
        input_grad,
        attn_grad,
        in_grad,
        out_grad,
        vector_grad,
        rows_new[0],
        cols_new[0],
        rows_new[1],
        cols_new[1],
        rows_new[2],
        cols_new[2],
        moment_new,
        new_weights[0],
        new_weights[1],
        new_weights[2],
        vectors_new,
    )


def solution(mesh):
    dp_count, fsdp_count = mesh.shape["dp"], mesh.shape["fsdp"]
    inner = jax.sharding.Mesh(mesh.devices.reshape(dp_count, fsdp_count // 2, 2), ALL)
    fsdp = ("chip", "core")
    split = P(ALL, None)
    block = P("dp", fsdp)
    stats = (P("dp"), P(fsdp)) * 3
    plain = dp_count == VDP and fsdp_count == 2 * VCHIP
    return jax.shard_map(
        body if plain else body_any,
        mesh=inner,
        in_specs=(split,) * 3 + (block,) * 4 + stats + (block,),
        out_specs=(split,) * 2 + (block,) * 4 + stats + (block,) * 5,
        check_vma=False,
    )
```

```python
import functools
import math

import jax
import jax.numpy as jnp
import numpy as np
from jax import lax
from jax.experimental import pallas as pl
from jax.experimental.pallas import tpu as pltpu
from jax.sharding import PartitionSpec as P

D = 256
FF = 2048
HEADS = 8
HEAD_DIM = 32
SEQ = 1024
HALF = 512
GROUP = 4
LANES = 128
QBLOCK = 256
WGRID = 32
STEP = 10
VEC = 16
TILE = 512
CHUNK = 512
SUB = 256
LEAD = 4
STRIP = 64
VDP = 4
VCHIP = 4
VROWS = 16

EPS_NORM = 1e-05
EPS_ONE = 1e-30
EPS_TWO = 0.001
CLIP_LIMIT = 1.0
STEP_RATE = 0.3
FAR = 1e30
LOG2_E = math.log2(math.e)
SCALE = HEAD_DIM ** (-0.5)
GELU_A = math.sqrt(2.0 / math.pi)
GELU_B = 0.044715
F32 = jnp.float32
BF16 = jnp.bfloat16
MIB = 1024 * 1024


def dot(left, right):
    return jnp.dot(left, right, preferred_element_type=F32)


def dot_nt(left, right):
    return lax.dot_general(left, right, (((1,), (1,)), ((), ())), preferred_element_type=F32)


def encode_table():
    half = D // 2
    feature = np.arange(half)
    freq = np.exp(
        (2 * (feature // 2)).astype(np.float32) * np.float32(-math.log(10000.0) / half)
    ).astype(np.float32)
    angles = np.arange(1, WGRID + 1, dtype=np.float32)[:, None] * freq[None, :]
    table = np.where(feature % 2 == 0, np.sin(angles), np.cos(angles)).astype(np.float32)
    low = jnp.bfloat16
    one = table.astype(low)
    rest = table - one.astype(np.float32)
    two = rest.astype(low)
    three = (rest - two.astype(np.float32)).astype(low)
    blank = np.zeros((LANES - 3 * WGRID, half), low)
    return np.concatenate([one, two, three, blank], axis=0)


def iota(shape, dim):
    return lax.broadcasted_iota(jnp.int32, shape, dim)


def norm_forward(rows):
    centered = rows - jnp.mean(rows, axis=-1, keepdims=True)
    inverse = lax.rsqrt(jnp.mean(centered * centered, axis=-1, keepdims=True) + EPS_NORM)
    return centered * inverse, inverse


def norm_backward(upstream, normed, inverse):
    return inverse * (
        upstream
        - jnp.mean(upstream, axis=-1, keepdims=True)
        - normed * jnp.mean(upstream * normed, axis=-1, keepdims=True)
    )

def vspec():
    return pl.BlockSpec(memory_space=pltpu.VMEM)


def params(mib=56, **more):
    return pltpu.CompilerParams(vmem_limit_bytes=mib * MIB, **more)


def pack_kernel(place, attn_ref, first_ref, second_ref, vector_ref, attn_out, ffn_out):
    owner = place[1] * 2 + place[2]
    vector = vector_ref[...]
    rows = vector.shape[0]
    wide = jnp.concatenate([vector] * (LANES // vector.shape[1]), axis=1)
    slot = iota((rows, LANES), 1) // vector.shape[1]
    per = LANES // vector.shape[1]
    parts = [attn_ref[...]]
    for half in range(2):
        parts.append(jnp.where(slot + half * per == owner, wide, 0.0))
    parts.append(jnp.zeros((VROWS - 2 * rows, LANES), F32))
    piece = jnp.concatenate(parts, axis=0).astype(BF16)
    first = first_ref[...].astype(BF16)
    second = second_ref[...].astype(BF16)
    for at in range(VDP * VCHIP):
        attn_out[at] = piece
        ffn_out[at, 0] = first
        ffn_out[at, 1] = second


def pack(place, attn_weight, ffn_in, ffn_out, vectors):
    count = VDP * VCHIP
    return pl.pallas_call(
        pack_kernel,
        out_shape=(
            jax.ShapeDtypeStruct((count, attn_weight.shape[0] + VROWS, LANES), BF16),
            jax.ShapeDtypeStruct((count, 2) + ffn_in.shape, BF16),
        ),
        in_specs=[pl.BlockSpec(memory_space=pltpu.SMEM)] + [vspec()] * 4,
        out_specs=(vspec(), vspec()),
        compiler_params=params(),
        name="pack",
    )(place, attn_weight, ffn_in, ffn_out, vectors)


def place_kernel(
    segment_ref, tokens_ref, back_ref, table_ref, qk_ref, x_ref, qk_t_ref, x_t_ref, turned_ref, marks_ref
):
    row = pl.program_id(0)
    starts = []
    for number in range(1, 4):
        at = jnp.int32(0)
        for step in (512, 256, 128, 64, 32, 16, 8, 4, 2, 1, 1):
            probe = jnp.minimum(at + (step - 1), SEQ - 1)
            at = jnp.where(segment_ref[row, probe] < number, at + step, at)
        starts.append(at)
    edges = [jnp.int32(0)] + starts + [jnp.int32(SEQ)]
    begin = jnp.int32(0)
    for number in range(3, -1, -1):
        begin = jnp.where(edges[number + 1] - edges[number] == HALF, edges[number], begin)
    for number in range(3):
        marks_ref[row, number] = starts[number]
    marks_ref[row, 3] = begin
    one, two, three = starts
    x = pltpu.roll(tokens_ref[...].astype(F32), (SEQ - begin) & (SEQ - 1), 0)
    x_ref[...] = x.astype(BF16)
    x_t_ref[...] = x.T.astype(BF16)
    back = back_ref[...].astype(F32)
    turned_ref[...] = pltpu.roll(back, (SEQ - begin) & (SEQ - 1), 0).astype(BF16)
    at = (iota((SEQ, LANES), 0) + begin) & (SEQ - 1)
    lane = iota((SEQ, LANES), 1)
    start = jnp.where(at >= three, three, jnp.where(at >= two, two, jnp.where(at >= one, one, 0)))
    local = at - start
    kept = lane < 3 * WGRID
    slot = lane & (WGRID - 1)
    hot_r = jnp.where(((local >> 5) == slot) & kept, 1.0, 0.0).astype(BF16)
    hot_c = jnp.where(((local & (WGRID - 1)) == slot) & kept, 1.0, 0.0).astype(BF16)
    table = table_ref[...]
    places = jnp.concatenate([dot(hot_r, table), dot(hot_c, table)], axis=1)
    qk = x + places
    qk_ref[...] = qk.astype(BF16)
    qk_t_ref[...] = qk.T.astype(BF16)


def place_tokens(segment_ids, tokens, cotangent, table):
    rows = segment_ids.shape[0]
    by_row = lambda r: (r, 0)
    return pl.pallas_call(
        place_kernel,
        out_shape=(
            jax.ShapeDtypeStruct(tokens.shape, BF16),
            jax.ShapeDtypeStruct(tokens.shape, BF16),
            jax.ShapeDtypeStruct((D, tokens.shape[0]), BF16),
            jax.ShapeDtypeStruct((D, tokens.shape[0]), BF16),
            jax.ShapeDtypeStruct(tokens.shape, BF16),
            jax.ShapeDtypeStruct((rows, 4), jnp.int32),
        ),
        grid=(rows,),
        in_specs=[
            pl.BlockSpec(memory_space=pltpu.SMEM),
            pl.BlockSpec((SEQ, D), by_row),
            pl.BlockSpec((SEQ, D), by_row),
            pl.BlockSpec((LANES, LANES), lambda r: (0, 0)),
        ],
        out_specs=(
            pl.BlockSpec((SEQ, D), by_row),
            pl.BlockSpec((SEQ, D), by_row),
            pl.BlockSpec((D, SEQ), lambda r: (0, r)),
            pl.BlockSpec((D, SEQ), lambda r: (0, r)),
            pl.BlockSpec((SEQ, D), by_row),
            pl.BlockSpec(memory_space=pltpu.SMEM),
        ),
        compiler_params=params(dimension_semantics=("arbitrary",)),
        cost_estimate=pl.CostEstimate(flops=600_000_000, bytes_accessed=4_000_000, transcendentals=0),
        name="place_tokens",
    )(segment_ids, tokens, cotangent, table)


def attend_kernel(
    marks,
    place,
    x_ref,
    qk_ref,
    x_t_ref,
    qk_t_ref,
    mine_ref,
    other_ref,
    query_t_ref,
    value_ref,
    key_t_ref,
    out_t_ref,
    inverse_ref,
    mixed_ref,
    mixed_t_ref,
    exps_ref,
    weight_ref,
    proj_ref,
    vector_ref,
    key_s,
    value_s,
    mark_k,
    mark_q,
    scores_s,
    weight_t_s,
    bias_s,
):
    row = pl.program_id(0)
    group = pl.program_id(1)
    begin = marks[row, 3]
    core = place[2]

    @pl.when((row == 0) & (group == 0))
    def _():
        tall = D // VDP
        for d in range(VDP):
            rows = slice(d * tall, (d + 1) * tall)
            total = jnp.zeros((8, LANES), F32)
            for c in range(VCHIP):
                for ref, half in ((mine_ref, core), (other_ref, 1 - core)):
                    if c < 3:
                        to = pl.ds(pl.multiple_of(c * D + half * LANES, LANES), LANES)
                        weight_ref[rows, to] = ref[d, c, :tall, :]
                    else:
                        to = pl.ds(pl.multiple_of(half * LANES, LANES), LANES)
                        proj_ref[rows, to] = ref[d, c, :tall, :]
                    total += ref[d, c, tall : tall + 8, :].astype(F32)
            vector_ref[d * 4 : (d + 1) * 4, :LANES] = total[:4]
            vector_ref[d * 4 : (d + 1) * 4, LANES:] = total[4:]
        weight_t_s[...] = weight_ref[...].astype(F32).T.astype(BF16)
        bias_s[...] = vector_ref[8:16, :].T

    @pl.when(group == 0)
    def _():
        qk_t = qk_t_ref[...]
        query_t = (dot(weight_t_s[:D, :], qk_t) + bias_s[:, 0:1]) * SCALE
        query_t_ref[...] = query_t.astype(BF16)
        key_t_ref[...] = dot(weight_t_s[D : 2 * D, :], qk_t).astype(BF16)
        key_s[...] = dot(qk_ref[...], weight_ref[:, D : 2 * D]).astype(BF16)
        value = dot(x_ref[...], weight_ref[:, 2 * D : 3 * D]) + vector_ref[9:10, :]
        value_ref[...] = value.astype(BF16)
        value_t = dot(weight_t_s[2 * D :, :], x_t_ref[...]) + bias_s[:, 1:2]
        value_t = value_t.astype(BF16)
        for head in range(HEADS):
            value_s[head, :HEAD_DIM, :] = value_t[head * HEAD_DIM : (head + 1) * HEAD_DIM, :]
            value_s[head, HEAD_DIM:, :] = jnp.ones((16, SEQ), BF16)
        one, two, three = marks[row, 0], marks[row, 1], marks[row, 2]

        def number_of(shape, dim):
            here = (iota(shape, dim) + (HALF + begin)) & (SEQ - 1)
            return (
                jnp.where(here >= one, 1, 0)
                + jnp.where(here >= two, 1, 0)
                + jnp.where(here >= three, 1, 0)
            )

        lane = iota((HALF, LANES), 1)
        number = number_of((HALF, LANES), 0)
        mark_k[...] = jnp.where((number != lane) & (lane < 4), -FAR, 0.0).astype(BF16)
        number = number_of((LANES, HALF), 1)
        mark_q[...] = jnp.where(number == iota((LANES, HALF), 0), 1.0, 0.0).astype(BF16)

    lanes = pl.ds(pl.multiple_of(group * LANES, LANES), LANES)
    head_of = iota((1, LANES), 1) // HEAD_DIM

    def scores_of(item):
        half, at_head, block = item
        mask = jnp.where(head_of == at_head, 1.0, 0.0).astype(BF16)
        key_m = key_s[half * HALF : (half + 1) * HALF, lanes] * mask
        at = half * HALF + block * QBLOCK
        query = query_t_ref[lanes, at : at + QBLOCK]
        if half == 1:
            key_m = jnp.concatenate([key_m, mark_k[...]], axis=1)
            query = jnp.concatenate(
                [query, mark_q[:, block * QBLOCK : (block + 1) * QBLOCK]], axis=0
            )
        return dot(key_m, query)

    def exps_of(item, slot):
        half, at_head, block = item
        cols = slice(at_head * HALF + block * QBLOCK, at_head * HALF + (block + 1) * QBLOCK)
        largest = scores_s[slot, :STRIP, :]
        for at in range(STRIP, HALF, STRIP):
            largest = jnp.maximum(largest, scores_s[slot, at : at + STRIP, :])
        largest = jnp.max(largest, axis=0, keepdims=True)
        for at in range(0, HALF, STRIP):
            exps = jnp.exp2((scores_s[slot, at : at + STRIP, :] - largest) * LOG2_E)
            exps_ref[0, 0, half, at : at + STRIP, cols] = exps.astype(BF16)

    def finish(item):
        half, at_head, block = item
        at = half * HALF + block * QBLOCK
        rows = slice(half * HALF, (half + 1) * HALF)
        cols = slice(at_head * HALF + block * QBLOCK, at_head * HALF + (block + 1) * QBLOCK)
        out = dot(value_s[group * GROUP + at_head, :, rows], exps_ref[0, 0, half, :, cols])
        inverse = 1.0 / out[HEAD_DIM : HEAD_DIM + 1, :]
        inverse_ref[0, at_head : at_head + 1, at : at + QBLOCK] = inverse
        out_t_ref[at_head * HEAD_DIM : (at_head + 1) * HEAD_DIM, at : at + QBLOCK] = (
            out[:HEAD_DIM, :] * inverse
        )

    items = [
        (half, at_head, block)
        for half in range(2)
        for at_head in range(GROUP)
        for block in range(HALF // QBLOCK)
    ]
    for i in range(len(items) + 2):
        if i < len(items):
            scores_s[i % 2] = scores_of(items[i])
        if 1 <= i <= len(items):
            exps_of(items[i - 1], (i - 1) % 2)
        if i >= 2:
            finish(items[i - 2])
    out_t = out_t_ref[...]
    mixed_t_ref[...] = out_t.astype(BF16)
    mixed_ref[...] = out_t.T.astype(BF16)


def attend_forward(marks, place, x, qk, x_t, qk_t, mine, other):
    total = x.shape[0]
    rows = total // SEQ
    by_row = lambda r, g, m, p: (r, 0)
    by_col = lambda r, g, m, p: (0, r)
    by_both = lambda r, g, m, p: (g, r)
    whole = lambda r, g, m, p: (0, 0)
    return pl.pallas_call(
        attend_kernel,
        out_shape=(
            jax.ShapeDtypeStruct((D, total), BF16),
            jax.ShapeDtypeStruct((total, D), BF16),
            jax.ShapeDtypeStruct((D, total), BF16),
            jax.ShapeDtypeStruct((D, total), F32),
            jax.ShapeDtypeStruct((2, 8, total), F32),
            jax.ShapeDtypeStruct((total, D), BF16),
            jax.ShapeDtypeStruct((D, total), BF16),
            jax.ShapeDtypeStruct((rows, 2, 2, HALF, GROUP * HALF), BF16),
            jax.ShapeDtypeStruct((D, 3 * D), BF16),
            jax.ShapeDtypeStruct((D, D), BF16),
            jax.ShapeDtypeStruct((VEC, D), F32),
        ),
        grid_spec=pltpu.PrefetchScalarGridSpec(
            num_scalar_prefetch=2,
            grid=(rows, 2),
            in_specs=[
                pl.BlockSpec((SEQ, D), by_row),
                pl.BlockSpec((SEQ, D), by_row),
                pl.BlockSpec((D, SEQ), by_col),
                pl.BlockSpec((D, SEQ), by_col),
                vspec(),
                vspec(),
            ],
            out_specs=[
                pl.BlockSpec((D, SEQ), by_col),
                pl.BlockSpec((SEQ, D), by_row),
                pl.BlockSpec((D, SEQ), by_col),
                pl.BlockSpec((LANES, SEQ), by_both),
                pl.BlockSpec((1, 8, SEQ), lambda r, g, m, p: (g, 0, r)),
                pl.BlockSpec((SEQ, LANES), lambda r, g, m, p: (r, g)),
                pl.BlockSpec((LANES, SEQ), by_both),
                pl.BlockSpec((1, 1, 2, HALF, GROUP * HALF), lambda r, g, m, p: (r, g, 0, 0, 0)),
                pl.BlockSpec((D, 3 * D), whole),
                pl.BlockSpec((D, D), whole),
                pl.BlockSpec((VEC, D), whole),
            ],
            scratch_shapes=[
                pltpu.VMEM((SEQ, D), BF16),
                pltpu.VMEM((HEADS, HEAD_DIM + 16, SEQ), BF16),
                pltpu.VMEM((HALF, LANES), BF16),
                pltpu.VMEM((LANES, HALF), BF16),
                pltpu.VMEM((2, HALF, QBLOCK), F32),
                pltpu.VMEM((3 * D, D), BF16),
                pltpu.VMEM((D, 8), F32),
            ],
        ),
        compiler_params=params(dimension_semantics=("arbitrary", "arbitrary")),
        cost_estimate=pl.CostEstimate(
            flops=20_000_000_000, bytes_accessed=30_000_000, transcendentals=8_400_000
        ),
        name="attend_forward",
    )(marks, place, x, qk, x_t, qk_t, mine, other)


def feed_kernel(
    marks,
    place,
    x_ref,
    back_ref,
    mixed_ref,
    mixed_t_ref,
    proj_ref,
    mine_ref,
    other_ref,
    vector_ref,
    block_ref,
    resid_ref,
    mixed_grad_ref,
    mine_out,
    other_out,
    proj_out,
    vector_out,
    first_w,
    second_w,
    first_acc,
    second_acc,
    proj_acc,
    vector_acc,
    hidden_s,
    slope_s,
    pre_s,
    work_s,
    first_low_s,
    branch_low_s,
    attended_s,
    block_s,
    eye_s,
):
    step = pl.program_id(0)
    core = place[2]
    tall = D // VDP
    wide = FF // (2 * VCHIP)

    @pl.when(step == 0)
    def _():
        first_acc[...] = jnp.zeros_like(first_acc)
        second_acc[...] = jnp.zeros_like(second_acc)
        proj_acc[...] = jnp.zeros_like(proj_acc)
        vector_acc[...] = jnp.zeros_like(vector_acc)
        eye_s[...] = jnp.where(iota((D, D), 0) == iota((D, D), 1), 1.0, 0.0).astype(BF16)
        for d in range(VDP):
            rows = slice(d * tall, (d + 1) * tall)
            for c in range(VCHIP):
                for ref, half in ((mine_ref, core), (other_ref, 1 - core)):
                    to = pl.ds(pl.multiple_of((2 * c + half) * wide, wide), wide)
                    first_w[rows, to] = ref[d, c, 0]
                    second_w[rows, to] = ref[d, c, 1]

    bias_o, bias_2 = vector_ref[10:11, :], vector_ref[11:12, :]
    gain_1, shift_1 = vector_ref[12:13, :], vector_ref[13:14, :]
    gain_2, shift_2 = vector_ref[14:15, :], vector_ref[15:16, :]
    at_row = pl.multiple_of((step % (SEQ // TILE)) * TILE, TILE)
    per = CHUNK // D
    chunks = FF // CHUNK

    def columns(at):
        return slice(at * CHUNK, (at + 1) * CHUNK)

    def hidden_of(rows_at, at, slot):
        for side in range(per):
            bias = vector_ref[at * per + side : at * per + side + 1, :]
            cols = slice(at * CHUNK + side * D, at * CHUNK + (side + 1) * D)
            for top in range(0, SUB, STRIP):
                rows = slice(rows_at + top, rows_at + top + STRIP)
                pre = work_s[slot, top : top + STRIP, side * D : (side + 1) * D] + bias
                pre = pre.astype(BF16)
                cube = BF16(GELU_A * GELU_B) * (pre * pre)
                gate = BF16(0.5) + BF16(0.5) * jnp.tanh(pre * (cube + BF16(GELU_A)))
                hidden_s[rows, cols] = pre * gate
                slope_s[rows, cols] = gate + (gate - gate * gate) * (
                    pre * (BF16(6.0) * cube + BF16(2.0 * GELU_A))
                )

    def pre_grad_of(rows_at, at, slot):
        for side in range(per):
            cols = slice(at * CHUNK + side * D, at * CHUNK + (side + 1) * D)
            for top in range(0, SUB, STRIP):
                rows = slice(rows_at + top, rows_at + top + STRIP)
                pull = work_s[slot, top : top + STRIP, side * D : (side + 1) * D]
                pre_s[rows, cols] = pull.astype(BF16) * slope_s[rows, cols]

    def stages(sub):
        rows_at = sub * SUB
        rows = slice(rows_at, rows_at + SUB)
        slots = (2 * sub, 2 * sub + 1)
        attended = dot(mixed_ref[rows, :], proj_ref[...]) + bias_o
        norm_1, inverse_1 = norm_forward(x_ref[rows, :].astype(F32) + attended)
        first = norm_1 * gain_1 + shift_1
        first_low = first.astype(BF16)
        first_low_s[rows, :] = first_low
        yield
        branch = jnp.zeros((SUB, D), F32)
        for i in range(chunks + 2):
            if i < chunks:
                work_s[slots[i % 2]] = dot(first_low, first_w[:, columns(i)])
            if 1 <= i <= chunks:
                hidden_of(rows_at, i - 1, slots[(i - 1) % 2])
            if i >= 2:
                cols = columns(i - 2)
                branch += dot_nt(hidden_s[rows, cols], second_w[:, cols])
            yield
        norm_2, inverse_2 = norm_forward(first + (branch + bias_2))
        block_s[pl.ds(at_row + rows_at, SUB), :] = norm_2 * gain_2 + shift_2
        back = back_ref[rows, :].astype(F32)
        vector_acc[14:15, :] += jnp.sum(back * norm_2, axis=0, keepdims=True)
        vector_acc[15:16, :] += jnp.sum(back, axis=0, keepdims=True)
        resid_2 = norm_backward(back * gain_2, norm_2, inverse_2)
        branch_low = resid_2.astype(BF16)
        branch_low_s[rows, :] = branch_low
        vector_acc[11:12, :] += jnp.sum(branch_low.astype(F32), axis=0, keepdims=True)
        yield
        first_back = resid_2
        if sub == 1:
            branch_t = dot_nt(eye_s[...], branch_low_s[...]).astype(BF16)
            first_t = dot_nt(eye_s[...], first_low_s[...]).astype(BF16)
            first_t = jnp.concatenate([first_t, jnp.ones((16, TILE), BF16)], axis=0)
        for i in range(chunks + 2):
            if i < chunks:
                work_s[slots[i % 2]] = dot(branch_low, second_w[:, columns(i)])
                if sub == 1:
                    second_acc[:, columns(i)] += dot(branch_t, hidden_s[:, columns(i)])
            if 1 <= i <= chunks:
                pre_grad_of(rows_at, i - 1, slots[(i - 1) % 2])
            if i >= 2:
                cols = columns(i - 2)
                first_back += dot_nt(pre_s[rows, cols], first_w[:, cols])
                if sub == 1:
                    first_acc[:, cols] += dot(first_t, pre_s[:, cols])
            yield
        vector_acc[12:13, :] += jnp.sum(first_back * norm_1, axis=0, keepdims=True)
        vector_acc[13:14, :] += jnp.sum(first_back, axis=0, keepdims=True)
        resid_1 = norm_backward(first_back * gain_1, norm_1, inverse_1)
        resid_ref[rows, :] = resid_1
        attended_low = resid_1.astype(BF16)
        attended_s[rows, :] = attended_low
        vector_acc[10:11, :] += jnp.sum(attended_low.astype(F32), axis=0, keepdims=True)
        mixed_grad_ref[:, rows] = dot_nt(proj_ref[...], attended_low).astype(BF16)
        yield

    ahead, behind = stages(0), stages(1)
    for _ in range(LEAD):
        next(ahead)
    running = [ahead, behind]
    while running:
        for program in list(running):
            if next(program, 0) == 0:
                running.remove(program)
    proj_acc[...] += dot(mixed_t_ref[...], attended_s[...])

    @pl.when(step % (SEQ // TILE) == SEQ // TILE - 1)
    def _():
        block_ref[...] = pltpu.roll(block_s[...], marks[step // (SEQ // TILE), 3], 0)

    @pl.when(step == pl.num_programs(0) - 1)
    def _():
        for d in range(VDP):
            rows = slice(d * tall, (d + 1) * tall)
            for c in range(VCHIP):
                for ref, half in ((mine_out, core), (other_out, 1 - core)):
                    to = pl.ds(pl.multiple_of((2 * c + half) * wide, wide), wide)
                    ref[d, c, 0] = first_acc[rows, to].astype(BF16)
                    ref[d, c, 1] = second_acc[rows, to].astype(BF16)
        proj_out[...] = proj_acc[...]
        for at in range(FF // D):
            vector_out[at : at + 1, :] = first_acc[D : D + 1, at * D : (at + 1) * D]
        vector_out[FF // D :, :] = vector_acc[FF // D :, :]


def feed_forward(marks, place, x, back, mixed, mixed_t, proj, mine, other, vector):
    total = x.shape[0]
    tile = lambda i, m, p: (i, 0)
    by_col = lambda i, m, p: (0, i)
    whole = lambda i, m, p: (0, 0)
    whole5 = lambda i, m, p: (0, 0, 0, 0, 0)
    return pl.pallas_call(
        feed_kernel,
        out_shape=(
            jax.ShapeDtypeStruct((total, D), F32),
            jax.ShapeDtypeStruct((total, D), F32),
            jax.ShapeDtypeStruct((D, total), BF16),
            jax.ShapeDtypeStruct(mine.shape, BF16),
            jax.ShapeDtypeStruct(mine.shape, BF16),
            jax.ShapeDtypeStruct((D, D), F32),
            jax.ShapeDtypeStruct((VEC, D), F32),
        ),
        grid_spec=pltpu.PrefetchScalarGridSpec(
            num_scalar_prefetch=2,
            grid=(total // TILE,),
            in_specs=[
                pl.BlockSpec((TILE, D), tile),
                pl.BlockSpec((TILE, D), tile),
                pl.BlockSpec((TILE, D), tile),
                pl.BlockSpec((D, TILE), by_col),
                pl.BlockSpec((D, D), whole),
                vspec(),
                vspec(),
                pl.BlockSpec((VEC, D), whole),
            ],
            out_specs=[
                pl.BlockSpec((SEQ, D), lambda i, m, p: (i // (SEQ // TILE), 0)),
                pl.BlockSpec((TILE, D), tile),
                pl.BlockSpec((D, TILE), by_col),
                pl.BlockSpec(mine.shape, whole5),
                pl.BlockSpec(mine.shape, whole5),
                pl.BlockSpec((D, D), whole),
                pl.BlockSpec((VEC, D), whole),
            ],
            scratch_shapes=[
                pltpu.VMEM((D, FF), BF16),
                pltpu.VMEM((D, FF), BF16),
                pltpu.VMEM((D + 16, FF), F32),
                pltpu.VMEM((D, FF), F32),
                pltpu.VMEM((D, D), F32),
                pltpu.VMEM((VEC, D), F32),
                pltpu.VMEM((TILE, FF), BF16),
                pltpu.VMEM((TILE, FF), BF16),
                pltpu.VMEM((TILE, FF), BF16),
                pltpu.VMEM((4, SUB, CHUNK), F32),
                pltpu.VMEM((TILE, D), BF16),
                pltpu.VMEM((TILE, D), BF16),
                pltpu.VMEM((TILE, D), BF16),
                pltpu.VMEM((SEQ, D), F32),
                pltpu.VMEM((D, D), BF16),
            ],
        ),
        compiler_params=params(dimension_semantics=("arbitrary",)),
        cost_estimate=pl.CostEstimate(
            flops=14_000_000_000, bytes_accessed=15_000_000, transcendentals=4_200_000
        ),
        name="feed_forward",
    )(marks, place, x, back, mixed, mixed_t, proj, mine, other, vector)


def pull_kernel(
    own,
    marks,
    place,
    grad_t_ref,
    query_t_ref,
    value_ref,
    key_t_ref,
    out_t_ref,
    inverse_ref,
    exps_ref,
    qk_t_ref,
    x_t_ref,
    weight_ref,
    proj_ref,
    *refs,
):
    if own:
        resid_ref, other_ref, pulled_ref, grads_ref, sums_ref = refs[:5]
    else:
        pulled_ref, grads_ref, sums_ref = refs[:3]
    dot_s, query_t_s, acc, sum_acc, scaled_s, query_s, value_s, scaled_t_s, score_s, work_s = refs[-10:]
    row = pl.program_id(0)
    begin = marks[row, 3]
    group = place[2] if own else 1 - place[2]

    @pl.when(row == 0)
    def _():
        acc[...] = jnp.zeros_like(acc)
        sum_acc[...] = jnp.zeros_like(sum_acc)

    grad_t = grad_t_ref[...].astype(F32)
    scaled_s[...] = jnp.zeros_like(scaled_s)
    query_s[...] = jnp.zeros_like(query_s)
    head_of = iota((1, LANES), 1) // HEAD_DIM
    for at_head in range(GROUP):
        heads = slice(at_head * HEAD_DIM, (at_head + 1) * HEAD_DIM)
        part = grad_t[heads, :] * inverse_ref[0, at_head : at_head + 1, :]
        dot_s[at_head : at_head + 1, :] = jnp.sum(part * out_t_ref[heads, :], axis=0, keepdims=True)
        part = part.astype(BF16)
        scaled_t_s[heads, :] = part
        mask = jnp.where(head_of == at_head, 1.0, 0.0).astype(BF16)
        for half in range(2):
            rows = slice(half * HALF, (half + 1) * HALF)
            to = slice(at_head * HALF, (at_head + 1) * HALF)
            scaled_s[half, heads, to] = part[:, rows]
            query_s[half, heads, to] = query_t_ref[heads, rows]
            value_s[half, to, :] = value_ref[rows, :] * mask
    key_parts = [jnp.zeros((HALF, LANES), F32) for _ in range(2)]
    value_parts = [jnp.zeros((HALF, LANES), F32) for _ in range(2)]

    def pull_of(item):
        half, at_head, block = item
        at = half * HALF + block * QBLOCK
        value = value_s[half, at_head * HALF : (at_head + 1) * HALF, :]
        return dot(value, scaled_t_s[:, at : at + QBLOCK])

    def score_grad_of(item, slot):
        half, at_head, block = item
        at = half * HALF + block * QBLOCK
        cols = slice(at_head * HALF + block * QBLOCK, at_head * HALF + (block + 1) * QBLOCK)
        shift = dot_s[at_head : at_head + 1, at : at + QBLOCK]
        for top in range(0, HALF, STRIP):
            rows = slice(top, top + STRIP)
            pull = (work_s[slot, rows, :] - shift).astype(BF16)
            score_s[half, rows, cols] = exps_ref[0, 0, half, rows, cols] * pull

    def finish(half, at_head):
        cols = slice(at_head * HALF, (at_head + 2) * HALF)
        rows = slice(half * HALF, (half + 1) * HALF)
        value_parts[half] += dot_nt(exps_ref[0, 0, half, :, cols], scaled_s[half, :, cols])
        key_parts[half] += dot_nt(score_s[half, :, cols], query_s[half, :, cols])
        for head in range(at_head, at_head + 2):
            heads = slice(head * HEAD_DIM, (head + 1) * HEAD_DIM)
            query_t_s[heads, rows] = dot(
                key_t_ref[heads, rows], score_s[half, :, head * HALF : (head + 1) * HALF]
            )

    items = [
        (half, at_head, block)
        for half in range(2)
        for at_head in range(GROUP)
        for block in range(HALF // QBLOCK)
    ]
    for i in range(len(items) + 1):
        if i < len(items):
            work_s[i % 2] = pull_of(items[i])
        if i >= 1:
            score_grad_of(items[i - 1], (i - 1) % 2)
            if i % 4 == 0:
                half, at_head, _ = items[i - 1]
                finish(half, at_head - 1)
    query_low = query_t_s[...].T.astype(BF16)
    key_low = jnp.concatenate(key_parts, axis=0).astype(BF16)
    value_low = jnp.concatenate(value_parts, axis=0).astype(BF16)
    sum_acc[0:1, :] += jnp.sum(query_low.astype(F32), axis=0, keepdims=True) * SCALE
    sum_acc[1:2, :] += jnp.sum(value_low.astype(F32), axis=0, keepdims=True)
    qk_t = qk_t_ref[...]
    x_t = x_t_ref[...]
    acc[:, :LANES] += dot(qk_t, query_low) * SCALE
    acc[:, LANES : 2 * LANES] += dot(qk_t, key_low)
    acc[:, 2 * LANES :] += dot(x_t, value_low)
    at = [pl.ds(pl.multiple_of(i * D + group * LANES, LANES), LANES) for i in range(3)]
    pulled = dot_nt(query_low, weight_ref[:, at[0]]) * SCALE + dot_nt(
        jnp.concatenate([key_low, value_low], axis=1),
        jnp.concatenate([weight_ref[:, at[1]], weight_ref[:, at[2]]], axis=1),
    )
    if own:
        pulled_ref[...] = pltpu.roll(resid_ref[...] + (pulled + other_ref[...]), begin, 0)
    else:
        pulled_ref[...] = pulled

    @pl.when(row == pl.num_programs(0) - 1)
    def _():
        tall = D // VDP
        for d in range(VDP):
            rows = slice(d * tall, (d + 1) * tall)
            for c in range(3):
                grads_ref[d, c] = acc[rows, c * LANES : (c + 1) * LANES].astype(BF16)
            grads_ref[d, 3] = proj_ref[rows, :].astype(BF16)
        sums_ref[...] = sum_acc[...]


def attend_back(own, marks, place, grad_t, query_t, value, key_t, out_t, inverse, exps, qk_t, x_t, weight, proj, *more):
    total = value.shape[0]
    rows = total // SEQ
    pick = (lambda p: p[2]) if own else (lambda p: 1 - p[2])
    by_group = lambda r, m, p: (r, pick(p))
    by_row = lambda r, m, p: (r, 0)
    whole = lambda r, m, p: (0, 0)
    in_specs = [
        pl.BlockSpec((LANES, SEQ), lambda r, m, p: (pick(p), r)),
        pl.BlockSpec((LANES, SEQ), lambda r, m, p: (pick(p), r)),
        pl.BlockSpec((SEQ, LANES), by_group),
        pl.BlockSpec((LANES, SEQ), lambda r, m, p: (pick(p), r)),
        pl.BlockSpec((LANES, SEQ), lambda r, m, p: (pick(p), r)),
        pl.BlockSpec((1, 8, SEQ), lambda r, m, p: (pick(p), 0, r)),
        pl.BlockSpec((1, 1, 2, HALF, GROUP * HALF), lambda r, m, p: (r, pick(p), 0, 0, 0)),
        pl.BlockSpec((D, SEQ), lambda r, m, p: (0, r)),
        pl.BlockSpec((D, SEQ), lambda r, m, p: (0, r)),
        pl.BlockSpec((D, 3 * D), whole),
        pl.BlockSpec((D, LANES), lambda r, m, p: (0, pick(p))),
    ] + [pl.BlockSpec((SEQ, D), by_row)] * len(more)
    return pl.pallas_call(
        functools.partial(pull_kernel, own),
        out_shape=(
            jax.ShapeDtypeStruct((total, D), F32),
            jax.ShapeDtypeStruct((VDP, VCHIP, D // VDP, LANES), BF16),
            jax.ShapeDtypeStruct((8, LANES), F32),
        ),
        grid_spec=pltpu.PrefetchScalarGridSpec(
            num_scalar_prefetch=2,
            grid=(rows,),
            in_specs=in_specs,
            out_specs=[
                pl.BlockSpec((SEQ, D), by_row),
                pl.BlockSpec((VDP, VCHIP, D // VDP, LANES), lambda r, m, p: (0, 0, 0, 0)),
                pl.BlockSpec((8, LANES), whole),
            ],
            scratch_shapes=[
                pltpu.VMEM((8, SEQ), F32),
                pltpu.VMEM((LANES, SEQ), F32),
                pltpu.VMEM((D, 3 * LANES), F32),
                pltpu.VMEM((8, LANES), F32),
                pltpu.VMEM((2, LANES, GROUP * HALF), BF16),
                pltpu.VMEM((2, LANES, GROUP * HALF), BF16),
                pltpu.VMEM((2, GROUP * HALF, LANES), BF16),
                pltpu.VMEM((LANES, SEQ), BF16),
                pltpu.VMEM((2, HALF, GROUP * HALF), BF16),
                pltpu.VMEM((2, HALF, QBLOCK), F32),
            ],
        ),
        compiler_params=params(dimension_semantics=("arbitrary",)),
        cost_estimate=pl.CostEstimate(
            flops=18_000_000_000, bytes_accessed=15_000_000, transcendentals=0
        ),
        name="attend_back",
    )(marks, place, grad_t, query_t, value, key_t, out_t, inverse, exps, qk_t, x_t, weight, proj, *more)


def sums_by_group(place, sums_own, sums_other):
    first = place[2] == 0
    return (
        jnp.where(first, sums_own, sums_other),
        jnp.where(first, sums_other, sums_own),
    )


def tail_send_kernel(
    place, mine_ref, got_ref, vector_ref, own_ref, other_ref, ffn_ref, send_ref, grad_ref
):
    tall = D // VDP
    low, high = sums_by_group(place, own_ref[...], other_ref[...])
    vector = jnp.concatenate(
        [
            vector_ref[:8, :],
            jnp.concatenate([low[:2], high[:2]], axis=1),
            vector_ref[10:, :],
        ],
        axis=0,
    )
    rows = VEC // VDP
    for d in range(VDP):
        for c in range(VCHIP):
            at = d * VCHIP + c
            both = mine_ref[d, c].astype(F32) + got_ref[d, c].astype(F32)
            send_ref[at, :tall, :] = both.astype(BF16)
            part = vector[d * rows : (d + 1) * rows, c * 64 : (c + 1) * 64]
            part = jnp.concatenate([part, jnp.zeros((rows, LANES - 64), F32)], axis=1)
            part = jnp.concatenate([part, jnp.zeros((VROWS - rows, LANES), F32)], axis=0)
            send_ref[at, tall:, :] = part.astype(BF16)
    for kind in range(2):
        total = ffn_ref[0, kind].astype(F32)
        for at in range(1, VDP * VCHIP):
            total = total + ffn_ref[at, kind].astype(F32)
        grad_ref[kind] = total


def column_to_row(columns, rows):
    lane = iota((rows, LANES), 1)
    wide = jnp.zeros((rows, LANES), F32)
    for i, column in enumerate(columns):
        wide = jnp.where(lane == i, column, wide)
    return wide.T[:8, :]


def tail_stats_kernel(
    place, got_ref, ffn_grad_ref, attn_ref, first_ref, second_ref, rows_0, rows_1, rows_2, vector_ref, grad_ref, send_ref
):
    tall = attn_ref.shape[0]
    rows = vector_ref.shape[0]
    total = got_ref[0, :tall, :].astype(F32)
    part = got_ref[0, tall : tall + rows, :].astype(F32)
    for at in range(1, got_ref.shape[0]):
        total = total + got_ref[at, :tall, :].astype(F32)
        part = part + got_ref[at, tall : tall + rows, :].astype(F32)
    grad_ref[...] = total
    grads = [total, ffn_grad_ref[0], ffn_grad_ref[1]]
    squares = [grad * grad + EPS_ONE for grad in grads]
    piece = []
    for square in squares:
        down = jnp.sum(square, axis=0, keepdims=True)
        for i in range(down.shape[1] // LANES):
            piece.append(down[:, i * LANES : (i + 1) * LANES])
    across = column_to_row([jnp.sum(square, axis=1, keepdims=True) for square in squares], tall)[:3]
    piece.append(jnp.concatenate([across, jnp.zeros((3, LANES - tall), F32)], axis=1))
    lane = iota((1, LANES), 1)
    scalars = jnp.zeros((1, LANES), F32)
    for i, ref in enumerate((attn_ref, first_ref, second_ref)):
        weight = ref[...]
        down = jnp.sum(weight * weight, axis=0, keepdims=True)
        scalars = jnp.where(lane == i, jnp.sum(down, axis=1, keepdims=True), scalars)
    for i, ref in enumerate((rows_0, rows_1, rows_2)):
        scalars = jnp.where(lane == 3 + i, jnp.sum(ref[...], axis=1, keepdims=True), scalars)
    piece.append(scalars)
    piece.append(jnp.zeros((3, LANES), F32))
    vector = vector_ref[...]
    power = jnp.sum(vector * vector, axis=1, keepdims=True)
    piece.append(jnp.where(iota((rows, LANES), 1) < 64, part, power))
    piece = jnp.concatenate(piece, axis=0)
    for at in range(send_ref.shape[0]):
        send_ref[at] = piece


def tail_update_kernel(
    place,
    got_ref,
    grad_ref,
    ffn_grad_ref,
    rows_0,
    rows_1,
    rows_2,
    cols_0,
    cols_1,
    cols_2,
    moment_ref,
    update_0,
    update_1,
    update_2,
    rows_out,
    cols_out_0,
    cols_out_1,
    cols_out_2,
    vector_grad_ref,
    moment_out,
    step_ref,
    kept_ref,
    send_ref,
):
    decay = 1.0 - STEP ** (-0.8)
    dp, chip, core = place[0], place[1], place[2]
    fsdp = 2 * VCHIP
    tall = grad_ref.shape[0]
    lane = iota((1, LANES), 1)
    mine = jnp.zeros((3, LANES), F32)
    every = jnp.zeros((3, LANES), F32)
    for f in range(fsdp):
        mine = mine + got_ref[pl.ds(dp * fsdp + f, 1), 5:8, :][0]
        for d in range(VDP):
            every = every + got_ref[d * fsdp + f, 5:8, :]
    down = jnp.zeros((5, LANES), F32)
    for d in range(VDP):
        down = down + got_ref[pl.ds(d * fsdp + chip * 2 + core, 1), 0:5, :][0]
    scalars = jnp.zeros((1, LANES), F32)
    olds = jnp.zeros((1, LANES), F32)
    for d in range(VDP):
        olds = olds + got_ref[d * fsdp, 8:9, :]
        for f in range(fsdp):
            scalars = scalars + got_ref[d * fsdp + f, 8:9, :]
    grads = [grad_ref[...], ffn_grad_ref[0], ffn_grad_ref[1]]
    downs = [
        down[0:1],
        jnp.concatenate([down[1:2], down[2:3]], axis=1),
        jnp.concatenate([down[3:4], down[4:5]], axis=1),
    ]
    row_total = tall * VDP
    new_rows, means = [], []
    for i, ref in enumerate((rows_0, rows_1, rows_2)):
        width = grads[i].shape[1] * fsdp
        new_rows.append(decay * ref[...] + (1.0 - decay) * (mine[i : i + 1, :tall] / width))
        old = jnp.sum(jnp.where(lane == 3 + i, olds, 0.0), axis=1, keepdims=True)
        fresh = jnp.sum(every[i : i + 1], axis=1, keepdims=True)
        means.append((decay * old + (1.0 - decay) * (fresh / width)) / row_total)
    tile = jnp.concatenate(new_rows + [jnp.zeros((5, tall), F32)], axis=0)
    rows_out[...] = tile
    tile = jnp.concatenate([tile, jnp.zeros((8, LANES - tall), F32)], axis=1)
    turned = jnp.concatenate([tile, jnp.zeros((LANES - 8, LANES), F32)], axis=0).T
    powers = jnp.zeros((1, LANES), F32)
    for i, (ref, out, to) in enumerate(
        ((cols_0, cols_out_0, update_0), (cols_1, cols_out_1, update_1), (cols_2, cols_out_2, update_2))
    ):
        cols = decay * ref[...] + (1.0 - decay) * (downs[i] / row_total)
        out[...] = cols
        second = turned[:tall, i : i + 1] * cols / means[i]
        update = grads[i] * lax.rsqrt(second)
        to[...] = update
        power = jnp.sum(jnp.sum(update * update, axis=0, keepdims=True), axis=1, keepdims=True)
        powers = jnp.where(lane == i, power, powers)
    rows, width = moment_ref.shape
    pair = dp * fsdp + chip * 2
    both = got_ref[pl.ds(pair, 1), 12 : 12 + rows, :][0] + got_ref[pl.ds(pair + 1, 1), 12 : 12 + rows, :][0]
    vector_grad = jnp.where(core == 0, both[:, :width], both[:, width : 2 * width])
    vector_grad_ref[...] = vector_grad
    moment = decay * moment_ref[...] + (1.0 - decay) * (vector_grad * vector_grad + EPS_ONE)
    moment_out[...] = moment
    step = vector_grad * lax.rsqrt(moment)
    step_ref[...] = step
    weight_rows = jnp.zeros((rows, LANES), F32)
    weight_bias = jnp.zeros((rows, LANES), F32)
    for f in range(fsdp):
        weight_rows = weight_rows + got_ref[pl.ds(dp * fsdp + f, 1), 12 : 12 + rows, :][0]
        for d in range(VDP // 2):
            weight_bias = weight_bias + got_ref[d * fsdp + f, 12 : 12 + rows, :]
    bias = jnp.sum(weight_bias, axis=0, keepdims=True)
    kept_ref[...] = jnp.concatenate([scalars, bias, jnp.zeros((2, LANES), F32), weight_rows], axis=0)
    power = jnp.broadcast_to(jnp.sum(step * step, axis=1, keepdims=True), (rows, LANES))
    piece = jnp.concatenate([powers, jnp.zeros((3, LANES), F32), power], axis=0)
    for at in range(send_ref.shape[0]):
        send_ref[at] = piece


def tail_apply_kernel(
    place,
    got_ref,
    kept_ref,
    update_0,
    update_1,
    update_2,
    weight_0,
    weight_1,
    weight_2,
    step_ref,
    vector_ref,
    new_0,
    new_1,
    new_2,
    vector_out,
):
    dp = place[0]
    fsdp = 2 * VCHIP
    rows = vector_ref.shape[0]
    lane = iota((1, LANES), 1)
    total = got_ref[0]
    for at in range(1, VDP * fsdp):
        total = total + got_ref[at]
    for i, (update, weight, new) in enumerate(
        ((update_0, weight_0, new_0), (update_1, weight_1, new_1), (update_2, weight_2, new_2))
    ):
        entries = float(weight.shape[0] * weight.shape[1] * VDP * fsdp)
        power = jnp.sum(jnp.where(lane == i, total[0:1], 0.0), axis=1, keepdims=True)
        size = jnp.sum(jnp.where(lane == i, kept_ref[0:1, :], 0.0), axis=1, keepdims=True)
        clip = jnp.maximum(1.0, jnp.sqrt(power / entries) / CLIP_LIMIT)
        rate = STEP_RATE * jnp.maximum(EPS_TWO, jnp.sqrt(size / entries))
        new[...] = weight[...] - rate / clip * update[...]
    mine = jnp.zeros((rows, LANES), F32)
    bias = jnp.zeros((rows, LANES), F32)
    for f in range(fsdp):
        mine = mine + got_ref[pl.ds(dp * fsdp + f, 1), 4 : 4 + rows, :][0]
        for d in range(VDP // 2):
            bias = bias + got_ref[d * fsdp + f, 4 : 4 + rows, :]
    is_bias = dp < VDP // 2
    power = jnp.where(is_bias, jnp.sum(bias, axis=0, keepdims=True), mine)[:, 64:65]
    size = jnp.where(is_bias, kept_ref[1:2, :], kept_ref[4 : 4 + rows, :])[:, 64:65]
    count = jnp.where(is_bias, float(FF), float(D))
    clip = jnp.maximum(1.0, jnp.sqrt(power / count) / CLIP_LIMIT)
    rate = STEP_RATE * jnp.maximum(EPS_TWO, jnp.sqrt(size / count))
    vector_out[...] = vector_ref[...] - rate / clip * step_ref[...]


def whole_call(kernel, name, place, outs, *operands):
    return pl.pallas_call(
        kernel,
        out_shape=[jax.ShapeDtypeStruct(shape, kind) for shape, kind in outs],
        in_specs=[pl.BlockSpec(memory_space=pltpu.SMEM)] + [vspec()] * len(operands),
        out_specs=[vspec()] * len(outs),
        compiler_params=params(),
        name=name,
    )(place, *operands)


def core_swap(block):
    return lax.ppermute(block, "core", [(0, 1), (1, 0)])


def exchange(blocks, axes):
    return lax.all_to_all(blocks, axes, split_axis=0, concat_axis=0, tiled=True)


def after(value, *earlier):
    return pl.pallas_call(
        lambda *refs: None,
        out_shape=jax.ShapeDtypeStruct(value.shape, value.dtype),
        in_specs=[pl.BlockSpec(memory_space=pltpu.HBM)] * (1 + len(earlier)),
        out_specs=pl.BlockSpec(memory_space=pltpu.HBM),
        input_output_aliases={0: 0},
        compiler_params=params(),
        name="after",
    )(value, *earlier)


def pair_kernel(mine_ref, got_ref, out_ref):
    out_ref[...] = (mine_ref[...].astype(F32) + got_ref[...].astype(F32)).astype(BF16)


def pair_sum(mine, got):
    return pl.pallas_call(
        pair_kernel,
        out_shape=jax.ShapeDtypeStruct(mine.shape, BF16),
        in_specs=[vspec(), vspec()],
        out_specs=vspec(),
        compiler_params=params(),
        name="pair_sum",
    )(mine, got)


CHIPS = ("dp", "chip")
ALL = ("dp", "chip", "core")


def layer(place, weights, segment_ids, tokens, cotangent, ffn_weights, send_core, send_ffn):
    table = jnp.asarray(encode_table())
    qk, x, qk_t, x_t, back, marks = place_tokens(segment_ids, tokens, cotangent, table)
    query_t, value, key_t, out_t, inverse, mixed, mixed_t, exps, weight, proj, vector = attend_forward(
        marks, place, x, qk, x_t, qk_t, *weights(marks)
    )
    ffn_mine, ffn_other = ffn_weights(marks, vector)
    block_out, resid, grad_t, ffn_mine, ffn_other, proj_g, vector_g = feed_forward(
        marks, place, x, back, mixed, mixed_t, proj, ffn_mine, ffn_other, vector
    )
    ffn_got, grad_t = send_ffn(ffn_mine, ffn_other, grad_t)
    shared = (marks, place, grad_t, query_t, value, key_t, out_t, inverse, exps, qk_t, x_t, weight, proj_g)
    pulled, grads_other, sums_other = attend_back(False, *shared)
    attn_got = send_core(grads_other)
    input_grad, grads_own, sums_own = attend_back(True, *shared, resid, pulled)
    return block_out, input_grad, grads_own, grads_other, attn_got, sums_own, sums_other, vector_g, ffn_got


def body(
    tokens,
    cotangent,
    segment_ids,
    attn_weight,
    ffn_in,
    ffn_out,
    vectors,
    attn_rows,
    attn_cols,
    in_rows,
    in_cols,
    out_rows,
    out_cols,
    vector_moment,
):
    place = jnp.stack([lax.axis_index("dp"), lax.axis_index("chip"), lax.axis_index("core")])
    place = place.astype(jnp.int32)
    pieces = VDP * VCHIP
    tall, wide = attn_weight.shape
    rows_v, cols_v = vectors.shape
    split = lambda array: array.reshape((VDP, VCHIP) + array.shape[1:])
    attn_sent, ffn_sent = pack(place, attn_weight, ffn_in, ffn_out, vectors)
    attn_mine = exchange(attn_sent, CHIPS)

    def attn_weights(marks):
        mine = split(after(attn_mine, marks))
        return mine, core_swap(mine)

    def ffn_weights(marks, vector):
        got = split(exchange(after(ffn_sent, attn_mine, marks), CHIPS))
        ffn_mine = after(got, vector)
        return ffn_mine, core_swap(ffn_mine)

    def send_ffn(mine, other, grad_t):
        both = pair_sum(mine, core_swap(other))
        got = exchange(both.reshape((pieces,) + mine.shape[2:]), CHIPS)
        return got, after(grad_t, both)

    (
        block_out,
        input_grad,
        grads_own,
        grads_other,
        attn_got,
        sums_own,
        sums_other,
        vector_g,
        ffn_got,
    ) = layer(place, attn_weights, segment_ids, tokens, cotangent, ffn_weights, core_swap, send_ffn)
    sent, ffn_grad = whole_call(
        tail_send_kernel,
        "tail_send",
        place,
        [((pieces, tall + VROWS, LANES), BF16), ((2,) + ffn_in.shape, F32)],
        grads_own,
        attn_got,
        vector_g,
        sums_own,
        sums_other,
        ffn_got,
    )
    got = exchange(sent, CHIPS)
    lay = lambda stat: stat.reshape(1, -1)
    rows_old = (lay(attn_rows), lay(in_rows), lay(out_rows))
    cols_old = (lay(attn_cols), lay(in_cols), lay(out_cols))
    attn_grad, sent = whole_call(
        tail_stats_kernel,
        "tail_stats",
        place,
        [(attn_weight.shape, F32), ((2 * pieces, 16, LANES), F32)],
        got,
        ffn_grad,
        attn_weight,
        ffn_in,
        ffn_out,
        *rows_old,
        vectors,
    )
    got = exchange(sent, ALL)
    (
        update_0,
        update_1,
        update_2,
        rows_new,
        cols_new_0,
        cols_new_1,
        cols_new_2,
        vector_grad,
        moment_new,
        step,
        kept,
        sent,
    ) = whole_call(
        tail_update_kernel,
        "tail_update",
        place,
        [
            (attn_weight.shape, F32),
            (ffn_in.shape, F32),
            (ffn_out.shape, F32),
            ((8, tall), F32),
            (cols_old[0].shape, F32),
            (cols_old[1].shape, F32),
            (cols_old[2].shape, F32),
            (vectors.shape, F32),
            (vectors.shape, F32),
            (vectors.shape, F32),
            ((8, LANES), F32),
            ((2 * pieces, 8, LANES), F32),
        ],
        got,
        attn_grad,
        ffn_grad,
        *rows_old,
        *cols_old,
        vector_moment,
    )
    got = exchange(sent, ALL)
    attn_new, in_new, out_new, vectors_new = whole_call(
        tail_apply_kernel,
        "tail_apply",
        place,
        [(attn_weight.shape, F32), (ffn_in.shape, F32), (ffn_out.shape, F32), (vectors.shape, F32)],
        got,
        kept,
        update_0,
        update_1,
        update_2,
        attn_weight,
        ffn_in,
        ffn_out,
        step,
        vectors,
    )
    return (
        block_out,
        input_grad,
        attn_grad,
        ffn_grad[0],
        ffn_grad[1],
        vector_grad,
        rows_new[0],
        cols_new_0.reshape(-1),
        rows_new[1],
        cols_new_1.reshape(-1),
        rows_new[2],
        cols_new_2.reshape(-1),
        moment_new,
        attn_new,
        in_new,
        out_new,
        vectors_new,
    )


def gather_all(block):
    shape = (lax.axis_size("dp"), lax.axis_size("chip") * 2)
    count = shape[0] * shape[1]
    got = exchange(jnp.broadcast_to(block[None], (count,) + block.shape), ALL)
    return got.reshape(shape + block.shape)


def unblock(parts):
    dp_count, fsdp_count, rows, cols = parts.shape
    return parts.transpose(0, 2, 1, 3).reshape(dp_count * rows, fsdp_count * cols)


def scatter_sum(full):
    dp_count = lax.axis_size("dp")
    fsdp_count = lax.axis_size("chip") * 2
    rows, cols = full.shape
    by_col = full.astype(BF16).reshape(rows, fsdp_count, cols // fsdp_count).transpose(1, 0, 2)
    got = exchange(by_col, ("chip", "core"))
    part = jnp.sum(got.astype(F32), axis=0).astype(BF16)
    by_row = part.reshape(dp_count, rows // dp_count, cols // fsdp_count)
    return jnp.sum(exchange(by_row, "dp").astype(F32), axis=0)


def body_any(
    tokens,
    cotangent,
    segment_ids,
    attn_weight,
    ffn_in,
    ffn_out,
    vectors,
    attn_rows,
    attn_cols,
    in_rows,
    in_cols,
    out_rows,
    out_cols,
    vector_moment,
):
    dp_count = lax.axis_size("dp")
    fsdp_count = lax.axis_size("chip") * 2
    dp_place = lax.axis_index("dp")
    fsdp_place = lax.axis_index("chip") * 2 + lax.axis_index("core")
    rows_w = attn_weight.shape[0]
    rows_v = vectors.shape[0]
    place = jnp.zeros((3,), jnp.int32)
    full_attn = unblock(gather_all(attn_weight.astype(BF16)))
    full_vector = unblock(gather_all(vectors.astype(BF16)))
    full_ffn = jnp.stack(
        [unblock(gather_all(ffn_in.astype(BF16))), unblock(gather_all(ffn_out.astype(BF16)))]
    )
    tall = D // VDP
    cut = full_attn.reshape(VDP, tall, VCHIP, 2, LANES).transpose(3, 0, 2, 1, 4)
    lines = full_vector.reshape(VDP, VEC // VDP, 2, LANES).transpose(0, 2, 1, 3)
    lines = lines.reshape(VDP, 1, 2 * VEC // VDP, LANES)
    lines = jnp.pad(lines, ((0, 0), (0, VCHIP - 1), (0, VROWS - 2 * VEC // VDP), (0, 0)))
    weights = (
        jnp.concatenate([cut[0], lines], axis=2),
        jnp.concatenate([cut[1], jnp.zeros_like(lines)], axis=2),
    )
    ffn_cut = full_ffn.reshape(2, VDP, tall, VCHIP, 2, FF // (2 * VCHIP))
    ffn_cut = ffn_cut.transpose(4, 1, 3, 0, 2, 5)
    (
        block_out,
        input_grad,
        grads_own,
        grads_other,
        _,
        sums_own,
        sums_other,
        vector_g,
        ffn_got,
    ) = layer(
        place,
        lambda marks: weights,
        segment_ids,
        tokens,
        cotangent,
        lambda marks, vector: (ffn_cut[0], ffn_cut[1]),
        lambda block: block,
        lambda mine, other, grad_t: (jnp.stack([mine, other]), grad_t),
    )
    attn_full = jnp.stack([grads_own, grads_other]).transpose(1, 3, 2, 0, 4).reshape(D, 4 * D)
    ffn_full = ffn_got.transpose(3, 1, 4, 2, 0, 5).reshape(2, D, FF)
    sums = jnp.concatenate([sums_own[:2], sums_other[:2]], axis=1)
    vector_full = jnp.concatenate([vector_g[:8], sums, vector_g[10:]], axis=0)
    attn_grad = scatter_sum(attn_full)
    in_grad = scatter_sum(ffn_full[0])
    out_grad = scatter_sum(ffn_full[1])
    vector_grad = scatter_sum(vector_full)

    decay = 1.0 - STEP ** (-0.8)
    gradients = (attn_grad, in_grad, out_grad)
    weights_old = (attn_weight, ffn_in, ffn_out)
    rows_old = (attn_rows, in_rows, out_rows)
    cols_old = (attn_cols, in_cols, out_cols)
    moment_new = decay * vector_moment + (1.0 - decay) * (vector_grad * vector_grad + EPS_ONE)
    vector_step = vector_grad * lax.rsqrt(moment_new)
    squares = [gradient * gradient + EPS_ONE for gradient in gradients]
    pieces = []
    for square in squares:
        pieces.append(jnp.sum(square, axis=1))
    for square in squares:
        pieces.append(jnp.sum(square, axis=0))
    pieces.append(jnp.sum(vector_step * vector_step, axis=1))
    pieces.append(jnp.sum(vectors * vectors, axis=1))
    pieces.append(jnp.stack([jnp.sum(weight * weight) for weight in weights_old]))
    pieces.append(jnp.stack([jnp.sum(old) for old in rows_old]))
    sizes = [piece.shape[0] for piece in pieces]
    flat = jnp.concatenate(pieces)
    flat = jnp.pad(flat, (0, -flat.shape[0] % 1024)).reshape(-1, LANES)
    got = gather_all(flat).reshape(dp_count, fsdp_count, -1)
    offsets = [0]
    for length in sizes:
        offsets.append(offsets[-1] + length)
    take = lambda i: got[:, :, offsets[i] : offsets[i + 1]]
    rows_new, cols_new, row_means, entries = [], [], [], []
    for i in range(3):
        count_rows = rows_w * dp_count
        count_cols = weights_old[i].shape[1] * fsdp_count
        entries.append(float(count_rows * count_cols))
        row_all = jnp.sum(take(i), axis=1)
        mine = lax.dynamic_index_in_dim(row_all, dp_place, 0, keepdims=False)
        rows_new.append(decay * rows_old[i] + (1.0 - decay) * mine / count_cols)
        col_all = jnp.sum(take(3 + i), axis=0)
        mine = lax.dynamic_index_in_dim(col_all, fsdp_place, 0, keepdims=False)
        cols_new.append(decay * cols_old[i] + (1.0 - decay) * mine / count_rows)
        old_total = jnp.sum(take(9)[:, 0, i])
        row_means.append(
            (decay * old_total + (1.0 - decay) * jnp.sum(row_all) / count_cols) / count_rows
        )
    step_rows = jnp.sum(take(6), axis=1).reshape(-1)
    weight_rows = jnp.sum(take(7), axis=1).reshape(-1)
    weight_totals = jnp.sum(take(8), axis=(0, 1))
    updates = []
    for i in range(3):
        second = rows_new[i][:, None] * cols_new[i][None, :] / row_means[i]
        updates.append(gradients[i] * lax.rsqrt(second))
    flat = jnp.stack([jnp.sum(update * update) for update in updates])
    flat = jnp.broadcast_to(jnp.pad(flat, (0, 5))[:, None], (8, LANES))
    totals = jnp.sum(gather_all(flat)[:, :, :, 0], axis=(0, 1))
    new_weights = []
    for i in range(3):
        clip_factor = jnp.maximum(1.0, jnp.sqrt(totals[i] / entries[i]) / CLIP_LIMIT)
        step_size = STEP_RATE * jnp.maximum(EPS_TWO, jnp.sqrt(weight_totals[i] / entries[i]))
        new_weights.append(weights_old[i] - step_size / clip_factor * updates[i])
    bias_rows = FF // D
    row_places = jnp.arange(VEC)
    counts = jnp.where(row_places < bias_rows, float(FF), float(D))
    grouped_updates = jnp.where(row_places < bias_rows, jnp.sum(step_rows[:bias_rows]), step_rows)
    grouped_weights = jnp.where(row_places < bias_rows, jnp.sum(weight_rows[:bias_rows]), weight_rows)
    clip_rows = jnp.maximum(1.0, jnp.sqrt(grouped_updates / counts) / CLIP_LIMIT)
    step_sizes = STEP_RATE * jnp.maximum(EPS_TWO, jnp.sqrt(grouped_weights / counts))
    factor_rows = lax.dynamic_slice_in_dim(step_sizes / clip_rows, dp_place * rows_v, rows_v)
    vectors_new = vectors - factor_rows[:, None] * vector_step
    return (
        block_out,
        input_grad,
        attn_grad,
        in_grad,
        out_grad,
        vector_grad,
        rows_new[0],
        cols_new[0],
        rows_new[1],
        cols_new[1],
        rows_new[2],
        cols_new[2],
        moment_new,
        new_weights[0],
        new_weights[1],
        new_weights[2],
        vectors_new,
    )


def solution(mesh):
    dp_count, fsdp_count = mesh.shape["dp"], mesh.shape["fsdp"]
    inner = jax.sharding.Mesh(mesh.devices.reshape(dp_count, fsdp_count // 2, 2), ALL)
    fsdp = ("chip", "core")
    split = P(ALL, None)
    block = P("dp", fsdp)
    stats = (P("dp"), P(fsdp)) * 3
    plain = dp_count == VDP and fsdp_count == 2 * VCHIP
    return jax.shard_map(
        body if plain else body_any,
        mesh=inner,
        in_specs=(split,) * 3 + (block,) * 4 + stats + (block,),
        out_specs=(split,) * 2 + (block,) * 4 + stats + (block,) * 5,
        check_vma=False,
    )
```

```python
import functools
import math

import jax
import jax.numpy as jnp
import numpy as np
from jax import lax
from jax.experimental import pallas as pl
from jax.experimental.pallas import tpu as pltpu
from jax.sharding import PartitionSpec as P

D = 256
FF = 2048
HEADS = 8
HEAD_DIM = 32
SEQ = 1024
HALF = 512
GROUP = 4
LANES = 128
QBLOCK = 256
WGRID = 32
STEP = 10
VEC = 16
TILE = 512
CHUNK = 512
SUB = 256
LEAD = 4
STRIP = 64
VDP = 4
VCHIP = 4
VROWS = 16

EPS_NORM = 1e-05
EPS_ONE = 1e-30
EPS_TWO = 0.001
CLIP_LIMIT = 1.0
STEP_RATE = 0.3
FAR = 1e30
LOG2_E = math.log2(math.e)
SCALE = HEAD_DIM ** (-0.5)
GELU_A = math.sqrt(2.0 / math.pi)
GELU_B = 0.044715
F32 = jnp.float32
BF16 = jnp.bfloat16
MIB = 1024 * 1024


def dot(left, right):
    return jnp.dot(left, right, preferred_element_type=F32)


def dot_nt(left, right):
    return lax.dot_general(left, right, (((1,), (1,)), ((), ())), preferred_element_type=F32)


def encode_table():
    half = D // 2
    feature = np.arange(half)
    freq = np.exp(
        (2 * (feature // 2)).astype(np.float32) * np.float32(-math.log(10000.0) / half)
    ).astype(np.float32)
    angles = np.arange(1, WGRID + 1, dtype=np.float32)[:, None] * freq[None, :]
    table = np.where(feature % 2 == 0, np.sin(angles), np.cos(angles)).astype(np.float32)
    low = jnp.bfloat16
    one = table.astype(low)
    rest = table - one.astype(np.float32)
    two = rest.astype(low)
    three = (rest - two.astype(np.float32)).astype(low)
    blank = np.zeros((LANES - 3 * WGRID, half), low)
    return np.concatenate([one, two, three, blank], axis=0)


def iota(shape, dim):
    return lax.broadcasted_iota(jnp.int32, shape, dim)


def norm_forward(rows):
    centered = rows - jnp.mean(rows, axis=-1, keepdims=True)
    inverse = lax.rsqrt(jnp.mean(centered * centered, axis=-1, keepdims=True) + EPS_NORM)
    return centered * inverse, inverse


def norm_backward(upstream, normed, inverse):
    return inverse * (
        upstream
        - jnp.mean(upstream, axis=-1, keepdims=True)
        - normed * jnp.mean(upstream * normed, axis=-1, keepdims=True)
    )

def vspec():
    return pl.BlockSpec(memory_space=pltpu.VMEM)


def params(mib=56, **more):
    return pltpu.CompilerParams(vmem_limit_bytes=mib * MIB, **more)


def pack_kernel(place, attn_ref, vector_ref, out_ref):
    owner = place[1] * 2 + place[2]
    vector = vector_ref[...]
    rows = vector.shape[0]
    wide = jnp.concatenate([vector] * (LANES // vector.shape[1]), axis=1)
    slot = iota((rows, LANES), 1) // vector.shape[1]
    per = LANES // vector.shape[1]
    parts = [attn_ref[...]]
    for half in range(2):
        parts.append(jnp.where(slot + half * per == owner, wide, 0.0))
    parts.append(jnp.zeros((VROWS - 2 * rows, LANES), F32))
    piece = jnp.concatenate(parts, axis=0).astype(BF16)
    for at in range(VDP * VCHIP):
        out_ref[at] = piece


def pack_attn(place, attn_weight, vectors):
    return pl.pallas_call(
        pack_kernel,
        out_shape=jax.ShapeDtypeStruct((VDP * VCHIP, attn_weight.shape[0] + VROWS, LANES), BF16),
        in_specs=[pl.BlockSpec(memory_space=pltpu.SMEM), vspec(), vspec()],
        out_specs=vspec(),
        compiler_params=params(),
        name="pack_attn",
    )(place, attn_weight, vectors)


def pack_ffn_kernel(first_ref, second_ref, *refs):
    out_ref = refs[-1]
    first = first_ref[...].astype(BF16)
    second = second_ref[...].astype(BF16)
    for at in range(VDP * VCHIP):
        out_ref[at, 0] = first
        out_ref[at, 1] = second


def pack_ffn(ffn_in, ffn_out, *earlier):
    return pl.pallas_call(
        pack_ffn_kernel,
        out_shape=jax.ShapeDtypeStruct((VDP * VCHIP, 2) + ffn_in.shape, BF16),
        in_specs=[vspec(), vspec()] + [pl.BlockSpec(memory_space=pl.ANY)] * len(earlier),
        out_specs=vspec(),
        compiler_params=params(),
        name="pack_ffn",
    )(ffn_in, ffn_out, *earlier)


def place_kernel(
    segment_ref, tokens_ref, back_ref, table_ref, qk_ref, x_ref, qk_t_ref, x_t_ref, turned_ref, marks_ref
):
    row = pl.program_id(0)
    starts = []
    for number in range(1, 4):
        at = jnp.int32(0)
        for step in (512, 256, 128, 64, 32, 16, 8, 4, 2, 1, 1):
            probe = jnp.minimum(at + (step - 1), SEQ - 1)
            at = jnp.where(segment_ref[row, probe] < number, at + step, at)
        starts.append(at)
    edges = [jnp.int32(0)] + starts + [jnp.int32(SEQ)]
    begin = jnp.int32(0)
    for number in range(3, -1, -1):
        begin = jnp.where(edges[number + 1] - edges[number] == HALF, edges[number], begin)
    for number in range(3):
        marks_ref[row, number] = starts[number]
    marks_ref[row, 3] = begin
    one, two, three = starts
    x = pltpu.roll(tokens_ref[...].astype(F32), (SEQ - begin) & (SEQ - 1), 0)
    x_ref[...] = x.astype(BF16)
    x_t_ref[...] = x.T.astype(BF16)
    back = back_ref[...].astype(F32)
    turned_ref[...] = pltpu.roll(back, (SEQ - begin) & (SEQ - 1), 0).astype(BF16)
    at = (iota((SEQ, LANES), 0) + begin) & (SEQ - 1)
    lane = iota((SEQ, LANES), 1)
    start = jnp.where(at >= three, three, jnp.where(at >= two, two, jnp.where(at >= one, one, 0)))
    local = at - start
    kept = lane < 3 * WGRID
    slot = lane & (WGRID - 1)
    hot_r = jnp.where(((local >> 5) == slot) & kept, 1.0, 0.0).astype(BF16)
    hot_c = jnp.where(((local & (WGRID - 1)) == slot) & kept, 1.0, 0.0).astype(BF16)
    table = table_ref[...]
    places = jnp.concatenate([dot(hot_r, table), dot(hot_c, table)], axis=1)
    qk = x + places
    qk_ref[...] = qk.astype(BF16)
    qk_t_ref[...] = qk.T.astype(BF16)


def place_tokens(segment_ids, tokens, cotangent, table):
    rows = segment_ids.shape[0]
    by_row = lambda r: (r, 0)
    return pl.pallas_call(
        place_kernel,
        out_shape=(
            jax.ShapeDtypeStruct(tokens.shape, BF16),
            jax.ShapeDtypeStruct(tokens.shape, BF16),
            jax.ShapeDtypeStruct((D, tokens.shape[0]), BF16),
            jax.ShapeDtypeStruct((D, tokens.shape[0]), BF16),
            jax.ShapeDtypeStruct(tokens.shape, BF16),
            jax.ShapeDtypeStruct((rows, 4), jnp.int32),
        ),
        grid=(rows,),
        in_specs=[
            pl.BlockSpec(memory_space=pltpu.SMEM),
            pl.BlockSpec((SEQ, D), by_row),
            pl.BlockSpec((SEQ, D), by_row),
            pl.BlockSpec((LANES, LANES), lambda r: (0, 0)),
        ],
        out_specs=(
            pl.BlockSpec((SEQ, D), by_row),
            pl.BlockSpec((SEQ, D), by_row),
            pl.BlockSpec((D, SEQ), lambda r: (0, r)),
            pl.BlockSpec((D, SEQ), lambda r: (0, r)),
            pl.BlockSpec((SEQ, D), by_row),
            pl.BlockSpec(memory_space=pltpu.SMEM),
        ),
        compiler_params=params(dimension_semantics=("arbitrary",)),
        cost_estimate=pl.CostEstimate(flops=600_000_000, bytes_accessed=4_000_000, transcendentals=0),
        name="place_tokens",
    )(segment_ids, tokens, cotangent, table)


def attend_kernel(
    marks,
    place,
    x_ref,
    qk_ref,
    x_t_ref,
    qk_t_ref,
    mine_ref,
    other_ref,
    query_t_ref,
    value_ref,
    key_t_ref,
    out_t_ref,
    inverse_ref,
    mixed_ref,
    mixed_t_ref,
    exps_ref,
    weight_ref,
    proj_ref,
    vector_ref,
    key_s,
    value_s,
    mark_k,
    mark_q,
    scores_s,
    weight_t_s,
    bias_s,
):
    row = pl.program_id(0)
    group = pl.program_id(1)
    begin = marks[row, 3]
    core = place[2]

    @pl.when((row == 0) & (group == 0))
    def _():
        tall = D // VDP
        for d in range(VDP):
            rows = slice(d * tall, (d + 1) * tall)
            total = jnp.zeros((8, LANES), F32)
            for c in range(VCHIP):
                for ref, half in ((mine_ref, core), (other_ref, 1 - core)):
                    if c < 3:
                        to = pl.ds(pl.multiple_of(c * D + half * LANES, LANES), LANES)
                        weight_ref[rows, to] = ref[d, c, :tall, :]
                    else:
                        to = pl.ds(pl.multiple_of(half * LANES, LANES), LANES)
                        proj_ref[rows, to] = ref[d, c, :tall, :]
                    total += ref[d, c, tall:, :].astype(F32)[:8]
            vector_ref[d * 4 : (d + 1) * 4, :LANES] = total[:4]
            vector_ref[d * 4 : (d + 1) * 4, LANES:] = total[4:]
        weight_t_s[...] = weight_ref[...].astype(F32).T.astype(BF16)
        bias_s[...] = vector_ref[8:16, :].T

    @pl.when(group == 0)
    def _():
        qk_t = qk_t_ref[...]
        query_t = (dot(weight_t_s[:D, :], qk_t) + bias_s[:, 0:1]) * SCALE
        query_t_ref[...] = query_t.astype(BF16)
        key_t_ref[...] = dot(weight_t_s[D : 2 * D, :], qk_t).astype(BF16)
        key_s[...] = dot(qk_ref[...], weight_ref[:, D : 2 * D]).astype(BF16)
        value = dot(x_ref[...], weight_ref[:, 2 * D : 3 * D]) + vector_ref[9:10, :]
        value_ref[...] = value.astype(BF16)
        value_t = dot(weight_t_s[2 * D :, :], x_t_ref[...]) + bias_s[:, 1:2]
        value_t = value_t.astype(BF16)
        for head in range(HEADS):
            value_s[head, :HEAD_DIM, :] = value_t[head * HEAD_DIM : (head + 1) * HEAD_DIM, :]
            value_s[head, HEAD_DIM:, :] = jnp.ones((16, SEQ), BF16)
        one, two, three = marks[row, 0], marks[row, 1], marks[row, 2]

        def number_of(shape, dim):
            here = (iota(shape, dim) + (HALF + begin)) & (SEQ - 1)
            return (
                jnp.where(here >= one, 1, 0)
                + jnp.where(here >= two, 1, 0)
                + jnp.where(here >= three, 1, 0)
            )

        lane = iota((HALF, LANES), 1)
        number = number_of((HALF, LANES), 0)
        mark_k[...] = jnp.where((number != lane) & (lane < 4), -FAR, 0.0).astype(BF16)
        number = number_of((LANES, HALF), 1)
        mark_q[...] = jnp.where(number == iota((LANES, HALF), 0), 1.0, 0.0).astype(BF16)

    lanes = pl.ds(pl.multiple_of(group * LANES, LANES), LANES)
    head_of = iota((1, LANES), 1) // HEAD_DIM

    def scores_of(item):
        half, at_head, block = item
        mask = jnp.where(head_of == at_head, 1.0, 0.0).astype(BF16)
        key_m = key_s[half * HALF : (half + 1) * HALF, lanes] * mask
        at = half * HALF + block * QBLOCK
        query = query_t_ref[lanes, at : at + QBLOCK]
        if half == 1:
            key_m = jnp.concatenate([key_m, mark_k[...]], axis=1)
            query = jnp.concatenate(
                [query, mark_q[:, block * QBLOCK : (block + 1) * QBLOCK]], axis=0
            )
        return dot(key_m, query)

    def exps_of(item, slot):
        half, at_head, block = item
        cols = slice(at_head * HALF + block * QBLOCK, at_head * HALF + (block + 1) * QBLOCK)
        largest = scores_s[slot, :STRIP, :]
        for at in range(STRIP, HALF, STRIP):
            largest = jnp.maximum(largest, scores_s[slot, at : at + STRIP, :])
        largest = jnp.max(largest, axis=0, keepdims=True)
        for at in range(0, HALF, STRIP):
            exps = jnp.exp2((scores_s[slot, at : at + STRIP, :] - largest) * LOG2_E)
            exps_ref[0, 0, half, at : at + STRIP, cols] = exps.astype(BF16)

    def finish(item):
        half, at_head, block = item
        at = half * HALF + block * QBLOCK
        rows = slice(half * HALF, (half + 1) * HALF)
        cols = slice(at_head * HALF + block * QBLOCK, at_head * HALF + (block + 1) * QBLOCK)
        out = dot(value_s[group * GROUP + at_head, :, rows], exps_ref[0, 0, half, :, cols])
        inverse = 1.0 / out[HEAD_DIM : HEAD_DIM + 1, :]
        inverse_ref[0, at_head : at_head + 1, at : at + QBLOCK] = inverse
        out_t_ref[at_head * HEAD_DIM : (at_head + 1) * HEAD_DIM, at : at + QBLOCK] = (
            out[:HEAD_DIM, :] * inverse
        )

    items = [
        (half, at_head, block)
        for half in range(2)
        for at_head in range(GROUP)
        for block in range(HALF // QBLOCK)
    ]
    for i in range(len(items) + 2):
        if i < len(items):
            scores_s[i % 2] = scores_of(items[i])
        if 1 <= i <= len(items):
            exps_of(items[i - 1], (i - 1) % 2)
        if i >= 2:
            finish(items[i - 2])
    out_t = out_t_ref[...]
    mixed_t_ref[...] = out_t.astype(BF16)
    mixed_ref[...] = out_t.T.astype(BF16)


def attend_forward(marks, place, x, qk, x_t, qk_t, mine, other):
    total = x.shape[0]
    rows = total // SEQ
    by_row = lambda r, g, m, p: (r, 0)
    by_col = lambda r, g, m, p: (0, r)
    by_both = lambda r, g, m, p: (g, r)
    whole = lambda r, g, m, p: (0, 0)
    return pl.pallas_call(
        attend_kernel,
        out_shape=(
            jax.ShapeDtypeStruct((D, total), BF16),
            jax.ShapeDtypeStruct((total, D), BF16),
            jax.ShapeDtypeStruct((D, total), BF16),
            jax.ShapeDtypeStruct((D, total), F32),
            jax.ShapeDtypeStruct((2, 8, total), F32),
            jax.ShapeDtypeStruct((total, D), BF16),
            jax.ShapeDtypeStruct((D, total), BF16),
            jax.ShapeDtypeStruct((rows, 2, 2, HALF, GROUP * HALF), BF16),
            jax.ShapeDtypeStruct((D, 3 * D), BF16),
            jax.ShapeDtypeStruct((D, D), BF16),
            jax.ShapeDtypeStruct((VEC, D), F32),
        ),
        grid_spec=pltpu.PrefetchScalarGridSpec(
            num_scalar_prefetch=2,
            grid=(rows, 2),
            in_specs=[
                pl.BlockSpec((SEQ, D), by_row),
                pl.BlockSpec((SEQ, D), by_row),
                pl.BlockSpec((D, SEQ), by_col),
                pl.BlockSpec((D, SEQ), by_col),
                vspec(),
                vspec(),
            ],
            out_specs=[
                pl.BlockSpec((D, SEQ), by_col),
                pl.BlockSpec((SEQ, D), by_row),
                pl.BlockSpec((D, SEQ), by_col),
                pl.BlockSpec((LANES, SEQ), by_both),
                pl.BlockSpec((1, 8, SEQ), lambda r, g, m, p: (g, 0, r)),
                pl.BlockSpec((SEQ, LANES), lambda r, g, m, p: (r, g)),
                pl.BlockSpec((LANES, SEQ), by_both),
                pl.BlockSpec((1, 1, 2, HALF, GROUP * HALF), lambda r, g, m, p: (r, g, 0, 0, 0)),
                pl.BlockSpec((D, 3 * D), whole),
                pl.BlockSpec((D, D), whole),
                pl.BlockSpec((VEC, D), whole),
            ],
            scratch_shapes=[
                pltpu.VMEM((SEQ, D), BF16),
                pltpu.VMEM((HEADS, HEAD_DIM + 16, SEQ), BF16),
                pltpu.VMEM((HALF, LANES), BF16),
                pltpu.VMEM((LANES, HALF), BF16),
                pltpu.VMEM((2, HALF, QBLOCK), F32),
                pltpu.VMEM((3 * D, D), BF16),
                pltpu.VMEM((D, 8), F32),
            ],
        ),
        compiler_params=params(dimension_semantics=("arbitrary", "arbitrary")),
        cost_estimate=pl.CostEstimate(
            flops=20_000_000_000, bytes_accessed=30_000_000, transcendentals=8_400_000
        ),
        name="attend_forward",
    )(marks, place, x, qk, x_t, qk_t, mine, other)


def feed_kernel(
    marks,
    place,
    x_ref,
    back_ref,
    mixed_ref,
    mixed_t_ref,
    proj_ref,
    mine_ref,
    other_ref,
    vector_ref,
    block_ref,
    resid_ref,
    mixed_grad_ref,
    mine_out,
    other_out,
    proj_out,
    vector_out,
    first_w,
    second_w,
    first_acc,
    second_acc,
    proj_acc,
    vector_acc,
    hidden_s,
    slope_s,
    pre_s,
    work_s,
    first_low_s,
    branch_low_s,
    attended_s,
    block_s,
    eye_s,
):
    step = pl.program_id(0)
    core = place[2]
    tall = D // VDP
    wide = FF // (2 * VCHIP)

    @pl.when(step == 0)
    def _():
        first_acc[...] = jnp.zeros_like(first_acc)
        second_acc[...] = jnp.zeros_like(second_acc)
        proj_acc[...] = jnp.zeros_like(proj_acc)
        vector_acc[...] = jnp.zeros_like(vector_acc)
        eye_s[...] = jnp.where(iota((D, D), 0) == iota((D, D), 1), 1.0, 0.0).astype(BF16)
        for d in range(VDP):
            rows = slice(d * tall, (d + 1) * tall)
            for c in range(VCHIP):
                for ref, half in ((mine_ref, core), (other_ref, 1 - core)):
                    to = pl.ds(pl.multiple_of((2 * c + half) * wide, wide), wide)
                    first_w[rows, to] = ref[d, c, 0]
                    second_w[rows, to] = ref[d, c, 1]

    bias_o, bias_2 = vector_ref[10:11, :], vector_ref[11:12, :]
    gain_1, shift_1 = vector_ref[12:13, :], vector_ref[13:14, :]
    gain_2, shift_2 = vector_ref[14:15, :], vector_ref[15:16, :]
    at_row = pl.multiple_of((step % (SEQ // TILE)) * TILE, TILE)
    per = CHUNK // D
    chunks = FF // CHUNK

    def columns(at):
        return slice(at * CHUNK, (at + 1) * CHUNK)

    def hidden_of(rows_at, at, slot):
        for side in range(per):
            bias = vector_ref[at * per + side : at * per + side + 1, :]
            cols = slice(at * CHUNK + side * D, at * CHUNK + (side + 1) * D)
            for top in range(0, SUB, STRIP):
                rows = slice(rows_at + top, rows_at + top + STRIP)
                pre = work_s[slot, top : top + STRIP, side * D : (side + 1) * D] + bias
                pre = pre.astype(BF16)
                cube = BF16(GELU_A * GELU_B) * (pre * pre)
                gate = BF16(0.5) + BF16(0.5) * jnp.tanh(pre * (cube + BF16(GELU_A)))
                hidden_s[rows, cols] = pre * gate
                slope_s[rows, cols] = gate + (gate - gate * gate) * (
                    pre * (BF16(6.0) * cube + BF16(2.0 * GELU_A))
                )

    def pre_grad_of(rows_at, at, slot):
        for side in range(per):
            cols = slice(at * CHUNK + side * D, at * CHUNK + (side + 1) * D)
            for top in range(0, SUB, STRIP):
                rows = slice(rows_at + top, rows_at + top + STRIP)
                pull = work_s[slot, top : top + STRIP, side * D : (side + 1) * D]
                pre_s[rows, cols] = pull.astype(BF16) * slope_s[rows, cols]

    def stages(sub):
        rows_at = sub * SUB
        rows = slice(rows_at, rows_at + SUB)
        slots = (2 * sub, 2 * sub + 1)
        attended = dot(mixed_ref[rows, :], proj_ref[...]) + bias_o
        norm_1, inverse_1 = norm_forward(x_ref[rows, :].astype(F32) + attended)
        first = norm_1 * gain_1 + shift_1
        first_low = first.astype(BF16)
        first_low_s[rows, :] = first_low
        yield
        branch = jnp.zeros((SUB, D), F32)
        for i in range(chunks + 2):
            if i < chunks:
                work_s[slots[i % 2]] = dot(first_low, first_w[:, columns(i)])
            if 1 <= i <= chunks:
                hidden_of(rows_at, i - 1, slots[(i - 1) % 2])
            if i >= 2:
                cols = columns(i - 2)
                branch += dot_nt(hidden_s[rows, cols], second_w[:, cols])
            yield
        norm_2, inverse_2 = norm_forward(first + (branch + bias_2))
        block_s[pl.ds(at_row + rows_at, SUB), :] = norm_2 * gain_2 + shift_2
        back = back_ref[rows, :].astype(F32)
        vector_acc[14:15, :] += jnp.sum(back * norm_2, axis=0, keepdims=True)
        vector_acc[15:16, :] += jnp.sum(back, axis=0, keepdims=True)
        resid_2 = norm_backward(back * gain_2, norm_2, inverse_2)
        branch_low = resid_2.astype(BF16)
        branch_low_s[rows, :] = branch_low
        vector_acc[11:12, :] += jnp.sum(branch_low.astype(F32), axis=0, keepdims=True)
        yield
        first_back = resid_2
        if sub == 1:
            branch_t = dot_nt(eye_s[...], branch_low_s[...]).astype(BF16)
            first_t = dot_nt(eye_s[...], first_low_s[...]).astype(BF16)
            first_t = jnp.concatenate([first_t, jnp.ones((16, TILE), BF16)], axis=0)
        for i in range(chunks + 2):
            if i < chunks:
                work_s[slots[i % 2]] = dot(branch_low, second_w[:, columns(i)])
                if sub == 1:
                    second_acc[:, columns(i)] += dot(branch_t, hidden_s[:, columns(i)])
            if 1 <= i <= chunks:
                pre_grad_of(rows_at, i - 1, slots[(i - 1) % 2])
            if i >= 2:
                cols = columns(i - 2)
                first_back += dot_nt(pre_s[rows, cols], first_w[:, cols])
                if sub == 1:
                    first_acc[:, cols] += dot(first_t, pre_s[:, cols])
            yield
        vector_acc[12:13, :] += jnp.sum(first_back * norm_1, axis=0, keepdims=True)
        vector_acc[13:14, :] += jnp.sum(first_back, axis=0, keepdims=True)
        resid_1 = norm_backward(first_back * gain_1, norm_1, inverse_1)
        resid_ref[rows, :] = resid_1
        attended_low = resid_1.astype(BF16)
        attended_s[rows, :] = attended_low
        vector_acc[10:11, :] += jnp.sum(attended_low.astype(F32), axis=0, keepdims=True)
        mixed_grad_ref[:, rows] = dot_nt(proj_ref[...], attended_low).astype(BF16)
        yield

    ahead, behind = stages(0), stages(1)
    for _ in range(LEAD):
        next(ahead)
    running = [ahead, behind]
    while running:
        for program in list(running):
            if next(program, 0) == 0:
                running.remove(program)
    proj_acc[...] += dot(mixed_t_ref[...], attended_s[...])

    @pl.when(step % (SEQ // TILE) == SEQ // TILE - 1)
    def _():
        block_ref[...] = pltpu.roll(block_s[...], marks[step // (SEQ // TILE), 3], 0)

    @pl.when(step == pl.num_programs(0) - 1)
    def _():
        for d in range(VDP):
            rows = slice(d * tall, (d + 1) * tall)
            for c in range(VCHIP):
                for ref, half in ((mine_out, core), (other_out, 1 - core)):
                    to = pl.ds(pl.multiple_of((2 * c + half) * wide, wide), wide)
                    ref[d, c, 0] = first_acc[rows, to].astype(BF16)
                    ref[d, c, 1] = second_acc[rows, to].astype(BF16)
        proj_out[...] = proj_acc[...]
        for at in range(FF // D):
            vector_out[at : at + 1, :] = first_acc[D : D + 1, at * D : (at + 1) * D]
        vector_out[FF // D :, :] = vector_acc[FF // D :, :]


def feed_forward(marks, place, x, back, mixed, mixed_t, proj, mine, other, vector):
    total = x.shape[0]
    tile = lambda i, m, p: (i, 0)
    by_col = lambda i, m, p: (0, i)
    whole = lambda i, m, p: (0, 0)
    whole5 = lambda i, m, p: (0, 0, 0, 0, 0)
    return pl.pallas_call(
        feed_kernel,
        out_shape=(
            jax.ShapeDtypeStruct((total, D), F32),
            jax.ShapeDtypeStruct((total, D), F32),
            jax.ShapeDtypeStruct((D, total), BF16),
            jax.ShapeDtypeStruct(mine.shape, BF16),
            jax.ShapeDtypeStruct(mine.shape, BF16),
            jax.ShapeDtypeStruct((D, D), F32),
            jax.ShapeDtypeStruct((VEC, D), F32),
        ),
        grid_spec=pltpu.PrefetchScalarGridSpec(
            num_scalar_prefetch=2,
            grid=(total // TILE,),
            in_specs=[
                pl.BlockSpec((TILE, D), tile),
                pl.BlockSpec((TILE, D), tile),
                pl.BlockSpec((TILE, D), tile),
                pl.BlockSpec((D, TILE), by_col),
                pl.BlockSpec((D, D), whole),
                vspec(),
                vspec(),
                pl.BlockSpec((VEC, D), whole),
            ],
            out_specs=[
                pl.BlockSpec((SEQ, D), lambda i, m, p: (i // (SEQ // TILE), 0)),
                pl.BlockSpec((TILE, D), tile),
                pl.BlockSpec((D, TILE), by_col),
                pl.BlockSpec(mine.shape, whole5),
                pl.BlockSpec(mine.shape, whole5),
                pl.BlockSpec((D, D), whole),
                pl.BlockSpec((VEC, D), whole),
            ],
            scratch_shapes=[
                pltpu.VMEM((D, FF), BF16),
                pltpu.VMEM((D, FF), BF16),
                pltpu.VMEM((D + 16, FF), F32),
                pltpu.VMEM((D, FF), F32),
                pltpu.VMEM((D, D), F32),
                pltpu.VMEM((VEC, D), F32),
                pltpu.VMEM((TILE, FF), BF16),
                pltpu.VMEM((TILE, FF), BF16),
                pltpu.VMEM((TILE, FF), BF16),
                pltpu.VMEM((4, SUB, CHUNK), F32),
                pltpu.VMEM((TILE, D), BF16),
                pltpu.VMEM((TILE, D), BF16),
                pltpu.VMEM((TILE, D), BF16),
                pltpu.VMEM((SEQ, D), F32),
                pltpu.VMEM((D, D), BF16),
            ],
        ),
        compiler_params=params(dimension_semantics=("arbitrary",)),
        cost_estimate=pl.CostEstimate(
            flops=14_000_000_000, bytes_accessed=15_000_000, transcendentals=4_200_000
        ),
        name="feed_forward",
    )(marks, place, x, back, mixed, mixed_t, proj, mine, other, vector)


def pull_kernel(
    own,
    marks,
    place,
    grad_t_ref,
    query_t_ref,
    value_ref,
    key_t_ref,
    out_t_ref,
    inverse_ref,
    exps_ref,
    qk_t_ref,
    x_t_ref,
    weight_ref,
    proj_ref,
    *refs,
):
    if own:
        resid_ref, other_ref, pulled_ref, grads_ref, sums_ref = refs[:5]
    else:
        pulled_ref, grads_ref, sums_ref = refs[:3]
    dot_s, query_g, key_g, value_g, acc, sum_acc, value_s, scaled_t_s, score_s, work_s = refs[-10:]
    row = pl.program_id(0)
    begin = marks[row, 3]
    group = place[2] if own else 1 - place[2]

    @pl.when(row == 0)
    def _():
        acc[...] = jnp.zeros_like(acc)
        sum_acc[...] = jnp.zeros_like(sum_acc)

    grad_t = grad_t_ref[...].astype(F32)
    head_of = iota((1, LANES), 1) // HEAD_DIM
    for at_head in range(GROUP):
        heads = slice(at_head * HEAD_DIM, (at_head + 1) * HEAD_DIM)
        part = grad_t[heads, :] * inverse_ref[0, at_head : at_head + 1, :]
        dot_s[at_head : at_head + 1, :] = jnp.sum(part * out_t_ref[heads, :], axis=0, keepdims=True)
        part = part.astype(BF16)
        scaled_t_s[heads, :] = part
        mask = jnp.where(head_of == at_head, 1.0, 0.0).astype(BF16)
        for half in range(2):
            rows = slice(half * HALF, (half + 1) * HALF)
            to = slice(at_head * HALF, (at_head + 1) * HALF)
            value_s[half, to, :] = value_ref[rows, :] * mask

    def pull_of(item):
        half, at_head, block = item
        at = half * HALF + block * QBLOCK
        value = value_s[half, at_head * HALF : (at_head + 1) * HALF, :]
        return dot(value, scaled_t_s[:, at : at + QBLOCK])

    def score_grad_of(item, slot):
        half, at_head, block = item
        at = half * HALF + block * QBLOCK
        cols = slice(at_head * HALF + block * QBLOCK, at_head * HALF + (block + 1) * QBLOCK)
        shift = dot_s[at_head : at_head + 1, at : at + QBLOCK]
        for top in range(0, HALF, STRIP):
            rows = slice(top, top + STRIP)
            pull = (work_s[slot, rows, :] - shift).astype(BF16)
            score_s[half, rows, cols] = exps_ref[0, 0, half, rows, cols] * pull

    def finish(half, at_head):
        cols = slice(at_head * HALF, (at_head + 1) * HALF)
        rows = slice(half * HALF, (half + 1) * HALF)
        heads = slice(at_head * HEAD_DIM, (at_head + 1) * HEAD_DIM)
        score_grad = score_s[half, :, cols]
        value_g[heads, rows] = dot_nt(scaled_t_s[heads, rows], exps_ref[0, 0, half, :, cols])
        query_g[heads, rows] = dot(key_t_ref[heads, rows], score_grad)
        key_g[heads, rows] = dot_nt(query_t_ref[heads, rows], score_grad)

    items = [
        (half, at_head, block)
        for half in range(2)
        for at_head in range(GROUP)
        for block in range(HALF // QBLOCK)
    ]
    for i in range(len(items) + 1):
        if i < len(items):
            work_s[i % 2] = pull_of(items[i])
        if i >= 1:
            score_grad_of(items[i - 1], (i - 1) % 2)
            if i % 2 == 0:
                half, at_head, _ = items[i - 1]
                finish(half, at_head)
    query_low = query_g[...].astype(BF16)
    both_low = jnp.concatenate([key_g[...].astype(BF16), value_g[...].astype(BF16)], axis=0)
    ones = jnp.ones((16, SEQ), BF16)
    sum_acc[0:1, :] += dot_nt(ones, query_low)[0:1, :] * SCALE
    sum_acc[1:2, :] += dot_nt(ones, both_low[LANES:, :])[0:1, :]
    qk_t = qk_t_ref[...]
    acc[:, :LANES] += dot_nt(qk_t, query_low) * SCALE
    acc[:, LANES : 2 * LANES] += dot_nt(qk_t, both_low[:LANES, :])
    acc[:, 2 * LANES :] += dot_nt(x_t_ref[...], both_low[LANES:, :])
    at = [pl.ds(pl.multiple_of(i * D + group * LANES, LANES), LANES) for i in range(3)]
    pulled = dot(weight_ref[:, at[0]], query_low) * SCALE + dot(
        jnp.concatenate([weight_ref[:, at[1]], weight_ref[:, at[2]]], axis=1), both_low
    )
    if own:
        pulled = (pulled + other_ref[...]).T
        pulled_ref[...] = pltpu.roll(resid_ref[...] + pulled, begin, 0)
    else:
        pulled_ref[...] = pulled

    @pl.when(row == pl.num_programs(0) - 1)
    def _():
        tall = D // VDP
        for d in range(VDP):
            rows = slice(d * tall, (d + 1) * tall)
            for c in range(3):
                grads_ref[d, c] = acc[rows, c * LANES : (c + 1) * LANES].astype(BF16)
            grads_ref[d, 3] = proj_ref[rows, :].astype(BF16)
        sums_ref[...] = sum_acc[...]


def attend_back(own, marks, place, grad_t, query_t, value, key_t, out_t, inverse, exps, qk_t, x_t, weight, proj, *more):
    total = value.shape[0]
    rows = total // SEQ
    pick = (lambda p: p[2]) if own else (lambda p: 1 - p[2])
    by_group = lambda r, m, p: (r, pick(p))
    by_row = lambda r, m, p: (r, 0)
    whole = lambda r, m, p: (0, 0)
    in_specs = [
        pl.BlockSpec((LANES, SEQ), lambda r, m, p: (pick(p), r)),
        pl.BlockSpec((LANES, SEQ), lambda r, m, p: (pick(p), r)),
        pl.BlockSpec((SEQ, LANES), by_group),
        pl.BlockSpec((LANES, SEQ), lambda r, m, p: (pick(p), r)),
        pl.BlockSpec((LANES, SEQ), lambda r, m, p: (pick(p), r)),
        pl.BlockSpec((1, 8, SEQ), lambda r, m, p: (pick(p), 0, r)),
        pl.BlockSpec((1, 1, 2, HALF, GROUP * HALF), lambda r, m, p: (r, pick(p), 0, 0, 0)),
        pl.BlockSpec((D, SEQ), lambda r, m, p: (0, r)),
        pl.BlockSpec((D, SEQ), lambda r, m, p: (0, r)),
        pl.BlockSpec((D, 3 * D), whole),
        pl.BlockSpec((D, LANES), lambda r, m, p: (0, pick(p))),
    ]
    by_col = pl.BlockSpec((D, SEQ), lambda r, m, p: (0, r))
    if own:
        in_specs += [pl.BlockSpec((SEQ, D), by_row), by_col]
    return pl.pallas_call(
        functools.partial(pull_kernel, own),
        out_shape=(
            jax.ShapeDtypeStruct((total, D) if own else (D, total), F32),
            jax.ShapeDtypeStruct((VDP, VCHIP, D // VDP, LANES), BF16),
            jax.ShapeDtypeStruct((8, LANES), F32),
        ),
        grid_spec=pltpu.PrefetchScalarGridSpec(
            num_scalar_prefetch=2,
            grid=(rows,),
            in_specs=in_specs,
            out_specs=[
                pl.BlockSpec((SEQ, D), by_row) if own else by_col,
                pl.BlockSpec((VDP, VCHIP, D // VDP, LANES), lambda r, m, p: (0, 0, 0, 0)),
                pl.BlockSpec((8, LANES), whole),
            ],
            scratch_shapes=[
                pltpu.VMEM((8, SEQ), F32),
                pltpu.VMEM((LANES, SEQ), F32),
                pltpu.VMEM((LANES, SEQ), F32),
                pltpu.VMEM((LANES, SEQ), F32),
                pltpu.VMEM((D, 3 * LANES), F32),
                pltpu.VMEM((8, LANES), F32),
                pltpu.VMEM((2, GROUP * HALF, LANES), BF16),
                pltpu.VMEM((LANES, SEQ), BF16),
                pltpu.VMEM((2, HALF, GROUP * HALF), BF16),
                pltpu.VMEM((2, HALF, QBLOCK), F32),
            ],
        ),
        compiler_params=params(dimension_semantics=("arbitrary",)),
        cost_estimate=pl.CostEstimate(
            flops=18_000_000_000, bytes_accessed=15_000_000, transcendentals=0
        ),
        name="attend_back",
    )(marks, place, grad_t, query_t, value, key_t, out_t, inverse, exps, qk_t, x_t, weight, proj, *more)


def sums_by_group(place, sums_own, sums_other):
    first = place[2] == 0
    return (
        jnp.where(first, sums_own, sums_other),
        jnp.where(first, sums_other, sums_own),
    )


def two_terms(rows):
    high = rows.astype(BF16)
    return jnp.concatenate([high.astype(F32), rows - high.astype(F32)], axis=0)


def column_to_row(columns, rows):
    lane = iota((rows, LANES), 1)
    wide = jnp.zeros((rows, LANES), F32)
    for i, column in enumerate(columns):
        wide = jnp.where(lane == i, column, wide)
    return wide.T[:8, :]


def total_of(array):
    return jnp.sum(jnp.sum(array, axis=0, keepdims=True), axis=1, keepdims=True)


def tail_ffn_kernel(place, ffn_ref, rows_1, rows_2, grad_ref, stat_ref):
    lane = iota((1, LANES), 1)
    piece, across = [], []
    for kind in range(2):
        total = ffn_ref[0, kind].astype(F32)
        for at in range(1, VDP * VCHIP):
            total = total + ffn_ref[at, kind].astype(F32)
        grad_ref[kind] = total
        square = total * total + EPS_ONE
        down = jnp.sum(square, axis=0, keepdims=True)
        piece += [down[:, :LANES], down[:, LANES:]]
        across.append(jnp.sum(square, axis=1, keepdims=True))
    across = column_to_row(across, total.shape[0])
    across = jnp.concatenate([across[0:1], across[1:2]], axis=1)
    olds = jnp.zeros((1, LANES), F32)
    for i, ref in enumerate((rows_1, rows_2)):
        olds = jnp.where(lane == i, jnp.sum(ref[...], axis=1, keepdims=True), olds)
    stat_ref[...] = jnp.concatenate([across] + piece + [olds, jnp.zeros((2, LANES), F32)], axis=0)


def tail_send_kernel(
    place, mine_ref, got_ref, vector_ref, own_ref, other_ref, stat_ref, stat_other_ref, send_ref
):
    tall = D // VDP
    low, high = sums_by_group(place, own_ref[...], other_ref[...])
    vector = jnp.concatenate(
        [
            vector_ref[:8, :],
            jnp.concatenate([low[:2], high[:2]], axis=1),
            vector_ref[10:, :],
        ],
        axis=0,
    )
    stat = jnp.concatenate([stat_ref[0:1, :] + stat_other_ref[0:1, :], stat_ref[1:6, :]], axis=0)
    stat = two_terms(stat)
    rows = VEC // VDP
    for d in range(VDP):
        for c in range(VCHIP):
            at = d * VCHIP + c
            both = mine_ref[d, c].astype(F32) + got_ref[d, c].astype(F32)
            send_ref[at, :tall, :] = both.astype(BF16)
            part = vector[d * rows : (d + 1) * rows, c * 64 : (c + 1) * 64]
            part = jnp.concatenate([part, jnp.zeros((rows, LANES - 64), F32)], axis=1)
            send_ref[at, tall:, :] = jnp.concatenate([part, stat], axis=0).astype(BF16)


def tail_reduce_kernel(
    place,
    got_ref,
    ffn_grad_ref,
    attn_ref,
    first_ref,
    second_ref,
    rows_0,
    rows_1,
    rows_2,
    cols_0,
    cols_1,
    cols_2,
    vector_ref,
    moment_ref,
    grad_ref,
    update_1,
    update_2,
    rows_out,
    cols_out_1,
    cols_out_2,
    send_ref,
):
    decay = 1.0 - STEP ** (-0.8)
    chip = place[1]
    dp = place[0]
    tall = attn_ref.shape[0]
    rows, width = vector_ref.shape
    pieces = VDP * VCHIP
    lane = iota((1, LANES), 1)
    total = got_ref[0, :tall, :].astype(F32)
    part = got_ref[0, tall:, :].astype(F32)[:rows]
    for at in range(1, pieces):
        total = total + got_ref[at, :tall, :].astype(F32)
        part = part + got_ref[at, tall:, :].astype(F32)[:rows]
    grad_ref[...] = total
    low = total.astype(BF16)

    def stat_of(at):
        both = got_ref[pl.ds(at, 1), tall:, :][0].astype(F32)[rows:]
        return both[:6] + both[6:12]

    every = jnp.zeros((1, LANES), F32)
    olds = jnp.zeros((1, LANES), F32)
    mine = jnp.zeros((1, LANES), F32)
    down = jnp.zeros((6, LANES), F32)
    for d in range(VDP):
        down = down + stat_of(d * VCHIP + chip)
        for c in range(VCHIP):
            stat = stat_of(d * VCHIP + c)
            every = every + stat[0:1]
            if c == 0:
                olds = olds + stat[5:6]
    for c in range(VCHIP):
        mine = mine + stat_of(dp * VCHIP + c)[0:1]
    row_total = tall * VDP
    new_rows, means = [], []
    for i, ref in enumerate((rows_1, rows_2)):
        count = first_ref.shape[1] * 2 * VCHIP
        new_rows.append(decay * ref[...] + (1.0 - decay) * (mine[:, i * tall : (i + 1) * tall] / count))
        old = jnp.sum(jnp.where(lane == i, olds, 0.0), axis=1, keepdims=True)
        fresh = jnp.sum(every[:, i * tall : (i + 1) * tall], axis=1, keepdims=True)
        means.append((decay * old + (1.0 - decay) * (fresh / count)) / row_total)
    tile = jnp.concatenate(new_rows + [jnp.zeros((6, tall), F32)], axis=0)
    rows_out[...] = tile
    tile = jnp.concatenate([tile, jnp.zeros((8, LANES - tall), F32)], axis=1)
    turned = jnp.concatenate([tile, jnp.zeros((LANES - 8, LANES), F32)], axis=0).T
    scalars = jnp.zeros((1, LANES), F32)
    for i, (old_ref, out_ref, to) in enumerate(
        ((cols_1, cols_out_1, update_1), (cols_2, cols_out_2, update_2))
    ):
        sums = jnp.concatenate([down[1 + 2 * i : 2 + 2 * i], down[2 + 2 * i : 3 + 2 * i]], axis=1)
        cols = decay * old_ref[...] + (1.0 - decay) * (sums / row_total)
        out_ref[...] = cols
        grad = ffn_grad_ref[i]
        update = grad * lax.rsqrt(turned[:tall, i : i + 1] * cols / means[i])
        to[...] = update
        scalars = jnp.where(lane == 67 + i, total_of(update * update), scalars)
    for i, ref in enumerate((attn_ref, first_ref, second_ref)):
        weight = ref[...]
        scalars = jnp.where(lane == 64 + i, total_of(weight * weight), scalars)
    scalars = jnp.concatenate([rows_0[...], scalars[:, tall:]], axis=1)
    vector = vector_ref[...]
    power = jnp.sum(vector * vector, axis=1, keepdims=True)
    lines = jnp.concatenate(
        [part[:, :64], moment_ref[...], jnp.broadcast_to(power, (rows, LANES - 64 - width))], axis=1
    )
    piece = jnp.concatenate(
        [two_terms(lines), two_terms(jnp.concatenate([cols_0[...], scalars], axis=0))]
        + [jnp.zeros((4, LANES), F32)],
        axis=0,
    ).astype(BF16)
    for at in range(pieces):
        send_ref[at, :tall, :] = low
        send_ref[at, tall:, :] = piece


def tail_apply_kernel(
    place,
    mine_ref,
    other_ref,
    grad_ref,
    update_1,
    update_2,
    weight_0,
    weight_1,
    weight_2,
    rows_0,
    cols_0,
    vector_ref,
    moment_ref,
    new_0,
    new_1,
    new_2,
    rows_out,
    cols_out,
    vector_grad_ref,
    moment_out,
    vector_out,
    sums_s,
    rows_s,
):
    decay = 1.0 - STEP ** (-0.8)
    dp, chip, core = place[0], place[1], place[2]
    tall = weight_0.shape[0]
    rows, width = vector_ref.shape
    fsdp = 2 * VCHIP
    lane = iota((1, LANES), 1)
    refs = (mine_ref, other_ref)
    row_total = float(tall * VDP)
    col_total = float(LANES * fsdp)

    def lines_of(ref, at):
        both = ref[at, tall:, :].astype(F32)
        return both[0:4] + both[4:8], both[8:10] + both[10:12]

    scalars = jnp.zeros((1, LANES), F32)
    for ref in refs:
        for at in range(VDP * VCHIP):
            scalars = scalars + lines_of(ref, at)[1][1:2]
    scalar = lambda at: jnp.sum(jnp.where(lane == at, scalars, 0.0), axis=1, keepdims=True)

    tile, fresh = [], []
    for d in range(VDP):
        wide = jnp.zeros((tall, LANES), F32)
        for ref in refs:
            for c in range(VCHIP):
                block = ref[d * VCHIP + c, :tall, :].astype(F32)
                wide = wide + (block * block + EPS_ONE)
        fresh.append(jnp.sum(wide, axis=1, keepdims=True))
        tile.append(lines_of(mine_ref, d * VCHIP)[1][1:2])
    tile = jnp.concatenate(tile + [jnp.zeros((LANES - VDP, LANES), F32)], axis=0).T
    mean = jnp.zeros((1, 1), F32)
    new_rows = []
    for d in range(VDP):
        new = decay * tile[:tall, d : d + 1] + (1.0 - decay) * (fresh[d] / col_total)
        new_rows.append(1.0 / new)
        mean = mean + jnp.sum(new, axis=0, keepdims=True)
        sums_s[d] = jnp.broadcast_to(fresh[d], (tall, LANES))
    mean = mean / row_total
    mine = sums_s[pl.ds(dp, 1)][0]
    rows_s[...] = mine.T
    rows_new = decay * rows_0[...] + (1.0 - decay) * (rows_s[0:1, :tall] / col_total)
    rows_out[...] = rows_new
    power = jnp.zeros((1, 1), F32)
    for half, ref in enumerate(refs):
        for c in range(VCHIP):
            down = jnp.zeros((tall, LANES), F32)
            weighted = jnp.zeros((tall, LANES), F32)
            for d in range(VDP):
                block = ref[d * VCHIP + c, :tall, :].astype(F32)
                square = block * block
                down = down + (square + EPS_ONE)
                weighted = weighted + square * new_rows[d]
            down = jnp.sum(down, axis=0, keepdims=True)
            old = lines_of(ref, c)[1][0:1]
            cols = decay * old + (1.0 - decay) * (down / row_total)
            weighted = jnp.sum(weighted, axis=0, keepdims=True) / cols
            power = power + jnp.sum(weighted, axis=1, keepdims=True)
            if half == 0:
                sums_s[VDP + c] = jnp.broadcast_to(down, (tall, LANES))
    power = power * mean
    down = sums_s[pl.ds(VDP + chip, 1)][0][0:1, :]
    cols_new = decay * cols_0[...] + (1.0 - decay) * (down / row_total)
    cols_out[...] = cols_new
    column = jnp.concatenate(
        [
            jnp.concatenate([rows_new, jnp.zeros((1, LANES - tall), F32)], axis=1),
            jnp.zeros((LANES - 1, LANES), F32),
        ],
        axis=0,
    ).T[:tall, 0:1]
    update_0 = grad_ref[...] * lax.rsqrt(column * cols_new / mean)
    powers = (power, scalar(67), scalar(68))
    for i, (update, weight, new) in enumerate(
        (
            (update_0, weight_0, new_0),
            (update_1[...], weight_1, new_1),
            (update_2[...], weight_2, new_2),
        )
    ):
        entries = float(weight.shape[0] * weight.shape[1] * VDP * fsdp)
        clip = jnp.maximum(1.0, jnp.sqrt(powers[i] / entries) / CLIP_LIMIT)
        rate = STEP_RATE * jnp.maximum(EPS_TWO, jnp.sqrt(scalar(64 + i) / entries))
        new[...] = weight[...] - rate / clip * update
    powers, sizes = [], []
    for d in range(VDP):
        power = jnp.zeros((rows, 1), F32)
        size = jnp.zeros((rows, 1), F32)
        for c in range(VCHIP):
            at = d * VCHIP + c
            first, second = lines_of(mine_ref, at)[0], lines_of(other_ref, at)[0]
            both = first[:, :64] + second[:, :64]
            size = size + first[:, LANES - 1 :] + second[:, LANES - 1 :]
            near = jnp.where(core == 0, first[:, 64 : 64 + width], second[:, 64 : 64 + width])
            far = jnp.where(core == 0, second[:, 64 : 64 + width], first[:, 64 : 64 + width])
            moment = jnp.concatenate([near, far], axis=1)
            moment = decay * moment + (1.0 - decay) * (both * both + EPS_ONE)
            power = power + jnp.sum(both * both / moment, axis=1, keepdims=True)
            wide = jnp.concatenate([both, jnp.zeros((rows, LANES - 64), F32)], axis=1)
            sums_s[2 * VDP + at, :rows, :] = wide
        powers.append(power)
        sizes.append(size)
    both = sums_s[pl.ds(2 * VDP + dp * VCHIP + chip, 1), :rows, :][0]
    vector_grad = jnp.where(core == 0, both[:, :width], both[:, width : 2 * width])
    vector_grad_ref[...] = vector_grad
    moment = decay * moment_ref[...] + (1.0 - decay) * (vector_grad * vector_grad + EPS_ONE)
    moment_out[...] = moment
    step = vector_grad * lax.rsqrt(moment)
    bias = VDP // 2
    bias_power = sum(jnp.sum(power, axis=0, keepdims=True) for power in powers[:bias])
    bias_size = sum(jnp.sum(size, axis=0, keepdims=True) for size in sizes[:bias])
    power, size = powers[bias], sizes[bias]
    for d in range(bias + 1, VDP):
        power = jnp.where(dp == d, powers[d], power)
        size = jnp.where(dp == d, sizes[d], size)
    is_bias = dp < bias
    power = jnp.where(is_bias, bias_power, power)
    size = jnp.where(is_bias, bias_size, size)
    count = jnp.where(is_bias, float(FF), float(D))
    clip = jnp.maximum(1.0, jnp.sqrt(power / count) / CLIP_LIMIT)
    rate = STEP_RATE * jnp.maximum(EPS_TWO, jnp.sqrt(size / count))
    vector_out[...] = vector_ref[...] - rate / clip * step


def whole_call(kernel, name, place, outs, *operands, scratch=()):
    return pl.pallas_call(
        kernel,
        out_shape=[jax.ShapeDtypeStruct(shape, kind) for shape, kind in outs],
        in_specs=[pl.BlockSpec(memory_space=pltpu.SMEM)] + [vspec()] * len(operands),
        out_specs=[vspec()] * len(outs),
        scratch_shapes=list(scratch),
        compiler_params=params(16),
        name=name,
    )(place, *operands)


def core_swap(block):
    return lax.ppermute(block, "core", [(0, 1), (1, 0)])


def exchange(blocks, axes):
    return lax.all_to_all(blocks, axes, split_axis=0, concat_axis=0, tiled=True)


def after(value, *earlier):
    return pl.pallas_call(
        lambda *refs: None,
        out_shape=jax.ShapeDtypeStruct(value.shape, value.dtype),
        in_specs=[pl.BlockSpec(memory_space=pltpu.HBM)] * (1 + len(earlier)),
        out_specs=pl.BlockSpec(memory_space=pltpu.HBM),
        input_output_aliases={0: 0},
        compiler_params=params(),
        name="after",
    )(value, *earlier)


def pair_kernel(mine_ref, got_ref, out_ref):
    out_ref[...] = (mine_ref[...].astype(F32) + got_ref[...].astype(F32)).astype(BF16)


def pair_sum(mine, got):
    return pl.pallas_call(
        pair_kernel,
        out_shape=jax.ShapeDtypeStruct(mine.shape, BF16),
        in_specs=[vspec(), vspec()],
        out_specs=vspec(),
        compiler_params=params(16),
        name="pair_sum",
    )(mine, got)


CHIPS = ("dp", "chip")
ALL = ("dp", "chip", "core")


def layer(place, weights, segment_ids, tokens, cotangent, ffn_weights, send_core, send_ffn):
    table = jnp.asarray(encode_table())
    qk, x, qk_t, x_t, back, marks = place_tokens(segment_ids, tokens, cotangent, table)
    query_t, value, key_t, out_t, inverse, mixed, mixed_t, exps, weight, proj, vector = attend_forward(
        marks, place, x, qk, x_t, qk_t, *weights(marks)
    )
    ffn_mine, ffn_other = ffn_weights(marks, vector)
    block_out, resid, grad_t, ffn_mine, ffn_other, proj_g, vector_g = feed_forward(
        marks, place, x, back, mixed, mixed_t, proj, ffn_mine, ffn_other, vector
    )
    ffn_got, grad_t = send_ffn(ffn_mine, ffn_other, grad_t)
    shared = (marks, place, grad_t, query_t, value, key_t, out_t, inverse, exps, qk_t, x_t, weight, proj_g)
    pulled, grads_other, sums_other = attend_back(False, *shared)
    attn_got = send_core(grads_other)
    input_grad, grads_own, sums_own = attend_back(True, *shared, resid, pulled)
    return block_out, input_grad, grads_own, grads_other, attn_got, sums_own, sums_other, vector_g, ffn_got


def body(
    tokens,
    cotangent,
    segment_ids,
    attn_weight,
    ffn_in,
    ffn_out,
    vectors,
    attn_rows,
    attn_cols,
    in_rows,
    in_cols,
    out_rows,
    out_cols,
    vector_moment,
):
    place = jnp.stack([lax.axis_index("dp"), lax.axis_index("chip"), lax.axis_index("core")])
    place = place.astype(jnp.int32)
    pieces = VDP * VCHIP
    tall, wide = attn_weight.shape
    rows_v, cols_v = vectors.shape
    split = lambda array: array.reshape((VDP, VCHIP) + array.shape[1:])
    attn_mine = exchange(pack_attn(place, attn_weight, vectors), CHIPS)

    def attn_weights(marks):
        mine = split(after(attn_mine, marks))
        return mine, core_swap(mine)

    def ffn_weights(marks, vector):
        got = split(exchange(pack_ffn(ffn_in, ffn_out, attn_mine, marks), CHIPS))
        ffn_mine = after(got, vector)
        return ffn_mine, core_swap(ffn_mine)

    def send_ffn(mine, other, grad_t):
        both = pair_sum(mine, core_swap(other))
        got = exchange(both.reshape((pieces,) + mine.shape[2:]), CHIPS)
        return got, after(grad_t, both)

    (
        block_out,
        input_grad,
        grads_own,
        grads_other,
        attn_got,
        sums_own,
        sums_other,
        vector_g,
        ffn_got,
    ) = layer(place, attn_weights, segment_ids, tokens, cotangent, ffn_weights, core_swap, send_ffn)
    lay = lambda stat: stat.reshape(1, -1)
    rows_old = (lay(attn_rows), lay(in_rows), lay(out_rows))
    cols_old = (lay(attn_cols), lay(in_cols), lay(out_cols))
    weights_old = (attn_weight, ffn_in, ffn_out)
    ffn_grad, stat = whole_call(
        tail_ffn_kernel,
        "tail_ffn",
        place,
        [((2,) + ffn_in.shape, F32), ((8, LANES), F32)],
        ffn_got,
        *rows_old[1:],
    )
    (sent,) = whole_call(
        tail_send_kernel,
        "tail_send",
        place,
        [((pieces, tall + VROWS, LANES), BF16)],
        grads_own,
        attn_got,
        vector_g,
        sums_own,
        sums_other,
        stat,
        core_swap(stat),
    )
    got = exchange(sent, CHIPS)
    attn_grad, update_1, update_2, rows_new, cols_new_1, cols_new_2, sent = whole_call(
        tail_reduce_kernel,
        "tail_reduce",
        place,
        [
            (attn_weight.shape, F32),
            (ffn_in.shape, F32),
            (ffn_out.shape, F32),
            ((8, tall), F32),
            (cols_old[1].shape, F32),
            (cols_old[2].shape, F32),
            ((pieces, tall + VROWS, LANES), BF16),
        ],
        got,
        ffn_grad,
        *weights_old,
        *rows_old,
        *cols_old,
        vectors,
        vector_moment,
    )
    mine = exchange(sent, CHIPS)
    attn_new, in_new, out_new, rows_new_0, cols_new_0, vector_grad, moment_new, vectors_new = whole_call(
        tail_apply_kernel,
        "tail_apply",
        place,
        [
            (attn_weight.shape, F32),
            (ffn_in.shape, F32),
            (ffn_out.shape, F32),
            (rows_old[0].shape, F32),
            (cols_old[0].shape, F32),
            (vectors.shape, F32),
            (vectors.shape, F32),
            (vectors.shape, F32),
        ],
        mine,
        core_swap(mine),
        attn_grad,
        update_1,
        update_2,
        *weights_old,
        rows_old[0],
        cols_old[0],
        vectors,
        vector_moment,
        scratch=[
            pltpu.VMEM((2 * VDP + pieces, tall, LANES), F32),
            pltpu.VMEM((LANES, tall), F32),
        ],
    )
    return (
        block_out,
        input_grad,
        attn_grad,
        ffn_grad[0],
        ffn_grad[1],
        vector_grad,
        rows_new_0.reshape(-1),
        cols_new_0.reshape(-1),
        rows_new[0],
        cols_new_1.reshape(-1),
        rows_new[1],
        cols_new_2.reshape(-1),
        moment_new,
        attn_new,
        in_new,
        out_new,
        vectors_new,
    )


def gather_all(block):
    shape = (lax.axis_size("dp"), lax.axis_size("chip") * 2)
    count = shape[0] * shape[1]
    got = exchange(jnp.broadcast_to(block[None], (count,) + block.shape), ALL)
    return got.reshape(shape + block.shape)


def unblock(parts):
    dp_count, fsdp_count, rows, cols = parts.shape
    return parts.transpose(0, 2, 1, 3).reshape(dp_count * rows, fsdp_count * cols)


def scatter_sum(full):
    dp_count = lax.axis_size("dp")
    fsdp_count = lax.axis_size("chip") * 2
    rows, cols = full.shape
    by_col = full.astype(BF16).reshape(rows, fsdp_count, cols // fsdp_count).transpose(1, 0, 2)
    got = exchange(by_col, ("chip", "core"))
    part = jnp.sum(got.astype(F32), axis=0).astype(BF16)
    by_row = part.reshape(dp_count, rows // dp_count, cols // fsdp_count)
    return jnp.sum(exchange(by_row, "dp").astype(F32), axis=0)


def body_any(
    tokens,
    cotangent,
    segment_ids,
    attn_weight,
    ffn_in,
    ffn_out,
    vectors,
    attn_rows,
    attn_cols,
    in_rows,
    in_cols,
    out_rows,
    out_cols,
    vector_moment,
):
    dp_count = lax.axis_size("dp")
    fsdp_count = lax.axis_size("chip") * 2
    dp_place = lax.axis_index("dp")
    fsdp_place = lax.axis_index("chip") * 2 + lax.axis_index("core")
    rows_w = attn_weight.shape[0]
    rows_v = vectors.shape[0]
    place = jnp.zeros((3,), jnp.int32)
    full_attn = unblock(gather_all(attn_weight.astype(BF16)))
    full_vector = unblock(gather_all(vectors.astype(BF16)))
    full_ffn = jnp.stack(
        [unblock(gather_all(ffn_in.astype(BF16))), unblock(gather_all(ffn_out.astype(BF16)))]
    )
    tall = D // VDP
    cut = full_attn.reshape(VDP, tall, VCHIP, 2, LANES).transpose(3, 0, 2, 1, 4)
    lines = full_vector.reshape(VDP, VEC // VDP, 2, LANES).transpose(0, 2, 1, 3)
    lines = lines.reshape(VDP, 1, 2 * VEC // VDP, LANES)
    lines = jnp.pad(lines, ((0, 0), (0, VCHIP - 1), (0, VROWS - 2 * VEC // VDP), (0, 0)))
    weights = (
        jnp.concatenate([cut[0], lines], axis=2),
        jnp.concatenate([cut[1], jnp.zeros_like(lines)], axis=2),
    )
    ffn_cut = full_ffn.reshape(2, VDP, tall, VCHIP, 2, FF // (2 * VCHIP))
    ffn_cut = ffn_cut.transpose(4, 1, 3, 0, 2, 5)
    (
        block_out,
        input_grad,
        grads_own,
        grads_other,
        _,
        sums_own,
        sums_other,
        vector_g,
        ffn_got,
    ) = layer(
        place,
        lambda marks: weights,
        segment_ids,
        tokens,
        cotangent,
        lambda marks, vector: (ffn_cut[0], ffn_cut[1]),
        lambda block: block,
        lambda mine, other, grad_t: (jnp.stack([mine, other]), grad_t),
    )
    attn_full = jnp.stack([grads_own, grads_other]).transpose(1, 3, 2, 0, 4).reshape(D, 4 * D)
    ffn_full = ffn_got.transpose(3, 1, 4, 2, 0, 5).reshape(2, D, FF)
    sums = jnp.concatenate([sums_own[:2], sums_other[:2]], axis=1)
    vector_full = jnp.concatenate([vector_g[:8], sums, vector_g[10:]], axis=0)
    attn_grad = scatter_sum(attn_full)
    in_grad = scatter_sum(ffn_full[0])
    out_grad = scatter_sum(ffn_full[1])
    vector_grad = scatter_sum(vector_full)

    decay = 1.0 - STEP ** (-0.8)
    gradients = (attn_grad, in_grad, out_grad)
    weights_old = (attn_weight, ffn_in, ffn_out)
    rows_old = (attn_rows, in_rows, out_rows)
    cols_old = (attn_cols, in_cols, out_cols)
    moment_new = decay * vector_moment + (1.0 - decay) * (vector_grad * vector_grad + EPS_ONE)
    vector_step = vector_grad * lax.rsqrt(moment_new)
    squares = [gradient * gradient + EPS_ONE for gradient in gradients]
    pieces = []
    for square in squares:
        pieces.append(jnp.sum(square, axis=1))
    for square in squares:
        pieces.append(jnp.sum(square, axis=0))
    pieces.append(jnp.sum(vector_step * vector_step, axis=1))
    pieces.append(jnp.sum(vectors * vectors, axis=1))
    pieces.append(jnp.stack([jnp.sum(weight * weight) for weight in weights_old]))
    pieces.append(jnp.stack([jnp.sum(old) for old in rows_old]))
    sizes = [piece.shape[0] for piece in pieces]
    flat = jnp.concatenate(pieces)
    flat = jnp.pad(flat, (0, -flat.shape[0] % 1024)).reshape(-1, LANES)
    got = gather_all(flat).reshape(dp_count, fsdp_count, -1)
    offsets = [0]
    for length in sizes:
        offsets.append(offsets[-1] + length)
    take = lambda i: got[:, :, offsets[i] : offsets[i + 1]]
    rows_new, cols_new, row_means, entries = [], [], [], []
    for i in range(3):
        count_rows = rows_w * dp_count
        count_cols = weights_old[i].shape[1] * fsdp_count
        entries.append(float(count_rows * count_cols))
        row_all = jnp.sum(take(i), axis=1)
        mine = lax.dynamic_index_in_dim(row_all, dp_place, 0, keepdims=False)
        rows_new.append(decay * rows_old[i] + (1.0 - decay) * mine / count_cols)
        col_all = jnp.sum(take(3 + i), axis=0)
        mine = lax.dynamic_index_in_dim(col_all, fsdp_place, 0, keepdims=False)
        cols_new.append(decay * cols_old[i] + (1.0 - decay) * mine / count_rows)
        old_total = jnp.sum(take(9)[:, 0, i])
        row_means.append(
            (decay * old_total + (1.0 - decay) * jnp.sum(row_all) / count_cols) / count_rows
        )
    step_rows = jnp.sum(take(6), axis=1).reshape(-1)
    weight_rows = jnp.sum(take(7), axis=1).reshape(-1)
    weight_totals = jnp.sum(take(8), axis=(0, 1))
    updates = []
    for i in range(3):
        second = rows_new[i][:, None] * cols_new[i][None, :] / row_means[i]
        updates.append(gradients[i] * lax.rsqrt(second))
    flat = jnp.stack([jnp.sum(update * update) for update in updates])
    flat = jnp.broadcast_to(jnp.pad(flat, (0, 5))[:, None], (8, LANES))
    totals = jnp.sum(gather_all(flat)[:, :, :, 0], axis=(0, 1))
    new_weights = []
    for i in range(3):
        clip_factor = jnp.maximum(1.0, jnp.sqrt(totals[i] / entries[i]) / CLIP_LIMIT)
        step_size = STEP_RATE * jnp.maximum(EPS_TWO, jnp.sqrt(weight_totals[i] / entries[i]))
        new_weights.append(weights_old[i] - step_size / clip_factor * updates[i])
    bias_rows = FF // D
    row_places = jnp.arange(VEC)
    counts = jnp.where(row_places < bias_rows, float(FF), float(D))
    grouped_updates = jnp.where(row_places < bias_rows, jnp.sum(step_rows[:bias_rows]), step_rows)
    grouped_weights = jnp.where(row_places < bias_rows, jnp.sum(weight_rows[:bias_rows]), weight_rows)
    clip_rows = jnp.maximum(1.0, jnp.sqrt(grouped_updates / counts) / CLIP_LIMIT)
    step_sizes = STEP_RATE * jnp.maximum(EPS_TWO, jnp.sqrt(grouped_weights / counts))
    factor_rows = lax.dynamic_slice_in_dim(step_sizes / clip_rows, dp_place * rows_v, rows_v)
    vectors_new = vectors - factor_rows[:, None] * vector_step
    return (
        block_out,
        input_grad,
        attn_grad,
        in_grad,
        out_grad,
        vector_grad,
        rows_new[0],
        cols_new[0],
        rows_new[1],
        cols_new[1],
        rows_new[2],
        cols_new[2],
        moment_new,
        new_weights[0],
        new_weights[1],
        new_weights[2],
        vectors_new,
    )


def solution(mesh):
    dp_count, fsdp_count = mesh.shape["dp"], mesh.shape["fsdp"]
    inner = jax.sharding.Mesh(mesh.devices.reshape(dp_count, fsdp_count // 2, 2), ALL)
    fsdp = ("chip", "core")
    split = P(ALL, None)
    block = P("dp", fsdp)
    stats = (P("dp"), P(fsdp)) * 3
    plain = dp_count == VDP and fsdp_count == 2 * VCHIP
    return jax.shard_map(
        body if plain else body_any,
        mesh=inner,
        in_specs=(split,) * 3 + (block,) * 4 + stats + (block,),
        out_specs=(split,) * 2 + (block,) * 4 + stats + (block,) * 5,
        check_vma=False,
    )
```

```python
import functools
import math

import jax
import jax.numpy as jnp
import numpy as np
from jax import lax
from jax.experimental import pallas as pl
from jax.experimental.pallas import tpu as pltpu
from jax.sharding import PartitionSpec as P

D = 256
FF = 2048
HEADS = 8
HEAD_DIM = 32
SEQ = 1024
HALF = 512
GROUP = 4
LANES = 128
QBLOCK = 256
WGRID = 32
STEP = 10
VEC = 16
TILE = 1024
CHUNK = 256
SUB = 512
LEAD = 5
STRIP = 64
VDP = 4
VCHIP = 4
VROWS = 16

EPS_NORM = 1e-05
EPS_ONE = 1e-30
EPS_TWO = 0.001
CLIP_LIMIT = 1.0
STEP_RATE = 0.3
FAR = 1e30
LOG2_E = math.log2(math.e)
SCALE = HEAD_DIM ** (-0.5)
GELU_A = math.sqrt(2.0 / math.pi)
GELU_B = 0.044715
F32 = jnp.float32
BF16 = jnp.bfloat16
MIB = 1024 * 1024


def dot(left, right):
    return jnp.dot(left, right, preferred_element_type=F32)


def dot_nt(left, right):
    return lax.dot_general(left, right, (((1,), (1,)), ((), ())), preferred_element_type=F32)


def encode_table():
    half = D // 2
    feature = np.arange(half)
    freq = np.exp(
        (2 * (feature // 2)).astype(np.float32) * np.float32(-math.log(10000.0) / half)
    ).astype(np.float32)
    angles = np.arange(1, WGRID + 1, dtype=np.float32)[:, None] * freq[None, :]
    table = np.where(feature % 2 == 0, np.sin(angles), np.cos(angles)).astype(np.float32)
    low = jnp.bfloat16
    one = table.astype(low)
    rest = table - one.astype(np.float32)
    two = rest.astype(low)
    three = (rest - two.astype(np.float32)).astype(low)
    blank = np.zeros((LANES - 3 * WGRID, half), low)
    return np.concatenate([one, two, three, blank], axis=0)


def iota(shape, dim):
    return lax.broadcasted_iota(jnp.int32, shape, dim)


def norm_forward(rows):
    centered = rows - jnp.mean(rows, axis=-1, keepdims=True)
    inverse = lax.rsqrt(jnp.mean(centered * centered, axis=-1, keepdims=True) + EPS_NORM)
    return centered * inverse, inverse


def norm_backward(upstream, normed, inverse):
    return inverse * (
        upstream
        - jnp.mean(upstream, axis=-1, keepdims=True)
        - normed * jnp.mean(upstream * normed, axis=-1, keepdims=True)
    )

def vspec():
    return pl.BlockSpec(memory_space=pltpu.VMEM)


def params(mib=56, **more):
    return pltpu.CompilerParams(vmem_limit_bytes=mib * MIB, **more)


def pack_kernel(place, attn_ref, vector_ref, out_ref):
    owner = place[1] * 2 + place[2]
    vector = vector_ref[...]
    rows = vector.shape[0]
    wide = jnp.concatenate([vector] * (LANES // vector.shape[1]), axis=1)
    slot = iota((rows, LANES), 1) // vector.shape[1]
    per = LANES // vector.shape[1]
    parts = [attn_ref[...]]
    for half in range(2):
        parts.append(jnp.where(slot + half * per == owner, wide, 0.0))
    parts.append(jnp.zeros((VROWS - 2 * rows, LANES), F32))
    piece = jnp.concatenate(parts, axis=0).astype(BF16)
    for at in range(VDP * VCHIP):
        out_ref[at] = piece


def pack_attn(place, attn_weight, vectors):
    return pl.pallas_call(
        pack_kernel,
        out_shape=jax.ShapeDtypeStruct((VDP * VCHIP, attn_weight.shape[0] + VROWS, LANES), BF16),
        in_specs=[pl.BlockSpec(memory_space=pltpu.SMEM), vspec(), vspec()],
        out_specs=vspec(),
        compiler_params=params(),
        name="pack_attn",
    )(place, attn_weight, vectors)


def pack_ffn_kernel(first_ref, second_ref, *refs):
    out_ref = refs[-1]
    first = first_ref[...].astype(BF16)
    second = second_ref[...].astype(BF16)
    for at in range(VDP * VCHIP):
        out_ref[at, 0] = first
        out_ref[at, 1] = second


def pack_ffn(ffn_in, ffn_out, *earlier):
    return pl.pallas_call(
        pack_ffn_kernel,
        out_shape=jax.ShapeDtypeStruct((VDP * VCHIP, 2) + ffn_in.shape, BF16),
        in_specs=[vspec(), vspec()] + [pl.BlockSpec(memory_space=pl.ANY)] * len(earlier),
        out_specs=vspec(),
        compiler_params=params(),
        name="pack_ffn",
    )(ffn_in, ffn_out, *earlier)


def place_kernel(
    segment_ref, tokens_ref, back_ref, table_ref, qk_ref, x_ref, qk_t_ref, x_t_ref, turned_ref, marks_ref
):
    row = pl.program_id(0)
    starts = []
    for number in range(1, 4):
        at = jnp.int32(0)
        for step in (512, 256, 128, 64, 32, 16, 8, 4, 2, 1, 1):
            probe = jnp.minimum(at + (step - 1), SEQ - 1)
            at = jnp.where(segment_ref[row, probe] < number, at + step, at)
        starts.append(at)
    edges = [jnp.int32(0)] + starts + [jnp.int32(SEQ)]
    begin = jnp.int32(0)
    for number in range(3, -1, -1):
        begin = jnp.where(edges[number + 1] - edges[number] == HALF, edges[number], begin)
    for number in range(3):
        marks_ref[row, number] = starts[number]
    marks_ref[row, 3] = begin
    one, two, three = starts
    x = pltpu.roll(tokens_ref[...].astype(F32), (SEQ - begin) & (SEQ - 1), 0)
    x_ref[...] = x.astype(BF16)
    x_t_ref[...] = x.T.astype(BF16)
    back = back_ref[...].astype(F32)
    turned_ref[...] = pltpu.roll(back, (SEQ - begin) & (SEQ - 1), 0).astype(BF16)
    at = (iota((SEQ, LANES), 0) + begin) & (SEQ - 1)
    lane = iota((SEQ, LANES), 1)
    start = jnp.where(at >= three, three, jnp.where(at >= two, two, jnp.where(at >= one, one, 0)))
    local = at - start
    kept = lane < 3 * WGRID
    slot = lane & (WGRID - 1)
    hot_r = jnp.where(((local >> 5) == slot) & kept, 1.0, 0.0).astype(BF16)
    hot_c = jnp.where(((local & (WGRID - 1)) == slot) & kept, 1.0, 0.0).astype(BF16)
    table = table_ref[...]
    places = jnp.concatenate([dot(hot_r, table), dot(hot_c, table)], axis=1)
    qk = x + places
    qk_ref[...] = qk.astype(BF16)
    qk_t_ref[...] = qk.T.astype(BF16)


def place_tokens(segment_ids, tokens, cotangent, table):
    rows = segment_ids.shape[0]
    by_row = lambda r: (r, 0)
    return pl.pallas_call(
        place_kernel,
        out_shape=(
            jax.ShapeDtypeStruct(tokens.shape, BF16),
            jax.ShapeDtypeStruct(tokens.shape, BF16),
            jax.ShapeDtypeStruct((D, tokens.shape[0]), BF16),
            jax.ShapeDtypeStruct((D, tokens.shape[0]), BF16),
            jax.ShapeDtypeStruct(tokens.shape, BF16),
            jax.ShapeDtypeStruct((rows, 4), jnp.int32),
        ),
        grid=(rows,),
        in_specs=[
            pl.BlockSpec(memory_space=pltpu.SMEM),
            pl.BlockSpec((SEQ, D), by_row),
            pl.BlockSpec((SEQ, D), by_row),
            pl.BlockSpec((LANES, LANES), lambda r: (0, 0)),
        ],
        out_specs=(
            pl.BlockSpec((SEQ, D), by_row),
            pl.BlockSpec((SEQ, D), by_row),
            pl.BlockSpec((D, SEQ), lambda r: (0, r)),
            pl.BlockSpec((D, SEQ), lambda r: (0, r)),
            pl.BlockSpec((SEQ, D), by_row),
            pl.BlockSpec(memory_space=pltpu.SMEM),
        ),
        compiler_params=params(dimension_semantics=("arbitrary",)),
        cost_estimate=pl.CostEstimate(flops=600_000_000, bytes_accessed=4_000_000, transcendentals=0),
        name="place_tokens",
    )(segment_ids, tokens, cotangent, table)


def attend_kernel(
    marks,
    place,
    x_ref,
    qk_ref,
    x_t_ref,
    qk_t_ref,
    mine_ref,
    other_ref,
    query_t_ref,
    value_ref,
    key_t_ref,
    out_t_ref,
    inverse_ref,
    mixed_ref,
    mixed_t_ref,
    exps_ref,
    weight_ref,
    proj_ref,
    vector_ref,
    key_s,
    value_s,
    mark_k,
    mark_q,
    masked_s,
    weight_t_s,
    bias_s,
):
    row = pl.program_id(0)
    group = pl.program_id(1)
    begin = marks[row, 3]
    core = place[2]

    @pl.when((row == 0) & (group == 0))
    def _():
        tall = D // VDP
        for d in range(VDP):
            rows = slice(d * tall, (d + 1) * tall)
            total = jnp.zeros((8, LANES), F32)
            for c in range(VCHIP):
                for ref, half in ((mine_ref, core), (other_ref, 1 - core)):
                    if c < 3:
                        to = pl.ds(pl.multiple_of(c * D + half * LANES, LANES), LANES)
                        weight_ref[rows, to] = ref[d, c, :tall, :]
                    else:
                        to = pl.ds(pl.multiple_of(half * LANES, LANES), LANES)
                        proj_ref[rows, to] = ref[d, c, :tall, :]
                    total += ref[d, c, tall:, :].astype(F32)[:8]
            vector_ref[d * 4 : (d + 1) * 4, :LANES] = total[:4]
            vector_ref[d * 4 : (d + 1) * 4, LANES:] = total[4:]
        weight_t_s[...] = weight_ref[...].astype(F32).T.astype(BF16)
        bias_s[...] = vector_ref[8:16, :].T

    @pl.when(group == 0)
    def _():
        qk_t = qk_t_ref[...]
        query_t = (dot(weight_t_s[:D, :], qk_t) + bias_s[:, 0:1]) * SCALE
        query_t_ref[...] = query_t.astype(BF16)
        key_t_ref[...] = dot(weight_t_s[D : 2 * D, :], qk_t).astype(BF16)
        key_s[...] = dot(qk_ref[...], weight_ref[:, D : 2 * D]).astype(BF16)
        value = dot(x_ref[...], weight_ref[:, 2 * D : 3 * D]) + vector_ref[9:10, :]
        value_ref[...] = value.astype(BF16)
        value_t = dot(weight_t_s[2 * D :, :], x_t_ref[...]) + bias_s[:, 1:2]
        value_t = value_t.astype(BF16)
        for head in range(HEADS):
            value_s[head, :HEAD_DIM, :] = value_t[head * HEAD_DIM : (head + 1) * HEAD_DIM, :]
            value_s[head, HEAD_DIM:, :] = jnp.ones((16, SEQ), BF16)
        one, two, three = marks[row, 0], marks[row, 1], marks[row, 2]

        def number_of(shape, dim):
            here = (iota(shape, dim) + (HALF + begin)) & (SEQ - 1)
            return (
                jnp.where(here >= one, 1, 0)
                + jnp.where(here >= two, 1, 0)
                + jnp.where(here >= three, 1, 0)
            )

        lane = iota((HALF, LANES), 1)
        number = number_of((HALF, LANES), 0)
        mark_k[...] = jnp.where((number != lane) & (lane < 4), -FAR, 0.0).astype(BF16)
        number = number_of((LANES, HALF), 1)
        mark_q[...] = jnp.where(number == iota((LANES, HALF), 0), 1.0, 0.0).astype(BF16)

    lanes = pl.ds(pl.multiple_of(group * LANES, LANES), LANES)
    head_of = iota((1, LANES), 1) // HEAD_DIM
    keys_here = key_s[:, lanes]
    for at_head in range(GROUP):
        mask = jnp.where(head_of == at_head, 1.0, 0.0).astype(BF16)
        masked_s[at_head] = keys_here * mask

    def scores_of(item):
        half, at_head, block = item
        key_m = masked_s[at_head, half * HALF : (half + 1) * HALF, :]
        at = half * HALF + block * QBLOCK
        query = query_t_ref[lanes, at : at + QBLOCK]
        if half == 1:
            key_m = jnp.concatenate([key_m, mark_k[...]], axis=1)
            query = jnp.concatenate(
                [query, mark_q[:, block * QBLOCK : (block + 1) * QBLOCK]], axis=0
            )
        return dot(key_m, query)

    def exps_of(item, largest):
        half, at_head, block = item
        cols = slice(at_head * HALF + block * QBLOCK, at_head * HALF + (block + 1) * QBLOCK)
        exps = jnp.exp2((scores_of(item) - largest) * LOG2_E)
        exps_ref[0, 0, half, :, cols] = exps.astype(BF16)

    def finish(item):
        half, at_head, block = item
        at = half * HALF + block * QBLOCK
        rows = slice(half * HALF, (half + 1) * HALF)
        cols = slice(at_head * HALF + block * QBLOCK, at_head * HALF + (block + 1) * QBLOCK)
        out = dot(value_s[group * GROUP + at_head, :, rows], exps_ref[0, 0, half, :, cols])
        inverse = 1.0 / out[HEAD_DIM : HEAD_DIM + 1, :]
        inverse_ref[0, at_head : at_head + 1, at : at + QBLOCK] = inverse
        out_t_ref[at_head * HEAD_DIM : (at_head + 1) * HEAD_DIM, at : at + QBLOCK] = (
            out[:HEAD_DIM, :] * inverse
        )

    items = [
        (half, at_head, block)
        for half in range(2)
        for at_head in range(GROUP)
        for block in range(HALF // QBLOCK)
    ]
    largest = {}
    for i in range(len(items) + 2):
        if i < len(items):
            largest[i] = jnp.max(scores_of(items[i]), axis=0, keepdims=True)
        if 1 <= i <= len(items):
            exps_of(items[i - 1], largest.pop(i - 1))
        if i >= 2:
            finish(items[i - 2])
    out_t = out_t_ref[...]
    mixed_t_ref[...] = out_t.astype(BF16)
    mixed_ref[...] = out_t.T.astype(BF16)


def attend_forward(marks, place, x, qk, x_t, qk_t, mine, other):
    total = x.shape[0]
    rows = total // SEQ
    by_row = lambda r, g, m, p: (r, 0)
    by_col = lambda r, g, m, p: (0, r)
    by_both = lambda r, g, m, p: (g, r)
    whole = lambda r, g, m, p: (0, 0)
    return pl.pallas_call(
        attend_kernel,
        out_shape=(
            jax.ShapeDtypeStruct((D, total), BF16),
            jax.ShapeDtypeStruct((total, D), BF16),
            jax.ShapeDtypeStruct((D, total), BF16),
            jax.ShapeDtypeStruct((D, total), F32),
            jax.ShapeDtypeStruct((2, 8, total), F32),
            jax.ShapeDtypeStruct((total, D), BF16),
            jax.ShapeDtypeStruct((D, total), BF16),
            jax.ShapeDtypeStruct((rows, 2, 2, HALF, GROUP * HALF), BF16),
            jax.ShapeDtypeStruct((D, 3 * D), BF16),
            jax.ShapeDtypeStruct((D, D), BF16),
            jax.ShapeDtypeStruct((VEC, D), F32),
        ),
        grid_spec=pltpu.PrefetchScalarGridSpec(
            num_scalar_prefetch=2,
            grid=(rows, 2),
            in_specs=[
                pl.BlockSpec((SEQ, D), by_row),
                pl.BlockSpec((SEQ, D), by_row),
                pl.BlockSpec((D, SEQ), by_col),
                pl.BlockSpec((D, SEQ), by_col),
                vspec(),
                vspec(),
            ],
            out_specs=[
                pl.BlockSpec((D, SEQ), by_col),
                pl.BlockSpec((SEQ, D), by_row),
                pl.BlockSpec((D, SEQ), by_col),
                pl.BlockSpec((LANES, SEQ), by_both),
                pl.BlockSpec((1, 8, SEQ), lambda r, g, m, p: (g, 0, r)),
                pl.BlockSpec((SEQ, LANES), lambda r, g, m, p: (r, g)),
                pl.BlockSpec((LANES, SEQ), by_both),
                pl.BlockSpec((1, 1, 2, HALF, GROUP * HALF), lambda r, g, m, p: (r, g, 0, 0, 0)),
                pl.BlockSpec((D, 3 * D), whole),
                pl.BlockSpec((D, D), whole),
                pl.BlockSpec((VEC, D), whole),
            ],
            scratch_shapes=[
                pltpu.VMEM((SEQ, D), BF16),
                pltpu.VMEM((HEADS, HEAD_DIM + 16, SEQ), BF16),
                pltpu.VMEM((HALF, LANES), BF16),
                pltpu.VMEM((LANES, HALF), BF16),
                pltpu.VMEM((GROUP, SEQ, LANES), BF16),
                pltpu.VMEM((3 * D, D), BF16),
                pltpu.VMEM((D, 8), F32),
            ],
        ),
        compiler_params=params(dimension_semantics=("arbitrary", "arbitrary")),
        cost_estimate=pl.CostEstimate(
            flops=20_000_000_000, bytes_accessed=30_000_000, transcendentals=8_400_000
        ),
        name="attend_forward",
    )(marks, place, x, qk, x_t, qk_t, mine, other)


def feed_kernel(
    marks,
    place,
    x_ref,
    back_ref,
    mixed_ref,
    mixed_t_ref,
    proj_ref,
    mine_ref,
    other_ref,
    vector_ref,
    block_ref,
    resid_ref,
    mixed_grad_ref,
    mine_out,
    other_out,
    proj_out,
    vector_out,
    first_w,
    second_w,
    first_acc,
    second_acc,
    proj_acc,
    vector_acc,
    hidden_s,
    slope_s,
    pre_s,
    first_low_s,
    branch_low_s,
    attended_s,
    block_s,
    eye_s,
):
    step = pl.program_id(0)
    core = place[2]
    tall = D // VDP
    wide = FF // (2 * VCHIP)

    @pl.when(step == 0)
    def _():
        first_acc[...] = jnp.zeros_like(first_acc)
        second_acc[...] = jnp.zeros_like(second_acc)
        proj_acc[...] = jnp.zeros_like(proj_acc)
        vector_acc[...] = jnp.zeros_like(vector_acc)
        eye_s[...] = jnp.where(iota((D, D), 0) == iota((D, D), 1), 1.0, 0.0).astype(BF16)
        for d in range(VDP):
            rows = slice(d * tall, (d + 1) * tall)
            for c in range(VCHIP):
                for ref, half in ((mine_ref, core), (other_ref, 1 - core)):
                    to = pl.ds(pl.multiple_of((2 * c + half) * wide, wide), wide)
                    first_w[rows, to] = ref[d, c, 0]
                    second_w[rows, to] = ref[d, c, 1]

    bias_o, bias_2 = vector_ref[10:11, :], vector_ref[11:12, :]
    gain_1, shift_1 = vector_ref[12:13, :], vector_ref[13:14, :]
    gain_2, shift_2 = vector_ref[14:15, :], vector_ref[15:16, :]
    at_row = pl.multiple_of((step % (SEQ // TILE)) * TILE, TILE)
    chunks = FF // CHUNK
    pair = 2

    def columns(at, count=1):
        return slice(at * CHUNK, (at + count) * CHUNK)

    def hidden_of(rows, at, pre):
        pre = (pre + vector_ref[at : at + 1, :]).astype(BF16)
        cube = BF16(GELU_A * GELU_B) * (pre * pre)
        gate = BF16(0.5) + BF16(0.5) * jnp.tanh(pre * (cube + BF16(GELU_A)))
        hidden_s[rows, columns(at)] = pre * gate
        slope_s[rows, columns(at)] = gate + (gate - gate * gate) * (
            pre * (BF16(6.0) * cube + BF16(2.0 * GELU_A))
        )

    def stages(sub):
        rows_at = sub * SUB
        rows = slice(rows_at, rows_at + SUB)
        attended = dot(mixed_ref[rows, :], proj_ref[...]) + bias_o
        norm_1, inverse_1 = norm_forward(x_ref[rows, :].astype(F32) + attended)
        first = norm_1 * gain_1 + shift_1
        first_low = first.astype(BF16)
        first_low_s[rows, :] = first_low
        yield
        branch = jnp.zeros((SUB, D), F32)
        for i in range(chunks + 1):
            if i < chunks:
                hidden_of(rows, i, dot(first_low, first_w[:, columns(i)]))
            if i >= pair and i % pair == 0:
                cols = columns(i - pair, pair)
                branch += dot_nt(hidden_s[rows, cols], second_w[:, cols])
            yield
        norm_2, inverse_2 = norm_forward(first + (branch + bias_2))
        block_s[pl.ds(at_row + rows_at, SUB), :] = norm_2 * gain_2 + shift_2
        back = back_ref[rows, :].astype(F32)
        vector_acc[14:15, :] += jnp.sum(back * norm_2, axis=0, keepdims=True)
        vector_acc[15:16, :] += jnp.sum(back, axis=0, keepdims=True)
        resid_2 = norm_backward(back * gain_2, norm_2, inverse_2)
        branch_low = resid_2.astype(BF16)
        branch_low_s[rows, :] = branch_low
        vector_acc[11:12, :] += jnp.sum(branch_low.astype(F32), axis=0, keepdims=True)
        yield
        first_back = resid_2
        if sub == 1:
            branch_t = dot_nt(eye_s[...], branch_low_s[...]).astype(BF16)
            first_t = dot_nt(eye_s[...], first_low_s[...]).astype(BF16)
            first_t = jnp.concatenate([first_t, jnp.ones((16, TILE), BF16)], axis=0)
        for i in range(chunks + 1):
            if i < chunks:
                pull = dot(branch_low, second_w[:, columns(i)]).astype(BF16)
                pre_s[rows, columns(i)] = pull * slope_s[rows, columns(i)]
                if sub == 1:
                    second_acc[:, columns(i)] += dot(branch_t, hidden_s[:, columns(i)])
            if i >= 1 and sub == 1:
                cols = columns(i - 1)
                first_acc[:, cols] += dot(first_t, pre_s[:, cols])
            if i >= pair and i % pair == 0:
                cols = columns(i - pair, pair)
                first_back += dot_nt(pre_s[rows, cols], first_w[:, cols])
            yield
        vector_acc[12:13, :] += jnp.sum(first_back * norm_1, axis=0, keepdims=True)
        vector_acc[13:14, :] += jnp.sum(first_back, axis=0, keepdims=True)
        resid_1 = norm_backward(first_back * gain_1, norm_1, inverse_1)
        resid_ref[rows, :] = resid_1
        attended_low = resid_1.astype(BF16)
        attended_s[rows, :] = attended_low
        vector_acc[10:11, :] += jnp.sum(attended_low.astype(F32), axis=0, keepdims=True)
        mixed_grad_ref[:, rows] = dot_nt(proj_ref[...], attended_low).astype(BF16)
        yield

    ahead, behind = stages(0), stages(1)
    for _ in range(LEAD):
        next(ahead)
    running = [ahead, behind]
    while running:
        for program in list(running):
            if next(program, 0) == 0:
                running.remove(program)
    proj_acc[...] += dot(mixed_t_ref[...], attended_s[...])

    @pl.when(step % (SEQ // TILE) == SEQ // TILE - 1)
    def _():
        block_ref[...] = pltpu.roll(block_s[...], marks[step // (SEQ // TILE), 3], 0)

    @pl.when(step == pl.num_programs(0) - 1)
    def _():
        for d in range(VDP):
            rows = slice(d * tall, (d + 1) * tall)
            for c in range(VCHIP):
                for ref, half in ((mine_out, core), (other_out, 1 - core)):
                    to = pl.ds(pl.multiple_of((2 * c + half) * wide, wide), wide)
                    ref[d, c, 0] = first_acc[rows, to].astype(BF16)
                    ref[d, c, 1] = second_acc[rows, to].astype(BF16)
        proj_out[...] = proj_acc[...]
        for at in range(FF // D):
            vector_out[at : at + 1, :] = first_acc[D : D + 1, at * D : (at + 1) * D]
        vector_out[FF // D :, :] = vector_acc[FF // D :, :]


def feed_forward(marks, place, x, back, mixed, mixed_t, proj, mine, other, vector):
    total = x.shape[0]
    tile = lambda i, m, p: (i, 0)
    by_col = lambda i, m, p: (0, i)
    whole = lambda i, m, p: (0, 0)
    whole5 = lambda i, m, p: (0, 0, 0, 0, 0)
    return pl.pallas_call(
        feed_kernel,
        out_shape=(
            jax.ShapeDtypeStruct((total, D), F32),
            jax.ShapeDtypeStruct((total, D), F32),
            jax.ShapeDtypeStruct((D, total), BF16),
            jax.ShapeDtypeStruct(mine.shape, BF16),
            jax.ShapeDtypeStruct(mine.shape, BF16),
            jax.ShapeDtypeStruct((D, D), F32),
            jax.ShapeDtypeStruct((VEC, D), F32),
        ),
        grid_spec=pltpu.PrefetchScalarGridSpec(
            num_scalar_prefetch=2,
            grid=(total // TILE,),
            in_specs=[
                pl.BlockSpec((TILE, D), tile),
                pl.BlockSpec((TILE, D), tile),
                pl.BlockSpec((TILE, D), tile),
                pl.BlockSpec((D, TILE), by_col),
                pl.BlockSpec((D, D), whole),
                vspec(),
                vspec(),
                pl.BlockSpec((VEC, D), whole),
            ],
            out_specs=[
                pl.BlockSpec((SEQ, D), lambda i, m, p: (i // (SEQ // TILE), 0)),
                pl.BlockSpec((TILE, D), tile),
                pl.BlockSpec((D, TILE), by_col),
                pl.BlockSpec(mine.shape, whole5),
                pl.BlockSpec(mine.shape, whole5),
                pl.BlockSpec((D, D), whole),
                pl.BlockSpec((VEC, D), whole),
            ],
            scratch_shapes=[
                pltpu.VMEM((D, FF), BF16),
                pltpu.VMEM((D, FF), BF16),
                pltpu.VMEM((D + 16, FF), F32),
                pltpu.VMEM((D, FF), F32),
                pltpu.VMEM((D, D), F32),
                pltpu.VMEM((VEC, D), F32),
                pltpu.VMEM((TILE, FF), BF16),
                pltpu.VMEM((TILE, FF), BF16),
                pltpu.VMEM((TILE, FF), BF16),
                pltpu.VMEM((TILE, D), BF16),
                pltpu.VMEM((TILE, D), BF16),
                pltpu.VMEM((TILE, D), BF16),
                pltpu.VMEM((SEQ, D), F32),
                pltpu.VMEM((D, D), BF16),
            ],
        ),
        compiler_params=params(dimension_semantics=("arbitrary",)),
        cost_estimate=pl.CostEstimate(
            flops=14_000_000_000, bytes_accessed=15_000_000, transcendentals=4_200_000
        ),
        name="feed_forward",
    )(marks, place, x, back, mixed, mixed_t, proj, mine, other, vector)


def pull_kernel(
    own,
    marks,
    place,
    grad_t_ref,
    query_t_ref,
    value_ref,
    key_t_ref,
    out_t_ref,
    inverse_ref,
    exps_ref,
    qk_t_ref,
    x_t_ref,
    weight_ref,
    proj_ref,
    *refs,
):
    if own:
        resid_ref, other_ref, pulled_ref, grads_ref, sums_ref = refs[:5]
    else:
        pulled_ref, grads_ref, sums_ref = refs[:3]
    dot_s, query_g, key_g, value_g, acc, sum_acc, value_s, scaled_t_s, score_s = refs[-9:]
    row = pl.program_id(0)
    begin = marks[row, 3]
    group = place[2] if own else 1 - place[2]

    @pl.when(row == 0)
    def _():
        acc[...] = jnp.zeros_like(acc)
        sum_acc[...] = jnp.zeros_like(sum_acc)

    grad_t = grad_t_ref[...].astype(F32)
    head_of = iota((1, LANES), 1) // HEAD_DIM
    for at_head in range(GROUP):
        heads = slice(at_head * HEAD_DIM, (at_head + 1) * HEAD_DIM)
        part = grad_t[heads, :] * inverse_ref[0, at_head : at_head + 1, :]
        dot_s[at_head : at_head + 1, :] = jnp.sum(part * out_t_ref[heads, :], axis=0, keepdims=True)
        part = part.astype(BF16)
        scaled_t_s[heads, :] = part
        mask = jnp.where(head_of == at_head, 1.0, 0.0).astype(BF16)
        for half in range(2):
            rows = slice(half * HALF, (half + 1) * HALF)
            to = slice(at_head * HALF, (at_head + 1) * HALF)
            value_s[half, to, :] = value_ref[rows, :] * mask

    def score_grad_of(item):
        half, at_head, block = item
        at = half * HALF + block * QBLOCK
        cols = slice(at_head * HALF + block * QBLOCK, at_head * HALF + (block + 1) * QBLOCK)
        value = value_s[half, at_head * HALF : (at_head + 1) * HALF, :]
        pull = dot(value, scaled_t_s[:, at : at + QBLOCK])
        pull = (pull - dot_s[at_head : at_head + 1, at : at + QBLOCK]).astype(BF16)
        score_s[half, :, cols] = exps_ref[0, 0, half, :, cols] * pull

    def finish(half, at_head):
        cols = slice(at_head * HALF, (at_head + 1) * HALF)
        rows = slice(half * HALF, (half + 1) * HALF)
        heads = slice(at_head * HEAD_DIM, (at_head + 1) * HEAD_DIM)
        score_grad = score_s[half, :, cols]
        value_g[heads, rows] = dot_nt(scaled_t_s[heads, rows], exps_ref[0, 0, half, :, cols])
        query_g[heads, rows] = dot(key_t_ref[heads, rows], score_grad)
        key_g[heads, rows] = dot_nt(query_t_ref[heads, rows], score_grad)

    items = [
        (half, at_head, block)
        for half in range(2)
        for at_head in range(GROUP)
        for block in range(HALF // QBLOCK)
    ]
    for i in range(len(items) + 1):
        if i < len(items):
            score_grad_of(items[i])
        if i >= 2 and i % 2 == 0:
            finish(*items[i - 1][:2])
    query_low = query_g[...].astype(BF16)
    both_low = jnp.concatenate([key_g[...].astype(BF16), value_g[...].astype(BF16)], axis=0)
    ones = jnp.ones((16, SEQ), BF16)
    sum_acc[0:1, :] += dot_nt(ones, query_low)[0:1, :] * SCALE
    sum_acc[1:2, :] += dot_nt(ones, both_low[LANES:, :])[0:1, :]
    qk_t = qk_t_ref[...]
    both = dot_nt(qk_t, jnp.concatenate([query_low, both_low[:LANES, :]], axis=0))
    acc[:, :LANES] += both[:, :LANES] * SCALE
    acc[:, LANES : 2 * LANES] += both[:, LANES:]
    acc[:, 2 * LANES :] += dot_nt(x_t_ref[...], both_low[LANES:, :])
    at = [pl.ds(pl.multiple_of(i * D + group * LANES, LANES), LANES) for i in range(3)]
    pulled = dot(weight_ref[:, at[0]], query_low) * SCALE + dot(
        jnp.concatenate([weight_ref[:, at[1]], weight_ref[:, at[2]]], axis=1), both_low
    )
    if own:
        pulled = (pulled + other_ref[...]).T
        pulled_ref[...] = pltpu.roll(resid_ref[...] + pulled, begin, 0)
    else:
        pulled_ref[...] = pulled

    @pl.when(row == pl.num_programs(0) - 1)
    def _():
        tall = D // VDP
        for d in range(VDP):
            rows = slice(d * tall, (d + 1) * tall)
            for c in range(3):
                grads_ref[d, c] = acc[rows, c * LANES : (c + 1) * LANES].astype(BF16)
            grads_ref[d, 3] = proj_ref[rows, :].astype(BF16)
        sums_ref[...] = sum_acc[...]


def attend_back(own, marks, place, grad_t, query_t, value, key_t, out_t, inverse, exps, qk_t, x_t, weight, proj, *more):
    total = value.shape[0]
    rows = total // SEQ
    pick = (lambda p: p[2]) if own else (lambda p: 1 - p[2])
    by_group = lambda r, m, p: (r, pick(p))
    by_row = lambda r, m, p: (r, 0)
    whole = lambda r, m, p: (0, 0)
    in_specs = [
        pl.BlockSpec((LANES, SEQ), lambda r, m, p: (pick(p), r)),
        pl.BlockSpec((LANES, SEQ), lambda r, m, p: (pick(p), r)),
        pl.BlockSpec((SEQ, LANES), by_group),
        pl.BlockSpec((LANES, SEQ), lambda r, m, p: (pick(p), r)),
        pl.BlockSpec((LANES, SEQ), lambda r, m, p: (pick(p), r)),
        pl.BlockSpec((1, 8, SEQ), lambda r, m, p: (pick(p), 0, r)),
        pl.BlockSpec((1, 1, 2, HALF, GROUP * HALF), lambda r, m, p: (r, pick(p), 0, 0, 0)),
        pl.BlockSpec((D, SEQ), lambda r, m, p: (0, r)),
        pl.BlockSpec((D, SEQ), lambda r, m, p: (0, r)),
        pl.BlockSpec((D, 3 * D), whole),
        pl.BlockSpec((D, LANES), lambda r, m, p: (0, pick(p))),
    ]
    by_col = pl.BlockSpec((D, SEQ), lambda r, m, p: (0, r))
    if own:
        in_specs += [pl.BlockSpec((SEQ, D), by_row), by_col]
    return pl.pallas_call(
        functools.partial(pull_kernel, own),
        out_shape=(
            jax.ShapeDtypeStruct((total, D) if own else (D, total), F32),
            jax.ShapeDtypeStruct((VDP, VCHIP, D // VDP, LANES), BF16),
            jax.ShapeDtypeStruct((8, LANES), F32),
        ),
        grid_spec=pltpu.PrefetchScalarGridSpec(
            num_scalar_prefetch=2,
            grid=(rows,),
            in_specs=in_specs,
            out_specs=[
                pl.BlockSpec((SEQ, D), by_row) if own else by_col,
                pl.BlockSpec((VDP, VCHIP, D // VDP, LANES), lambda r, m, p: (0, 0, 0, 0)),
                pl.BlockSpec((8, LANES), whole),
            ],
            scratch_shapes=[
                pltpu.VMEM((8, SEQ), F32),
                pltpu.VMEM((LANES, SEQ), F32),
                pltpu.VMEM((LANES, SEQ), F32),
                pltpu.VMEM((LANES, SEQ), F32),
                pltpu.VMEM((D, 3 * LANES), F32),
                pltpu.VMEM((8, LANES), F32),
                pltpu.VMEM((2, GROUP * HALF, LANES), BF16),
                pltpu.VMEM((LANES, SEQ), BF16),
                pltpu.VMEM((2, HALF, GROUP * HALF), BF16),
            ],
        ),
        compiler_params=params(dimension_semantics=("arbitrary",)),
        cost_estimate=pl.CostEstimate(
            flops=18_000_000_000, bytes_accessed=15_000_000, transcendentals=0
        ),
        name="attend_back",
    )(marks, place, grad_t, query_t, value, key_t, out_t, inverse, exps, qk_t, x_t, weight, proj, *more)


def sums_by_group(place, sums_own, sums_other):
    first = place[2] == 0
    return (
        jnp.where(first, sums_own, sums_other),
        jnp.where(first, sums_other, sums_own),
    )


def two_terms(rows):
    high = rows.astype(BF16)
    return jnp.concatenate([high.astype(F32), rows - high.astype(F32)], axis=0)


def column_to_row(columns, rows):
    lane = iota((rows, LANES), 1)
    wide = jnp.zeros((rows, LANES), F32)
    for i, column in enumerate(columns):
        wide = jnp.where(lane == i, column, wide)
    return wide.T[:8, :]


def total_of(array):
    return jnp.sum(jnp.sum(array, axis=0, keepdims=True), axis=1, keepdims=True)


def tail_ffn_kernel(place, ffn_ref, rows_1, rows_2, last_ref, grad_ref, stat_ref):
    lane = iota((1, LANES), 1)
    piece, across = [], []
    for kind in range(2):
        total = ffn_ref[0, kind].astype(F32)
        for at in range(1, VDP * VCHIP):
            total = total + ffn_ref[at, kind].astype(F32)
        grad_ref[kind] = total
        square = total * total + EPS_ONE
        down = jnp.sum(square, axis=0, keepdims=True)
        piece += [down[:, :LANES], down[:, LANES:]]
        across.append(jnp.sum(square, axis=1, keepdims=True))
    across = column_to_row(across, total.shape[0])
    across = jnp.concatenate([across[0:1], across[1:2]], axis=1)
    olds = jnp.zeros((1, LANES), F32)
    for i, ref in enumerate((rows_1, rows_2)):
        olds = jnp.where(lane == i, jnp.sum(ref[...], axis=1, keepdims=True), olds)
    stat_ref[...] = jnp.concatenate([across] + piece + [olds, jnp.zeros((2, LANES), F32)], axis=0)


def tail_send_kernel(
    place, mine_ref, got_ref, vector_ref, own_ref, other_ref, stat_ref, stat_other_ref, send_ref
):
    tall = D // VDP
    low, high = sums_by_group(place, own_ref[...], other_ref[...])
    vector = jnp.concatenate(
        [
            vector_ref[:8, :],
            jnp.concatenate([low[:2], high[:2]], axis=1),
            vector_ref[10:, :],
        ],
        axis=0,
    )
    stat = jnp.concatenate([stat_ref[0:1, :] + stat_other_ref[0:1, :], stat_ref[1:6, :]], axis=0)
    stat = two_terms(stat)
    rows = VEC // VDP
    for d in range(VDP):
        for c in range(VCHIP):
            at = d * VCHIP + c
            both = mine_ref[d, c].astype(F32) + got_ref[d, c].astype(F32)
            send_ref[at, :tall, :] = both.astype(BF16)
            part = vector[d * rows : (d + 1) * rows, c * 64 : (c + 1) * 64]
            part = jnp.concatenate([part, jnp.zeros((rows, LANES - 64), F32)], axis=1)
            send_ref[at, tall:, :] = jnp.concatenate([part, stat], axis=0).astype(BF16)


def tail_reduce_kernel(
    place,
    got_ref,
    ffn_grad_ref,
    attn_ref,
    first_ref,
    second_ref,
    rows_0,
    rows_1,
    rows_2,
    cols_0,
    cols_1,
    cols_2,
    vector_ref,
    moment_ref,
    grad_ref,
    update_1,
    update_2,
    rows_out_1,
    rows_out_2,
    cols_out_1,
    cols_out_2,
    send_ref,
):
    decay = 1.0 - STEP ** (-0.8)
    chip = place[1]
    dp = place[0]
    tall = attn_ref.shape[0]
    rows, width = vector_ref.shape
    pieces = VDP * VCHIP
    lane = iota((1, LANES), 1)
    total = got_ref[0, :tall, :].astype(F32)
    part = got_ref[0, tall:, :].astype(F32)[:rows]
    for at in range(1, pieces):
        total = total + got_ref[at, :tall, :].astype(F32)
        part = part + got_ref[at, tall:, :].astype(F32)[:rows]
    grad_ref[...] = total
    low = total.astype(BF16)

    def stat_of(at):
        both = got_ref[pl.ds(at, 1), tall:, :][0].astype(F32)[rows:]
        return both[:6] + both[6:12]

    every = jnp.zeros((1, LANES), F32)
    olds = jnp.zeros((1, LANES), F32)
    mine = jnp.zeros((1, LANES), F32)
    down = jnp.zeros((6, LANES), F32)
    for d in range(VDP):
        down = down + stat_of(d * VCHIP + chip)
        for c in range(VCHIP):
            stat = stat_of(d * VCHIP + c)
            every = every + stat[0:1]
            if c == 0:
                olds = olds + stat[5:6]
    for c in range(VCHIP):
        mine = mine + stat_of(dp * VCHIP + c)[0:1]
    row_total = tall * VDP
    new_rows, means = [], []
    for i, ref in enumerate((rows_1, rows_2)):
        count = first_ref.shape[1] * 2 * VCHIP
        new_rows.append(decay * ref[...] + (1.0 - decay) * (mine[:, i * tall : (i + 1) * tall] / count))
        old = jnp.sum(jnp.where(lane == i, olds, 0.0), axis=1, keepdims=True)
        fresh = jnp.sum(every[:, i * tall : (i + 1) * tall], axis=1, keepdims=True)
        means.append((decay * old + (1.0 - decay) * (fresh / count)) / row_total)
    tile = jnp.concatenate(new_rows + [jnp.zeros((6, tall), F32)], axis=0)
    rows_out_1[...] = new_rows[0]
    rows_out_2[...] = new_rows[1]
    tile = jnp.concatenate([tile, jnp.zeros((8, LANES - tall), F32)], axis=1)
    turned = jnp.concatenate([tile, jnp.zeros((LANES - 8, LANES), F32)], axis=0).T
    scalars = jnp.zeros((1, LANES), F32)
    for i, (old_ref, out_ref, to) in enumerate(
        ((cols_1, cols_out_1, update_1), (cols_2, cols_out_2, update_2))
    ):
        sums = jnp.concatenate([down[1 + 2 * i : 2 + 2 * i], down[2 + 2 * i : 3 + 2 * i]], axis=1)
        cols = decay * old_ref[...] + (1.0 - decay) * (sums / row_total)
        out_ref[...] = cols
        grad = ffn_grad_ref[i]
        update = grad * lax.rsqrt(turned[:tall, i : i + 1] * cols / means[i])
        to[...] = update
        scalars = jnp.where(lane == 67 + i, total_of(update * update), scalars)
    for i, ref in enumerate((attn_ref, first_ref, second_ref)):
        weight = ref[...]
        scalars = jnp.where(lane == 64 + i, total_of(weight * weight), scalars)
    scalars = jnp.concatenate([rows_0[...], scalars[:, tall:]], axis=1)
    vector = vector_ref[...]
    power = jnp.sum(vector * vector, axis=1, keepdims=True)
    lines = jnp.concatenate(
        [part[:, :64], moment_ref[...], jnp.broadcast_to(power, (rows, LANES - 64 - width))], axis=1
    )
    piece = jnp.concatenate(
        [two_terms(lines), two_terms(jnp.concatenate([cols_0[...], scalars], axis=0))]
        + [jnp.zeros((4, LANES), F32)],
        axis=0,
    ).astype(BF16)
    for at in range(pieces):
        send_ref[at, :tall, :] = low
        send_ref[at, tall:, :] = piece


def tail_apply_kernel(
    place,
    mine_ref,
    other_ref,
    grad_ref,
    update_1,
    update_2,
    weight_0,
    weight_1,
    weight_2,
    rows_0,
    cols_0,
    vector_ref,
    moment_ref,
    new_0,
    new_1,
    new_2,
    rows_out,
    cols_out,
    vector_grad_ref,
    moment_out,
    vector_out,
    sums_s,
    rows_s,
):
    decay = 1.0 - STEP ** (-0.8)
    dp, chip, core = place[0], place[1], place[2]
    tall = weight_0.shape[0]
    rows, width = vector_ref.shape
    fsdp = 2 * VCHIP
    lane = iota((1, LANES), 1)
    refs = (mine_ref, other_ref)
    row_total = float(tall * VDP)
    col_total = float(LANES * fsdp)

    def lines_of(ref, at):
        both = ref[at, tall:, :].astype(F32)
        return both[0:4] + both[4:8], both[8:10] + both[10:12]

    scalars = jnp.zeros((1, LANES), F32)
    for ref in refs:
        for at in range(VDP * VCHIP):
            scalars = scalars + lines_of(ref, at)[1][1:2]
    scalar = lambda at: jnp.sum(jnp.where(lane == at, scalars, 0.0), axis=1, keepdims=True)

    tile, fresh = [], []
    for d in range(VDP):
        wide = jnp.zeros((tall, LANES), F32)
        for ref in refs:
            for c in range(VCHIP):
                block = ref[d * VCHIP + c, :tall, :].astype(F32)
                wide = wide + (block * block + EPS_ONE)
        fresh.append(jnp.sum(wide, axis=1, keepdims=True))
        tile.append(lines_of(mine_ref, d * VCHIP)[1][1:2])
    tile = jnp.concatenate(tile + [jnp.zeros((LANES - VDP, LANES), F32)], axis=0).T
    mean = jnp.zeros((1, 1), F32)
    new_rows = []
    for d in range(VDP):
        new = decay * tile[:tall, d : d + 1] + (1.0 - decay) * (fresh[d] / col_total)
        new_rows.append(1.0 / new)
        mean = mean + jnp.sum(new, axis=0, keepdims=True)
        sums_s[d] = jnp.broadcast_to(fresh[d], (tall, LANES))
    mean = mean / row_total
    mine = sums_s[pl.ds(dp, 1)][0]
    rows_s[...] = mine.T
    rows_new = decay * rows_0[...] + (1.0 - decay) * (rows_s[0:1, :tall] / col_total)
    rows_out[...] = rows_new
    power = jnp.zeros((1, 1), F32)
    for half, ref in enumerate(refs):
        for c in range(VCHIP):
            down = jnp.zeros((tall, LANES), F32)
            weighted = jnp.zeros((tall, LANES), F32)
            for d in range(VDP):
                block = ref[d * VCHIP + c, :tall, :].astype(F32)
                square = block * block
                down = down + (square + EPS_ONE)
                weighted = weighted + square * new_rows[d]
            down = jnp.sum(down, axis=0, keepdims=True)
            old = lines_of(ref, c)[1][0:1]
            cols = decay * old + (1.0 - decay) * (down / row_total)
            weighted = jnp.sum(weighted, axis=0, keepdims=True) / cols
            power = power + jnp.sum(weighted, axis=1, keepdims=True)
            if half == 0:
                sums_s[VDP + c] = jnp.broadcast_to(down, (tall, LANES))
    power = power * mean
    down = sums_s[pl.ds(VDP + chip, 1)][0][0:1, :]
    cols_new = decay * cols_0[...] + (1.0 - decay) * (down / row_total)
    cols_out[...] = cols_new
    column = jnp.concatenate(
        [
            jnp.concatenate([rows_new, jnp.zeros((1, LANES - tall), F32)], axis=1),
            jnp.zeros((LANES - 1, LANES), F32),
        ],
        axis=0,
    ).T[:tall, 0:1]
    update_0 = grad_ref[...] * lax.rsqrt(column * cols_new / mean)
    powers = (power, scalar(67), scalar(68))
    for i, (update, weight, new) in enumerate(
        (
            (update_0, weight_0, new_0),
            (update_1[...], weight_1, new_1),
            (update_2[...], weight_2, new_2),
        )
    ):
        entries = float(weight.shape[0] * weight.shape[1] * VDP * fsdp)
        clip = jnp.maximum(1.0, jnp.sqrt(powers[i] / entries) / CLIP_LIMIT)
        rate = STEP_RATE * jnp.maximum(EPS_TWO, jnp.sqrt(scalar(64 + i) / entries))
        new[...] = weight[...] - rate / clip * update
    powers, sizes = [], []
    for d in range(VDP):
        power = jnp.zeros((rows, 1), F32)
        size = jnp.zeros((rows, 1), F32)
        for c in range(VCHIP):
            at = d * VCHIP + c
            first, second = lines_of(mine_ref, at)[0], lines_of(other_ref, at)[0]
            both = first[:, :64] + second[:, :64]
            size = size + first[:, LANES - 1 :] + second[:, LANES - 1 :]
            near = jnp.where(core == 0, first[:, 64 : 64 + width], second[:, 64 : 64 + width])
            far = jnp.where(core == 0, second[:, 64 : 64 + width], first[:, 64 : 64 + width])
            moment = jnp.concatenate([near, far], axis=1)
            moment = decay * moment + (1.0 - decay) * (both * both + EPS_ONE)
            power = power + jnp.sum(both * both / moment, axis=1, keepdims=True)
            wide = jnp.concatenate([both, jnp.zeros((rows, LANES - 64), F32)], axis=1)
            sums_s[2 * VDP + at, :rows, :] = wide
        powers.append(power)
        sizes.append(size)
    both = sums_s[pl.ds(2 * VDP + dp * VCHIP + chip, 1), :rows, :][0]
    vector_grad = jnp.where(core == 0, both[:, :width], both[:, width : 2 * width])
    vector_grad_ref[...] = vector_grad
    moment = decay * moment_ref[...] + (1.0 - decay) * (vector_grad * vector_grad + EPS_ONE)
    moment_out[...] = moment
    step = vector_grad * lax.rsqrt(moment)
    bias = VDP // 2
    bias_power = sum(jnp.sum(power, axis=0, keepdims=True) for power in powers[:bias])
    bias_size = sum(jnp.sum(size, axis=0, keepdims=True) for size in sizes[:bias])
    power, size = powers[bias], sizes[bias]
    for d in range(bias + 1, VDP):
        power = jnp.where(dp == d, powers[d], power)
        size = jnp.where(dp == d, sizes[d], size)
    is_bias = dp < bias
    power = jnp.where(is_bias, bias_power, power)
    size = jnp.where(is_bias, bias_size, size)
    count = jnp.where(is_bias, float(FF), float(D))
    clip = jnp.maximum(1.0, jnp.sqrt(power / count) / CLIP_LIMIT)
    rate = STEP_RATE * jnp.maximum(EPS_TWO, jnp.sqrt(size / count))
    vector_out[...] = vector_ref[...] - rate / clip * step


def whole_call(kernel, name, place, outs, *operands, scratch=()):
    return pl.pallas_call(
        kernel,
        out_shape=[jax.ShapeDtypeStruct(shape, kind) for shape, kind in outs],
        in_specs=[pl.BlockSpec(memory_space=pltpu.SMEM)] + [vspec()] * len(operands),
        out_specs=[vspec()] * len(outs),
        scratch_shapes=list(scratch),
        compiler_params=params(16),
        name=name,
    )(place, *operands)


def core_swap(block):
    return lax.ppermute(block, "core", [(0, 1), (1, 0)])


def exchange(blocks, axes):
    return lax.all_to_all(blocks, axes, split_axis=0, concat_axis=0, tiled=True)


def after(value, *earlier):
    return pl.pallas_call(
        lambda *refs: None,
        out_shape=jax.ShapeDtypeStruct(value.shape, value.dtype),
        in_specs=[pl.BlockSpec(memory_space=pltpu.HBM)] * (1 + len(earlier)),
        out_specs=pl.BlockSpec(memory_space=pltpu.HBM),
        input_output_aliases={0: 0},
        compiler_params=params(),
        name="after",
    )(value, *earlier)


def pair_kernel(mine_ref, got_ref, out_ref):
    out_ref[...] = (mine_ref[...].astype(F32) + got_ref[...].astype(F32)).astype(BF16)


def pair_sum(mine, got):
    return pl.pallas_call(
        pair_kernel,
        out_shape=jax.ShapeDtypeStruct(mine.shape, BF16),
        in_specs=[vspec(), vspec()],
        out_specs=vspec(),
        compiler_params=params(16),
        name="pair_sum",
    )(mine, got)


CHIPS = ("dp", "chip")
ALL = ("dp", "chip", "core")


def layer(place, weights, segment_ids, tokens, cotangent, ffn_weights, send_core, send_ffn):
    table = jnp.asarray(encode_table())
    qk, x, qk_t, x_t, back, marks = place_tokens(segment_ids, tokens, cotangent, table)
    query_t, value, key_t, out_t, inverse, mixed, mixed_t, exps, weight, proj, vector = attend_forward(
        marks, place, x, qk, x_t, qk_t, *weights(marks)
    )
    ffn_mine, ffn_other = ffn_weights(marks, vector)
    block_out, resid, grad_t, ffn_mine, ffn_other, proj_g, vector_g = feed_forward(
        marks, place, x, back, mixed, mixed_t, proj, ffn_mine, ffn_other, vector
    )
    ffn_got, grad_t = send_ffn(ffn_mine, ffn_other, grad_t)
    shared = (marks, place, grad_t, query_t, value, key_t, out_t, inverse, exps, qk_t, x_t, weight, proj_g)
    pulled, grads_other, sums_other = attend_back(False, *shared)
    attn_got = send_core(grads_other)
    input_grad, grads_own, sums_own = attend_back(True, *shared, resid, pulled)
    return block_out, input_grad, grads_own, grads_other, attn_got, sums_own, sums_other, vector_g, ffn_got


def body(
    tokens,
    cotangent,
    segment_ids,
    attn_weight,
    ffn_in,
    ffn_out,
    vectors,
    attn_rows,
    attn_cols,
    in_rows,
    in_cols,
    out_rows,
    out_cols,
    vector_moment,
):
    place = jnp.stack([lax.axis_index("dp"), lax.axis_index("chip"), lax.axis_index("core")])
    place = place.astype(jnp.int32)
    pieces = VDP * VCHIP
    tall, wide = attn_weight.shape
    rows_v, cols_v = vectors.shape
    split = lambda array: array.reshape((VDP, VCHIP) + array.shape[1:])
    attn_mine = exchange(pack_attn(place, attn_weight, vectors), CHIPS)

    def attn_weights(marks):
        mine = split(after(attn_mine, marks))
        return mine, core_swap(mine)

    def ffn_weights(marks, vector):
        got = split(exchange(pack_ffn(ffn_in, ffn_out, marks), CHIPS))
        ffn_mine = after(got, vector)
        return ffn_mine, core_swap(ffn_mine)

    def send_ffn(mine, other, grad_t):
        both = pair_sum(mine, core_swap(other))
        got = exchange(both.reshape((pieces,) + mine.shape[2:]), CHIPS)
        return got, after(grad_t, both)

    (
        block_out,
        input_grad,
        grads_own,
        grads_other,
        attn_got,
        sums_own,
        sums_other,
        vector_g,
        ffn_got,
    ) = layer(place, attn_weights, segment_ids, tokens, cotangent, ffn_weights, core_swap, send_ffn)
    lay = lambda stat: stat.reshape(1, -1)
    rows_old = (lay(attn_rows), lay(in_rows), lay(out_rows))
    cols_old = (lay(attn_cols), lay(in_cols), lay(out_cols))
    weights_old = (attn_weight, ffn_in, ffn_out)
    ffn_grad, stat = whole_call(
        tail_ffn_kernel,
        "tail_ffn",
        place,
        [((2,) + ffn_in.shape, F32), ((8, LANES), F32)],
        ffn_got,
        *rows_old[1:],
        sums_own,
    )
    (sent,) = whole_call(
        tail_send_kernel,
        "tail_send",
        place,
        [((pieces, tall + VROWS, LANES), BF16)],
        grads_own,
        attn_got,
        vector_g,
        sums_own,
        sums_other,
        stat,
        core_swap(stat),
    )
    got = exchange(sent, CHIPS)
    attn_grad, update_1, update_2, rows_new_1, rows_new_2, cols_new_1, cols_new_2, sent = whole_call(
        tail_reduce_kernel,
        "tail_reduce",
        place,
        [
            (attn_weight.shape, F32),
            (ffn_in.shape, F32),
            (ffn_out.shape, F32),
            (rows_old[1].shape, F32),
            (rows_old[2].shape, F32),
            (cols_old[1].shape, F32),
            (cols_old[2].shape, F32),
            ((pieces, tall + VROWS, LANES), BF16),
        ],
        got,
        ffn_grad,
        *weights_old,
        *rows_old,
        *cols_old,
        vectors,
        vector_moment,
    )
    mine = exchange(sent, CHIPS)
    attn_new, in_new, out_new, rows_new_0, cols_new_0, vector_grad, moment_new, vectors_new = whole_call(
        tail_apply_kernel,
        "tail_apply",
        place,
        [
            (attn_weight.shape, F32),
            (ffn_in.shape, F32),
            (ffn_out.shape, F32),
            (rows_old[0].shape, F32),
            (cols_old[0].shape, F32),
            (vectors.shape, F32),
            (vectors.shape, F32),
            (vectors.shape, F32),
        ],
        mine,
        core_swap(mine),
        attn_grad,
        update_1,
        update_2,
        *weights_old,
        rows_old[0],
        cols_old[0],
        vectors,
        vector_moment,
        scratch=[
            pltpu.VMEM((2 * VDP + pieces, tall, LANES), F32),
            pltpu.VMEM((LANES, tall), F32),
        ],
    )
    return (
        block_out,
        input_grad,
        attn_grad,
        ffn_grad[0],
        ffn_grad[1],
        vector_grad,
        rows_new_0.reshape(-1),
        cols_new_0.reshape(-1),
        rows_new_1.reshape(-1),
        cols_new_1.reshape(-1),
        rows_new_2.reshape(-1),
        cols_new_2.reshape(-1),
        moment_new,
        attn_new,
        in_new,
        out_new,
        vectors_new,
    )


def gather_all(block):
    shape = (lax.axis_size("dp"), lax.axis_size("chip") * 2)
    count = shape[0] * shape[1]
    got = exchange(jnp.broadcast_to(block[None], (count,) + block.shape), ALL)
    return got.reshape(shape + block.shape)


def unblock(parts):
    dp_count, fsdp_count, rows, cols = parts.shape
    return parts.transpose(0, 2, 1, 3).reshape(dp_count * rows, fsdp_count * cols)


def scatter_sum(full):
    dp_count = lax.axis_size("dp")
    fsdp_count = lax.axis_size("chip") * 2
    rows, cols = full.shape
    by_col = full.astype(BF16).reshape(rows, fsdp_count, cols // fsdp_count).transpose(1, 0, 2)
    got = exchange(by_col, ("chip", "core"))
    part = jnp.sum(got.astype(F32), axis=0).astype(BF16)
    by_row = part.reshape(dp_count, rows // dp_count, cols // fsdp_count)
    return jnp.sum(exchange(by_row, "dp").astype(F32), axis=0)


def body_any(
    tokens,
    cotangent,
    segment_ids,
    attn_weight,
    ffn_in,
    ffn_out,
    vectors,
    attn_rows,
    attn_cols,
    in_rows,
    in_cols,
    out_rows,
    out_cols,
    vector_moment,
):
    dp_count = lax.axis_size("dp")
    fsdp_count = lax.axis_size("chip") * 2
    dp_place = lax.axis_index("dp")
    fsdp_place = lax.axis_index("chip") * 2 + lax.axis_index("core")
    rows_w = attn_weight.shape[0]
    rows_v = vectors.shape[0]
    place = jnp.zeros((3,), jnp.int32)
    full_attn = unblock(gather_all(attn_weight.astype(BF16)))
    full_vector = unblock(gather_all(vectors.astype(BF16)))
    full_ffn = jnp.stack(
        [unblock(gather_all(ffn_in.astype(BF16))), unblock(gather_all(ffn_out.astype(BF16)))]
    )
    tall = D // VDP
    cut = full_attn.reshape(VDP, tall, VCHIP, 2, LANES).transpose(3, 0, 2, 1, 4)
    lines = full_vector.reshape(VDP, VEC // VDP, 2, LANES).transpose(0, 2, 1, 3)
    lines = lines.reshape(VDP, 1, 2 * VEC // VDP, LANES)
    lines = jnp.pad(lines, ((0, 0), (0, VCHIP - 1), (0, VROWS - 2 * VEC // VDP), (0, 0)))
    weights = (
        jnp.concatenate([cut[0], lines], axis=2),
        jnp.concatenate([cut[1], jnp.zeros_like(lines)], axis=2),
    )
    ffn_cut = full_ffn.reshape(2, VDP, tall, VCHIP, 2, FF // (2 * VCHIP))
    ffn_cut = ffn_cut.transpose(4, 1, 3, 0, 2, 5)
    (
        block_out,
        input_grad,
        grads_own,
        grads_other,
        _,
        sums_own,
        sums_other,
        vector_g,
        ffn_got,
    ) = layer(
        place,
        lambda marks: weights,
        segment_ids,
        tokens,
        cotangent,
        lambda marks, vector: (ffn_cut[0], ffn_cut[1]),
        lambda block: block,
        lambda mine, other, grad_t: (jnp.stack([mine, other]), grad_t),
    )
    attn_full = jnp.stack([grads_own, grads_other]).transpose(1, 3, 2, 0, 4).reshape(D, 4 * D)
    ffn_full = ffn_got.transpose(3, 1, 4, 2, 0, 5).reshape(2, D, FF)
    sums = jnp.concatenate([sums_own[:2], sums_other[:2]], axis=1)
    vector_full = jnp.concatenate([vector_g[:8], sums, vector_g[10:]], axis=0)
    attn_grad = scatter_sum(attn_full)
    in_grad = scatter_sum(ffn_full[0])
    out_grad = scatter_sum(ffn_full[1])
    vector_grad = scatter_sum(vector_full)

    decay = 1.0 - STEP ** (-0.8)
    gradients = (attn_grad, in_grad, out_grad)
    weights_old = (attn_weight, ffn_in, ffn_out)
    rows_old = (attn_rows, in_rows, out_rows)
    cols_old = (attn_cols, in_cols, out_cols)
    moment_new = decay * vector_moment + (1.0 - decay) * (vector_grad * vector_grad + EPS_ONE)
    vector_step = vector_grad * lax.rsqrt(moment_new)
    squares = [gradient * gradient + EPS_ONE for gradient in gradients]
    pieces = []
    for square in squares:
        pieces.append(jnp.sum(square, axis=1))
    for square in squares:
        pieces.append(jnp.sum(square, axis=0))
    pieces.append(jnp.sum(vector_step * vector_step, axis=1))
    pieces.append(jnp.sum(vectors * vectors, axis=1))
    pieces.append(jnp.stack([jnp.sum(weight * weight) for weight in weights_old]))
    pieces.append(jnp.stack([jnp.sum(old) for old in rows_old]))
    sizes = [piece.shape[0] for piece in pieces]
    flat = jnp.concatenate(pieces)
    flat = jnp.pad(flat, (0, -flat.shape[0] % 1024)).reshape(-1, LANES)
    got = gather_all(flat).reshape(dp_count, fsdp_count, -1)
    offsets = [0]
    for length in sizes:
        offsets.append(offsets[-1] + length)
    take = lambda i: got[:, :, offsets[i] : offsets[i + 1]]
    rows_new, cols_new, row_means, entries = [], [], [], []
    for i in range(3):
        count_rows = rows_w * dp_count
        count_cols = weights_old[i].shape[1] * fsdp_count
        entries.append(float(count_rows * count_cols))
        row_all = jnp.sum(take(i), axis=1)
        mine = lax.dynamic_index_in_dim(row_all, dp_place, 0, keepdims=False)
        rows_new.append(decay * rows_old[i] + (1.0 - decay) * mine / count_cols)
        col_all = jnp.sum(take(3 + i), axis=0)
        mine = lax.dynamic_index_in_dim(col_all, fsdp_place, 0, keepdims=False)
        cols_new.append(decay * cols_old[i] + (1.0 - decay) * mine / count_rows)
        old_total = jnp.sum(take(9)[:, 0, i])
        row_means.append(
            (decay * old_total + (1.0 - decay) * jnp.sum(row_all) / count_cols) / count_rows
        )
    step_rows = jnp.sum(take(6), axis=1).reshape(-1)
    weight_rows = jnp.sum(take(7), axis=1).reshape(-1)
    weight_totals = jnp.sum(take(8), axis=(0, 1))
    updates = []
    for i in range(3):
        second = rows_new[i][:, None] * cols_new[i][None, :] / row_means[i]
        updates.append(gradients[i] * lax.rsqrt(second))
    flat = jnp.stack([jnp.sum(update * update) for update in updates])
    flat = jnp.broadcast_to(jnp.pad(flat, (0, 5))[:, None], (8, LANES))
    totals = jnp.sum(gather_all(flat)[:, :, :, 0], axis=(0, 1))
    new_weights = []
    for i in range(3):
        clip_factor = jnp.maximum(1.0, jnp.sqrt(totals[i] / entries[i]) / CLIP_LIMIT)
        step_size = STEP_RATE * jnp.maximum(EPS_TWO, jnp.sqrt(weight_totals[i] / entries[i]))
        new_weights.append(weights_old[i] - step_size / clip_factor * updates[i])
    bias_rows = FF // D
    row_places = jnp.arange(VEC)
    counts = jnp.where(row_places < bias_rows, float(FF), float(D))
    grouped_updates = jnp.where(row_places < bias_rows, jnp.sum(step_rows[:bias_rows]), step_rows)
    grouped_weights = jnp.where(row_places < bias_rows, jnp.sum(weight_rows[:bias_rows]), weight_rows)
    clip_rows = jnp.maximum(1.0, jnp.sqrt(grouped_updates / counts) / CLIP_LIMIT)
    step_sizes = STEP_RATE * jnp.maximum(EPS_TWO, jnp.sqrt(grouped_weights / counts))
    factor_rows = lax.dynamic_slice_in_dim(step_sizes / clip_rows, dp_place * rows_v, rows_v)
    vectors_new = vectors - factor_rows[:, None] * vector_step
    return (
        block_out,
        input_grad,
        attn_grad,
        in_grad,
        out_grad,
        vector_grad,
        rows_new[0],
        cols_new[0],
        rows_new[1],
        cols_new[1],
        rows_new[2],
        cols_new[2],
        moment_new,
        new_weights[0],
        new_weights[1],
        new_weights[2],
        vectors_new,
    )


def solution(mesh):
    dp_count, fsdp_count = mesh.shape["dp"], mesh.shape["fsdp"]
    inner = jax.sharding.Mesh(mesh.devices.reshape(dp_count, fsdp_count // 2, 2), ALL)
    fsdp = ("chip", "core")
    split = P(ALL, None)
    block = P("dp", fsdp)
    stats = (P("dp"), P(fsdp)) * 3
    plain = dp_count == VDP and fsdp_count == 2 * VCHIP
    return jax.shard_map(
        body if plain else body_any,
        mesh=inner,
        in_specs=(split,) * 3 + (block,) * 4 + stats + (block,),
        out_specs=(split,) * 2 + (block,) * 4 + stats + (block,) * 5,
        check_vma=False,
    )
```

```python
import functools
import math

import jax
import jax.numpy as jnp
import numpy as np
from jax import lax
from jax.experimental import pallas as pl
from jax.experimental.pallas import tpu as pltpu
from jax.sharding import PartitionSpec as P

D = 256
FF = 2048
HEADS = 8
HEAD_DIM = 32
SEQ = 1024
HALF = 512
GROUP = 4
LANES = 128
QBLOCK = 256
WGRID = 32
STEP = 10
VEC = 16
TILE = 1024
CHUNK = 256
SUB = 512
LEAD = 5
STRIP = 64
VDP = 4
VCHIP = 4
VROWS = 16

EPS_NORM = 1e-05
EPS_ONE = 1e-30
EPS_TWO = 0.001
CLIP_LIMIT = 1.0
STEP_RATE = 0.3
FAR = 1e30
LOG2_E = math.log2(math.e)
SCALE = HEAD_DIM ** (-0.5)
GELU_A = math.sqrt(2.0 / math.pi)
GELU_B = 0.044715
F32 = jnp.float32
BF16 = jnp.bfloat16
MIB = 1024 * 1024


def dot(left, right):
    return jnp.dot(left, right, preferred_element_type=F32)


def dot_nt(left, right):
    return lax.dot_general(left, right, (((1,), (1,)), ((), ())), preferred_element_type=F32)


def encode_table():
    half = D // 2
    feature = np.arange(half)
    freq = np.exp(
        (2 * (feature // 2)).astype(np.float32) * np.float32(-math.log(10000.0) / half)
    ).astype(np.float32)
    angles = np.arange(1, WGRID + 1, dtype=np.float32)[:, None] * freq[None, :]
    table = np.where(feature % 2 == 0, np.sin(angles), np.cos(angles)).astype(np.float32)
    low = jnp.bfloat16
    one = table.astype(low)
    rest = table - one.astype(np.float32)
    two = rest.astype(low)
    three = (rest - two.astype(np.float32)).astype(low)
    blank = np.zeros((LANES - 3 * WGRID, half), low)
    return np.concatenate([one, two, three, blank], axis=0)


def iota(shape, dim):
    return lax.broadcasted_iota(jnp.int32, shape, dim)


def norm_forward(rows):
    centered = rows - jnp.mean(rows, axis=-1, keepdims=True)
    inverse = lax.rsqrt(jnp.mean(centered * centered, axis=-1, keepdims=True) + EPS_NORM)
    return centered * inverse, inverse


def norm_backward(upstream, normed, inverse):
    return inverse * (
        upstream
        - jnp.mean(upstream, axis=-1, keepdims=True)
        - normed * jnp.mean(upstream * normed, axis=-1, keepdims=True)
    )

def vspec():
    return pl.BlockSpec(memory_space=pltpu.VMEM)


def params(mib=56, **more):
    return pltpu.CompilerParams(vmem_limit_bytes=mib * MIB, **more)


def pack_kernel(place, attn_ref, vector_ref, out_ref):
    owner = place[1] * 2 + place[2]
    vector = vector_ref[...]
    rows = vector.shape[0]
    wide = jnp.concatenate([vector] * (LANES // vector.shape[1]), axis=1)
    slot = iota((rows, LANES), 1) // vector.shape[1]
    per = LANES // vector.shape[1]
    parts = [attn_ref[...]]
    for half in range(2):
        parts.append(jnp.where(slot + half * per == owner, wide, 0.0))
    parts.append(jnp.zeros((VROWS - 2 * rows, LANES), F32))
    piece = jnp.concatenate(parts, axis=0).astype(BF16)
    for at in range(VDP * VCHIP):
        out_ref[at] = piece


def pack_attn(place, attn_weight, vectors):
    return pl.pallas_call(
        pack_kernel,
        out_shape=jax.ShapeDtypeStruct((VDP * VCHIP, attn_weight.shape[0] + VROWS, LANES), BF16),
        in_specs=[pl.BlockSpec(memory_space=pltpu.SMEM), vspec(), vspec()],
        out_specs=vspec(),
        compiler_params=params(),
        name="pack_attn",
    )(place, attn_weight, vectors)


def pack_ffn_kernel(early_ref, *refs):
    out_ref = refs[-1]
    for at in range(VCHIP):
        out_ref[at] = early_ref[...]


def pack_ffn(early, *earlier):
    return pl.pallas_call(
        pack_ffn_kernel,
        out_shape=jax.ShapeDtypeStruct((VCHIP,) + early.shape, BF16),
        in_specs=[vspec()] + [pl.BlockSpec(memory_space=pl.ANY)] * len(earlier),
        out_specs=vspec(),
        compiler_params=params(),
        name="pack_ffn",
    )(early, *earlier)


def place_kernel(
    segment_ref, tokens_ref, back_ref, table_ref, qk_ref, x_ref, qk_t_ref, x_t_ref, turned_ref, marks_ref
):
    row = pl.program_id(0)
    starts = []
    for number in range(1, 4):
        at = jnp.int32(0)
        for step in (512, 256, 128, 64, 32, 16, 8, 4, 2, 1, 1):
            probe = jnp.minimum(at + (step - 1), SEQ - 1)
            at = jnp.where(segment_ref[row, probe] < number, at + step, at)
        starts.append(at)
    edges = [jnp.int32(0)] + starts + [jnp.int32(SEQ)]
    begin = jnp.int32(0)
    for number in range(3, -1, -1):
        begin = jnp.where(edges[number + 1] - edges[number] == HALF, edges[number], begin)
    for number in range(3):
        marks_ref[row, number] = starts[number]
    marks_ref[row, 3] = begin
    one, two, three = starts
    x = pltpu.roll(tokens_ref[...].astype(F32), (SEQ - begin) & (SEQ - 1), 0)
    x_ref[...] = x.astype(BF16)
    x_t_ref[...] = x.T.astype(BF16)
    back = back_ref[...].astype(F32)
    turned_ref[...] = pltpu.roll(back, (SEQ - begin) & (SEQ - 1), 0).astype(BF16)
    at = (iota((SEQ, LANES), 0) + begin) & (SEQ - 1)
    lane = iota((SEQ, LANES), 1)
    start = jnp.where(at >= three, three, jnp.where(at >= two, two, jnp.where(at >= one, one, 0)))
    local = at - start
    kept = lane < 3 * WGRID
    slot = lane & (WGRID - 1)
    hot_r = jnp.where(((local >> 5) == slot) & kept, 1.0, 0.0).astype(BF16)
    hot_c = jnp.where(((local & (WGRID - 1)) == slot) & kept, 1.0, 0.0).astype(BF16)
    table = table_ref[...]
    places = jnp.concatenate([dot(hot_r, table), dot(hot_c, table)], axis=1)
    qk = x + places
    qk_ref[...] = qk.astype(BF16)
    qk_t_ref[...] = qk.T.astype(BF16)


def place_tokens(segment_ids, tokens, cotangent, table):
    rows = segment_ids.shape[0]
    by_row = lambda r: (r, 0)
    return pl.pallas_call(
        place_kernel,
        out_shape=(
            jax.ShapeDtypeStruct(tokens.shape, BF16),
            jax.ShapeDtypeStruct(tokens.shape, BF16),
            jax.ShapeDtypeStruct((D, tokens.shape[0]), BF16),
            jax.ShapeDtypeStruct((D, tokens.shape[0]), BF16),
            jax.ShapeDtypeStruct(tokens.shape, BF16),
            jax.ShapeDtypeStruct((rows, 4), jnp.int32),
        ),
        grid=(rows,),
        in_specs=[
            pl.BlockSpec(memory_space=pltpu.SMEM),
            pl.BlockSpec((SEQ, D), by_row),
            pl.BlockSpec((SEQ, D), by_row),
            pl.BlockSpec((LANES, LANES), lambda r: (0, 0)),
        ],
        out_specs=(
            pl.BlockSpec((SEQ, D), by_row),
            pl.BlockSpec((SEQ, D), by_row),
            pl.BlockSpec((D, SEQ), lambda r: (0, r)),
            pl.BlockSpec((D, SEQ), lambda r: (0, r)),
            pl.BlockSpec((SEQ, D), by_row),
            pl.BlockSpec(memory_space=pltpu.SMEM),
        ),
        compiler_params=params(dimension_semantics=("arbitrary",)),
        cost_estimate=pl.CostEstimate(flops=600_000_000, bytes_accessed=4_000_000, transcendentals=0),
        name="place_tokens",
    )(segment_ids, tokens, cotangent, table)


def attend_kernel(
    marks,
    place,
    x_ref,
    qk_ref,
    x_t_ref,
    qk_t_ref,
    mine_ref,
    other_ref,
    query_t_ref,
    value_ref,
    key_t_ref,
    out_t_ref,
    inverse_ref,
    mixed_ref,
    mixed_t_ref,
    exps_ref,
    weight_ref,
    proj_ref,
    vector_ref,
    key_s,
    value_s,
    mark_k,
    mark_q,
    masked_s,
    weight_t_s,
    bias_s,
    exps_s,
    exps_sem,
):
    row = pl.program_id(0)
    group = pl.program_id(1)
    begin = marks[row, 3]
    core = place[2]

    @pl.when((row == 0) & (group == 0))
    def _():
        tall = D // VDP
        for d in range(VDP):
            rows = slice(d * tall, (d + 1) * tall)
            total = jnp.zeros((8, LANES), F32)
            for c in range(VCHIP):
                for ref, half in ((mine_ref, core), (other_ref, 1 - core)):
                    if c < 3:
                        to = pl.ds(pl.multiple_of(c * D + half * LANES, LANES), LANES)
                        weight_ref[rows, to] = ref[d, c, :tall, :]
                    else:
                        to = pl.ds(pl.multiple_of(half * LANES, LANES), LANES)
                        proj_ref[rows, to] = ref[d, c, :tall, :]
                    total += ref[d, c, tall:, :].astype(F32)[:8]
            vector_ref[d * 4 : (d + 1) * 4, :LANES] = total[:4]
            vector_ref[d * 4 : (d + 1) * 4, LANES:] = total[4:]
        weight_t_s[...] = weight_ref[...].astype(F32).T.astype(BF16)
        bias_s[...] = vector_ref[8:16, :].T

    @pl.when(group == 0)
    def _():
        qk_t = qk_t_ref[...]
        query_t = (dot(weight_t_s[:D, :], qk_t) + bias_s[:, 0:1]) * SCALE
        query_t_ref[...] = query_t.astype(BF16)
        key_t_ref[...] = dot(weight_t_s[D : 2 * D, :], qk_t).astype(BF16)
        key_s[...] = dot(qk_ref[...], weight_ref[:, D : 2 * D]).astype(BF16)
        value = dot(x_ref[...], weight_ref[:, 2 * D : 3 * D]) + vector_ref[9:10, :]
        value_ref[...] = value.astype(BF16)
        value_t = dot(weight_t_s[2 * D :, :], x_t_ref[...]) + bias_s[:, 1:2]
        value_t = value_t.astype(BF16)
        for head in range(HEADS):
            value_s[head, :HEAD_DIM, :] = value_t[head * HEAD_DIM : (head + 1) * HEAD_DIM, :]
            value_s[head, HEAD_DIM:, :] = jnp.ones((16, SEQ), BF16)
        one, two, three = marks[row, 0], marks[row, 1], marks[row, 2]

        def number_of(shape, dim):
            here = (iota(shape, dim) + (HALF + begin)) & (SEQ - 1)
            return (
                jnp.where(here >= one, 1, 0)
                + jnp.where(here >= two, 1, 0)
                + jnp.where(here >= three, 1, 0)
            )

        lane = iota((HALF, LANES), 1)
        number = number_of((HALF, LANES), 0)
        mark_k[...] = jnp.where((number != lane) & (lane < 4), -FAR, 0.0).astype(BF16)
        number = number_of((LANES, HALF), 1)
        mark_q[...] = jnp.where(number == iota((LANES, HALF), 0), 1.0, 0.0).astype(BF16)

    lanes = pl.ds(pl.multiple_of(group * LANES, LANES), LANES)
    head_of = iota((1, LANES), 1) // HEAD_DIM
    keys_here = key_s[:, lanes]
    for at_head in range(GROUP):
        mask = jnp.where(head_of == at_head, 1.0, 0.0).astype(BF16)
        masked_s[at_head] = keys_here * mask

    slot = (row * 2 + group) * (2 * GROUP)

    def copy_of(row, group, half, at_head, slot):
        return pltpu.make_async_copy(
            exps_s.at[slot], exps_ref.at[row, group, half, at_head], exps_sem.at[slot]
        )

    def scores_of(item):
        half, at_head, block = item
        key_m = masked_s[at_head, half * HALF : (half + 1) * HALF, :]
        at = half * HALF + block * QBLOCK
        query = query_t_ref[lanes, at : at + QBLOCK]
        if half == 1:
            key_m = jnp.concatenate([key_m, mark_k[...]], axis=1)
            query = jnp.concatenate(
                [query, mark_q[:, block * QBLOCK : (block + 1) * QBLOCK]], axis=0
            )
        return dot(key_m, query)

    def exps_of(item, largest):
        half, at_head, block = item
        cols = slice(block * QBLOCK, (block + 1) * QBLOCK)
        exps = jnp.exp2((scores_of(item) - largest) * LOG2_E)
        exps_s[slot + half * GROUP + at_head, :, cols] = exps.astype(BF16)
        if block == HALF // QBLOCK - 1:
            copy_of(row, group, half, at_head, slot + half * GROUP + at_head).start()

    def finish(item):
        half, at_head, block = item
        at = half * HALF + block * QBLOCK
        rows = slice(half * HALF, (half + 1) * HALF)
        cols = slice(block * QBLOCK, (block + 1) * QBLOCK)
        out = dot(
            value_s[group * GROUP + at_head, :, rows], exps_s[slot + half * GROUP + at_head, :, cols]
        )
        inverse = 1.0 / out[HEAD_DIM : HEAD_DIM + 1, :]
        inverse_ref[0, at_head : at_head + 1, at : at + QBLOCK] = inverse
        out_t_ref[at_head * HEAD_DIM : (at_head + 1) * HEAD_DIM, at : at + QBLOCK] = (
            out[:HEAD_DIM, :] * inverse
        )

    items = [
        (half, at_head, block)
        for half in range(2)
        for at_head in range(GROUP)
        for block in range(HALF // QBLOCK)
    ]
    largest = {}
    for i in range(len(items) + 2):
        if i < len(items):
            largest[i] = jnp.max(scores_of(items[i]), axis=0, keepdims=True)
        if 1 <= i <= len(items):
            exps_of(items[i - 1], largest.pop(i - 1))
        if i >= 2:
            finish(items[i - 2])
    out_t = out_t_ref[...]
    mixed_t_ref[...] = out_t.astype(BF16)
    mixed_ref[...] = out_t.T.astype(BF16)

    @pl.when((row == pl.num_programs(0) - 1) & (group == 1))
    def _():
        for at in range(exps_s.shape[0]):
            copy_of(at // 16, at // 8 % 2, at // GROUP % 2, at % GROUP, at).wait()


def attend_forward(marks, place, x, qk, x_t, qk_t, mine, other):
    total = x.shape[0]
    rows = total // SEQ
    by_row = lambda r, g, m, p: (r, 0)
    by_col = lambda r, g, m, p: (0, r)
    by_both = lambda r, g, m, p: (g, r)
    whole = lambda r, g, m, p: (0, 0)
    return pl.pallas_call(
        attend_kernel,
        out_shape=(
            jax.ShapeDtypeStruct((D, total), BF16),
            jax.ShapeDtypeStruct((total, D), BF16),
            jax.ShapeDtypeStruct((D, total), BF16),
            jax.ShapeDtypeStruct((D, total), F32),
            jax.ShapeDtypeStruct((2, 8, total), F32),
            jax.ShapeDtypeStruct((total, D), BF16),
            jax.ShapeDtypeStruct((D, total), BF16),
            jax.ShapeDtypeStruct((rows, 2, 2, GROUP, HALF, HALF), BF16),
            jax.ShapeDtypeStruct((D, 3 * D), BF16),
            jax.ShapeDtypeStruct((D, D), BF16),
            jax.ShapeDtypeStruct((VEC, D), F32),
        ),
        grid_spec=pltpu.PrefetchScalarGridSpec(
            num_scalar_prefetch=2,
            grid=(rows, 2),
            in_specs=[
                pl.BlockSpec((SEQ, D), by_row),
                pl.BlockSpec((SEQ, D), by_row),
                pl.BlockSpec((D, SEQ), by_col),
                pl.BlockSpec((D, SEQ), by_col),
                vspec(),
                vspec(),
            ],
            out_specs=[
                pl.BlockSpec((D, SEQ), by_col),
                pl.BlockSpec((SEQ, D), by_row),
                pl.BlockSpec((D, SEQ), by_col),
                pl.BlockSpec((LANES, SEQ), by_both),
                pl.BlockSpec((1, 8, SEQ), lambda r, g, m, p: (g, 0, r)),
                pl.BlockSpec((SEQ, LANES), lambda r, g, m, p: (r, g)),
                pl.BlockSpec((LANES, SEQ), by_both),
                pl.BlockSpec(memory_space=pl.ANY),
                pl.BlockSpec((D, 3 * D), whole),
                pl.BlockSpec((D, D), whole),
                pl.BlockSpec((VEC, D), whole),
            ],
            scratch_shapes=[
                pltpu.VMEM((SEQ, D), BF16),
                pltpu.VMEM((HEADS, HEAD_DIM + 16, SEQ), BF16),
                pltpu.VMEM((HALF, LANES), BF16),
                pltpu.VMEM((LANES, HALF), BF16),
                pltpu.VMEM((GROUP, SEQ, LANES), BF16),
                pltpu.VMEM((3 * D, D), BF16),
                pltpu.VMEM((D, 8), F32),
                pltpu.VMEM((rows * 4 * GROUP, HALF, HALF), BF16),
                pltpu.SemaphoreType.DMA((rows * 4 * GROUP,)),
            ],
        ),
        compiler_params=params(dimension_semantics=("arbitrary", "arbitrary")),
        cost_estimate=pl.CostEstimate(
            flops=20_000_000_000, bytes_accessed=30_000_000, transcendentals=8_400_000
        ),
        name="attend_forward",
    )(marks, place, x, qk, x_t, qk_t, mine, other)


def feed_kernel(
    marks,
    place,
    x_ref,
    back_ref,
    mixed_ref,
    mixed_t_ref,
    proj_ref,
    mine_ref,
    other_ref,
    vector_ref,
    block_ref,
    resid_ref,
    mixed_grad_ref,
    mine_out,
    other_out,
    proj_out,
    vector_out,
    first_w,
    second_w,
    first_acc,
    second_acc,
    proj_acc,
    vector_acc,
    hidden_s,
    slope_s,
    pre_s,
    first_low_s,
    branch_low_s,
    attended_s,
    block_s,
    eye_s,
):
    step = pl.program_id(0)
    core = place[2]
    tall = D // VDP
    wide = FF // (2 * VCHIP)

    @pl.when(step == 0)
    def _():
        first_acc[...] = jnp.zeros_like(first_acc)
        second_acc[...] = jnp.zeros_like(second_acc)
        proj_acc[...] = jnp.zeros_like(proj_acc)
        vector_acc[...] = jnp.zeros_like(vector_acc)
        eye_s[...] = jnp.where(iota((D, D), 0) == iota((D, D), 1), 1.0, 0.0).astype(BF16)
        for d in range(VDP):
            rows = slice(d * tall, (d + 1) * tall)
            for c in range(VCHIP):
                for ref, half in ((mine_ref, core), (other_ref, 1 - core)):
                    to = pl.ds(pl.multiple_of((2 * c + half) * wide, wide), wide)
                    first_w[rows, to] = ref[c, d, 0]
                    second_w[rows, to] = ref[c, d, 1]

    bias_o, bias_2 = vector_ref[10:11, :], vector_ref[11:12, :]
    gain_1, shift_1 = vector_ref[12:13, :], vector_ref[13:14, :]
    gain_2, shift_2 = vector_ref[14:15, :], vector_ref[15:16, :]
    at_row = pl.multiple_of((step % (SEQ // TILE)) * TILE, TILE)
    chunks = FF // CHUNK
    pair = 2

    def columns(at, count=1):
        return slice(at * CHUNK, (at + count) * CHUNK)

    def hidden_of(rows, at, pre):
        pre = (pre + vector_ref[at : at + 1, :]).astype(BF16)
        cube = BF16(GELU_A * GELU_B) * (pre * pre)
        gate = BF16(0.5) + BF16(0.5) * jnp.tanh(pre * (cube + BF16(GELU_A)))
        hidden_s[rows, columns(at)] = pre * gate
        slope_s[rows, columns(at)] = gate + (gate - gate * gate) * (
            pre * (BF16(6.0) * cube + BF16(2.0 * GELU_A))
        )

    def stages(sub):
        rows_at = sub * SUB
        rows = slice(rows_at, rows_at + SUB)
        attended = dot(mixed_ref[rows, :], proj_ref[...]) + bias_o
        norm_1, inverse_1 = norm_forward(x_ref[rows, :].astype(F32) + attended)
        first = norm_1 * gain_1 + shift_1
        first_low = first.astype(BF16)
        first_low_s[rows, :] = first_low
        yield
        branch = jnp.zeros((SUB, D), F32)
        for i in range(chunks + 1):
            if i < chunks:
                hidden_of(rows, i, dot(first_low, first_w[:, columns(i)]))
            if i >= pair and i % pair == 0:
                cols = columns(i - pair, pair)
                branch += dot_nt(hidden_s[rows, cols], second_w[:, cols])
            yield
        norm_2, inverse_2 = norm_forward(first + (branch + bias_2))
        block_s[pl.ds(at_row + rows_at, SUB), :] = norm_2 * gain_2 + shift_2
        back = back_ref[rows, :].astype(F32)
        vector_acc[14:15, :] += jnp.sum(back * norm_2, axis=0, keepdims=True)
        vector_acc[15:16, :] += jnp.sum(back, axis=0, keepdims=True)
        resid_2 = norm_backward(back * gain_2, norm_2, inverse_2)
        branch_low = resid_2.astype(BF16)
        branch_low_s[rows, :] = branch_low
        vector_acc[11:12, :] += jnp.sum(branch_low.astype(F32), axis=0, keepdims=True)
        yield
        first_back = resid_2
        if sub == 1:
            branch_t = dot_nt(eye_s[...], branch_low_s[...]).astype(BF16)
            first_t = dot_nt(eye_s[...], first_low_s[...]).astype(BF16)
            first_t = jnp.concatenate([first_t, jnp.ones((16, TILE), BF16)], axis=0)
        for i in range(chunks + 1):
            if i < chunks:
                pull = dot(branch_low, second_w[:, columns(i)]).astype(BF16)
                pre_s[rows, columns(i)] = pull * slope_s[rows, columns(i)]
                if sub == 1:
                    second_acc[:, columns(i)] += dot(branch_t, hidden_s[:, columns(i)])
            if i >= 1 and sub == 1:
                cols = columns(i - 1)
                first_acc[:, cols] += dot(first_t, pre_s[:, cols])
            if i >= pair and i % pair == 0:
                cols = columns(i - pair, pair)
                first_back += dot_nt(pre_s[rows, cols], first_w[:, cols])
            yield
        vector_acc[12:13, :] += jnp.sum(first_back * norm_1, axis=0, keepdims=True)
        vector_acc[13:14, :] += jnp.sum(first_back, axis=0, keepdims=True)
        resid_1 = norm_backward(first_back * gain_1, norm_1, inverse_1)
        resid_ref[rows, :] = resid_1
        attended_low = resid_1.astype(BF16)
        attended_s[rows, :] = attended_low
        vector_acc[10:11, :] += jnp.sum(attended_low.astype(F32), axis=0, keepdims=True)
        mixed_grad_ref[:, rows] = dot_nt(proj_ref[...], attended_low).astype(BF16)
        yield

    ahead, behind = stages(0), stages(1)
    for _ in range(LEAD):
        next(ahead)
    running = [ahead, behind]
    while running:
        for program in list(running):
            if next(program, 0) == 0:
                running.remove(program)
    proj_acc[...] += dot(mixed_t_ref[...], attended_s[...])

    @pl.when(step % (SEQ // TILE) == SEQ // TILE - 1)
    def _():
        block_ref[...] = pltpu.roll(block_s[...], marks[step // (SEQ // TILE), 3], 0)

    @pl.when(step == pl.num_programs(0) - 1)
    def _():
        for d in range(VDP):
            rows = slice(d * tall, (d + 1) * tall)
            for c in range(VCHIP):
                for ref, half in ((mine_out, core), (other_out, 1 - core)):
                    to = pl.ds(pl.multiple_of((2 * c + half) * wide, wide), wide)
                    ref[d, c, 0] = first_acc[rows, to].astype(BF16)
                    ref[d, c, 1] = second_acc[rows, to].astype(BF16)
        proj_out[...] = proj_acc[...]
        for at in range(FF // D):
            vector_out[at : at + 1, :] = first_acc[D : D + 1, at * D : (at + 1) * D]
        vector_out[FF // D :, :] = vector_acc[FF // D :, :]


def feed_forward(marks, place, x, back, mixed, mixed_t, proj, mine, other, vector):
    total = x.shape[0]
    tile = lambda i, m, p: (i, 0)
    by_col = lambda i, m, p: (0, i)
    whole = lambda i, m, p: (0, 0)
    whole5 = lambda i, m, p: (0, 0, 0, 0, 0)
    return pl.pallas_call(
        feed_kernel,
        out_shape=(
            jax.ShapeDtypeStruct((total, D), F32),
            jax.ShapeDtypeStruct((total, D), F32),
            jax.ShapeDtypeStruct((D, total), BF16),
            jax.ShapeDtypeStruct(mine.shape, BF16),
            jax.ShapeDtypeStruct(mine.shape, BF16),
            jax.ShapeDtypeStruct((D, D), F32),
            jax.ShapeDtypeStruct((VEC, D), F32),
        ),
        grid_spec=pltpu.PrefetchScalarGridSpec(
            num_scalar_prefetch=2,
            grid=(total // TILE,),
            in_specs=[
                pl.BlockSpec((TILE, D), tile),
                pl.BlockSpec((TILE, D), tile),
                pl.BlockSpec((TILE, D), tile),
                pl.BlockSpec((D, TILE), by_col),
                pl.BlockSpec((D, D), whole),
                vspec(),
                vspec(),
                pl.BlockSpec((VEC, D), whole),
            ],
            out_specs=[
                pl.BlockSpec((SEQ, D), lambda i, m, p: (i // (SEQ // TILE), 0)),
                pl.BlockSpec((TILE, D), tile),
                pl.BlockSpec((D, TILE), by_col),
                pl.BlockSpec(mine.shape, whole5),
                pl.BlockSpec(mine.shape, whole5),
                pl.BlockSpec((D, D), whole),
                pl.BlockSpec((VEC, D), whole),
            ],
            scratch_shapes=[
                pltpu.VMEM((D, FF), BF16),
                pltpu.VMEM((D, FF), BF16),
                pltpu.VMEM((D + 16, FF), F32),
                pltpu.VMEM((D, FF), F32),
                pltpu.VMEM((D, D), F32),
                pltpu.VMEM((VEC, D), F32),
                pltpu.VMEM((TILE, FF), BF16),
                pltpu.VMEM((TILE, FF), BF16),
                pltpu.VMEM((TILE, FF), BF16),
                pltpu.VMEM((TILE, D), BF16),
                pltpu.VMEM((TILE, D), BF16),
                pltpu.VMEM((TILE, D), BF16),
                pltpu.VMEM((SEQ, D), F32),
                pltpu.VMEM((D, D), BF16),
            ],
        ),
        compiler_params=params(dimension_semantics=("arbitrary",)),
        cost_estimate=pl.CostEstimate(
            flops=14_000_000_000, bytes_accessed=15_000_000, transcendentals=4_200_000
        ),
        name="feed_forward",
    )(marks, place, x, back, mixed, mixed_t, proj, mine, other, vector)


def pull_kernel(
    own,
    marks,
    place,
    grad_t_ref,
    query_t_ref,
    value_ref,
    key_t_ref,
    out_t_ref,
    inverse_ref,
    exps_ref,
    qk_t_ref,
    x_t_ref,
    weight_ref,
    proj_ref,
    *refs,
):
    if own:
        resid_ref, other_ref, pulled_ref, grads_ref, sums_ref = refs[:5]
    else:
        pulled_ref, grads_ref, sums_ref = refs[:3]
    dot_s, query_g, key_g, value_g, acc, sum_acc, value_s, scaled_t_s, score_s, exps_s, exps_sem = refs[-11:]
    row = pl.program_id(0)
    begin = marks[row, 3]
    group = place[2] if own else 1 - place[2]

    def copy_of(row, half):
        return pltpu.make_async_copy(
            exps_ref.at[row, group, half], exps_s.at[row * 2 + half], exps_sem.at[row * 2 + half]
        )

    @pl.when(row == 0)
    def _():
        for at in range(exps_s.shape[0]):
            copy_of(at // 2, at % 2).start()
        acc[...] = jnp.zeros_like(acc)
        sum_acc[...] = jnp.zeros_like(sum_acc)

    grad_t = grad_t_ref[...].astype(F32)
    head_of = iota((1, LANES), 1) // HEAD_DIM
    for at_head in range(GROUP):
        heads = slice(at_head * HEAD_DIM, (at_head + 1) * HEAD_DIM)
        part = grad_t[heads, :] * inverse_ref[0, at_head : at_head + 1, :]
        dot_s[at_head : at_head + 1, :] = jnp.sum(part * out_t_ref[heads, :], axis=0, keepdims=True)
        part = part.astype(BF16)
        scaled_t_s[heads, :] = part
        mask = jnp.where(head_of == at_head, 1.0, 0.0).astype(BF16)
        for half in range(2):
            rows = slice(half * HALF, (half + 1) * HALF)
            to = slice(at_head * HALF, (at_head + 1) * HALF)
            value_s[half, to, :] = value_ref[rows, :] * mask

    def score_grad_of(item):
        half, at_head, block = item
        at = half * HALF + block * QBLOCK
        if at_head == 0 and block == 0:
            copy_of(row, half).wait()
        cols = slice(block * QBLOCK, (block + 1) * QBLOCK)
        value = value_s[half, at_head * HALF : (at_head + 1) * HALF, :]
        pull = dot(value, scaled_t_s[:, at : at + QBLOCK])
        pull = (pull - dot_s[at_head : at_head + 1, at : at + QBLOCK]).astype(BF16)
        score_s[half * GROUP + at_head, :, cols] = exps_s[row * 2 + half, at_head, :, cols] * pull

    def finish(half, at_head):
        rows = slice(half * HALF, (half + 1) * HALF)
        heads = slice(at_head * HEAD_DIM, (at_head + 1) * HEAD_DIM)
        score_grad = score_s[half * GROUP + at_head]
        value_g[heads, rows] = dot_nt(scaled_t_s[heads, rows], exps_s[row * 2 + half, at_head])
        query_g[heads, rows] = dot(key_t_ref[heads, rows], score_grad)
        key_g[heads, rows] = dot_nt(query_t_ref[heads, rows], score_grad)

    items = [
        (half, at_head, block)
        for half in range(2)
        for at_head in range(GROUP)
        for block in range(HALF // QBLOCK)
    ]
    for i in range(len(items) + 1):
        if i < len(items):
            score_grad_of(items[i])
        if i >= 2 and i % 2 == 0:
            finish(*items[i - 1][:2])
    query_low = query_g[...].astype(BF16)
    both_low = jnp.concatenate([key_g[...].astype(BF16), value_g[...].astype(BF16)], axis=0)
    ones = jnp.ones((16, SEQ), BF16)
    sum_acc[0:1, :] += dot_nt(ones, query_low)[0:1, :] * SCALE
    sum_acc[1:2, :] += dot_nt(ones, both_low[LANES:, :])[0:1, :]
    qk_t = qk_t_ref[...]
    both = dot_nt(qk_t, jnp.concatenate([query_low, both_low[:LANES, :]], axis=0))
    acc[:, :LANES] += both[:, :LANES] * SCALE
    acc[:, LANES : 2 * LANES] += both[:, LANES:]
    acc[:, 2 * LANES :] += dot_nt(x_t_ref[...], both_low[LANES:, :])
    at = [pl.ds(pl.multiple_of(i * D + group * LANES, LANES), LANES) for i in range(3)]
    pulled = dot(weight_ref[:, at[0]], query_low) * SCALE + dot(
        jnp.concatenate([weight_ref[:, at[1]], weight_ref[:, at[2]]], axis=1), both_low
    )
    if own:
        pulled = (pulled + other_ref[...]).T
        pulled_ref[...] = pltpu.roll(resid_ref[...] + pulled, begin, 0)
    else:
        pulled_ref[...] = pulled

    @pl.when(row == pl.num_programs(0) - 1)
    def _():
        tall = D // VDP
        for d in range(VDP):
            rows = slice(d * tall, (d + 1) * tall)
            for c in range(3):
                grads_ref[d, c] = acc[rows, c * LANES : (c + 1) * LANES].astype(BF16)
            grads_ref[d, 3] = proj_ref[rows, :].astype(BF16)
        sums_ref[...] = sum_acc[...]


def attend_back(own, marks, place, grad_t, query_t, value, key_t, out_t, inverse, exps, qk_t, x_t, weight, proj, *more):
    total = value.shape[0]
    rows = total // SEQ
    pick = (lambda p: p[2]) if own else (lambda p: 1 - p[2])
    by_group = lambda r, m, p: (r, pick(p))
    by_row = lambda r, m, p: (r, 0)
    whole = lambda r, m, p: (0, 0)
    in_specs = [
        pl.BlockSpec((LANES, SEQ), lambda r, m, p: (pick(p), r)),
        pl.BlockSpec((LANES, SEQ), lambda r, m, p: (pick(p), r)),
        pl.BlockSpec((SEQ, LANES), by_group),
        pl.BlockSpec((LANES, SEQ), lambda r, m, p: (pick(p), r)),
        pl.BlockSpec((LANES, SEQ), lambda r, m, p: (pick(p), r)),
        pl.BlockSpec((1, 8, SEQ), lambda r, m, p: (pick(p), 0, r)),
        pl.BlockSpec(memory_space=pl.ANY),
        pl.BlockSpec((D, SEQ), lambda r, m, p: (0, r)),
        pl.BlockSpec((D, SEQ), lambda r, m, p: (0, r)),
        pl.BlockSpec((D, 3 * D), whole),
        pl.BlockSpec((D, LANES), lambda r, m, p: (0, pick(p))),
    ]
    by_col = pl.BlockSpec((D, SEQ), lambda r, m, p: (0, r))
    if own:
        in_specs += [pl.BlockSpec((SEQ, D), by_row), by_col]
    return pl.pallas_call(
        functools.partial(pull_kernel, own),
        out_shape=(
            jax.ShapeDtypeStruct((total, D) if own else (D, total), F32),
            jax.ShapeDtypeStruct((VDP, VCHIP, D // VDP, LANES), BF16),
            jax.ShapeDtypeStruct((8, LANES), F32),
        ),
        grid_spec=pltpu.PrefetchScalarGridSpec(
            num_scalar_prefetch=2,
            grid=(rows,),
            in_specs=in_specs,
            out_specs=[
                pl.BlockSpec((SEQ, D), by_row) if own else by_col,
                pl.BlockSpec((VDP, VCHIP, D // VDP, LANES), lambda r, m, p: (0, 0, 0, 0)),
                pl.BlockSpec((8, LANES), whole),
            ],
            scratch_shapes=[
                pltpu.VMEM((8, SEQ), F32),
                pltpu.VMEM((LANES, SEQ), F32),
                pltpu.VMEM((LANES, SEQ), F32),
                pltpu.VMEM((LANES, SEQ), F32),
                pltpu.VMEM((D, 3 * LANES), F32),
                pltpu.VMEM((8, LANES), F32),
                pltpu.VMEM((2, GROUP * HALF, LANES), BF16),
                pltpu.VMEM((LANES, SEQ), BF16),
                pltpu.VMEM((2 * GROUP, HALF, HALF), BF16),
                pltpu.VMEM((2 * rows, GROUP, HALF, HALF), BF16),
                pltpu.SemaphoreType.DMA((2 * rows,)),
            ],
        ),
        compiler_params=params(dimension_semantics=("arbitrary",)),
        cost_estimate=pl.CostEstimate(
            flops=18_000_000_000, bytes_accessed=15_000_000, transcendentals=0
        ),
        name="attend_back",
    )(marks, place, grad_t, query_t, value, key_t, out_t, inverse, exps, qk_t, x_t, weight, proj, *more)


def sums_by_group(place, sums_own, sums_other):
    first = place[2] == 0
    return (
        jnp.where(first, sums_own, sums_other),
        jnp.where(first, sums_other, sums_own),
    )


def two_terms(rows):
    high = rows.astype(BF16)
    return jnp.concatenate([high.astype(F32), rows - high.astype(F32)], axis=0)


def column_to_row(columns, rows):
    lane = iota((rows, LANES), 1)
    wide = jnp.zeros((rows, LANES), F32)
    for i, column in enumerate(columns):
        wide = jnp.where(lane == i, column, wide)
    return wide.T[:8, :]


def total_of(array):
    return jnp.sum(jnp.sum(array, axis=0, keepdims=True), axis=1, keepdims=True)


def tail_ffn_kernel(place, ffn_ref, rows_1, rows_2, last_ref, grad_ref, stat_ref):
    lane = iota((1, LANES), 1)
    piece, across = [], []
    for kind in range(2):
        total = ffn_ref[0, kind].astype(F32)
        for at in range(1, VDP * VCHIP):
            total = total + ffn_ref[at, kind].astype(F32)
        grad_ref[kind] = total
        square = total * total + EPS_ONE
        down = jnp.sum(square, axis=0, keepdims=True)
        piece += [down[:, :LANES], down[:, LANES:]]
        across.append(jnp.sum(square, axis=1, keepdims=True))
    across = column_to_row(across, total.shape[0])
    across = jnp.concatenate([across[0:1], across[1:2]], axis=1)
    olds = jnp.zeros((1, LANES), F32)
    for i, ref in enumerate((rows_1, rows_2)):
        olds = jnp.where(lane == i, jnp.sum(ref[...], axis=1, keepdims=True), olds)
    stat_ref[...] = jnp.concatenate([across] + piece + [olds, jnp.zeros((2, LANES), F32)], axis=0)


def tail_send_kernel(
    place, mine_ref, got_ref, vector_ref, own_ref, other_ref, stat_ref, stat_other_ref, send_ref
):
    tall = D // VDP
    low, high = sums_by_group(place, own_ref[...], other_ref[...])
    vector = jnp.concatenate(
        [
            vector_ref[:8, :],
            jnp.concatenate([low[:2], high[:2]], axis=1),
            vector_ref[10:, :],
        ],
        axis=0,
    )
    stat = jnp.concatenate([stat_ref[0:1, :] + stat_other_ref[0:1, :], stat_ref[1:6, :]], axis=0)
    stat = two_terms(stat)
    rows = VEC // VDP
    for d in range(VDP):
        for c in range(VCHIP):
            at = d * VCHIP + c
            both = mine_ref[d, c].astype(F32) + got_ref[d, c].astype(F32)
            send_ref[at, :tall, :] = both.astype(BF16)
            part = vector[d * rows : (d + 1) * rows, c * 64 : (c + 1) * 64]
            part = jnp.concatenate([part, jnp.zeros((rows, LANES - 64), F32)], axis=1)
            send_ref[at, tall:, :] = jnp.concatenate([part, stat], axis=0).astype(BF16)


def tail_reduce_kernel(
    place,
    got_ref,
    ffn_grad_ref,
    attn_ref,
    first_ref,
    second_ref,
    rows_0,
    rows_1,
    rows_2,
    cols_0,
    cols_1,
    cols_2,
    vector_ref,
    moment_ref,
    grad_ref,
    update_1,
    update_2,
    rows_out_1,
    rows_out_2,
    cols_out_1,
    cols_out_2,
    send_ref,
):
    decay = 1.0 - STEP ** (-0.8)
    chip = place[1]
    dp = place[0]
    tall = attn_ref.shape[0]
    rows, width = vector_ref.shape
    pieces = VDP * VCHIP
    lane = iota((1, LANES), 1)
    total = got_ref[0, :tall, :].astype(F32)
    part = got_ref[0, tall:, :].astype(F32)[:rows]
    for at in range(1, pieces):
        total = total + got_ref[at, :tall, :].astype(F32)
        part = part + got_ref[at, tall:, :].astype(F32)[:rows]
    grad_ref[...] = total
    low = total.astype(BF16)

    def stat_of(at):
        both = got_ref[pl.ds(at, 1), tall:, :][0].astype(F32)[rows:]
        return both[:6] + both[6:12]

    every = jnp.zeros((1, LANES), F32)
    olds = jnp.zeros((1, LANES), F32)
    mine = jnp.zeros((1, LANES), F32)
    down = jnp.zeros((6, LANES), F32)
    for d in range(VDP):
        down = down + stat_of(d * VCHIP + chip)
        for c in range(VCHIP):
            stat = stat_of(d * VCHIP + c)
            every = every + stat[0:1]
            if c == 0:
                olds = olds + stat[5:6]
    for c in range(VCHIP):
        mine = mine + stat_of(dp * VCHIP + c)[0:1]
    row_total = tall * VDP
    new_rows, means = [], []
    for i, ref in enumerate((rows_1, rows_2)):
        count = first_ref.shape[1] * 2 * VCHIP
        new_rows.append(decay * ref[...] + (1.0 - decay) * (mine[:, i * tall : (i + 1) * tall] / count))
        old = jnp.sum(jnp.where(lane == i, olds, 0.0), axis=1, keepdims=True)
        fresh = jnp.sum(every[:, i * tall : (i + 1) * tall], axis=1, keepdims=True)
        means.append((decay * old + (1.0 - decay) * (fresh / count)) / row_total)
    tile = jnp.concatenate(new_rows + [jnp.zeros((6, tall), F32)], axis=0)
    rows_out_1[...] = new_rows[0]
    rows_out_2[...] = new_rows[1]
    tile = jnp.concatenate([tile, jnp.zeros((8, LANES - tall), F32)], axis=1)
    turned = jnp.concatenate([tile, jnp.zeros((LANES - 8, LANES), F32)], axis=0).T
    scalars = jnp.zeros((1, LANES), F32)
    for i, (old_ref, out_ref, to) in enumerate(
        ((cols_1, cols_out_1, update_1), (cols_2, cols_out_2, update_2))
    ):
        sums = jnp.concatenate([down[1 + 2 * i : 2 + 2 * i], down[2 + 2 * i : 3 + 2 * i]], axis=1)
        cols = decay * old_ref[...] + (1.0 - decay) * (sums / row_total)
        out_ref[...] = cols
        grad = ffn_grad_ref[i]
        update = grad * lax.rsqrt(turned[:tall, i : i + 1] * cols / means[i])
        to[...] = update
        scalars = jnp.where(lane == 67 + i, total_of(update * update), scalars)
    for i, ref in enumerate((attn_ref, first_ref, second_ref)):
        weight = ref[...]
        scalars = jnp.where(lane == 64 + i, total_of(weight * weight), scalars)
    scalars = jnp.concatenate([rows_0[...], scalars[:, tall:]], axis=1)
    vector = vector_ref[...]
    power = jnp.sum(vector * vector, axis=1, keepdims=True)
    lines = jnp.concatenate(
        [part[:, :64], moment_ref[...], jnp.broadcast_to(power, (rows, LANES - 64 - width))], axis=1
    )
    piece = jnp.concatenate(
        [two_terms(lines), two_terms(jnp.concatenate([cols_0[...], scalars], axis=0))]
        + [jnp.zeros((4, LANES), F32)],
        axis=0,
    ).astype(BF16)
    for at in range(pieces):
        send_ref[at, :tall, :] = low
        send_ref[at, tall:, :] = piece


def tail_apply_kernel(
    place,
    mine_ref,
    other_ref,
    grad_ref,
    update_1,
    update_2,
    weight_0,
    weight_1,
    weight_2,
    rows_0,
    cols_0,
    vector_ref,
    moment_ref,
    new_0,
    new_1,
    new_2,
    rows_out,
    cols_out,
    vector_grad_ref,
    moment_out,
    vector_out,
    sums_s,
    rows_s,
):
    decay = 1.0 - STEP ** (-0.8)
    dp, chip, core = place[0], place[1], place[2]
    tall = weight_0.shape[0]
    rows, width = vector_ref.shape
    fsdp = 2 * VCHIP
    lane = iota((1, LANES), 1)
    refs = (mine_ref, other_ref)
    row_total = float(tall * VDP)
    col_total = float(LANES * fsdp)

    def lines_of(ref, at):
        both = ref[at, tall:, :].astype(F32)
        return both[0:4] + both[4:8], both[8:10] + both[10:12]

    scalars = jnp.zeros((1, LANES), F32)
    for ref in refs:
        for at in range(VDP * VCHIP):
            scalars = scalars + lines_of(ref, at)[1][1:2]
    scalar = lambda at: jnp.sum(jnp.where(lane == at, scalars, 0.0), axis=1, keepdims=True)

    tile, fresh = [], []
    for d in range(VDP):
        wide = jnp.zeros((tall, LANES), F32)
        for ref in refs:
            for c in range(VCHIP):
                block = ref[d * VCHIP + c, :tall, :].astype(F32)
                wide = wide + (block * block + EPS_ONE)
        fresh.append(jnp.sum(wide, axis=1, keepdims=True))
        tile.append(lines_of(mine_ref, d * VCHIP)[1][1:2])
    tile = jnp.concatenate(tile + [jnp.zeros((LANES - VDP, LANES), F32)], axis=0).T
    mean = jnp.zeros((1, 1), F32)
    new_rows = []
    for d in range(VDP):
        new = decay * tile[:tall, d : d + 1] + (1.0 - decay) * (fresh[d] / col_total)
        new_rows.append(1.0 / new)
        mean = mean + jnp.sum(new, axis=0, keepdims=True)
        sums_s[d] = jnp.broadcast_to(fresh[d], (tall, LANES))
    mean = mean / row_total
    mine = sums_s[pl.ds(dp, 1)][0]
    rows_s[...] = mine.T
    rows_new = decay * rows_0[...] + (1.0 - decay) * (rows_s[0:1, :tall] / col_total)
    rows_out[...] = rows_new
    power = jnp.zeros((1, 1), F32)
    for half, ref in enumerate(refs):
        for c in range(VCHIP):
            down = jnp.zeros((tall, LANES), F32)
            weighted = jnp.zeros((tall, LANES), F32)
            for d in range(VDP):
                block = ref[d * VCHIP + c, :tall, :].astype(F32)
                square = block * block
                down = down + (square + EPS_ONE)
                weighted = weighted + square * new_rows[d]
            down = jnp.sum(down, axis=0, keepdims=True)
            old = lines_of(ref, c)[1][0:1]
            cols = decay * old + (1.0 - decay) * (down / row_total)
            weighted = jnp.sum(weighted, axis=0, keepdims=True) / cols
            power = power + jnp.sum(weighted, axis=1, keepdims=True)
            if half == 0:
                sums_s[VDP + c] = jnp.broadcast_to(down, (tall, LANES))
    power = power * mean
    down = sums_s[pl.ds(VDP + chip, 1)][0][0:1, :]
    cols_new = decay * cols_0[...] + (1.0 - decay) * (down / row_total)
    cols_out[...] = cols_new
    column = jnp.concatenate(
        [
            jnp.concatenate([rows_new, jnp.zeros((1, LANES - tall), F32)], axis=1),
            jnp.zeros((LANES - 1, LANES), F32),
        ],
        axis=0,
    ).T[:tall, 0:1]
    update_0 = grad_ref[...] * lax.rsqrt(column * cols_new / mean)
    powers = (power, scalar(67), scalar(68))
    for i, (update, weight, new) in enumerate(
        (
            (update_0, weight_0, new_0),
            (update_1[...], weight_1, new_1),
            (update_2[...], weight_2, new_2),
        )
    ):
        entries = float(weight.shape[0] * weight.shape[1] * VDP * fsdp)
        clip = jnp.maximum(1.0, jnp.sqrt(powers[i] / entries) / CLIP_LIMIT)
        rate = STEP_RATE * jnp.maximum(EPS_TWO, jnp.sqrt(scalar(64 + i) / entries))
        new[...] = weight[...] - rate / clip * update
    powers, sizes = [], []
    for d in range(VDP):
        power = jnp.zeros((rows, 1), F32)
        size = jnp.zeros((rows, 1), F32)
        for c in range(VCHIP):
            at = d * VCHIP + c
            first, second = lines_of(mine_ref, at)[0], lines_of(other_ref, at)[0]
            both = first[:, :64] + second[:, :64]
            size = size + first[:, LANES - 1 :] + second[:, LANES - 1 :]
            near = jnp.where(core == 0, first[:, 64 : 64 + width], second[:, 64 : 64 + width])
            far = jnp.where(core == 0, second[:, 64 : 64 + width], first[:, 64 : 64 + width])
            moment = jnp.concatenate([near, far], axis=1)
            moment = decay * moment + (1.0 - decay) * (both * both + EPS_ONE)
            power = power + jnp.sum(both * both / moment, axis=1, keepdims=True)
            wide = jnp.concatenate([both, jnp.zeros((rows, LANES - 64), F32)], axis=1)
            sums_s[2 * VDP + at, :rows, :] = wide
        powers.append(power)
        sizes.append(size)
    both = sums_s[pl.ds(2 * VDP + dp * VCHIP + chip, 1), :rows, :][0]
    vector_grad = jnp.where(core == 0, both[:, :width], both[:, width : 2 * width])
    vector_grad_ref[...] = vector_grad
    moment = decay * moment_ref[...] + (1.0 - decay) * (vector_grad * vector_grad + EPS_ONE)
    moment_out[...] = moment
    step = vector_grad * lax.rsqrt(moment)
    bias = VDP // 2
    bias_power = sum(jnp.sum(power, axis=0, keepdims=True) for power in powers[:bias])
    bias_size = sum(jnp.sum(size, axis=0, keepdims=True) for size in sizes[:bias])
    power, size = powers[bias], sizes[bias]
    for d in range(bias + 1, VDP):
        power = jnp.where(dp == d, powers[d], power)
        size = jnp.where(dp == d, sizes[d], size)
    is_bias = dp < bias
    power = jnp.where(is_bias, bias_power, power)
    size = jnp.where(is_bias, bias_size, size)
    count = jnp.where(is_bias, float(FF), float(D))
    clip = jnp.maximum(1.0, jnp.sqrt(power / count) / CLIP_LIMIT)
    rate = STEP_RATE * jnp.maximum(EPS_TWO, jnp.sqrt(size / count))
    vector_out[...] = vector_ref[...] - rate / clip * step


def whole_call(kernel, name, place, outs, *operands, scratch=()):
    return pl.pallas_call(
        kernel,
        out_shape=[jax.ShapeDtypeStruct(shape, kind) for shape, kind in outs],
        in_specs=[pl.BlockSpec(memory_space=pltpu.SMEM)] + [vspec()] * len(operands),
        out_specs=[vspec()] * len(outs),
        scratch_shapes=list(scratch),
        compiler_params=params(16),
        name=name,
    )(place, *operands)


def core_swap(block):
    return lax.ppermute(block, "core", [(0, 1), (1, 0)])


def exchange(blocks, axes):
    return lax.all_to_all(blocks, axes, split_axis=0, concat_axis=0, tiled=True)


def after(value, *earlier):
    return pl.pallas_call(
        lambda *refs: None,
        out_shape=jax.ShapeDtypeStruct(value.shape, value.dtype),
        in_specs=[pl.BlockSpec(memory_space=pltpu.HBM)] * (1 + len(earlier)),
        out_specs=pl.BlockSpec(memory_space=pltpu.HBM),
        input_output_aliases={0: 0},
        compiler_params=params(),
        name="after",
    )(value, *earlier)


def pair_kernel(mine_ref, got_ref, out_ref):
    out_ref[...] = (mine_ref[...].astype(F32) + got_ref[...].astype(F32)).astype(BF16)


def pair_sum(mine, got):
    return pl.pallas_call(
        pair_kernel,
        out_shape=jax.ShapeDtypeStruct(mine.shape, BF16),
        in_specs=[vspec(), vspec()],
        out_specs=vspec(),
        compiler_params=params(16),
        name="pair_sum",
    )(mine, got)


CHIPS = ("dp", "chip")
ALL = ("dp", "chip", "core")


def layer(place, weights, segment_ids, tokens, cotangent, ffn_weights, send_core, send_ffn):
    table = jnp.asarray(encode_table())
    qk, x, qk_t, x_t, back, marks = place_tokens(segment_ids, tokens, cotangent, table)
    query_t, value, key_t, out_t, inverse, mixed, mixed_t, exps, weight, proj, vector = attend_forward(
        marks, place, x, qk, x_t, qk_t, *weights(marks)
    )
    ffn_mine, ffn_other = ffn_weights(marks, vector)
    block_out, resid, grad_t, ffn_mine, ffn_other, proj_g, vector_g = feed_forward(
        marks, place, x, back, mixed, mixed_t, proj, ffn_mine, ffn_other, vector
    )
    ffn_got, grad_t = send_ffn(ffn_mine, ffn_other, grad_t)
    shared = (marks, place, grad_t, query_t, value, key_t, out_t, inverse, exps, qk_t, x_t, weight, proj_g)
    pulled, grads_other, sums_other = attend_back(False, *shared)
    attn_got = send_core(grads_other)
    input_grad, grads_own, sums_own = attend_back(True, *shared, resid, pulled)
    return block_out, input_grad, grads_own, grads_other, attn_got, sums_own, sums_other, vector_g, ffn_got


def body(
    tokens,
    cotangent,
    segment_ids,
    attn_weight,
    ffn_in,
    ffn_out,
    vectors,
    attn_rows,
    attn_cols,
    in_rows,
    in_cols,
    out_rows,
    out_cols,
    vector_moment,
):
    place = jnp.stack([lax.axis_index("dp"), lax.axis_index("chip"), lax.axis_index("core")])
    place = place.astype(jnp.int32)
    pieces = VDP * VCHIP
    tall, wide = attn_weight.shape
    rows_v, cols_v = vectors.shape
    split = lambda array: array.reshape((VDP, VCHIP) + array.shape[1:])
    ffn_low = jnp.stack([ffn_in, ffn_out]).astype(BF16)
    attn_mine = exchange(pack_attn(place, attn_weight, vectors), CHIPS)

    def attn_weights(marks):
        mine = split(after(attn_mine, marks))
        return mine, core_swap(mine)

    def ffn_weights(marks, vector):
        early = lax.all_gather(ffn_low, "dp", axis=0, tiled=False)
        got = exchange(pack_ffn(early, marks), "chip")
        ffn_mine = after(got, vector)
        return ffn_mine, core_swap(ffn_mine)

    def send_ffn(mine, other, grad_t):
        both = pair_sum(mine, core_swap(other))
        got = exchange(both.reshape((pieces,) + mine.shape[2:]), CHIPS)
        return got, after(grad_t, both)

    (
        block_out,
        input_grad,
        grads_own,
        grads_other,
        attn_got,
        sums_own,
        sums_other,
        vector_g,
        ffn_got,
    ) = layer(place, attn_weights, segment_ids, tokens, cotangent, ffn_weights, core_swap, send_ffn)
    lay = lambda stat: stat.reshape(1, -1)
    rows_old = (lay(attn_rows), lay(in_rows), lay(out_rows))
    cols_old = (lay(attn_cols), lay(in_cols), lay(out_cols))
    weights_old = (attn_weight, ffn_in, ffn_out)
    ffn_grad, stat = whole_call(
        tail_ffn_kernel,
        "tail_ffn",
        place,
        [((2,) + ffn_in.shape, F32), ((8, LANES), F32)],
        ffn_got,
        *rows_old[1:],
        sums_own,
    )
    (sent,) = whole_call(
        tail_send_kernel,
        "tail_send",
        place,
        [((pieces, tall + VROWS, LANES), BF16)],
        grads_own,
        attn_got,
        vector_g,
        sums_own,
        sums_other,
        stat,
        core_swap(stat),
    )
    got = exchange(sent, CHIPS)
    attn_grad, update_1, update_2, rows_new_1, rows_new_2, cols_new_1, cols_new_2, sent = whole_call(
        tail_reduce_kernel,
        "tail_reduce",
        place,
        [
            (attn_weight.shape, F32),
            (ffn_in.shape, F32),
            (ffn_out.shape, F32),
            (rows_old[1].shape, F32),
            (rows_old[2].shape, F32),
            (cols_old[1].shape, F32),
            (cols_old[2].shape, F32),
            ((pieces, tall + VROWS, LANES), BF16),
        ],
        got,
        ffn_grad,
        *weights_old,
        *rows_old,
        *cols_old,
        vectors,
        vector_moment,
    )
    mine = exchange(sent, CHIPS)
    attn_new, in_new, out_new, rows_new_0, cols_new_0, vector_grad, moment_new, vectors_new = whole_call(
        tail_apply_kernel,
        "tail_apply",
        place,
        [
            (attn_weight.shape, F32),
            (ffn_in.shape, F32),
            (ffn_out.shape, F32),
            (rows_old[0].shape, F32),
            (cols_old[0].shape, F32),
            (vectors.shape, F32),
            (vectors.shape, F32),
            (vectors.shape, F32),
        ],
        mine,
        core_swap(mine),
        attn_grad,
        update_1,
        update_2,
        *weights_old,
        rows_old[0],
        cols_old[0],
        vectors,
        vector_moment,
        scratch=[
            pltpu.VMEM((2 * VDP + pieces, tall, LANES), F32),
            pltpu.VMEM((LANES, tall), F32),
        ],
    )
    return (
        block_out,
        input_grad,
        attn_grad,
        ffn_grad[0],
        ffn_grad[1],
        vector_grad,
        rows_new_0.reshape(-1),
        cols_new_0.reshape(-1),
        rows_new_1.reshape(-1),
        cols_new_1.reshape(-1),
        rows_new_2.reshape(-1),
        cols_new_2.reshape(-1),
        moment_new,
        attn_new,
        in_new,
        out_new,
        vectors_new,
    )


def gather_all(block):
    shape = (lax.axis_size("dp"), lax.axis_size("chip") * 2)
    count = shape[0] * shape[1]
    got = exchange(jnp.broadcast_to(block[None], (count,) + block.shape), ALL)
    return got.reshape(shape + block.shape)


def unblock(parts):
    dp_count, fsdp_count, rows, cols = parts.shape
    return parts.transpose(0, 2, 1, 3).reshape(dp_count * rows, fsdp_count * cols)


def scatter_sum(full):
    dp_count = lax.axis_size("dp")
    fsdp_count = lax.axis_size("chip") * 2
    rows, cols = full.shape
    by_col = full.astype(BF16).reshape(rows, fsdp_count, cols // fsdp_count).transpose(1, 0, 2)
    got = exchange(by_col, ("chip", "core"))
    part = jnp.sum(got.astype(F32), axis=0).astype(BF16)
    by_row = part.reshape(dp_count, rows // dp_count, cols // fsdp_count)
    return jnp.sum(exchange(by_row, "dp").astype(F32), axis=0)


def body_any(
    tokens,
    cotangent,
    segment_ids,
    attn_weight,
    ffn_in,
    ffn_out,
    vectors,
    attn_rows,
    attn_cols,
    in_rows,
    in_cols,
    out_rows,
    out_cols,
    vector_moment,
):
    dp_count = lax.axis_size("dp")
    fsdp_count = lax.axis_size("chip") * 2
    dp_place = lax.axis_index("dp")
    fsdp_place = lax.axis_index("chip") * 2 + lax.axis_index("core")
    rows_w = attn_weight.shape[0]
    rows_v = vectors.shape[0]
    place = jnp.zeros((3,), jnp.int32)
    full_attn = unblock(gather_all(attn_weight.astype(BF16)))
    full_vector = unblock(gather_all(vectors.astype(BF16)))
    full_ffn = jnp.stack(
        [unblock(gather_all(ffn_in.astype(BF16))), unblock(gather_all(ffn_out.astype(BF16)))]
    )
    tall = D // VDP
    cut = full_attn.reshape(VDP, tall, VCHIP, 2, LANES).transpose(3, 0, 2, 1, 4)
    lines = full_vector.reshape(VDP, VEC // VDP, 2, LANES).transpose(0, 2, 1, 3)
    lines = lines.reshape(VDP, 1, 2 * VEC // VDP, LANES)
    lines = jnp.pad(lines, ((0, 0), (0, VCHIP - 1), (0, VROWS - 2 * VEC // VDP), (0, 0)))
    weights = (
        jnp.concatenate([cut[0], lines], axis=2),
        jnp.concatenate([cut[1], jnp.zeros_like(lines)], axis=2),
    )
    ffn_cut = full_ffn.reshape(2, VDP, tall, VCHIP, 2, FF // (2 * VCHIP))
    ffn_cut = ffn_cut.transpose(4, 3, 1, 0, 2, 5)
    (
        block_out,
        input_grad,
        grads_own,
        grads_other,
        _,
        sums_own,
        sums_other,
        vector_g,
        ffn_got,
    ) = layer(
        place,
        lambda marks: weights,
        segment_ids,
        tokens,
        cotangent,
        lambda marks, vector: (ffn_cut[0], ffn_cut[1]),
        lambda block: block,
        lambda mine, other, grad_t: (jnp.stack([mine, other]), grad_t),
    )
    attn_full = jnp.stack([grads_own, grads_other]).transpose(1, 3, 2, 0, 4).reshape(D, 4 * D)
    ffn_full = ffn_got.transpose(3, 1, 4, 2, 0, 5).reshape(2, D, FF)
    sums = jnp.concatenate([sums_own[:2], sums_other[:2]], axis=1)
    vector_full = jnp.concatenate([vector_g[:8], sums, vector_g[10:]], axis=0)
    attn_grad = scatter_sum(attn_full)
    in_grad = scatter_sum(ffn_full[0])
    out_grad = scatter_sum(ffn_full[1])
    vector_grad = scatter_sum(vector_full)

    decay = 1.0 - STEP ** (-0.8)
    gradients = (attn_grad, in_grad, out_grad)
    weights_old = (attn_weight, ffn_in, ffn_out)
    rows_old = (attn_rows, in_rows, out_rows)
    cols_old = (attn_cols, in_cols, out_cols)
    moment_new = decay * vector_moment + (1.0 - decay) * (vector_grad * vector_grad + EPS_ONE)
    vector_step = vector_grad * lax.rsqrt(moment_new)
    squares = [gradient * gradient + EPS_ONE for gradient in gradients]
    pieces = []
    for square in squares:
        pieces.append(jnp.sum(square, axis=1))
    for square in squares:
        pieces.append(jnp.sum(square, axis=0))
    pieces.append(jnp.sum(vector_step * vector_step, axis=1))
    pieces.append(jnp.sum(vectors * vectors, axis=1))
    pieces.append(jnp.stack([jnp.sum(weight * weight) for weight in weights_old]))
    pieces.append(jnp.stack([jnp.sum(old) for old in rows_old]))
    sizes = [piece.shape[0] for piece in pieces]
    flat = jnp.concatenate(pieces)
    flat = jnp.pad(flat, (0, -flat.shape[0] % 1024)).reshape(-1, LANES)
    got = gather_all(flat).reshape(dp_count, fsdp_count, -1)
    offsets = [0]
    for length in sizes:
        offsets.append(offsets[-1] + length)
    take = lambda i: got[:, :, offsets[i] : offsets[i + 1]]
    rows_new, cols_new, row_means, entries = [], [], [], []
    for i in range(3):
        count_rows = rows_w * dp_count
        count_cols = weights_old[i].shape[1] * fsdp_count
        entries.append(float(count_rows * count_cols))
        row_all = jnp.sum(take(i), axis=1)
        mine = lax.dynamic_index_in_dim(row_all, dp_place, 0, keepdims=False)
        rows_new.append(decay * rows_old[i] + (1.0 - decay) * mine / count_cols)
        col_all = jnp.sum(take(3 + i), axis=0)
        mine = lax.dynamic_index_in_dim(col_all, fsdp_place, 0, keepdims=False)
        cols_new.append(decay * cols_old[i] + (1.0 - decay) * mine / count_rows)
        old_total = jnp.sum(take(9)[:, 0, i])
        row_means.append(
            (decay * old_total + (1.0 - decay) * jnp.sum(row_all) / count_cols) / count_rows
        )
    step_rows = jnp.sum(take(6), axis=1).reshape(-1)
    weight_rows = jnp.sum(take(7), axis=1).reshape(-1)
    weight_totals = jnp.sum(take(8), axis=(0, 1))
    updates = []
    for i in range(3):
        second = rows_new[i][:, None] * cols_new[i][None, :] / row_means[i]
        updates.append(gradients[i] * lax.rsqrt(second))
    flat = jnp.stack([jnp.sum(update * update) for update in updates])
    flat = jnp.broadcast_to(jnp.pad(flat, (0, 5))[:, None], (8, LANES))
    totals = jnp.sum(gather_all(flat)[:, :, :, 0], axis=(0, 1))
    new_weights = []
    for i in range(3):
        clip_factor = jnp.maximum(1.0, jnp.sqrt(totals[i] / entries[i]) / CLIP_LIMIT)
        step_size = STEP_RATE * jnp.maximum(EPS_TWO, jnp.sqrt(weight_totals[i] / entries[i]))
        new_weights.append(weights_old[i] - step_size / clip_factor * updates[i])
    bias_rows = FF // D
    row_places = jnp.arange(VEC)
    counts = jnp.where(row_places < bias_rows, float(FF), float(D))
    grouped_updates = jnp.where(row_places < bias_rows, jnp.sum(step_rows[:bias_rows]), step_rows)
    grouped_weights = jnp.where(row_places < bias_rows, jnp.sum(weight_rows[:bias_rows]), weight_rows)
    clip_rows = jnp.maximum(1.0, jnp.sqrt(grouped_updates / counts) / CLIP_LIMIT)
    step_sizes = STEP_RATE * jnp.maximum(EPS_TWO, jnp.sqrt(grouped_weights / counts))
    factor_rows = lax.dynamic_slice_in_dim(step_sizes / clip_rows, dp_place * rows_v, rows_v)
    vectors_new = vectors - factor_rows[:, None] * vector_step
    return (
        block_out,
        input_grad,
        attn_grad,
        in_grad,
        out_grad,
        vector_grad,
        rows_new[0],
        cols_new[0],
        rows_new[1],
        cols_new[1],
        rows_new[2],
        cols_new[2],
        moment_new,
        new_weights[0],
        new_weights[1],
        new_weights[2],
        vectors_new,
    )


def solution(mesh):
    dp_count, fsdp_count = mesh.shape["dp"], mesh.shape["fsdp"]
    inner = jax.sharding.Mesh(mesh.devices.reshape(dp_count, fsdp_count // 2, 2), ALL)
    fsdp = ("chip", "core")
    split = P(ALL, None)
    block = P("dp", fsdp)
    stats = (P("dp"), P(fsdp)) * 3
    plain = dp_count == VDP and fsdp_count == 2 * VCHIP
    return jax.shard_map(
        body if plain else body_any,
        mesh=inner,
        in_specs=(split,) * 3 + (block,) * 4 + stats + (block,),
        out_specs=(split,) * 2 + (block,) * 4 + stats + (block,) * 5,
        check_vma=False,
    )
```

```python
import functools
import math

import jax
import jax.numpy as jnp
import numpy as np
from jax import lax
from jax.experimental import pallas as pl
from jax.experimental.pallas import tpu as pltpu
from jax.sharding import PartitionSpec as P

D = 256
FF = 2048
HEADS = 8
HEAD_DIM = 32
SEQ = 1024
HALF = 512
GROUP = 4
LANES = 128
QBLOCK = 256
WGRID = 32
STEP = 10
VEC = 16
TILE = 1024
CHUNK = 256
SUB = 512
LEAD = 5
STRIP = 64
VDP = 4
VCHIP = 4
VROWS = 16

EPS_NORM = 1e-05
EPS_ONE = 1e-30
EPS_TWO = 0.001
CLIP_LIMIT = 1.0
STEP_RATE = 0.3
FAR = 1e30
LOG2_E = math.log2(math.e)
SCALE = HEAD_DIM ** (-0.5)
GELU_A = math.sqrt(2.0 / math.pi)
GELU_B = 0.044715
F32 = jnp.float32
BF16 = jnp.bfloat16
MIB = 1024 * 1024


def dot(left, right):
    return jnp.dot(left, right, preferred_element_type=F32)


def dot_nt(left, right):
    return lax.dot_general(left, right, (((1,), (1,)), ((), ())), preferred_element_type=F32)


def encode_table():
    half = D // 2
    feature = np.arange(half)
    freq = np.exp(
        (2 * (feature // 2)).astype(np.float32) * np.float32(-math.log(10000.0) / half)
    ).astype(np.float32)
    angles = np.arange(1, WGRID + 1, dtype=np.float32)[:, None] * freq[None, :]
    table = np.where(feature % 2 == 0, np.sin(angles), np.cos(angles)).astype(np.float32)
    low = jnp.bfloat16
    one = table.astype(low)
    rest = table - one.astype(np.float32)
    two = rest.astype(low)
    three = (rest - two.astype(np.float32)).astype(low)
    blank = np.zeros((LANES - 3 * WGRID, half), low)
    return np.concatenate([one, two, three, blank], axis=0)


def iota(shape, dim):
    return lax.broadcasted_iota(jnp.int32, shape, dim)


def norm_forward(rows):
    centered = rows - jnp.mean(rows, axis=-1, keepdims=True)
    inverse = lax.rsqrt(jnp.mean(centered * centered, axis=-1, keepdims=True) + EPS_NORM)
    return centered * inverse, inverse


def norm_backward(upstream, normed, inverse):
    return inverse * (
        upstream
        - jnp.mean(upstream, axis=-1, keepdims=True)
        - normed * jnp.mean(upstream * normed, axis=-1, keepdims=True)
    )

def vspec():
    return pl.BlockSpec(memory_space=pltpu.VMEM)


def params(mib=56, **more):
    return pltpu.CompilerParams(vmem_limit_bytes=mib * MIB, **more)


def pack_kernel(place, attn_ref, vector_ref, out_ref):
    owner = place[1] * 2 + place[2]
    vector = vector_ref[...]
    rows = vector.shape[0]
    wide = jnp.concatenate([vector] * (LANES // vector.shape[1]), axis=1)
    slot = iota((rows, LANES), 1) // vector.shape[1]
    per = LANES // vector.shape[1]
    parts = [attn_ref[...]]
    for half in range(2):
        parts.append(jnp.where(slot + half * per == owner, wide, 0.0))
    parts.append(jnp.zeros((VROWS - 2 * rows, LANES), F32))
    piece = jnp.concatenate(parts, axis=0).astype(BF16)
    for at in range(VDP * VCHIP):
        out_ref[at] = piece


def pack_attn(place, attn_weight, vectors):
    return pl.pallas_call(
        pack_kernel,
        out_shape=jax.ShapeDtypeStruct((VDP * VCHIP, attn_weight.shape[0] + VROWS, LANES), BF16),
        in_specs=[pl.BlockSpec(memory_space=pltpu.SMEM), vspec(), vspec()],
        out_specs=vspec(),
        compiler_params=params(),
        name="pack_attn",
    )(place, attn_weight, vectors)


def pack_ffn_kernel(first_ref, second_ref, *refs):
    out_ref = refs[-1]
    first = first_ref[...].astype(BF16)
    second = second_ref[...].astype(BF16)
    for at in range(VDP * VCHIP):
        out_ref[at, 0] = first
        out_ref[at, 1] = second


def pack_ffn(ffn_in, ffn_out, *earlier):
    return pl.pallas_call(
        pack_ffn_kernel,
        out_shape=jax.ShapeDtypeStruct((VDP * VCHIP, 2) + ffn_in.shape, BF16),
        in_specs=[vspec(), vspec()] + [pl.BlockSpec(memory_space=pl.ANY)] * len(earlier),
        out_specs=vspec(),
        compiler_params=params(),
        name="pack_ffn",
    )(ffn_in, ffn_out, *earlier)


def place_kernel(
    segment_ref, tokens_ref, back_ref, table_ref, qk_ref, x_ref, qk_t_ref, x_t_ref, turned_ref, marks_ref
):
    row = pl.program_id(0)
    starts = []
    for number in range(1, 4):
        at = jnp.int32(0)
        for step in (512, 256, 128, 64, 32, 16, 8, 4, 2, 1, 1):
            probe = jnp.minimum(at + (step - 1), SEQ - 1)
            at = jnp.where(segment_ref[row, probe] < number, at + step, at)
        starts.append(at)
    edges = [jnp.int32(0)] + starts + [jnp.int32(SEQ)]
    begin = jnp.int32(0)
    for number in range(3, -1, -1):
        begin = jnp.where(edges[number + 1] - edges[number] == HALF, edges[number], begin)
    for number in range(3):
        marks_ref[row, number] = starts[number]
    marks_ref[row, 3] = begin
    one, two, three = starts
    x = pltpu.roll(tokens_ref[...].astype(F32), (SEQ - begin) & (SEQ - 1), 0)
    x_ref[...] = x.astype(BF16)
    x_t_ref[...] = x.T.astype(BF16)
    back = back_ref[...].astype(F32)
    turned_ref[...] = pltpu.roll(back, (SEQ - begin) & (SEQ - 1), 0).astype(BF16)
    at = (iota((SEQ, LANES), 0) + begin) & (SEQ - 1)
    lane = iota((SEQ, LANES), 1)
    start = jnp.where(at >= three, three, jnp.where(at >= two, two, jnp.where(at >= one, one, 0)))
    local = at - start
    kept = lane < 3 * WGRID
    slot = lane & (WGRID - 1)
    hot_r = jnp.where(((local >> 5) == slot) & kept, 1.0, 0.0).astype(BF16)
    hot_c = jnp.where(((local & (WGRID - 1)) == slot) & kept, 1.0, 0.0).astype(BF16)
    table = table_ref[...]
    places = jnp.concatenate([dot(hot_r, table), dot(hot_c, table)], axis=1)
    qk = x + places
    qk_ref[...] = qk.astype(BF16)
    qk_t_ref[...] = qk.T.astype(BF16)


def place_tokens(segment_ids, tokens, cotangent, table):
    rows = segment_ids.shape[0]
    by_row = lambda r: (r, 0)
    return pl.pallas_call(
        place_kernel,
        out_shape=(
            jax.ShapeDtypeStruct(tokens.shape, BF16),
            jax.ShapeDtypeStruct(tokens.shape, BF16),
            jax.ShapeDtypeStruct((D, tokens.shape[0]), BF16),
            jax.ShapeDtypeStruct((D, tokens.shape[0]), BF16),
            jax.ShapeDtypeStruct(tokens.shape, BF16),
            jax.ShapeDtypeStruct((rows, 4), jnp.int32),
        ),
        grid=(rows,),
        in_specs=[
            pl.BlockSpec(memory_space=pltpu.SMEM),
            pl.BlockSpec((SEQ, D), by_row),
            pl.BlockSpec((SEQ, D), by_row),
            pl.BlockSpec((LANES, LANES), lambda r: (0, 0)),
        ],
        out_specs=(
            pl.BlockSpec((SEQ, D), by_row),
            pl.BlockSpec((SEQ, D), by_row),
            pl.BlockSpec((D, SEQ), lambda r: (0, r)),
            pl.BlockSpec((D, SEQ), lambda r: (0, r)),
            pl.BlockSpec((SEQ, D), by_row),
            pl.BlockSpec(memory_space=pltpu.SMEM),
        ),
        compiler_params=params(dimension_semantics=("arbitrary",)),
        cost_estimate=pl.CostEstimate(flops=600_000_000, bytes_accessed=4_000_000, transcendentals=0),
        name="place_tokens",
    )(segment_ids, tokens, cotangent, table)


def attend_kernel(
    marks,
    place,
    x_ref,
    qk_ref,
    x_t_ref,
    qk_t_ref,
    mine_ref,
    other_ref,
    query_t_ref,
    value_ref,
    key_t_ref,
    out_t_ref,
    inverse_ref,
    mixed_ref,
    mixed_t_ref,
    exps_ref,
    weight_ref,
    proj_ref,
    vector_ref,
    key_s,
    value_s,
    mark_k,
    mark_q,
    masked_s,
    weight_t_s,
    bias_s,
):
    row = pl.program_id(0)
    group = pl.program_id(1)
    begin = marks[row, 3]
    core = place[2]

    @pl.when((row == 0) & (group == 0))
    def _():
        tall = D // VDP
        for d in range(VDP):
            rows = slice(d * tall, (d + 1) * tall)
            total = jnp.zeros((8, LANES), F32)
            for c in range(VCHIP):
                for ref, half in ((mine_ref, core), (other_ref, 1 - core)):
                    if c < 3:
                        to = pl.ds(pl.multiple_of(c * D + half * LANES, LANES), LANES)
                        weight_ref[rows, to] = ref[d, c, :tall, :]
                    else:
                        to = pl.ds(pl.multiple_of(half * LANES, LANES), LANES)
                        proj_ref[rows, to] = ref[d, c, :tall, :]
                    total += ref[d, c, tall:, :].astype(F32)[:8]
            vector_ref[d * 4 : (d + 1) * 4, :LANES] = total[:4]
            vector_ref[d * 4 : (d + 1) * 4, LANES:] = total[4:]
        weight_t_s[...] = weight_ref[...].astype(F32).T.astype(BF16)
        bias_s[...] = vector_ref[8:16, :].T

    @pl.when(group == 0)
    def _():
        qk_t = qk_t_ref[...]
        query_t = (dot(weight_t_s[:D, :], qk_t) + bias_s[:, 0:1]) * SCALE
        query_t_ref[...] = query_t.astype(BF16)
        key_t_ref[...] = dot(weight_t_s[D : 2 * D, :], qk_t).astype(BF16)
        key_s[...] = dot(qk_ref[...], weight_ref[:, D : 2 * D]).astype(BF16)
        value = dot(x_ref[...], weight_ref[:, 2 * D : 3 * D]) + vector_ref[9:10, :]
        value_ref[...] = value.astype(BF16)
        value_t = dot(weight_t_s[2 * D :, :], x_t_ref[...]) + bias_s[:, 1:2]
        value_t = value_t.astype(BF16)
        for head in range(HEADS):
            value_s[head, :HEAD_DIM, :] = value_t[head * HEAD_DIM : (head + 1) * HEAD_DIM, :]
            value_s[head, HEAD_DIM:, :] = jnp.ones((16, SEQ), BF16)
        one, two, three = marks[row, 0], marks[row, 1], marks[row, 2]

        def number_of(shape, dim):
            here = (iota(shape, dim) + (HALF + begin)) & (SEQ - 1)
            return (
                jnp.where(here >= one, 1, 0)
                + jnp.where(here >= two, 1, 0)
                + jnp.where(here >= three, 1, 0)
            )

        lane = iota((HALF, LANES), 1)
        number = number_of((HALF, LANES), 0)
        mark_k[...] = jnp.where((number != lane) & (lane < 4), -FAR, 0.0).astype(BF16)
        number = number_of((LANES, HALF), 1)
        mark_q[...] = jnp.where(number == iota((LANES, HALF), 0), 1.0, 0.0).astype(BF16)

    lanes = pl.ds(pl.multiple_of(group * LANES, LANES), LANES)
    head_of = iota((1, LANES), 1) // HEAD_DIM
    keys_here = key_s[:, lanes]
    for at_head in range(GROUP):
        mask = jnp.where(head_of == at_head, 1.0, 0.0).astype(BF16)
        masked_s[at_head] = keys_here * mask

    def scores_of(item):
        half, at_head, block = item
        key_m = masked_s[at_head, half * HALF : (half + 1) * HALF, :]
        at = half * HALF + block * QBLOCK
        query = query_t_ref[lanes, at : at + QBLOCK]
        if half == 1:
            key_m = jnp.concatenate([key_m, mark_k[...]], axis=1)
            query = jnp.concatenate(
                [query, mark_q[:, block * QBLOCK : (block + 1) * QBLOCK]], axis=0
            )
        return dot(key_m, query)

    def exps_of(item):
        half, at_head, block = item
        cols = slice(at_head * HALF + block * QBLOCK, at_head * HALF + (block + 1) * QBLOCK)
        scores = scores_of(item)
        below = (scores - jnp.max(scores, axis=0, keepdims=True)) * LOG2_E
        exps_ref[0, 0, half, :, cols] = jnp.exp2(below.astype(BF16))

    def finish(item):
        half, at_head, block = item
        at = half * HALF + block * QBLOCK
        rows = slice(half * HALF, (half + 1) * HALF)
        cols = slice(at_head * HALF + block * QBLOCK, at_head * HALF + (block + 1) * QBLOCK)
        out = dot(value_s[group * GROUP + at_head, :, rows], exps_ref[0, 0, half, :, cols])
        inverse = 1.0 / out[HEAD_DIM : HEAD_DIM + 1, :]
        inverse_ref[0, at_head : at_head + 1, at : at + QBLOCK] = inverse
        out_t_ref[at_head * HEAD_DIM : (at_head + 1) * HEAD_DIM, at : at + QBLOCK] = (
            out[:HEAD_DIM, :] * inverse
        )

    items = [
        (half, at_head, block)
        for half in range(2)
        for at_head in range(GROUP)
        for block in range(HALF // QBLOCK)
    ]
    for i in range(len(items) + 1):
        if i < len(items):
            exps_of(items[i])
        if i >= 1:
            finish(items[i - 1])
    out_t = out_t_ref[...]
    mixed_t_ref[...] = out_t.astype(BF16)
    mixed_ref[...] = out_t.T.astype(BF16)


def attend_forward(marks, place, x, qk, x_t, qk_t, mine, other):
    total = x.shape[0]
    rows = total // SEQ
    by_row = lambda r, g, m, p: (r, 0)
    by_col = lambda r, g, m, p: (0, r)
    by_both = lambda r, g, m, p: (g, r)
    whole = lambda r, g, m, p: (0, 0)
    return pl.pallas_call(
        attend_kernel,
        out_shape=(
            jax.ShapeDtypeStruct((D, total), BF16),
            jax.ShapeDtypeStruct((total, D), BF16),
            jax.ShapeDtypeStruct((D, total), BF16),
            jax.ShapeDtypeStruct((D, total), F32),
            jax.ShapeDtypeStruct((2, 8, total), F32),
            jax.ShapeDtypeStruct((total, D), BF16),
            jax.ShapeDtypeStruct((D, total), BF16),
            jax.ShapeDtypeStruct((rows, 2, 2, HALF, GROUP * HALF), BF16),
            jax.ShapeDtypeStruct((D, 3 * D), BF16),
            jax.ShapeDtypeStruct((D, D), BF16),
            jax.ShapeDtypeStruct((VEC, D), F32),
        ),
        grid_spec=pltpu.PrefetchScalarGridSpec(
            num_scalar_prefetch=2,
            grid=(rows, 2),
            in_specs=[
                pl.BlockSpec((SEQ, D), by_row),
                pl.BlockSpec((SEQ, D), by_row),
                pl.BlockSpec((D, SEQ), by_col),
                pl.BlockSpec((D, SEQ), by_col),
                vspec(),
                vspec(),
            ],
            out_specs=[
                pl.BlockSpec((D, SEQ), by_col),
                pl.BlockSpec((SEQ, D), by_row),
                pl.BlockSpec((D, SEQ), by_col),
                pl.BlockSpec((LANES, SEQ), by_both),
                pl.BlockSpec((1, 8, SEQ), lambda r, g, m, p: (g, 0, r)),
                pl.BlockSpec((SEQ, LANES), lambda r, g, m, p: (r, g)),
                pl.BlockSpec((LANES, SEQ), by_both),
                pl.BlockSpec((1, 1, 2, HALF, GROUP * HALF), lambda r, g, m, p: (r, g, 0, 0, 0)),
                pl.BlockSpec((D, 3 * D), whole),
                pl.BlockSpec((D, D), whole),
                pl.BlockSpec((VEC, D), whole),
            ],
            scratch_shapes=[
                pltpu.VMEM((SEQ, D), BF16),
                pltpu.VMEM((HEADS, HEAD_DIM + 16, SEQ), BF16),
                pltpu.VMEM((HALF, LANES), BF16),
                pltpu.VMEM((LANES, HALF), BF16),
                pltpu.VMEM((GROUP, SEQ, LANES), BF16),
                pltpu.VMEM((3 * D, D), BF16),
                pltpu.VMEM((D, 8), F32),
            ],
        ),
        compiler_params=params(dimension_semantics=("arbitrary", "arbitrary")),
        cost_estimate=pl.CostEstimate(
            flops=20_000_000_000, bytes_accessed=30_000_000, transcendentals=8_400_000
        ),
        name="attend_forward",
    )(marks, place, x, qk, x_t, qk_t, mine, other)


def feed_kernel(
    marks,
    place,
    x_ref,
    back_ref,
    mixed_ref,
    mixed_t_ref,
    proj_ref,
    mine_ref,
    other_ref,
    vector_ref,
    block_ref,
    resid_ref,
    mixed_grad_ref,
    mine_out,
    other_out,
    proj_out,
    vector_out,
    first_w,
    second_w,
    first_acc,
    second_acc,
    proj_acc,
    vector_acc,
    hidden_s,
    slope_s,
    pre_s,
    first_low_s,
    branch_low_s,
    attended_s,
    block_s,
    eye_s,
):
    step = pl.program_id(0)
    core = place[2]
    tall = D // VDP
    wide = FF // (2 * VCHIP)

    @pl.when(step == 0)
    def _():
        first_acc[...] = jnp.zeros_like(first_acc)
        second_acc[...] = jnp.zeros_like(second_acc)
        proj_acc[...] = jnp.zeros_like(proj_acc)
        vector_acc[...] = jnp.zeros_like(vector_acc)
        eye_s[...] = jnp.where(iota((D, D), 0) == iota((D, D), 1), 1.0, 0.0).astype(BF16)
        for d in range(VDP):
            rows = slice(d * tall, (d + 1) * tall)
            for c in range(VCHIP):
                for ref, half in ((mine_ref, core), (other_ref, 1 - core)):
                    to = pl.ds(pl.multiple_of((2 * c + half) * wide, wide), wide)
                    first_w[rows, to] = ref[d, c, 0]
                    second_w[rows, to] = ref[d, c, 1]

    bias_o, bias_2 = vector_ref[10:11, :], vector_ref[11:12, :]
    gain_1, shift_1 = vector_ref[12:13, :], vector_ref[13:14, :]
    gain_2, shift_2 = vector_ref[14:15, :], vector_ref[15:16, :]
    at_row = pl.multiple_of((step % (SEQ // TILE)) * TILE, TILE)
    chunks = FF // CHUNK
    pair = 2

    def columns(at, count=1):
        return slice(at * CHUNK, (at + count) * CHUNK)

    def hidden_of(rows, at, pre):
        pre = (pre + vector_ref[at : at + 1, :]).astype(BF16)
        cube = BF16(GELU_A * GELU_B) * (pre * pre)
        gate = BF16(0.5) + BF16(0.5) * jnp.tanh(pre * (cube + BF16(GELU_A)))
        hidden_s[rows, columns(at)] = pre * gate
        slope_s[rows, columns(at)] = gate + (gate - gate * gate) * (
            pre * (BF16(6.0) * cube + BF16(2.0 * GELU_A))
        )

    def stages(sub):
        rows_at = sub * SUB
        rows = slice(rows_at, rows_at + SUB)
        attended = dot(mixed_ref[rows, :], proj_ref[...]) + bias_o
        norm_1, inverse_1 = norm_forward(x_ref[rows, :].astype(F32) + attended)
        first = norm_1 * gain_1 + shift_1
        first_low = first.astype(BF16)
        first_low_s[rows, :] = first_low
        yield
        branch = jnp.zeros((SUB, D), F32)
        for i in range(chunks + 1):
            if i < chunks:
                hidden_of(rows, i, dot(first_low, first_w[:, columns(i)]))
            if i >= pair and i % pair == 0:
                cols = columns(i - pair, pair)
                branch += dot_nt(hidden_s[rows, cols], second_w[:, cols])
            yield
        norm_2, inverse_2 = norm_forward(first + (branch + bias_2))
        block_s[pl.ds(at_row + rows_at, SUB), :] = norm_2 * gain_2 + shift_2
        back = back_ref[rows, :].astype(F32)
        vector_acc[14:15, :] += jnp.sum(back * norm_2, axis=0, keepdims=True)
        vector_acc[15:16, :] += jnp.sum(back, axis=0, keepdims=True)
        resid_2 = norm_backward(back * gain_2, norm_2, inverse_2)
        branch_low = resid_2.astype(BF16)
        branch_low_s[rows, :] = branch_low
        vector_acc[11:12, :] += jnp.sum(branch_low.astype(F32), axis=0, keepdims=True)
        yield
        first_back = resid_2
        if sub == 1:
            branch_t = dot_nt(eye_s[...], branch_low_s[...]).astype(BF16)
            first_t = dot_nt(eye_s[...], first_low_s[...]).astype(BF16)
            first_t = jnp.concatenate([first_t, jnp.ones((16, TILE), BF16)], axis=0)
        for i in range(chunks + 1):
            if i < chunks:
                pull = dot(branch_low, second_w[:, columns(i)]).astype(BF16)
                pre_s[rows, columns(i)] = pull * slope_s[rows, columns(i)]
                if sub == 1:
                    second_acc[:, columns(i)] += dot(branch_t, hidden_s[:, columns(i)])
            if i >= 1 and sub == 1:
                cols = columns(i - 1)
                first_acc[:, cols] += dot(first_t, pre_s[:, cols])
            if i >= pair and i % pair == 0:
                cols = columns(i - pair, pair)
                first_back += dot_nt(pre_s[rows, cols], first_w[:, cols])
            yield
        vector_acc[12:13, :] += jnp.sum(first_back * norm_1, axis=0, keepdims=True)
        vector_acc[13:14, :] += jnp.sum(first_back, axis=0, keepdims=True)
        resid_1 = norm_backward(first_back * gain_1, norm_1, inverse_1)
        resid_ref[rows, :] = resid_1
        attended_low = resid_1.astype(BF16)
        attended_s[rows, :] = attended_low
        vector_acc[10:11, :] += jnp.sum(attended_low.astype(F32), axis=0, keepdims=True)
        mixed_grad_ref[:, rows] = dot_nt(proj_ref[...], attended_low).astype(BF16)
        yield

    ahead, behind = stages(0), stages(1)
    for _ in range(LEAD):
        next(ahead)
    running = [ahead, behind]
    while running:
        for program in list(running):
            if next(program, 0) == 0:
                running.remove(program)
    proj_acc[...] += dot(mixed_t_ref[...], attended_s[...])

    @pl.when(step % (SEQ // TILE) == SEQ // TILE - 1)
    def _():
        block_ref[...] = pltpu.roll(block_s[...], marks[step // (SEQ // TILE), 3], 0)

    @pl.when(step == pl.num_programs(0) - 1)
    def _():
        for d in range(VDP):
            rows = slice(d * tall, (d + 1) * tall)
            for c in range(VCHIP):
                for ref, half in ((mine_out, core), (other_out, 1 - core)):
                    to = pl.ds(pl.multiple_of((2 * c + half) * wide, wide), wide)
                    ref[d, c, 0] = first_acc[rows, to].astype(BF16)
                    ref[d, c, 1] = second_acc[rows, to].astype(BF16)
        proj_out[...] = proj_acc[...]
        for at in range(FF // D):
            vector_out[at : at + 1, :] = first_acc[D : D + 1, at * D : (at + 1) * D]
        vector_out[FF // D :, :] = vector_acc[FF // D :, :]


def feed_forward(marks, place, x, back, mixed, mixed_t, proj, mine, other, vector):
    total = x.shape[0]
    tile = lambda i, m, p: (i, 0)
    by_col = lambda i, m, p: (0, i)
    whole = lambda i, m, p: (0, 0)
    whole5 = lambda i, m, p: (0, 0, 0, 0, 0)
    return pl.pallas_call(
        feed_kernel,
        out_shape=(
            jax.ShapeDtypeStruct((total, D), F32),
            jax.ShapeDtypeStruct((total, D), F32),
            jax.ShapeDtypeStruct((D, total), BF16),
            jax.ShapeDtypeStruct(mine.shape, BF16),
            jax.ShapeDtypeStruct(mine.shape, BF16),
            jax.ShapeDtypeStruct((D, D), F32),
            jax.ShapeDtypeStruct((VEC, D), F32),
        ),
        grid_spec=pltpu.PrefetchScalarGridSpec(
            num_scalar_prefetch=2,
            grid=(total // TILE,),
            in_specs=[
                pl.BlockSpec((TILE, D), tile),
                pl.BlockSpec((TILE, D), tile),
                pl.BlockSpec((TILE, D), tile),
                pl.BlockSpec((D, TILE), by_col),
                pl.BlockSpec((D, D), whole),
                vspec(),
                vspec(),
                pl.BlockSpec((VEC, D), whole),
            ],
            out_specs=[
                pl.BlockSpec((SEQ, D), lambda i, m, p: (i // (SEQ // TILE), 0)),
                pl.BlockSpec((TILE, D), tile),
                pl.BlockSpec((D, TILE), by_col),
                pl.BlockSpec(mine.shape, whole5),
                pl.BlockSpec(mine.shape, whole5),
                pl.BlockSpec((D, D), whole),
                pl.BlockSpec((VEC, D), whole),
            ],
            scratch_shapes=[
                pltpu.VMEM((D, FF), BF16),
                pltpu.VMEM((D, FF), BF16),
                pltpu.VMEM((D + 16, FF), F32),
                pltpu.VMEM((D, FF), F32),
                pltpu.VMEM((D, D), F32),
                pltpu.VMEM((VEC, D), F32),
                pltpu.VMEM((TILE, FF), BF16),
                pltpu.VMEM((TILE, FF), BF16),
                pltpu.VMEM((TILE, FF), BF16),
                pltpu.VMEM((TILE, D), BF16),
                pltpu.VMEM((TILE, D), BF16),
                pltpu.VMEM((TILE, D), BF16),
                pltpu.VMEM((SEQ, D), F32),
                pltpu.VMEM((D, D), BF16),
            ],
        ),
        compiler_params=params(dimension_semantics=("arbitrary",)),
        cost_estimate=pl.CostEstimate(
            flops=14_000_000_000, bytes_accessed=15_000_000, transcendentals=4_200_000
        ),
        name="feed_forward",
    )(marks, place, x, back, mixed, mixed_t, proj, mine, other, vector)


def pull_kernel(
    own,
    marks,
    place,
    grad_t_ref,
    query_t_ref,
    value_ref,
    key_t_ref,
    out_t_ref,
    inverse_ref,
    exps_ref,
    qk_t_ref,
    x_t_ref,
    weight_ref,
    proj_ref,
    *refs,
):
    if own:
        resid_ref, other_ref, pulled_ref, grads_ref, sums_ref = refs[:5]
    else:
        pulled_ref, grads_ref, sums_ref = refs[:3]
    dot_s, query_g, key_g, scaled_s, acc, sum_acc, value_s, scaled_t_s, score_s = refs[-9:]
    row = pl.program_id(0)
    begin = marks[row, 3]
    group = place[2] if own else 1 - place[2]

    @pl.when(row == 0)
    def _():
        acc[...] = jnp.zeros_like(acc)
        sum_acc[...] = jnp.zeros_like(sum_acc)

    grad_t = grad_t_ref[...].astype(F32)
    scaled_s[...] = jnp.zeros_like(scaled_s)
    head_of = iota((1, LANES), 1) // HEAD_DIM
    for at_head in range(GROUP):
        heads = slice(at_head * HEAD_DIM, (at_head + 1) * HEAD_DIM)
        part = grad_t[heads, :] * inverse_ref[0, at_head : at_head + 1, :]
        dot_s[at_head : at_head + 1, :] = jnp.sum(part * out_t_ref[heads, :], axis=0, keepdims=True)
        part = part.astype(BF16)
        scaled_t_s[heads, :] = part
        mask = jnp.where(head_of == at_head, 1.0, 0.0).astype(BF16)
        for half in range(2):
            rows = slice(half * HALF, (half + 1) * HALF)
            to = slice(at_head * HALF, (at_head + 1) * HALF)
            value_s[half, to, :] = value_ref[rows, :] * mask
            scaled_s[half, heads, to] = part[:, rows]

    def score_grad_of(item):
        half, at_head, block = item
        at = half * HALF + block * QBLOCK
        cols = slice(at_head * HALF + block * QBLOCK, at_head * HALF + (block + 1) * QBLOCK)
        value = value_s[half, at_head * HALF : (at_head + 1) * HALF, :]
        pull = dot(value, scaled_t_s[:, at : at + QBLOCK])
        pull = (pull - dot_s[at_head : at_head + 1, at : at + QBLOCK]).astype(BF16)
        score_s[half, :, cols] = exps_ref[0, 0, half, :, cols] * pull

    def finish(half, at_head):
        cols = slice(at_head * HALF, (at_head + 1) * HALF)
        rows = slice(half * HALF, (half + 1) * HALF)
        heads = slice(at_head * HEAD_DIM, (at_head + 1) * HEAD_DIM)
        score_grad = score_s[half, :, cols]
        if at_head % 2 == 1:
            cols = slice((at_head - 1) * HALF, (at_head + 1) * HALF)
            value_parts[half] += dot_nt(exps_ref[0, 0, half, :, cols], scaled_s[half, :, cols])
        query_g[heads, rows] = dot(key_t_ref[heads, rows], score_grad)
        key_g[heads, rows] = dot_nt(query_t_ref[heads, rows], score_grad)

    value_parts = [jnp.zeros((HALF, LANES), F32) for _ in range(2)]
    items = [
        (half, at_head, block)
        for half in range(2)
        for at_head in range(GROUP)
        for block in range(HALF // QBLOCK)
    ]
    for i in range(len(items) + 1):
        if i < len(items):
            score_grad_of(items[i])
        if i >= 2 and i % 2 == 0:
            finish(*items[i - 1][:2])
    query_low = query_g[...].astype(BF16)
    key_low = key_g[...].astype(BF16)
    value_low = jnp.concatenate(value_parts, axis=0).astype(BF16)
    ones = jnp.ones((16, SEQ), BF16)
    sum_acc[0:1, :] += dot_nt(ones, query_low)[0:1, :] * SCALE
    sum_acc[1:2, :] += dot(ones, value_low)[0:1, :]
    qk_t = qk_t_ref[...]
    both = dot_nt(qk_t, jnp.concatenate([query_low, key_low], axis=0))
    acc[:, :LANES] += both[:, :LANES] * SCALE
    acc[:, LANES : 2 * LANES] += both[:, LANES:]
    acc[:, 2 * LANES :] += dot(x_t_ref[...], value_low)
    at = [pl.ds(pl.multiple_of(i * D + group * LANES, LANES), LANES) for i in range(3)]
    pulled = dot(weight_ref[:, at[0]], query_low) * SCALE + (
        dot(weight_ref[:, at[1]], key_low) + dot_nt(weight_ref[:, at[2]], value_low)
    )
    if own:
        pulled = (pulled + other_ref[...]).T
        pulled_ref[...] = pltpu.roll(resid_ref[...] + pulled, begin, 0)
    else:
        pulled_ref[...] = pulled

    @pl.when(row == pl.num_programs(0) - 1)
    def _():
        tall = D // VDP
        for d in range(VDP):
            rows = slice(d * tall, (d + 1) * tall)
            for c in range(3):
                grads_ref[d, c] = acc[rows, c * LANES : (c + 1) * LANES].astype(BF16)
            grads_ref[d, 3] = proj_ref[rows, :].astype(BF16)
        sums_ref[...] = sum_acc[...]


def attend_back(own, marks, place, grad_t, query_t, value, key_t, out_t, inverse, exps, qk_t, x_t, weight, proj, *more):
    total = value.shape[0]
    rows = total // SEQ
    pick = (lambda p: p[2]) if own else (lambda p: 1 - p[2])
    by_group = lambda r, m, p: (r, pick(p))
    by_row = lambda r, m, p: (r, 0)
    whole = lambda r, m, p: (0, 0)
    in_specs = [
        pl.BlockSpec((LANES, SEQ), lambda r, m, p: (pick(p), r)),
        pl.BlockSpec((LANES, SEQ), lambda r, m, p: (pick(p), r)),
        pl.BlockSpec((SEQ, LANES), by_group),
        pl.BlockSpec((LANES, SEQ), lambda r, m, p: (pick(p), r)),
        pl.BlockSpec((LANES, SEQ), lambda r, m, p: (pick(p), r)),
        pl.BlockSpec((1, 8, SEQ), lambda r, m, p: (pick(p), 0, r)),
        pl.BlockSpec((1, 1, 2, HALF, GROUP * HALF), lambda r, m, p: (r, pick(p), 0, 0, 0)),
        pl.BlockSpec((D, SEQ), lambda r, m, p: (0, r)),
        pl.BlockSpec((D, SEQ), lambda r, m, p: (0, r)),
        pl.BlockSpec((D, 3 * D), whole),
        pl.BlockSpec((D, LANES), lambda r, m, p: (0, pick(p))),
    ]
    by_col = pl.BlockSpec((D, SEQ), lambda r, m, p: (0, r))
    if own:
        in_specs += [pl.BlockSpec((SEQ, D), by_row), by_col]
    return pl.pallas_call(
        functools.partial(pull_kernel, own),
        out_shape=(
            jax.ShapeDtypeStruct((total, D) if own else (D, total), F32),
            jax.ShapeDtypeStruct((VDP, VCHIP, D // VDP, LANES), BF16),
            jax.ShapeDtypeStruct((8, LANES), F32),
        ),
        grid_spec=pltpu.PrefetchScalarGridSpec(
            num_scalar_prefetch=2,
            grid=(rows,),
            in_specs=in_specs,
            out_specs=[
                pl.BlockSpec((SEQ, D), by_row) if own else by_col,
                pl.BlockSpec((VDP, VCHIP, D // VDP, LANES), lambda r, m, p: (0, 0, 0, 0)),
                pl.BlockSpec((8, LANES), whole),
            ],
            scratch_shapes=[
                pltpu.VMEM((8, SEQ), F32),
                pltpu.VMEM((LANES, SEQ), F32),
                pltpu.VMEM((LANES, SEQ), F32),
                pltpu.VMEM((2, LANES, GROUP * HALF), BF16),
                pltpu.VMEM((D, 3 * LANES), F32),
                pltpu.VMEM((8, LANES), F32),
                pltpu.VMEM((2, GROUP * HALF, LANES), BF16),
                pltpu.VMEM((LANES, SEQ), BF16),
                pltpu.VMEM((2, HALF, GROUP * HALF), BF16),
            ],
        ),
        compiler_params=params(dimension_semantics=("arbitrary",)),
        cost_estimate=pl.CostEstimate(
            flops=18_000_000_000, bytes_accessed=15_000_000, transcendentals=0
        ),
        name="attend_back",
    )(marks, place, grad_t, query_t, value, key_t, out_t, inverse, exps, qk_t, x_t, weight, proj, *more)


def sums_by_group(place, sums_own, sums_other):
    first = place[2] == 0
    return (
        jnp.where(first, sums_own, sums_other),
        jnp.where(first, sums_other, sums_own),
    )


def two_terms(rows):
    high = rows.astype(BF16)
    return jnp.concatenate([high.astype(F32), rows - high.astype(F32)], axis=0)


def column_to_row(columns, rows):
    lane = iota((rows, LANES), 1)
    wide = jnp.zeros((rows, LANES), F32)
    for i, column in enumerate(columns):
        wide = jnp.where(lane == i, column, wide)
    return wide.T[:8, :]


def total_of(array):
    return jnp.sum(jnp.sum(array, axis=0, keepdims=True), axis=1, keepdims=True)


def tail_ffn_kernel(place, ffn_ref, rows_1, rows_2, last_ref, grad_ref, stat_ref):
    lane = iota((1, LANES), 1)
    piece, across = [], []
    for kind in range(2):
        total = ffn_ref[0, kind].astype(F32)
        for at in range(1, VDP * VCHIP):
            total = total + ffn_ref[at, kind].astype(F32)
        grad_ref[kind] = total
        square = total * total + EPS_ONE
        down = jnp.sum(square, axis=0, keepdims=True)
        piece += [down[:, :LANES], down[:, LANES:]]
        across.append(jnp.sum(square, axis=1, keepdims=True))
    across = column_to_row(across, total.shape[0])
    across = jnp.concatenate([across[0:1], across[1:2]], axis=1)
    olds = jnp.zeros((1, LANES), F32)
    for i, ref in enumerate((rows_1, rows_2)):
        olds = jnp.where(lane == i, jnp.sum(ref[...], axis=1, keepdims=True), olds)
    stat_ref[...] = jnp.concatenate([across] + piece + [olds, jnp.zeros((2, LANES), F32)], axis=0)


def tail_send_kernel(
    place, mine_ref, got_ref, vector_ref, own_ref, other_ref, stat_ref, stat_other_ref, send_ref
):
    tall = D // VDP
    low, high = sums_by_group(place, own_ref[...], other_ref[...])
    vector = jnp.concatenate(
        [
            vector_ref[:8, :],
            jnp.concatenate([low[:2], high[:2]], axis=1),
            vector_ref[10:, :],
        ],
        axis=0,
    )
    stat = jnp.concatenate([stat_ref[0:1, :] + stat_other_ref[0:1, :], stat_ref[1:6, :]], axis=0)
    stat = two_terms(stat)
    rows = VEC // VDP
    for d in range(VDP):
        for c in range(VCHIP):
            at = d * VCHIP + c
            both = mine_ref[d, c].astype(F32) + got_ref[d, c].astype(F32)
            send_ref[at, :tall, :] = both.astype(BF16)
            part = vector[d * rows : (d + 1) * rows, c * 64 : (c + 1) * 64]
            part = jnp.concatenate([part, jnp.zeros((rows, LANES - 64), F32)], axis=1)
            send_ref[at, tall:, :] = jnp.concatenate([part, stat], axis=0).astype(BF16)


def tail_reduce_kernel(
    place,
    got_ref,
    ffn_grad_ref,
    attn_ref,
    first_ref,
    second_ref,
    rows_0,
    rows_1,
    rows_2,
    cols_0,
    cols_1,
    cols_2,
    vector_ref,
    moment_ref,
    grad_ref,
    update_1,
    update_2,
    rows_out_1,
    rows_out_2,
    cols_out_1,
    cols_out_2,
    send_ref,
):
    decay = 1.0 - STEP ** (-0.8)
    chip = place[1]
    dp = place[0]
    tall = attn_ref.shape[0]
    rows, width = vector_ref.shape
    pieces = VDP * VCHIP
    lane = iota((1, LANES), 1)
    total = got_ref[0, :tall, :].astype(F32)
    part = got_ref[0, tall:, :].astype(F32)[:rows]
    for at in range(1, pieces):
        total = total + got_ref[at, :tall, :].astype(F32)
        part = part + got_ref[at, tall:, :].astype(F32)[:rows]
    grad_ref[...] = total
    low = total.astype(BF16)

    def stat_of(at):
        both = got_ref[pl.ds(at, 1), tall:, :][0].astype(F32)[rows:]
        return both[:6] + both[6:12]

    every = jnp.zeros((1, LANES), F32)
    olds = jnp.zeros((1, LANES), F32)
    mine = jnp.zeros((1, LANES), F32)
    down = jnp.zeros((6, LANES), F32)
    for d in range(VDP):
        down = down + stat_of(d * VCHIP + chip)
        for c in range(VCHIP):
            stat = stat_of(d * VCHIP + c)
            every = every + stat[0:1]
            if c == 0:
                olds = olds + stat[5:6]
    for c in range(VCHIP):
        mine = mine + stat_of(dp * VCHIP + c)[0:1]
    row_total = tall * VDP
    new_rows, means = [], []
    for i, ref in enumerate((rows_1, rows_2)):
        count = first_ref.shape[1] * 2 * VCHIP
        new_rows.append(decay * ref[...] + (1.0 - decay) * (mine[:, i * tall : (i + 1) * tall] / count))
        old = jnp.sum(jnp.where(lane == i, olds, 0.0), axis=1, keepdims=True)
        fresh = jnp.sum(every[:, i * tall : (i + 1) * tall], axis=1, keepdims=True)
        means.append((decay * old + (1.0 - decay) * (fresh / count)) / row_total)
    tile = jnp.concatenate(new_rows + [jnp.zeros((6, tall), F32)], axis=0)
    rows_out_1[...] = new_rows[0]
    rows_out_2[...] = new_rows[1]
    tile = jnp.concatenate([tile, jnp.zeros((8, LANES - tall), F32)], axis=1)
    turned = jnp.concatenate([tile, jnp.zeros((LANES - 8, LANES), F32)], axis=0).T
    scalars = jnp.zeros((1, LANES), F32)
    for i, (old_ref, out_ref, to) in enumerate(
        ((cols_1, cols_out_1, update_1), (cols_2, cols_out_2, update_2))
    ):
        sums = jnp.concatenate([down[1 + 2 * i : 2 + 2 * i], down[2 + 2 * i : 3 + 2 * i]], axis=1)
        cols = decay * old_ref[...] + (1.0 - decay) * (sums / row_total)
        out_ref[...] = cols
        grad = ffn_grad_ref[i]
        update = grad * lax.rsqrt(turned[:tall, i : i + 1] * cols / means[i])
        to[...] = update
        scalars = jnp.where(lane == 67 + i, total_of(update * update), scalars)
    for i, ref in enumerate((attn_ref, first_ref, second_ref)):
        weight = ref[...]
        scalars = jnp.where(lane == 64 + i, total_of(weight * weight), scalars)
    scalars = jnp.concatenate([rows_0[...], scalars[:, tall:]], axis=1)
    vector = vector_ref[...]
    power = jnp.sum(vector * vector, axis=1, keepdims=True)
    lines = jnp.concatenate(
        [part[:, :64], moment_ref[...], jnp.broadcast_to(power, (rows, LANES - 64 - width))], axis=1
    )
    piece = jnp.concatenate(
        [two_terms(lines), two_terms(jnp.concatenate([cols_0[...], scalars], axis=0))]
        + [jnp.zeros((4, LANES), F32)],
        axis=0,
    ).astype(BF16)
    for at in range(pieces):
        send_ref[at, :tall, :] = low
        send_ref[at, tall:, :] = piece


def tail_apply_kernel(
    place,
    mine_ref,
    other_ref,
    grad_ref,
    update_1,
    update_2,
    weight_0,
    weight_1,
    weight_2,
    rows_0,
    cols_0,
    vector_ref,
    moment_ref,
    new_0,
    new_1,
    new_2,
    rows_out,
    cols_out,
    vector_grad_ref,
    moment_out,
    vector_out,
    sums_s,
    rows_s,
):
    decay = 1.0 - STEP ** (-0.8)
    dp, chip, core = place[0], place[1], place[2]
    tall = weight_0.shape[0]
    rows, width = vector_ref.shape
    fsdp = 2 * VCHIP
    lane = iota((1, LANES), 1)
    refs = (mine_ref, other_ref)
    row_total = float(tall * VDP)
    col_total = float(LANES * fsdp)

    def lines_of(ref, at):
        both = ref[at, tall:, :].astype(F32)
        return both[0:4] + both[4:8], both[8:10] + both[10:12]

    scalars = jnp.zeros((1, LANES), F32)
    for ref in refs:
        for at in range(VDP * VCHIP):
            scalars = scalars + lines_of(ref, at)[1][1:2]
    scalar = lambda at: jnp.sum(jnp.where(lane == at, scalars, 0.0), axis=1, keepdims=True)

    tile, fresh = [], []
    for d in range(VDP):
        wide = jnp.zeros((tall, LANES), F32)
        for ref in refs:
            for c in range(VCHIP):
                block = ref[d * VCHIP + c, :tall, :].astype(F32)
                wide = wide + (block * block + EPS_ONE)
        fresh.append(jnp.sum(wide, axis=1, keepdims=True))
        tile.append(lines_of(mine_ref, d * VCHIP)[1][1:2])
    tile = jnp.concatenate(tile + [jnp.zeros((LANES - VDP, LANES), F32)], axis=0).T
    mean = jnp.zeros((1, 1), F32)
    new_rows = []
    for d in range(VDP):
        new = decay * tile[:tall, d : d + 1] + (1.0 - decay) * (fresh[d] / col_total)
        new_rows.append(1.0 / new)
        mean = mean + jnp.sum(new, axis=0, keepdims=True)
        sums_s[d] = jnp.broadcast_to(fresh[d], (tall, LANES))
    mean = mean / row_total
    mine = sums_s[pl.ds(dp, 1)][0]
    rows_s[...] = mine.T
    rows_new = decay * rows_0[...] + (1.0 - decay) * (rows_s[0:1, :tall] / col_total)
    rows_out[...] = rows_new
    power = jnp.zeros((1, 1), F32)
    for half, ref in enumerate(refs):
        for c in range(VCHIP):
            down = jnp.zeros((tall, LANES), F32)
            weighted = jnp.zeros((tall, LANES), F32)
            for d in range(VDP):
                block = ref[d * VCHIP + c, :tall, :].astype(F32)
                square = block * block
                down = down + (square + EPS_ONE)
                weighted = weighted + square * new_rows[d]
            down = jnp.sum(down, axis=0, keepdims=True)
            old = lines_of(ref, c)[1][0:1]
            cols = decay * old + (1.0 - decay) * (down / row_total)
            weighted = jnp.sum(weighted, axis=0, keepdims=True) / cols
            power = power + jnp.sum(weighted, axis=1, keepdims=True)
            if half == 0:
                sums_s[VDP + c] = jnp.broadcast_to(down, (tall, LANES))
    power = power * mean
    down = sums_s[pl.ds(VDP + chip, 1)][0][0:1, :]
    cols_new = decay * cols_0[...] + (1.0 - decay) * (down / row_total)
    cols_out[...] = cols_new
    column = jnp.concatenate(
        [
            jnp.concatenate([rows_new, jnp.zeros((1, LANES - tall), F32)], axis=1),
            jnp.zeros((LANES - 1, LANES), F32),
        ],
        axis=0,
    ).T[:tall, 0:1]
    update_0 = grad_ref[...] * lax.rsqrt(column * cols_new / mean)
    powers = (power, scalar(67), scalar(68))
    for i, (update, weight, new) in enumerate(
        (
            (update_0, weight_0, new_0),
            (update_1[...], weight_1, new_1),
            (update_2[...], weight_2, new_2),
        )
    ):
        entries = float(weight.shape[0] * weight.shape[1] * VDP * fsdp)
        clip = jnp.maximum(1.0, jnp.sqrt(powers[i] / entries) / CLIP_LIMIT)
        rate = STEP_RATE * jnp.maximum(EPS_TWO, jnp.sqrt(scalar(64 + i) / entries))
        new[...] = weight[...] - rate / clip * update
    powers, sizes = [], []
    for d in range(VDP):
        power = jnp.zeros((rows, 1), F32)
        size = jnp.zeros((rows, 1), F32)
        for c in range(VCHIP):
            at = d * VCHIP + c
            first, second = lines_of(mine_ref, at)[0], lines_of(other_ref, at)[0]
            both = first[:, :64] + second[:, :64]
            size = size + first[:, LANES - 1 :] + second[:, LANES - 1 :]
            near = jnp.where(core == 0, first[:, 64 : 64 + width], second[:, 64 : 64 + width])
            far = jnp.where(core == 0, second[:, 64 : 64 + width], first[:, 64 : 64 + width])
            moment = jnp.concatenate([near, far], axis=1)
            moment = decay * moment + (1.0 - decay) * (both * both + EPS_ONE)
            power = power + jnp.sum(both * both / moment, axis=1, keepdims=True)
            wide = jnp.concatenate([both, jnp.zeros((rows, LANES - 64), F32)], axis=1)
            sums_s[2 * VDP + at, :rows, :] = wide
        powers.append(power)
        sizes.append(size)
    both = sums_s[pl.ds(2 * VDP + dp * VCHIP + chip, 1), :rows, :][0]
    vector_grad = jnp.where(core == 0, both[:, :width], both[:, width : 2 * width])
    vector_grad_ref[...] = vector_grad
    moment = decay * moment_ref[...] + (1.0 - decay) * (vector_grad * vector_grad + EPS_ONE)
    moment_out[...] = moment
    step = vector_grad * lax.rsqrt(moment)
    bias = VDP // 2
    bias_power = sum(jnp.sum(power, axis=0, keepdims=True) for power in powers[:bias])
    bias_size = sum(jnp.sum(size, axis=0, keepdims=True) for size in sizes[:bias])
    power, size = powers[bias], sizes[bias]
    for d in range(bias + 1, VDP):
        power = jnp.where(dp == d, powers[d], power)
        size = jnp.where(dp == d, sizes[d], size)
    is_bias = dp < bias
    power = jnp.where(is_bias, bias_power, power)
    size = jnp.where(is_bias, bias_size, size)
    count = jnp.where(is_bias, float(FF), float(D))
    clip = jnp.maximum(1.0, jnp.sqrt(power / count) / CLIP_LIMIT)
    rate = STEP_RATE * jnp.maximum(EPS_TWO, jnp.sqrt(size / count))
    vector_out[...] = vector_ref[...] - rate / clip * step


def whole_call(kernel, name, place, outs, *operands, scratch=()):
    return pl.pallas_call(
        kernel,
        out_shape=[jax.ShapeDtypeStruct(shape, kind) for shape, kind in outs],
        in_specs=[pl.BlockSpec(memory_space=pltpu.SMEM)] + [vspec()] * len(operands),
        out_specs=[vspec()] * len(outs),
        scratch_shapes=list(scratch),
        compiler_params=params(16),
        name=name,
    )(place, *operands)


def core_swap(block):
    return lax.ppermute(block, "core", [(0, 1), (1, 0)])


def exchange(blocks, axes):
    return lax.all_to_all(blocks, axes, split_axis=0, concat_axis=0, tiled=True)


def after(value, *earlier):
    return pl.pallas_call(
        lambda *refs: None,
        out_shape=jax.ShapeDtypeStruct(value.shape, value.dtype),
        in_specs=[pl.BlockSpec(memory_space=pltpu.HBM)] * (1 + len(earlier)),
        out_specs=pl.BlockSpec(memory_space=pltpu.HBM),
        input_output_aliases={0: 0},
        compiler_params=params(),
        name="after",
    )(value, *earlier)


def pair_kernel(mine_ref, got_ref, out_ref):
    out_ref[...] = (mine_ref[...].astype(F32) + got_ref[...].astype(F32)).astype(BF16)


def pair_sum(mine, got):
    return pl.pallas_call(
        pair_kernel,
        out_shape=jax.ShapeDtypeStruct(mine.shape, BF16),
        in_specs=[vspec(), vspec()],
        out_specs=vspec(),
        compiler_params=params(16),
        name="pair_sum",
    )(mine, got)


CHIPS = ("dp", "chip")
ALL = ("dp", "chip", "core")


def layer(place, weights, segment_ids, tokens, cotangent, ffn_weights, send_core, send_ffn):
    table = jnp.asarray(encode_table())
    qk, x, qk_t, x_t, back, marks = place_tokens(segment_ids, tokens, cotangent, table)
    query_t, value, key_t, out_t, inverse, mixed, mixed_t, exps, weight, proj, vector = attend_forward(
        marks, place, x, qk, x_t, qk_t, *weights(marks)
    )
    ffn_mine, ffn_other = ffn_weights(marks, vector)
    block_out, resid, grad_t, ffn_mine, ffn_other, proj_g, vector_g = feed_forward(
        marks, place, x, back, mixed, mixed_t, proj, ffn_mine, ffn_other, vector
    )
    ffn_got, grad_t = send_ffn(ffn_mine, ffn_other, grad_t)
    shared = (marks, place, grad_t, query_t, value, key_t, out_t, inverse, exps, qk_t, x_t, weight, proj_g)
    pulled, grads_other, sums_other = attend_back(False, *shared)
    attn_got = send_core(grads_other)
    input_grad, grads_own, sums_own = attend_back(True, *shared, resid, pulled)
    return block_out, input_grad, grads_own, grads_other, attn_got, sums_own, sums_other, vector_g, ffn_got


def body(
    tokens,
    cotangent,
    segment_ids,
    attn_weight,
    ffn_in,
    ffn_out,
    vectors,
    attn_rows,
    attn_cols,
    in_rows,
    in_cols,
    out_rows,
    out_cols,
    vector_moment,
):
    place = jnp.stack([lax.axis_index("dp"), lax.axis_index("chip"), lax.axis_index("core")])
    place = place.astype(jnp.int32)
    pieces = VDP * VCHIP
    tall, wide = attn_weight.shape
    rows_v, cols_v = vectors.shape
    split = lambda array: array.reshape((VDP, VCHIP) + array.shape[1:])
    attn_mine = exchange(pack_attn(place, attn_weight, vectors), CHIPS)

    ffn_sent = pack_ffn(ffn_in, ffn_out)

    def attn_weights(marks):
        mine = split(after(attn_mine, marks, ffn_sent))
        return mine, core_swap(mine)

    def ffn_weights(marks, vector):
        got = split(exchange(after(ffn_sent, marks), CHIPS))
        ffn_mine = after(got, vector)
        return ffn_mine, core_swap(ffn_mine)

    def send_ffn(mine, other, grad_t):
        both = pair_sum(mine, core_swap(other))
        got = exchange(both.reshape((pieces,) + mine.shape[2:]), CHIPS)
        return got, after(grad_t, both)

    (
        block_out,
        input_grad,
        grads_own,
        grads_other,
        attn_got,
        sums_own,
        sums_other,
        vector_g,
        ffn_got,
    ) = layer(place, attn_weights, segment_ids, tokens, cotangent, ffn_weights, core_swap, send_ffn)
    lay = lambda stat: stat.reshape(1, -1)
    rows_old = (lay(attn_rows), lay(in_rows), lay(out_rows))
    cols_old = (lay(attn_cols), lay(in_cols), lay(out_cols))
    weights_old = (attn_weight, ffn_in, ffn_out)
    ffn_grad, stat = whole_call(
        tail_ffn_kernel,
        "tail_ffn",
        place,
        [((2,) + ffn_in.shape, F32), ((8, LANES), F32)],
        ffn_got,
        *rows_old[1:],
        sums_own,
    )
    (sent,) = whole_call(
        tail_send_kernel,
        "tail_send",
        place,
        [((pieces, tall + VROWS, LANES), BF16)],
        grads_own,
        attn_got,
        vector_g,
        sums_own,
        sums_other,
        stat,
        core_swap(stat),
    )
    got = exchange(sent, CHIPS)
    attn_grad, update_1, update_2, rows_new_1, rows_new_2, cols_new_1, cols_new_2, sent = whole_call(
        tail_reduce_kernel,
        "tail_reduce",
        place,
        [
            (attn_weight.shape, F32),
            (ffn_in.shape, F32),
            (ffn_out.shape, F32),
            (rows_old[1].shape, F32),
            (rows_old[2].shape, F32),
            (cols_old[1].shape, F32),
            (cols_old[2].shape, F32),
            ((pieces, tall + VROWS, LANES), BF16),
        ],
        got,
        ffn_grad,
        *weights_old,
        *rows_old,
        *cols_old,
        vectors,
        vector_moment,
    )
    mine = exchange(sent, CHIPS)
    attn_new, in_new, out_new, rows_new_0, cols_new_0, vector_grad, moment_new, vectors_new = whole_call(
        tail_apply_kernel,
        "tail_apply",
        place,
        [
            (attn_weight.shape, F32),
            (ffn_in.shape, F32),
            (ffn_out.shape, F32),
            (rows_old[0].shape, F32),
            (cols_old[0].shape, F32),
            (vectors.shape, F32),
            (vectors.shape, F32),
            (vectors.shape, F32),
        ],
        mine,
        core_swap(mine),
        attn_grad,
        update_1,
        update_2,
        *weights_old,
        rows_old[0],
        cols_old[0],
        vectors,
        vector_moment,
        scratch=[
            pltpu.VMEM((2 * VDP + pieces, tall, LANES), F32),
            pltpu.VMEM((LANES, tall), F32),
        ],
    )
    return (
        block_out,
        input_grad,
        attn_grad,
        ffn_grad[0],
        ffn_grad[1],
        vector_grad,
        rows_new_0.reshape(-1),
        cols_new_0.reshape(-1),
        rows_new_1.reshape(-1),
        cols_new_1.reshape(-1),
        rows_new_2.reshape(-1),
        cols_new_2.reshape(-1),
        moment_new,
        attn_new,
        in_new,
        out_new,
        vectors_new,
    )


def gather_all(block):
    shape = (lax.axis_size("dp"), lax.axis_size("chip") * 2)
    count = shape[0] * shape[1]
    got = exchange(jnp.broadcast_to(block[None], (count,) + block.shape), ALL)
    return got.reshape(shape + block.shape)


def unblock(parts):
    dp_count, fsdp_count, rows, cols = parts.shape
    return parts.transpose(0, 2, 1, 3).reshape(dp_count * rows, fsdp_count * cols)


def scatter_sum(full):
    dp_count = lax.axis_size("dp")
    fsdp_count = lax.axis_size("chip") * 2
    rows, cols = full.shape
    by_col = full.astype(BF16).reshape(rows, fsdp_count, cols // fsdp_count).transpose(1, 0, 2)
    got = exchange(by_col, ("chip", "core"))
    part = jnp.sum(got.astype(F32), axis=0).astype(BF16)
    by_row = part.reshape(dp_count, rows // dp_count, cols // fsdp_count)
    return jnp.sum(exchange(by_row, "dp").astype(F32), axis=0)


def body_any(
    tokens,
    cotangent,
    segment_ids,
    attn_weight,
    ffn_in,
    ffn_out,
    vectors,
    attn_rows,
    attn_cols,
    in_rows,
    in_cols,
    out_rows,
    out_cols,
    vector_moment,
):
    dp_count = lax.axis_size("dp")
    fsdp_count = lax.axis_size("chip") * 2
    dp_place = lax.axis_index("dp")
    fsdp_place = lax.axis_index("chip") * 2 + lax.axis_index("core")
    rows_w = attn_weight.shape[0]
    rows_v = vectors.shape[0]
    place = jnp.zeros((3,), jnp.int32)
    full_attn = unblock(gather_all(attn_weight.astype(BF16)))
    full_vector = unblock(gather_all(vectors.astype(BF16)))
    full_ffn = jnp.stack(
        [unblock(gather_all(ffn_in.astype(BF16))), unblock(gather_all(ffn_out.astype(BF16)))]
    )
    tall = D // VDP
    cut = full_attn.reshape(VDP, tall, VCHIP, 2, LANES).transpose(3, 0, 2, 1, 4)
    lines = full_vector.reshape(VDP, VEC // VDP, 2, LANES).transpose(0, 2, 1, 3)
    lines = lines.reshape(VDP, 1, 2 * VEC // VDP, LANES)
    lines = jnp.pad(lines, ((0, 0), (0, VCHIP - 1), (0, VROWS - 2 * VEC // VDP), (0, 0)))
    weights = (
        jnp.concatenate([cut[0], lines], axis=2),
        jnp.concatenate([cut[1], jnp.zeros_like(lines)], axis=2),
    )
    ffn_cut = full_ffn.reshape(2, VDP, tall, VCHIP, 2, FF // (2 * VCHIP))
    ffn_cut = ffn_cut.transpose(4, 1, 3, 0, 2, 5)
    (
        block_out,
        input_grad,
        grads_own,
        grads_other,
        _,
        sums_own,
        sums_other,
        vector_g,
        ffn_got,
    ) = layer(
        place,
        lambda marks: weights,
        segment_ids,
        tokens,
        cotangent,
        lambda marks, vector: (ffn_cut[0], ffn_cut[1]),
        lambda block: block,
        lambda mine, other, grad_t: (jnp.stack([mine, other]), grad_t),
    )
    attn_full = jnp.stack([grads_own, grads_other]).transpose(1, 3, 2, 0, 4).reshape(D, 4 * D)
    ffn_full = ffn_got.transpose(3, 1, 4, 2, 0, 5).reshape(2, D, FF)
    sums = jnp.concatenate([sums_own[:2], sums_other[:2]], axis=1)
    vector_full = jnp.concatenate([vector_g[:8], sums, vector_g[10:]], axis=0)
    attn_grad = scatter_sum(attn_full)
    in_grad = scatter_sum(ffn_full[0])
    out_grad = scatter_sum(ffn_full[1])
    vector_grad = scatter_sum(vector_full)

    decay = 1.0 - STEP ** (-0.8)
    gradients = (attn_grad, in_grad, out_grad)
    weights_old = (attn_weight, ffn_in, ffn_out)
    rows_old = (attn_rows, in_rows, out_rows)
    cols_old = (attn_cols, in_cols, out_cols)
    moment_new = decay * vector_moment + (1.0 - decay) * (vector_grad * vector_grad + EPS_ONE)
    vector_step = vector_grad * lax.rsqrt(moment_new)
    squares = [gradient * gradient + EPS_ONE for gradient in gradients]
    pieces = []
    for square in squares:
        pieces.append(jnp.sum(square, axis=1))
    for square in squares:
        pieces.append(jnp.sum(square, axis=0))
    pieces.append(jnp.sum(vector_step * vector_step, axis=1))
    pieces.append(jnp.sum(vectors * vectors, axis=1))
    pieces.append(jnp.stack([jnp.sum(weight * weight) for weight in weights_old]))
    pieces.append(jnp.stack([jnp.sum(old) for old in rows_old]))
    sizes = [piece.shape[0] for piece in pieces]
    flat = jnp.concatenate(pieces)
    flat = jnp.pad(flat, (0, -flat.shape[0] % 1024)).reshape(-1, LANES)
    got = gather_all(flat).reshape(dp_count, fsdp_count, -1)
    offsets = [0]
    for length in sizes:
        offsets.append(offsets[-1] + length)
    take = lambda i: got[:, :, offsets[i] : offsets[i + 1]]
    rows_new, cols_new, row_means, entries = [], [], [], []
    for i in range(3):
        count_rows = rows_w * dp_count
        count_cols = weights_old[i].shape[1] * fsdp_count
        entries.append(float(count_rows * count_cols))
        row_all = jnp.sum(take(i), axis=1)
        mine = lax.dynamic_index_in_dim(row_all, dp_place, 0, keepdims=False)
        rows_new.append(decay * rows_old[i] + (1.0 - decay) * mine / count_cols)
        col_all = jnp.sum(take(3 + i), axis=0)
        mine = lax.dynamic_index_in_dim(col_all, fsdp_place, 0, keepdims=False)
        cols_new.append(decay * cols_old[i] + (1.0 - decay) * mine / count_rows)
        old_total = jnp.sum(take(9)[:, 0, i])
        row_means.append(
            (decay * old_total + (1.0 - decay) * jnp.sum(row_all) / count_cols) / count_rows
        )
    step_rows = jnp.sum(take(6), axis=1).reshape(-1)
    weight_rows = jnp.sum(take(7), axis=1).reshape(-1)
    weight_totals = jnp.sum(take(8), axis=(0, 1))
    updates = []
    for i in range(3):
        second = rows_new[i][:, None] * cols_new[i][None, :] / row_means[i]
        updates.append(gradients[i] * lax.rsqrt(second))
    flat = jnp.stack([jnp.sum(update * update) for update in updates])
    flat = jnp.broadcast_to(jnp.pad(flat, (0, 5))[:, None], (8, LANES))
    totals = jnp.sum(gather_all(flat)[:, :, :, 0], axis=(0, 1))
    new_weights = []
    for i in range(3):
        clip_factor = jnp.maximum(1.0, jnp.sqrt(totals[i] / entries[i]) / CLIP_LIMIT)
        step_size = STEP_RATE * jnp.maximum(EPS_TWO, jnp.sqrt(weight_totals[i] / entries[i]))
        new_weights.append(weights_old[i] - step_size / clip_factor * updates[i])
    bias_rows = FF // D
    row_places = jnp.arange(VEC)
    counts = jnp.where(row_places < bias_rows, float(FF), float(D))
    grouped_updates = jnp.where(row_places < bias_rows, jnp.sum(step_rows[:bias_rows]), step_rows)
    grouped_weights = jnp.where(row_places < bias_rows, jnp.sum(weight_rows[:bias_rows]), weight_rows)
    clip_rows = jnp.maximum(1.0, jnp.sqrt(grouped_updates / counts) / CLIP_LIMIT)
    step_sizes = STEP_RATE * jnp.maximum(EPS_TWO, jnp.sqrt(grouped_weights / counts))
    factor_rows = lax.dynamic_slice_in_dim(step_sizes / clip_rows, dp_place * rows_v, rows_v)
    vectors_new = vectors - factor_rows[:, None] * vector_step
    return (
        block_out,
        input_grad,
        attn_grad,
        in_grad,
        out_grad,
        vector_grad,
        rows_new[0],
        cols_new[0],
        rows_new[1],
        cols_new[1],
        rows_new[2],
        cols_new[2],
        moment_new,
        new_weights[0],
        new_weights[1],
        new_weights[2],
        vectors_new,
    )


def solution(mesh):
    dp_count, fsdp_count = mesh.shape["dp"], mesh.shape["fsdp"]
    inner = jax.sharding.Mesh(mesh.devices.reshape(dp_count, fsdp_count // 2, 2), ALL)
    fsdp = ("chip", "core")
    split = P(ALL, None)
    block = P("dp", fsdp)
    stats = (P("dp"), P(fsdp)) * 3
    plain = dp_count == VDP and fsdp_count == 2 * VCHIP
    return jax.shard_map(
        body if plain else body_any,
        mesh=inner,
        in_specs=(split,) * 3 + (block,) * 4 + stats + (block,),
        out_specs=(split,) * 2 + (block,) * 4 + stats + (block,) * 5,
        check_vma=False,
    )
```

```python
import functools
import math

import jax
import jax.numpy as jnp
import numpy as np
from jax import lax
from jax.experimental import pallas as pl
from jax.experimental.pallas import tpu as pltpu
from jax.sharding import PartitionSpec as P

D = 256
FF = 2048
HEADS = 8
HEAD_DIM = 32
SEQ = 1024
HALF = 512
GROUP = 4
LANES = 128
QBLOCK = 256
WGRID = 32
STEP = 10
VEC = 16
TILE = 1024
CHUNK = 256
SUB = 512
LEAD = 5
STRIP = 64
VDP = 4
VCHIP = 4
VROWS = 16

EPS_NORM = 1e-05
EPS_ONE = 1e-30
EPS_TWO = 0.001
CLIP_LIMIT = 1.0
STEP_RATE = 0.3
FAR = 1e30
TAME = 40.0
LOG2_E = math.log2(math.e)
SCALE = HEAD_DIM ** (-0.5)
GELU_A = math.sqrt(2.0 / math.pi)
GELU_B = 0.044715
F32 = jnp.float32
BF16 = jnp.bfloat16
MIB = 1024 * 1024


def dot(left, right):
    return jnp.dot(left, right, preferred_element_type=F32)


def dot_nt(left, right):
    return lax.dot_general(left, right, (((1,), (1,)), ((), ())), preferred_element_type=F32)


def encode_table():
    half = D // 2
    feature = np.arange(half)
    freq = np.exp(
        (2 * (feature // 2)).astype(np.float32) * np.float32(-math.log(10000.0) / half)
    ).astype(np.float32)
    angles = np.arange(1, WGRID + 1, dtype=np.float32)[:, None] * freq[None, :]
    table = np.where(feature % 2 == 0, np.sin(angles), np.cos(angles)).astype(np.float32)
    low = jnp.bfloat16
    one = table.astype(low)
    rest = table - one.astype(np.float32)
    two = rest.astype(low)
    three = (rest - two.astype(np.float32)).astype(low)
    blank = np.zeros((LANES - 3 * WGRID, half), low)
    return np.concatenate([one, two, three, blank], axis=0)


def iota(shape, dim):
    return lax.broadcasted_iota(jnp.int32, shape, dim)


def norm_forward(rows):
    centered = rows - jnp.mean(rows, axis=-1, keepdims=True)
    inverse = lax.rsqrt(jnp.mean(centered * centered, axis=-1, keepdims=True) + EPS_NORM)
    return centered * inverse, inverse


def norm_backward(upstream, normed, inverse):
    return inverse * (
        upstream
        - jnp.mean(upstream, axis=-1, keepdims=True)
        - normed * jnp.mean(upstream * normed, axis=-1, keepdims=True)
    )

def vspec():
    return pl.BlockSpec(memory_space=pltpu.VMEM)


def params(mib=56, **more):
    return pltpu.CompilerParams(vmem_limit_bytes=mib * MIB, **more)


def pack_kernel(place, attn_ref, vector_ref, out_ref):
    owner = place[1] * 2 + place[2]
    vector = vector_ref[...]
    rows = vector.shape[0]
    wide = jnp.concatenate([vector] * (LANES // vector.shape[1]), axis=1)
    slot = iota((rows, LANES), 1) // vector.shape[1]
    per = LANES // vector.shape[1]
    parts = [attn_ref[...]]
    for half in range(2):
        parts.append(jnp.where(slot + half * per == owner, wide, 0.0))
    parts.append(jnp.zeros((VROWS - 2 * rows, LANES), F32))
    piece = jnp.concatenate(parts, axis=0).astype(BF16)
    for at in range(VDP * VCHIP):
        out_ref[at] = piece


def pack_attn(place, attn_weight, vectors):
    return pl.pallas_call(
        pack_kernel,
        out_shape=jax.ShapeDtypeStruct((VDP * VCHIP, attn_weight.shape[0] + VROWS, LANES), BF16),
        in_specs=[pl.BlockSpec(memory_space=pltpu.SMEM), vspec(), vspec()],
        out_specs=vspec(),
        compiler_params=params(),
        name="pack_attn",
    )(place, attn_weight, vectors)


def pack_ffn_kernel(place, first_ref, second_ref, *refs):
    out_ref = refs[-1]
    first = first_ref[...].astype(BF16)
    second = second_ref[...].astype(BF16)
    for at in range(VCHIP):
        out_ref[at, pl.ds(place[0], 1), 0] = first[None]
        out_ref[at, pl.ds(place[0], 1), 1] = second[None]
        for step in range(1, VDP):
            out_ref[at, pl.ds(place[0] ^ step, 1)] = refs[step - 1][...][None]


def pack_ffn(place, ffn_in, ffn_out, parts):
    return pl.pallas_call(
        pack_ffn_kernel,
        out_shape=jax.ShapeDtypeStruct((VCHIP, VDP, 2) + ffn_in.shape, BF16),
        in_specs=[pl.BlockSpec(memory_space=pltpu.SMEM)] + [vspec()] * (2 + len(parts)),
        out_specs=vspec(),
        compiler_params=params(),
        name="pack_ffn",
    )(place, ffn_in, ffn_out, *parts)


def place_kernel(
    segment_ref, tokens_ref, back_ref, table_ref, qk_ref, x_ref, qk_t_ref, x_t_ref, turned_ref, marks_ref
):
    row = pl.program_id(0)
    starts = []
    for number in range(1, 4):
        at = jnp.int32(0)
        for step in (512, 256, 128, 64, 32, 16, 8, 4, 2, 1, 1):
            probe = jnp.minimum(at + (step - 1), SEQ - 1)
            at = jnp.where(segment_ref[row, probe] < number, at + step, at)
        starts.append(at)
    edges = [jnp.int32(0)] + starts + [jnp.int32(SEQ)]
    begin = jnp.int32(0)
    for number in range(3, -1, -1):
        begin = jnp.where(edges[number + 1] - edges[number] == HALF, edges[number], begin)
    for number in range(3):
        marks_ref[row, number] = starts[number]
    marks_ref[row, 3] = begin
    one, two, three = starts
    x = pltpu.roll(tokens_ref[...].astype(F32), (SEQ - begin) & (SEQ - 1), 0)
    x_ref[...] = x.astype(BF16)
    x_t_ref[...] = x.T.astype(BF16)
    back = back_ref[...].astype(F32)
    turned_ref[...] = pltpu.roll(back, (SEQ - begin) & (SEQ - 1), 0).astype(BF16)
    at = (iota((SEQ, LANES), 0) + begin) & (SEQ - 1)
    lane = iota((SEQ, LANES), 1)
    start = jnp.where(at >= three, three, jnp.where(at >= two, two, jnp.where(at >= one, one, 0)))
    local = at - start
    kept = lane < 3 * WGRID
    slot = lane & (WGRID - 1)
    hot_r = jnp.where(((local >> 5) == slot) & kept, 1.0, 0.0).astype(BF16)
    hot_c = jnp.where(((local & (WGRID - 1)) == slot) & kept, 1.0, 0.0).astype(BF16)
    table = table_ref[...]
    places = jnp.concatenate([dot(hot_r, table), dot(hot_c, table)], axis=1)
    qk = x + places
    qk_ref[...] = qk.astype(BF16)
    qk_t_ref[...] = qk.T.astype(BF16)


def place_tokens(segment_ids, tokens, cotangent, table):
    rows = segment_ids.shape[0]
    by_row = lambda r: (r, 0)
    return pl.pallas_call(
        place_kernel,
        out_shape=(
            jax.ShapeDtypeStruct(tokens.shape, BF16),
            jax.ShapeDtypeStruct(tokens.shape, BF16),
            jax.ShapeDtypeStruct((D, tokens.shape[0]), BF16),
            jax.ShapeDtypeStruct((D, tokens.shape[0]), BF16),
            jax.ShapeDtypeStruct(tokens.shape, BF16),
            jax.ShapeDtypeStruct((rows, 4), jnp.int32),
        ),
        grid=(rows,),
        in_specs=[
            pl.BlockSpec(memory_space=pltpu.SMEM),
            pl.BlockSpec((SEQ, D), by_row),
            pl.BlockSpec((SEQ, D), by_row),
            pl.BlockSpec((LANES, LANES), lambda r: (0, 0)),
        ],
        out_specs=(
            pl.BlockSpec((SEQ, D), by_row),
            pl.BlockSpec((SEQ, D), by_row),
            pl.BlockSpec((D, SEQ), lambda r: (0, r)),
            pl.BlockSpec((D, SEQ), lambda r: (0, r)),
            pl.BlockSpec((SEQ, D), by_row),
            pl.BlockSpec(memory_space=pltpu.SMEM),
        ),
        compiler_params=params(dimension_semantics=("arbitrary",)),
        cost_estimate=pl.CostEstimate(flops=600_000_000, bytes_accessed=4_000_000, transcendentals=0),
        name="place_tokens",
    )(segment_ids, tokens, cotangent, table)


def attend_kernel(
    marks,
    place,
    x_ref,
    qk_ref,
    x_t_ref,
    qk_t_ref,
    mine_ref,
    other_ref,
    query_t_ref,
    value_ref,
    key_t_ref,
    out_t_ref,
    inverse_ref,
    mixed_ref,
    mixed_t_ref,
    exps_ref,
    weight_ref,
    proj_ref,
    vector_ref,
    key_s,
    value_s,
    mark_k,
    mark_q,
    first_s,
    second_s,
    weight_t_s,
    bias_s,
    tame_s,
):
    row = pl.program_id(0)
    group = pl.program_id(1)
    begin = marks[row, 3]
    core = place[2]

    @pl.when((row == 0) & (group == 0))
    def _():
        tall = D // VDP
        for d in range(VDP):
            rows = slice(d * tall, (d + 1) * tall)
            total = jnp.zeros((8, LANES), F32)
            for c in range(VCHIP):
                for ref, half in ((mine_ref, core), (other_ref, 1 - core)):
                    if c < 3:
                        to = pl.ds(pl.multiple_of(c * D + half * LANES, LANES), LANES)
                        weight_ref[rows, to] = ref[d, c, :tall, :]
                    else:
                        to = pl.ds(pl.multiple_of(half * LANES, LANES), LANES)
                        proj_ref[rows, to] = ref[d, c, :tall, :]
                    total += ref[d, c, tall:, :].astype(F32)[:8]
            vector_ref[d * 4 : (d + 1) * 4, :LANES] = total[:4]
            vector_ref[d * 4 : (d + 1) * 4, LANES:] = total[4:]
        weight_t_s[...] = weight_ref[...].astype(F32).T.astype(BF16)
        bias_s[...] = vector_ref[8:16, :].T

    @pl.when(group == 0)
    def _():
        qk_t = qk_t_ref[...]
        query_t = (dot(weight_t_s[:D, :], qk_t) + bias_s[:, 0:1]) * SCALE
        query_t = query_t.astype(BF16)
        query_t_ref[...] = query_t
        key_t = dot(weight_t_s[D : 2 * D, :], qk_t).astype(BF16)
        key_t_ref[...] = key_t

        def largest_norms(rows):
            rows = rows.astype(F32)
            rows = rows * rows
            sums = [
                jnp.sum(rows[head * HEAD_DIM : (head + 1) * HEAD_DIM], axis=0, keepdims=True)
                for head in range(HEADS)
            ]
            return jnp.max(jnp.concatenate(sums, axis=0), axis=1, keepdims=True)

        bound = jnp.max(largest_norms(query_t) * largest_norms(key_t))
        tame_s[0] = jnp.where(bound <= TAME * TAME, 1, 0)
        key_s[...] = dot(qk_ref[...], weight_ref[:, D : 2 * D]).astype(BF16)
        value = dot(x_ref[...], weight_ref[:, 2 * D : 3 * D]) + vector_ref[9:10, :]
        value_ref[...] = value.astype(BF16)
        value_t = dot(weight_t_s[2 * D :, :], x_t_ref[...]) + bias_s[:, 1:2]
        value_t = value_t.astype(BF16)
        for head in range(HEADS):
            value_s[head, :HEAD_DIM, :] = value_t[head * HEAD_DIM : (head + 1) * HEAD_DIM, :]
            value_s[head, HEAD_DIM:, :] = jnp.ones((16, SEQ), BF16)
        one, two, three = marks[row, 0], marks[row, 1], marks[row, 2]

        def number_of(shape, dim):
            here = (iota(shape, dim) + (HALF + begin)) & (SEQ - 1)
            return (
                jnp.where(here >= one, 1, 0)
                + jnp.where(here >= two, 1, 0)
                + jnp.where(here >= three, 1, 0)
            )

        lane = iota((HALF, LANES), 1)
        number = number_of((HALF, LANES), 0)
        mark_k[...] = jnp.where((number != lane) & (lane < 4), -FAR, 0.0).astype(BF16)
        number = number_of((LANES, HALF), 1)
        mark_q[...] = jnp.where(number == iota((LANES, HALF), 0), 1.0, 0.0).astype(BF16)

    lanes = pl.ds(pl.multiple_of(group * LANES, LANES), LANES)
    head_of = iota((1, LANES), 1) // HEAD_DIM
    keys_here = key_s[:, lanes]
    for at_head in range(GROUP):
        mask = jnp.where(head_of == at_head, 1.0, 0.0).astype(BF16)
        rows = slice(at_head * HALF, (at_head + 1) * HALF)
        first_s[rows, :] = keys_here[:HALF] * mask
        second_s[rows, :LANES] = keys_here[HALF:] * mask
        second_s[rows, LANES:] = mark_k[...]

    def scores_of(half, block, rows):
        at = half * HALF + block * QBLOCK
        query = query_t_ref[lanes, at : at + QBLOCK]
        if half == 0:
            return dot(first_s[rows, :], query)
        marks_here = mark_q[:, block * QBLOCK : (block + 1) * QBLOCK]
        return dot(second_s[rows, :], jnp.concatenate([query, marks_here], axis=0))

    def place_of(at_head, block):
        at = at_head * HALF + block * QBLOCK
        return slice(at, at + QBLOCK)

    def exps_plain(half, block):
        scores = scores_of(half, block, slice(0, GROUP * HALF))
        for at_head in range(GROUP):
            exps = jnp.exp2(scores[at_head * HALF : (at_head + 1) * HALF, :] * LOG2_E)
            exps_ref[0, 0, half, :, place_of(at_head, block)] = exps.astype(BF16)

    def exps_shifted(half, block):
        for at_head in range(GROUP):
            rows = slice(at_head * HALF, (at_head + 1) * HALF)
            largest = jnp.max(scores_of(half, block, rows), axis=0, keepdims=True)
            exps = jnp.exp2((scores_of(half, block, rows) - largest) * LOG2_E)
            exps_ref[0, 0, half, :, place_of(at_head, block)] = exps.astype(BF16)

    def finish(half, block):
        at = half * HALF + block * QBLOCK
        rows = slice(half * HALF, (half + 1) * HALF)
        for at_head in range(GROUP):
            out = dot(
                value_s[group * GROUP + at_head, :, rows],
                exps_ref[0, 0, half, :, place_of(at_head, block)],
            )
            inverse = 1.0 / out[HEAD_DIM : HEAD_DIM + 1, :]
            inverse_ref[0, at_head : at_head + 1, at : at + QBLOCK] = inverse
            out_t_ref[at_head * HEAD_DIM : (at_head + 1) * HEAD_DIM, at : at + QBLOCK] = (
                out[:HEAD_DIM, :] * inverse
            )

    def run(exps_of):
        items = [(half, block) for half in range(2) for block in range(HALF // QBLOCK)]
        for i in range(len(items) + 1):
            if i < len(items):
                exps_of(*items[i])
            if i >= 1:
                finish(*items[i - 1])

    @pl.when(tame_s[0] == 1)
    def _():
        run(exps_plain)

    @pl.when(tame_s[0] == 0)
    def _():
        run(exps_shifted)

    out_t = out_t_ref[...]
    mixed_t_ref[...] = out_t.astype(BF16)
    mixed_ref[...] = out_t.T.astype(BF16)


def attend_forward(marks, place, x, qk, x_t, qk_t, mine, other):
    total = x.shape[0]
    rows = total // SEQ
    by_row = lambda r, g, m, p: (r, 0)
    by_col = lambda r, g, m, p: (0, r)
    by_both = lambda r, g, m, p: (g, r)
    whole = lambda r, g, m, p: (0, 0)
    return pl.pallas_call(
        attend_kernel,
        out_shape=(
            jax.ShapeDtypeStruct((D, total), BF16),
            jax.ShapeDtypeStruct((total, D), BF16),
            jax.ShapeDtypeStruct((D, total), BF16),
            jax.ShapeDtypeStruct((D, total), F32),
            jax.ShapeDtypeStruct((2, 8, total), F32),
            jax.ShapeDtypeStruct((total, D), BF16),
            jax.ShapeDtypeStruct((D, total), BF16),
            jax.ShapeDtypeStruct((rows, 2, 2, HALF, GROUP * HALF), BF16),
            jax.ShapeDtypeStruct((D, 3 * D), BF16),
            jax.ShapeDtypeStruct((D, D), BF16),
            jax.ShapeDtypeStruct((VEC, D), F32),
        ),
        grid_spec=pltpu.PrefetchScalarGridSpec(
            num_scalar_prefetch=2,
            grid=(rows, 2),
            in_specs=[
                pl.BlockSpec((SEQ, D), by_row),
                pl.BlockSpec((SEQ, D), by_row),
                pl.BlockSpec((D, SEQ), by_col),
                pl.BlockSpec((D, SEQ), by_col),
                vspec(),
                vspec(),
            ],
            out_specs=[
                pl.BlockSpec((D, SEQ), by_col),
                pl.BlockSpec((SEQ, D), by_row),
                pl.BlockSpec((D, SEQ), by_col),
                pl.BlockSpec((LANES, SEQ), by_both),
                pl.BlockSpec((1, 8, SEQ), lambda r, g, m, p: (g, 0, r)),
                pl.BlockSpec((SEQ, LANES), lambda r, g, m, p: (r, g)),
                pl.BlockSpec((LANES, SEQ), by_both),
                pl.BlockSpec((1, 1, 2, HALF, GROUP * HALF), lambda r, g, m, p: (r, g, 0, 0, 0)),
                pl.BlockSpec((D, 3 * D), whole),
                pl.BlockSpec((D, D), whole),
                pl.BlockSpec((VEC, D), whole),
            ],
            scratch_shapes=[
                pltpu.VMEM((SEQ, D), BF16),
                pltpu.VMEM((HEADS, HEAD_DIM + 16, SEQ), BF16),
                pltpu.VMEM((HALF, LANES), BF16),
                pltpu.VMEM((LANES, HALF), BF16),
                pltpu.VMEM((GROUP * HALF, LANES), BF16),
                pltpu.VMEM((GROUP * HALF, 2 * LANES), BF16),
                pltpu.VMEM((3 * D, D), BF16),
                pltpu.VMEM((D, 8), F32),
                pltpu.SMEM((1,), jnp.int32),
            ],
        ),
        compiler_params=params(dimension_semantics=("arbitrary", "arbitrary")),
        cost_estimate=pl.CostEstimate(
            flops=20_000_000_000, bytes_accessed=30_000_000, transcendentals=8_400_000
        ),
        name="attend_forward",
    )(marks, place, x, qk, x_t, qk_t, mine, other)


def feed_kernel(
    marks,
    place,
    x_ref,
    back_ref,
    mixed_ref,
    mixed_t_ref,
    proj_ref,
    mine_ref,
    other_ref,
    vector_ref,
    block_ref,
    resid_ref,
    mixed_grad_ref,
    mine_out,
    other_out,
    proj_out,
    vector_out,
    first_w,
    second_w,
    first_acc,
    second_acc,
    proj_acc,
    vector_acc,
    hidden_s,
    slope_s,
    pre_s,
    first_low_s,
    branch_low_s,
    attended_s,
    block_s,
    eye_s,
):
    step = pl.program_id(0)
    core = place[2]
    tall = D // VDP
    wide = FF // (2 * VCHIP)

    @pl.when(step == 0)
    def _():
        first_acc[...] = jnp.zeros_like(first_acc)
        second_acc[...] = jnp.zeros_like(second_acc)
        proj_acc[...] = jnp.zeros_like(proj_acc)
        vector_acc[...] = jnp.zeros_like(vector_acc)
        eye_s[...] = jnp.where(iota((D, D), 0) == iota((D, D), 1), 1.0, 0.0).astype(BF16)
        for d in range(VDP):
            rows = slice(d * tall, (d + 1) * tall)
            for c in range(VCHIP):
                for ref, half in ((mine_ref, core), (other_ref, 1 - core)):
                    to = pl.ds(pl.multiple_of((2 * c + half) * wide, wide), wide)
                    first_w[rows, to] = ref[c, d, 0]
                    second_w[rows, to] = ref[c, d, 1]

    bias_o, bias_2 = vector_ref[10:11, :], vector_ref[11:12, :]
    gain_1, shift_1 = vector_ref[12:13, :], vector_ref[13:14, :]
    gain_2, shift_2 = vector_ref[14:15, :], vector_ref[15:16, :]
    at_row = pl.multiple_of((step % (SEQ // TILE)) * TILE, TILE)
    chunks = FF // CHUNK
    pair = 2

    def columns(at, count=1):
        return slice(at * CHUNK, (at + count) * CHUNK)

    def hidden_of(rows, at, pre):
        pre = (pre + vector_ref[at : at + 1, :]).astype(BF16)
        cube = BF16(GELU_A * GELU_B) * (pre * pre)
        gate = BF16(0.5) + BF16(0.5) * jnp.tanh(pre * (cube + BF16(GELU_A)))
        hidden_s[rows, columns(at)] = pre * gate
        slope_s[rows, columns(at)] = gate + (gate - gate * gate) * (
            pre * (BF16(6.0) * cube + BF16(2.0 * GELU_A))
        )

    def stages(sub):
        rows_at = sub * SUB
        rows = slice(rows_at, rows_at + SUB)
        attended = dot(mixed_ref[rows, :], proj_ref[...]) + bias_o
        norm_1, inverse_1 = norm_forward(x_ref[rows, :].astype(F32) + attended)
        first = norm_1 * gain_1 + shift_1
        first_low = first.astype(BF16)
        first_low_s[rows, :] = first_low
        yield
        branch = jnp.zeros((SUB, D), F32)
        for i in range(chunks + 1):
            if i < chunks:
                hidden_of(rows, i, dot(first_low, first_w[:, columns(i)]))
            if i >= pair and i % pair == 0:
                cols = columns(i - pair, pair)
                branch += dot_nt(hidden_s[rows, cols], second_w[:, cols])
            yield
        norm_2, inverse_2 = norm_forward(first + (branch + bias_2))
        block_s[pl.ds(at_row + rows_at, SUB), :] = norm_2 * gain_2 + shift_2
        back = back_ref[rows, :].astype(F32)
        vector_acc[14:15, :] += jnp.sum(back * norm_2, axis=0, keepdims=True)
        vector_acc[15:16, :] += jnp.sum(back, axis=0, keepdims=True)
        resid_2 = norm_backward(back * gain_2, norm_2, inverse_2)
        branch_low = resid_2.astype(BF16)
        branch_low_s[rows, :] = branch_low
        vector_acc[11:12, :] += jnp.sum(branch_low.astype(F32), axis=0, keepdims=True)
        yield
        first_back = resid_2
        if sub == 1:
            branch_t = dot_nt(eye_s[...], branch_low_s[...]).astype(BF16)
            first_t = dot_nt(eye_s[...], first_low_s[...]).astype(BF16)
            first_t = jnp.concatenate([first_t, jnp.ones((16, TILE), BF16)], axis=0)
        for i in range(chunks + 1):
            if i < chunks:
                pull = dot(branch_low, second_w[:, columns(i)]).astype(BF16)
                pre_s[rows, columns(i)] = pull * slope_s[rows, columns(i)]
                if sub == 1:
                    second_acc[:, columns(i)] += dot(branch_t, hidden_s[:, columns(i)])
            if i >= 1 and sub == 1:
                cols = columns(i - 1)
                first_acc[:, cols] += dot(first_t, pre_s[:, cols])
            if i >= pair and i % pair == 0:
                cols = columns(i - pair, pair)
                first_back += dot_nt(pre_s[rows, cols], first_w[:, cols])
            yield
        vector_acc[12:13, :] += jnp.sum(first_back * norm_1, axis=0, keepdims=True)
        vector_acc[13:14, :] += jnp.sum(first_back, axis=0, keepdims=True)
        resid_1 = norm_backward(first_back * gain_1, norm_1, inverse_1)
        resid_ref[rows, :] = resid_1
        attended_low = resid_1.astype(BF16)
        attended_s[rows, :] = attended_low
        vector_acc[10:11, :] += jnp.sum(attended_low.astype(F32), axis=0, keepdims=True)
        mixed_grad_ref[:, rows] = dot_nt(proj_ref[...], attended_low).astype(BF16)
        yield

    ahead, behind = stages(0), stages(1)
    for _ in range(LEAD):
        next(ahead)
    running = [ahead, behind]
    while running:
        for program in list(running):
            if next(program, 0) == 0:
                running.remove(program)
    proj_acc[...] += dot(mixed_t_ref[...], attended_s[...])

    @pl.when(step % (SEQ // TILE) == SEQ // TILE - 1)
    def _():
        block_ref[...] = pltpu.roll(block_s[...], marks[step // (SEQ // TILE), 3], 0)

    @pl.when(step == pl.num_programs(0) - 1)
    def _():
        for d in range(VDP):
            rows = slice(d * tall, (d + 1) * tall)
            for c in range(VCHIP):
                for ref, half in ((mine_out, core), (other_out, 1 - core)):
                    to = pl.ds(pl.multiple_of((2 * c + half) * wide, wide), wide)
                    ref[d, c, 0] = first_acc[rows, to].astype(BF16)
                    ref[d, c, 1] = second_acc[rows, to].astype(BF16)
        proj_out[...] = proj_acc[...]
        for at in range(FF // D):
            vector_out[at : at + 1, :] = first_acc[D : D + 1, at * D : (at + 1) * D]
        vector_out[FF // D :, :] = vector_acc[FF // D :, :]


def feed_forward(marks, place, x, back, mixed, mixed_t, proj, mine, other, vector):
    total = x.shape[0]
    tile = lambda i, m, p: (i, 0)
    by_col = lambda i, m, p: (0, i)
    whole = lambda i, m, p: (0, 0)
    whole5 = lambda i, m, p: (0, 0, 0, 0, 0)
    return pl.pallas_call(
        feed_kernel,
        out_shape=(
            jax.ShapeDtypeStruct((total, D), F32),
            jax.ShapeDtypeStruct((total, D), F32),
            jax.ShapeDtypeStruct((D, total), BF16),
            jax.ShapeDtypeStruct(mine.shape, BF16),
            jax.ShapeDtypeStruct(mine.shape, BF16),
            jax.ShapeDtypeStruct((D, D), F32),
            jax.ShapeDtypeStruct((VEC, D), F32),
        ),
        grid_spec=pltpu.PrefetchScalarGridSpec(
            num_scalar_prefetch=2,
            grid=(total // TILE,),
            in_specs=[
                pl.BlockSpec((TILE, D), tile),
                pl.BlockSpec((TILE, D), tile),
                pl.BlockSpec((TILE, D), tile),
                pl.BlockSpec((D, TILE), by_col),
                pl.BlockSpec((D, D), whole),
                vspec(),
                vspec(),
                pl.BlockSpec((VEC, D), whole),
            ],
            out_specs=[
                pl.BlockSpec((SEQ, D), lambda i, m, p: (i // (SEQ // TILE), 0)),
                pl.BlockSpec((TILE, D), tile),
                pl.BlockSpec((D, TILE), by_col),
                pl.BlockSpec(mine.shape, whole5),
                pl.BlockSpec(mine.shape, whole5),
                pl.BlockSpec((D, D), whole),
                pl.BlockSpec((VEC, D), whole),
            ],
            scratch_shapes=[
                pltpu.VMEM((D, FF), BF16),
                pltpu.VMEM((D, FF), BF16),
                pltpu.VMEM((D + 16, FF), F32),
                pltpu.VMEM((D, FF), F32),
                pltpu.VMEM((D, D), F32),
                pltpu.VMEM((VEC, D), F32),
                pltpu.VMEM((TILE, FF), BF16),
                pltpu.VMEM((TILE, FF), BF16),
                pltpu.VMEM((TILE, FF), BF16),
                pltpu.VMEM((TILE, D), BF16),
                pltpu.VMEM((TILE, D), BF16),
                pltpu.VMEM((TILE, D), BF16),
                pltpu.VMEM((SEQ, D), F32),
                pltpu.VMEM((D, D), BF16),
            ],
        ),
        compiler_params=params(dimension_semantics=("arbitrary",)),
        cost_estimate=pl.CostEstimate(
            flops=14_000_000_000, bytes_accessed=15_000_000, transcendentals=4_200_000
        ),
        name="feed_forward",
    )(marks, place, x, back, mixed, mixed_t, proj, mine, other, vector)


def pull_kernel(
    own,
    marks,
    place,
    grad_t_ref,
    query_t_ref,
    value_ref,
    key_t_ref,
    out_t_ref,
    inverse_ref,
    exps_ref,
    qk_t_ref,
    x_t_ref,
    weight_ref,
    proj_ref,
    *refs,
):
    if own:
        resid_ref, other_ref, pulled_ref, grads_ref, sums_ref = refs[:5]
    else:
        pulled_ref, grads_ref, sums_ref = refs[:3]
    dot_s, query_g, key_g, value_g, acc, sum_acc, value_s, scaled_t_s, score_s = refs[-9:]
    row = pl.program_id(0)
    begin = marks[row, 3]
    group = place[2] if own else 1 - place[2]

    @pl.when(row == 0)
    def _():
        acc[...] = jnp.zeros_like(acc)
        sum_acc[...] = jnp.zeros_like(sum_acc)

    grad_t = grad_t_ref[...].astype(F32)
    head_of = iota((1, LANES), 1) // HEAD_DIM
    for at_head in range(GROUP):
        heads = slice(at_head * HEAD_DIM, (at_head + 1) * HEAD_DIM)
        part = grad_t[heads, :] * inverse_ref[0, at_head : at_head + 1, :]
        dot_s[at_head : at_head + 1, :] = jnp.sum(part * out_t_ref[heads, :], axis=0, keepdims=True)
        part = part.astype(BF16)
        scaled_t_s[heads, :] = part
        mask = jnp.where(head_of == at_head, 1.0, 0.0).astype(BF16)
        for half in range(2):
            rows = slice(half * HALF, (half + 1) * HALF)
            to = slice(at_head * HALF, (at_head + 1) * HALF)
            value_s[half, to, :] = value_ref[rows, :] * mask

    def score_grads_of(half, block):
        at = half * HALF + block * QBLOCK
        pulls = dot(value_s[half], scaled_t_s[:, at : at + QBLOCK])
        for at_head in range(GROUP):
            cols = slice(at_head * HALF + block * QBLOCK, at_head * HALF + (block + 1) * QBLOCK)
            pull = pulls[at_head * HALF : (at_head + 1) * HALF, :]
            pull = (pull - dot_s[at_head : at_head + 1, at : at + QBLOCK]).astype(BF16)
            score_s[half, :, cols] = exps_ref[0, 0, half, :, cols] * pull

    def finish(half, at_head):
        cols = slice(at_head * HALF, (at_head + 1) * HALF)
        rows = slice(half * HALF, (half + 1) * HALF)
        heads = slice(at_head * HEAD_DIM, (at_head + 1) * HEAD_DIM)
        score_grad = score_s[half, :, cols]
        value_g[heads, rows] = dot_nt(scaled_t_s[heads, rows], exps_ref[0, 0, half, :, cols])
        query_g[heads, rows] = dot(key_t_ref[heads, rows], score_grad)
        key_g[heads, rows] = dot_nt(query_t_ref[heads, rows], score_grad)

    score_grads_of(0, 0)
    score_grads_of(0, 1)
    for block in range(HALF // QBLOCK):
        score_grads_of(1, block)
        for at_head in range(2 * block, 2 * block + 2):
            finish(0, at_head)
    for at_head in range(GROUP):
        finish(1, at_head)
    query_low = query_g[...].astype(BF16)
    both_low = jnp.concatenate([key_g[...].astype(BF16), value_g[...].astype(BF16)], axis=0)
    ones = jnp.ones((16, SEQ), BF16)
    sum_acc[0:1, :] += dot_nt(ones, query_low)[0:1, :] * SCALE
    sum_acc[1:2, :] += dot_nt(ones, both_low[LANES:, :])[0:1, :]
    qk_t = qk_t_ref[...]
    both = dot_nt(qk_t, jnp.concatenate([query_low, both_low[:LANES, :]], axis=0))
    acc[:, :LANES] += both[:, :LANES] * SCALE
    acc[:, LANES : 2 * LANES] += both[:, LANES:]
    acc[:, 2 * LANES :] += dot_nt(x_t_ref[...], both_low[LANES:, :])
    at = [pl.ds(pl.multiple_of(i * D + group * LANES, LANES), LANES) for i in range(3)]
    pulled = dot(weight_ref[:, at[0]], query_low) * SCALE + dot(
        jnp.concatenate([weight_ref[:, at[1]], weight_ref[:, at[2]]], axis=1), both_low
    )
    if own:
        pulled = (pulled + other_ref[...]).T
        pulled_ref[...] = pltpu.roll(resid_ref[...] + pulled, begin, 0)
    else:
        pulled_ref[...] = pulled

    @pl.when(row == pl.num_programs(0) - 1)
    def _():
        tall = D // VDP
        for d in range(VDP):
            rows = slice(d * tall, (d + 1) * tall)
            for c in range(3):
                grads_ref[d, c] = acc[rows, c * LANES : (c + 1) * LANES].astype(BF16)
            grads_ref[d, 3] = proj_ref[rows, :].astype(BF16)
        sums_ref[...] = sum_acc[...]


def attend_back(own, marks, place, grad_t, query_t, value, key_t, out_t, inverse, exps, qk_t, x_t, weight, proj, *more):
    total = value.shape[0]
    rows = total // SEQ
    pick = (lambda p: p[2]) if own else (lambda p: 1 - p[2])
    by_group = lambda r, m, p: (r, pick(p))
    by_row = lambda r, m, p: (r, 0)
    whole = lambda r, m, p: (0, 0)
    in_specs = [
        pl.BlockSpec((LANES, SEQ), lambda r, m, p: (pick(p), r)),
        pl.BlockSpec((LANES, SEQ), lambda r, m, p: (pick(p), r)),
        pl.BlockSpec((SEQ, LANES), by_group),
        pl.BlockSpec((LANES, SEQ), lambda r, m, p: (pick(p), r)),
        pl.BlockSpec((LANES, SEQ), lambda r, m, p: (pick(p), r)),
        pl.BlockSpec((1, 8, SEQ), lambda r, m, p: (pick(p), 0, r)),
        pl.BlockSpec((1, 1, 2, HALF, GROUP * HALF), lambda r, m, p: (r, pick(p), 0, 0, 0)),
        pl.BlockSpec((D, SEQ), lambda r, m, p: (0, r)),
        pl.BlockSpec((D, SEQ), lambda r, m, p: (0, r)),
        pl.BlockSpec((D, 3 * D), whole),
        pl.BlockSpec((D, LANES), lambda r, m, p: (0, pick(p))),
    ]
    by_col = pl.BlockSpec((D, SEQ), lambda r, m, p: (0, r))
    if own:
        in_specs += [pl.BlockSpec((SEQ, D), by_row), by_col]
    return pl.pallas_call(
        functools.partial(pull_kernel, own),
        out_shape=(
            jax.ShapeDtypeStruct((total, D) if own else (D, total), F32),
            jax.ShapeDtypeStruct((VDP, VCHIP, D // VDP, LANES), BF16),
            jax.ShapeDtypeStruct((8, LANES), F32),
        ),
        grid_spec=pltpu.PrefetchScalarGridSpec(
            num_scalar_prefetch=2,
            grid=(rows,),
            in_specs=in_specs,
            out_specs=[
                pl.BlockSpec((SEQ, D), by_row) if own else by_col,
                pl.BlockSpec((VDP, VCHIP, D // VDP, LANES), lambda r, m, p: (0, 0, 0, 0)),
                pl.BlockSpec((8, LANES), whole),
            ],
            scratch_shapes=[
                pltpu.VMEM((8, SEQ), F32),
                pltpu.VMEM((LANES, SEQ), F32),
                pltpu.VMEM((LANES, SEQ), F32),
                pltpu.VMEM((LANES, SEQ), F32),
                pltpu.VMEM((D, 3 * LANES), F32),
                pltpu.VMEM((8, LANES), F32),
                pltpu.VMEM((2, GROUP * HALF, LANES), BF16),
                pltpu.VMEM((LANES, SEQ), BF16),
                pltpu.VMEM((2, HALF, GROUP * HALF), BF16),
            ],
        ),
        compiler_params=params(dimension_semantics=("arbitrary",)),
        cost_estimate=pl.CostEstimate(
            flops=18_000_000_000, bytes_accessed=15_000_000, transcendentals=0
        ),
        name="attend_back",
    )(marks, place, grad_t, query_t, value, key_t, out_t, inverse, exps, qk_t, x_t, weight, proj, *more)


def sums_by_group(place, sums_own, sums_other):
    first = place[2] == 0
    return (
        jnp.where(first, sums_own, sums_other),
        jnp.where(first, sums_other, sums_own),
    )


def two_terms(rows):
    high = rows.astype(BF16)
    return jnp.concatenate([high.astype(F32), rows - high.astype(F32)], axis=0)


def column_to_row(columns, rows):
    lane = iota((rows, LANES), 1)
    wide = jnp.zeros((rows, LANES), F32)
    for i, column in enumerate(columns):
        wide = jnp.where(lane == i, column, wide)
    return wide.T[:8, :]


def total_of(array):
    return jnp.sum(jnp.sum(array, axis=0, keepdims=True), axis=1, keepdims=True)


def tail_ffn_kernel(place, ffn_ref, rows_1, rows_2, last_ref, grad_ref, stat_ref):
    lane = iota((1, LANES), 1)
    piece, across = [], []
    for kind in range(2):
        total = ffn_ref[0, kind].astype(F32)
        for at in range(1, VDP * VCHIP):
            total = total + ffn_ref[at, kind].astype(F32)
        grad_ref[kind] = total
        square = total * total + EPS_ONE
        down = jnp.sum(square, axis=0, keepdims=True)
        piece += [down[:, :LANES], down[:, LANES:]]
        across.append(jnp.sum(square, axis=1, keepdims=True))
    across = column_to_row(across, total.shape[0])
    across = jnp.concatenate([across[0:1], across[1:2]], axis=1)
    olds = jnp.zeros((1, LANES), F32)
    for i, ref in enumerate((rows_1, rows_2)):
        olds = jnp.where(lane == i, jnp.sum(ref[...], axis=1, keepdims=True), olds)
    stat_ref[...] = jnp.concatenate([across] + piece + [olds, jnp.zeros((2, LANES), F32)], axis=0)


def tail_send_kernel(
    place, mine_ref, got_ref, vector_ref, own_ref, other_ref, stat_ref, stat_other_ref, send_ref
):
    tall = D // VDP
    low, high = sums_by_group(place, own_ref[...], other_ref[...])
    vector = jnp.concatenate(
        [
            vector_ref[:8, :],
            jnp.concatenate([low[:2], high[:2]], axis=1),
            vector_ref[10:, :],
        ],
        axis=0,
    )
    stat = jnp.concatenate([stat_ref[0:1, :] + stat_other_ref[0:1, :], stat_ref[1:6, :]], axis=0)
    stat = two_terms(stat)
    rows = VEC // VDP
    for d in range(VDP):
        for c in range(VCHIP):
            at = d * VCHIP + c
            both = mine_ref[d, c].astype(F32) + got_ref[d, c].astype(F32)
            send_ref[at, :tall, :] = both.astype(BF16)
            part = vector[d * rows : (d + 1) * rows, c * 64 : (c + 1) * 64]
            part = jnp.concatenate([part, jnp.zeros((rows, LANES - 64), F32)], axis=1)
            send_ref[at, tall:, :] = jnp.concatenate([part, stat], axis=0).astype(BF16)


def tail_reduce_kernel(
    place,
    got_ref,
    ffn_grad_ref,
    attn_ref,
    first_ref,
    second_ref,
    rows_0,
    rows_1,
    rows_2,
    cols_0,
    cols_1,
    cols_2,
    vector_ref,
    moment_ref,
    grad_ref,
    update_1,
    update_2,
    rows_out_1,
    rows_out_2,
    cols_out_1,
    cols_out_2,
    send_ref,
):
    decay = 1.0 - STEP ** (-0.8)
    chip = place[1]
    dp = place[0]
    tall = attn_ref.shape[0]
    rows, width = vector_ref.shape
    pieces = VDP * VCHIP
    lane = iota((1, LANES), 1)
    total = got_ref[0, :tall, :].astype(F32)
    part = got_ref[0, tall:, :].astype(F32)[:rows]
    for at in range(1, pieces):
        total = total + got_ref[at, :tall, :].astype(F32)
        part = part + got_ref[at, tall:, :].astype(F32)[:rows]
    grad_ref[...] = total
    low = total.astype(BF16)

    def stat_of(at):
        both = got_ref[pl.ds(at, 1), tall:, :][0].astype(F32)[rows:]
        return both[:6] + both[6:12]

    every = jnp.zeros((1, LANES), F32)
    olds = jnp.zeros((1, LANES), F32)
    mine = jnp.zeros((1, LANES), F32)
    down = jnp.zeros((6, LANES), F32)
    for d in range(VDP):
        down = down + stat_of(d * VCHIP + chip)
        for c in range(VCHIP):
            stat = stat_of(d * VCHIP + c)
            every = every + stat[0:1]
            if c == 0:
                olds = olds + stat[5:6]
    for c in range(VCHIP):
        mine = mine + stat_of(dp * VCHIP + c)[0:1]
    row_total = tall * VDP
    new_rows, means = [], []
    for i, ref in enumerate((rows_1, rows_2)):
        count = first_ref.shape[1] * 2 * VCHIP
        new_rows.append(decay * ref[...] + (1.0 - decay) * (mine[:, i * tall : (i + 1) * tall] / count))
        old = jnp.sum(jnp.where(lane == i, olds, 0.0), axis=1, keepdims=True)
        fresh = jnp.sum(every[:, i * tall : (i + 1) * tall], axis=1, keepdims=True)
        means.append((decay * old + (1.0 - decay) * (fresh / count)) / row_total)
    tile = jnp.concatenate(new_rows + [jnp.zeros((6, tall), F32)], axis=0)
    rows_out_1[...] = new_rows[0]
    rows_out_2[...] = new_rows[1]
    tile = jnp.concatenate([tile, jnp.zeros((8, LANES - tall), F32)], axis=1)
    turned = jnp.concatenate([tile, jnp.zeros((LANES - 8, LANES), F32)], axis=0).T
    scalars = jnp.zeros((1, LANES), F32)
    for i, (old_ref, out_ref, to) in enumerate(
        ((cols_1, cols_out_1, update_1), (cols_2, cols_out_2, update_2))
    ):
        sums = jnp.concatenate([down[1 + 2 * i : 2 + 2 * i], down[2 + 2 * i : 3 + 2 * i]], axis=1)
        cols = decay * old_ref[...] + (1.0 - decay) * (sums / row_total)
        out_ref[...] = cols
        grad = ffn_grad_ref[i]
        update = grad * lax.rsqrt(turned[:tall, i : i + 1] * cols / means[i])
        to[...] = update
        scalars = jnp.where(lane == 67 + i, total_of(update * update), scalars)
    for i, ref in enumerate((attn_ref, first_ref, second_ref)):
        weight = ref[...]
        scalars = jnp.where(lane == 64 + i, total_of(weight * weight), scalars)
    scalars = jnp.concatenate([rows_0[...], scalars[:, tall:]], axis=1)
    vector = vector_ref[...]
    power = jnp.sum(vector * vector, axis=1, keepdims=True)
    lines = jnp.concatenate(
        [part[:, :64], moment_ref[...], jnp.broadcast_to(power, (rows, LANES - 64 - width))], axis=1
    )
    piece = jnp.concatenate(
        [two_terms(lines), two_terms(jnp.concatenate([cols_0[...], scalars], axis=0))]
        + [jnp.zeros((4, LANES), F32)],
        axis=0,
    ).astype(BF16)
    for at in range(pieces):
        send_ref[at, :tall, :] = low
        send_ref[at, tall:, :] = piece


def tail_apply_kernel(
    place,
    mine_ref,
    other_ref,
    grad_ref,
    update_1,
    update_2,
    weight_0,
    weight_1,
    weight_2,
    rows_0,
    cols_0,
    vector_ref,
    moment_ref,
    new_0,
    new_1,
    new_2,
    rows_out,
    cols_out,
    vector_grad_ref,
    moment_out,
    vector_out,
    sums_s,
    rows_s,
):
    decay = 1.0 - STEP ** (-0.8)
    dp, chip, core = place[0], place[1], place[2]
    tall = weight_0.shape[0]
    rows, width = vector_ref.shape
    fsdp = 2 * VCHIP
    lane = iota((1, LANES), 1)
    refs = (mine_ref, other_ref)
    row_total = float(tall * VDP)
    col_total = float(LANES * fsdp)

    def lines_of(ref, at):
        both = ref[at, tall:, :].astype(F32)
        return both[0:4] + both[4:8], both[8:10] + both[10:12]

    scalars = jnp.zeros((1, LANES), F32)
    for ref in refs:
        for at in range(VDP * VCHIP):
            scalars = scalars + lines_of(ref, at)[1][1:2]
    scalar = lambda at: jnp.sum(jnp.where(lane == at, scalars, 0.0), axis=1, keepdims=True)

    tile, fresh = [], []
    for d in range(VDP):
        wide = jnp.zeros((tall, LANES), F32)
        for ref in refs:
            for c in range(VCHIP):
                block = ref[d * VCHIP + c, :tall, :].astype(F32)
                wide = wide + (block * block + EPS_ONE)
        fresh.append(jnp.sum(wide, axis=1, keepdims=True))
        tile.append(lines_of(mine_ref, d * VCHIP)[1][1:2])
    tile = jnp.concatenate(tile + [jnp.zeros((LANES - VDP, LANES), F32)], axis=0).T
    mean = jnp.zeros((1, 1), F32)
    new_rows = []
    for d in range(VDP):
        new = decay * tile[:tall, d : d + 1] + (1.0 - decay) * (fresh[d] / col_total)
        new_rows.append(1.0 / new)
        mean = mean + jnp.sum(new, axis=0, keepdims=True)
        sums_s[d] = jnp.broadcast_to(fresh[d], (tall, LANES))
    mean = mean / row_total
    mine = sums_s[pl.ds(dp, 1)][0]
    rows_s[...] = mine.T
    rows_new = decay * rows_0[...] + (1.0 - decay) * (rows_s[0:1, :tall] / col_total)
    rows_out[...] = rows_new
    power = jnp.zeros((1, 1), F32)
    for half, ref in enumerate(refs):
        for c in range(VCHIP):
            down = jnp.zeros((tall, LANES), F32)
            weighted = jnp.zeros((tall, LANES), F32)
            for d in range(VDP):
                block = ref[d * VCHIP + c, :tall, :].astype(F32)
                square = block * block
                down = down + (square + EPS_ONE)
                weighted = weighted + square * new_rows[d]
            down = jnp.sum(down, axis=0, keepdims=True)
            old = lines_of(ref, c)[1][0:1]
            cols = decay * old + (1.0 - decay) * (down / row_total)
            weighted = jnp.sum(weighted, axis=0, keepdims=True) / cols
            power = power + jnp.sum(weighted, axis=1, keepdims=True)
            if half == 0:
                sums_s[VDP + c] = jnp.broadcast_to(down, (tall, LANES))
    power = power * mean
    down = sums_s[pl.ds(VDP + chip, 1)][0][0:1, :]
    cols_new = decay * cols_0[...] + (1.0 - decay) * (down / row_total)
    cols_out[...] = cols_new
    column = jnp.concatenate(
        [
            jnp.concatenate([rows_new, jnp.zeros((1, LANES - tall), F32)], axis=1),
            jnp.zeros((LANES - 1, LANES), F32),
        ],
        axis=0,
    ).T[:tall, 0:1]
    update_0 = grad_ref[...] * lax.rsqrt(column * cols_new / mean)
    powers = (power, scalar(67), scalar(68))
    for i, (update, weight, new) in enumerate(
        (
            (update_0, weight_0, new_0),
            (update_1[...], weight_1, new_1),
            (update_2[...], weight_2, new_2),
        )
    ):
        entries = float(weight.shape[0] * weight.shape[1] * VDP * fsdp)
        clip = jnp.maximum(1.0, jnp.sqrt(powers[i] / entries) / CLIP_LIMIT)
        rate = STEP_RATE * jnp.maximum(EPS_TWO, jnp.sqrt(scalar(64 + i) / entries))
        new[...] = weight[...] - rate / clip * update
    powers, sizes = [], []
    for d in range(VDP):
        power = jnp.zeros((rows, 1), F32)
        size = jnp.zeros((rows, 1), F32)
        for c in range(VCHIP):
            at = d * VCHIP + c
            first, second = lines_of(mine_ref, at)[0], lines_of(other_ref, at)[0]
            both = first[:, :64] + second[:, :64]
            size = size + first[:, LANES - 1 :] + second[:, LANES - 1 :]
            near = jnp.where(core == 0, first[:, 64 : 64 + width], second[:, 64 : 64 + width])
            far = jnp.where(core == 0, second[:, 64 : 64 + width], first[:, 64 : 64 + width])
            moment = jnp.concatenate([near, far], axis=1)
            moment = decay * moment + (1.0 - decay) * (both * both + EPS_ONE)
            power = power + jnp.sum(both * both / moment, axis=1, keepdims=True)
            wide = jnp.concatenate([both, jnp.zeros((rows, LANES - 64), F32)], axis=1)
            sums_s[2 * VDP + at, :rows, :] = wide
        powers.append(power)
        sizes.append(size)
    both = sums_s[pl.ds(2 * VDP + dp * VCHIP + chip, 1), :rows, :][0]
    vector_grad = jnp.where(core == 0, both[:, :width], both[:, width : 2 * width])
    vector_grad_ref[...] = vector_grad
    moment = decay * moment_ref[...] + (1.0 - decay) * (vector_grad * vector_grad + EPS_ONE)
    moment_out[...] = moment
    step = vector_grad * lax.rsqrt(moment)
    bias = VDP // 2
    bias_power = sum(jnp.sum(power, axis=0, keepdims=True) for power in powers[:bias])
    bias_size = sum(jnp.sum(size, axis=0, keepdims=True) for size in sizes[:bias])
    power, size = powers[bias], sizes[bias]
    for d in range(bias + 1, VDP):
        power = jnp.where(dp == d, powers[d], power)
        size = jnp.where(dp == d, sizes[d], size)
    is_bias = dp < bias
    power = jnp.where(is_bias, bias_power, power)
    size = jnp.where(is_bias, bias_size, size)
    count = jnp.where(is_bias, float(FF), float(D))
    clip = jnp.maximum(1.0, jnp.sqrt(power / count) / CLIP_LIMIT)
    rate = STEP_RATE * jnp.maximum(EPS_TWO, jnp.sqrt(size / count))
    vector_out[...] = vector_ref[...] - rate / clip * step


def whole_call(kernel, name, place, outs, *operands, scratch=()):
    return pl.pallas_call(
        kernel,
        out_shape=[jax.ShapeDtypeStruct(shape, kind) for shape, kind in outs],
        in_specs=[pl.BlockSpec(memory_space=pltpu.SMEM)] + [vspec()] * len(operands),
        out_specs=[vspec()] * len(outs),
        scratch_shapes=list(scratch),
        compiler_params=params(16),
        name=name,
    )(place, *operands)


def core_swap(block):
    return lax.ppermute(block, "core", [(0, 1), (1, 0)])


def exchange(blocks, axes):
    return lax.all_to_all(blocks, axes, split_axis=0, concat_axis=0, tiled=True)


def after(value, *earlier):
    return pl.pallas_call(
        lambda *refs: None,
        out_shape=jax.ShapeDtypeStruct(value.shape, value.dtype),
        in_specs=[pl.BlockSpec(memory_space=pltpu.HBM)] * (1 + len(earlier)),
        out_specs=pl.BlockSpec(memory_space=pltpu.HBM),
        input_output_aliases={0: 0},
        compiler_params=params(),
        name="after",
    )(value, *earlier)


def pair_kernel(mine_ref, got_ref, out_ref):
    out_ref[...] = (mine_ref[...].astype(F32) + got_ref[...].astype(F32)).astype(BF16)


def pair_sum(mine, got):
    return pl.pallas_call(
        pair_kernel,
        out_shape=jax.ShapeDtypeStruct(mine.shape, BF16),
        in_specs=[vspec(), vspec()],
        out_specs=vspec(),
        compiler_params=params(16),
        name="pair_sum",
    )(mine, got)


CHIPS = ("dp", "chip")
ALL = ("dp", "chip", "core")


def layer(place, weights, segment_ids, tokens, cotangent, ffn_weights, send_core, send_ffn):
    table = jnp.asarray(encode_table())
    qk, x, qk_t, x_t, back, marks = place_tokens(segment_ids, tokens, cotangent, table)
    query_t, value, key_t, out_t, inverse, mixed, mixed_t, exps, weight, proj, vector = attend_forward(
        marks, place, x, qk, x_t, qk_t, *weights(marks)
    )
    ffn_mine, ffn_other = ffn_weights(marks, vector)
    block_out, resid, grad_t, ffn_mine, ffn_other, proj_g, vector_g = feed_forward(
        marks, place, x, back, mixed, mixed_t, proj, ffn_mine, ffn_other, vector
    )
    ffn_got, grad_t = send_ffn(ffn_mine, ffn_other, grad_t)
    shared = (marks, place, grad_t, query_t, value, key_t, out_t, inverse, exps, qk_t, x_t, weight, proj_g)
    pulled, grads_other, sums_other = attend_back(False, *shared)
    attn_got = send_core(grads_other)
    input_grad, grads_own, sums_own = attend_back(True, *shared, resid, pulled)
    return block_out, input_grad, grads_own, grads_other, attn_got, sums_own, sums_other, vector_g, ffn_got


def body(
    tokens,
    cotangent,
    segment_ids,
    attn_weight,
    ffn_in,
    ffn_out,
    vectors,
    attn_rows,
    attn_cols,
    in_rows,
    in_cols,
    out_rows,
    out_cols,
    vector_moment,
):
    place = jnp.stack([lax.axis_index("dp"), lax.axis_index("chip"), lax.axis_index("core")])
    place = place.astype(jnp.int32)
    pieces = VDP * VCHIP
    tall, wide = attn_weight.shape
    rows_v, cols_v = vectors.shape
    split = lambda array: array.reshape((VDP, VCHIP) + array.shape[1:])
    attn_mine = exchange(pack_attn(place, attn_weight, vectors), CHIPS)

    ffn_low = jnp.stack([ffn_in, ffn_out]).astype(BF16)
    parts = [
        lax.ppermute(ffn_low, "dp", [(i, i ^ step) for i in range(VDP)]) for step in range(1, VDP)
    ]
    ffn_sent = pack_ffn(place, ffn_in, ffn_out, parts)

    def attn_weights(marks):
        mine = split(after(attn_mine, marks, ffn_sent))
        return mine, core_swap(mine)

    def ffn_weights(marks, vector):
        got = exchange(after(ffn_sent, marks), "chip")
        ffn_mine = after(got, vector)
        return ffn_mine, core_swap(ffn_mine)

    def send_ffn(mine, other, grad_t):
        both = pair_sum(mine, core_swap(other))
        got = exchange(both.reshape((pieces,) + mine.shape[2:]), CHIPS)
        return got, after(grad_t, both)

    (
        block_out,
        input_grad,
        grads_own,
        grads_other,
        attn_got,
        sums_own,
        sums_other,
        vector_g,
        ffn_got,
    ) = layer(place, attn_weights, segment_ids, tokens, cotangent, ffn_weights, core_swap, send_ffn)
    lay = lambda stat: stat.reshape(1, -1)
    rows_old = (lay(attn_rows), lay(in_rows), lay(out_rows))
    cols_old = (lay(attn_cols), lay(in_cols), lay(out_cols))
    weights_old = (attn_weight, ffn_in, ffn_out)
    ffn_grad, stat = whole_call(
        tail_ffn_kernel,
        "tail_ffn",
        place,
        [((2,) + ffn_in.shape, F32), ((8, LANES), F32)],
        ffn_got,
        *rows_old[1:],
        sums_own,
    )
    (sent,) = whole_call(
        tail_send_kernel,
        "tail_send",
        place,
        [((pieces, tall + VROWS, LANES), BF16)],
        grads_own,
        attn_got,
        vector_g,
        sums_own,
        sums_other,
        stat,
        core_swap(stat),
    )
    got = exchange(sent, CHIPS)
    attn_grad, update_1, update_2, rows_new_1, rows_new_2, cols_new_1, cols_new_2, sent = whole_call(
        tail_reduce_kernel,
        "tail_reduce",
        place,
        [
            (attn_weight.shape, F32),
            (ffn_in.shape, F32),
            (ffn_out.shape, F32),
            (rows_old[1].shape, F32),
            (rows_old[2].shape, F32),
            (cols_old[1].shape, F32),
            (cols_old[2].shape, F32),
            ((pieces, tall + VROWS, LANES), BF16),
        ],
        got,
        ffn_grad,
        *weights_old,
        *rows_old,
        *cols_old,
        vectors,
        vector_moment,
    )
    mine = exchange(sent, CHIPS)
    attn_new, in_new, out_new, rows_new_0, cols_new_0, vector_grad, moment_new, vectors_new = whole_call(
        tail_apply_kernel,
        "tail_apply",
        place,
        [
            (attn_weight.shape, F32),
            (ffn_in.shape, F32),
            (ffn_out.shape, F32),
            (rows_old[0].shape, F32),
            (cols_old[0].shape, F32),
            (vectors.shape, F32),
            (vectors.shape, F32),
            (vectors.shape, F32),
        ],
        mine,
        core_swap(mine),
        attn_grad,
        update_1,
        update_2,
        *weights_old,
        rows_old[0],
        cols_old[0],
        vectors,
        vector_moment,
        scratch=[
            pltpu.VMEM((2 * VDP + pieces, tall, LANES), F32),
            pltpu.VMEM((LANES, tall), F32),
        ],
    )
    return (
        block_out,
        input_grad,
        attn_grad,
        ffn_grad[0],
        ffn_grad[1],
        vector_grad,
        rows_new_0.reshape(-1),
        cols_new_0.reshape(-1),
        rows_new_1.reshape(-1),
        cols_new_1.reshape(-1),
        rows_new_2.reshape(-1),
        cols_new_2.reshape(-1),
        moment_new,
        attn_new,
        in_new,
        out_new,
        vectors_new,
    )


def gather_all(block):
    shape = (lax.axis_size("dp"), lax.axis_size("chip") * 2)
    count = shape[0] * shape[1]
    got = exchange(jnp.broadcast_to(block[None], (count,) + block.shape), ALL)
    return got.reshape(shape + block.shape)


def unblock(parts):
    dp_count, fsdp_count, rows, cols = parts.shape
    return parts.transpose(0, 2, 1, 3).reshape(dp_count * rows, fsdp_count * cols)


def scatter_sum(full):
    dp_count = lax.axis_size("dp")
    fsdp_count = lax.axis_size("chip") * 2
    rows, cols = full.shape
    by_col = full.astype(BF16).reshape(rows, fsdp_count, cols // fsdp_count).transpose(1, 0, 2)
    got = exchange(by_col, ("chip", "core"))
    part = jnp.sum(got.astype(F32), axis=0).astype(BF16)
    by_row = part.reshape(dp_count, rows // dp_count, cols // fsdp_count)
    return jnp.sum(exchange(by_row, "dp").astype(F32), axis=0)


def body_any(
    tokens,
    cotangent,
    segment_ids,
    attn_weight,
    ffn_in,
    ffn_out,
    vectors,
    attn_rows,
    attn_cols,
    in_rows,
    in_cols,
    out_rows,
    out_cols,
    vector_moment,
):
    dp_count = lax.axis_size("dp")
    fsdp_count = lax.axis_size("chip") * 2
    dp_place = lax.axis_index("dp")
    fsdp_place = lax.axis_index("chip") * 2 + lax.axis_index("core")
    rows_w = attn_weight.shape[0]
    rows_v = vectors.shape[0]
    place = jnp.zeros((3,), jnp.int32)
    full_attn = unblock(gather_all(attn_weight.astype(BF16)))
    full_vector = unblock(gather_all(vectors.astype(BF16)))
    full_ffn = jnp.stack(
        [unblock(gather_all(ffn_in.astype(BF16))), unblock(gather_all(ffn_out.astype(BF16)))]
    )
    tall = D // VDP
    cut = full_attn.reshape(VDP, tall, VCHIP, 2, LANES).transpose(3, 0, 2, 1, 4)
    lines = full_vector.reshape(VDP, VEC // VDP, 2, LANES).transpose(0, 2, 1, 3)
    lines = lines.reshape(VDP, 1, 2 * VEC // VDP, LANES)
    lines = jnp.pad(lines, ((0, 0), (0, VCHIP - 1), (0, VROWS - 2 * VEC // VDP), (0, 0)))
    weights = (
        jnp.concatenate([cut[0], lines], axis=2),
        jnp.concatenate([cut[1], jnp.zeros_like(lines)], axis=2),
    )
    ffn_cut = full_ffn.reshape(2, VDP, tall, VCHIP, 2, FF // (2 * VCHIP))
    ffn_cut = ffn_cut.transpose(4, 3, 1, 0, 2, 5)
    (
        block_out,
        input_grad,
        grads_own,
        grads_other,
        _,
        sums_own,
        sums_other,
        vector_g,
        ffn_got,
    ) = layer(
        place,
        lambda marks: weights,
        segment_ids,
        tokens,
        cotangent,
        lambda marks, vector: (ffn_cut[0], ffn_cut[1]),
        lambda block: block,
        lambda mine, other, grad_t: (jnp.stack([mine, other]), grad_t),
    )
    attn_full = jnp.stack([grads_own, grads_other]).transpose(1, 3, 2, 0, 4).reshape(D, 4 * D)
    ffn_full = ffn_got.transpose(3, 1, 4, 2, 0, 5).reshape(2, D, FF)
    sums = jnp.concatenate([sums_own[:2], sums_other[:2]], axis=1)
    vector_full = jnp.concatenate([vector_g[:8], sums, vector_g[10:]], axis=0)
    attn_grad = scatter_sum(attn_full)
    in_grad = scatter_sum(ffn_full[0])
    out_grad = scatter_sum(ffn_full[1])
    vector_grad = scatter_sum(vector_full)

    decay = 1.0 - STEP ** (-0.8)
    gradients = (attn_grad, in_grad, out_grad)
    weights_old = (attn_weight, ffn_in, ffn_out)
    rows_old = (attn_rows, in_rows, out_rows)
    cols_old = (attn_cols, in_cols, out_cols)
    moment_new = decay * vector_moment + (1.0 - decay) * (vector_grad * vector_grad + EPS_ONE)
    vector_step = vector_grad * lax.rsqrt(moment_new)
    squares = [gradient * gradient + EPS_ONE for gradient in gradients]
    pieces = []
    for square in squares:
        pieces.append(jnp.sum(square, axis=1))
    for square in squares:
        pieces.append(jnp.sum(square, axis=0))
    pieces.append(jnp.sum(vector_step * vector_step, axis=1))
    pieces.append(jnp.sum(vectors * vectors, axis=1))
    pieces.append(jnp.stack([jnp.sum(weight * weight) for weight in weights_old]))
    pieces.append(jnp.stack([jnp.sum(old) for old in rows_old]))
    sizes = [piece.shape[0] for piece in pieces]
    flat = jnp.concatenate(pieces)
    flat = jnp.pad(flat, (0, -flat.shape[0] % 1024)).reshape(-1, LANES)
    got = gather_all(flat).reshape(dp_count, fsdp_count, -1)
    offsets = [0]
    for length in sizes:
        offsets.append(offsets[-1] + length)
    take = lambda i: got[:, :, offsets[i] : offsets[i + 1]]
    rows_new, cols_new, row_means, entries = [], [], [], []
    for i in range(3):
        count_rows = rows_w * dp_count
        count_cols = weights_old[i].shape[1] * fsdp_count
        entries.append(float(count_rows * count_cols))
        row_all = jnp.sum(take(i), axis=1)
        mine = lax.dynamic_index_in_dim(row_all, dp_place, 0, keepdims=False)
        rows_new.append(decay * rows_old[i] + (1.0 - decay) * mine / count_cols)
        col_all = jnp.sum(take(3 + i), axis=0)
        mine = lax.dynamic_index_in_dim(col_all, fsdp_place, 0, keepdims=False)
        cols_new.append(decay * cols_old[i] + (1.0 - decay) * mine / count_rows)
        old_total = jnp.sum(take(9)[:, 0, i])
        row_means.append(
            (decay * old_total + (1.0 - decay) * jnp.sum(row_all) / count_cols) / count_rows
        )
    step_rows = jnp.sum(take(6), axis=1).reshape(-1)
    weight_rows = jnp.sum(take(7), axis=1).reshape(-1)
    weight_totals = jnp.sum(take(8), axis=(0, 1))
    updates = []
    for i in range(3):
        second = rows_new[i][:, None] * cols_new[i][None, :] / row_means[i]
        updates.append(gradients[i] * lax.rsqrt(second))
    flat = jnp.stack([jnp.sum(update * update) for update in updates])
    flat = jnp.broadcast_to(jnp.pad(flat, (0, 5))[:, None], (8, LANES))
    totals = jnp.sum(gather_all(flat)[:, :, :, 0], axis=(0, 1))
    new_weights = []
    for i in range(3):
        clip_factor = jnp.maximum(1.0, jnp.sqrt(totals[i] / entries[i]) / CLIP_LIMIT)
        step_size = STEP_RATE * jnp.maximum(EPS_TWO, jnp.sqrt(weight_totals[i] / entries[i]))
        new_weights.append(weights_old[i] - step_size / clip_factor * updates[i])
    bias_rows = FF // D
    row_places = jnp.arange(VEC)
    counts = jnp.where(row_places < bias_rows, float(FF), float(D))
    grouped_updates = jnp.where(row_places < bias_rows, jnp.sum(step_rows[:bias_rows]), step_rows)
    grouped_weights = jnp.where(row_places < bias_rows, jnp.sum(weight_rows[:bias_rows]), weight_rows)
    clip_rows = jnp.maximum(1.0, jnp.sqrt(grouped_updates / counts) / CLIP_LIMIT)
    step_sizes = STEP_RATE * jnp.maximum(EPS_TWO, jnp.sqrt(grouped_weights / counts))
    factor_rows = lax.dynamic_slice_in_dim(step_sizes / clip_rows, dp_place * rows_v, rows_v)
    vectors_new = vectors - factor_rows[:, None] * vector_step
    return (
        block_out,
        input_grad,
        attn_grad,
        in_grad,
        out_grad,
        vector_grad,
        rows_new[0],
        cols_new[0],
        rows_new[1],
        cols_new[1],
        rows_new[2],
        cols_new[2],
        moment_new,
        new_weights[0],
        new_weights[1],
        new_weights[2],
        vectors_new,
    )


def solution(mesh):
    dp_count, fsdp_count = mesh.shape["dp"], mesh.shape["fsdp"]
    inner = jax.sharding.Mesh(mesh.devices.reshape(dp_count, fsdp_count // 2, 2), ALL)
    fsdp = ("chip", "core")
    split = P(ALL, None)
    block = P("dp", fsdp)
    stats = (P("dp"), P(fsdp)) * 3
    plain = dp_count == VDP and fsdp_count == 2 * VCHIP
    return jax.shard_map(
        body if plain else body_any,
        mesh=inner,
        in_specs=(split,) * 3 + (block,) * 4 + stats + (block,),
        out_specs=(split,) * 2 + (block,) * 4 + stats + (block,) * 5,
        check_vma=False,
    )
```

```python
import functools
import math

import jax
import jax.numpy as jnp
import numpy as np
from jax import lax
from jax.experimental import pallas as pl
from jax.experimental.pallas import tpu as pltpu
from jax.sharding import PartitionSpec as P

D = 256
FF = 2048
HEADS = 8
HEAD_DIM = 32
SEQ = 1024
HALF = 512
GROUP = 4
LANES = 128
QBLOCK = 512
WGRID = 32
STEP = 10
VEC = 16
TILE = 1024
CHUNK = 512
SUB = 512
LEAD = 5
STRIP = 64
VDP = 4
VCHIP = 4
VROWS = 16

EPS_NORM = 1e-05
EPS_ONE = 1e-30
EPS_TWO = 0.001
CLIP_LIMIT = 1.0
STEP_RATE = 0.3
FAR = 1e30
TAME = 40.0
LOG2_E = math.log2(math.e)
SCALE = HEAD_DIM ** (-0.5)
GELU_A = math.sqrt(2.0 / math.pi)
GELU_B = 0.044715
F32 = jnp.float32
BF16 = jnp.bfloat16
MIB = 1024 * 1024


def dot(left, right):
    return jnp.dot(left, right, preferred_element_type=F32)


def dot_nt(left, right):
    return lax.dot_general(left, right, (((1,), (1,)), ((), ())), preferred_element_type=F32)


def encode_table():
    half = D // 2
    feature = np.arange(half)
    freq = np.exp(
        (2 * (feature // 2)).astype(np.float32) * np.float32(-math.log(10000.0) / half)
    ).astype(np.float32)
    angles = np.arange(1, WGRID + 1, dtype=np.float32)[:, None] * freq[None, :]
    table = np.where(feature % 2 == 0, np.sin(angles), np.cos(angles)).astype(np.float32)
    low = jnp.bfloat16
    one = table.astype(low)
    rest = table - one.astype(np.float32)
    two = rest.astype(low)
    three = (rest - two.astype(np.float32)).astype(low)
    blank = np.zeros((LANES - 3 * WGRID, half), low)
    return np.concatenate([one, two, three, blank], axis=0)


def iota(shape, dim):
    return lax.broadcasted_iota(jnp.int32, shape, dim)


def norm_forward(rows):
    centered = rows - jnp.mean(rows, axis=-1, keepdims=True)
    inverse = lax.rsqrt(jnp.mean(centered * centered, axis=-1, keepdims=True) + EPS_NORM)
    return centered * inverse, inverse


def norm_backward(upstream, normed, inverse):
    return inverse * (
        upstream
        - jnp.mean(upstream, axis=-1, keepdims=True)
        - normed * jnp.mean(upstream * normed, axis=-1, keepdims=True)
    )

def vspec():
    return pl.BlockSpec(memory_space=pltpu.VMEM)


def params(mib=56, **more):
    return pltpu.CompilerParams(vmem_limit_bytes=mib * MIB, **more)


def pack_kernel(place, attn_ref, vector_ref, out_ref):
    owner = place[1] * 2 + place[2]
    vector = vector_ref[...]
    rows = vector.shape[0]
    wide = jnp.concatenate([vector] * (LANES // vector.shape[1]), axis=1)
    slot = iota((rows, LANES), 1) // vector.shape[1]
    per = LANES // vector.shape[1]
    parts = [attn_ref[...]]
    for half in range(2):
        parts.append(jnp.where(slot + half * per == owner, wide, 0.0))
    parts.append(jnp.zeros((VROWS - 2 * rows, LANES), F32))
    piece = jnp.concatenate(parts, axis=0).astype(BF16)
    for at in range(VDP * VCHIP):
        out_ref[at] = piece


def pack_attn(place, attn_weight, vectors):
    return pl.pallas_call(
        pack_kernel,
        out_shape=jax.ShapeDtypeStruct((VDP * VCHIP, attn_weight.shape[0] + VROWS, LANES), BF16),
        in_specs=[pl.BlockSpec(memory_space=pltpu.SMEM), vspec(), vspec()],
        out_specs=vspec(),
        compiler_params=params(),
        name="pack_attn",
    )(place, attn_weight, vectors)


def pack_ffn_kernel(place, first_ref, second_ref, *refs):
    out_ref = refs[-1]
    first = first_ref[...].astype(BF16)
    second = second_ref[...].astype(BF16)
    for at in range(VCHIP):
        out_ref[at, pl.ds(place[0], 1), 0] = first[None]
        out_ref[at, pl.ds(place[0], 1), 1] = second[None]
        for step in range(1, VDP):
            out_ref[at, pl.ds(place[0] ^ step, 1)] = refs[step - 1][...][None]


def pack_ffn(place, ffn_in, ffn_out, parts):
    return pl.pallas_call(
        pack_ffn_kernel,
        out_shape=jax.ShapeDtypeStruct((VCHIP, VDP, 2) + ffn_in.shape, BF16),
        in_specs=[pl.BlockSpec(memory_space=pltpu.SMEM)] + [vspec()] * (2 + len(parts)),
        out_specs=vspec(),
        compiler_params=params(16),
        name="pack_ffn",
    )(place, ffn_in, ffn_out, *parts)


def place_kernel(
    segment_ref, tokens_ref, back_ref, table_ref, qk_ref, x_ref, qk_t_ref, x_t_ref, turned_ref, marks_ref
):
    row = pl.program_id(0)
    starts = []
    for number in range(1, 4):
        at = jnp.int32(0)
        for step in (512, 256, 128, 64, 32, 16, 8, 4, 2, 1, 1):
            probe = jnp.minimum(at + (step - 1), SEQ - 1)
            at = jnp.where(segment_ref[row, probe] < number, at + step, at)
        starts.append(at)
    edges = [jnp.int32(0)] + starts + [jnp.int32(SEQ)]
    begin = jnp.int32(0)
    for number in range(3, -1, -1):
        begin = jnp.where(edges[number + 1] - edges[number] == HALF, edges[number], begin)
    for number in range(3):
        marks_ref[row, number] = starts[number]
    marks_ref[row, 3] = begin
    one, two, three = starts
    x = pltpu.roll(tokens_ref[...].astype(F32), (SEQ - begin) & (SEQ - 1), 0)
    x_ref[...] = x.astype(BF16)
    x_t_ref[...] = x.T.astype(BF16)
    back = back_ref[...].astype(F32)
    turned_ref[...] = pltpu.roll(back, (SEQ - begin) & (SEQ - 1), 0).astype(BF16)
    at = (iota((SEQ, LANES), 0) + begin) & (SEQ - 1)
    lane = iota((SEQ, LANES), 1)
    start = jnp.where(at >= three, three, jnp.where(at >= two, two, jnp.where(at >= one, one, 0)))
    local = at - start
    kept = lane < 3 * WGRID
    slot = lane & (WGRID - 1)
    hot_r = jnp.where(((local >> 5) == slot) & kept, 1.0, 0.0).astype(BF16)
    hot_c = jnp.where(((local & (WGRID - 1)) == slot) & kept, 1.0, 0.0).astype(BF16)
    table = table_ref[...]
    places = jnp.concatenate([dot(hot_r, table), dot(hot_c, table)], axis=1)
    qk = x + places
    qk_ref[...] = qk.astype(BF16)
    qk_t_ref[...] = qk.T.astype(BF16)


def place_tokens(segment_ids, tokens, cotangent, table):
    rows = segment_ids.shape[0]
    by_row = lambda r: (r, 0)
    return pl.pallas_call(
        place_kernel,
        out_shape=(
            jax.ShapeDtypeStruct(tokens.shape, BF16),
            jax.ShapeDtypeStruct(tokens.shape, BF16),
            jax.ShapeDtypeStruct((D, tokens.shape[0]), BF16),
            jax.ShapeDtypeStruct((D, tokens.shape[0]), BF16),
            jax.ShapeDtypeStruct(tokens.shape, BF16),
            jax.ShapeDtypeStruct((rows, 4), jnp.int32),
        ),
        grid=(rows,),
        in_specs=[
            pl.BlockSpec(memory_space=pltpu.SMEM),
            pl.BlockSpec((SEQ, D), by_row),
            pl.BlockSpec((SEQ, D), by_row),
            pl.BlockSpec((LANES, LANES), lambda r: (0, 0)),
        ],
        out_specs=(
            pl.BlockSpec((SEQ, D), by_row),
            pl.BlockSpec((SEQ, D), by_row),
            pl.BlockSpec((D, SEQ), lambda r: (0, r)),
            pl.BlockSpec((D, SEQ), lambda r: (0, r)),
            pl.BlockSpec((SEQ, D), by_row),
            pl.BlockSpec(memory_space=pltpu.SMEM),
        ),
        compiler_params=params(dimension_semantics=("arbitrary",)),
        cost_estimate=pl.CostEstimate(flops=600_000_000, bytes_accessed=4_000_000, transcendentals=0),
        name="place_tokens",
    )(segment_ids, tokens, cotangent, table)


def attend_kernel(
    marks,
    place,
    x_ref,
    qk_ref,
    x_t_ref,
    qk_t_ref,
    mine_ref,
    other_ref,
    query_t_ref,
    value_ref,
    key_t_ref,
    out_t_ref,
    inverse_ref,
    mixed_ref,
    mixed_t_ref,
    exps_ref,
    weight_ref,
    proj_ref,
    vector_ref,
    key_s,
    value_s,
    mark_k,
    mark_q,
    first_s,
    second_s,
    weight_t_s,
    bias_s,
    tame_s,
):
    row = pl.program_id(0)
    group = pl.program_id(1)
    begin = marks[row, 3]
    core = place[2]

    @pl.when((row == 0) & (group == 0))
    def _():
        tall = D // VDP
        for d in range(VDP):
            rows = slice(d * tall, (d + 1) * tall)
            total = jnp.zeros((8, LANES), F32)
            for c in range(VCHIP):
                for ref, half in ((mine_ref, core), (other_ref, 1 - core)):
                    if c < 3:
                        to = pl.ds(pl.multiple_of(c * D + half * LANES, LANES), LANES)
                        weight_ref[rows, to] = ref[d, c, :tall, :]
                    else:
                        to = pl.ds(pl.multiple_of(half * LANES, LANES), LANES)
                        proj_ref[rows, to] = ref[d, c, :tall, :]
                    total += ref[d, c, tall:, :].astype(F32)[:8]
            vector_ref[d * 4 : (d + 1) * 4, :LANES] = total[:4]
            vector_ref[d * 4 : (d + 1) * 4, LANES:] = total[4:]
        weight_t_s[...] = weight_ref[...].astype(F32).T.astype(BF16)
        bias_s[...] = vector_ref[8:16, :].T

    @pl.when(group == 0)
    def _():
        qk_t = qk_t_ref[...]
        query_t = (dot(weight_t_s[:D, :], qk_t) + bias_s[:, 0:1]) * SCALE
        query_t = query_t.astype(BF16)
        query_t_ref[...] = query_t
        key_t = dot(weight_t_s[D : 2 * D, :], qk_t).astype(BF16)
        key_t_ref[...] = key_t

        def largest_norms(rows):
            rows = rows.astype(F32)
            rows = rows * rows
            sums = [
                jnp.sum(rows[head * HEAD_DIM : (head + 1) * HEAD_DIM], axis=0, keepdims=True)
                for head in range(HEADS)
            ]
            return jnp.max(jnp.concatenate(sums, axis=0), axis=1, keepdims=True)

        bound = jnp.max(largest_norms(query_t) * largest_norms(key_t))
        tame_s[0] = jnp.where(bound <= TAME * TAME, 1, 0)
        key_s[...] = dot(qk_ref[...], weight_ref[:, D : 2 * D]).astype(BF16)
        value = dot(x_ref[...], weight_ref[:, 2 * D : 3 * D]) + vector_ref[9:10, :]
        value_ref[...] = value.astype(BF16)
        value_t = dot(weight_t_s[2 * D :, :], x_t_ref[...]) + bias_s[:, 1:2]
        value_t = value_t.astype(BF16)
        for head in range(HEADS):
            value_s[head, :HEAD_DIM, :] = value_t[head * HEAD_DIM : (head + 1) * HEAD_DIM, :]
            value_s[head, HEAD_DIM:, :] = jnp.ones((16, SEQ), BF16)
        one, two, three = marks[row, 0], marks[row, 1], marks[row, 2]

        def number_of(shape, dim):
            here = (iota(shape, dim) + (HALF + begin)) & (SEQ - 1)
            return (
                jnp.where(here >= one, 1, 0)
                + jnp.where(here >= two, 1, 0)
                + jnp.where(here >= three, 1, 0)
            )

        lane = iota((HALF, LANES), 1)
        number = number_of((HALF, LANES), 0)
        mark_k[...] = jnp.where((number != lane) & (lane < 4), -FAR, 0.0).astype(BF16)
        number = number_of((LANES, HALF), 1)
        mark_q[...] = jnp.where(number == iota((LANES, HALF), 0), 1.0, 0.0).astype(BF16)

    lanes = pl.ds(pl.multiple_of(group * LANES, LANES), LANES)
    head_of = iota((1, LANES), 1) // HEAD_DIM
    keys_here = key_s[:, lanes]
    for at_head in range(GROUP):
        mask = jnp.where(head_of == at_head, 1.0, 0.0).astype(BF16)
        rows = slice(at_head * HALF, (at_head + 1) * HALF)
        first_s[rows, :] = keys_here[:HALF] * mask
        second_s[rows, :LANES] = keys_here[HALF:] * mask
        second_s[rows, LANES:] = mark_k[...]

    def scores_of(half, block, rows):
        at = half * HALF + block * QBLOCK
        query = query_t_ref[lanes, at : at + QBLOCK]
        if half == 0:
            return dot(first_s[rows, :], query)
        marks_here = mark_q[:, block * QBLOCK : (block + 1) * QBLOCK]
        return dot(second_s[rows, :], jnp.concatenate([query, marks_here], axis=0))

    def place_of(at_head, block):
        at = at_head * HALF + block * QBLOCK
        return slice(at, at + QBLOCK)

    def exps_plain(half, block):
        scores = scores_of(half, block, slice(0, GROUP * HALF))
        for at_head in range(GROUP):
            exps = jnp.exp2(scores[at_head * HALF : (at_head + 1) * HALF, :] * LOG2_E)
            exps_ref[0, 0, half, :, place_of(at_head, block)] = exps.astype(BF16)

    def exps_shifted(half, block):
        for at_head in range(GROUP):
            rows = slice(at_head * HALF, (at_head + 1) * HALF)
            largest = jnp.max(scores_of(half, block, rows), axis=0, keepdims=True)
            exps = jnp.exp2((scores_of(half, block, rows) - largest) * LOG2_E)
            exps_ref[0, 0, half, :, place_of(at_head, block)] = exps.astype(BF16)

    def finish(half, block):
        at = half * HALF + block * QBLOCK
        rows = slice(half * HALF, (half + 1) * HALF)
        for at_head in range(GROUP):
            out = dot(
                value_s[group * GROUP + at_head, :, rows],
                exps_ref[0, 0, half, :, place_of(at_head, block)],
            )
            inverse = 1.0 / out[HEAD_DIM : HEAD_DIM + 1, :]
            inverse_ref[0, at_head : at_head + 1, at : at + QBLOCK] = inverse
            out_t_ref[at_head * HEAD_DIM : (at_head + 1) * HEAD_DIM, at : at + QBLOCK] = (
                out[:HEAD_DIM, :] * inverse
            )

    def run(exps_of):
        items = [(half, block) for half in range(2) for block in range(HALF // QBLOCK)]
        for i in range(len(items) + 1):
            if i < len(items):
                exps_of(*items[i])
            if i >= 1:
                finish(*items[i - 1])

    @pl.when(tame_s[0] == 1)
    def _():
        run(exps_plain)

    @pl.when(tame_s[0] == 0)
    def _():
        run(exps_shifted)

    out_t = out_t_ref[...]
    mixed_t_ref[...] = out_t.astype(BF16)
    mixed_ref[...] = out_t.T.astype(BF16)


def attend_forward(marks, place, x, qk, x_t, qk_t, mine, other):
    total = x.shape[0]
    rows = total // SEQ
    by_row = lambda r, g, m, p: (r, 0)
    by_col = lambda r, g, m, p: (0, r)
    by_both = lambda r, g, m, p: (g, r)
    whole = lambda r, g, m, p: (0, 0)
    return pl.pallas_call(
        attend_kernel,
        out_shape=(
            jax.ShapeDtypeStruct((D, total), BF16),
            jax.ShapeDtypeStruct((total, D), BF16),
            jax.ShapeDtypeStruct((D, total), BF16),
            jax.ShapeDtypeStruct((D, total), F32),
            jax.ShapeDtypeStruct((2, 8, total), F32),
            jax.ShapeDtypeStruct((total, D), BF16),
            jax.ShapeDtypeStruct((D, total), BF16),
            jax.ShapeDtypeStruct((rows, 2, 2, HALF, GROUP * HALF), BF16),
            jax.ShapeDtypeStruct((D, 3 * D), BF16),
            jax.ShapeDtypeStruct((D, D), BF16),
            jax.ShapeDtypeStruct((VEC, D), F32),
        ),
        grid_spec=pltpu.PrefetchScalarGridSpec(
            num_scalar_prefetch=2,
            grid=(rows, 2),
            in_specs=[
                pl.BlockSpec((SEQ, D), by_row),
                pl.BlockSpec((SEQ, D), by_row),
                pl.BlockSpec((D, SEQ), by_col),
                pl.BlockSpec((D, SEQ), by_col),
                vspec(),
                vspec(),
            ],
            out_specs=[
                pl.BlockSpec((D, SEQ), by_col),
                pl.BlockSpec((SEQ, D), by_row),
                pl.BlockSpec((D, SEQ), by_col),
                pl.BlockSpec((LANES, SEQ), by_both),
                pl.BlockSpec((1, 8, SEQ), lambda r, g, m, p: (g, 0, r)),
                pl.BlockSpec((SEQ, LANES), lambda r, g, m, p: (r, g)),
                pl.BlockSpec((LANES, SEQ), by_both),
                pl.BlockSpec((1, 1, 2, HALF, GROUP * HALF), lambda r, g, m, p: (r, g, 0, 0, 0)),
                pl.BlockSpec((D, 3 * D), whole),
                pl.BlockSpec((D, D), whole),
                pl.BlockSpec((VEC, D), whole),
            ],
            scratch_shapes=[
                pltpu.VMEM((SEQ, D), BF16),
                pltpu.VMEM((HEADS, HEAD_DIM + 16, SEQ), BF16),
                pltpu.VMEM((HALF, LANES), BF16),
                pltpu.VMEM((LANES, HALF), BF16),
                pltpu.VMEM((GROUP * HALF, LANES), BF16),
                pltpu.VMEM((GROUP * HALF, 2 * LANES), BF16),
                pltpu.VMEM((3 * D, D), BF16),
                pltpu.VMEM((D, 8), F32),
                pltpu.SMEM((1,), jnp.int32),
            ],
        ),
        compiler_params=params(dimension_semantics=("arbitrary", "arbitrary")),
        cost_estimate=pl.CostEstimate(
            flops=20_000_000_000, bytes_accessed=30_000_000, transcendentals=8_400_000
        ),
        name="attend_forward",
    )(marks, place, x, qk, x_t, qk_t, mine, other)


def feed_kernel(
    marks,
    place,
    x_ref,
    back_ref,
    mixed_ref,
    mixed_t_ref,
    proj_ref,
    mine_ref,
    other_ref,
    vector_ref,
    block_ref,
    resid_ref,
    mixed_grad_ref,
    mine_out,
    other_out,
    proj_out,
    vector_out,
    first_w,
    second_w,
    first_acc,
    second_acc,
    proj_acc,
    vector_acc,
    hidden_s,
    slope_s,
    pre_s,
    first_low_s,
    branch_low_s,
    attended_s,
    block_s,
    eye_s,
):
    step = pl.program_id(0)
    core = place[2]
    tall = D // VDP
    wide = FF // (2 * VCHIP)

    @pl.when(step == 0)
    def _():
        first_acc[...] = jnp.zeros_like(first_acc)
        second_acc[...] = jnp.zeros_like(second_acc)
        proj_acc[...] = jnp.zeros_like(proj_acc)
        vector_acc[...] = jnp.zeros_like(vector_acc)
        eye_s[...] = jnp.where(iota((D, D), 0) == iota((D, D), 1), 1.0, 0.0).astype(BF16)
        for d in range(VDP):
            rows = slice(d * tall, (d + 1) * tall)
            for c in range(VCHIP):
                for ref, half in ((mine_ref, core), (other_ref, 1 - core)):
                    to = pl.ds(pl.multiple_of((2 * c + half) * wide, wide), wide)
                    first_w[rows, to] = ref[c, d, 0]
                    second_w[rows, to] = ref[c, d, 1]

    bias_o, bias_2 = vector_ref[10:11, :], vector_ref[11:12, :]
    gain_1, shift_1 = vector_ref[12:13, :], vector_ref[13:14, :]
    gain_2, shift_2 = vector_ref[14:15, :], vector_ref[15:16, :]
    at_row = pl.multiple_of((step % (SEQ // TILE)) * TILE, TILE)
    chunks = FF // CHUNK
    pair = 1

    def columns(at, count=1):
        return slice(at * CHUNK, (at + count) * CHUNK)

    def hidden_of(rows, at, pre):
        per = CHUNK // D
        bias = [vector_ref[at * per + i : at * per + i + 1, :] for i in range(per)]
        pre = (pre + jnp.concatenate(bias, axis=1)).astype(BF16)
        cube = BF16(GELU_A * GELU_B) * (pre * pre)
        gate = BF16(0.5) + BF16(0.5) * jnp.tanh(pre * (cube + BF16(GELU_A)))
        hidden_s[rows, columns(at)] = pre * gate
        slope_s[rows, columns(at)] = gate + (gate - gate * gate) * (
            pre * (BF16(6.0) * cube + BF16(2.0 * GELU_A))
        )

    def stages(sub):
        rows_at = sub * SUB
        rows = slice(rows_at, rows_at + SUB)
        attended = dot(mixed_ref[rows, :], proj_ref[...]) + bias_o
        norm_1, inverse_1 = norm_forward(x_ref[rows, :].astype(F32) + attended)
        first = norm_1 * gain_1 + shift_1
        first_low = first.astype(BF16)
        first_low_s[rows, :] = first_low
        yield
        branch = jnp.zeros((SUB, D), F32)
        for i in range(chunks + 1):
            if i < chunks:
                hidden_of(rows, i, dot(first_low, first_w[:, columns(i)]))
            if i >= pair and i % pair == 0:
                cols = columns(i - pair, pair)
                branch += dot_nt(hidden_s[rows, cols], second_w[:, cols])
            yield
        norm_2, inverse_2 = norm_forward(first + (branch + bias_2))
        block_s[pl.ds(at_row + rows_at, SUB), :] = norm_2 * gain_2 + shift_2
        back = back_ref[rows, :].astype(F32)
        vector_acc[14:15, :] += jnp.sum(back * norm_2, axis=0, keepdims=True)
        vector_acc[15:16, :] += jnp.sum(back, axis=0, keepdims=True)
        resid_2 = norm_backward(back * gain_2, norm_2, inverse_2)
        branch_low = resid_2.astype(BF16)
        branch_low_s[rows, :] = branch_low
        vector_acc[11:12, :] += jnp.sum(branch_low.astype(F32), axis=0, keepdims=True)
        yield
        first_back = resid_2
        if sub == 1:
            branch_t = dot_nt(eye_s[...], branch_low_s[...]).astype(BF16)
            first_t = dot_nt(eye_s[...], first_low_s[...]).astype(BF16)
            first_t = jnp.concatenate([first_t, jnp.ones((16, TILE), BF16)], axis=0)
        for i in range(chunks + 1):
            if i < chunks:
                pull = dot(branch_low, second_w[:, columns(i)]).astype(BF16)
                pre_s[rows, columns(i)] = pull * slope_s[rows, columns(i)]
                if sub == 1:
                    second_acc[:, columns(i)] += dot(branch_t, hidden_s[:, columns(i)])
            if i >= 1 and sub == 1:
                cols = columns(i - 1)
                first_acc[:, cols] += dot(first_t, pre_s[:, cols])
            if i >= pair and i % pair == 0:
                cols = columns(i - pair, pair)
                first_back += dot_nt(pre_s[rows, cols], first_w[:, cols])
            yield
        vector_acc[12:13, :] += jnp.sum(first_back * norm_1, axis=0, keepdims=True)
        vector_acc[13:14, :] += jnp.sum(first_back, axis=0, keepdims=True)
        resid_1 = norm_backward(first_back * gain_1, norm_1, inverse_1)
        resid_ref[rows, :] = resid_1
        attended_low = resid_1.astype(BF16)
        attended_s[rows, :] = attended_low
        vector_acc[10:11, :] += jnp.sum(attended_low.astype(F32), axis=0, keepdims=True)
        mixed_grad_ref[:, rows] = dot_nt(proj_ref[...], attended_low).astype(BF16)
        yield

    ahead, behind = stages(0), stages(1)
    for _ in range(LEAD):
        next(ahead)
    running = [ahead, behind]
    while running:
        for program in list(running):
            if next(program, 0) == 0:
                running.remove(program)
    proj_acc[...] += dot(mixed_t_ref[...], attended_s[...])

    @pl.when(step % (SEQ // TILE) == SEQ // TILE - 1)
    def _():
        block_ref[...] = pltpu.roll(block_s[...], marks[step // (SEQ // TILE), 3], 0)

    @pl.when(step == pl.num_programs(0) - 1)
    def _():
        for d in range(VDP):
            rows = slice(d * tall, (d + 1) * tall)
            for c in range(VCHIP):
                for ref, half in ((mine_out, core), (other_out, 1 - core)):
                    to = pl.ds(pl.multiple_of((2 * c + half) * wide, wide), wide)
                    ref[d, c, 0] = first_acc[rows, to].astype(BF16)
                    ref[d, c, 1] = second_acc[rows, to].astype(BF16)
        proj_out[...] = proj_acc[...]
        for at in range(FF // D):
            vector_out[at : at + 1, :] = first_acc[D : D + 1, at * D : (at + 1) * D]
        vector_out[FF // D :, :] = vector_acc[FF // D :, :]


def feed_forward(marks, place, x, back, mixed, mixed_t, proj, mine, other, vector):
    total = x.shape[0]
    tile = lambda i, m, p: (i, 0)
    by_col = lambda i, m, p: (0, i)
    whole = lambda i, m, p: (0, 0)
    whole5 = lambda i, m, p: (0, 0, 0, 0, 0)
    return pl.pallas_call(
        feed_kernel,
        out_shape=(
            jax.ShapeDtypeStruct((total, D), F32),
            jax.ShapeDtypeStruct((total, D), F32),
            jax.ShapeDtypeStruct((D, total), BF16),
            jax.ShapeDtypeStruct(mine.shape, BF16),
            jax.ShapeDtypeStruct(mine.shape, BF16),
            jax.ShapeDtypeStruct((D, D), F32),
            jax.ShapeDtypeStruct((VEC, D), F32),
        ),
        grid_spec=pltpu.PrefetchScalarGridSpec(
            num_scalar_prefetch=2,
            grid=(total // TILE,),
            in_specs=[
                pl.BlockSpec((TILE, D), tile),
                pl.BlockSpec((TILE, D), tile),
                pl.BlockSpec((TILE, D), tile),
                pl.BlockSpec((D, TILE), by_col),
                pl.BlockSpec((D, D), whole),
                vspec(),
                vspec(),
                pl.BlockSpec((VEC, D), whole),
            ],
            out_specs=[
                pl.BlockSpec((SEQ, D), lambda i, m, p: (i // (SEQ // TILE), 0)),
                pl.BlockSpec((TILE, D), tile),
                pl.BlockSpec((D, TILE), by_col),
                pl.BlockSpec(mine.shape, whole5),
                pl.BlockSpec(mine.shape, whole5),
                pl.BlockSpec((D, D), whole),
                pl.BlockSpec((VEC, D), whole),
            ],
            scratch_shapes=[
                pltpu.VMEM((D, FF), BF16),
                pltpu.VMEM((D, FF), BF16),
                pltpu.VMEM((D + 16, FF), F32),
                pltpu.VMEM((D, FF), F32),
                pltpu.VMEM((D, D), F32),
                pltpu.VMEM((VEC, D), F32),
                pltpu.VMEM((TILE, FF), BF16),
                pltpu.VMEM((TILE, FF), BF16),
                pltpu.VMEM((TILE, FF), BF16),
                pltpu.VMEM((TILE, D), BF16),
                pltpu.VMEM((TILE, D), BF16),
                pltpu.VMEM((TILE, D), BF16),
                pltpu.VMEM((SEQ, D), F32),
                pltpu.VMEM((D, D), BF16),
            ],
        ),
        compiler_params=params(dimension_semantics=("arbitrary",)),
        cost_estimate=pl.CostEstimate(
            flops=14_000_000_000, bytes_accessed=15_000_000, transcendentals=4_200_000
        ),
        name="feed_forward",
    )(marks, place, x, back, mixed, mixed_t, proj, mine, other, vector)


def pull_kernel(
    own,
    marks,
    place,
    grad_t_ref,
    query_t_ref,
    value_ref,
    key_t_ref,
    out_t_ref,
    inverse_ref,
    exps_ref,
    qk_t_ref,
    x_t_ref,
    weight_ref,
    proj_ref,
    *refs,
):
    if own:
        resid_ref, other_ref, pulled_ref, grads_ref, sums_ref = refs[:5]
    else:
        pulled_ref, grads_ref, sums_ref = refs[:3]
    dot_s, query_g, key_g, value_g, acc, sum_acc, value_s, scaled_t_s, score_s = refs[-9:]
    row = pl.program_id(0)
    begin = marks[row, 3]
    group = place[2] if own else 1 - place[2]

    @pl.when(row == 0)
    def _():
        acc[...] = jnp.zeros_like(acc)
        sum_acc[...] = jnp.zeros_like(sum_acc)

    grad_t = grad_t_ref[...].astype(F32)
    head_of = iota((1, LANES), 1) // HEAD_DIM
    for at_head in range(GROUP):
        heads = slice(at_head * HEAD_DIM, (at_head + 1) * HEAD_DIM)
        part = grad_t[heads, :] * inverse_ref[0, at_head : at_head + 1, :]
        dot_s[at_head : at_head + 1, :] = jnp.sum(part * out_t_ref[heads, :], axis=0, keepdims=True)
        part = part.astype(BF16)
        scaled_t_s[heads, :] = part
        mask = jnp.where(head_of == at_head, 1.0, 0.0).astype(BF16)
        for half in range(2):
            rows = slice(half * HALF, (half + 1) * HALF)
            to = slice(at_head * HALF, (at_head + 1) * HALF)
            value_s[half, to, :] = value_ref[rows, :] * mask

    def score_grads_of(half, block):
        at = half * HALF + block * QBLOCK
        pulls = dot(value_s[half], scaled_t_s[:, at : at + QBLOCK])
        for at_head in range(GROUP):
            cols = slice(at_head * HALF + block * QBLOCK, at_head * HALF + (block + 1) * QBLOCK)
            pull = pulls[at_head * HALF : (at_head + 1) * HALF, :]
            pull = (pull - dot_s[at_head : at_head + 1, at : at + QBLOCK]).astype(BF16)
            score_s[half, :, cols] = exps_ref[0, 0, half, :, cols] * pull

    def finish(half, at_head):
        cols = slice(at_head * HALF, (at_head + 1) * HALF)
        rows = slice(half * HALF, (half + 1) * HALF)
        heads = slice(at_head * HEAD_DIM, (at_head + 1) * HEAD_DIM)
        score_grad = score_s[half, :, cols]
        value_g[heads, rows] = dot_nt(scaled_t_s[heads, rows], exps_ref[0, 0, half, :, cols])
        query_g[heads, rows] = dot(key_t_ref[heads, rows], score_grad)
        key_g[heads, rows] = dot_nt(query_t_ref[heads, rows], score_grad)

    blocks = HALF // QBLOCK
    each = GROUP // blocks
    for block in range(blocks):
        score_grads_of(0, block)
    for block in range(blocks):
        score_grads_of(1, block)
        for at_head in range(each * block, each * (block + 1)):
            finish(0, at_head)
    for at_head in range(GROUP):
        finish(1, at_head)
    query_low = query_g[...].astype(BF16)
    both_low = jnp.concatenate([key_g[...].astype(BF16), value_g[...].astype(BF16)], axis=0)
    ones = jnp.ones((16, SEQ), BF16)
    sum_acc[0:1, :] += dot_nt(ones, query_low)[0:1, :] * SCALE
    sum_acc[1:2, :] += dot_nt(ones, both_low[LANES:, :])[0:1, :]
    qk_t = qk_t_ref[...]
    both = dot_nt(qk_t, jnp.concatenate([query_low, both_low[:LANES, :]], axis=0))
    acc[:, :LANES] += both[:, :LANES] * SCALE
    acc[:, LANES : 2 * LANES] += both[:, LANES:]
    acc[:, 2 * LANES :] += dot_nt(x_t_ref[...], both_low[LANES:, :])
    at = [pl.ds(pl.multiple_of(i * D + group * LANES, LANES), LANES) for i in range(3)]
    pulled = dot(weight_ref[:, at[0]], query_low) * SCALE + dot(
        jnp.concatenate([weight_ref[:, at[1]], weight_ref[:, at[2]]], axis=1), both_low
    )
    if own:
        pulled = (pulled + other_ref[...]).T
        pulled_ref[...] = pltpu.roll(resid_ref[...] + pulled, begin, 0)
    else:
        pulled_ref[...] = pulled

    @pl.when(row == pl.num_programs(0) - 1)
    def _():
        tall = D // VDP
        for d in range(VDP):
            rows = slice(d * tall, (d + 1) * tall)
            for c in range(3):
                grads_ref[d, c] = acc[rows, c * LANES : (c + 1) * LANES].astype(BF16)
            grads_ref[d, 3] = proj_ref[rows, :].astype(BF16)
        sums_ref[...] = sum_acc[...]


def attend_back(own, marks, place, grad_t, query_t, value, key_t, out_t, inverse, exps, qk_t, x_t, weight, proj, *more):
    total = value.shape[0]
    rows = total // SEQ
    pick = (lambda p: p[2]) if own else (lambda p: 1 - p[2])
    by_group = lambda r, m, p: (r, pick(p))
    by_row = lambda r, m, p: (r, 0)
    whole = lambda r, m, p: (0, 0)
    in_specs = [
        pl.BlockSpec((LANES, SEQ), lambda r, m, p: (pick(p), r)),
        pl.BlockSpec((LANES, SEQ), lambda r, m, p: (pick(p), r)),
        pl.BlockSpec((SEQ, LANES), by_group),
        pl.BlockSpec((LANES, SEQ), lambda r, m, p: (pick(p), r)),
        pl.BlockSpec((LANES, SEQ), lambda r, m, p: (pick(p), r)),
        pl.BlockSpec((1, 8, SEQ), lambda r, m, p: (pick(p), 0, r)),
        pl.BlockSpec((1, 1, 2, HALF, GROUP * HALF), lambda r, m, p: (r, pick(p), 0, 0, 0)),
        pl.BlockSpec((D, SEQ), lambda r, m, p: (0, r)),
        pl.BlockSpec((D, SEQ), lambda r, m, p: (0, r)),
        pl.BlockSpec((D, 3 * D), whole),
        pl.BlockSpec((D, LANES), lambda r, m, p: (0, pick(p))),
    ]
    by_col = pl.BlockSpec((D, SEQ), lambda r, m, p: (0, r))
    if own:
        in_specs += [pl.BlockSpec((SEQ, D), by_row), by_col]
    return pl.pallas_call(
        functools.partial(pull_kernel, own),
        out_shape=(
            jax.ShapeDtypeStruct((total, D) if own else (D, total), F32),
            jax.ShapeDtypeStruct((VDP, VCHIP, D // VDP, LANES), BF16),
            jax.ShapeDtypeStruct((8, LANES), F32),
        ),
        grid_spec=pltpu.PrefetchScalarGridSpec(
            num_scalar_prefetch=2,
            grid=(rows,),
            in_specs=in_specs,
            out_specs=[
                pl.BlockSpec((SEQ, D), by_row) if own else by_col,
                pl.BlockSpec((VDP, VCHIP, D // VDP, LANES), lambda r, m, p: (0, 0, 0, 0)),
                pl.BlockSpec((8, LANES), whole),
            ],
            scratch_shapes=[
                pltpu.VMEM((8, SEQ), F32),
                pltpu.VMEM((LANES, SEQ), F32),
                pltpu.VMEM((LANES, SEQ), F32),
                pltpu.VMEM((LANES, SEQ), F32),
                pltpu.VMEM((D, 3 * LANES), F32),
                pltpu.VMEM((8, LANES), F32),
                pltpu.VMEM((2, GROUP * HALF, LANES), BF16),
                pltpu.VMEM((LANES, SEQ), BF16),
                pltpu.VMEM((2, HALF, GROUP * HALF), BF16),
            ],
        ),
        compiler_params=params(dimension_semantics=("arbitrary",)),
        cost_estimate=pl.CostEstimate(
            flops=18_000_000_000, bytes_accessed=15_000_000, transcendentals=0
        ),
        name="attend_back",
    )(marks, place, grad_t, query_t, value, key_t, out_t, inverse, exps, qk_t, x_t, weight, proj, *more)


def sums_by_group(place, sums_own, sums_other):
    first = place[2] == 0
    return (
        jnp.where(first, sums_own, sums_other),
        jnp.where(first, sums_other, sums_own),
    )


def two_terms(rows):
    high = rows.astype(BF16)
    return jnp.concatenate([high.astype(F32), rows - high.astype(F32)], axis=0)


def column_to_row(columns, rows):
    lane = iota((rows, LANES), 1)
    wide = jnp.zeros((rows, LANES), F32)
    for i, column in enumerate(columns):
        wide = jnp.where(lane == i, column, wide)
    return wide.T[:8, :]


def total_of(array):
    return jnp.sum(jnp.sum(array, axis=0, keepdims=True), axis=1, keepdims=True)


def tail_ffn_kernel(place, ffn_ref, rows_1, rows_2, last_ref, grad_ref, stat_ref):
    lane = iota((1, LANES), 1)
    piece, across = [], []
    for kind in range(2):
        total = ffn_ref[0, kind].astype(F32)
        for at in range(1, VDP * VCHIP):
            total = total + ffn_ref[at, kind].astype(F32)
        grad_ref[kind] = total
        square = total * total + EPS_ONE
        down = jnp.sum(square, axis=0, keepdims=True)
        piece += [down[:, :LANES], down[:, LANES:]]
        across.append(jnp.sum(square, axis=1, keepdims=True))
    across = column_to_row(across, total.shape[0])
    across = jnp.concatenate([across[0:1], across[1:2]], axis=1)
    olds = jnp.zeros((1, LANES), F32)
    for i, ref in enumerate((rows_1, rows_2)):
        olds = jnp.where(lane == i, jnp.sum(ref[...], axis=1, keepdims=True), olds)
    stat_ref[...] = jnp.concatenate([across] + piece + [olds, jnp.zeros((2, LANES), F32)], axis=0)


def tail_send_kernel(
    place, mine_ref, got_ref, vector_ref, own_ref, other_ref, stat_ref, stat_other_ref, send_ref
):
    tall = D // VDP
    low, high = sums_by_group(place, own_ref[...], other_ref[...])
    vector = jnp.concatenate(
        [
            vector_ref[:8, :],
            jnp.concatenate([low[:2], high[:2]], axis=1),
            vector_ref[10:, :],
        ],
        axis=0,
    )
    stat = jnp.concatenate([stat_ref[0:1, :] + stat_other_ref[0:1, :], stat_ref[1:6, :]], axis=0)
    stat = two_terms(stat)
    rows = VEC // VDP
    for d in range(VDP):
        for c in range(VCHIP):
            at = d * VCHIP + c
            both = mine_ref[d, c].astype(F32) + got_ref[d, c].astype(F32)
            send_ref[at, :tall, :] = both.astype(BF16)
            part = vector[d * rows : (d + 1) * rows, c * 64 : (c + 1) * 64]
            part = jnp.concatenate([part, jnp.zeros((rows, LANES - 64), F32)], axis=1)
            send_ref[at, tall:, :] = jnp.concatenate([part, stat], axis=0).astype(BF16)


def tail_reduce_kernel(
    place,
    got_ref,
    ffn_grad_ref,
    attn_ref,
    first_ref,
    second_ref,
    rows_0,
    rows_1,
    rows_2,
    cols_0,
    cols_1,
    cols_2,
    vector_ref,
    moment_ref,
    grad_ref,
    update_1,
    update_2,
    rows_out_1,
    rows_out_2,
    cols_out_1,
    cols_out_2,
    send_ref,
):
    decay = 1.0 - STEP ** (-0.8)
    chip = place[1]
    dp = place[0]
    tall = attn_ref.shape[0]
    rows, width = vector_ref.shape
    pieces = VDP * VCHIP
    lane = iota((1, LANES), 1)
    total = got_ref[0, :tall, :].astype(F32)
    part = got_ref[0, tall:, :].astype(F32)[:rows]
    for at in range(1, pieces):
        total = total + got_ref[at, :tall, :].astype(F32)
        part = part + got_ref[at, tall:, :].astype(F32)[:rows]
    grad_ref[...] = total
    low = total.astype(BF16)

    def stat_of(at):
        both = got_ref[pl.ds(at, 1), tall:, :][0].astype(F32)[rows:]
        return both[:6] + both[6:12]

    every = jnp.zeros((1, LANES), F32)
    olds = jnp.zeros((1, LANES), F32)
    mine = jnp.zeros((1, LANES), F32)
    down = jnp.zeros((6, LANES), F32)
    for d in range(VDP):
        down = down + stat_of(d * VCHIP + chip)
        for c in range(VCHIP):
            stat = stat_of(d * VCHIP + c)
            every = every + stat[0:1]
            if c == 0:
                olds = olds + stat[5:6]
    for c in range(VCHIP):
        mine = mine + stat_of(dp * VCHIP + c)[0:1]
    row_total = tall * VDP
    new_rows, means = [], []
    for i, ref in enumerate((rows_1, rows_2)):
        count = first_ref.shape[1] * 2 * VCHIP
        new_rows.append(decay * ref[...] + (1.0 - decay) * (mine[:, i * tall : (i + 1) * tall] / count))
        old = jnp.sum(jnp.where(lane == i, olds, 0.0), axis=1, keepdims=True)
        fresh = jnp.sum(every[:, i * tall : (i + 1) * tall], axis=1, keepdims=True)
        means.append((decay * old + (1.0 - decay) * (fresh / count)) / row_total)
    tile = jnp.concatenate(new_rows + [jnp.zeros((6, tall), F32)], axis=0)
    rows_out_1[...] = new_rows[0]
    rows_out_2[...] = new_rows[1]
    tile = jnp.concatenate([tile, jnp.zeros((8, LANES - tall), F32)], axis=1)
    turned = jnp.concatenate([tile, jnp.zeros((LANES - 8, LANES), F32)], axis=0).T
    scalars = jnp.zeros((1, LANES), F32)
    for i, (old_ref, out_ref, to) in enumerate(
        ((cols_1, cols_out_1, update_1), (cols_2, cols_out_2, update_2))
    ):
        sums = jnp.concatenate([down[1 + 2 * i : 2 + 2 * i], down[2 + 2 * i : 3 + 2 * i]], axis=1)
        cols = decay * old_ref[...] + (1.0 - decay) * (sums / row_total)
        out_ref[...] = cols
        grad = ffn_grad_ref[i]
        update = grad * lax.rsqrt(turned[:tall, i : i + 1] * cols / means[i])
        to[...] = update
        scalars = jnp.where(lane == 67 + i, total_of(update * update), scalars)
    for i, ref in enumerate((attn_ref, first_ref, second_ref)):
        weight = ref[...]
        scalars = jnp.where(lane == 64 + i, total_of(weight * weight), scalars)
    scalars = jnp.concatenate([rows_0[...], scalars[:, tall:]], axis=1)
    vector = vector_ref[...]
    power = jnp.sum(vector * vector, axis=1, keepdims=True)
    lines = jnp.concatenate(
        [part[:, :64], moment_ref[...], jnp.broadcast_to(power, (rows, LANES - 64 - width))], axis=1
    )
    piece = jnp.concatenate(
        [two_terms(lines), two_terms(jnp.concatenate([cols_0[...], scalars], axis=0))]
        + [jnp.zeros((4, LANES), F32)],
        axis=0,
    ).astype(BF16)
    for at in range(pieces):
        send_ref[at, :tall, :] = low
        send_ref[at, tall:, :] = piece


def tail_apply_kernel(
    place,
    mine_ref,
    other_ref,
    grad_ref,
    update_1,
    update_2,
    weight_0,
    weight_1,
    weight_2,
    rows_0,
    cols_0,
    vector_ref,
    moment_ref,
    new_0,
    new_1,
    new_2,
    rows_out,
    cols_out,
    vector_grad_ref,
    moment_out,
    vector_out,
    sums_s,
    rows_s,
):
    decay = 1.0 - STEP ** (-0.8)
    dp, chip, core = place[0], place[1], place[2]
    tall = weight_0.shape[0]
    rows, width = vector_ref.shape
    fsdp = 2 * VCHIP
    lane = iota((1, LANES), 1)
    refs = (mine_ref, other_ref)
    row_total = float(tall * VDP)
    col_total = float(LANES * fsdp)

    def lines_of(ref, at):
        both = ref[at, tall:, :].astype(F32)
        return both[0:4] + both[4:8], both[8:10] + both[10:12]

    scalars = jnp.zeros((1, LANES), F32)
    for ref in refs:
        for at in range(VDP * VCHIP):
            scalars = scalars + lines_of(ref, at)[1][1:2]
    scalar = lambda at: jnp.sum(jnp.where(lane == at, scalars, 0.0), axis=1, keepdims=True)

    tile, fresh = [], []
    for d in range(VDP):
        wide = jnp.zeros((tall, LANES), F32)
        for ref in refs:
            for c in range(VCHIP):
                block = ref[d * VCHIP + c, :tall, :].astype(F32)
                wide = wide + (block * block + EPS_ONE)
        fresh.append(jnp.sum(wide, axis=1, keepdims=True))
        tile.append(lines_of(mine_ref, d * VCHIP)[1][1:2])
    tile = jnp.concatenate(tile + [jnp.zeros((LANES - VDP, LANES), F32)], axis=0).T
    mean = jnp.zeros((1, 1), F32)
    new_rows = []
    for d in range(VDP):
        new = decay * tile[:tall, d : d + 1] + (1.0 - decay) * (fresh[d] / col_total)
        new_rows.append(1.0 / new)
        mean = mean + jnp.sum(new, axis=0, keepdims=True)
        sums_s[d] = jnp.broadcast_to(fresh[d], (tall, LANES))
    mean = mean / row_total
    mine = sums_s[pl.ds(dp, 1)][0]
    rows_s[...] = mine.T
    rows_new = decay * rows_0[...] + (1.0 - decay) * (rows_s[0:1, :tall] / col_total)
    rows_out[...] = rows_new
    power = jnp.zeros((1, 1), F32)
    for half, ref in enumerate(refs):
        for c in range(VCHIP):
            down = jnp.zeros((tall, LANES), F32)
            weighted = jnp.zeros((tall, LANES), F32)
            for d in range(VDP):
                block = ref[d * VCHIP + c, :tall, :].astype(F32)
                square = block * block
                down = down + (square + EPS_ONE)
                weighted = weighted + square * new_rows[d]
            down = jnp.sum(down, axis=0, keepdims=True)
            old = lines_of(ref, c)[1][0:1]
            cols = decay * old + (1.0 - decay) * (down / row_total)
            weighted = jnp.sum(weighted, axis=0, keepdims=True) / cols
            power = power + jnp.sum(weighted, axis=1, keepdims=True)
            if half == 0:
                sums_s[VDP + c] = jnp.broadcast_to(down, (tall, LANES))
    power = power * mean
    down = sums_s[pl.ds(VDP + chip, 1)][0][0:1, :]
    cols_new = decay * cols_0[...] + (1.0 - decay) * (down / row_total)
    cols_out[...] = cols_new
    column = jnp.concatenate(
        [
            jnp.concatenate([rows_new, jnp.zeros((1, LANES - tall), F32)], axis=1),
            jnp.zeros((LANES - 1, LANES), F32),
        ],
        axis=0,
    ).T[:tall, 0:1]
    update_0 = grad_ref[...] * lax.rsqrt(column * cols_new / mean)
    powers = (power, scalar(67), scalar(68))
    for i, (update, weight, new) in enumerate(
        (
            (update_0, weight_0, new_0),
            (update_1[...], weight_1, new_1),
            (update_2[...], weight_2, new_2),
        )
    ):
        entries = float(weight.shape[0] * weight.shape[1] * VDP * fsdp)
        clip = jnp.maximum(1.0, jnp.sqrt(powers[i] / entries) / CLIP_LIMIT)
        rate = STEP_RATE * jnp.maximum(EPS_TWO, jnp.sqrt(scalar(64 + i) / entries))
        new[...] = weight[...] - rate / clip * update
    powers, sizes = [], []
    for d in range(VDP):
        power = jnp.zeros((rows, 1), F32)
        size = jnp.zeros((rows, 1), F32)
        for c in range(VCHIP):
            at = d * VCHIP + c
            first, second = lines_of(mine_ref, at)[0], lines_of(other_ref, at)[0]
            both = first[:, :64] + second[:, :64]
            size = size + first[:, LANES - 1 :] + second[:, LANES - 1 :]
            near = jnp.where(core == 0, first[:, 64 : 64 + width], second[:, 64 : 64 + width])
            far = jnp.where(core == 0, second[:, 64 : 64 + width], first[:, 64 : 64 + width])
            moment = jnp.concatenate([near, far], axis=1)
            moment = decay * moment + (1.0 - decay) * (both * both + EPS_ONE)
            power = power + jnp.sum(both * both / moment, axis=1, keepdims=True)
            wide = jnp.concatenate([both, jnp.zeros((rows, LANES - 64), F32)], axis=1)
            sums_s[2 * VDP + at, :rows, :] = wide
        powers.append(power)
        sizes.append(size)
    both = sums_s[pl.ds(2 * VDP + dp * VCHIP + chip, 1), :rows, :][0]
    vector_grad = jnp.where(core == 0, both[:, :width], both[:, width : 2 * width])
    vector_grad_ref[...] = vector_grad
    moment = decay * moment_ref[...] + (1.0 - decay) * (vector_grad * vector_grad + EPS_ONE)
    moment_out[...] = moment
    step = vector_grad * lax.rsqrt(moment)
    bias = VDP // 2
    bias_power = sum(jnp.sum(power, axis=0, keepdims=True) for power in powers[:bias])
    bias_size = sum(jnp.sum(size, axis=0, keepdims=True) for size in sizes[:bias])
    power, size = powers[bias], sizes[bias]
    for d in range(bias + 1, VDP):
        power = jnp.where(dp == d, powers[d], power)
        size = jnp.where(dp == d, sizes[d], size)
    is_bias = dp < bias
    power = jnp.where(is_bias, bias_power, power)
    size = jnp.where(is_bias, bias_size, size)
    count = jnp.where(is_bias, float(FF), float(D))
    clip = jnp.maximum(1.0, jnp.sqrt(power / count) / CLIP_LIMIT)
    rate = STEP_RATE * jnp.maximum(EPS_TWO, jnp.sqrt(size / count))
    vector_out[...] = vector_ref[...] - rate / clip * step


def whole_call(kernel, name, place, outs, *operands, scratch=()):
    return pl.pallas_call(
        kernel,
        out_shape=[jax.ShapeDtypeStruct(shape, kind) for shape, kind in outs],
        in_specs=[pl.BlockSpec(memory_space=pltpu.SMEM)] + [vspec()] * len(operands),
        out_specs=[vspec()] * len(outs),
        scratch_shapes=list(scratch),
        compiler_params=params(16),
        name=name,
    )(place, *operands)


def core_swap(block):
    return lax.ppermute(block, "core", [(0, 1), (1, 0)])


def exchange(blocks, axes):
    return lax.all_to_all(blocks, axes, split_axis=0, concat_axis=0, tiled=True)


def after(value, *earlier, mib=8):
    return pl.pallas_call(
        lambda *refs: None,
        out_shape=jax.ShapeDtypeStruct(value.shape, value.dtype),
        in_specs=[pl.BlockSpec(memory_space=pltpu.HBM)] * (1 + len(earlier)),
        out_specs=pl.BlockSpec(memory_space=pltpu.HBM),
        input_output_aliases={0: 0},
        compiler_params=params(mib),
        name="after",
    )(value, *earlier)


def pair_kernel(mine_ref, got_ref, out_ref):
    out_ref[...] = (mine_ref[...].astype(F32) + got_ref[...].astype(F32)).astype(BF16)


def pair_sum(mine, got):
    return pl.pallas_call(
        pair_kernel,
        out_shape=jax.ShapeDtypeStruct(mine.shape, BF16),
        in_specs=[vspec(), vspec()],
        out_specs=vspec(),
        compiler_params=params(16),
        name="pair_sum",
    )(mine, got)


CHIPS = ("dp", "chip")
ALL = ("dp", "chip", "core")


def layer(place, weights, segment_ids, tokens, cotangent, ffn_weights, send_core, send_ffn):
    table = jnp.asarray(encode_table())
    qk, x, qk_t, x_t, back, marks = place_tokens(segment_ids, tokens, cotangent, table)
    query_t, value, key_t, out_t, inverse, mixed, mixed_t, exps, weight, proj, vector = attend_forward(
        marks, place, x, qk, x_t, qk_t, *weights(marks)
    )
    ffn_mine, ffn_other = ffn_weights(marks, vector)
    block_out, resid, grad_t, ffn_mine, ffn_other, proj_g, vector_g = feed_forward(
        marks, place, x, back, mixed, mixed_t, proj, ffn_mine, ffn_other, vector
    )
    ffn_got, grad_t = send_ffn(ffn_mine, ffn_other, grad_t)
    shared = (marks, place, grad_t, query_t, value, key_t, out_t, inverse, exps, qk_t, x_t, weight, proj_g)
    pulled, grads_other, sums_other = attend_back(False, *shared)
    attn_got = send_core(grads_other)
    input_grad, grads_own, sums_own = attend_back(True, *shared, resid, pulled)
    return block_out, input_grad, grads_own, grads_other, attn_got, sums_own, sums_other, vector_g, ffn_got


def body(
    tokens,
    cotangent,
    segment_ids,
    attn_weight,
    ffn_in,
    ffn_out,
    vectors,
    attn_rows,
    attn_cols,
    in_rows,
    in_cols,
    out_rows,
    out_cols,
    vector_moment,
):
    place = jnp.stack([lax.axis_index("dp"), lax.axis_index("chip"), lax.axis_index("core")])
    place = place.astype(jnp.int32)
    pieces = VDP * VCHIP
    tall, wide = attn_weight.shape
    rows_v, cols_v = vectors.shape
    split = lambda array: array.reshape((VDP, VCHIP) + array.shape[1:])
    attn_mine = exchange(pack_attn(place, attn_weight, vectors), CHIPS)

    ffn_low = jnp.stack([ffn_in, ffn_out]).astype(BF16)
    parts = [
        lax.ppermute(ffn_low, "dp", [(i, i ^ step) for i in range(VDP)]) for step in range(1, VDP)
    ]
    ffn_sent = pack_ffn(place, ffn_in, ffn_out, parts)

    def attn_weights(marks):
        mine = split(after(attn_mine, marks, ffn_sent))
        return mine, core_swap(mine)

    def ffn_weights(marks, vector):
        got = exchange(after(ffn_sent, marks), "chip")
        ffn_mine = after(got, vector)
        return ffn_mine, core_swap(ffn_mine)

    def send_ffn(mine, other, grad_t):
        both = pair_sum(mine, core_swap(other))
        got = exchange(both.reshape((pieces,) + mine.shape[2:]), CHIPS)
        return got, after(grad_t, both, mib=56)

    (
        block_out,
        input_grad,
        grads_own,
        grads_other,
        attn_got,
        sums_own,
        sums_other,
        vector_g,
        ffn_got,
    ) = layer(place, attn_weights, segment_ids, tokens, cotangent, ffn_weights, core_swap, send_ffn)
    lay = lambda stat: stat.reshape(1, -1)
    rows_old = (lay(attn_rows), lay(in_rows), lay(out_rows))
    cols_old = (lay(attn_cols), lay(in_cols), lay(out_cols))
    weights_old = (attn_weight, ffn_in, ffn_out)
    ffn_grad, stat = whole_call(
        tail_ffn_kernel,
        "tail_ffn",
        place,
        [((2,) + ffn_in.shape, F32), ((8, LANES), F32)],
        ffn_got,
        *rows_old[1:],
        sums_own,
    )
    (sent,) = whole_call(
        tail_send_kernel,
        "tail_send",
        place,
        [((pieces, tall + VROWS, LANES), BF16)],
        grads_own,
        attn_got,
        vector_g,
        sums_own,
        sums_other,
        stat,
        core_swap(stat),
    )
    got = exchange(sent, CHIPS)
    attn_grad, update_1, update_2, rows_new_1, rows_new_2, cols_new_1, cols_new_2, sent = whole_call(
        tail_reduce_kernel,
        "tail_reduce",
        place,
        [
            (attn_weight.shape, F32),
            (ffn_in.shape, F32),
            (ffn_out.shape, F32),
            (rows_old[1].shape, F32),
            (rows_old[2].shape, F32),
            (cols_old[1].shape, F32),
            (cols_old[2].shape, F32),
            ((pieces, tall + VROWS, LANES), BF16),
        ],
        got,
        ffn_grad,
        *weights_old,
        *rows_old,
        *cols_old,
        vectors,
        vector_moment,
    )
    mine = exchange(sent, CHIPS)
    attn_new, in_new, out_new, rows_new_0, cols_new_0, vector_grad, moment_new, vectors_new = whole_call(
        tail_apply_kernel,
        "tail_apply",
        place,
        [
            (attn_weight.shape, F32),
            (ffn_in.shape, F32),
            (ffn_out.shape, F32),
            (rows_old[0].shape, F32),
            (cols_old[0].shape, F32),
            (vectors.shape, F32),
            (vectors.shape, F32),
            (vectors.shape, F32),
        ],
        mine,
        core_swap(mine),
        attn_grad,
        update_1,
        update_2,
        *weights_old,
        rows_old[0],
        cols_old[0],
        vectors,
        vector_moment,
        scratch=[
            pltpu.VMEM((2 * VDP + pieces, tall, LANES), F32),
            pltpu.VMEM((LANES, tall), F32),
        ],
    )
    return (
        block_out,
        input_grad,
        attn_grad,
        ffn_grad[0],
        ffn_grad[1],
        vector_grad,
        rows_new_0.reshape(-1),
        cols_new_0.reshape(-1),
        rows_new_1.reshape(-1),
        cols_new_1.reshape(-1),
        rows_new_2.reshape(-1),
        cols_new_2.reshape(-1),
        moment_new,
        attn_new,
        in_new,
        out_new,
        vectors_new,
    )


def gather_all(block):
    shape = (lax.axis_size("dp"), lax.axis_size("chip") * 2)
    count = shape[0] * shape[1]
    got = exchange(jnp.broadcast_to(block[None], (count,) + block.shape), ALL)
    return got.reshape(shape + block.shape)


def unblock(parts):
    dp_count, fsdp_count, rows, cols = parts.shape
    return parts.transpose(0, 2, 1, 3).reshape(dp_count * rows, fsdp_count * cols)


def scatter_sum(full):
    dp_count = lax.axis_size("dp")
    fsdp_count = lax.axis_size("chip") * 2
    rows, cols = full.shape
    by_col = full.astype(BF16).reshape(rows, fsdp_count, cols // fsdp_count).transpose(1, 0, 2)
    got = exchange(by_col, ("chip", "core"))
    part = jnp.sum(got.astype(F32), axis=0).astype(BF16)
    by_row = part.reshape(dp_count, rows // dp_count, cols // fsdp_count)
    return jnp.sum(exchange(by_row, "dp").astype(F32), axis=0)


def body_any(
    tokens,
    cotangent,
    segment_ids,
    attn_weight,
    ffn_in,
    ffn_out,
    vectors,
    attn_rows,
    attn_cols,
    in_rows,
    in_cols,
    out_rows,
    out_cols,
    vector_moment,
):
    dp_count = lax.axis_size("dp")
    fsdp_count = lax.axis_size("chip") * 2
    dp_place = lax.axis_index("dp")
    fsdp_place = lax.axis_index("chip") * 2 + lax.axis_index("core")
    rows_w = attn_weight.shape[0]
    rows_v = vectors.shape[0]
    place = jnp.zeros((3,), jnp.int32)
    full_attn = unblock(gather_all(attn_weight.astype(BF16)))
    full_vector = unblock(gather_all(vectors.astype(BF16)))
    full_ffn = jnp.stack(
        [unblock(gather_all(ffn_in.astype(BF16))), unblock(gather_all(ffn_out.astype(BF16)))]
    )
    tall = D // VDP
    cut = full_attn.reshape(VDP, tall, VCHIP, 2, LANES).transpose(3, 0, 2, 1, 4)
    lines = full_vector.reshape(VDP, VEC // VDP, 2, LANES).transpose(0, 2, 1, 3)
    lines = lines.reshape(VDP, 1, 2 * VEC // VDP, LANES)
    lines = jnp.pad(lines, ((0, 0), (0, VCHIP - 1), (0, VROWS - 2 * VEC // VDP), (0, 0)))
    weights = (
        jnp.concatenate([cut[0], lines], axis=2),
        jnp.concatenate([cut[1], jnp.zeros_like(lines)], axis=2),
    )
    ffn_cut = full_ffn.reshape(2, VDP, tall, VCHIP, 2, FF // (2 * VCHIP))
    ffn_cut = ffn_cut.transpose(4, 3, 1, 0, 2, 5)
    (
        block_out,
        input_grad,
        grads_own,
        grads_other,
        _,
        sums_own,
        sums_other,
        vector_g,
        ffn_got,
    ) = layer(
        place,
        lambda marks: weights,
        segment_ids,
        tokens,
        cotangent,
        lambda marks, vector: (ffn_cut[0], ffn_cut[1]),
        lambda block: block,
        lambda mine, other, grad_t: (jnp.stack([mine, other]), grad_t),
    )
    attn_full = jnp.stack([grads_own, grads_other]).transpose(1, 3, 2, 0, 4).reshape(D, 4 * D)
    ffn_full = ffn_got.transpose(3, 1, 4, 2, 0, 5).reshape(2, D, FF)
    sums = jnp.concatenate([sums_own[:2], sums_other[:2]], axis=1)
    vector_full = jnp.concatenate([vector_g[:8], sums, vector_g[10:]], axis=0)
    attn_grad = scatter_sum(attn_full)
    in_grad = scatter_sum(ffn_full[0])
    out_grad = scatter_sum(ffn_full[1])
    vector_grad = scatter_sum(vector_full)

    decay = 1.0 - STEP ** (-0.8)
    gradients = (attn_grad, in_grad, out_grad)
    weights_old = (attn_weight, ffn_in, ffn_out)
    rows_old = (attn_rows, in_rows, out_rows)
    cols_old = (attn_cols, in_cols, out_cols)
    moment_new = decay * vector_moment + (1.0 - decay) * (vector_grad * vector_grad + EPS_ONE)
    vector_step = vector_grad * lax.rsqrt(moment_new)
    squares = [gradient * gradient + EPS_ONE for gradient in gradients]
    pieces = []
    for square in squares:
        pieces.append(jnp.sum(square, axis=1))
    for square in squares:
        pieces.append(jnp.sum(square, axis=0))
    pieces.append(jnp.sum(vector_step * vector_step, axis=1))
    pieces.append(jnp.sum(vectors * vectors, axis=1))
    pieces.append(jnp.stack([jnp.sum(weight * weight) for weight in weights_old]))
    pieces.append(jnp.stack([jnp.sum(old) for old in rows_old]))
    sizes = [piece.shape[0] for piece in pieces]
    flat = jnp.concatenate(pieces)
    flat = jnp.pad(flat, (0, -flat.shape[0] % 1024)).reshape(-1, LANES)
    got = gather_all(flat).reshape(dp_count, fsdp_count, -1)
    offsets = [0]
    for length in sizes:
        offsets.append(offsets[-1] + length)
    take = lambda i: got[:, :, offsets[i] : offsets[i + 1]]
    rows_new, cols_new, row_means, entries = [], [], [], []
    for i in range(3):
        count_rows = rows_w * dp_count
        count_cols = weights_old[i].shape[1] * fsdp_count
        entries.append(float(count_rows * count_cols))
        row_all = jnp.sum(take(i), axis=1)
        mine = lax.dynamic_index_in_dim(row_all, dp_place, 0, keepdims=False)
        rows_new.append(decay * rows_old[i] + (1.0 - decay) * mine / count_cols)
        col_all = jnp.sum(take(3 + i), axis=0)
        mine = lax.dynamic_index_in_dim(col_all, fsdp_place, 0, keepdims=False)
        cols_new.append(decay * cols_old[i] + (1.0 - decay) * mine / count_rows)
        old_total = jnp.sum(take(9)[:, 0, i])
        row_means.append(
            (decay * old_total + (1.0 - decay) * jnp.sum(row_all) / count_cols) / count_rows
        )
    step_rows = jnp.sum(take(6), axis=1).reshape(-1)
    weight_rows = jnp.sum(take(7), axis=1).reshape(-1)
    weight_totals = jnp.sum(take(8), axis=(0, 1))
    updates = []
    for i in range(3):
        second = rows_new[i][:, None] * cols_new[i][None, :] / row_means[i]
        updates.append(gradients[i] * lax.rsqrt(second))
    flat = jnp.stack([jnp.sum(update * update) for update in updates])
    flat = jnp.broadcast_to(jnp.pad(flat, (0, 5))[:, None], (8, LANES))
    totals = jnp.sum(gather_all(flat)[:, :, :, 0], axis=(0, 1))
    new_weights = []
    for i in range(3):
        clip_factor = jnp.maximum(1.0, jnp.sqrt(totals[i] / entries[i]) / CLIP_LIMIT)
        step_size = STEP_RATE * jnp.maximum(EPS_TWO, jnp.sqrt(weight_totals[i] / entries[i]))
        new_weights.append(weights_old[i] - step_size / clip_factor * updates[i])
    bias_rows = FF // D
    row_places = jnp.arange(VEC)
    counts = jnp.where(row_places < bias_rows, float(FF), float(D))
    grouped_updates = jnp.where(row_places < bias_rows, jnp.sum(step_rows[:bias_rows]), step_rows)
    grouped_weights = jnp.where(row_places < bias_rows, jnp.sum(weight_rows[:bias_rows]), weight_rows)
    clip_rows = jnp.maximum(1.0, jnp.sqrt(grouped_updates / counts) / CLIP_LIMIT)
    step_sizes = STEP_RATE * jnp.maximum(EPS_TWO, jnp.sqrt(grouped_weights / counts))
    factor_rows = lax.dynamic_slice_in_dim(step_sizes / clip_rows, dp_place * rows_v, rows_v)
    vectors_new = vectors - factor_rows[:, None] * vector_step
    return (
        block_out,
        input_grad,
        attn_grad,
        in_grad,
        out_grad,
        vector_grad,
        rows_new[0],
        cols_new[0],
        rows_new[1],
        cols_new[1],
        rows_new[2],
        cols_new[2],
        moment_new,
        new_weights[0],
        new_weights[1],
        new_weights[2],
        vectors_new,
    )


def solution(mesh):
    dp_count, fsdp_count = mesh.shape["dp"], mesh.shape["fsdp"]
    inner = jax.sharding.Mesh(mesh.devices.reshape(dp_count, fsdp_count // 2, 2), ALL)
    fsdp = ("chip", "core")
    split = P(ALL, None)
    block = P("dp", fsdp)
    stats = (P("dp"), P(fsdp)) * 3
    plain = dp_count == VDP and fsdp_count == 2 * VCHIP
    return jax.shard_map(
        body if plain else body_any,
        mesh=inner,
        in_specs=(split,) * 3 + (block,) * 4 + stats + (block,),
        out_specs=(split,) * 2 + (block,) * 4 + stats + (block,) * 5,
        check_vma=False,
    )
```

```python
import functools
import math

import jax
import jax.numpy as jnp
import numpy as np
from jax import lax
from jax.experimental import pallas as pl
from jax.experimental.pallas import tpu as pltpu
from jax.sharding import PartitionSpec as P

D = 256
FF = 2048
HEADS = 8
HEAD_DIM = 32
SEQ = 1024
HALF = 512
GROUP = 4
LANES = 128
QBLOCK = 512
WGRID = 32
STEP = 10
VEC = 16
TILE = 1024
CHUNK = 256
SUB = 512
LEAD = 5
STRIP = 64
VDP = 4
VCHIP = 4
VROWS = 16

EPS_NORM = 1e-05
EPS_ONE = 1e-30
EPS_TWO = 0.001
CLIP_LIMIT = 1.0
STEP_RATE = 0.3
FAR = 1e30
TAME = 40.0
LOG2_E = math.log2(math.e)
SCALE = HEAD_DIM ** (-0.5)
GELU_A = math.sqrt(2.0 / math.pi)
GELU_B = 0.044715
F32 = jnp.float32
BF16 = jnp.bfloat16
MIB = 1024 * 1024


def dot(left, right):
    return jnp.dot(left, right, preferred_element_type=F32)


def dot_nt(left, right):
    return lax.dot_general(left, right, (((1,), (1,)), ((), ())), preferred_element_type=F32)


def encode_table():
    half = D // 2
    feature = np.arange(half)
    freq = np.exp(
        (2 * (feature // 2)).astype(np.float32) * np.float32(-math.log(10000.0) / half)
    ).astype(np.float32)
    angles = np.arange(1, WGRID + 1, dtype=np.float32)[:, None] * freq[None, :]
    table = np.where(feature % 2 == 0, np.sin(angles), np.cos(angles)).astype(np.float32)
    low = jnp.bfloat16
    one = table.astype(low)
    rest = table - one.astype(np.float32)
    two = rest.astype(low)
    three = (rest - two.astype(np.float32)).astype(low)
    blank = np.zeros((LANES - 3 * WGRID, half), low)
    return np.concatenate([one, two, three, blank], axis=0)


def iota(shape, dim):
    return lax.broadcasted_iota(jnp.int32, shape, dim)


def norm_forward(rows):
    centered = rows - jnp.mean(rows, axis=-1, keepdims=True)
    inverse = lax.rsqrt(jnp.mean(centered * centered, axis=-1, keepdims=True) + EPS_NORM)
    return centered * inverse, inverse


def norm_backward(upstream, normed, inverse):
    return inverse * (
        upstream
        - jnp.mean(upstream, axis=-1, keepdims=True)
        - normed * jnp.mean(upstream * normed, axis=-1, keepdims=True)
    )

def vspec():
    return pl.BlockSpec(memory_space=pltpu.VMEM)


def params(mib=56, **more):
    return pltpu.CompilerParams(vmem_limit_bytes=mib * MIB, **more)


def pack_kernel(place, attn_ref, first_ref, second_ref, vector_ref, out_ref, ffn_ref):
    owner = place[1] * 2 + place[2]
    vector = vector_ref[...]
    rows = vector.shape[0]
    wide = jnp.concatenate([vector] * (LANES // vector.shape[1]), axis=1)
    slot = iota((rows, LANES), 1) // vector.shape[1]
    per = LANES // vector.shape[1]
    parts = [attn_ref[...]]
    for half in range(2):
        parts.append(jnp.where(slot + half * per == owner, wide, 0.0))
    parts.append(jnp.zeros((VROWS - 2 * rows, LANES), F32))
    piece = jnp.concatenate(parts, axis=0).astype(BF16)
    for at in range(VDP * VCHIP):
        out_ref[at] = piece
    ffn_ref[0] = first_ref[...].astype(BF16)
    ffn_ref[1] = second_ref[...].astype(BF16)


def pack_attn(place, attn_weight, ffn_in, ffn_out, vectors):
    return pl.pallas_call(
        pack_kernel,
        out_shape=(
            jax.ShapeDtypeStruct((VDP * VCHIP, attn_weight.shape[0] + VROWS, LANES), BF16),
            jax.ShapeDtypeStruct((2,) + ffn_in.shape, BF16),
        ),
        in_specs=[pl.BlockSpec(memory_space=pltpu.SMEM)] + [vspec()] * 4,
        out_specs=(vspec(), vspec()),
        compiler_params=params(),
        name="pack_attn",
    )(place, attn_weight, ffn_in, ffn_out, vectors)


def pack_ffn_kernel(place, own_ref, *refs):
    out_ref = refs[-1]
    for at in range(VCHIP):
        out_ref[at, pl.ds(place[0], 1)] = own_ref[...][None]
        for step in range(1, VDP):
            out_ref[at, pl.ds(place[0] ^ step, 1)] = refs[step - 1][...][None]


def pack_ffn(place, own, parts):
    return pl.pallas_call(
        pack_ffn_kernel,
        out_shape=jax.ShapeDtypeStruct((VCHIP, VDP) + own.shape, BF16),
        in_specs=[pl.BlockSpec(memory_space=pltpu.SMEM)] + [vspec()] * (1 + len(parts)),
        out_specs=vspec(),
        compiler_params=params(16),
        name="pack_ffn",
    )(place, own, *parts)


def place_kernel(
    segment_ref, tokens_ref, back_ref, table_ref, qk_ref, x_ref, qk_t_ref, x_t_ref, turned_ref, marks_ref
):
    row = pl.program_id(0)
    starts = []
    for number in range(1, 4):
        at = jnp.int32(0)
        for step in (512, 256, 128, 64, 32, 16, 8, 4, 2, 1, 1):
            probe = jnp.minimum(at + (step - 1), SEQ - 1)
            at = jnp.where(segment_ref[row, probe] < number, at + step, at)
        starts.append(at)
    edges = [jnp.int32(0)] + starts + [jnp.int32(SEQ)]
    begin = jnp.int32(0)
    for number in range(3, -1, -1):
        begin = jnp.where(edges[number + 1] - edges[number] == HALF, edges[number], begin)
    for number in range(3):
        marks_ref[row, number] = starts[number]
    marks_ref[row, 3] = begin
    one, two, three = starts
    x = pltpu.roll(tokens_ref[...].astype(F32), (SEQ - begin) & (SEQ - 1), 0)
    x_low = x.astype(BF16)
    x_ref[...] = x_low
    eye = jnp.where(iota((D, D), 0) == iota((D, D), 1), 1.0, 0.0).astype(BF16)
    x_t_ref[...] = dot_nt(eye, x_low).astype(BF16)
    back = back_ref[...].astype(F32)
    turned_ref[...] = pltpu.roll(back, (SEQ - begin) & (SEQ - 1), 0).astype(BF16)
    at = (iota((SEQ, LANES), 0) + begin) & (SEQ - 1)
    lane = iota((SEQ, LANES), 1)
    start = jnp.where(at >= three, three, jnp.where(at >= two, two, jnp.where(at >= one, one, 0)))
    local = at - start
    kept = lane < 3 * WGRID
    slot = lane & (WGRID - 1)
    hot_r = jnp.where(((local >> 5) == slot) & kept, 1.0, 0.0).astype(BF16)
    hot_c = jnp.where(((local & (WGRID - 1)) == slot) & kept, 1.0, 0.0).astype(BF16)
    table = table_ref[...]
    places = jnp.concatenate([dot(hot_r, table), dot(hot_c, table)], axis=1)
    qk = (x + places).astype(BF16)
    qk_ref[...] = qk
    qk_t_ref[...] = dot_nt(eye, qk).astype(BF16)


def place_tokens(segment_ids, tokens, cotangent, table):
    rows = segment_ids.shape[0]
    by_row = lambda r: (r, 0)
    return pl.pallas_call(
        place_kernel,
        out_shape=(
            jax.ShapeDtypeStruct(tokens.shape, BF16),
            jax.ShapeDtypeStruct(tokens.shape, BF16),
            jax.ShapeDtypeStruct((D, tokens.shape[0]), BF16),
            jax.ShapeDtypeStruct((D, tokens.shape[0]), BF16),
            jax.ShapeDtypeStruct(tokens.shape, BF16),
            jax.ShapeDtypeStruct((rows, 4), jnp.int32),
        ),
        grid=(rows,),
        in_specs=[
            pl.BlockSpec(memory_space=pltpu.SMEM),
            pl.BlockSpec((SEQ, D), by_row),
            pl.BlockSpec((SEQ, D), by_row),
            pl.BlockSpec((LANES, LANES), lambda r: (0, 0)),
        ],
        out_specs=(
            pl.BlockSpec((SEQ, D), by_row),
            pl.BlockSpec((SEQ, D), by_row),
            pl.BlockSpec((D, SEQ), lambda r: (0, r)),
            pl.BlockSpec((D, SEQ), lambda r: (0, r)),
            pl.BlockSpec((SEQ, D), by_row),
            pl.BlockSpec(memory_space=pltpu.SMEM),
        ),
        compiler_params=params(dimension_semantics=("arbitrary",)),
        cost_estimate=pl.CostEstimate(flops=600_000_000, bytes_accessed=4_000_000, transcendentals=0),
        name="place_tokens",
    )(segment_ids, tokens, cotangent, table)


def attend_kernel(
    marks,
    place,
    x_ref,
    qk_ref,
    x_t_ref,
    qk_t_ref,
    mine_ref,
    other_ref,
    query_t_ref,
    value_ref,
    key_t_ref,
    out_t_ref,
    inverse_ref,
    mixed_ref,
    mixed_t_ref,
    exps_ref,
    weight_ref,
    proj_ref,
    vector_ref,
    key_s,
    value_s,
    mark_k,
    mark_q,
    first_s,
    second_s,
    weight_t_s,
    bias_s,
    tame_s,
    exps_s,
    exps_sem,
):
    row = pl.program_id(0)
    begin = marks[row, 3]
    core = place[2]

    def copy_of(group, half):
        return pltpu.make_async_copy(
            exps_s.at[group, half], exps_ref.at[row, group, half], exps_sem.at[group * 2 + half]
        )

    @pl.when(row == 0)
    def _():
        tall = D // VDP
        for d in range(VDP):
            rows = slice(d * tall, (d + 1) * tall)
            total = jnp.zeros((8, LANES), F32)
            for c in range(VCHIP):
                for ref, half in ((mine_ref, core), (other_ref, 1 - core)):
                    if c < 3:
                        to = pl.ds(pl.multiple_of(c * D + half * LANES, LANES), LANES)
                        weight_ref[rows, to] = ref[d, c, :tall, :]
                    else:
                        to = pl.ds(pl.multiple_of(half * LANES, LANES), LANES)
                        proj_ref[rows, to] = ref[d, c, :tall, :]
                    total += ref[d, c, tall:, :].astype(F32)[:8]
            vector_ref[d * 4 : (d + 1) * 4, :LANES] = total[:4]
            vector_ref[d * 4 : (d + 1) * 4, LANES:] = total[4:]
        weight_t_s[...] = weight_ref[...].astype(F32).T.astype(BF16)
        bias_s[...] = vector_ref[8:16, :].T

    qk_t = qk_t_ref[...]
    query_t = (dot(weight_t_s[:D, :], qk_t) + bias_s[:, 0:1]) * SCALE
    query_t = query_t.astype(BF16)
    query_t_ref[...] = query_t
    key_t = dot(weight_t_s[D : 2 * D, :], qk_t).astype(BF16)
    key_t_ref[...] = key_t

    def largest_norms(rows):
        rows = rows.astype(F32)
        rows = rows * rows
        sums = [
            jnp.sum(rows[head * HEAD_DIM : (head + 1) * HEAD_DIM], axis=0, keepdims=True)
            for head in range(HEADS)
        ]
        return jnp.max(jnp.concatenate(sums, axis=0), axis=1, keepdims=True)

    bound = jnp.max(largest_norms(query_t) * largest_norms(key_t))
    tame_s[0] = jnp.where(bound <= TAME * TAME, 1, 0)
    key_s[...] = dot(qk_ref[...], weight_ref[:, D : 2 * D]).astype(BF16)
    value = dot(x_ref[...], weight_ref[:, 2 * D : 3 * D]) + vector_ref[9:10, :]
    value_ref[...] = value.astype(BF16)
    value_t = dot(weight_t_s[2 * D :, :], x_t_ref[...]) + bias_s[:, 1:2]
    value_t = value_t.astype(BF16)
    for head in range(HEADS):
        value_s[head, :HEAD_DIM, :] = value_t[head * HEAD_DIM : (head + 1) * HEAD_DIM, :]
        value_s[head, HEAD_DIM:, :] = jnp.ones((16, SEQ), BF16)
    one, two, three = marks[row, 0], marks[row, 1], marks[row, 2]

    def number_of(shape, dim):
        here = (iota(shape, dim) + (HALF + begin)) & (SEQ - 1)
        return (
            jnp.where(here >= one, 1, 0)
            + jnp.where(here >= two, 1, 0)
            + jnp.where(here >= three, 1, 0)
        )

    lane = iota((HALF, LANES), 1)
    number = number_of((HALF, LANES), 0)
    mark_k[...] = jnp.where((number != lane) & (lane < 4), -FAR, 0.0).astype(BF16)
    number = number_of((LANES, HALF), 1)
    mark_q[...] = jnp.where(number == iota((LANES, HALF), 0), 1.0, 0.0).astype(BF16)

    head_of = iota((1, LANES), 1) // HEAD_DIM
    for group in range(2):
        keys_here = key_s[:, group * LANES : (group + 1) * LANES]
        for at_head in range(GROUP):
            mask = jnp.where(head_of == at_head, 1.0, 0.0).astype(BF16)
            rows = slice(at_head * HALF, (at_head + 1) * HALF)
            first_s[group, rows, :] = keys_here[:HALF] * mask
            second_s[group, rows, :LANES] = keys_here[HALF:] * mask
            second_s[group, rows, LANES:] = mark_k[...]

    @pl.when(row > 0)
    def _():
        for group in range(2):
            for half in range(2):
                copy_of(group, half).wait()

    def scores_of(group, half, rows):
        query = query_t_ref[group * LANES : (group + 1) * LANES, half * HALF : (half + 1) * HALF]
        if half == 0:
            return dot(first_s[group, rows, :], query)
        return dot(second_s[group, rows, :], jnp.concatenate([query, mark_q[...]], axis=0))

    def place_of(at_head):
        return slice(at_head * HALF, (at_head + 1) * HALF)

    def exps_plain(group, half):
        scores = scores_of(group, half, slice(0, GROUP * HALF))
        for at_head in range(GROUP):
            exps = jnp.exp2(scores[place_of(at_head), :] * LOG2_E)
            exps_s[group, half, :, place_of(at_head)] = exps.astype(BF16)

    def exps_shifted(group, half):
        for at_head in range(GROUP):
            rows = place_of(at_head)
            largest = jnp.max(scores_of(group, half, rows), axis=0, keepdims=True)
            exps = jnp.exp2((scores_of(group, half, rows) - largest) * LOG2_E)
            exps_s[group, half, :, rows] = exps.astype(BF16)

    def finish(group, half):
        rows = slice(half * HALF, (half + 1) * HALF)
        for at_head in range(GROUP):
            head = group * GROUP + at_head
            out = dot(value_s[head, :, rows], exps_s[group, half, :, place_of(at_head)])
            inverse = 1.0 / out[HEAD_DIM : HEAD_DIM + 1, :]
            inverse_ref[group, at_head : at_head + 1, rows] = inverse
            out_t_ref[head * HEAD_DIM : (head + 1) * HEAD_DIM, rows] = out[:HEAD_DIM, :] * inverse

    def run(exps_of):
        items = [(group, half) for group in range(2) for half in range(2)]
        for i in range(len(items) + 1):
            if i < len(items):
                exps_of(*items[i])
                copy_of(*items[i]).start()
            if i >= 1:
                finish(*items[i - 1])

    @pl.when(tame_s[0] == 1)
    def _():
        run(exps_plain)

    @pl.when(tame_s[0] == 0)
    def _():
        run(exps_shifted)

    out_t = out_t_ref[...]
    mixed_t_ref[...] = out_t.astype(BF16)
    mixed_ref[...] = out_t.T.astype(BF16)

    @pl.when(row == pl.num_programs(0) - 1)
    def _():
        for group in range(2):
            for half in range(2):
                copy_of(group, half).wait()


def attend_forward(marks, place, x, qk, x_t, qk_t, mine, other):
    total = x.shape[0]
    rows = total // SEQ
    by_row = lambda r, m, p: (r, 0)
    by_col = lambda r, m, p: (0, r)
    whole = lambda r, m, p: (0, 0)
    return pl.pallas_call(
        attend_kernel,
        out_shape=(
            jax.ShapeDtypeStruct((D, total), BF16),
            jax.ShapeDtypeStruct((total, D), BF16),
            jax.ShapeDtypeStruct((D, total), BF16),
            jax.ShapeDtypeStruct((D, total), F32),
            jax.ShapeDtypeStruct((2, 8, total), F32),
            jax.ShapeDtypeStruct((total, D), BF16),
            jax.ShapeDtypeStruct((D, total), BF16),
            jax.ShapeDtypeStruct((rows, 2, 2, HALF, GROUP * HALF), BF16),
            jax.ShapeDtypeStruct((D, 3 * D), BF16),
            jax.ShapeDtypeStruct((D, D), BF16),
            jax.ShapeDtypeStruct((VEC, D), F32),
        ),
        grid_spec=pltpu.PrefetchScalarGridSpec(
            num_scalar_prefetch=2,
            grid=(rows,),
            in_specs=[
                pl.BlockSpec((SEQ, D), by_row),
                pl.BlockSpec((SEQ, D), by_row),
                pl.BlockSpec((D, SEQ), by_col),
                pl.BlockSpec((D, SEQ), by_col),
                vspec(),
                vspec(),
            ],
            out_specs=[
                pl.BlockSpec((D, SEQ), by_col),
                pl.BlockSpec((SEQ, D), by_row),
                pl.BlockSpec((D, SEQ), by_col),
                pl.BlockSpec((D, SEQ), by_col),
                pl.BlockSpec((2, 8, SEQ), lambda r, m, p: (0, 0, r)),
                pl.BlockSpec((SEQ, D), by_row),
                pl.BlockSpec((D, SEQ), by_col),
                pl.BlockSpec(memory_space=pl.ANY),
                pl.BlockSpec((D, 3 * D), whole),
                pl.BlockSpec((D, D), whole),
                pl.BlockSpec((VEC, D), whole),
            ],
            scratch_shapes=[
                pltpu.VMEM((SEQ, D), BF16),
                pltpu.VMEM((HEADS, HEAD_DIM + 16, SEQ), BF16),
                pltpu.VMEM((HALF, LANES), BF16),
                pltpu.VMEM((LANES, HALF), BF16),
                pltpu.VMEM((2, GROUP * HALF, LANES), BF16),
                pltpu.VMEM((2, GROUP * HALF, 2 * LANES), BF16),
                pltpu.VMEM((3 * D, D), BF16),
                pltpu.VMEM((D, 8), F32),
                pltpu.SMEM((1,), jnp.int32),
                pltpu.VMEM((2, 2, HALF, GROUP * HALF), BF16),
                pltpu.SemaphoreType.DMA((4,)),
            ],
        ),
        compiler_params=params(dimension_semantics=("arbitrary",)),
        cost_estimate=pl.CostEstimate(
            flops=20_000_000_000, bytes_accessed=30_000_000, transcendentals=8_400_000
        ),
        name="attend_forward",
    )(marks, place, x, qk, x_t, qk_t, mine, other)


def feed_kernel(
    marks,
    place,
    x_ref,
    back_ref,
    mixed_ref,
    mixed_t_ref,
    proj_ref,
    mine_ref,
    other_ref,
    vector_ref,
    block_ref,
    resid_ref,
    mixed_grad_ref,
    mine_out,
    other_out,
    proj_out,
    vector_out,
    first_w,
    second_w,
    first_acc,
    second_acc,
    proj_acc,
    vector_acc,
    hidden_s,
    slope_s,
    pre_s,
    first_low_s,
    branch_low_s,
    attended_s,
    block_s,
    eye_s,
):
    step = pl.program_id(0)
    core = place[2]
    tall = D // VDP
    wide = FF // (2 * VCHIP)

    @pl.when(step == 0)
    def _():
        first_acc[...] = jnp.zeros_like(first_acc)
        second_acc[...] = jnp.zeros_like(second_acc)
        proj_acc[...] = jnp.zeros_like(proj_acc)
        vector_acc[...] = jnp.zeros_like(vector_acc)
        eye_s[...] = jnp.where(iota((D, D), 0) == iota((D, D), 1), 1.0, 0.0).astype(BF16)
        for d in range(VDP):
            rows = slice(d * tall, (d + 1) * tall)
            for c in range(VCHIP):
                for ref, half in ((mine_ref, core), (other_ref, 1 - core)):
                    to = pl.ds(pl.multiple_of((2 * c + half) * wide, wide), wide)
                    first_w[rows, to] = ref[c, d, 0]
                    second_w[rows, to] = ref[c, d, 1]

    bias_o, bias_2 = vector_ref[10:11, :], vector_ref[11:12, :]
    gain_1, shift_1 = vector_ref[12:13, :], vector_ref[13:14, :]
    gain_2, shift_2 = vector_ref[14:15, :], vector_ref[15:16, :]
    at_row = pl.multiple_of((step % (SEQ // TILE)) * TILE, TILE)
    chunks = FF // CHUNK
    pair = 2

    def columns(at, count=1):
        return slice(at * CHUNK, (at + count) * CHUNK)

    def hidden_of(rows, at, pre):
        per = CHUNK // D
        bias = [vector_ref[at * per + i : at * per + i + 1, :] for i in range(per)]
        pre = (pre + jnp.concatenate(bias, axis=1)).astype(BF16)
        cube = BF16(GELU_A * GELU_B) * (pre * pre)
        gate = BF16(0.5) + BF16(0.5) * jnp.tanh(pre * (cube + BF16(GELU_A)))
        hidden_s[rows, columns(at)] = pre * gate
        slope_s[rows, columns(at)] = gate + (gate - gate * gate) * (
            pre * (BF16(6.0) * cube + BF16(2.0 * GELU_A))
        )

    def stages(sub):
        rows_at = sub * SUB
        rows = slice(rows_at, rows_at + SUB)
        attended = dot(mixed_ref[rows, :], proj_ref[...]) + bias_o
        norm_1, inverse_1 = norm_forward(x_ref[rows, :].astype(F32) + attended)
        first = norm_1 * gain_1 + shift_1
        first_low = first.astype(BF16)
        first_low_s[rows, :] = first_low
        yield
        branch = jnp.zeros((SUB, D), F32)
        for i in range(chunks + 1):
            if i < chunks:
                hidden_of(rows, i, dot(first_low, first_w[:, columns(i)]))
            if i >= pair and i % pair == 0:
                cols = columns(i - pair, pair)
                branch += dot_nt(hidden_s[rows, cols], second_w[:, cols])
            yield
        norm_2, inverse_2 = norm_forward(first + (branch + bias_2))
        block_s[pl.ds(at_row + rows_at, SUB), :] = norm_2 * gain_2 + shift_2
        back = back_ref[rows, :].astype(F32)
        vector_acc[14:15, :] += jnp.sum(back * norm_2, axis=0, keepdims=True)
        vector_acc[15:16, :] += jnp.sum(back, axis=0, keepdims=True)
        resid_2 = norm_backward(back * gain_2, norm_2, inverse_2)
        branch_low = resid_2.astype(BF16)
        branch_low_s[rows, :] = branch_low
        vector_acc[11:12, :] += jnp.sum(branch_low.astype(F32), axis=0, keepdims=True)
        yield
        first_back = resid_2
        if sub == 1:
            branch_t = dot_nt(eye_s[...], branch_low_s[...]).astype(BF16)
            first_t = dot_nt(eye_s[...], first_low_s[...]).astype(BF16)
            first_t = jnp.concatenate([first_t, jnp.ones((16, TILE), BF16)], axis=0)
        for i in range(chunks + 1):
            if i < chunks:
                pull = dot(branch_low, second_w[:, columns(i)]).astype(BF16)
                pre_s[rows, columns(i)] = pull * slope_s[rows, columns(i)]
                if sub == 1:
                    second_acc[:, columns(i)] += dot(branch_t, hidden_s[:, columns(i)])
            if i >= 1 and sub == 1:
                cols = columns(i - 1)
                first_acc[:, cols] += dot(first_t, pre_s[:, cols])
            if i >= pair and i % pair == 0:
                cols = columns(i - pair, pair)
                first_back += dot_nt(pre_s[rows, cols], first_w[:, cols])
            yield
        vector_acc[12:13, :] += jnp.sum(first_back * norm_1, axis=0, keepdims=True)
        vector_acc[13:14, :] += jnp.sum(first_back, axis=0, keepdims=True)
        resid_1 = norm_backward(first_back * gain_1, norm_1, inverse_1)
        resid_ref[rows, :] = resid_1
        attended_low = resid_1.astype(BF16)
        attended_s[rows, :] = attended_low
        vector_acc[10:11, :] += jnp.sum(attended_low.astype(F32), axis=0, keepdims=True)
        mixed_grad_ref[:, rows] = dot_nt(proj_ref[...], attended_low).astype(BF16)
        yield

    ahead, behind = stages(0), stages(1)
    for _ in range(LEAD):
        next(ahead)
    running = [ahead, behind]
    while running:
        for program in list(running):
            if next(program, 0) == 0:
                running.remove(program)
    proj_acc[...] += dot(mixed_t_ref[...], attended_s[...])

    @pl.when(step % (SEQ // TILE) == SEQ // TILE - 1)
    def _():
        block_ref[...] = pltpu.roll(block_s[...], marks[step // (SEQ // TILE), 3], 0)

    @pl.when(step == pl.num_programs(0) - 1)
    def _():
        for d in range(VDP):
            rows = slice(d * tall, (d + 1) * tall)
            for c in range(VCHIP):
                for ref, half in ((mine_out, core), (other_out, 1 - core)):
                    to = pl.ds(pl.multiple_of((2 * c + half) * wide, wide), wide)
                    ref[d, c, 0] = first_acc[rows, to].astype(BF16)
                    ref[d, c, 1] = second_acc[rows, to].astype(BF16)
        proj_out[...] = proj_acc[...]
        for at in range(FF // D):
            vector_out[at : at + 1, :] = first_acc[D : D + 1, at * D : (at + 1) * D]
        vector_out[FF // D :, :] = vector_acc[FF // D :, :]


def feed_forward(marks, place, x, back, mixed, mixed_t, proj, mine, other, vector):
    total = x.shape[0]
    tile = lambda i, m, p: (i, 0)
    by_col = lambda i, m, p: (0, i)
    whole = lambda i, m, p: (0, 0)
    whole5 = lambda i, m, p: (0, 0, 0, 0, 0)
    return pl.pallas_call(
        feed_kernel,
        out_shape=(
            jax.ShapeDtypeStruct((total, D), F32),
            jax.ShapeDtypeStruct((total, D), F32),
            jax.ShapeDtypeStruct((D, total), BF16),
            jax.ShapeDtypeStruct(mine.shape, BF16),
            jax.ShapeDtypeStruct(mine.shape, BF16),
            jax.ShapeDtypeStruct((D, D), F32),
            jax.ShapeDtypeStruct((VEC, D), F32),
        ),
        grid_spec=pltpu.PrefetchScalarGridSpec(
            num_scalar_prefetch=2,
            grid=(total // TILE,),
            in_specs=[
                pl.BlockSpec((TILE, D), tile),
                pl.BlockSpec((TILE, D), tile),
                pl.BlockSpec((TILE, D), tile),
                pl.BlockSpec((D, TILE), by_col),
                pl.BlockSpec((D, D), whole),
                vspec(),
                vspec(),
                pl.BlockSpec((VEC, D), whole),
            ],
            out_specs=[
                pl.BlockSpec((SEQ, D), lambda i, m, p: (i // (SEQ // TILE), 0)),
                pl.BlockSpec((TILE, D), tile),
                pl.BlockSpec((D, TILE), by_col),
                pl.BlockSpec(mine.shape, whole5),
                pl.BlockSpec(mine.shape, whole5),
                pl.BlockSpec((D, D), whole),
                pl.BlockSpec((VEC, D), whole),
            ],
            scratch_shapes=[
                pltpu.VMEM((D, FF), BF16),
                pltpu.VMEM((D, FF), BF16),
                pltpu.VMEM((D + 16, FF), F32),
                pltpu.VMEM((D, FF), F32),
                pltpu.VMEM((D, D), F32),
                pltpu.VMEM((VEC, D), F32),
                pltpu.VMEM((TILE, FF), BF16),
                pltpu.VMEM((TILE, FF), BF16),
                pltpu.VMEM((TILE, FF), BF16),
                pltpu.VMEM((TILE, D), BF16),
                pltpu.VMEM((TILE, D), BF16),
                pltpu.VMEM((TILE, D), BF16),
                pltpu.VMEM((SEQ, D), F32),
                pltpu.VMEM((D, D), BF16),
            ],
        ),
        compiler_params=params(dimension_semantics=("arbitrary",)),
        cost_estimate=pl.CostEstimate(
            flops=14_000_000_000, bytes_accessed=15_000_000, transcendentals=4_200_000
        ),
        name="feed_forward",
    )(marks, place, x, back, mixed, mixed_t, proj, mine, other, vector)


def pull_kernel(own, rows, marks, place, *refs):
    count = 13 if own else 11
    inputs, refs = refs[:count], refs[count:]
    (pulled_ref, grads_ref, sums_ref), refs = refs[:3], refs[3:]
    buffers, refs = refs[:count], refs[count:]
    pulled_v, dot_s, query_g, key_g, value_g, acc, value_s, scaled_t_s, score_s, in_sem, out_sem = refs
    group = place[2] if own else 1 - place[2]
    heads_at = pl.ds(pl.multiple_of(group * LANES, LANES), LANES)
    names = ["grad", "inverse", "out", "value", "query", "key", "exps", "qk", "x", "weight", "proj"]
    names += ["resid", "other"] if own else []
    buffer = dict(zip(names, buffers))
    source = dict(zip(names, inputs))

    def copy_of(name, row=0, half=0):
        here = pl.ds(row * SEQ, SEQ)
        at = names.index(name)
        ref, to = source[name], buffer[name]
        if name == "exps":
            ref, to, slot = ref.at[row, group, half], to.at[row, half], len(names) * rows + row * 2 + half
        else:
            slot = at * rows + row
            if name in ("grad", "out", "query", "key"):
                ref, to = ref.at[heads_at, here], to.at[row]
            elif name == "inverse":
                ref, to = ref.at[group, :, here], to.at[row]
            elif name == "value":
                ref, to = ref.at[here, heads_at], to.at[row]
            elif name in ("qk", "x", "other"):
                ref, to = ref.at[:, here], to.at[row]
            elif name == "resid":
                ref, to = ref.at[here, :], to.at[row]
            elif name == "proj":
                ref = ref.at[:, heads_at]
        return pltpu.make_async_copy(ref, to, in_sem.at[slot])

    def write_of(row):
        here = pl.ds(row * SEQ, SEQ)
        to = pulled_ref.at[here, :] if own else pulled_ref.at[:, here]
        return pltpu.make_async_copy(pulled_v.at[row], to, out_sem.at[row])

    early = ("grad", "inverse", "out", "value", "query", "key")
    late = ("qk", "x", "resid", "other") if own else ("qk", "x")
    for row in range(rows):
        for name in early:
            copy_of(name, row).start()
        for half in range(2):
            copy_of("exps", row, half).start()
        if row == 0:
            copy_of("weight").start()
            copy_of("proj").start()
        for name in late:
            copy_of(name, row).start()

    head_of = iota((1, LANES), 1) // HEAD_DIM

    for row in range(rows):
        begin = marks[row, 3]
        for name in early:
            copy_of(name, row).wait()
        grad_t = buffer["grad"][row].astype(F32)
        for at_head in range(GROUP):
            heads = slice(at_head * HEAD_DIM, (at_head + 1) * HEAD_DIM)
            part = grad_t[heads, :] * buffer["inverse"][row, at_head : at_head + 1, :]
            dot_s[at_head : at_head + 1, :] = jnp.sum(
                part * buffer["out"][row, heads, :], axis=0, keepdims=True
            )
            scaled_t_s[heads, :] = part.astype(BF16)
            mask = jnp.where(head_of == at_head, 1.0, 0.0).astype(BF16)
            for half in range(2):
                here = slice(half * HALF, (half + 1) * HALF)
                to = slice(at_head * HALF, (at_head + 1) * HALF)
                value_s[half, to, :] = buffer["value"][row, here, :] * mask

        def score_grads_of(half):
            here = slice(half * HALF, (half + 1) * HALF)
            pulls = dot(value_s[half], scaled_t_s[:, here])
            for at_head in range(GROUP):
                cols = slice(at_head * HALF, (at_head + 1) * HALF)
                pull = (pulls[cols, :] - dot_s[at_head : at_head + 1, here]).astype(BF16)
                score_s[half, :, cols] = buffer["exps"][row, half, :, cols] * pull

        def finish(half, at_head):
            cols = slice(at_head * HALF, (at_head + 1) * HALF)
            here = slice(half * HALF, (half + 1) * HALF)
            heads = slice(at_head * HEAD_DIM, (at_head + 1) * HEAD_DIM)
            score_grad = score_s[half, :, cols]
            value_g[heads, here] = dot_nt(scaled_t_s[heads, here], buffer["exps"][row, half, :, cols])
            query_g[heads, here] = dot(buffer["key"][row, heads, here], score_grad)
            key_g[heads, here] = dot_nt(buffer["query"][row, heads, here], score_grad)

        copy_of("exps", row, 0).wait()
        score_grads_of(0)
        copy_of("exps", row, 1).wait()
        score_grads_of(1)
        for half in range(2):
            for at_head in range(GROUP):
                finish(half, at_head)
        query_low = query_g[...].astype(BF16)
        both_low = jnp.concatenate([key_g[...].astype(BF16), value_g[...].astype(BF16)], axis=0)
        if row == 0:
            copy_of("weight").wait()
            copy_of("proj").wait()
        for name in late:
            copy_of(name, row).wait()
        ones = jnp.ones((16, SEQ), BF16)
        sums = [
            dot_nt(ones, query_low)[0:1, :] * SCALE,
            dot_nt(ones, both_low[LANES:, :])[0:1, :],
            jnp.zeros((6, LANES), F32),
        ]
        both = dot_nt(buffer["qk"][row], jnp.concatenate([query_low, both_low[:LANES, :]], axis=0))
        third = dot_nt(buffer["x"][row], both_low[LANES:, :])
        grads = jnp.concatenate([both[:, :LANES] * SCALE, both[:, LANES:], third], axis=1)
        if row == 0:
            acc[...] = grads
            sums_ref[...] = jnp.concatenate(sums, axis=0)
        else:
            acc[...] += grads
            sums_ref[...] += jnp.concatenate(sums, axis=0)
        weight = buffer["weight"]
        at = [pl.ds(pl.multiple_of(i * D + group * LANES, LANES), LANES) for i in range(3)]
        pulled = dot(weight[:, at[0]], query_low) * SCALE + dot(
            jnp.concatenate([weight[:, at[1]], weight[:, at[2]]], axis=1), both_low
        )
        if own:
            pulled = (pulled + buffer["other"][row]).T
            pulled = pltpu.roll(buffer["resid"][row] + pulled, begin, 0)
        pulled_v[row] = pulled
        write_of(row).start()

    tall = D // VDP
    for d in range(VDP):
        here = slice(d * tall, (d + 1) * tall)
        for c in range(3):
            grads_ref[d, c] = acc[here, c * LANES : (c + 1) * LANES].astype(BF16)
        grads_ref[d, 3] = buffer["proj"][here, :].astype(BF16)
    for row in range(rows):
        write_of(row).wait()


def attend_back(own, marks, place, grad_t, query_t, value, key_t, out_t, inverse, exps, qk_t, x_t, weight, proj, *more):
    total = value.shape[0]
    rows = total // SEQ
    inputs = (grad_t, inverse, out_t, value, query_t, key_t, exps, qk_t, x_t, weight, proj) + more
    anywhere = pl.BlockSpec(memory_space=pl.ANY)
    by_head = pltpu.VMEM((rows, LANES, SEQ), BF16)
    by_col = pltpu.VMEM((rows, D, SEQ), BF16)
    wide = pltpu.VMEM((rows, SEQ, D), F32)
    tall = pltpu.VMEM((rows, D, SEQ), F32)
    buffers = [
        by_head,
        pltpu.VMEM((rows, 8, SEQ), F32),
        pltpu.VMEM((rows, LANES, SEQ), F32),
        pltpu.VMEM((rows, SEQ, LANES), BF16),
        by_head,
        by_head,
        pltpu.VMEM((rows, 2, HALF, GROUP * HALF), BF16),
        by_col,
        by_col,
        pltpu.VMEM((D, 3 * D), BF16),
        pltpu.VMEM((D, LANES), F32),
    ]
    buffers += [wide, tall] if own else []
    copies = len(buffers) * rows + 2 * rows
    return pl.pallas_call(
        functools.partial(pull_kernel, own, rows),
        out_shape=(
            jax.ShapeDtypeStruct((total, D) if own else (D, total), F32),
            jax.ShapeDtypeStruct((VDP, VCHIP, D // VDP, LANES), BF16),
            jax.ShapeDtypeStruct((8, LANES), F32),
        ),
        grid_spec=pltpu.PrefetchScalarGridSpec(
            num_scalar_prefetch=2,
            grid=(1,),
            in_specs=[anywhere] * len(inputs),
            out_specs=[
                anywhere,
                pl.BlockSpec((VDP, VCHIP, D // VDP, LANES), lambda r, m, p: (0, 0, 0, 0)),
                pl.BlockSpec((8, LANES), lambda r, m, p: (0, 0)),
            ],
            scratch_shapes=buffers
            + [
                wide if own else tall,
                pltpu.VMEM((8, SEQ), F32),
                pltpu.VMEM((LANES, SEQ), F32),
                pltpu.VMEM((LANES, SEQ), F32),
                pltpu.VMEM((LANES, SEQ), F32),
                pltpu.VMEM((D, 3 * LANES), F32),
                pltpu.VMEM((2, GROUP * HALF, LANES), BF16),
                pltpu.VMEM((LANES, SEQ), BF16),
                pltpu.VMEM((2, HALF, GROUP * HALF), BF16),
                pltpu.SemaphoreType.DMA((copies,)),
                pltpu.SemaphoreType.DMA((rows,)),
            ],
        ),
        compiler_params=params(dimension_semantics=("arbitrary",)),
        cost_estimate=pl.CostEstimate(
            flops=18_000_000_000, bytes_accessed=15_000_000, transcendentals=0
        ),
        name="attend_back",
    )(marks, place, *inputs)


def sums_by_group(place, sums_own, sums_other):
    first = place[2] == 0
    return (
        jnp.where(first, sums_own, sums_other),
        jnp.where(first, sums_other, sums_own),
    )


def two_terms(rows):
    high = rows.astype(BF16)
    return jnp.concatenate([high.astype(F32), rows - high.astype(F32)], axis=0)


def column_to_row(columns, rows):
    lane = iota((rows, LANES), 1)
    wide = jnp.zeros((rows, LANES), F32)
    for i, column in enumerate(columns):
        wide = jnp.where(lane == i, column, wide)
    return wide.T[:8, :]


def total_of(array):
    return jnp.sum(jnp.sum(array, axis=0, keepdims=True), axis=1, keepdims=True)


def tail_ffn_kernel(place, ffn_ref, rows_1, rows_2, last_ref, grad_1, grad_2, stat_ref):
    lane = iota((1, LANES), 1)
    piece, across = [], []
    for kind in range(2):
        total = ffn_ref[0, kind].astype(F32)
        for at in range(1, VDP * VCHIP):
            total = total + ffn_ref[at, kind].astype(F32)
        (grad_1, grad_2)[kind][...] = total
        square = total * total + EPS_ONE
        down = jnp.sum(square, axis=0, keepdims=True)
        piece += [down[:, :LANES], down[:, LANES:]]
        across.append(jnp.sum(square, axis=1, keepdims=True))
    across = column_to_row(across, total.shape[0])
    across = jnp.concatenate([across[0:1], across[1:2]], axis=1)
    olds = jnp.zeros((1, LANES), F32)
    for i, ref in enumerate((rows_1, rows_2)):
        olds = jnp.where(lane == i, jnp.sum(ref[...], axis=1, keepdims=True), olds)
    stat_ref[...] = jnp.concatenate([across] + piece + [olds, jnp.zeros((2, LANES), F32)], axis=0)


def tail_send_kernel(
    place, mine_ref, got_ref, vector_ref, own_ref, other_ref, stat_ref, stat_other_ref, send_ref
):
    tall = D // VDP
    low, high = sums_by_group(place, own_ref[...], other_ref[...])
    vector = jnp.concatenate(
        [
            vector_ref[:8, :],
            jnp.concatenate([low[:2], high[:2]], axis=1),
            vector_ref[10:, :],
        ],
        axis=0,
    )
    stat = jnp.concatenate([stat_ref[0:1, :] + stat_other_ref[0:1, :], stat_ref[1:6, :]], axis=0)
    stat = two_terms(stat)
    rows = VEC // VDP
    for d in range(VDP):
        for c in range(VCHIP):
            at = d * VCHIP + c
            both = mine_ref[d, c].astype(F32) + got_ref[d, c].astype(F32)
            send_ref[at, :tall, :] = both.astype(BF16)
            part = vector[d * rows : (d + 1) * rows, c * 64 : (c + 1) * 64]
            part = jnp.concatenate([part, jnp.zeros((rows, LANES - 64), F32)], axis=1)
            send_ref[at, tall:, :] = jnp.concatenate([part, stat], axis=0).astype(BF16)


def tail_reduce_kernel(
    place,
    got_ref,
    ffn_grad_1,
    ffn_grad_2,
    attn_ref,
    first_ref,
    second_ref,
    rows_0,
    rows_1,
    rows_2,
    cols_0,
    cols_1,
    cols_2,
    vector_ref,
    moment_ref,
    grad_ref,
    update_1,
    update_2,
    rows_out_1,
    rows_out_2,
    cols_out_1,
    cols_out_2,
    send_ref,
):
    decay = 1.0 - STEP ** (-0.8)
    chip = place[1]
    dp = place[0]
    tall = attn_ref.shape[0]
    rows, width = vector_ref.shape
    pieces = VDP * VCHIP
    lane = iota((1, LANES), 1)
    total = got_ref[0, :tall, :].astype(F32)
    part = got_ref[0, tall:, :].astype(F32)[:rows]
    for at in range(1, pieces):
        total = total + got_ref[at, :tall, :].astype(F32)
        part = part + got_ref[at, tall:, :].astype(F32)[:rows]
    grad_ref[...] = total
    low = total.astype(BF16)

    def stat_of(at):
        both = got_ref[pl.ds(at, 1), tall:, :][0].astype(F32)[rows:]
        return both[:6] + both[6:12]

    every = jnp.zeros((1, LANES), F32)
    olds = jnp.zeros((1, LANES), F32)
    mine = jnp.zeros((1, LANES), F32)
    down = jnp.zeros((6, LANES), F32)
    for d in range(VDP):
        down = down + stat_of(d * VCHIP + chip)
        for c in range(VCHIP):
            stat = stat_of(d * VCHIP + c)
            every = every + stat[0:1]
            if c == 0:
                olds = olds + stat[5:6]
    for c in range(VCHIP):
        mine = mine + stat_of(dp * VCHIP + c)[0:1]
    row_total = tall * VDP
    new_rows, means = [], []
    for i, ref in enumerate((rows_1, rows_2)):
        count = first_ref.shape[1] * 2 * VCHIP
        new_rows.append(decay * ref[...] + (1.0 - decay) * (mine[:, i * tall : (i + 1) * tall] / count))
        old = jnp.sum(jnp.where(lane == i, olds, 0.0), axis=1, keepdims=True)
        fresh = jnp.sum(every[:, i * tall : (i + 1) * tall], axis=1, keepdims=True)
        means.append((decay * old + (1.0 - decay) * (fresh / count)) / row_total)
    tile = jnp.concatenate(new_rows + [jnp.zeros((6, tall), F32)], axis=0)
    rows_out_1[...] = new_rows[0]
    rows_out_2[...] = new_rows[1]
    tile = jnp.concatenate([tile, jnp.zeros((8, LANES - tall), F32)], axis=1)
    turned = jnp.concatenate([tile, jnp.zeros((LANES - 8, LANES), F32)], axis=0).T
    scalars = jnp.zeros((1, LANES), F32)
    for i, (old_ref, out_ref, to) in enumerate(
        ((cols_1, cols_out_1, update_1), (cols_2, cols_out_2, update_2))
    ):
        sums = jnp.concatenate([down[1 + 2 * i : 2 + 2 * i], down[2 + 2 * i : 3 + 2 * i]], axis=1)
        cols = decay * old_ref[...] + (1.0 - decay) * (sums / row_total)
        out_ref[...] = cols
        grad = (ffn_grad_1, ffn_grad_2)[i][...]
        update = grad * lax.rsqrt(turned[:tall, i : i + 1] * cols / means[i])
        to[...] = update
        scalars = jnp.where(lane == 67 + i, total_of(update * update), scalars)
    for i, ref in enumerate((attn_ref, first_ref, second_ref)):
        weight = ref[...]
        scalars = jnp.where(lane == 64 + i, total_of(weight * weight), scalars)
    scalars = jnp.concatenate([rows_0[...], scalars[:, tall:]], axis=1)
    vector = vector_ref[...]
    power = jnp.sum(vector * vector, axis=1, keepdims=True)
    lines = jnp.concatenate(
        [part[:, :64], moment_ref[...], jnp.broadcast_to(power, (rows, LANES - 64 - width))], axis=1
    )
    piece = jnp.concatenate(
        [two_terms(lines), two_terms(jnp.concatenate([cols_0[...], scalars], axis=0))]
        + [jnp.zeros((4, LANES), F32)],
        axis=0,
    ).astype(BF16)
    for at in range(pieces):
        send_ref[at, :tall, :] = low
        send_ref[at, tall:, :] = piece


def tail_apply_kernel(
    place,
    mine_ref,
    other_ref,
    grad_ref,
    update_1,
    update_2,
    weight_0,
    weight_1,
    weight_2,
    rows_0,
    cols_0,
    vector_ref,
    moment_ref,
    new_0,
    new_1,
    new_2,
    rows_out,
    cols_out,
    vector_grad_ref,
    moment_out,
    vector_out,
    sums_s,
    rows_s,
):
    decay = 1.0 - STEP ** (-0.8)
    dp, chip, core = place[0], place[1], place[2]
    tall = weight_0.shape[0]
    rows, width = vector_ref.shape
    fsdp = 2 * VCHIP
    lane = iota((1, LANES), 1)
    refs = (mine_ref, other_ref)
    row_total = float(tall * VDP)
    col_total = float(LANES * fsdp)

    def lines_of(ref, at):
        both = ref[at, tall:, :].astype(F32)
        return both[0:4] + both[4:8], both[8:10] + both[10:12]

    scalars = jnp.zeros((1, LANES), F32)
    for ref in refs:
        for at in range(VDP * VCHIP):
            scalars = scalars + lines_of(ref, at)[1][1:2]
    scalar = lambda at: jnp.sum(jnp.where(lane == at, scalars, 0.0), axis=1, keepdims=True)

    tile, fresh = [], []
    for d in range(VDP):
        wide = jnp.zeros((tall, LANES), F32)
        for ref in refs:
            for c in range(VCHIP):
                block = ref[d * VCHIP + c, :tall, :].astype(F32)
                wide = wide + (block * block + EPS_ONE)
        fresh.append(jnp.sum(wide, axis=1, keepdims=True))
        tile.append(lines_of(mine_ref, d * VCHIP)[1][1:2])
    tile = jnp.concatenate(tile + [jnp.zeros((LANES - VDP, LANES), F32)], axis=0).T
    mean = jnp.zeros((1, 1), F32)
    new_rows = []
    for d in range(VDP):
        new = decay * tile[:tall, d : d + 1] + (1.0 - decay) * (fresh[d] / col_total)
        new_rows.append(1.0 / new)
        mean = mean + jnp.sum(new, axis=0, keepdims=True)
        sums_s[d] = jnp.broadcast_to(fresh[d], (tall, LANES))
    mean = mean / row_total
    mine = sums_s[pl.ds(dp, 1)][0]
    rows_s[...] = mine.T
    rows_new = decay * rows_0[...] + (1.0 - decay) * (rows_s[0:1, :tall] / col_total)
    rows_out[...] = rows_new
    power = jnp.zeros((1, 1), F32)
    for half, ref in enumerate(refs):
        for c in range(VCHIP):
            down = jnp.zeros((tall, LANES), F32)
            weighted = jnp.zeros((tall, LANES), F32)
            for d in range(VDP):
                block = ref[d * VCHIP + c, :tall, :].astype(F32)
                square = block * block
                down = down + (square + EPS_ONE)
                weighted = weighted + square * new_rows[d]
            down = jnp.sum(down, axis=0, keepdims=True)
            old = lines_of(ref, c)[1][0:1]
            cols = decay * old + (1.0 - decay) * (down / row_total)
            weighted = jnp.sum(weighted, axis=0, keepdims=True) / cols
            power = power + jnp.sum(weighted, axis=1, keepdims=True)
            if half == 0:
                sums_s[VDP + c] = jnp.broadcast_to(down, (tall, LANES))
    power = power * mean
    down = sums_s[pl.ds(VDP + chip, 1)][0][0:1, :]
    cols_new = decay * cols_0[...] + (1.0 - decay) * (down / row_total)
    cols_out[...] = cols_new
    column = jnp.concatenate(
        [
            jnp.concatenate([rows_new, jnp.zeros((1, LANES - tall), F32)], axis=1),
            jnp.zeros((LANES - 1, LANES), F32),
        ],
        axis=0,
    ).T[:tall, 0:1]
    update_0 = grad_ref[...] * lax.rsqrt(column * cols_new / mean)
    powers = (power, scalar(67), scalar(68))
    for i, (update, weight, new) in enumerate(
        (
            (update_0, weight_0, new_0),
            (update_1[...], weight_1, new_1),
            (update_2[...], weight_2, new_2),
        )
    ):
        entries = float(weight.shape[0] * weight.shape[1] * VDP * fsdp)
        clip = jnp.maximum(1.0, jnp.sqrt(powers[i] / entries) / CLIP_LIMIT)
        rate = STEP_RATE * jnp.maximum(EPS_TWO, jnp.sqrt(scalar(64 + i) / entries))
        new[...] = weight[...] - rate / clip * update
    powers, sizes = [], []
    for d in range(VDP):
        power = jnp.zeros((rows, 1), F32)
        size = jnp.zeros((rows, 1), F32)
        for c in range(VCHIP):
            at = d * VCHIP + c
            first, second = lines_of(mine_ref, at)[0], lines_of(other_ref, at)[0]
            both = first[:, :64] + second[:, :64]
            size = size + first[:, LANES - 1 :] + second[:, LANES - 1 :]
            near = jnp.where(core == 0, first[:, 64 : 64 + width], second[:, 64 : 64 + width])
            far = jnp.where(core == 0, second[:, 64 : 64 + width], first[:, 64 : 64 + width])
            moment = jnp.concatenate([near, far], axis=1)
            moment = decay * moment + (1.0 - decay) * (both * both + EPS_ONE)
            power = power + jnp.sum(both * both / moment, axis=1, keepdims=True)
            wide = jnp.concatenate([both, jnp.zeros((rows, LANES - 64), F32)], axis=1)
            sums_s[2 * VDP + at, :rows, :] = wide
        powers.append(power)
        sizes.append(size)
    both = sums_s[pl.ds(2 * VDP + dp * VCHIP + chip, 1), :rows, :][0]
    vector_grad = jnp.where(core == 0, both[:, :width], both[:, width : 2 * width])
    vector_grad_ref[...] = vector_grad
    moment = decay * moment_ref[...] + (1.0 - decay) * (vector_grad * vector_grad + EPS_ONE)
    moment_out[...] = moment
    step = vector_grad * lax.rsqrt(moment)
    bias = VDP // 2
    bias_power = sum(jnp.sum(power, axis=0, keepdims=True) for power in powers[:bias])
    bias_size = sum(jnp.sum(size, axis=0, keepdims=True) for size in sizes[:bias])
    power, size = powers[bias], sizes[bias]
    for d in range(bias + 1, VDP):
        power = jnp.where(dp == d, powers[d], power)
        size = jnp.where(dp == d, sizes[d], size)
    is_bias = dp < bias
    power = jnp.where(is_bias, bias_power, power)
    size = jnp.where(is_bias, bias_size, size)
    count = jnp.where(is_bias, float(FF), float(D))
    clip = jnp.maximum(1.0, jnp.sqrt(power / count) / CLIP_LIMIT)
    rate = STEP_RATE * jnp.maximum(EPS_TWO, jnp.sqrt(size / count))
    vector_out[...] = vector_ref[...] - rate / clip * step


def whole_call(kernel, name, place, outs, *operands, scratch=()):
    return pl.pallas_call(
        kernel,
        out_shape=[jax.ShapeDtypeStruct(shape, kind) for shape, kind in outs],
        in_specs=[pl.BlockSpec(memory_space=pltpu.SMEM)] + [vspec()] * len(operands),
        out_specs=[vspec()] * len(outs),
        scratch_shapes=list(scratch),
        compiler_params=params(16),
        name=name,
    )(place, *operands)


def core_swap(block):
    return lax.ppermute(block, "core", [(0, 1), (1, 0)])


def exchange(blocks, axes):
    return lax.all_to_all(blocks, axes, split_axis=0, concat_axis=0, tiled=True)


def after(value, *earlier, mib=8):
    return pl.pallas_call(
        lambda *refs: None,
        out_shape=jax.ShapeDtypeStruct(value.shape, value.dtype),
        in_specs=[pl.BlockSpec(memory_space=pltpu.HBM)] * (1 + len(earlier)),
        out_specs=pl.BlockSpec(memory_space=pltpu.HBM),
        input_output_aliases={0: 0},
        compiler_params=params(mib),
        name="after",
    )(value, *earlier)


def pair_kernel(mine_ref, got_ref, out_ref):
    out_ref[...] = (mine_ref[...].astype(F32) + got_ref[...].astype(F32)).astype(BF16)


def pair_sum(mine, got):
    return pl.pallas_call(
        pair_kernel,
        out_shape=jax.ShapeDtypeStruct(mine.shape, BF16),
        in_specs=[vspec(), vspec()],
        out_specs=vspec(),
        compiler_params=params(16),
        name="pair_sum",
    )(mine, got)


CHIPS = ("dp", "chip")
ALL = ("dp", "chip", "core")


def layer(place, weights, segment_ids, tokens, cotangent, ffn_weights, send_core, send_ffn):
    table = jnp.asarray(encode_table())
    qk, x, qk_t, x_t, back, marks = place_tokens(segment_ids, tokens, cotangent, table)
    query_t, value, key_t, out_t, inverse, mixed, mixed_t, exps, weight, proj, vector = attend_forward(
        marks, place, x, qk, x_t, qk_t, *weights(marks)
    )
    ffn_mine, ffn_other = ffn_weights(marks, vector)
    block_out, resid, grad_t, ffn_mine, ffn_other, proj_g, vector_g = feed_forward(
        marks, place, x, back, mixed, mixed_t, proj, ffn_mine, ffn_other, vector
    )
    ffn_got, grad_t = send_ffn(ffn_mine, ffn_other, grad_t)
    shared = (marks, place, grad_t, query_t, value, key_t, out_t, inverse, exps, qk_t, x_t, weight, proj_g)
    pulled, grads_other, sums_other = attend_back(False, *shared)
    attn_got = send_core(grads_other)
    input_grad, grads_own, sums_own = attend_back(True, *shared, resid, pulled)
    return block_out, input_grad, grads_own, grads_other, attn_got, sums_own, sums_other, vector_g, ffn_got


def body(
    tokens,
    cotangent,
    segment_ids,
    attn_weight,
    ffn_in,
    ffn_out,
    vectors,
    attn_rows,
    attn_cols,
    in_rows,
    in_cols,
    out_rows,
    out_cols,
    vector_moment,
):
    place = jnp.stack([lax.axis_index("dp"), lax.axis_index("chip"), lax.axis_index("core")])
    place = place.astype(jnp.int32)
    pieces = VDP * VCHIP
    tall, wide = attn_weight.shape
    rows_v, cols_v = vectors.shape
    split = lambda array: array.reshape((VDP, VCHIP) + array.shape[1:])
    attn_sent, ffn_low = pack_attn(place, attn_weight, ffn_in, ffn_out, vectors)
    attn_mine = exchange(attn_sent, CHIPS)

    parts = [
        lax.ppermute(ffn_low, "dp", [(i, i ^ step) for i in range(VDP)]) for step in range(1, VDP)
    ]
    ffn_sent = pack_ffn(place, ffn_low, parts)

    def attn_weights(marks):
        mine = split(after(attn_mine, marks, ffn_sent))
        return mine, core_swap(mine)

    def ffn_weights(marks, vector):
        got = exchange(after(ffn_sent, marks), "chip")
        ffn_mine = after(got, vector)
        return ffn_mine, core_swap(ffn_mine)

    def send_ffn(mine, other, grad_t):
        both = pair_sum(mine, core_swap(other))
        got = exchange(both.reshape((pieces,) + mine.shape[2:]), CHIPS)
        return got, after(grad_t, both, mib=56)

    (
        block_out,
        input_grad,
        grads_own,
        grads_other,
        attn_got,
        sums_own,
        sums_other,
        vector_g,
        ffn_got,
    ) = layer(place, attn_weights, segment_ids, tokens, cotangent, ffn_weights, core_swap, send_ffn)
    lay = lambda stat: stat.reshape(1, -1)
    rows_old = (lay(attn_rows), lay(in_rows), lay(out_rows))
    cols_old = (lay(attn_cols), lay(in_cols), lay(out_cols))
    weights_old = (attn_weight, ffn_in, ffn_out)
    in_grad, out_grad, stat = whole_call(
        tail_ffn_kernel,
        "tail_ffn",
        place,
        [(ffn_in.shape, F32), (ffn_out.shape, F32), ((8, LANES), F32)],
        ffn_got,
        *rows_old[1:],
        sums_own,
    )
    (sent,) = whole_call(
        tail_send_kernel,
        "tail_send",
        place,
        [((pieces, tall + VROWS, LANES), BF16)],
        grads_own,
        attn_got,
        vector_g,
        sums_own,
        sums_other,
        stat,
        core_swap(stat),
    )
    got = exchange(sent, CHIPS)
    attn_grad, update_1, update_2, rows_new_1, rows_new_2, cols_new_1, cols_new_2, sent = whole_call(
        tail_reduce_kernel,
        "tail_reduce",
        place,
        [
            (attn_weight.shape, F32),
            (ffn_in.shape, F32),
            (ffn_out.shape, F32),
            (rows_old[1].shape, F32),
            (rows_old[2].shape, F32),
            (cols_old[1].shape, F32),
            (cols_old[2].shape, F32),
            ((pieces, tall + VROWS, LANES), BF16),
        ],
        got,
        in_grad,
        out_grad,
        *weights_old,
        *rows_old,
        *cols_old,
        vectors,
        vector_moment,
    )
    mine = exchange(sent, CHIPS)
    attn_new, in_new, out_new, rows_new_0, cols_new_0, vector_grad, moment_new, vectors_new = whole_call(
        tail_apply_kernel,
        "tail_apply",
        place,
        [
            (attn_weight.shape, F32),
            (ffn_in.shape, F32),
            (ffn_out.shape, F32),
            (rows_old[0].shape, F32),
            (cols_old[0].shape, F32),
            (vectors.shape, F32),
            (vectors.shape, F32),
            (vectors.shape, F32),
        ],
        mine,
        core_swap(mine),
        attn_grad,
        update_1,
        update_2,
        *weights_old,
        rows_old[0],
        cols_old[0],
        vectors,
        vector_moment,
        scratch=[
            pltpu.VMEM((2 * VDP + pieces, tall, LANES), F32),
            pltpu.VMEM((LANES, tall), F32),
        ],
    )
    return (
        block_out,
        input_grad,
        attn_grad,
        in_grad,
        out_grad,
        vector_grad,
        rows_new_0.reshape(-1),
        cols_new_0.reshape(-1),
        rows_new_1.reshape(-1),
        cols_new_1.reshape(-1),
        rows_new_2.reshape(-1),
        cols_new_2.reshape(-1),
        moment_new,
        attn_new,
        in_new,
        out_new,
        vectors_new,
    )


def gather_all(block):
    shape = (lax.axis_size("dp"), lax.axis_size("chip") * 2)
    count = shape[0] * shape[1]
    got = exchange(jnp.broadcast_to(block[None], (count,) + block.shape), ALL)
    return got.reshape(shape + block.shape)


def unblock(parts):
    dp_count, fsdp_count, rows, cols = parts.shape
    return parts.transpose(0, 2, 1, 3).reshape(dp_count * rows, fsdp_count * cols)


def scatter_sum(full):
    dp_count = lax.axis_size("dp")
    fsdp_count = lax.axis_size("chip") * 2
    rows, cols = full.shape
    by_col = full.astype(BF16).reshape(rows, fsdp_count, cols // fsdp_count).transpose(1, 0, 2)
    got = exchange(by_col, ("chip", "core"))
    part = jnp.sum(got.astype(F32), axis=0).astype(BF16)
    by_row = part.reshape(dp_count, rows // dp_count, cols // fsdp_count)
    return jnp.sum(exchange(by_row, "dp").astype(F32), axis=0)


def body_any(
    tokens,
    cotangent,
    segment_ids,
    attn_weight,
    ffn_in,
    ffn_out,
    vectors,
    attn_rows,
    attn_cols,
    in_rows,
    in_cols,
    out_rows,
    out_cols,
    vector_moment,
):
    dp_count = lax.axis_size("dp")
    fsdp_count = lax.axis_size("chip") * 2
    dp_place = lax.axis_index("dp")
    fsdp_place = lax.axis_index("chip") * 2 + lax.axis_index("core")
    rows_w = attn_weight.shape[0]
    rows_v = vectors.shape[0]
    place = jnp.zeros((3,), jnp.int32)
    full_attn = unblock(gather_all(attn_weight.astype(BF16)))
    full_vector = unblock(gather_all(vectors.astype(BF16)))
    full_ffn = jnp.stack(
        [unblock(gather_all(ffn_in.astype(BF16))), unblock(gather_all(ffn_out.astype(BF16)))]
    )
    tall = D // VDP
    cut = full_attn.reshape(VDP, tall, VCHIP, 2, LANES).transpose(3, 0, 2, 1, 4)
    lines = full_vector.reshape(VDP, VEC // VDP, 2, LANES).transpose(0, 2, 1, 3)
    lines = lines.reshape(VDP, 1, 2 * VEC // VDP, LANES)
    lines = jnp.pad(lines, ((0, 0), (0, VCHIP - 1), (0, VROWS - 2 * VEC // VDP), (0, 0)))
    weights = (
        jnp.concatenate([cut[0], lines], axis=2),
        jnp.concatenate([cut[1], jnp.zeros_like(lines)], axis=2),
    )
    ffn_cut = full_ffn.reshape(2, VDP, tall, VCHIP, 2, FF // (2 * VCHIP))
    ffn_cut = ffn_cut.transpose(4, 3, 1, 0, 2, 5)
    (
        block_out,
        input_grad,
        grads_own,
        grads_other,
        _,
        sums_own,
        sums_other,
        vector_g,
        ffn_got,
    ) = layer(
        place,
        lambda marks: weights,
        segment_ids,
        tokens,
        cotangent,
        lambda marks, vector: (ffn_cut[0], ffn_cut[1]),
        lambda block: block,
        lambda mine, other, grad_t: (jnp.stack([mine, other]), grad_t),
    )
    attn_full = jnp.stack([grads_own, grads_other]).transpose(1, 3, 2, 0, 4).reshape(D, 4 * D)
    ffn_full = ffn_got.transpose(3, 1, 4, 2, 0, 5).reshape(2, D, FF)
    sums = jnp.concatenate([sums_own[:2], sums_other[:2]], axis=1)
    vector_full = jnp.concatenate([vector_g[:8], sums, vector_g[10:]], axis=0)
    attn_grad = scatter_sum(attn_full)
    in_grad = scatter_sum(ffn_full[0])
    out_grad = scatter_sum(ffn_full[1])
    vector_grad = scatter_sum(vector_full)

    decay = 1.0 - STEP ** (-0.8)
    gradients = (attn_grad, in_grad, out_grad)
    weights_old = (attn_weight, ffn_in, ffn_out)
    rows_old = (attn_rows, in_rows, out_rows)
    cols_old = (attn_cols, in_cols, out_cols)
    moment_new = decay * vector_moment + (1.0 - decay) * (vector_grad * vector_grad + EPS_ONE)
    vector_step = vector_grad * lax.rsqrt(moment_new)
    squares = [gradient * gradient + EPS_ONE for gradient in gradients]
    pieces = []
    for square in squares:
        pieces.append(jnp.sum(square, axis=1))
    for square in squares:
        pieces.append(jnp.sum(square, axis=0))
    pieces.append(jnp.sum(vector_step * vector_step, axis=1))
    pieces.append(jnp.sum(vectors * vectors, axis=1))
    pieces.append(jnp.stack([jnp.sum(weight * weight) for weight in weights_old]))
    pieces.append(jnp.stack([jnp.sum(old) for old in rows_old]))
    sizes = [piece.shape[0] for piece in pieces]
    flat = jnp.concatenate(pieces)
    flat = jnp.pad(flat, (0, -flat.shape[0] % 1024)).reshape(-1, LANES)
    got = gather_all(flat).reshape(dp_count, fsdp_count, -1)
    offsets = [0]
    for length in sizes:
        offsets.append(offsets[-1] + length)
    take = lambda i: got[:, :, offsets[i] : offsets[i + 1]]
    rows_new, cols_new, row_means, entries = [], [], [], []
    for i in range(3):
        count_rows = rows_w * dp_count
        count_cols = weights_old[i].shape[1] * fsdp_count
        entries.append(float(count_rows * count_cols))
        row_all = jnp.sum(take(i), axis=1)
        mine = lax.dynamic_index_in_dim(row_all, dp_place, 0, keepdims=False)
        rows_new.append(decay * rows_old[i] + (1.0 - decay) * mine / count_cols)
        col_all = jnp.sum(take(3 + i), axis=0)
        mine = lax.dynamic_index_in_dim(col_all, fsdp_place, 0, keepdims=False)
        cols_new.append(decay * cols_old[i] + (1.0 - decay) * mine / count_rows)
        old_total = jnp.sum(take(9)[:, 0, i])
        row_means.append(
            (decay * old_total + (1.0 - decay) * jnp.sum(row_all) / count_cols) / count_rows
        )
    step_rows = jnp.sum(take(6), axis=1).reshape(-1)
    weight_rows = jnp.sum(take(7), axis=1).reshape(-1)
    weight_totals = jnp.sum(take(8), axis=(0, 1))
    updates = []
    for i in range(3):
        second = rows_new[i][:, None] * cols_new[i][None, :] / row_means[i]
        updates.append(gradients[i] * lax.rsqrt(second))
    flat = jnp.stack([jnp.sum(update * update) for update in updates])
    flat = jnp.broadcast_to(jnp.pad(flat, (0, 5))[:, None], (8, LANES))
    totals = jnp.sum(gather_all(flat)[:, :, :, 0], axis=(0, 1))
    new_weights = []
    for i in range(3):
        clip_factor = jnp.maximum(1.0, jnp.sqrt(totals[i] / entries[i]) / CLIP_LIMIT)
        step_size = STEP_RATE * jnp.maximum(EPS_TWO, jnp.sqrt(weight_totals[i] / entries[i]))
        new_weights.append(weights_old[i] - step_size / clip_factor * updates[i])
    bias_rows = FF // D
    row_places = jnp.arange(VEC)
    counts = jnp.where(row_places < bias_rows, float(FF), float(D))
    grouped_updates = jnp.where(row_places < bias_rows, jnp.sum(step_rows[:bias_rows]), step_rows)
    grouped_weights = jnp.where(row_places < bias_rows, jnp.sum(weight_rows[:bias_rows]), weight_rows)
    clip_rows = jnp.maximum(1.0, jnp.sqrt(grouped_updates / counts) / CLIP_LIMIT)
    step_sizes = STEP_RATE * jnp.maximum(EPS_TWO, jnp.sqrt(grouped_weights / counts))
    factor_rows = lax.dynamic_slice_in_dim(step_sizes / clip_rows, dp_place * rows_v, rows_v)
    vectors_new = vectors - factor_rows[:, None] * vector_step
    return (
        block_out,
        input_grad,
        attn_grad,
        in_grad,
        out_grad,
        vector_grad,
        rows_new[0],
        cols_new[0],
        rows_new[1],
        cols_new[1],
        rows_new[2],
        cols_new[2],
        moment_new,
        new_weights[0],
        new_weights[1],
        new_weights[2],
        vectors_new,
    )


def solution(mesh):
    dp_count, fsdp_count = mesh.shape["dp"], mesh.shape["fsdp"]
    inner = jax.sharding.Mesh(mesh.devices.reshape(dp_count, fsdp_count // 2, 2), ALL)
    fsdp = ("chip", "core")
    split = P(ALL, None)
    block = P("dp", fsdp)
    stats = (P("dp"), P(fsdp)) * 3
    plain = dp_count == VDP and fsdp_count == 2 * VCHIP
    return jax.shard_map(
        body if plain else body_any,
        mesh=inner,
        in_specs=(split,) * 3 + (block,) * 4 + stats + (block,),
        out_specs=(split,) * 2 + (block,) * 4 + stats + (block,) * 5,
        check_vma=False,
    )
```

```python
import functools
import math

import jax
import jax.numpy as jnp
import numpy as np
from jax import lax
from jax.experimental import pallas as pl
from jax.experimental.pallas import tpu as pltpu
from jax.sharding import PartitionSpec as P

D = 256
FF = 2048
HEADS = 8
HEAD_DIM = 32
SEQ = 1024
HALF = 512
GROUP = 4
LANES = 128
QBLOCK = 512
WGRID = 32
STEP = 10
VEC = 16
TILE = 1024
CHUNK = 256
SUB = 512
LEAD = 5
STRIP = 64
VDP = 4
VCHIP = 4
VROWS = 16

EPS_NORM = 1e-05
EPS_ONE = 1e-30
EPS_TWO = 0.001
CLIP_LIMIT = 1.0
STEP_RATE = 0.3
FAR = 1e30
TAME = 40.0
LOG2_E = math.log2(math.e)
SCALE = HEAD_DIM ** (-0.5)
GELU_A = math.sqrt(2.0 / math.pi)
GELU_B = 0.044715
F32 = jnp.float32
BF16 = jnp.bfloat16
MIB = 1024 * 1024


def dot(left, right):
    return jnp.dot(left, right, preferred_element_type=F32)


def dot_nt(left, right):
    return lax.dot_general(left, right, (((1,), (1,)), ((), ())), preferred_element_type=F32)


def encode_table():
    half = D // 2
    feature = np.arange(half)
    freq = np.exp(
        (2 * (feature // 2)).astype(np.float32) * np.float32(-math.log(10000.0) / half)
    ).astype(np.float32)
    angles = np.arange(1, WGRID + 1, dtype=np.float32)[:, None] * freq[None, :]
    table = np.where(feature % 2 == 0, np.sin(angles), np.cos(angles)).astype(np.float32)
    low = jnp.bfloat16
    one = table.astype(low)
    rest = table - one.astype(np.float32)
    two = rest.astype(low)
    three = (rest - two.astype(np.float32)).astype(low)
    blank = np.zeros((LANES - 3 * WGRID, half), low)
    return np.concatenate([one, two, three, blank], axis=0)


def iota(shape, dim):
    return lax.broadcasted_iota(jnp.int32, shape, dim)


def norm_forward(rows):
    centered = rows - jnp.mean(rows, axis=-1, keepdims=True)
    inverse = lax.rsqrt(jnp.mean(centered * centered, axis=-1, keepdims=True) + EPS_NORM)
    return centered * inverse, inverse


def norm_backward(upstream, normed, inverse):
    return inverse * (
        upstream
        - jnp.mean(upstream, axis=-1, keepdims=True)
        - normed * jnp.mean(upstream * normed, axis=-1, keepdims=True)
    )

def vspec():
    return pl.BlockSpec(memory_space=pltpu.VMEM)


def params(mib=56, **more):
    return pltpu.CompilerParams(vmem_limit_bytes=mib * MIB, **more)


def pack_kernel(place, attn_ref, first_ref, second_ref, vector_ref, out_ref, ffn_ref):
    owner = place[1] * 2 + place[2]
    vector = vector_ref[...]
    rows = vector.shape[0]
    wide = jnp.concatenate([vector] * (LANES // vector.shape[1]), axis=1)
    slot = iota((rows, LANES), 1) // vector.shape[1]
    per = LANES // vector.shape[1]
    parts = [attn_ref[...]]
    for half in range(2):
        parts.append(jnp.where(slot + half * per == owner, wide, 0.0))
    parts.append(jnp.zeros((VROWS - 2 * rows, LANES), F32))
    piece = jnp.concatenate(parts, axis=0).astype(BF16)
    for at in range(VDP * VCHIP):
        out_ref[at] = piece
    ffn_ref[0] = first_ref[...].astype(BF16)
    ffn_ref[1] = second_ref[...].astype(BF16)


def pack_attn(place, attn_weight, ffn_in, ffn_out, vectors):
    return pl.pallas_call(
        pack_kernel,
        out_shape=(
            jax.ShapeDtypeStruct((VDP * VCHIP, attn_weight.shape[0] + VROWS, LANES), BF16),
            jax.ShapeDtypeStruct((2,) + ffn_in.shape, BF16),
        ),
        in_specs=[pl.BlockSpec(memory_space=pltpu.SMEM)] + [vspec()] * 4,
        out_specs=(vspec(), vspec()),
        compiler_params=params(),
        name="pack_attn",
    )(place, attn_weight, ffn_in, ffn_out, vectors)


def pack_ffn_kernel(place, own_ref, *refs):
    out_ref = refs[-1]
    for at in range(VCHIP):
        out_ref[at, pl.ds(place[0], 1)] = own_ref[...][None]
        for step in range(1, VDP):
            out_ref[at, pl.ds(place[0] ^ step, 1)] = refs[step - 1][...][None]


def pack_ffn(place, own, parts):
    return pl.pallas_call(
        pack_ffn_kernel,
        out_shape=jax.ShapeDtypeStruct((VCHIP, VDP) + own.shape, BF16),
        in_specs=[pl.BlockSpec(memory_space=pltpu.SMEM)] + [vspec()] * (1 + len(parts)),
        out_specs=vspec(),
        compiler_params=params(16),
        name="pack_ffn",
    )(place, own, *parts)


def place_kernel(
    segment_ref, tokens_ref, back_ref, table_ref, qk_ref, x_ref, qk_t_ref, x_t_ref, turned_ref, marks_ref
):
    row = pl.program_id(0)
    starts = []
    for number in range(1, 4):
        at = jnp.int32(0)
        for step in (512, 256, 128, 64, 32, 16, 8, 4, 2, 1, 1):
            probe = jnp.minimum(at + (step - 1), SEQ - 1)
            at = jnp.where(segment_ref[row, probe] < number, at + step, at)
        starts.append(at)
    edges = [jnp.int32(0)] + starts + [jnp.int32(SEQ)]
    begin = jnp.int32(0)
    for number in range(3, -1, -1):
        begin = jnp.where(edges[number + 1] - edges[number] == HALF, edges[number], begin)
    for number in range(3):
        marks_ref[row, number] = starts[number]
    marks_ref[row, 3] = begin
    one, two, three = starts
    x = pltpu.roll(tokens_ref[...].astype(F32), (SEQ - begin) & (SEQ - 1), 0)
    x_ref[...] = x.astype(BF16)
    x_t_ref[...] = x.T.astype(BF16)
    back = back_ref[...].astype(F32)
    turned_ref[...] = pltpu.roll(back, (SEQ - begin) & (SEQ - 1), 0).astype(BF16)
    at = (iota((SEQ, LANES), 0) + begin) & (SEQ - 1)
    lane = iota((SEQ, LANES), 1)
    start = jnp.where(at >= three, three, jnp.where(at >= two, two, jnp.where(at >= one, one, 0)))
    local = at - start
    kept = lane < 3 * WGRID
    slot = lane & (WGRID - 1)
    hot_r = jnp.where(((local >> 5) == slot) & kept, 1.0, 0.0).astype(BF16)
    hot_c = jnp.where(((local & (WGRID - 1)) == slot) & kept, 1.0, 0.0).astype(BF16)
    table = table_ref[...]
    places = jnp.concatenate([dot(hot_r, table), dot(hot_c, table)], axis=1)
    qk = x + places
    qk_ref[...] = qk.astype(BF16)
    qk_t_ref[...] = qk.T.astype(BF16)


def place_tokens(segment_ids, tokens, cotangent, table):
    rows = segment_ids.shape[0]
    by_row = lambda r: (r, 0)
    return pl.pallas_call(
        place_kernel,
        out_shape=(
            jax.ShapeDtypeStruct(tokens.shape, BF16),
            jax.ShapeDtypeStruct(tokens.shape, BF16),
            jax.ShapeDtypeStruct((D, tokens.shape[0]), BF16),
            jax.ShapeDtypeStruct((D, tokens.shape[0]), BF16),
            jax.ShapeDtypeStruct(tokens.shape, BF16),
            jax.ShapeDtypeStruct((rows, 4), jnp.int32),
        ),
        grid=(rows,),
        in_specs=[
            pl.BlockSpec(memory_space=pltpu.SMEM),
            pl.BlockSpec((SEQ, D), by_row),
            pl.BlockSpec((SEQ, D), by_row),
            pl.BlockSpec((LANES, LANES), lambda r: (0, 0)),
        ],
        out_specs=(
            pl.BlockSpec((SEQ, D), by_row),
            pl.BlockSpec((SEQ, D), by_row),
            pl.BlockSpec((D, SEQ), lambda r: (0, r)),
            pl.BlockSpec((D, SEQ), lambda r: (0, r)),
            pl.BlockSpec((SEQ, D), by_row),
            pl.BlockSpec(memory_space=pltpu.SMEM),
        ),
        compiler_params=params(dimension_semantics=("arbitrary",)),
        cost_estimate=pl.CostEstimate(flops=600_000_000, bytes_accessed=4_000_000, transcendentals=0),
        name="place_tokens",
    )(segment_ids, tokens, cotangent, table)


def attend_kernel(
    marks,
    place,
    x_ref,
    qk_ref,
    x_t_ref,
    qk_t_ref,
    mine_ref,
    other_ref,
    query_t_ref,
    value_ref,
    key_t_ref,
    out_t_ref,
    inverse_ref,
    mixed_ref,
    mixed_t_ref,
    exps_ref,
    weight_ref,
    proj_ref,
    vector_ref,
    key_s,
    value_s,
    mark_k,
    mark_q,
    first_s,
    second_s,
    weight_t_s,
    bias_s,
    tame_s,
    exps_s,
    exps_sem,
):
    row = pl.program_id(0)
    begin = marks[row, 3]
    core = place[2]

    def copy_of(group, half):
        return pltpu.make_async_copy(
            exps_s.at[group, half], exps_ref.at[row, group, half], exps_sem.at[group * 2 + half]
        )

    @pl.when(row == 0)
    def _():
        tall = D // VDP
        for d in range(VDP):
            rows = slice(d * tall, (d + 1) * tall)
            total = jnp.zeros((8, LANES), F32)
            for c in range(VCHIP):
                for ref, half in ((mine_ref, core), (other_ref, 1 - core)):
                    if c < 3:
                        to = pl.ds(pl.multiple_of(c * D + half * LANES, LANES), LANES)
                        weight_ref[rows, to] = ref[d, c, :tall, :]
                    else:
                        to = pl.ds(pl.multiple_of(half * LANES, LANES), LANES)
                        proj_ref[rows, to] = ref[d, c, :tall, :]
                    total += ref[d, c, tall:, :].astype(F32)[:8]
            vector_ref[d * 4 : (d + 1) * 4, :LANES] = total[:4]
            vector_ref[d * 4 : (d + 1) * 4, LANES:] = total[4:]
        weight_t_s[...] = weight_ref[...].astype(F32).T.astype(BF16)
        bias_s[...] = vector_ref[8:16, :].T

    qk_t = qk_t_ref[...]
    query_t = (dot(weight_t_s[:D, :], qk_t) + bias_s[:, 0:1]) * SCALE
    query_t = query_t.astype(BF16)
    query_t_ref[...] = query_t
    key_t = dot(weight_t_s[D : 2 * D, :], qk_t).astype(BF16)
    key_t_ref[...] = key_t

    def largest_norms(rows):
        rows = rows.astype(F32)
        rows = rows * rows
        sums = [
            jnp.sum(rows[head * HEAD_DIM : (head + 1) * HEAD_DIM], axis=0, keepdims=True)
            for head in range(HEADS)
        ]
        return jnp.max(jnp.concatenate(sums, axis=0), axis=1, keepdims=True)

    bound = jnp.max(largest_norms(query_t) * largest_norms(key_t))
    tame_s[0] = jnp.where(bound <= TAME * TAME, 1, 0)
    key_s[...] = dot(qk_ref[...], weight_ref[:, D : 2 * D]).astype(BF16)
    value = dot(x_ref[...], weight_ref[:, 2 * D : 3 * D]) + vector_ref[9:10, :]
    value_ref[...] = value.astype(BF16)
    value_t = dot(weight_t_s[2 * D :, :], x_t_ref[...]) + bias_s[:, 1:2]
    value_t = value_t.astype(BF16)
    for head in range(HEADS):
        value_s[head, :HEAD_DIM, :] = value_t[head * HEAD_DIM : (head + 1) * HEAD_DIM, :]
        value_s[head, HEAD_DIM:, :] = jnp.ones((16, SEQ), BF16)
    one, two, three = marks[row, 0], marks[row, 1], marks[row, 2]

    def number_of(shape, dim):
        here = (iota(shape, dim) + (HALF + begin)) & (SEQ - 1)
        return (
            jnp.where(here >= one, 1, 0)
            + jnp.where(here >= two, 1, 0)
            + jnp.where(here >= three, 1, 0)
        )

    lane = iota((HALF, LANES), 1)
    number = number_of((HALF, LANES), 0)
    mark_k[...] = jnp.where((number != lane) & (lane < 4), -FAR, 0.0).astype(BF16)
    number = number_of((LANES, HALF), 1)
    mark_q[...] = jnp.where(number == iota((LANES, HALF), 0), 1.0, 0.0).astype(BF16)

    head_of = iota((1, LANES), 1) // HEAD_DIM
    for group in range(2):
        keys_here = key_s[:, group * LANES : (group + 1) * LANES]
        for at_head in range(GROUP):
            mask = jnp.where(head_of == at_head, 1.0, 0.0).astype(BF16)
            rows = slice(at_head * HALF, (at_head + 1) * HALF)
            first_s[group, rows, :] = keys_here[:HALF] * mask
            second_s[group, rows, :LANES] = keys_here[HALF:] * mask
            second_s[group, rows, LANES:] = mark_k[...]

    @pl.when(row > 0)
    def _():
        for group in range(2):
            for half in range(2):
                copy_of(group, half).wait()

    def scores_of(group, half, rows):
        query = query_t_ref[group * LANES : (group + 1) * LANES, half * HALF : (half + 1) * HALF]
        if half == 0:
            return dot(first_s[group, rows, :], query)
        return dot(second_s[group, rows, :], jnp.concatenate([query, mark_q[...]], axis=0))

    def place_of(at_head):
        return slice(at_head * HALF, (at_head + 1) * HALF)

    def exps_plain(group, half):
        scores = scores_of(group, half, slice(0, GROUP * HALF))
        for at_head in range(GROUP):
            exps = jnp.exp2(scores[place_of(at_head), :] * LOG2_E)
            exps_s[group, half, :, place_of(at_head)] = exps.astype(BF16)

    def exps_shifted(group, half):
        for at_head in range(GROUP):
            rows = place_of(at_head)
            largest = jnp.max(scores_of(group, half, rows), axis=0, keepdims=True)
            exps = jnp.exp2((scores_of(group, half, rows) - largest) * LOG2_E)
            exps_s[group, half, :, rows] = exps.astype(BF16)

    def finish(group, half):
        rows = slice(half * HALF, (half + 1) * HALF)
        for at_head in range(GROUP):
            head = group * GROUP + at_head
            out = dot(value_s[head, :, rows], exps_s[group, half, :, place_of(at_head)])
            inverse = 1.0 / out[HEAD_DIM : HEAD_DIM + 1, :]
            inverse_ref[group, at_head : at_head + 1, rows] = inverse
            out_t_ref[head * HEAD_DIM : (head + 1) * HEAD_DIM, rows] = out[:HEAD_DIM, :] * inverse

    def run(exps_of):
        items = [(group, half) for group in range(2) for half in range(2)]
        for i in range(len(items) + 1):
            if i < len(items):
                exps_of(*items[i])
                copy_of(*items[i]).start()
            if i >= 1:
                finish(*items[i - 1])

    @pl.when(tame_s[0] == 1)
    def _():
        run(exps_plain)

    @pl.when(tame_s[0] == 0)
    def _():
        run(exps_shifted)

    out_t = out_t_ref[...]
    mixed_t_ref[...] = out_t.astype(BF16)
    mixed_ref[...] = out_t.T.astype(BF16)

    @pl.when(row == pl.num_programs(0) - 1)
    def _():
        for group in range(2):
            for half in range(2):
                copy_of(group, half).wait()


def attend_forward(marks, place, x, qk, x_t, qk_t, mine, other):
    total = x.shape[0]
    rows = total // SEQ
    by_row = lambda r, m, p: (r, 0)
    by_col = lambda r, m, p: (0, r)
    whole = lambda r, m, p: (0, 0)
    return pl.pallas_call(
        attend_kernel,
        out_shape=(
            jax.ShapeDtypeStruct((D, total), BF16),
            jax.ShapeDtypeStruct((total, D), BF16),
            jax.ShapeDtypeStruct((D, total), BF16),
            jax.ShapeDtypeStruct((D, total), F32),
            jax.ShapeDtypeStruct((2, 8, total), F32),
            jax.ShapeDtypeStruct((total, D), BF16),
            jax.ShapeDtypeStruct((D, total), BF16),
            jax.ShapeDtypeStruct((rows, 2, 2, HALF, GROUP * HALF), BF16),
            jax.ShapeDtypeStruct((D, 3 * D), BF16),
            jax.ShapeDtypeStruct((D, D), BF16),
            jax.ShapeDtypeStruct((VEC, D), F32),
        ),
        grid_spec=pltpu.PrefetchScalarGridSpec(
            num_scalar_prefetch=2,
            grid=(rows,),
            in_specs=[
                pl.BlockSpec((SEQ, D), by_row),
                pl.BlockSpec((SEQ, D), by_row),
                pl.BlockSpec((D, SEQ), by_col),
                pl.BlockSpec((D, SEQ), by_col),
                vspec(),
                vspec(),
            ],
            out_specs=[
                pl.BlockSpec((D, SEQ), by_col),
                pl.BlockSpec((SEQ, D), by_row),
                pl.BlockSpec((D, SEQ), by_col),
                pl.BlockSpec((D, SEQ), by_col),
                pl.BlockSpec((2, 8, SEQ), lambda r, m, p: (0, 0, r)),
                pl.BlockSpec((SEQ, D), by_row),
                pl.BlockSpec((D, SEQ), by_col),
                pl.BlockSpec(memory_space=pl.ANY),
                pl.BlockSpec((D, 3 * D), whole),
                pl.BlockSpec((D, D), whole),
                pl.BlockSpec((VEC, D), whole),
            ],
            scratch_shapes=[
                pltpu.VMEM((SEQ, D), BF16),
                pltpu.VMEM((HEADS, HEAD_DIM + 16, SEQ), BF16),
                pltpu.VMEM((HALF, LANES), BF16),
                pltpu.VMEM((LANES, HALF), BF16),
                pltpu.VMEM((2, GROUP * HALF, LANES), BF16),
                pltpu.VMEM((2, GROUP * HALF, 2 * LANES), BF16),
                pltpu.VMEM((3 * D, D), BF16),
                pltpu.VMEM((D, 8), F32),
                pltpu.SMEM((1,), jnp.int32),
                pltpu.VMEM((2, 2, HALF, GROUP * HALF), BF16),
                pltpu.SemaphoreType.DMA((4,)),
            ],
        ),
        compiler_params=params(dimension_semantics=("arbitrary",)),
        cost_estimate=pl.CostEstimate(
            flops=20_000_000_000, bytes_accessed=30_000_000, transcendentals=8_400_000
        ),
        name="attend_forward",
    )(marks, place, x, qk, x_t, qk_t, mine, other)


def feed_kernel(
    marks,
    place,
    x_ref,
    back_ref,
    mixed_ref,
    mixed_t_ref,
    proj_ref,
    mine_ref,
    other_ref,
    vector_ref,
    block_ref,
    resid_ref,
    mixed_grad_ref,
    mine_out,
    other_out,
    proj_out,
    vector_out,
    first_w,
    second_w,
    first_acc,
    second_acc,
    proj_acc,
    vector_acc,
    hidden_s,
    slope_s,
    pre_s,
    first_low_s,
    branch_low_s,
    attended_s,
    block_s,
    eye_s,
):
    step = pl.program_id(0)
    core = place[2]
    tall = D // VDP
    wide = FF // (2 * VCHIP)

    @pl.when(step == 0)
    def _():
        first_acc[...] = jnp.zeros_like(first_acc)
        second_acc[...] = jnp.zeros_like(second_acc)
        proj_acc[...] = jnp.zeros_like(proj_acc)
        vector_acc[...] = jnp.zeros_like(vector_acc)
        eye_s[...] = jnp.where(iota((D, D), 0) == iota((D, D), 1), 1.0, 0.0).astype(BF16)
        for d in range(VDP):
            rows = slice(d * tall, (d + 1) * tall)
            for c in range(VCHIP):
                for ref, half in ((mine_ref, core), (other_ref, 1 - core)):
                    to = pl.ds(pl.multiple_of((2 * c + half) * wide, wide), wide)
                    first_w[rows, to] = ref[c, d, 0]
                    second_w[rows, to] = ref[c, d, 1]

    bias_o, bias_2 = vector_ref[10:11, :], vector_ref[11:12, :]
    gain_1, shift_1 = vector_ref[12:13, :], vector_ref[13:14, :]
    gain_2, shift_2 = vector_ref[14:15, :], vector_ref[15:16, :]
    at_row = pl.multiple_of((step % (SEQ // TILE)) * TILE, TILE)
    chunks = FF // CHUNK
    pair = 2

    def columns(at, count=1):
        return slice(at * CHUNK, (at + count) * CHUNK)

    def hidden_of(rows, at, pre):
        per = CHUNK // D
        bias = [vector_ref[at * per + i : at * per + i + 1, :] for i in range(per)]
        pre = (pre + jnp.concatenate(bias, axis=1)).astype(BF16)
        cube = BF16(GELU_A * GELU_B) * (pre * pre)
        gate = BF16(0.5) + BF16(0.5) * jnp.tanh(pre * (cube + BF16(GELU_A)))
        hidden_s[rows, columns(at)] = pre * gate
        slope_s[rows, columns(at)] = gate + (gate - gate * gate) * (
            pre * (BF16(6.0) * cube + BF16(2.0 * GELU_A))
        )

    def stages(sub):
        rows_at = sub * SUB
        rows = slice(rows_at, rows_at + SUB)
        attended = dot(mixed_ref[rows, :], proj_ref[...]) + bias_o
        norm_1, inverse_1 = norm_forward(x_ref[rows, :].astype(F32) + attended)
        first = norm_1 * gain_1 + shift_1
        first_low = first.astype(BF16)
        first_low_s[rows, :] = first_low
        yield
        branch = jnp.zeros((SUB, D), F32)
        for i in range(chunks + 1):
            if i < chunks:
                hidden_of(rows, i, dot(first_low, first_w[:, columns(i)]))
            if i >= pair and i % pair == 0:
                cols = columns(i - pair, pair)
                branch += dot_nt(hidden_s[rows, cols], second_w[:, cols])
            yield
        norm_2, inverse_2 = norm_forward(first + (branch + bias_2))
        block_s[pl.ds(at_row + rows_at, SUB), :] = norm_2 * gain_2 + shift_2
        back = back_ref[rows, :].astype(F32)
        vector_acc[14:15, :] += jnp.sum(back * norm_2, axis=0, keepdims=True)
        vector_acc[15:16, :] += jnp.sum(back, axis=0, keepdims=True)
        resid_2 = norm_backward(back * gain_2, norm_2, inverse_2)
        branch_low = resid_2.astype(BF16)
        branch_low_s[rows, :] = branch_low
        vector_acc[11:12, :] += jnp.sum(branch_low.astype(F32), axis=0, keepdims=True)
        yield
        first_back = resid_2
        if sub == 1:
            branch_t = dot_nt(eye_s[...], branch_low_s[...]).astype(BF16)
            first_t = dot_nt(eye_s[...], first_low_s[...]).astype(BF16)
            first_t = jnp.concatenate([first_t, jnp.ones((16, TILE), BF16)], axis=0)
        for i in range(chunks + 1):
            if i < chunks:
                pull = dot(branch_low, second_w[:, columns(i)]).astype(BF16)
                pre_s[rows, columns(i)] = pull * slope_s[rows, columns(i)]
                if sub == 1:
                    second_acc[:, columns(i)] += dot(branch_t, hidden_s[:, columns(i)])
            if i >= 1 and sub == 1:
                cols = columns(i - 1)
                first_acc[:, cols] += dot(first_t, pre_s[:, cols])
            if i >= pair and i % pair == 0:
                cols = columns(i - pair, pair)
                first_back += dot_nt(pre_s[rows, cols], first_w[:, cols])
            yield
        vector_acc[12:13, :] += jnp.sum(first_back * norm_1, axis=0, keepdims=True)
        vector_acc[13:14, :] += jnp.sum(first_back, axis=0, keepdims=True)
        resid_1 = norm_backward(first_back * gain_1, norm_1, inverse_1)
        resid_ref[rows, :] = resid_1
        attended_low = resid_1.astype(BF16)
        attended_s[rows, :] = attended_low
        vector_acc[10:11, :] += jnp.sum(attended_low.astype(F32), axis=0, keepdims=True)
        mixed_grad_ref[:, rows] = dot_nt(proj_ref[...], attended_low).astype(BF16)
        yield

    ahead, behind = stages(0), stages(1)
    for _ in range(LEAD):
        next(ahead)
    running = [ahead, behind]
    while running:
        for program in list(running):
            if next(program, 0) == 0:
                running.remove(program)
    proj_acc[...] += dot(mixed_t_ref[...], attended_s[...])

    @pl.when(step % (SEQ // TILE) == SEQ // TILE - 1)
    def _():
        block_ref[...] = pltpu.roll(block_s[...], marks[step // (SEQ // TILE), 3], 0)

    @pl.when(step == pl.num_programs(0) - 1)
    def _():
        for d in range(VDP):
            rows = slice(d * tall, (d + 1) * tall)
            for c in range(VCHIP):
                for ref, half in ((mine_out, core), (other_out, 1 - core)):
                    to = pl.ds(pl.multiple_of((2 * c + half) * wide, wide), wide)
                    ref[d, c, 0] = first_acc[rows, to].astype(BF16)
                    ref[d, c, 1] = second_acc[rows, to].astype(BF16)
        proj_out[...] = proj_acc[...]
        for at in range(FF // D):
            vector_out[at : at + 1, :] = first_acc[D : D + 1, at * D : (at + 1) * D]
        vector_out[FF // D :, :] = vector_acc[FF // D :, :]


def feed_forward(marks, place, x, back, mixed, mixed_t, proj, mine, other, vector):
    total = x.shape[0]
    tile = lambda i, m, p: (i, 0)
    by_col = lambda i, m, p: (0, i)
    whole = lambda i, m, p: (0, 0)
    whole5 = lambda i, m, p: (0, 0, 0, 0, 0)
    return pl.pallas_call(
        feed_kernel,
        out_shape=(
            jax.ShapeDtypeStruct((total, D), F32),
            jax.ShapeDtypeStruct((total, D), F32),
            jax.ShapeDtypeStruct((D, total), BF16),
            jax.ShapeDtypeStruct(mine.shape, BF16),
            jax.ShapeDtypeStruct(mine.shape, BF16),
            jax.ShapeDtypeStruct((D, D), F32),
            jax.ShapeDtypeStruct((VEC, D), F32),
        ),
        grid_spec=pltpu.PrefetchScalarGridSpec(
            num_scalar_prefetch=2,
            grid=(total // TILE,),
            in_specs=[
                pl.BlockSpec((TILE, D), tile),
                pl.BlockSpec((TILE, D), tile),
                pl.BlockSpec((TILE, D), tile),
                pl.BlockSpec((D, TILE), by_col),
                pl.BlockSpec((D, D), whole),
                vspec(),
                vspec(),
                pl.BlockSpec((VEC, D), whole),
            ],
            out_specs=[
                pl.BlockSpec((SEQ, D), lambda i, m, p: (i // (SEQ // TILE), 0)),
                pl.BlockSpec((TILE, D), tile),
                pl.BlockSpec((D, TILE), by_col),
                pl.BlockSpec(mine.shape, whole5),
                pl.BlockSpec(mine.shape, whole5),
                pl.BlockSpec((D, D), whole),
                pl.BlockSpec((VEC, D), whole),
            ],
            scratch_shapes=[
                pltpu.VMEM((D, FF), BF16),
                pltpu.VMEM((D, FF), BF16),
                pltpu.VMEM((D + 16, FF), F32),
                pltpu.VMEM((D, FF), F32),
                pltpu.VMEM((D, D), F32),
                pltpu.VMEM((VEC, D), F32),
                pltpu.VMEM((TILE, FF), BF16),
                pltpu.VMEM((TILE, FF), BF16),
                pltpu.VMEM((TILE, FF), BF16),
                pltpu.VMEM((TILE, D), BF16),
                pltpu.VMEM((TILE, D), BF16),
                pltpu.VMEM((TILE, D), BF16),
                pltpu.VMEM((SEQ, D), F32),
                pltpu.VMEM((D, D), BF16),
            ],
        ),
        compiler_params=params(dimension_semantics=("arbitrary",)),
        cost_estimate=pl.CostEstimate(
            flops=14_000_000_000, bytes_accessed=15_000_000, transcendentals=4_200_000
        ),
        name="feed_forward",
    )(marks, place, x, back, mixed, mixed_t, proj, mine, other, vector)


def pull_kernel(
    marks,
    place,
    grad_t_ref,
    query_t_ref,
    value_ref,
    key_t_ref,
    out_t_ref,
    inverse_ref,
    exps_ref,
    qk_t_ref,
    x_t_ref,
    weight_ref,
    proj_ref,
    resid_ref,
    pulled_ref,
    own_ref,
    other_ref,
    sums_ref,
    dot_s,
    query_g,
    key_g,
    value_g,
    acc,
    sum_acc,
    value_s,
    scaled_t_s,
    score_s,
    pulled_s,
):
    group = pl.program_id(0)
    row = pl.program_id(1)
    begin = marks[row, 3]

    @pl.when(row == 0)
    def _():
        acc[...] = jnp.zeros_like(acc)
        sum_acc[...] = jnp.zeros_like(sum_acc)

    grad_t = grad_t_ref[...].astype(F32)
    head_of = iota((1, LANES), 1) // HEAD_DIM
    for at_head in range(GROUP):
        heads = slice(at_head * HEAD_DIM, (at_head + 1) * HEAD_DIM)
        part = grad_t[heads, :] * inverse_ref[0, at_head : at_head + 1, :]
        dot_s[at_head : at_head + 1, :] = jnp.sum(part * out_t_ref[heads, :], axis=0, keepdims=True)
        part = part.astype(BF16)
        scaled_t_s[heads, :] = part
        mask = jnp.where(head_of == at_head, 1.0, 0.0).astype(BF16)
        for half in range(2):
            rows = slice(half * HALF, (half + 1) * HALF)
            to = slice(at_head * HALF, (at_head + 1) * HALF)
            value_s[half, to, :] = value_ref[rows, :] * mask

    def score_grads_of(half, block):
        at = half * HALF + block * QBLOCK
        pulls = dot(value_s[half], scaled_t_s[:, at : at + QBLOCK])
        for at_head in range(GROUP):
            cols = slice(at_head * HALF + block * QBLOCK, at_head * HALF + (block + 1) * QBLOCK)
            pull = pulls[at_head * HALF : (at_head + 1) * HALF, :]
            pull = (pull - dot_s[at_head : at_head + 1, at : at + QBLOCK]).astype(BF16)
            score_s[half, :, cols] = exps_ref[0, 0, half, :, cols] * pull

    def finish(half, at_head):
        cols = slice(at_head * HALF, (at_head + 1) * HALF)
        rows = slice(half * HALF, (half + 1) * HALF)
        heads = slice(at_head * HEAD_DIM, (at_head + 1) * HEAD_DIM)
        score_grad = score_s[half, :, cols]
        value_g[heads, rows] = dot_nt(scaled_t_s[heads, rows], exps_ref[0, 0, half, :, cols])
        query_g[heads, rows] = dot(key_t_ref[heads, rows], score_grad)
        key_g[heads, rows] = dot_nt(query_t_ref[heads, rows], score_grad)

    blocks = HALF // QBLOCK
    each = GROUP // blocks
    for block in range(blocks):
        score_grads_of(0, block)
    for block in range(blocks):
        score_grads_of(1, block)
        for at_head in range(each * block, each * (block + 1)):
            finish(0, at_head)
    for at_head in range(GROUP):
        finish(1, at_head)
    query_low = query_g[...].astype(BF16)
    both_low = jnp.concatenate([key_g[...].astype(BF16), value_g[...].astype(BF16)], axis=0)
    ones = jnp.ones((16, SEQ), BF16)
    sum_acc[0:1, :] += dot_nt(ones, query_low)[0:1, :] * SCALE
    sum_acc[1:2, :] += dot_nt(ones, both_low[LANES:, :])[0:1, :]
    qk_t = qk_t_ref[...]
    both = dot_nt(qk_t, jnp.concatenate([query_low, both_low[:LANES, :]], axis=0))
    acc[:, :LANES] += both[:, :LANES] * SCALE
    acc[:, LANES : 2 * LANES] += both[:, LANES:]
    acc[:, 2 * LANES :] += dot_nt(x_t_ref[...], both_low[LANES:, :])
    at = [pl.ds(pl.multiple_of(i * D + group * LANES, LANES), LANES) for i in range(3)]
    pulled = dot(weight_ref[:, at[0]], query_low) * SCALE + dot(
        jnp.concatenate([weight_ref[:, at[1]], weight_ref[:, at[2]]], axis=1), both_low
    )

    @pl.when(group == 0)
    def _():
        pulled_s[row] = pulled

    @pl.when(group == 1)
    def _():
        both = (pulled + pulled_s[row]).T
        pulled_ref[...] = pltpu.roll(resid_ref[...] + both, begin, 0)

    def write(ref):
        tall = D // VDP
        for d in range(VDP):
            rows = slice(d * tall, (d + 1) * tall)
            for c in range(3):
                ref[d, c] = acc[rows, c * LANES : (c + 1) * LANES].astype(BF16)
            ref[d, 3] = proj_ref[rows, :].astype(BF16)

    last = row == pl.num_programs(1) - 1

    @pl.when(last & (group == place[2]))
    def _():
        write(own_ref)

    @pl.when(last & (group != place[2]))
    def _():
        write(other_ref)

    @pl.when(last)
    def _():
        sums_ref[pl.ds(group, 1)] = sum_acc[...][None]


def attend_back(marks, place, grad_t, query_t, value, key_t, out_t, inverse, exps, qk_t, x_t, weight, proj, resid):
    total = value.shape[0]
    rows = total // SEQ
    by_both = lambda g, r, m, p: (g, r)
    by_col = lambda g, r, m, p: (0, r)
    later = lambda g, r, m, p: (g * r, 0)
    whole = lambda g, r, m, p: (0, 0)
    grads = jax.ShapeDtypeStruct((VDP, VCHIP, D // VDP, LANES), BF16)
    grads_spec = pl.BlockSpec(grads.shape, lambda g, r, m, p: (0, 0, 0, 0))
    return pl.pallas_call(
        pull_kernel,
        out_shape=(
            jax.ShapeDtypeStruct((total, D), F32),
            grads,
            grads,
            jax.ShapeDtypeStruct((2, 8, LANES), F32),
        ),
        grid_spec=pltpu.PrefetchScalarGridSpec(
            num_scalar_prefetch=2,
            grid=(2, rows),
            in_specs=[
                pl.BlockSpec((LANES, SEQ), by_both),
                pl.BlockSpec((LANES, SEQ), by_both),
                pl.BlockSpec((SEQ, LANES), lambda g, r, m, p: (r, g)),
                pl.BlockSpec((LANES, SEQ), by_both),
                pl.BlockSpec((LANES, SEQ), by_both),
                pl.BlockSpec((1, 8, SEQ), lambda g, r, m, p: (g, 0, r)),
                pl.BlockSpec((1, 1, 2, HALF, GROUP * HALF), lambda g, r, m, p: (r, g, 0, 0, 0)),
                pl.BlockSpec((D, SEQ), by_col),
                pl.BlockSpec((D, SEQ), by_col),
                pl.BlockSpec((D, 3 * D), whole),
                pl.BlockSpec((D, LANES), lambda g, r, m, p: (0, g)),
                pl.BlockSpec((SEQ, D), later),
            ],
            out_specs=[
                pl.BlockSpec((SEQ, D), later),
                grads_spec,
                grads_spec,
                pl.BlockSpec((2, 8, LANES), lambda g, r, m, p: (0, 0, 0)),
            ],
            scratch_shapes=[
                pltpu.VMEM((8, SEQ), F32),
                pltpu.VMEM((LANES, SEQ), F32),
                pltpu.VMEM((LANES, SEQ), F32),
                pltpu.VMEM((LANES, SEQ), F32),
                pltpu.VMEM((D, 3 * LANES), F32),
                pltpu.VMEM((8, LANES), F32),
                pltpu.VMEM((2, GROUP * HALF, LANES), BF16),
                pltpu.VMEM((LANES, SEQ), BF16),
                pltpu.VMEM((2, HALF, GROUP * HALF), BF16),
                pltpu.VMEM((rows, D, SEQ), F32),
            ],
        ),
        compiler_params=params(dimension_semantics=("arbitrary", "arbitrary")),
        cost_estimate=pl.CostEstimate(
            flops=36_000_000_000, bytes_accessed=30_000_000, transcendentals=0
        ),
        name="attend_back",
    )(marks, place, grad_t, query_t, value, key_t, out_t, inverse, exps, qk_t, x_t, weight, proj, resid)


def two_terms(rows):
    high = rows.astype(BF16)
    return jnp.concatenate([high.astype(F32), rows - high.astype(F32)], axis=0)


def column_to_row(columns, rows):
    lane = iota((rows, LANES), 1)
    wide = jnp.zeros((rows, LANES), F32)
    for i, column in enumerate(columns):
        wide = jnp.where(lane == i, column, wide)
    return wide.T[:8, :]


def total_of(array):
    return jnp.sum(jnp.sum(array, axis=0, keepdims=True), axis=1, keepdims=True)


def tail_ffn_kernel(place, ffn_ref, rows_1, rows_2, last_ref, grad_1, grad_2, grad_ref, stat_ref):
    lane = iota((1, LANES), 1)
    piece, across = [], []
    for kind in range(2):
        total = ffn_ref[0, kind].astype(F32)
        for at in range(1, VDP * VCHIP):
            total = total + ffn_ref[at, kind].astype(F32)
        (grad_1, grad_2)[kind][...] = total
        grad_ref[kind] = total
        square = total * total + EPS_ONE
        down = jnp.sum(square, axis=0, keepdims=True)
        piece += [down[:, :LANES], down[:, LANES:]]
        across.append(jnp.sum(square, axis=1, keepdims=True))
    across = column_to_row(across, total.shape[0])
    across = jnp.concatenate([across[0:1], across[1:2]], axis=1)
    olds = jnp.zeros((1, LANES), F32)
    for i, ref in enumerate((rows_1, rows_2)):
        olds = jnp.where(lane == i, jnp.sum(ref[...], axis=1, keepdims=True), olds)
    stat_ref[...] = jnp.concatenate([across] + piece + [olds, jnp.zeros((2, LANES), F32)], axis=0)


def tail_send_kernel(
    place, mine_ref, got_ref, vector_ref, sums_ref, stat_ref, stat_other_ref, send_ref
):
    tall = D // VDP
    low, high = sums_ref[0], sums_ref[1]
    vector = jnp.concatenate(
        [
            vector_ref[:8, :],
            jnp.concatenate([low[:2], high[:2]], axis=1),
            vector_ref[10:, :],
        ],
        axis=0,
    )
    stat = jnp.concatenate([stat_ref[0:1, :] + stat_other_ref[0:1, :], stat_ref[1:6, :]], axis=0)
    stat = two_terms(stat)
    rows = VEC // VDP
    for d in range(VDP):
        for c in range(VCHIP):
            at = d * VCHIP + c
            both = mine_ref[d, c].astype(F32) + got_ref[d, c].astype(F32)
            send_ref[at, :tall, :] = both.astype(BF16)
            part = vector[d * rows : (d + 1) * rows, c * 64 : (c + 1) * 64]
            part = jnp.concatenate([part, jnp.zeros((rows, LANES - 64), F32)], axis=1)
            send_ref[at, tall:, :] = jnp.concatenate([part, stat], axis=0).astype(BF16)


def tail_reduce_kernel(
    place,
    got_ref,
    ffn_grad_ref,
    attn_ref,
    first_ref,
    second_ref,
    rows_0,
    rows_1,
    rows_2,
    cols_0,
    cols_1,
    cols_2,
    vector_ref,
    moment_ref,
    grad_ref,
    update_1,
    update_2,
    rows_out_1,
    rows_out_2,
    cols_out_1,
    cols_out_2,
    send_ref,
):
    decay = 1.0 - STEP ** (-0.8)
    chip = place[1]
    dp = place[0]
    tall = attn_ref.shape[0]
    rows, width = vector_ref.shape
    pieces = VDP * VCHIP
    lane = iota((1, LANES), 1)
    total = got_ref[0, :tall, :].astype(F32)
    part = got_ref[0, tall:, :].astype(F32)[:rows]
    for at in range(1, pieces):
        total = total + got_ref[at, :tall, :].astype(F32)
        part = part + got_ref[at, tall:, :].astype(F32)[:rows]
    grad_ref[...] = total
    low = total.astype(BF16)

    def stat_of(at):
        both = got_ref[pl.ds(at, 1), tall:, :][0].astype(F32)[rows:]
        return both[:6] + both[6:12]

    every = jnp.zeros((1, LANES), F32)
    olds = jnp.zeros((1, LANES), F32)
    mine = jnp.zeros((1, LANES), F32)
    down = jnp.zeros((6, LANES), F32)
    for d in range(VDP):
        down = down + stat_of(d * VCHIP + chip)
        for c in range(VCHIP):
            stat = stat_of(d * VCHIP + c)
            every = every + stat[0:1]
            if c == 0:
                olds = olds + stat[5:6]
    for c in range(VCHIP):
        mine = mine + stat_of(dp * VCHIP + c)[0:1]
    row_total = tall * VDP
    new_rows, means = [], []
    for i, ref in enumerate((rows_1, rows_2)):
        count = first_ref.shape[1] * 2 * VCHIP
        new_rows.append(decay * ref[...] + (1.0 - decay) * (mine[:, i * tall : (i + 1) * tall] / count))
        old = jnp.sum(jnp.where(lane == i, olds, 0.0), axis=1, keepdims=True)
        fresh = jnp.sum(every[:, i * tall : (i + 1) * tall], axis=1, keepdims=True)
        means.append((decay * old + (1.0 - decay) * (fresh / count)) / row_total)
    tile = jnp.concatenate(new_rows + [jnp.zeros((6, tall), F32)], axis=0)
    rows_out_1[...] = new_rows[0]
    rows_out_2[...] = new_rows[1]
    tile = jnp.concatenate([tile, jnp.zeros((8, LANES - tall), F32)], axis=1)
    turned = jnp.concatenate([tile, jnp.zeros((LANES - 8, LANES), F32)], axis=0).T
    scalars = jnp.zeros((1, LANES), F32)
    for i, (old_ref, out_ref, to) in enumerate(
        ((cols_1, cols_out_1, update_1), (cols_2, cols_out_2, update_2))
    ):
        sums = jnp.concatenate([down[1 + 2 * i : 2 + 2 * i], down[2 + 2 * i : 3 + 2 * i]], axis=1)
        cols = decay * old_ref[...] + (1.0 - decay) * (sums / row_total)
        out_ref[...] = cols
        grad = ffn_grad_ref[i]
        update = grad * lax.rsqrt(turned[:tall, i : i + 1] * cols / means[i])
        to[...] = update
        scalars = jnp.where(lane == 67 + i, total_of(update * update), scalars)
    for i, ref in enumerate((attn_ref, first_ref, second_ref)):
        weight = ref[...]
        scalars = jnp.where(lane == 64 + i, total_of(weight * weight), scalars)
    scalars = jnp.concatenate([rows_0[...], scalars[:, tall:]], axis=1)
    vector = vector_ref[...]
    power = jnp.sum(vector * vector, axis=1, keepdims=True)
    lines = jnp.concatenate(
        [part[:, :64], moment_ref[...], jnp.broadcast_to(power, (rows, LANES - 64 - width))], axis=1
    )
    piece = jnp.concatenate(
        [two_terms(lines), two_terms(jnp.concatenate([cols_0[...], scalars], axis=0))]
        + [jnp.zeros((4, LANES), F32)],
        axis=0,
    ).astype(BF16)
    for at in range(pieces):
        send_ref[at, :tall, :] = low
        send_ref[at, tall:, :] = piece


def tail_apply_kernel(
    place,
    mine_ref,
    other_ref,
    grad_ref,
    update_1,
    update_2,
    weight_0,
    weight_1,
    weight_2,
    rows_0,
    cols_0,
    vector_ref,
    moment_ref,
    new_0,
    new_1,
    new_2,
    rows_out,
    cols_out,
    vector_grad_ref,
    moment_out,
    vector_out,
    sums_s,
    rows_s,
):
    decay = 1.0 - STEP ** (-0.8)
    dp, chip, core = place[0], place[1], place[2]
    tall = weight_0.shape[0]
    rows, width = vector_ref.shape
    fsdp = 2 * VCHIP
    lane = iota((1, LANES), 1)
    refs = (mine_ref, other_ref)
    row_total = float(tall * VDP)
    col_total = float(LANES * fsdp)

    def lines_of(ref, at):
        both = ref[at, tall:, :].astype(F32)
        return both[0:4] + both[4:8], both[8:10] + both[10:12]

    scalars = jnp.zeros((1, LANES), F32)
    for ref in refs:
        for at in range(VDP * VCHIP):
            scalars = scalars + lines_of(ref, at)[1][1:2]
    scalar = lambda at: jnp.sum(jnp.where(lane == at, scalars, 0.0), axis=1, keepdims=True)

    tile, fresh = [], []
    for d in range(VDP):
        wide = jnp.zeros((tall, LANES), F32)
        for ref in refs:
            for c in range(VCHIP):
                block = ref[d * VCHIP + c, :tall, :].astype(F32)
                wide = wide + (block * block + EPS_ONE)
        fresh.append(jnp.sum(wide, axis=1, keepdims=True))
        tile.append(lines_of(mine_ref, d * VCHIP)[1][1:2])
    tile = jnp.concatenate(tile + [jnp.zeros((LANES - VDP, LANES), F32)], axis=0).T
    mean = jnp.zeros((1, 1), F32)
    new_rows = []
    for d in range(VDP):
        new = decay * tile[:tall, d : d + 1] + (1.0 - decay) * (fresh[d] / col_total)
        new_rows.append(1.0 / new)
        mean = mean + jnp.sum(new, axis=0, keepdims=True)
        sums_s[d] = jnp.broadcast_to(fresh[d], (tall, LANES))
    mean = mean / row_total
    mine = sums_s[pl.ds(dp, 1)][0]
    rows_s[...] = mine.T
    rows_new = decay * rows_0[...] + (1.0 - decay) * (rows_s[0:1, :tall] / col_total)
    rows_out[...] = rows_new
    power = jnp.zeros((1, 1), F32)
    for half, ref in enumerate(refs):
        for c in range(VCHIP):
            down = jnp.zeros((tall, LANES), F32)
            weighted = jnp.zeros((tall, LANES), F32)
            for d in range(VDP):
                block = ref[d * VCHIP + c, :tall, :].astype(F32)
                square = block * block
                down = down + (square + EPS_ONE)
                weighted = weighted + square * new_rows[d]
            down = jnp.sum(down, axis=0, keepdims=True)
            old = lines_of(ref, c)[1][0:1]
            cols = decay * old + (1.0 - decay) * (down / row_total)
            weighted = jnp.sum(weighted, axis=0, keepdims=True) / cols
            power = power + jnp.sum(weighted, axis=1, keepdims=True)
            if half == 0:
                sums_s[VDP + c] = jnp.broadcast_to(down, (tall, LANES))
    power = power * mean
    down = sums_s[pl.ds(VDP + chip, 1)][0][0:1, :]
    cols_new = decay * cols_0[...] + (1.0 - decay) * (down / row_total)
    cols_out[...] = cols_new
    column = jnp.concatenate(
        [
            jnp.concatenate([rows_new, jnp.zeros((1, LANES - tall), F32)], axis=1),
            jnp.zeros((LANES - 1, LANES), F32),
        ],
        axis=0,
    ).T[:tall, 0:1]
    update_0 = grad_ref[...] * lax.rsqrt(column * cols_new / mean)
    powers = (power, scalar(67), scalar(68))
    for i, (update, weight, new) in enumerate(
        (
            (update_0, weight_0, new_0),
            (update_1[...], weight_1, new_1),
            (update_2[...], weight_2, new_2),
        )
    ):
        entries = float(weight.shape[0] * weight.shape[1] * VDP * fsdp)
        clip = jnp.maximum(1.0, jnp.sqrt(powers[i] / entries) / CLIP_LIMIT)
        rate = STEP_RATE * jnp.maximum(EPS_TWO, jnp.sqrt(scalar(64 + i) / entries))
        new[...] = weight[...] - rate / clip * update
    powers, sizes = [], []
    for d in range(VDP):
        power = jnp.zeros((rows, 1), F32)
        size = jnp.zeros((rows, 1), F32)
        for c in range(VCHIP):
            at = d * VCHIP + c
            first, second = lines_of(mine_ref, at)[0], lines_of(other_ref, at)[0]
            both = first[:, :64] + second[:, :64]
            size = size + first[:, LANES - 1 :] + second[:, LANES - 1 :]
            near = jnp.where(core == 0, first[:, 64 : 64 + width], second[:, 64 : 64 + width])
            far = jnp.where(core == 0, second[:, 64 : 64 + width], first[:, 64 : 64 + width])
            moment = jnp.concatenate([near, far], axis=1)
            moment = decay * moment + (1.0 - decay) * (both * both + EPS_ONE)
            power = power + jnp.sum(both * both / moment, axis=1, keepdims=True)
            wide = jnp.concatenate([both, jnp.zeros((rows, LANES - 64), F32)], axis=1)
            sums_s[2 * VDP + at, :rows, :] = wide
        powers.append(power)
        sizes.append(size)
    both = sums_s[pl.ds(2 * VDP + dp * VCHIP + chip, 1), :rows, :][0]
    vector_grad = jnp.where(core == 0, both[:, :width], both[:, width : 2 * width])
    vector_grad_ref[...] = vector_grad
    moment = decay * moment_ref[...] + (1.0 - decay) * (vector_grad * vector_grad + EPS_ONE)
    moment_out[...] = moment
    step = vector_grad * lax.rsqrt(moment)
    bias = VDP // 2
    bias_power = sum(jnp.sum(power, axis=0, keepdims=True) for power in powers[:bias])
    bias_size = sum(jnp.sum(size, axis=0, keepdims=True) for size in sizes[:bias])
    power, size = powers[bias], sizes[bias]
    for d in range(bias + 1, VDP):
        power = jnp.where(dp == d, powers[d], power)
        size = jnp.where(dp == d, sizes[d], size)
    is_bias = dp < bias
    power = jnp.where(is_bias, bias_power, power)
    size = jnp.where(is_bias, bias_size, size)
    count = jnp.where(is_bias, float(FF), float(D))
    clip = jnp.maximum(1.0, jnp.sqrt(power / count) / CLIP_LIMIT)
    rate = STEP_RATE * jnp.maximum(EPS_TWO, jnp.sqrt(size / count))
    vector_out[...] = vector_ref[...] - rate / clip * step


def whole_call(kernel, name, place, outs, *operands, scratch=()):
    return pl.pallas_call(
        kernel,
        out_shape=[jax.ShapeDtypeStruct(shape, kind) for shape, kind in outs],
        in_specs=[pl.BlockSpec(memory_space=pltpu.SMEM)] + [vspec()] * len(operands),
        out_specs=[vspec()] * len(outs),
        scratch_shapes=list(scratch),
        compiler_params=params(16),
        name=name,
    )(place, *operands)


def core_swap(block):
    return lax.ppermute(block, "core", [(0, 1), (1, 0)])


def exchange(blocks, axes):
    return lax.all_to_all(blocks, axes, split_axis=0, concat_axis=0, tiled=True)


def after(value, *earlier, mib=8):
    return pl.pallas_call(
        lambda *refs: None,
        out_shape=jax.ShapeDtypeStruct(value.shape, value.dtype),
        in_specs=[pl.BlockSpec(memory_space=pltpu.HBM)] * (1 + len(earlier)),
        out_specs=pl.BlockSpec(memory_space=pltpu.HBM),
        input_output_aliases={0: 0},
        compiler_params=params(mib),
        name="after",
    )(value, *earlier)


def pair_kernel(mine_ref, got_ref, out_ref):
    out_ref[...] = (mine_ref[...].astype(F32) + got_ref[...].astype(F32)).astype(BF16)


def pair_sum(mine, got):
    return pl.pallas_call(
        pair_kernel,
        out_shape=jax.ShapeDtypeStruct(mine.shape, BF16),
        in_specs=[vspec(), vspec()],
        out_specs=vspec(),
        compiler_params=params(16),
        name="pair_sum",
    )(mine, got)


CHIPS = ("dp", "chip")
ALL = ("dp", "chip", "core")


def layer(place, weights, segment_ids, tokens, cotangent, ffn_weights, send_core, send_ffn):
    table = jnp.asarray(encode_table())
    qk, x, qk_t, x_t, back, marks = place_tokens(segment_ids, tokens, cotangent, table)
    query_t, value, key_t, out_t, inverse, mixed, mixed_t, exps, weight, proj, vector = attend_forward(
        marks, place, x, qk, x_t, qk_t, *weights(marks)
    )
    ffn_mine, ffn_other = ffn_weights(marks, vector)
    block_out, resid, grad_t, ffn_mine, ffn_other, proj_g, vector_g = feed_forward(
        marks, place, x, back, mixed, mixed_t, proj, ffn_mine, ffn_other, vector
    )
    ffn_got, grad_t = send_ffn(ffn_mine, ffn_other, grad_t)
    input_grad, grads_own, grads_other, sums = attend_back(
        marks, place, grad_t, query_t, value, key_t, out_t, inverse, exps, qk_t, x_t, weight, proj_g, resid
    )
    attn_got = send_core(grads_other)
    return block_out, input_grad, grads_own, grads_other, attn_got, sums, vector_g, ffn_got


def body(
    tokens,
    cotangent,
    segment_ids,
    attn_weight,
    ffn_in,
    ffn_out,
    vectors,
    attn_rows,
    attn_cols,
    in_rows,
    in_cols,
    out_rows,
    out_cols,
    vector_moment,
):
    place = jnp.stack([lax.axis_index("dp"), lax.axis_index("chip"), lax.axis_index("core")])
    place = place.astype(jnp.int32)
    pieces = VDP * VCHIP
    tall, wide = attn_weight.shape
    rows_v, cols_v = vectors.shape
    split = lambda array: array.reshape((VDP, VCHIP) + array.shape[1:])
    attn_sent, ffn_low = pack_attn(place, attn_weight, ffn_in, ffn_out, vectors)
    attn_mine = exchange(attn_sent, CHIPS)

    parts = [
        lax.ppermute(ffn_low, "dp", [(i, i ^ step) for i in range(VDP)]) for step in range(1, VDP)
    ]
    ffn_sent = pack_ffn(place, ffn_low, parts)

    def attn_weights(marks):
        mine = split(after(attn_mine, marks, ffn_sent))
        return mine, core_swap(mine)

    def ffn_weights(marks, vector):
        got = exchange(after(ffn_sent, marks), "chip")
        ffn_mine = after(got, vector)
        return ffn_mine, core_swap(ffn_mine)

    def send_ffn(mine, other, grad_t):
        both = pair_sum(mine, core_swap(other))
        got = exchange(both.reshape((pieces,) + mine.shape[2:]), CHIPS)
        return got, after(grad_t, both, mib=56)

    (
        block_out,
        input_grad,
        grads_own,
        grads_other,
        attn_got,
        sums,
        vector_g,
        ffn_got,
    ) = layer(place, attn_weights, segment_ids, tokens, cotangent, ffn_weights, core_swap, send_ffn)
    lay = lambda stat: stat.reshape(1, -1)
    rows_old = (lay(attn_rows), lay(in_rows), lay(out_rows))
    cols_old = (lay(attn_cols), lay(in_cols), lay(out_cols))
    weights_old = (attn_weight, ffn_in, ffn_out)
    in_grad, out_grad, ffn_grad, stat = whole_call(
        tail_ffn_kernel,
        "tail_ffn",
        place,
        [(ffn_in.shape, F32), (ffn_out.shape, F32), ((2,) + ffn_in.shape, F32), ((8, LANES), F32)],
        ffn_got,
        *rows_old[1:],
        sums,
    )
    (sent,) = whole_call(
        tail_send_kernel,
        "tail_send",
        place,
        [((pieces, tall + VROWS, LANES), BF16)],
        grads_own,
        attn_got,
        vector_g,
        sums,
        stat,
        core_swap(stat),
    )
    got = exchange(sent, CHIPS)
    attn_grad, update_1, update_2, rows_new_1, rows_new_2, cols_new_1, cols_new_2, sent = whole_call(
        tail_reduce_kernel,
        "tail_reduce",
        place,
        [
            (attn_weight.shape, F32),
            (ffn_in.shape, F32),
            (ffn_out.shape, F32),
            (rows_old[1].shape, F32),
            (rows_old[2].shape, F32),
            (cols_old[1].shape, F32),
            (cols_old[2].shape, F32),
            ((pieces, tall + VROWS, LANES), BF16),
        ],
        got,
        ffn_grad,
        *weights_old,
        *rows_old,
        *cols_old,
        vectors,
        vector_moment,
    )
    mine = exchange(sent, CHIPS)
    attn_new, in_new, out_new, rows_new_0, cols_new_0, vector_grad, moment_new, vectors_new = whole_call(
        tail_apply_kernel,
        "tail_apply",
        place,
        [
            (attn_weight.shape, F32),
            (ffn_in.shape, F32),
            (ffn_out.shape, F32),
            (rows_old[0].shape, F32),
            (cols_old[0].shape, F32),
            (vectors.shape, F32),
            (vectors.shape, F32),
            (vectors.shape, F32),
        ],
        mine,
        core_swap(mine),
        attn_grad,
        update_1,
        update_2,
        *weights_old,
        rows_old[0],
        cols_old[0],
        vectors,
        vector_moment,
        scratch=[
            pltpu.VMEM((2 * VDP + pieces, tall, LANES), F32),
            pltpu.VMEM((LANES, tall), F32),
        ],
    )
    return (
        block_out,
        input_grad,
        attn_grad,
        in_grad,
        out_grad,
        vector_grad,
        rows_new_0.reshape(-1),
        cols_new_0.reshape(-1),
        rows_new_1.reshape(-1),
        cols_new_1.reshape(-1),
        rows_new_2.reshape(-1),
        cols_new_2.reshape(-1),
        moment_new,
        attn_new,
        in_new,
        out_new,
        vectors_new,
    )


def gather_all(block):
    shape = (lax.axis_size("dp"), lax.axis_size("chip") * 2)
    count = shape[0] * shape[1]
    got = exchange(jnp.broadcast_to(block[None], (count,) + block.shape), ALL)
    return got.reshape(shape + block.shape)


def unblock(parts):
    dp_count, fsdp_count, rows, cols = parts.shape
    return parts.transpose(0, 2, 1, 3).reshape(dp_count * rows, fsdp_count * cols)


def scatter_sum(full):
    dp_count = lax.axis_size("dp")
    fsdp_count = lax.axis_size("chip") * 2
    rows, cols = full.shape
    by_col = full.astype(BF16).reshape(rows, fsdp_count, cols // fsdp_count).transpose(1, 0, 2)
    got = exchange(by_col, ("chip", "core"))
    part = jnp.sum(got.astype(F32), axis=0).astype(BF16)
    by_row = part.reshape(dp_count, rows // dp_count, cols // fsdp_count)
    return jnp.sum(exchange(by_row, "dp").astype(F32), axis=0)


def body_any(
    tokens,
    cotangent,
    segment_ids,
    attn_weight,
    ffn_in,
    ffn_out,
    vectors,
    attn_rows,
    attn_cols,
    in_rows,
    in_cols,
    out_rows,
    out_cols,
    vector_moment,
):
    dp_count = lax.axis_size("dp")
    fsdp_count = lax.axis_size("chip") * 2
    dp_place = lax.axis_index("dp")
    fsdp_place = lax.axis_index("chip") * 2 + lax.axis_index("core")
    rows_w = attn_weight.shape[0]
    rows_v = vectors.shape[0]
    place = jnp.zeros((3,), jnp.int32)
    full_attn = unblock(gather_all(attn_weight.astype(BF16)))
    full_vector = unblock(gather_all(vectors.astype(BF16)))
    full_ffn = jnp.stack(
        [unblock(gather_all(ffn_in.astype(BF16))), unblock(gather_all(ffn_out.astype(BF16)))]
    )
    tall = D // VDP
    cut = full_attn.reshape(VDP, tall, VCHIP, 2, LANES).transpose(3, 0, 2, 1, 4)
    lines = full_vector.reshape(VDP, VEC // VDP, 2, LANES).transpose(0, 2, 1, 3)
    lines = lines.reshape(VDP, 1, 2 * VEC // VDP, LANES)
    lines = jnp.pad(lines, ((0, 0), (0, VCHIP - 1), (0, VROWS - 2 * VEC // VDP), (0, 0)))
    weights = (
        jnp.concatenate([cut[0], lines], axis=2),
        jnp.concatenate([cut[1], jnp.zeros_like(lines)], axis=2),
    )
    ffn_cut = full_ffn.reshape(2, VDP, tall, VCHIP, 2, FF // (2 * VCHIP))
    ffn_cut = ffn_cut.transpose(4, 3, 1, 0, 2, 5)
    (
        block_out,
        input_grad,
        grads_own,
        grads_other,
        _,
        sums,
        vector_g,
        ffn_got,
    ) = layer(
        place,
        lambda marks: weights,
        segment_ids,
        tokens,
        cotangent,
        lambda marks, vector: (ffn_cut[0], ffn_cut[1]),
        lambda block: block,
        lambda mine, other, grad_t: (jnp.stack([mine, other]), grad_t),
    )
    attn_full = jnp.stack([grads_own, grads_other]).transpose(1, 3, 2, 0, 4).reshape(D, 4 * D)
    ffn_full = ffn_got.transpose(3, 1, 4, 2, 0, 5).reshape(2, D, FF)
    sums = jnp.concatenate([sums[0, :2], sums[1, :2]], axis=1)
    vector_full = jnp.concatenate([vector_g[:8], sums, vector_g[10:]], axis=0)
    attn_grad = scatter_sum(attn_full)
    in_grad = scatter_sum(ffn_full[0])
    out_grad = scatter_sum(ffn_full[1])
    vector_grad = scatter_sum(vector_full)

    decay = 1.0 - STEP ** (-0.8)
    gradients = (attn_grad, in_grad, out_grad)
    weights_old = (attn_weight, ffn_in, ffn_out)
    rows_old = (attn_rows, in_rows, out_rows)
    cols_old = (attn_cols, in_cols, out_cols)
    moment_new = decay * vector_moment + (1.0 - decay) * (vector_grad * vector_grad + EPS_ONE)
    vector_step = vector_grad * lax.rsqrt(moment_new)
    squares = [gradient * gradient + EPS_ONE for gradient in gradients]
    pieces = []
    for square in squares:
        pieces.append(jnp.sum(square, axis=1))
    for square in squares:
        pieces.append(jnp.sum(square, axis=0))
    pieces.append(jnp.sum(vector_step * vector_step, axis=1))
    pieces.append(jnp.sum(vectors * vectors, axis=1))
    pieces.append(jnp.stack([jnp.sum(weight * weight) for weight in weights_old]))
    pieces.append(jnp.stack([jnp.sum(old) for old in rows_old]))
    sizes = [piece.shape[0] for piece in pieces]
    flat = jnp.concatenate(pieces)
    flat = jnp.pad(flat, (0, -flat.shape[0] % 1024)).reshape(-1, LANES)
    got = gather_all(flat).reshape(dp_count, fsdp_count, -1)
    offsets = [0]
    for length in sizes:
        offsets.append(offsets[-1] + length)
    take = lambda i: got[:, :, offsets[i] : offsets[i + 1]]
    rows_new, cols_new, row_means, entries = [], [], [], []
    for i in range(3):
        count_rows = rows_w * dp_count
        count_cols = weights_old[i].shape[1] * fsdp_count
        entries.append(float(count_rows * count_cols))
        row_all = jnp.sum(take(i), axis=1)
        mine = lax.dynamic_index_in_dim(row_all, dp_place, 0, keepdims=False)
        rows_new.append(decay * rows_old[i] + (1.0 - decay) * mine / count_cols)
        col_all = jnp.sum(take(3 + i), axis=0)
        mine = lax.dynamic_index_in_dim(col_all, fsdp_place, 0, keepdims=False)
        cols_new.append(decay * cols_old[i] + (1.0 - decay) * mine / count_rows)
        old_total = jnp.sum(take(9)[:, 0, i])
        row_means.append(
            (decay * old_total + (1.0 - decay) * jnp.sum(row_all) / count_cols) / count_rows
        )
    step_rows = jnp.sum(take(6), axis=1).reshape(-1)
    weight_rows = jnp.sum(take(7), axis=1).reshape(-1)
    weight_totals = jnp.sum(take(8), axis=(0, 1))
    updates = []
    for i in range(3):
        second = rows_new[i][:, None] * cols_new[i][None, :] / row_means[i]
        updates.append(gradients[i] * lax.rsqrt(second))
    flat = jnp.stack([jnp.sum(update * update) for update in updates])
    flat = jnp.broadcast_to(jnp.pad(flat, (0, 5))[:, None], (8, LANES))
    totals = jnp.sum(gather_all(flat)[:, :, :, 0], axis=(0, 1))
    new_weights = []
    for i in range(3):
        clip_factor = jnp.maximum(1.0, jnp.sqrt(totals[i] / entries[i]) / CLIP_LIMIT)
        step_size = STEP_RATE * jnp.maximum(EPS_TWO, jnp.sqrt(weight_totals[i] / entries[i]))
        new_weights.append(weights_old[i] - step_size / clip_factor * updates[i])
    bias_rows = FF // D
    row_places = jnp.arange(VEC)
    counts = jnp.where(row_places < bias_rows, float(FF), float(D))
    grouped_updates = jnp.where(row_places < bias_rows, jnp.sum(step_rows[:bias_rows]), step_rows)
    grouped_weights = jnp.where(row_places < bias_rows, jnp.sum(weight_rows[:bias_rows]), weight_rows)
    clip_rows = jnp.maximum(1.0, jnp.sqrt(grouped_updates / counts) / CLIP_LIMIT)
    step_sizes = STEP_RATE * jnp.maximum(EPS_TWO, jnp.sqrt(grouped_weights / counts))
    factor_rows = lax.dynamic_slice_in_dim(step_sizes / clip_rows, dp_place * rows_v, rows_v)
    vectors_new = vectors - factor_rows[:, None] * vector_step
    return (
        block_out,
        input_grad,
        attn_grad,
        in_grad,
        out_grad,
        vector_grad,
        rows_new[0],
        cols_new[0],
        rows_new[1],
        cols_new[1],
        rows_new[2],
        cols_new[2],
        moment_new,
        new_weights[0],
        new_weights[1],
        new_weights[2],
        vectors_new,
    )


def solution(mesh):
    dp_count, fsdp_count = mesh.shape["dp"], mesh.shape["fsdp"]
    inner = jax.sharding.Mesh(mesh.devices.reshape(dp_count, fsdp_count // 2, 2), ALL)
    fsdp = ("chip", "core")
    split = P(ALL, None)
    block = P("dp", fsdp)
    stats = (P("dp"), P(fsdp)) * 3
    plain = dp_count == VDP and fsdp_count == 2 * VCHIP
    return jax.shard_map(
        body if plain else body_any,
        mesh=inner,
        in_specs=(split,) * 3 + (block,) * 4 + stats + (block,),
        out_specs=(split,) * 2 + (block,) * 4 + stats + (block,) * 5,
        check_vma=False,
    )
```

```python
import functools
import math

import jax
import jax.numpy as jnp
import numpy as np
from jax import lax
from jax.experimental import pallas as pl
from jax.experimental.pallas import tpu as pltpu
from jax.sharding import PartitionSpec as P

D = 256
FF = 2048
HEADS = 8
HEAD_DIM = 32
SEQ = 1024
HALF = 512
GROUP = 4
LANES = 128
QBLOCK = 512
WGRID = 32
STEP = 10
VEC = 16
TILE = 1024
CHUNK = 256
SUB = 512
LEAD = 5
STRIP = 64
VDP = 4
VCHIP = 4
VROWS = 16

EPS_NORM = 1e-05
EPS_ONE = 1e-30
EPS_TWO = 0.001
CLIP_LIMIT = 1.0
STEP_RATE = 0.3
FAR = 1e30
TAME = 40.0
LOG2_E = math.log2(math.e)
SCALE = HEAD_DIM ** (-0.5)
GELU_A = math.sqrt(2.0 / math.pi)
GELU_B = 0.044715
F32 = jnp.float32
BF16 = jnp.bfloat16
MIB = 1024 * 1024


def dot(left, right):
    return jnp.dot(left, right, preferred_element_type=F32)


def dot_nt(left, right):
    return lax.dot_general(left, right, (((1,), (1,)), ((), ())), preferred_element_type=F32)


def encode_table():
    half = D // 2
    feature = np.arange(half)
    freq = np.exp(
        (2 * (feature // 2)).astype(np.float32) * np.float32(-math.log(10000.0) / half)
    ).astype(np.float32)
    angles = np.arange(1, WGRID + 1, dtype=np.float32)[:, None] * freq[None, :]
    table = np.where(feature % 2 == 0, np.sin(angles), np.cos(angles)).astype(np.float32)
    low = jnp.bfloat16
    one = table.astype(low)
    rest = table - one.astype(np.float32)
    two = rest.astype(low)
    three = (rest - two.astype(np.float32)).astype(low)
    blank = np.zeros((LANES - 3 * WGRID, half), low)
    return np.concatenate([one, two, three, blank], axis=0)


def iota(shape, dim):
    return lax.broadcasted_iota(jnp.int32, shape, dim)


def norm_forward(rows):
    centered = rows - jnp.mean(rows, axis=-1, keepdims=True)
    inverse = lax.rsqrt(jnp.mean(centered * centered, axis=-1, keepdims=True) + EPS_NORM)
    return centered * inverse, inverse


def norm_backward(upstream, normed, inverse):
    return inverse * (
        upstream
        - jnp.mean(upstream, axis=-1, keepdims=True)
        - normed * jnp.mean(upstream * normed, axis=-1, keepdims=True)
    )

def vspec():
    return pl.BlockSpec(memory_space=pltpu.VMEM)


def params(mib=56, **more):
    return pltpu.CompilerParams(vmem_limit_bytes=mib * MIB, **more)


def pack_kernel(place, attn_ref, first_ref, second_ref, vector_ref, out_ref, ffn_ref):
    owner = place[1] * 2 + place[2]
    vector = vector_ref[...]
    rows = vector.shape[0]
    wide = jnp.concatenate([vector] * (LANES // vector.shape[1]), axis=1)
    slot = iota((rows, LANES), 1) // vector.shape[1]
    per = LANES // vector.shape[1]
    parts = [attn_ref[...]]
    for half in range(2):
        parts.append(jnp.where(slot + half * per == owner, wide, 0.0))
    parts.append(jnp.zeros((VROWS - 2 * rows, LANES), F32))
    piece = jnp.concatenate(parts, axis=0).astype(BF16)
    for at in range(VDP * VCHIP):
        out_ref[at] = piece
    ffn_ref[0] = first_ref[...].astype(BF16)
    ffn_ref[1] = second_ref[...].astype(BF16)


def pack_attn(place, attn_weight, ffn_in, ffn_out, vectors):
    return pl.pallas_call(
        pack_kernel,
        out_shape=(
            jax.ShapeDtypeStruct((VDP * VCHIP, attn_weight.shape[0] + VROWS, LANES), BF16),
            jax.ShapeDtypeStruct((2,) + ffn_in.shape, BF16),
        ),
        in_specs=[pl.BlockSpec(memory_space=pltpu.SMEM)] + [vspec()] * 4,
        out_specs=(vspec(), vspec()),
        compiler_params=params(),
        name="pack_attn",
    )(place, attn_weight, ffn_in, ffn_out, vectors)


def pack_ffn_kernel(place, own_ref, *refs):
    out_ref = refs[-1]
    for at in range(VCHIP):
        out_ref[at, pl.ds(place[0], 1)] = own_ref[...][None]
        for step in range(1, VDP):
            out_ref[at, pl.ds(place[0] ^ step, 1)] = refs[step - 1][...][None]


def pack_ffn(place, own, parts):
    return pl.pallas_call(
        pack_ffn_kernel,
        out_shape=jax.ShapeDtypeStruct((VCHIP, VDP) + own.shape, BF16),
        in_specs=[pl.BlockSpec(memory_space=pltpu.SMEM)] + [vspec()] * (1 + len(parts)),
        out_specs=vspec(),
        compiler_params=params(16),
        name="pack_ffn",
    )(place, own, *parts)


def place_kernel(
    segment_ref, tokens_ref, table_ref, qk_ref, x_ref, qk_t_ref, x_t_ref, marks_ref
):
    row = pl.program_id(0)
    starts = []
    for number in range(1, 4):
        at = jnp.int32(0)
        for step in (512, 256, 128, 64, 32, 16, 8, 4, 2, 1, 1):
            probe = jnp.minimum(at + (step - 1), SEQ - 1)
            at = jnp.where(segment_ref[row, probe] < number, at + step, at)
        starts.append(at)
    edges = [jnp.int32(0)] + starts + [jnp.int32(SEQ)]
    begin = jnp.int32(0)
    for number in range(3, -1, -1):
        begin = jnp.where(edges[number + 1] - edges[number] == HALF, edges[number], begin)
    for number in range(3):
        marks_ref[row, number] = starts[number]
    marks_ref[row, 3] = begin
    one, two, three = starts
    x = pltpu.roll(tokens_ref[...].astype(F32), (SEQ - begin) & (SEQ - 1), 0)
    x_ref[...] = x.astype(BF16)
    x_t_ref[...] = x.T.astype(BF16)
    at = (iota((SEQ, LANES), 0) + begin) & (SEQ - 1)
    lane = iota((SEQ, LANES), 1)
    start = jnp.where(at >= three, three, jnp.where(at >= two, two, jnp.where(at >= one, one, 0)))
    local = at - start
    kept = lane < 3 * WGRID
    slot = lane & (WGRID - 1)
    hot_r = jnp.where(((local >> 5) == slot) & kept, 1.0, 0.0).astype(BF16)
    hot_c = jnp.where(((local & (WGRID - 1)) == slot) & kept, 1.0, 0.0).astype(BF16)
    table = table_ref[...]
    places = jnp.concatenate([dot(hot_r, table), dot(hot_c, table)], axis=1)
    qk = x + places
    qk_ref[...] = qk.astype(BF16)
    qk_t_ref[...] = qk.T.astype(BF16)


def place_tokens(segment_ids, tokens, table):
    rows = segment_ids.shape[0]
    by_row = lambda r: (r, 0)
    return pl.pallas_call(
        place_kernel,
        out_shape=(
            jax.ShapeDtypeStruct(tokens.shape, BF16),
            jax.ShapeDtypeStruct(tokens.shape, BF16),
            jax.ShapeDtypeStruct((D, tokens.shape[0]), BF16),
            jax.ShapeDtypeStruct((D, tokens.shape[0]), BF16),
            jax.ShapeDtypeStruct((rows, 4), jnp.int32),
        ),
        grid=(rows,),
        in_specs=[
            pl.BlockSpec(memory_space=pltpu.SMEM),
            pl.BlockSpec((SEQ, D), by_row),
            pl.BlockSpec((LANES, LANES), lambda r: (0, 0)),
        ],
        out_specs=(
            pl.BlockSpec((SEQ, D), by_row),
            pl.BlockSpec((SEQ, D), by_row),
            pl.BlockSpec((D, SEQ), lambda r: (0, r)),
            pl.BlockSpec((D, SEQ), lambda r: (0, r)),
            pl.BlockSpec(memory_space=pltpu.SMEM),
        ),
        compiler_params=params(dimension_semantics=("arbitrary",)),
        cost_estimate=pl.CostEstimate(flops=600_000_000, bytes_accessed=4_000_000, transcendentals=0),
        name="place_tokens",
    )(segment_ids, tokens, table)


def attend_kernel(
    marks,
    place,
    x_ref,
    qk_ref,
    x_t_ref,
    qk_t_ref,
    mine_ref,
    other_ref,
    query_t_ref,
    value_ref,
    key_t_ref,
    out_t_ref,
    inverse_ref,
    mixed_ref,
    mixed_t_ref,
    exps_ref,
    weight_ref,
    proj_ref,
    vector_ref,
    key_s,
    value_s,
    mark_k,
    mark_q,
    first_s,
    second_s,
    weight_t_s,
    bias_s,
    tame_s,
    exps_s,
    exps_sem,
):
    row = pl.program_id(0)
    begin = marks[row, 3]
    core = place[2]

    def copy_of(group, half):
        return pltpu.make_async_copy(
            exps_s.at[group, half], exps_ref.at[row, group, half], exps_sem.at[group * 2 + half]
        )

    @pl.when(row == 0)
    def _():
        tall = D // VDP
        for d in range(VDP):
            rows = slice(d * tall, (d + 1) * tall)
            total = jnp.zeros((8, LANES), F32)
            for c in range(VCHIP):
                for ref, half in ((mine_ref, core), (other_ref, 1 - core)):
                    if c < 3:
                        to = pl.ds(pl.multiple_of(c * D + half * LANES, LANES), LANES)
                        weight_ref[rows, to] = ref[d, c, :tall, :]
                    else:
                        to = pl.ds(pl.multiple_of(half * LANES, LANES), LANES)
                        proj_ref[rows, to] = ref[d, c, :tall, :]
                    total += ref[d, c, tall:, :].astype(F32)[:8]
            vector_ref[d * 4 : (d + 1) * 4, :LANES] = total[:4]
            vector_ref[d * 4 : (d + 1) * 4, LANES:] = total[4:]
        weight_t_s[...] = weight_ref[...].astype(F32).T.astype(BF16)
        bias_s[...] = vector_ref[8:16, :].T

    qk_t = qk_t_ref[...]
    query_t = (dot(weight_t_s[:D, :], qk_t) + bias_s[:, 0:1]) * SCALE
    query_t = query_t.astype(BF16)
    query_t_ref[...] = query_t
    key_t = dot(weight_t_s[D : 2 * D, :], qk_t).astype(BF16)
    key_t_ref[...] = key_t

    def largest_norms(rows):
        rows = rows.astype(F32)
        rows = rows * rows
        sums = [
            jnp.sum(rows[head * HEAD_DIM : (head + 1) * HEAD_DIM], axis=0, keepdims=True)
            for head in range(HEADS)
        ]
        return jnp.max(jnp.concatenate(sums, axis=0), axis=1, keepdims=True)

    bound = jnp.max(largest_norms(query_t) * largest_norms(key_t))
    tame_s[0] = jnp.where(bound <= TAME * TAME, 1, 0)
    key_s[...] = dot(qk_ref[...], weight_ref[:, D : 2 * D]).astype(BF16)
    value = dot(x_ref[...], weight_ref[:, 2 * D : 3 * D]) + vector_ref[9:10, :]
    value_ref[...] = value.astype(BF16)
    value_t = dot(weight_t_s[2 * D :, :], x_t_ref[...]) + bias_s[:, 1:2]
    value_t = value_t.astype(BF16)
    for head in range(HEADS):
        value_s[head, :HEAD_DIM, :] = value_t[head * HEAD_DIM : (head + 1) * HEAD_DIM, :]
        value_s[head, HEAD_DIM:, :] = jnp.ones((16, SEQ), BF16)
    one, two, three = marks[row, 0], marks[row, 1], marks[row, 2]

    def number_of(shape, dim):
        here = (iota(shape, dim) + (HALF + begin)) & (SEQ - 1)
        return (
            jnp.where(here >= one, 1, 0)
            + jnp.where(here >= two, 1, 0)
            + jnp.where(here >= three, 1, 0)
        )

    lane = iota((HALF, LANES), 1)
    number = number_of((HALF, LANES), 0)
    mark_k[...] = jnp.where((number != lane) & (lane < 4), -FAR, 0.0).astype(BF16)
    number = number_of((LANES, HALF), 1)
    mark_q[...] = jnp.where(number == iota((LANES, HALF), 0), 1.0, 0.0).astype(BF16)

    head_of = iota((1, LANES), 1) // HEAD_DIM
    for group in range(2):
        keys_here = key_s[:, group * LANES : (group + 1) * LANES]
        for at_head in range(GROUP):
            mask = jnp.where(head_of == at_head, 1.0, 0.0).astype(BF16)
            rows = slice(at_head * HALF, (at_head + 1) * HALF)
            first_s[group, rows, :] = keys_here[:HALF] * mask
            second_s[group, rows, :LANES] = keys_here[HALF:] * mask
            second_s[group, rows, LANES:] = mark_k[...]

    @pl.when(row > 0)
    def _():
        for group in range(2):
            for half in range(2):
                copy_of(group, half).wait()

    def scores_of(group, half, rows):
        query = query_t_ref[group * LANES : (group + 1) * LANES, half * HALF : (half + 1) * HALF]
        if half == 0:
            return dot(first_s[group, rows, :], query)
        return dot(second_s[group, rows, :], jnp.concatenate([query, mark_q[...]], axis=0))

    def place_of(at_head):
        return slice(at_head * HALF, (at_head + 1) * HALF)

    def exps_plain(group, half):
        scores = scores_of(group, half, slice(0, GROUP * HALF))
        for at_head in range(GROUP):
            exps = jnp.exp2(scores[place_of(at_head), :] * LOG2_E)
            exps_s[group, half, :, place_of(at_head)] = exps.astype(BF16)

    def exps_shifted(group, half):
        for at_head in range(GROUP):
            rows = place_of(at_head)
            largest = jnp.max(scores_of(group, half, rows), axis=0, keepdims=True)
            exps = jnp.exp2((scores_of(group, half, rows) - largest) * LOG2_E)
            exps_s[group, half, :, rows] = exps.astype(BF16)

    def finish(group, half):
        rows = slice(half * HALF, (half + 1) * HALF)
        for at_head in range(GROUP):
            head = group * GROUP + at_head
            out = dot(value_s[head, :, rows], exps_s[group, half, :, place_of(at_head)])
            inverse = 1.0 / out[HEAD_DIM : HEAD_DIM + 1, :]
            inverse_ref[group, at_head : at_head + 1, rows] = inverse
            out_t_ref[head * HEAD_DIM : (head + 1) * HEAD_DIM, rows] = out[:HEAD_DIM, :] * inverse

    def run(exps_of):
        items = [(group, half) for group in range(2) for half in range(2)]
        for i in range(len(items) + 1):
            if i < len(items):
                exps_of(*items[i])
                copy_of(*items[i]).start()
            if i >= 1:
                finish(*items[i - 1])

    @pl.when(tame_s[0] == 1)
    def _():
        run(exps_plain)

    @pl.when(tame_s[0] == 0)
    def _():
        run(exps_shifted)

    out_t = out_t_ref[...]
    mixed_t_ref[...] = out_t.astype(BF16)
    mixed_ref[...] = out_t.T.astype(BF16)

    @pl.when(row == pl.num_programs(0) - 1)
    def _():
        for group in range(2):
            for half in range(2):
                copy_of(group, half).wait()


def attend_forward(marks, place, x, qk, x_t, qk_t, mine, other):
    total = x.shape[0]
    rows = total // SEQ
    by_row = lambda r, m, p: (r, 0)
    by_col = lambda r, m, p: (0, r)
    whole = lambda r, m, p: (0, 0)
    return pl.pallas_call(
        attend_kernel,
        out_shape=(
            jax.ShapeDtypeStruct((D, total), BF16),
            jax.ShapeDtypeStruct((total, D), BF16),
            jax.ShapeDtypeStruct((D, total), BF16),
            jax.ShapeDtypeStruct((D, total), F32),
            jax.ShapeDtypeStruct((2, 8, total), F32),
            jax.ShapeDtypeStruct((total, D), BF16),
            jax.ShapeDtypeStruct((D, total), BF16),
            jax.ShapeDtypeStruct((rows, 2, 2, HALF, GROUP * HALF), BF16),
            jax.ShapeDtypeStruct((D, 3 * D), BF16),
            jax.ShapeDtypeStruct((D, D), BF16),
            jax.ShapeDtypeStruct((VEC, D), F32),
        ),
        grid_spec=pltpu.PrefetchScalarGridSpec(
            num_scalar_prefetch=2,
            grid=(rows,),
            in_specs=[
                pl.BlockSpec((SEQ, D), by_row),
                pl.BlockSpec((SEQ, D), by_row),
                pl.BlockSpec((D, SEQ), by_col),
                pl.BlockSpec((D, SEQ), by_col),
                vspec(),
                vspec(),
            ],
            out_specs=[
                pl.BlockSpec((D, SEQ), by_col),
                pl.BlockSpec((SEQ, D), by_row),
                pl.BlockSpec((D, SEQ), by_col),
                pl.BlockSpec((D, SEQ), by_col),
                pl.BlockSpec((2, 8, SEQ), lambda r, m, p: (0, 0, r)),
                pl.BlockSpec((SEQ, D), by_row),
                pl.BlockSpec((D, SEQ), by_col),
                pl.BlockSpec(memory_space=pl.ANY),
                pl.BlockSpec((D, 3 * D), whole),
                pl.BlockSpec((D, D), whole),
                pl.BlockSpec((VEC, D), whole),
            ],
            scratch_shapes=[
                pltpu.VMEM((SEQ, D), BF16),
                pltpu.VMEM((HEADS, HEAD_DIM + 16, SEQ), BF16),
                pltpu.VMEM((HALF, LANES), BF16),
                pltpu.VMEM((LANES, HALF), BF16),
                pltpu.VMEM((2, GROUP * HALF, LANES), BF16),
                pltpu.VMEM((2, GROUP * HALF, 2 * LANES), BF16),
                pltpu.VMEM((3 * D, D), BF16),
                pltpu.VMEM((D, 8), F32),
                pltpu.SMEM((1,), jnp.int32),
                pltpu.VMEM((2, 2, HALF, GROUP * HALF), BF16),
                pltpu.SemaphoreType.DMA((4,)),
            ],
        ),
        compiler_params=params(dimension_semantics=("arbitrary",)),
        cost_estimate=pl.CostEstimate(
            flops=20_000_000_000, bytes_accessed=30_000_000, transcendentals=8_400_000
        ),
        name="attend_forward",
    )(marks, place, x, qk, x_t, qk_t, mine, other)


def feed_kernel(
    marks,
    place,
    x_ref,
    back_ref,
    mixed_ref,
    mixed_t_ref,
    proj_ref,
    mine_ref,
    other_ref,
    vector_ref,
    block_ref,
    resid_ref,
    mixed_grad_ref,
    mine_out,
    other_out,
    proj_out,
    vector_out,
    first_w,
    second_w,
    first_acc,
    second_acc,
    proj_acc,
    vector_acc,
    hidden_s,
    slope_s,
    pre_s,
    first_low_s,
    branch_low_s,
    attended_s,
    back_s,
    eye_s,
):
    step = pl.program_id(0)
    core = place[2]
    tall = D // VDP
    wide = FF // (2 * VCHIP)

    @pl.when(step == 0)
    def _():
        first_acc[...] = jnp.zeros_like(first_acc)
        second_acc[...] = jnp.zeros_like(second_acc)
        proj_acc[...] = jnp.zeros_like(proj_acc)
        vector_acc[...] = jnp.zeros_like(vector_acc)
        eye_s[...] = jnp.where(iota((D, D), 0) == iota((D, D), 1), 1.0, 0.0).astype(BF16)
        for d in range(VDP):
            rows = slice(d * tall, (d + 1) * tall)
            for c in range(VCHIP):
                for ref, half in ((mine_ref, core), (other_ref, 1 - core)):
                    to = pl.ds(pl.multiple_of((2 * c + half) * wide, wide), wide)
                    first_w[rows, to] = ref[c, d, 0]
                    second_w[rows, to] = ref[c, d, 1]

    bias_o, bias_2 = vector_ref[10:11, :], vector_ref[11:12, :]
    gain_1, shift_1 = vector_ref[12:13, :], vector_ref[13:14, :]
    gain_2, shift_2 = vector_ref[14:15, :], vector_ref[15:16, :]
    turn = (SEQ - marks[step, 3]) & (SEQ - 1)
    back_s[...] = pltpu.roll(back_ref[...].astype(F32), turn, 0)
    chunks = FF // CHUNK
    pair = 2

    def columns(at, count=1):
        return slice(at * CHUNK, (at + count) * CHUNK)

    def hidden_of(rows, at, pre):
        per = CHUNK // D
        bias = [vector_ref[at * per + i : at * per + i + 1, :] for i in range(per)]
        pre = (pre + jnp.concatenate(bias, axis=1)).astype(BF16)
        cube = BF16(GELU_A * GELU_B) * (pre * pre)
        gate = BF16(0.5) + BF16(0.5) * jnp.tanh(pre * (cube + BF16(GELU_A)))
        hidden_s[rows, columns(at)] = pre * gate
        slope_s[rows, columns(at)] = gate + (gate - gate * gate) * (
            pre * (BF16(6.0) * cube + BF16(2.0 * GELU_A))
        )

    def stages(sub):
        rows_at = sub * SUB
        rows = slice(rows_at, rows_at + SUB)
        attended = dot(mixed_ref[rows, :], proj_ref[...]) + bias_o
        norm_1, inverse_1 = norm_forward(x_ref[rows, :].astype(F32) + attended)
        first = norm_1 * gain_1 + shift_1
        first_low = first.astype(BF16)
        first_low_s[rows, :] = first_low
        yield
        branch = jnp.zeros((SUB, D), F32)
        for i in range(chunks + 1):
            if i < chunks:
                hidden_of(rows, i, dot(first_low, first_w[:, columns(i)]))
            if i >= pair and i % pair == 0:
                cols = columns(i - pair, pair)
                branch += dot_nt(hidden_s[rows, cols], second_w[:, cols])
            yield
        norm_2, inverse_2 = norm_forward(first + (branch + bias_2))
        block_ref[rows, :] = norm_2 * gain_2 + shift_2
        back = back_s[rows, :]
        vector_acc[14:15, :] += jnp.sum(back * norm_2, axis=0, keepdims=True)
        vector_acc[15:16, :] += jnp.sum(back, axis=0, keepdims=True)
        resid_2 = norm_backward(back * gain_2, norm_2, inverse_2)
        branch_low = resid_2.astype(BF16)
        branch_low_s[rows, :] = branch_low
        vector_acc[11:12, :] += jnp.sum(branch_low.astype(F32), axis=0, keepdims=True)
        yield
        first_back = resid_2
        if sub == 1:
            branch_t = dot_nt(eye_s[...], branch_low_s[...]).astype(BF16)
            first_t = dot_nt(eye_s[...], first_low_s[...]).astype(BF16)
            first_t = jnp.concatenate([first_t, jnp.ones((16, TILE), BF16)], axis=0)
        for i in range(chunks + 1):
            if i < chunks:
                pull = dot(branch_low, second_w[:, columns(i)]).astype(BF16)
                pre_s[rows, columns(i)] = pull * slope_s[rows, columns(i)]
                if sub == 1:
                    second_acc[:, columns(i)] += dot(branch_t, hidden_s[:, columns(i)])
            if i >= 1 and sub == 1:
                cols = columns(i - 1)
                first_acc[:, cols] += dot(first_t, pre_s[:, cols])
            if i >= pair and i % pair == 0:
                cols = columns(i - pair, pair)
                first_back += dot_nt(pre_s[rows, cols], first_w[:, cols])
            yield
        vector_acc[12:13, :] += jnp.sum(first_back * norm_1, axis=0, keepdims=True)
        vector_acc[13:14, :] += jnp.sum(first_back, axis=0, keepdims=True)
        resid_1 = norm_backward(first_back * gain_1, norm_1, inverse_1)
        resid_ref[rows, :] = resid_1
        attended_low = resid_1.astype(BF16)
        attended_s[rows, :] = attended_low
        vector_acc[10:11, :] += jnp.sum(attended_low.astype(F32), axis=0, keepdims=True)
        mixed_grad_ref[:, rows] = dot_nt(proj_ref[...], attended_low).astype(BF16)
        yield

    ahead, behind = stages(0), stages(1)
    for _ in range(LEAD):
        next(ahead)
    running = [ahead, behind]
    while running:
        for program in list(running):
            if next(program, 0) == 0:
                running.remove(program)
    proj_acc[...] += dot(mixed_t_ref[...], attended_s[...])

    @pl.when(step == pl.num_programs(0) - 1)
    def _():
        for d in range(VDP):
            rows = slice(d * tall, (d + 1) * tall)
            for c in range(VCHIP):
                for ref, half in ((mine_out, core), (other_out, 1 - core)):
                    to = pl.ds(pl.multiple_of((2 * c + half) * wide, wide), wide)
                    ref[d, c, 0] = first_acc[rows, to].astype(BF16)
                    ref[d, c, 1] = second_acc[rows, to].astype(BF16)
        proj_out[...] = proj_acc[...]
        for at in range(FF // D):
            vector_out[at : at + 1, :] = first_acc[D : D + 1, at * D : (at + 1) * D]
        vector_out[FF // D :, :] = vector_acc[FF // D :, :]


def feed_forward(marks, place, x, back, mixed, mixed_t, proj, mine, other, vector):
    total = x.shape[0]
    tile = lambda i, m, p: (i, 0)
    by_col = lambda i, m, p: (0, i)
    whole = lambda i, m, p: (0, 0)
    whole5 = lambda i, m, p: (0, 0, 0, 0, 0)
    return pl.pallas_call(
        feed_kernel,
        out_shape=(
            jax.ShapeDtypeStruct((total, D), F32),
            jax.ShapeDtypeStruct((total, D), F32),
            jax.ShapeDtypeStruct((D, total), BF16),
            jax.ShapeDtypeStruct(mine.shape, BF16),
            jax.ShapeDtypeStruct(mine.shape, BF16),
            jax.ShapeDtypeStruct((D, D), F32),
            jax.ShapeDtypeStruct((VEC, D), F32),
        ),
        grid_spec=pltpu.PrefetchScalarGridSpec(
            num_scalar_prefetch=2,
            grid=(total // TILE,),
            in_specs=[
                pl.BlockSpec((TILE, D), tile),
                pl.BlockSpec((TILE, D), tile),
                pl.BlockSpec((TILE, D), tile),
                pl.BlockSpec((D, TILE), by_col),
                pl.BlockSpec((D, D), whole),
                vspec(),
                vspec(),
                pl.BlockSpec((VEC, D), whole),
            ],
            out_specs=[
                pl.BlockSpec((TILE, D), tile),
                pl.BlockSpec((TILE, D), tile),
                pl.BlockSpec((D, TILE), by_col),
                pl.BlockSpec(mine.shape, whole5),
                pl.BlockSpec(mine.shape, whole5),
                pl.BlockSpec((D, D), whole),
                pl.BlockSpec((VEC, D), whole),
            ],
            scratch_shapes=[
                pltpu.VMEM((D, FF), BF16),
                pltpu.VMEM((D, FF), BF16),
                pltpu.VMEM((D + 16, FF), F32),
                pltpu.VMEM((D, FF), F32),
                pltpu.VMEM((D, D), F32),
                pltpu.VMEM((VEC, D), F32),
                pltpu.VMEM((TILE, FF), BF16),
                pltpu.VMEM((TILE, FF), BF16),
                pltpu.VMEM((TILE, FF), BF16),
                pltpu.VMEM((TILE, D), BF16),
                pltpu.VMEM((TILE, D), BF16),
                pltpu.VMEM((TILE, D), BF16),
                pltpu.VMEM((SEQ, D), F32),
                pltpu.VMEM((D, D), BF16),
            ],
        ),
        compiler_params=params(dimension_semantics=("arbitrary",)),
        cost_estimate=pl.CostEstimate(
            flops=14_000_000_000, bytes_accessed=15_000_000, transcendentals=4_200_000
        ),
        name="feed_forward",
    )(marks, place, x, back, mixed, mixed_t, proj, mine, other, vector)


def pull_kernel(
    marks,
    place,
    grad_t_ref,
    query_t_ref,
    value_ref,
    key_t_ref,
    out_t_ref,
    inverse_ref,
    exps_ref,
    qk_t_ref,
    x_t_ref,
    proj_ref,
    low_ref,
    own_ref,
    other_ref,
    sums_ref,
    dot_s,
    query_g,
    key_g,
    value_g,
    acc,
    sum_acc,
    value_s,
    scaled_t_s,
    score_s,
):
    group = pl.program_id(0)
    row = pl.program_id(1)
    begin = marks[row, 3]

    @pl.when(row == 0)
    def _():
        acc[...] = jnp.zeros_like(acc)
        sum_acc[...] = jnp.zeros_like(sum_acc)

    grad_t = grad_t_ref[...].astype(F32)
    head_of = iota((1, LANES), 1) // HEAD_DIM
    for at_head in range(GROUP):
        heads = slice(at_head * HEAD_DIM, (at_head + 1) * HEAD_DIM)
        part = grad_t[heads, :] * inverse_ref[0, at_head : at_head + 1, :]
        dot_s[at_head : at_head + 1, :] = jnp.sum(part * out_t_ref[heads, :], axis=0, keepdims=True)
        part = part.astype(BF16)
        scaled_t_s[heads, :] = part
        mask = jnp.where(head_of == at_head, 1.0, 0.0).astype(BF16)
        for half in range(2):
            rows = slice(half * HALF, (half + 1) * HALF)
            to = slice(at_head * HALF, (at_head + 1) * HALF)
            value_s[half, to, :] = value_ref[rows, :] * mask

    def score_grads_of(half, block):
        at = half * HALF + block * QBLOCK
        pulls = dot(value_s[half], scaled_t_s[:, at : at + QBLOCK])
        for at_head in range(GROUP):
            cols = slice(at_head * HALF + block * QBLOCK, at_head * HALF + (block + 1) * QBLOCK)
            pull = pulls[at_head * HALF : (at_head + 1) * HALF, :]
            pull = (pull - dot_s[at_head : at_head + 1, at : at + QBLOCK]).astype(BF16)
            score_s[half, :, cols] = exps_ref[0, 0, half, :, cols] * pull

    def finish(half, at_head):
        cols = slice(at_head * HALF, (at_head + 1) * HALF)
        rows = slice(half * HALF, (half + 1) * HALF)
        heads = slice(at_head * HEAD_DIM, (at_head + 1) * HEAD_DIM)
        score_grad = score_s[half, :, cols]
        value_g[heads, rows] = dot_nt(scaled_t_s[heads, rows], exps_ref[0, 0, half, :, cols])
        query_g[heads, rows] = dot(key_t_ref[heads, rows], score_grad)
        key_g[heads, rows] = dot_nt(query_t_ref[heads, rows], score_grad)

    blocks = HALF // QBLOCK
    each = GROUP // blocks
    for block in range(blocks):
        score_grads_of(0, block)
    for block in range(blocks):
        score_grads_of(1, block)
        for at_head in range(each * block, each * (block + 1)):
            finish(0, at_head)
    for at_head in range(GROUP):
        finish(1, at_head)
    query_low = query_g[...].astype(BF16)
    both_low = jnp.concatenate([key_g[...].astype(BF16), value_g[...].astype(BF16)], axis=0)
    ones = jnp.ones((16, SEQ), BF16)
    sum_acc[0:1, :] += dot_nt(ones, query_low)[0:1, :] * SCALE
    sum_acc[1:2, :] += dot_nt(ones, both_low[LANES:, :])[0:1, :]
    qk_t = qk_t_ref[...]
    both = dot_nt(qk_t, jnp.concatenate([query_low, both_low[:LANES, :]], axis=0))
    acc[:, :LANES] += both[:, :LANES] * SCALE
    acc[:, LANES : 2 * LANES] += both[:, LANES:]
    acc[:, 2 * LANES :] += dot_nt(x_t_ref[...], both_low[LANES:, :])
    low_ref[0, :LANES, :] = query_low
    low_ref[0, LANES:, :] = both_low

    def write(ref):
        tall = D // VDP
        for d in range(VDP):
            rows = slice(d * tall, (d + 1) * tall)
            for c in range(3):
                ref[d, c] = acc[rows, c * LANES : (c + 1) * LANES].astype(BF16)
            ref[d, 3] = proj_ref[rows, :].astype(BF16)

    last = row == pl.num_programs(1) - 1

    @pl.when(last & (group == place[2]))
    def _():
        write(own_ref)

    @pl.when(last & (group != place[2]))
    def _():
        write(other_ref)

    @pl.when(last)
    def _():
        sums_ref[pl.ds(group, 1)] = sum_acc[...][None]


def attend_back(marks, place, grad_t, query_t, value, key_t, out_t, inverse, exps, qk_t, x_t, proj):
    total = value.shape[0]
    rows = total // SEQ
    by_both = lambda g, r, m, p: (g, r)
    by_col = lambda g, r, m, p: (0, r)
    grads = jax.ShapeDtypeStruct((VDP, VCHIP, D // VDP, LANES), BF16)
    grads_spec = pl.BlockSpec(grads.shape, lambda g, r, m, p: (0, 0, 0, 0))
    return pl.pallas_call(
        pull_kernel,
        out_shape=(
            jax.ShapeDtypeStruct((2, 3 * LANES, total), BF16),
            grads,
            grads,
            jax.ShapeDtypeStruct((2, 8, LANES), F32),
        ),
        grid_spec=pltpu.PrefetchScalarGridSpec(
            num_scalar_prefetch=2,
            grid=(2, rows),
            in_specs=[
                pl.BlockSpec((LANES, SEQ), by_both),
                pl.BlockSpec((LANES, SEQ), by_both),
                pl.BlockSpec((SEQ, LANES), lambda g, r, m, p: (r, g)),
                pl.BlockSpec((LANES, SEQ), by_both),
                pl.BlockSpec((LANES, SEQ), by_both),
                pl.BlockSpec((1, 8, SEQ), lambda g, r, m, p: (g, 0, r)),
                pl.BlockSpec((1, 1, 2, HALF, GROUP * HALF), lambda g, r, m, p: (r, g, 0, 0, 0)),
                pl.BlockSpec((D, SEQ), by_col),
                pl.BlockSpec((D, SEQ), by_col),
                pl.BlockSpec((D, LANES), lambda g, r, m, p: (0, g)),
            ],
            out_specs=[
                pl.BlockSpec((1, 3 * LANES, SEQ), lambda g, r, m, p: (g, 0, r)),
                grads_spec,
                grads_spec,
                pl.BlockSpec((2, 8, LANES), lambda g, r, m, p: (0, 0, 0)),
            ],
            scratch_shapes=[
                pltpu.VMEM((8, SEQ), F32),
                pltpu.VMEM((LANES, SEQ), F32),
                pltpu.VMEM((LANES, SEQ), F32),
                pltpu.VMEM((LANES, SEQ), F32),
                pltpu.VMEM((D, 3 * LANES), F32),
                pltpu.VMEM((8, LANES), F32),
                pltpu.VMEM((2, GROUP * HALF, LANES), BF16),
                pltpu.VMEM((LANES, SEQ), BF16),
                pltpu.VMEM((2, HALF, GROUP * HALF), BF16),
            ],
        ),
        compiler_params=params(dimension_semantics=("arbitrary", "arbitrary")),
        cost_estimate=pl.CostEstimate(
            flops=36_000_000_000, bytes_accessed=30_000_000, transcendentals=0
        ),
        name="attend_back",
    )(marks, place, grad_t, query_t, value, key_t, out_t, inverse, exps, qk_t, x_t, proj)


def input_kernel(marks, low_ref, weight_ref, resid_ref, earlier_ref, input_ref, token_ref):
    token_ref[...] = jnp.zeros_like(token_ref)
    at = slice(0, LANES), slice(LANES, 2 * LANES), slice(2 * LANES, 3 * LANES)
    parts = [jnp.concatenate([low_ref[0, rows, :], low_ref[1, rows, :]], axis=0) for rows in at]
    pulled = dot(weight_ref[:, :D], parts[0]) * SCALE + (
        dot(weight_ref[:, D : 2 * D], parts[1]) + dot(weight_ref[:, 2 * D :], parts[2])
    )
    begin = marks[pl.program_id(0), 3]
    input_ref[...] = pltpu.roll(resid_ref[...] + pulled.T, begin, 0)


def input_pull(marks, low, weight, resid, earlier):
    total = resid.shape[0]
    by_row = pl.BlockSpec((SEQ, D), lambda r, m: (r, 0))
    return pl.pallas_call(
        input_kernel,
        out_shape=(
            jax.ShapeDtypeStruct((total, D), F32),
            jax.ShapeDtypeStruct((8, LANES), F32),
        ),
        grid_spec=pltpu.PrefetchScalarGridSpec(
            num_scalar_prefetch=1,
            grid=(total // SEQ,),
            in_specs=[
                pl.BlockSpec((2, 3 * LANES, SEQ), lambda r, m: (0, 0, r)),
                pl.BlockSpec((D, 3 * D), lambda r, m: (0, 0)),
                by_row,
                pl.BlockSpec(memory_space=pl.ANY),
            ],
            out_specs=[by_row, pl.BlockSpec((8, LANES), lambda r, m: (0, 0))],
        ),
        compiler_params=params(dimension_semantics=("arbitrary",)),
        cost_estimate=pl.CostEstimate(
            flops=1_000_000_000, bytes_accessed=8_000_000, transcendentals=0
        ),
        name="input_pull",
    )(marks, low, weight, resid, earlier)


def unroll_kernel(marks, turned_ref, earlier_ref, out_ref, token_ref):
    token_ref[...] = jnp.zeros_like(token_ref)
    out_ref[...] = pltpu.roll(turned_ref[...], marks[pl.program_id(0), 3], 0)


def unroll(marks, turned, earlier):
    by_row = pl.BlockSpec((SEQ, D), lambda r, m: (r, 0))
    return pl.pallas_call(
        unroll_kernel,
        out_shape=(
            jax.ShapeDtypeStruct(turned.shape, F32),
            jax.ShapeDtypeStruct((8, LANES), F32),
        ),
        grid_spec=pltpu.PrefetchScalarGridSpec(
            num_scalar_prefetch=1,
            grid=(turned.shape[0] // SEQ,),
            in_specs=[by_row, pl.BlockSpec(memory_space=pl.ANY)],
            out_specs=[by_row, pl.BlockSpec((8, LANES), lambda r, m: (0, 0))],
        ),
        compiler_params=params(dimension_semantics=("arbitrary",)),
        cost_estimate=pl.CostEstimate(flops=1_000_000, bytes_accessed=4_000_000, transcendentals=0),
        name="unroll",
    )(marks, turned, earlier)


def two_terms(rows):
    high = rows.astype(BF16)
    return jnp.concatenate([high.astype(F32), rows - high.astype(F32)], axis=0)


def column_to_row(columns, rows):
    lane = iota((rows, LANES), 1)
    wide = jnp.zeros((rows, LANES), F32)
    for i, column in enumerate(columns):
        wide = jnp.where(lane == i, column, wide)
    return wide.T[:8, :]


def total_of(array):
    return jnp.sum(jnp.sum(array, axis=0, keepdims=True), axis=1, keepdims=True)


def tail_ffn_kernel(place, ffn_ref, rows_1, rows_2, last_ref, grad_1, grad_2, grad_ref, stat_ref):
    lane = iota((1, LANES), 1)
    piece, across = [], []
    for kind in range(2):
        total = ffn_ref[0, kind].astype(F32)
        for at in range(1, VDP * VCHIP):
            total = total + ffn_ref[at, kind].astype(F32)
        (grad_1, grad_2)[kind][...] = total
        grad_ref[kind] = total
        square = total * total + EPS_ONE
        down = jnp.sum(square, axis=0, keepdims=True)
        piece += [down[:, :LANES], down[:, LANES:]]
        across.append(jnp.sum(square, axis=1, keepdims=True))
    across = column_to_row(across, total.shape[0])
    across = jnp.concatenate([across[0:1], across[1:2]], axis=1)
    olds = jnp.zeros((1, LANES), F32)
    for i, ref in enumerate((rows_1, rows_2)):
        olds = jnp.where(lane == i, jnp.sum(ref[...], axis=1, keepdims=True), olds)
    stat_ref[...] = jnp.concatenate([across] + piece + [olds, jnp.zeros((2, LANES), F32)], axis=0)


def tail_send_kernel(
    place, mine_ref, got_ref, vector_ref, sums_ref, stat_ref, stat_other_ref, send_ref, token_ref
):
    tall = D // VDP
    low, high = sums_ref[0], sums_ref[1]
    vector = jnp.concatenate(
        [
            vector_ref[:8, :],
            jnp.concatenate([low[:2], high[:2]], axis=1),
            vector_ref[10:, :],
        ],
        axis=0,
    )
    stat = jnp.concatenate([stat_ref[0:1, :] + stat_other_ref[0:1, :], stat_ref[1:6, :]], axis=0)
    stat = two_terms(stat)
    token_ref[...] = jnp.zeros_like(token_ref)
    rows = VEC // VDP
    for d in range(VDP):
        for c in range(VCHIP):
            at = d * VCHIP + c
            both = mine_ref[d, c].astype(F32) + got_ref[d, c].astype(F32)
            send_ref[at, :tall, :] = both.astype(BF16)
            part = vector[d * rows : (d + 1) * rows, c * 64 : (c + 1) * 64]
            part = jnp.concatenate([part, jnp.zeros((rows, LANES - 64), F32)], axis=1)
            send_ref[at, tall:, :] = jnp.concatenate([part, stat], axis=0).astype(BF16)


def tail_reduce_kernel(
    place,
    earlier_ref,
    got_ref,
    ffn_grad_ref,
    attn_ref,
    first_ref,
    second_ref,
    rows_0,
    rows_1,
    rows_2,
    cols_0,
    cols_1,
    cols_2,
    vector_ref,
    moment_ref,
    grad_ref,
    update_1,
    update_2,
    rows_out_1,
    rows_out_2,
    cols_out_1,
    cols_out_2,
    send_ref,
):
    decay = 1.0 - STEP ** (-0.8)
    chip = place[1]
    dp = place[0]
    tall = attn_ref.shape[0]
    rows, width = vector_ref.shape
    pieces = VDP * VCHIP
    lane = iota((1, LANES), 1)
    total = got_ref[0, :tall, :].astype(F32)
    part = got_ref[0, tall:, :].astype(F32)[:rows]
    for at in range(1, pieces):
        total = total + got_ref[at, :tall, :].astype(F32)
        part = part + got_ref[at, tall:, :].astype(F32)[:rows]
    grad_ref[...] = total
    low = total.astype(BF16)

    def stat_of(at):
        both = got_ref[pl.ds(at, 1), tall:, :][0].astype(F32)[rows:]
        return both[:6] + both[6:12]

    every = jnp.zeros((1, LANES), F32)
    olds = jnp.zeros((1, LANES), F32)
    mine = jnp.zeros((1, LANES), F32)
    down = jnp.zeros((6, LANES), F32)
    for d in range(VDP):
        down = down + stat_of(d * VCHIP + chip)
        for c in range(VCHIP):
            stat = stat_of(d * VCHIP + c)
            every = every + stat[0:1]
            if c == 0:
                olds = olds + stat[5:6]
    for c in range(VCHIP):
        mine = mine + stat_of(dp * VCHIP + c)[0:1]
    row_total = tall * VDP
    new_rows, means = [], []
    for i, ref in enumerate((rows_1, rows_2)):
        count = first_ref.shape[1] * 2 * VCHIP
        new_rows.append(decay * ref[...] + (1.0 - decay) * (mine[:, i * tall : (i + 1) * tall] / count))
        old = jnp.sum(jnp.where(lane == i, olds, 0.0), axis=1, keepdims=True)
        fresh = jnp.sum(every[:, i * tall : (i + 1) * tall], axis=1, keepdims=True)
        means.append((decay * old + (1.0 - decay) * (fresh / count)) / row_total)
    tile = jnp.concatenate(new_rows + [jnp.zeros((6, tall), F32)], axis=0)
    rows_out_1[...] = new_rows[0]
    rows_out_2[...] = new_rows[1]
    tile = jnp.concatenate([tile, jnp.zeros((8, LANES - tall), F32)], axis=1)
    turned = jnp.concatenate([tile, jnp.zeros((LANES - 8, LANES), F32)], axis=0).T
    scalars = jnp.zeros((1, LANES), F32)
    for i, (old_ref, out_ref, to) in enumerate(
        ((cols_1, cols_out_1, update_1), (cols_2, cols_out_2, update_2))
    ):
        sums = jnp.concatenate([down[1 + 2 * i : 2 + 2 * i], down[2 + 2 * i : 3 + 2 * i]], axis=1)
        cols = decay * old_ref[...] + (1.0 - decay) * (sums / row_total)
        out_ref[...] = cols
        grad = ffn_grad_ref[i]
        update = grad * lax.rsqrt(turned[:tall, i : i + 1] * cols / means[i])
        to[...] = update
        scalars = jnp.where(lane == 67 + i, total_of(update * update), scalars)
    for i, ref in enumerate((attn_ref, first_ref, second_ref)):
        weight = ref[...]
        scalars = jnp.where(lane == 64 + i, total_of(weight * weight), scalars)
    scalars = jnp.concatenate([rows_0[...], scalars[:, tall:]], axis=1)
    vector = vector_ref[...]
    power = jnp.sum(vector * vector, axis=1, keepdims=True)
    lines = jnp.concatenate(
        [part[:, :64], moment_ref[...], jnp.broadcast_to(power, (rows, LANES - 64 - width))], axis=1
    )
    piece = jnp.concatenate(
        [two_terms(lines), two_terms(jnp.concatenate([cols_0[...], scalars], axis=0))]
        + [jnp.zeros((4, LANES), F32)],
        axis=0,
    ).astype(BF16)
    for at in range(pieces):
        send_ref[at, :tall, :] = low
        send_ref[at, tall:, :] = piece


def tail_apply_kernel(
    place,
    mine_ref,
    other_ref,
    grad_ref,
    update_1,
    update_2,
    weight_0,
    weight_1,
    weight_2,
    rows_0,
    cols_0,
    vector_ref,
    moment_ref,
    new_0,
    new_1,
    new_2,
    rows_out,
    cols_out,
    vector_grad_ref,
    moment_out,
    vector_out,
    sums_s,
    rows_s,
):
    decay = 1.0 - STEP ** (-0.8)
    dp, chip, core = place[0], place[1], place[2]
    tall = weight_0.shape[0]
    rows, width = vector_ref.shape
    fsdp = 2 * VCHIP
    lane = iota((1, LANES), 1)
    refs = (mine_ref, other_ref)
    row_total = float(tall * VDP)
    col_total = float(LANES * fsdp)

    def lines_of(ref, at):
        both = ref[at, tall:, :].astype(F32)
        return both[0:4] + both[4:8], both[8:10] + both[10:12]

    scalars = jnp.zeros((1, LANES), F32)
    for ref in refs:
        for at in range(VDP * VCHIP):
            scalars = scalars + lines_of(ref, at)[1][1:2]
    scalar = lambda at: jnp.sum(jnp.where(lane == at, scalars, 0.0), axis=1, keepdims=True)

    tile, fresh = [], []
    for d in range(VDP):
        wide = jnp.zeros((tall, LANES), F32)
        for ref in refs:
            for c in range(VCHIP):
                block = ref[d * VCHIP + c, :tall, :].astype(F32)
                wide = wide + (block * block + EPS_ONE)
        fresh.append(jnp.sum(wide, axis=1, keepdims=True))
        tile.append(lines_of(mine_ref, d * VCHIP)[1][1:2])
    tile = jnp.concatenate(tile + [jnp.zeros((LANES - VDP, LANES), F32)], axis=0).T
    mean = jnp.zeros((1, 1), F32)
    new_rows = []
    for d in range(VDP):
        new = decay * tile[:tall, d : d + 1] + (1.0 - decay) * (fresh[d] / col_total)
        new_rows.append(1.0 / new)
        mean = mean + jnp.sum(new, axis=0, keepdims=True)
        sums_s[d] = jnp.broadcast_to(fresh[d], (tall, LANES))
    mean = mean / row_total
    mine = sums_s[pl.ds(dp, 1)][0]
    rows_s[...] = mine.T
    rows_new = decay * rows_0[...] + (1.0 - decay) * (rows_s[0:1, :tall] / col_total)
    rows_out[...] = rows_new
    power = jnp.zeros((1, 1), F32)
    for half, ref in enumerate(refs):
        for c in range(VCHIP):
            down = jnp.zeros((tall, LANES), F32)
            weighted = jnp.zeros((tall, LANES), F32)
            for d in range(VDP):
                block = ref[d * VCHIP + c, :tall, :].astype(F32)
                square = block * block
                down = down + (square + EPS_ONE)
                weighted = weighted + square * new_rows[d]
            down = jnp.sum(down, axis=0, keepdims=True)
            old = lines_of(ref, c)[1][0:1]
            cols = decay * old + (1.0 - decay) * (down / row_total)
            weighted = jnp.sum(weighted, axis=0, keepdims=True) / cols
            power = power + jnp.sum(weighted, axis=1, keepdims=True)
            if half == 0:
                sums_s[VDP + c] = jnp.broadcast_to(down, (tall, LANES))
    power = power * mean
    down = sums_s[pl.ds(VDP + chip, 1)][0][0:1, :]
    cols_new = decay * cols_0[...] + (1.0 - decay) * (down / row_total)
    cols_out[...] = cols_new
    column = jnp.concatenate(
        [
            jnp.concatenate([rows_new, jnp.zeros((1, LANES - tall), F32)], axis=1),
            jnp.zeros((LANES - 1, LANES), F32),
        ],
        axis=0,
    ).T[:tall, 0:1]
    update_0 = grad_ref[...] * lax.rsqrt(column * cols_new / mean)
    powers = (power, scalar(67), scalar(68))
    for i, (update, weight, new) in enumerate(
        (
            (update_0, weight_0, new_0),
            (update_1[...], weight_1, new_1),
            (update_2[...], weight_2, new_2),
        )
    ):
        entries = float(weight.shape[0] * weight.shape[1] * VDP * fsdp)
        clip = jnp.maximum(1.0, jnp.sqrt(powers[i] / entries) / CLIP_LIMIT)
        rate = STEP_RATE * jnp.maximum(EPS_TWO, jnp.sqrt(scalar(64 + i) / entries))
        new[...] = weight[...] - rate / clip * update
    powers, sizes = [], []
    for d in range(VDP):
        power = jnp.zeros((rows, 1), F32)
        size = jnp.zeros((rows, 1), F32)
        for c in range(VCHIP):
            at = d * VCHIP + c
            first, second = lines_of(mine_ref, at)[0], lines_of(other_ref, at)[0]
            both = first[:, :64] + second[:, :64]
            size = size + first[:, LANES - 1 :] + second[:, LANES - 1 :]
            near = jnp.where(core == 0, first[:, 64 : 64 + width], second[:, 64 : 64 + width])
            far = jnp.where(core == 0, second[:, 64 : 64 + width], first[:, 64 : 64 + width])
            moment = jnp.concatenate([near, far], axis=1)
            moment = decay * moment + (1.0 - decay) * (both * both + EPS_ONE)
            power = power + jnp.sum(both * both / moment, axis=1, keepdims=True)
            wide = jnp.concatenate([both, jnp.zeros((rows, LANES - 64), F32)], axis=1)
            sums_s[2 * VDP + at, :rows, :] = wide
        powers.append(power)
        sizes.append(size)
    both = sums_s[pl.ds(2 * VDP + dp * VCHIP + chip, 1), :rows, :][0]
    vector_grad = jnp.where(core == 0, both[:, :width], both[:, width : 2 * width])
    vector_grad_ref[...] = vector_grad
    moment = decay * moment_ref[...] + (1.0 - decay) * (vector_grad * vector_grad + EPS_ONE)
    moment_out[...] = moment
    step = vector_grad * lax.rsqrt(moment)
    bias = VDP // 2
    bias_power = sum(jnp.sum(power, axis=0, keepdims=True) for power in powers[:bias])
    bias_size = sum(jnp.sum(size, axis=0, keepdims=True) for size in sizes[:bias])
    power, size = powers[bias], sizes[bias]
    for d in range(bias + 1, VDP):
        power = jnp.where(dp == d, powers[d], power)
        size = jnp.where(dp == d, sizes[d], size)
    is_bias = dp < bias
    power = jnp.where(is_bias, bias_power, power)
    size = jnp.where(is_bias, bias_size, size)
    count = jnp.where(is_bias, float(FF), float(D))
    clip = jnp.maximum(1.0, jnp.sqrt(power / count) / CLIP_LIMIT)
    rate = STEP_RATE * jnp.maximum(EPS_TWO, jnp.sqrt(size / count))
    vector_out[...] = vector_ref[...] - rate / clip * step


def whole_call(kernel, name, place, outs, *operands, scratch=(), earlier=None):
    tied = () if earlier is None else (earlier,)
    return pl.pallas_call(
        kernel,
        out_shape=[jax.ShapeDtypeStruct(shape, kind) for shape, kind in outs],
        in_specs=[pl.BlockSpec(memory_space=pltpu.SMEM)]
        + [pl.BlockSpec(memory_space=pl.ANY)] * len(tied)
        + [vspec()] * len(operands),
        out_specs=[vspec()] * len(outs),
        scratch_shapes=list(scratch),
        compiler_params=params(16),
        name=name,
    )(place, *tied, *operands)


def core_swap(block):
    return lax.ppermute(block, "core", [(0, 1), (1, 0)])


def exchange(blocks, axes):
    return lax.all_to_all(blocks, axes, split_axis=0, concat_axis=0, tiled=True)


def after(value, *earlier, mib=8):
    return pl.pallas_call(
        lambda *refs: None,
        out_shape=jax.ShapeDtypeStruct(value.shape, value.dtype),
        in_specs=[pl.BlockSpec(memory_space=pltpu.HBM)] * (1 + len(earlier)),
        out_specs=pl.BlockSpec(memory_space=pltpu.HBM),
        input_output_aliases={0: 0},
        compiler_params=params(mib),
        name="after",
    )(value, *earlier)


def pair_kernel(mine_ref, got_ref, out_ref):
    out_ref[...] = (mine_ref[...].astype(F32) + got_ref[...].astype(F32)).astype(BF16)


def pair_sum(mine, got):
    return pl.pallas_call(
        pair_kernel,
        out_shape=jax.ShapeDtypeStruct(mine.shape, BF16),
        in_specs=[vspec(), vspec()],
        out_specs=vspec(),
        compiler_params=params(16),
        name="pair_sum",
    )(mine, got)


CHIPS = ("dp", "chip")
ALL = ("dp", "chip", "core")


def layer(place, weights, segment_ids, tokens, cotangent, ffn_weights, send_core, send_ffn):
    table = jnp.asarray(encode_table())
    qk, x, qk_t, x_t, marks = place_tokens(segment_ids, tokens, table)
    query_t, value, key_t, out_t, inverse, mixed, mixed_t, exps, weight, proj, vector = attend_forward(
        marks, place, x, qk, x_t, qk_t, *weights(marks)
    )
    ffn_mine, ffn_other = ffn_weights(marks, vector)
    block_out, resid, grad_t, ffn_mine, ffn_other, proj_g, vector_g = feed_forward(
        marks, place, x, cotangent, mixed, mixed_t, proj, ffn_mine, ffn_other, vector
    )
    ffn_got, grad_t = send_ffn(ffn_mine, ffn_other, grad_t)
    low, grads_own, grads_other, sums = attend_back(
        marks, place, grad_t, query_t, value, key_t, out_t, inverse, exps, qk_t, x_t, proj_g
    )
    attn_got = send_core(grads_other)
    pull = lambda earlier: input_pull(marks, low, weight, resid, earlier)
    unrolled = lambda earlier: unroll(marks, block_out, earlier)
    return unrolled, pull, grads_own, grads_other, attn_got, sums, vector_g, ffn_got


def body(
    tokens,
    cotangent,
    segment_ids,
    attn_weight,
    ffn_in,
    ffn_out,
    vectors,
    attn_rows,
    attn_cols,
    in_rows,
    in_cols,
    out_rows,
    out_cols,
    vector_moment,
):
    place = jnp.stack([lax.axis_index("dp"), lax.axis_index("chip"), lax.axis_index("core")])
    place = place.astype(jnp.int32)
    pieces = VDP * VCHIP
    tall, wide = attn_weight.shape
    rows_v, cols_v = vectors.shape
    split = lambda array: array.reshape((VDP, VCHIP) + array.shape[1:])
    attn_sent, ffn_low = pack_attn(place, attn_weight, ffn_in, ffn_out, vectors)
    attn_mine = exchange(attn_sent, CHIPS)

    parts = [
        lax.ppermute(ffn_low, "dp", [(i, i ^ step) for i in range(VDP)]) for step in range(1, VDP)
    ]
    ffn_sent = pack_ffn(place, ffn_low, parts)

    def attn_weights(marks):
        mine = split(after(attn_mine, marks))
        return mine, core_swap(mine)

    def ffn_weights(marks, vector):
        got = exchange(after(ffn_sent, marks), "chip")
        ffn_mine = after(got, vector)
        return ffn_mine, core_swap(ffn_mine)

    def send_ffn(mine, other, grad_t):
        both = pair_sum(mine, core_swap(other))
        got = exchange(both.reshape((pieces,) + mine.shape[2:]), CHIPS)
        return got, after(grad_t, both, mib=56)

    (
        unrolled,
        pull,
        grads_own,
        grads_other,
        attn_got,
        sums,
        vector_g,
        ffn_got,
    ) = layer(place, attn_weights, segment_ids, tokens, cotangent, ffn_weights, core_swap, send_ffn)
    lay = lambda stat: stat.reshape(1, -1)
    rows_old = (lay(attn_rows), lay(in_rows), lay(out_rows))
    cols_old = (lay(attn_cols), lay(in_cols), lay(out_cols))
    weights_old = (attn_weight, ffn_in, ffn_out)
    in_grad, out_grad, ffn_grad, stat = whole_call(
        tail_ffn_kernel,
        "tail_ffn",
        place,
        [(ffn_in.shape, F32), (ffn_out.shape, F32), ((2,) + ffn_in.shape, F32), ((8, LANES), F32)],
        ffn_got,
        *rows_old[1:],
        sums,
    )
    sent, token = whole_call(
        tail_send_kernel,
        "tail_send",
        place,
        [((pieces, tall + VROWS, LANES), BF16), ((8, LANES), F32)],
        grads_own,
        attn_got,
        vector_g,
        sums,
        stat,
        core_swap(stat),
    )
    input_grad, token = pull(token)
    got = exchange(sent, CHIPS)
    attn_grad, update_1, update_2, rows_new_1, rows_new_2, cols_new_1, cols_new_2, sent = whole_call(
        tail_reduce_kernel,
        "tail_reduce",
        place,
        [
            (attn_weight.shape, F32),
            (ffn_in.shape, F32),
            (ffn_out.shape, F32),
            (rows_old[1].shape, F32),
            (rows_old[2].shape, F32),
            (cols_old[1].shape, F32),
            (cols_old[2].shape, F32),
            ((pieces, tall + VROWS, LANES), BF16),
        ],
        got,
        ffn_grad,
        *weights_old,
        *rows_old,
        *cols_old,
        vectors,
        vector_moment,
        earlier=token,
    )
    block_out, token = unrolled(rows_new_1)
    mine = after(exchange(sent, CHIPS), token)
    attn_new, in_new, out_new, rows_new_0, cols_new_0, vector_grad, moment_new, vectors_new = whole_call(
        tail_apply_kernel,
        "tail_apply",
        place,
        [
            (attn_weight.shape, F32),
            (ffn_in.shape, F32),
            (ffn_out.shape, F32),
            (rows_old[0].shape, F32),
            (cols_old[0].shape, F32),
            (vectors.shape, F32),
            (vectors.shape, F32),
            (vectors.shape, F32),
        ],
        mine,
        core_swap(mine),
        attn_grad,
        update_1,
        update_2,
        *weights_old,
        rows_old[0],
        cols_old[0],
        vectors,
        vector_moment,
        scratch=[
            pltpu.VMEM((2 * VDP + pieces, tall, LANES), F32),
            pltpu.VMEM((LANES, tall), F32),
        ],
    )
    return (
        block_out,
        input_grad,
        attn_grad,
        in_grad,
        out_grad,
        vector_grad,
        rows_new_0.reshape(-1),
        cols_new_0.reshape(-1),
        rows_new_1.reshape(-1),
        cols_new_1.reshape(-1),
        rows_new_2.reshape(-1),
        cols_new_2.reshape(-1),
        moment_new,
        attn_new,
        in_new,
        out_new,
        vectors_new,
    )


def gather_all(block):
    shape = (lax.axis_size("dp"), lax.axis_size("chip") * 2)
    count = shape[0] * shape[1]
    got = exchange(jnp.broadcast_to(block[None], (count,) + block.shape), ALL)
    return got.reshape(shape + block.shape)


def unblock(parts):
    dp_count, fsdp_count, rows, cols = parts.shape
    return parts.transpose(0, 2, 1, 3).reshape(dp_count * rows, fsdp_count * cols)


def scatter_sum(full):
    dp_count = lax.axis_size("dp")
    fsdp_count = lax.axis_size("chip") * 2
    rows, cols = full.shape
    by_col = full.astype(BF16).reshape(rows, fsdp_count, cols // fsdp_count).transpose(1, 0, 2)
    got = exchange(by_col, ("chip", "core"))
    part = jnp.sum(got.astype(F32), axis=0).astype(BF16)
    by_row = part.reshape(dp_count, rows // dp_count, cols // fsdp_count)
    return jnp.sum(exchange(by_row, "dp").astype(F32), axis=0)


def body_any(
    tokens,
    cotangent,
    segment_ids,
    attn_weight,
    ffn_in,
    ffn_out,
    vectors,
    attn_rows,
    attn_cols,
    in_rows,
    in_cols,
    out_rows,
    out_cols,
    vector_moment,
):
    dp_count = lax.axis_size("dp")
    fsdp_count = lax.axis_size("chip") * 2
    dp_place = lax.axis_index("dp")
    fsdp_place = lax.axis_index("chip") * 2 + lax.axis_index("core")
    rows_w = attn_weight.shape[0]
    rows_v = vectors.shape[0]
    place = jnp.zeros((3,), jnp.int32)
    full_attn = unblock(gather_all(attn_weight.astype(BF16)))
    full_vector = unblock(gather_all(vectors.astype(BF16)))
    full_ffn = jnp.stack(
        [unblock(gather_all(ffn_in.astype(BF16))), unblock(gather_all(ffn_out.astype(BF16)))]
    )
    tall = D // VDP
    cut = full_attn.reshape(VDP, tall, VCHIP, 2, LANES).transpose(3, 0, 2, 1, 4)
    lines = full_vector.reshape(VDP, VEC // VDP, 2, LANES).transpose(0, 2, 1, 3)
    lines = lines.reshape(VDP, 1, 2 * VEC // VDP, LANES)
    lines = jnp.pad(lines, ((0, 0), (0, VCHIP - 1), (0, VROWS - 2 * VEC // VDP), (0, 0)))
    weights = (
        jnp.concatenate([cut[0], lines], axis=2),
        jnp.concatenate([cut[1], jnp.zeros_like(lines)], axis=2),
    )
    ffn_cut = full_ffn.reshape(2, VDP, tall, VCHIP, 2, FF // (2 * VCHIP))
    ffn_cut = ffn_cut.transpose(4, 3, 1, 0, 2, 5)
    (
        unrolled,
        pull,
        grads_own,
        grads_other,
        _,
        sums,
        vector_g,
        ffn_got,
    ) = layer(
        place,
        lambda marks: weights,
        segment_ids,
        tokens,
        cotangent,
        lambda marks, vector: (ffn_cut[0], ffn_cut[1]),
        lambda block: block,
        lambda mine, other, grad_t: (jnp.stack([mine, other]), grad_t),
    )
    block_out = unrolled(sums)[0]
    input_grad = pull(sums)[0]
    attn_full = jnp.stack([grads_own, grads_other]).transpose(1, 3, 2, 0, 4).reshape(D, 4 * D)
    ffn_full = ffn_got.transpose(3, 1, 4, 2, 0, 5).reshape(2, D, FF)
    sums = jnp.concatenate([sums[0, :2], sums[1, :2]], axis=1)
    vector_full = jnp.concatenate([vector_g[:8], sums, vector_g[10:]], axis=0)
    attn_grad = scatter_sum(attn_full)
    in_grad = scatter_sum(ffn_full[0])
    out_grad = scatter_sum(ffn_full[1])
    vector_grad = scatter_sum(vector_full)

    decay = 1.0 - STEP ** (-0.8)
    gradients = (attn_grad, in_grad, out_grad)
    weights_old = (attn_weight, ffn_in, ffn_out)
    rows_old = (attn_rows, in_rows, out_rows)
    cols_old = (attn_cols, in_cols, out_cols)
    moment_new = decay * vector_moment + (1.0 - decay) * (vector_grad * vector_grad + EPS_ONE)
    vector_step = vector_grad * lax.rsqrt(moment_new)
    squares = [gradient * gradient + EPS_ONE for gradient in gradients]
    pieces = []
    for square in squares:
        pieces.append(jnp.sum(square, axis=1))
    for square in squares:
        pieces.append(jnp.sum(square, axis=0))
    pieces.append(jnp.sum(vector_step * vector_step, axis=1))
    pieces.append(jnp.sum(vectors * vectors, axis=1))
    pieces.append(jnp.stack([jnp.sum(weight * weight) for weight in weights_old]))
    pieces.append(jnp.stack([jnp.sum(old) for old in rows_old]))
    sizes = [piece.shape[0] for piece in pieces]
    flat = jnp.concatenate(pieces)
    flat = jnp.pad(flat, (0, -flat.shape[0] % 1024)).reshape(-1, LANES)
    got = gather_all(flat).reshape(dp_count, fsdp_count, -1)
    offsets = [0]
    for length in sizes:
        offsets.append(offsets[-1] + length)
    take = lambda i: got[:, :, offsets[i] : offsets[i + 1]]
    rows_new, cols_new, row_means, entries = [], [], [], []
    for i in range(3):
        count_rows = rows_w * dp_count
        count_cols = weights_old[i].shape[1] * fsdp_count
        entries.append(float(count_rows * count_cols))
        row_all = jnp.sum(take(i), axis=1)
        mine = lax.dynamic_index_in_dim(row_all, dp_place, 0, keepdims=False)
        rows_new.append(decay * rows_old[i] + (1.0 - decay) * mine / count_cols)
        col_all = jnp.sum(take(3 + i), axis=0)
        mine = lax.dynamic_index_in_dim(col_all, fsdp_place, 0, keepdims=False)
        cols_new.append(decay * cols_old[i] + (1.0 - decay) * mine / count_rows)
        old_total = jnp.sum(take(9)[:, 0, i])
        row_means.append(
            (decay * old_total + (1.0 - decay) * jnp.sum(row_all) / count_cols) / count_rows
        )
    step_rows = jnp.sum(take(6), axis=1).reshape(-1)
    weight_rows = jnp.sum(take(7), axis=1).reshape(-1)
    weight_totals = jnp.sum(take(8), axis=(0, 1))
    updates = []
    for i in range(3):
        second = rows_new[i][:, None] * cols_new[i][None, :] / row_means[i]
        updates.append(gradients[i] * lax.rsqrt(second))
    flat = jnp.stack([jnp.sum(update * update) for update in updates])
    flat = jnp.broadcast_to(jnp.pad(flat, (0, 5))[:, None], (8, LANES))
    totals = jnp.sum(gather_all(flat)[:, :, :, 0], axis=(0, 1))
    new_weights = []
    for i in range(3):
        clip_factor = jnp.maximum(1.0, jnp.sqrt(totals[i] / entries[i]) / CLIP_LIMIT)
        step_size = STEP_RATE * jnp.maximum(EPS_TWO, jnp.sqrt(weight_totals[i] / entries[i]))
        new_weights.append(weights_old[i] - step_size / clip_factor * updates[i])
    bias_rows = FF // D
    row_places = jnp.arange(VEC)
    counts = jnp.where(row_places < bias_rows, float(FF), float(D))
    grouped_updates = jnp.where(row_places < bias_rows, jnp.sum(step_rows[:bias_rows]), step_rows)
    grouped_weights = jnp.where(row_places < bias_rows, jnp.sum(weight_rows[:bias_rows]), weight_rows)
    clip_rows = jnp.maximum(1.0, jnp.sqrt(grouped_updates / counts) / CLIP_LIMIT)
    step_sizes = STEP_RATE * jnp.maximum(EPS_TWO, jnp.sqrt(grouped_weights / counts))
    factor_rows = lax.dynamic_slice_in_dim(step_sizes / clip_rows, dp_place * rows_v, rows_v)
    vectors_new = vectors - factor_rows[:, None] * vector_step
    return (
        block_out,
        input_grad,
        attn_grad,
        in_grad,
        out_grad,
        vector_grad,
        rows_new[0],
        cols_new[0],
        rows_new[1],
        cols_new[1],
        rows_new[2],
        cols_new[2],
        moment_new,
        new_weights[0],
        new_weights[1],
        new_weights[2],
        vectors_new,
    )


def solution(mesh):
    dp_count, fsdp_count = mesh.shape["dp"], mesh.shape["fsdp"]
    inner = jax.sharding.Mesh(mesh.devices.reshape(dp_count, fsdp_count // 2, 2), ALL)
    fsdp = ("chip", "core")
    split = P(ALL, None)
    block = P("dp", fsdp)
    stats = (P("dp"), P(fsdp)) * 3
    plain = dp_count == VDP and fsdp_count == 2 * VCHIP
    return jax.shard_map(
        body if plain else body_any,
        mesh=inner,
        in_specs=(split,) * 3 + (block,) * 4 + stats + (block,),
        out_specs=(split,) * 2 + (block,) * 4 + stats + (block,) * 5,
        check_vma=False,
    )
```

```python
import functools
import math

import jax
import jax.numpy as jnp
import numpy as np
from jax import lax
from jax.experimental import pallas as pl
from jax.experimental.pallas import tpu as pltpu
from jax.sharding import PartitionSpec as P

D = 256
FF = 2048
HEADS = 8
HEAD_DIM = 32
SEQ = 1024
HALF = 512
GROUP = 4
LANES = 128
QBLOCK = 512
WGRID = 32
STEP = 10
VEC = 16
TILE = 1024
CHUNK = 256
SUB = 512
LEAD = 5
STRIP = 64
VDP = 4
VCHIP = 4
VROWS = 16

EPS_NORM = 1e-05
EPS_ONE = 1e-30
EPS_TWO = 0.001
CLIP_LIMIT = 1.0
STEP_RATE = 0.3
FAR = 1e30
TAME = 40.0
LOG2_E = math.log2(math.e)
SCALE = HEAD_DIM ** (-0.5)
GELU_A = math.sqrt(2.0 / math.pi)
GELU_B = 0.044715
F32 = jnp.float32
BF16 = jnp.bfloat16
MIB = 1024 * 1024


def dot(left, right):
    return jnp.dot(left, right, preferred_element_type=F32)


def dot_nt(left, right):
    return lax.dot_general(left, right, (((1,), (1,)), ((), ())), preferred_element_type=F32)


def encode_table():
    half = D // 2
    feature = np.arange(half)
    freq = np.exp(
        (2 * (feature // 2)).astype(np.float32) * np.float32(-math.log(10000.0) / half)
    ).astype(np.float32)
    angles = np.arange(1, WGRID + 1, dtype=np.float32)[:, None] * freq[None, :]
    table = np.where(feature % 2 == 0, np.sin(angles), np.cos(angles)).astype(np.float32)
    low = jnp.bfloat16
    one = table.astype(low)
    rest = table - one.astype(np.float32)
    two = rest.astype(low)
    three = (rest - two.astype(np.float32)).astype(low)
    blank = np.zeros((LANES - 3 * WGRID, half), low)
    return np.concatenate([one, two, three, blank], axis=0)


def iota(shape, dim):
    return lax.broadcasted_iota(jnp.int32, shape, dim)


def norm_forward(rows):
    centered = rows - jnp.mean(rows, axis=-1, keepdims=True)
    inverse = lax.rsqrt(jnp.mean(centered * centered, axis=-1, keepdims=True) + EPS_NORM)
    return centered * inverse, inverse


def norm_backward(upstream, normed, inverse):
    return inverse * (
        upstream
        - jnp.mean(upstream, axis=-1, keepdims=True)
        - normed * jnp.mean(upstream * normed, axis=-1, keepdims=True)
    )

def vspec():
    return pl.BlockSpec(memory_space=pltpu.VMEM)


def params(mib=56, **more):
    return pltpu.CompilerParams(vmem_limit_bytes=mib * MIB, **more)


def pack_kernel(place, attn_ref, first_ref, second_ref, vector_ref, out_ref, ffn_ref):
    owner = place[1] * 2 + place[2]
    vector = vector_ref[...]
    rows = vector.shape[0]
    wide = jnp.concatenate([vector] * (LANES // vector.shape[1]), axis=1)
    slot = iota((rows, LANES), 1) // vector.shape[1]
    per = LANES // vector.shape[1]
    parts = [attn_ref[...]]
    for half in range(2):
        parts.append(jnp.where(slot + half * per == owner, wide, 0.0))
    parts.append(jnp.zeros((VROWS - 2 * rows, LANES), F32))
    piece = jnp.concatenate(parts, axis=0).astype(BF16)
    for at in range(VDP * VCHIP):
        out_ref[at] = piece
    ffn_ref[0] = first_ref[...].astype(BF16)
    ffn_ref[1] = second_ref[...].astype(BF16)


def pack_attn(place, attn_weight, ffn_in, ffn_out, vectors):
    return pl.pallas_call(
        pack_kernel,
        out_shape=(
            jax.ShapeDtypeStruct((VDP * VCHIP, attn_weight.shape[0] + VROWS, LANES), BF16),
            jax.ShapeDtypeStruct((2,) + ffn_in.shape, BF16),
        ),
        in_specs=[pl.BlockSpec(memory_space=pltpu.SMEM)] + [vspec()] * 4,
        out_specs=(vspec(), vspec()),
        compiler_params=params(),
        name="pack_attn",
    )(place, attn_weight, ffn_in, ffn_out, vectors)


def pack_ffn_kernel(place, own_ref, *refs):
    out_ref = refs[-1]
    for at in range(VCHIP):
        out_ref[at, pl.ds(place[0], 1)] = own_ref[...][None]
        for step in range(1, VDP):
            out_ref[at, pl.ds(place[0] ^ step, 1)] = refs[step - 1][...][None]


def pack_ffn(place, own, parts):
    return pl.pallas_call(
        pack_ffn_kernel,
        out_shape=jax.ShapeDtypeStruct((VCHIP, VDP) + own.shape, BF16),
        in_specs=[pl.BlockSpec(memory_space=pltpu.SMEM)] + [vspec()] * (1 + len(parts)),
        out_specs=vspec(),
        compiler_params=params(16),
        name="pack_ffn",
    )(place, own, *parts)


def place_kernel(
    segment_ref, tokens_ref, table_ref, qk_ref, x_ref, qk_t_ref, x_t_ref, marks_ref
):
    row = pl.program_id(0)
    starts = []
    for number in range(1, 4):
        at = jnp.int32(0)
        for step in (512, 256, 128, 64, 32, 16, 8, 4, 2, 1, 1):
            probe = jnp.minimum(at + (step - 1), SEQ - 1)
            at = jnp.where(segment_ref[row, probe] < number, at + step, at)
        starts.append(at)
    edges = [jnp.int32(0)] + starts + [jnp.int32(SEQ)]
    begin = jnp.int32(0)
    for number in range(3, -1, -1):
        begin = jnp.where(edges[number + 1] - edges[number] == HALF, edges[number], begin)
    for number in range(3):
        marks_ref[row, number] = starts[number]
    marks_ref[row, 3] = begin
    one, two, three = starts
    x = pltpu.roll(tokens_ref[...].astype(F32), (SEQ - begin) & (SEQ - 1), 0)
    x_ref[...] = x.astype(BF16)
    x_t_ref[...] = x.T.astype(BF16)
    at = (iota((SEQ, LANES), 0) + begin) & (SEQ - 1)
    lane = iota((SEQ, LANES), 1)
    start = jnp.where(at >= three, three, jnp.where(at >= two, two, jnp.where(at >= one, one, 0)))
    local = at - start
    kept = lane < 3 * WGRID
    slot = lane & (WGRID - 1)
    hot_r = jnp.where(((local >> 5) == slot) & kept, 1.0, 0.0).astype(BF16)
    hot_c = jnp.where(((local & (WGRID - 1)) == slot) & kept, 1.0, 0.0).astype(BF16)
    table = table_ref[...]
    places = jnp.concatenate([dot(hot_r, table), dot(hot_c, table)], axis=1)
    qk = x + places
    qk_ref[...] = qk.astype(BF16)
    qk_t_ref[...] = qk.T.astype(BF16)


def place_tokens(segment_ids, tokens, table):
    rows = segment_ids.shape[0]
    by_row = lambda r: (r, 0)
    return pl.pallas_call(
        place_kernel,
        out_shape=(
            jax.ShapeDtypeStruct(tokens.shape, BF16),
            jax.ShapeDtypeStruct(tokens.shape, BF16),
            jax.ShapeDtypeStruct((D, tokens.shape[0]), BF16),
            jax.ShapeDtypeStruct((D, tokens.shape[0]), BF16),
            jax.ShapeDtypeStruct((rows, 4), jnp.int32),
        ),
        grid=(rows,),
        in_specs=[
            pl.BlockSpec(memory_space=pltpu.SMEM),
            pl.BlockSpec((SEQ, D), by_row),
            pl.BlockSpec((LANES, LANES), lambda r: (0, 0)),
        ],
        out_specs=(
            pl.BlockSpec((SEQ, D), by_row),
            pl.BlockSpec((SEQ, D), by_row),
            pl.BlockSpec((D, SEQ), lambda r: (0, r)),
            pl.BlockSpec((D, SEQ), lambda r: (0, r)),
            pl.BlockSpec(memory_space=pltpu.SMEM),
        ),
        compiler_params=params(dimension_semantics=("arbitrary",)),
        cost_estimate=pl.CostEstimate(flops=600_000_000, bytes_accessed=4_000_000, transcendentals=0),
        name="place_tokens",
    )(segment_ids, tokens, table)


def attend_kernel(
    marks,
    place,
    x_ref,
    qk_ref,
    x_t_ref,
    qk_t_ref,
    mine_ref,
    other_ref,
    query_t_ref,
    value_ref,
    key_t_ref,
    out_t_ref,
    inverse_ref,
    mixed_ref,
    mixed_t_ref,
    exps_ref,
    weight_ref,
    proj_ref,
    vector_ref,
    key_s,
    value_s,
    mark_k,
    mark_q,
    first_s,
    second_s,
    weight_t_s,
    bias_s,
    tame_s,
    exps_s,
    exps_sem,
):
    row = pl.program_id(0)
    begin = marks[row, 3]
    core = place[2]

    def copy_of(group, half):
        return pltpu.make_async_copy(
            exps_s.at[group, half], exps_ref.at[row, group, half], exps_sem.at[group * 2 + half]
        )

    @pl.when(row == 0)
    def _():
        tall = D // VDP
        for d in range(VDP):
            rows = slice(d * tall, (d + 1) * tall)
            total = jnp.zeros((8, LANES), F32)
            for c in range(VCHIP):
                for ref, half in ((mine_ref, core), (other_ref, 1 - core)):
                    if c < 3:
                        to = pl.ds(pl.multiple_of(c * D + half * LANES, LANES), LANES)
                        weight_ref[rows, to] = ref[d, c, :tall, :]
                    else:
                        to = pl.ds(pl.multiple_of(half * LANES, LANES), LANES)
                        proj_ref[rows, to] = ref[d, c, :tall, :]
                    total += ref[d, c, tall:, :].astype(F32)[:8]
            vector_ref[d * 4 : (d + 1) * 4, :LANES] = total[:4]
            vector_ref[d * 4 : (d + 1) * 4, LANES:] = total[4:]
        weight_t_s[...] = weight_ref[...].astype(F32).T.astype(BF16)
        bias_s[...] = vector_ref[8:16, :].T

    qk_t = qk_t_ref[...]
    query_t = (dot(weight_t_s[:D, :], qk_t) + bias_s[:, 0:1]) * SCALE
    query_t = query_t.astype(BF16)
    query_t_ref[...] = query_t
    key_t = dot(weight_t_s[D : 2 * D, :], qk_t).astype(BF16)
    key_t_ref[...] = key_t

    def largest_norms(rows):
        rows = rows.astype(F32)
        rows = rows * rows
        sums = [
            jnp.sum(rows[head * HEAD_DIM : (head + 1) * HEAD_DIM], axis=0, keepdims=True)
            for head in range(HEADS)
        ]
        return jnp.max(jnp.concatenate(sums, axis=0), axis=1, keepdims=True)

    bound = jnp.max(largest_norms(query_t) * largest_norms(key_t))
    tame_s[0] = jnp.where(bound <= TAME * TAME, 1, 0)
    key_s[...] = dot(qk_ref[...], weight_ref[:, D : 2 * D]).astype(BF16)
    value = dot(x_ref[...], weight_ref[:, 2 * D : 3 * D]) + vector_ref[9:10, :]
    value_ref[...] = value.astype(BF16)
    value_t = dot(weight_t_s[2 * D :, :], x_t_ref[...]) + bias_s[:, 1:2]
    value_t = value_t.astype(BF16)
    for head in range(HEADS):
        value_s[head, :HEAD_DIM, :] = value_t[head * HEAD_DIM : (head + 1) * HEAD_DIM, :]
        value_s[head, HEAD_DIM:, :] = jnp.ones((16, SEQ), BF16)
    one, two, three = marks[row, 0], marks[row, 1], marks[row, 2]

    def number_of(shape, dim):
        here = (iota(shape, dim) + (HALF + begin)) & (SEQ - 1)
        return (
            jnp.where(here >= one, 1, 0)
            + jnp.where(here >= two, 1, 0)
            + jnp.where(here >= three, 1, 0)
        )

    lane = iota((HALF, LANES), 1)
    number = number_of((HALF, LANES), 0)
    mark_k[...] = jnp.where((number != lane) & (lane < 4), -FAR, 0.0).astype(BF16)
    number = number_of((LANES, HALF), 1)
    mark_q[...] = jnp.where(number == iota((LANES, HALF), 0), 1.0, 0.0).astype(BF16)

    head_of = iota((1, LANES), 1) // HEAD_DIM
    for group in range(2):
        keys_here = key_s[:, group * LANES : (group + 1) * LANES]
        for at_head in range(GROUP):
            mask = jnp.where(head_of == at_head, 1.0, 0.0).astype(BF16)
            rows = slice(at_head * HALF, (at_head + 1) * HALF)
            first_s[group, rows, :] = keys_here[:HALF] * mask
            second_s[group, rows, :LANES] = keys_here[HALF:] * mask
            second_s[group, rows, LANES:] = mark_k[...]

    @pl.when(row > 0)
    def _():
        for group in range(2):
            for half in range(2):
                copy_of(group, half).wait()

    def scores_of(group, half, rows):
        query = query_t_ref[group * LANES : (group + 1) * LANES, half * HALF : (half + 1) * HALF]
        if half == 0:
            return dot(first_s[group, rows, :], query)
        return dot(second_s[group, rows, :], jnp.concatenate([query, mark_q[...]], axis=0))

    def place_of(at_head):
        return slice(at_head * HALF, (at_head + 1) * HALF)

    def exps_plain(group, half):
        scores = scores_of(group, half, slice(0, GROUP * HALF))
        for at_head in range(GROUP):
            exps = jnp.exp2(scores[place_of(at_head), :] * LOG2_E)
            exps_s[group, half, :, place_of(at_head)] = exps.astype(BF16)

    def exps_shifted(group, half):
        for at_head in range(GROUP):
            rows = place_of(at_head)
            largest = jnp.max(scores_of(group, half, rows), axis=0, keepdims=True)
            exps = jnp.exp2((scores_of(group, half, rows) - largest) * LOG2_E)
            exps_s[group, half, :, rows] = exps.astype(BF16)

    def finish(group, half):
        rows = slice(half * HALF, (half + 1) * HALF)
        for at_head in range(GROUP):
            head = group * GROUP + at_head
            out = dot(value_s[head, :, rows], exps_s[group, half, :, place_of(at_head)])
            inverse = 1.0 / out[HEAD_DIM : HEAD_DIM + 1, :]
            inverse_ref[group, at_head : at_head + 1, rows] = inverse
            out_t_ref[head * HEAD_DIM : (head + 1) * HEAD_DIM, rows] = out[:HEAD_DIM, :] * inverse

    def run(exps_of):
        items = [(group, half) for group in range(2) for half in range(2)]
        for i in range(len(items) + 1):
            if i < len(items):
                exps_of(*items[i])
                copy_of(*items[i]).start()
            if i >= 1:
                finish(*items[i - 1])

    @pl.when(tame_s[0] == 1)
    def _():
        run(exps_plain)

    @pl.when(tame_s[0] == 0)
    def _():
        run(exps_shifted)

    out_t = out_t_ref[...]
    mixed_t_ref[...] = out_t.astype(BF16)
    mixed_ref[...] = out_t.T.astype(BF16)

    @pl.when(row == pl.num_programs(0) - 1)
    def _():
        for group in range(2):
            for half in range(2):
                copy_of(group, half).wait()


def attend_forward(marks, place, x, qk, x_t, qk_t, mine, other):
    total = x.shape[0]
    rows = total // SEQ
    by_row = lambda r, m, p: (r, 0)
    by_col = lambda r, m, p: (0, r)
    whole = lambda r, m, p: (0, 0)
    return pl.pallas_call(
        attend_kernel,
        out_shape=(
            jax.ShapeDtypeStruct((D, total), BF16),
            jax.ShapeDtypeStruct((total, D), BF16),
            jax.ShapeDtypeStruct((D, total), BF16),
            jax.ShapeDtypeStruct((D, total), F32),
            jax.ShapeDtypeStruct((2, 8, total), F32),
            jax.ShapeDtypeStruct((total, D), BF16),
            jax.ShapeDtypeStruct((D, total), BF16),
            jax.ShapeDtypeStruct((rows, 2, 2, HALF, GROUP * HALF), BF16),
            jax.ShapeDtypeStruct((D, 3 * D), BF16),
            jax.ShapeDtypeStruct((D, D), BF16),
            jax.ShapeDtypeStruct((VEC, D), F32),
        ),
        grid_spec=pltpu.PrefetchScalarGridSpec(
            num_scalar_prefetch=2,
            grid=(rows,),
            in_specs=[
                pl.BlockSpec((SEQ, D), by_row),
                pl.BlockSpec((SEQ, D), by_row),
                pl.BlockSpec((D, SEQ), by_col),
                pl.BlockSpec((D, SEQ), by_col),
                vspec(),
                vspec(),
            ],
            out_specs=[
                pl.BlockSpec((D, SEQ), by_col),
                pl.BlockSpec((SEQ, D), by_row),
                pl.BlockSpec((D, SEQ), by_col),
                pl.BlockSpec((D, SEQ), by_col),
                pl.BlockSpec((2, 8, SEQ), lambda r, m, p: (0, 0, r)),
                pl.BlockSpec((SEQ, D), by_row),
                pl.BlockSpec((D, SEQ), by_col),
                pl.BlockSpec(memory_space=pl.ANY),
                pl.BlockSpec((D, 3 * D), whole),
                pl.BlockSpec((D, D), whole),
                pl.BlockSpec((VEC, D), whole),
            ],
            scratch_shapes=[
                pltpu.VMEM((SEQ, D), BF16),
                pltpu.VMEM((HEADS, HEAD_DIM + 16, SEQ), BF16),
                pltpu.VMEM((HALF, LANES), BF16),
                pltpu.VMEM((LANES, HALF), BF16),
                pltpu.VMEM((2, GROUP * HALF, LANES), BF16),
                pltpu.VMEM((2, GROUP * HALF, 2 * LANES), BF16),
                pltpu.VMEM((3 * D, D), BF16),
                pltpu.VMEM((D, 8), F32),
                pltpu.SMEM((1,), jnp.int32),
                pltpu.VMEM((2, 2, HALF, GROUP * HALF), BF16),
                pltpu.SemaphoreType.DMA((4,)),
            ],
        ),
        compiler_params=params(dimension_semantics=("arbitrary",)),
        cost_estimate=pl.CostEstimate(
            flops=20_000_000_000, bytes_accessed=30_000_000, transcendentals=8_400_000
        ),
        name="attend_forward",
    )(marks, place, x, qk, x_t, qk_t, mine, other)


def feed_kernel(
    marks,
    place,
    x_ref,
    back_ref,
    mixed_ref,
    mixed_t_ref,
    proj_ref,
    mine_ref,
    other_ref,
    vector_ref,
    block_ref,
    resid_ref,
    mixed_grad_ref,
    mine_out,
    other_out,
    proj_out,
    vector_out,
    first_w,
    second_w,
    first_acc,
    second_acc,
    proj_acc,
    vector_acc,
    hidden_s,
    slope_s,
    pre_s,
    first_low_s,
    branch_low_s,
    attended_s,
    back_s,
    eye_s,
):
    step = pl.program_id(0)
    core = place[2]
    tall = D // VDP
    wide = FF // (2 * VCHIP)

    @pl.when(step == 0)
    def _():
        first_acc[...] = jnp.zeros_like(first_acc)
        second_acc[...] = jnp.zeros_like(second_acc)
        proj_acc[...] = jnp.zeros_like(proj_acc)
        vector_acc[...] = jnp.zeros_like(vector_acc)
        eye_s[...] = jnp.where(iota((D, D), 0) == iota((D, D), 1), 1.0, 0.0).astype(BF16)
        for d in range(VDP):
            rows = slice(d * tall, (d + 1) * tall)
            for c in range(VCHIP):
                for ref, half in ((mine_ref, core), (other_ref, 1 - core)):
                    to = pl.ds(pl.multiple_of((2 * c + half) * wide, wide), wide)
                    first_w[rows, to] = ref[c, d, 0]
                    second_w[rows, to] = ref[c, d, 1]

    bias_o, bias_2 = vector_ref[10:11, :], vector_ref[11:12, :]
    gain_1, shift_1 = vector_ref[12:13, :], vector_ref[13:14, :]
    gain_2, shift_2 = vector_ref[14:15, :], vector_ref[15:16, :]
    turn = (SEQ - marks[step, 3]) & (SEQ - 1)
    back_s[...] = pltpu.roll(back_ref[...].astype(F32), turn, 0)
    chunks = FF // CHUNK
    pair = 2

    def columns(at, count=1):
        return slice(at * CHUNK, (at + count) * CHUNK)

    def hidden_of(rows, at, pre):
        per = CHUNK // D
        bias = [vector_ref[at * per + i : at * per + i + 1, :] for i in range(per)]
        pre = (pre + jnp.concatenate(bias, axis=1)).astype(BF16)
        cube = BF16(GELU_A * GELU_B) * (pre * pre)
        gate = BF16(0.5) + BF16(0.5) * jnp.tanh(pre * (cube + BF16(GELU_A)))
        hidden_s[rows, columns(at)] = pre * gate
        slope_s[rows, columns(at)] = gate + (gate - gate * gate) * (
            pre * (BF16(6.0) * cube + BF16(2.0 * GELU_A))
        )

    def stages(sub):
        rows_at = sub * SUB
        rows = slice(rows_at, rows_at + SUB)
        attended = dot(mixed_ref[rows, :], proj_ref[...]) + bias_o
        norm_1, inverse_1 = norm_forward(x_ref[rows, :].astype(F32) + attended)
        first = norm_1 * gain_1 + shift_1
        first_low = first.astype(BF16)
        first_low_s[rows, :] = first_low
        yield
        branch = jnp.zeros((SUB, D), F32)
        for i in range(chunks + 1):
            if i < chunks:
                hidden_of(rows, i, dot(first_low, first_w[:, columns(i)]))
            if i >= pair and i % pair == 0:
                cols = columns(i - pair, pair)
                branch += dot_nt(hidden_s[rows, cols], second_w[:, cols])
            yield
        norm_2, inverse_2 = norm_forward(first + (branch + bias_2))
        block_ref[rows, :] = norm_2 * gain_2 + shift_2
        back = back_s[rows, :]
        vector_acc[14:15, :] += jnp.sum(back * norm_2, axis=0, keepdims=True)
        vector_acc[15:16, :] += jnp.sum(back, axis=0, keepdims=True)
        resid_2 = norm_backward(back * gain_2, norm_2, inverse_2)
        branch_low = resid_2.astype(BF16)
        branch_low_s[rows, :] = branch_low
        vector_acc[11:12, :] += jnp.sum(branch_low.astype(F32), axis=0, keepdims=True)
        yield
        first_back = resid_2
        if sub == 1:
            branch_t = dot_nt(eye_s[...], branch_low_s[...]).astype(BF16)
            first_t = dot_nt(eye_s[...], first_low_s[...]).astype(BF16)
            first_t = jnp.concatenate([first_t, jnp.ones((16, TILE), BF16)], axis=0)
        for i in range(chunks + 1):
            if i < chunks:
                pull = dot(branch_low, second_w[:, columns(i)]).astype(BF16)
                pre_s[rows, columns(i)] = pull * slope_s[rows, columns(i)]
                if sub == 1:
                    second_acc[:, columns(i)] += dot(branch_t, hidden_s[:, columns(i)])
            if i >= 1 and sub == 1:
                cols = columns(i - 1)
                first_acc[:, cols] += dot(first_t, pre_s[:, cols])
            if i >= pair and i % pair == 0:
                cols = columns(i - pair, pair)
                first_back += dot_nt(pre_s[rows, cols], first_w[:, cols])
            yield
        vector_acc[12:13, :] += jnp.sum(first_back * norm_1, axis=0, keepdims=True)
        vector_acc[13:14, :] += jnp.sum(first_back, axis=0, keepdims=True)
        resid_1 = norm_backward(first_back * gain_1, norm_1, inverse_1)
        resid_ref[rows, :] = resid_1
        attended_low = resid_1.astype(BF16)
        attended_s[rows, :] = attended_low
        vector_acc[10:11, :] += jnp.sum(attended_low.astype(F32), axis=0, keepdims=True)
        mixed_grad_ref[:, rows] = dot_nt(proj_ref[...], attended_low).astype(BF16)
        yield

    ahead, behind = stages(0), stages(1)
    for _ in range(LEAD):
        next(ahead)
    running = [ahead, behind]
    while running:
        for program in list(running):
            if next(program, 0) == 0:
                running.remove(program)
    proj_acc[...] += dot(mixed_t_ref[...], attended_s[...])

    @pl.when(step == pl.num_programs(0) - 1)
    def _():
        for d in range(VDP):
            rows = slice(d * tall, (d + 1) * tall)
            for c in range(VCHIP):
                for ref, half in ((mine_out, core), (other_out, 1 - core)):
                    to = pl.ds(pl.multiple_of((2 * c + half) * wide, wide), wide)
                    ref[d, c, 0] = first_acc[rows, to].astype(BF16)
                    ref[d, c, 1] = second_acc[rows, to].astype(BF16)
        proj_out[...] = proj_acc[...]
        for at in range(FF // D):
            vector_out[at : at + 1, :] = first_acc[D : D + 1, at * D : (at + 1) * D]
        vector_out[FF // D :, :] = vector_acc[FF // D :, :]


def feed_forward(marks, place, x, back, mixed, mixed_t, proj, mine, other, vector):
    total = x.shape[0]
    tile = lambda i, m, p: (i, 0)
    by_col = lambda i, m, p: (0, i)
    whole = lambda i, m, p: (0, 0)
    whole5 = lambda i, m, p: (0, 0, 0, 0, 0)
    return pl.pallas_call(
        feed_kernel,
        out_shape=(
            jax.ShapeDtypeStruct((total, D), F32),
            jax.ShapeDtypeStruct((total, D), F32),
            jax.ShapeDtypeStruct((D, total), BF16),
            jax.ShapeDtypeStruct(mine.shape, BF16),
            jax.ShapeDtypeStruct(mine.shape, BF16),
            jax.ShapeDtypeStruct((D, D), F32),
            jax.ShapeDtypeStruct((VEC, D), F32),
        ),
        grid_spec=pltpu.PrefetchScalarGridSpec(
            num_scalar_prefetch=2,
            grid=(total // TILE,),
            in_specs=[
                pl.BlockSpec((TILE, D), tile),
                pl.BlockSpec((TILE, D), tile),
                pl.BlockSpec((TILE, D), tile),
                pl.BlockSpec((D, TILE), by_col),
                pl.BlockSpec((D, D), whole),
                vspec(),
                vspec(),
                pl.BlockSpec((VEC, D), whole),
            ],
            out_specs=[
                pl.BlockSpec((TILE, D), tile),
                pl.BlockSpec((TILE, D), tile),
                pl.BlockSpec((D, TILE), by_col),
                pl.BlockSpec(mine.shape, whole5),
                pl.BlockSpec(mine.shape, whole5),
                pl.BlockSpec((D, D), whole),
                pl.BlockSpec((VEC, D), whole),
            ],
            scratch_shapes=[
                pltpu.VMEM((D, FF), BF16),
                pltpu.VMEM((D, FF), BF16),
                pltpu.VMEM((D + 16, FF), F32),
                pltpu.VMEM((D, FF), F32),
                pltpu.VMEM((D, D), F32),
                pltpu.VMEM((VEC, D), F32),
                pltpu.VMEM((TILE, FF), BF16),
                pltpu.VMEM((TILE, FF), BF16),
                pltpu.VMEM((TILE, FF), BF16),
                pltpu.VMEM((TILE, D), BF16),
                pltpu.VMEM((TILE, D), BF16),
                pltpu.VMEM((TILE, D), BF16),
                pltpu.VMEM((SEQ, D), F32),
                pltpu.VMEM((D, D), BF16),
            ],
        ),
        compiler_params=params(dimension_semantics=("arbitrary",)),
        cost_estimate=pl.CostEstimate(
            flops=14_000_000_000, bytes_accessed=15_000_000, transcendentals=4_200_000
        ),
        name="feed_forward",
    )(marks, place, x, back, mixed, mixed_t, proj, mine, other, vector)


def pull_kernel(
    marks,
    place,
    grad_t_ref,
    query_t_ref,
    value_ref,
    key_t_ref,
    out_t_ref,
    inverse_ref,
    exps_ref,
    qk_t_ref,
    x_t_ref,
    proj_ref,
    low_ref,
    own_ref,
    other_ref,
    sums_ref,
    dot_s,
    query_g,
    key_g,
    value_g,
    acc,
    sum_acc,
    value_s,
    scaled_t_s,
    score_s,
):
    group = pl.program_id(0)
    row = pl.program_id(1)
    begin = marks[row, 3]

    @pl.when(row == 0)
    def _():
        acc[...] = jnp.zeros_like(acc)
        sum_acc[...] = jnp.zeros_like(sum_acc)

    grad_t = grad_t_ref[...].astype(F32)
    head_of = iota((1, LANES), 1) // HEAD_DIM
    for at_head in range(GROUP):
        heads = slice(at_head * HEAD_DIM, (at_head + 1) * HEAD_DIM)
        part = grad_t[heads, :] * inverse_ref[0, at_head : at_head + 1, :]
        dot_s[at_head : at_head + 1, :] = jnp.sum(part * out_t_ref[heads, :], axis=0, keepdims=True)
        part = part.astype(BF16)
        scaled_t_s[heads, :] = part
        mask = jnp.where(head_of == at_head, 1.0, 0.0).astype(BF16)
        for half in range(2):
            rows = slice(half * HALF, (half + 1) * HALF)
            to = slice(at_head * HALF, (at_head + 1) * HALF)
            value_s[half, to, :] = value_ref[rows, :] * mask

    def score_grads_of(half, block):
        at = half * HALF + block * QBLOCK
        pulls = dot(value_s[half], scaled_t_s[:, at : at + QBLOCK])
        for at_head in range(GROUP):
            cols = slice(at_head * HALF + block * QBLOCK, at_head * HALF + (block + 1) * QBLOCK)
            pull = pulls[at_head * HALF : (at_head + 1) * HALF, :]
            pull = (pull - dot_s[at_head : at_head + 1, at : at + QBLOCK]).astype(BF16)
            score_s[half, :, cols] = exps_ref[0, 0, half, :, cols] * pull

    def finish(half, at_head):
        cols = slice(at_head * HALF, (at_head + 1) * HALF)
        rows = slice(half * HALF, (half + 1) * HALF)
        heads = slice(at_head * HEAD_DIM, (at_head + 1) * HEAD_DIM)
        score_grad = score_s[half, :, cols]
        value_g[heads, rows] = dot_nt(scaled_t_s[heads, rows], exps_ref[0, 0, half, :, cols])
        query_g[heads, rows] = dot(key_t_ref[heads, rows], score_grad)
        key_g[heads, rows] = dot_nt(query_t_ref[heads, rows], score_grad)

    blocks = HALF // QBLOCK
    each = GROUP // blocks
    for block in range(blocks):
        score_grads_of(0, block)
    for block in range(blocks):
        score_grads_of(1, block)
        for at_head in range(each * block, each * (block + 1)):
            finish(0, at_head)
    for at_head in range(GROUP):
        finish(1, at_head)
    query_low = query_g[...].astype(BF16)
    both_low = jnp.concatenate([key_g[...].astype(BF16), value_g[...].astype(BF16)], axis=0)
    ones = jnp.ones((16, SEQ), BF16)
    sum_acc[0:1, :] += dot_nt(ones, query_low)[0:1, :] * SCALE
    sum_acc[1:2, :] += dot_nt(ones, both_low[LANES:, :])[0:1, :]
    qk_t = qk_t_ref[...]
    both = dot_nt(qk_t, jnp.concatenate([query_low, both_low[:LANES, :]], axis=0))
    acc[:, :LANES] += both[:, :LANES] * SCALE
    acc[:, LANES : 2 * LANES] += both[:, LANES:]
    acc[:, 2 * LANES :] += dot_nt(x_t_ref[...], both_low[LANES:, :])
    low_ref[0, :LANES, :] = query_low
    low_ref[0, LANES:, :] = both_low

    def write(ref):
        tall = D // VDP
        for d in range(VDP):
            rows = slice(d * tall, (d + 1) * tall)
            for c in range(3):
                ref[d, c] = acc[rows, c * LANES : (c + 1) * LANES].astype(BF16)
            ref[d, 3] = proj_ref[rows, :].astype(BF16)

    last = row == pl.num_programs(1) - 1

    @pl.when(last & (group == place[2]))
    def _():
        write(own_ref)

    @pl.when(last & (group != place[2]))
    def _():
        write(other_ref)

    @pl.when(last)
    def _():
        sums_ref[pl.ds(group, 1)] = sum_acc[...][None]


def attend_back(marks, place, grad_t, query_t, value, key_t, out_t, inverse, exps, qk_t, x_t, proj):
    total = value.shape[0]
    rows = total // SEQ
    by_both = lambda g, r, m, p: (g, r)
    by_col = lambda g, r, m, p: (0, r)
    grads = jax.ShapeDtypeStruct((VDP, VCHIP, D // VDP, LANES), BF16)
    grads_spec = pl.BlockSpec(grads.shape, lambda g, r, m, p: (0, 0, 0, 0))
    return pl.pallas_call(
        pull_kernel,
        out_shape=(
            jax.ShapeDtypeStruct((2, 3 * LANES, total), BF16),
            grads,
            grads,
            jax.ShapeDtypeStruct((2, 8, LANES), F32),
        ),
        grid_spec=pltpu.PrefetchScalarGridSpec(
            num_scalar_prefetch=2,
            grid=(2, rows),
            in_specs=[
                pl.BlockSpec((LANES, SEQ), by_both),
                pl.BlockSpec((LANES, SEQ), by_both),
                pl.BlockSpec((SEQ, LANES), lambda g, r, m, p: (r, g)),
                pl.BlockSpec((LANES, SEQ), by_both),
                pl.BlockSpec((LANES, SEQ), by_both),
                pl.BlockSpec((1, 8, SEQ), lambda g, r, m, p: (g, 0, r)),
                pl.BlockSpec((1, 1, 2, HALF, GROUP * HALF), lambda g, r, m, p: (r, g, 0, 0, 0)),
                pl.BlockSpec((D, SEQ), by_col),
                pl.BlockSpec((D, SEQ), by_col),
                pl.BlockSpec((D, LANES), lambda g, r, m, p: (0, g)),
            ],
            out_specs=[
                pl.BlockSpec((1, 3 * LANES, SEQ), lambda g, r, m, p: (g, 0, r)),
                grads_spec,
                grads_spec,
                pl.BlockSpec((2, 8, LANES), lambda g, r, m, p: (0, 0, 0)),
            ],
            scratch_shapes=[
                pltpu.VMEM((8, SEQ), F32),
                pltpu.VMEM((LANES, SEQ), F32),
                pltpu.VMEM((LANES, SEQ), F32),
                pltpu.VMEM((LANES, SEQ), F32),
                pltpu.VMEM((D, 3 * LANES), F32),
                pltpu.VMEM((8, LANES), F32),
                pltpu.VMEM((2, GROUP * HALF, LANES), BF16),
                pltpu.VMEM((LANES, SEQ), BF16),
                pltpu.VMEM((2, HALF, GROUP * HALF), BF16),
            ],
        ),
        compiler_params=params(dimension_semantics=("arbitrary", "arbitrary")),
        cost_estimate=pl.CostEstimate(
            flops=36_000_000_000, bytes_accessed=30_000_000, transcendentals=0
        ),
        name="attend_back",
    )(marks, place, grad_t, query_t, value, key_t, out_t, inverse, exps, qk_t, x_t, proj)


def input_kernel(
    marks, low_ref, weight_ref, resid_ref, turned_ref, earlier_ref, block_ref, input_ref, token_ref
):
    token_ref[...] = jnp.zeros_like(token_ref)
    at = slice(0, LANES), slice(LANES, 2 * LANES), slice(2 * LANES, 3 * LANES)
    parts = [jnp.concatenate([low_ref[0, rows, :], low_ref[1, rows, :]], axis=0) for rows in at]
    pulled = dot(weight_ref[:, :D], parts[0]) * SCALE + (
        dot(weight_ref[:, D : 2 * D], parts[1]) + dot(weight_ref[:, 2 * D :], parts[2])
    )
    begin = marks[pl.program_id(0), 3]
    input_ref[...] = pltpu.roll(resid_ref[...] + pulled.T, begin, 0)
    block_ref[...] = pltpu.roll(turned_ref[...], begin, 0)


def input_pull(marks, low, weight, resid, turned, earlier):
    total = resid.shape[0]
    by_row = pl.BlockSpec((SEQ, D), lambda r, m: (r, 0))
    return pl.pallas_call(
        input_kernel,
        out_shape=(
            jax.ShapeDtypeStruct((total, D), F32),
            jax.ShapeDtypeStruct((total, D), F32),
            jax.ShapeDtypeStruct((8, LANES), F32),
        ),
        grid_spec=pltpu.PrefetchScalarGridSpec(
            num_scalar_prefetch=1,
            grid=(total // SEQ,),
            in_specs=[
                pl.BlockSpec((2, 3 * LANES, SEQ), lambda r, m: (0, 0, r)),
                pl.BlockSpec((D, 3 * D), lambda r, m: (0, 0)),
                by_row,
                by_row,
                pl.BlockSpec(memory_space=pl.ANY),
            ],
            out_specs=[by_row, by_row, pl.BlockSpec((8, LANES), lambda r, m: (0, 0))],
        ),
        compiler_params=params(dimension_semantics=("arbitrary",)),
        cost_estimate=pl.CostEstimate(
            flops=1_000_000_000, bytes_accessed=8_000_000, transcendentals=0
        ),
        name="input_pull",
    )(marks, low, weight, resid, turned, earlier)


def two_terms(rows):
    high = rows.astype(BF16)
    return jnp.concatenate([high.astype(F32), rows - high.astype(F32)], axis=0)


def column_to_row(columns, rows):
    lane = iota((rows, LANES), 1)
    wide = jnp.zeros((rows, LANES), F32)
    for i, column in enumerate(columns):
        wide = jnp.where(lane == i, column, wide)
    return wide.T[:8, :]


def total_of(array):
    return jnp.sum(jnp.sum(array, axis=0, keepdims=True), axis=1, keepdims=True)


def tail_ffn_kernel(place, ffn_ref, rows_1, rows_2, last_ref, grad_1, grad_2, grad_ref, stat_ref):
    lane = iota((1, LANES), 1)
    piece, across = [], []
    for kind in range(2):
        total = ffn_ref[0, kind].astype(F32)
        for at in range(1, VDP * VCHIP):
            total = total + ffn_ref[at, kind].astype(F32)
        (grad_1, grad_2)[kind][...] = total
        grad_ref[kind] = total
        square = total * total + EPS_ONE
        down = jnp.sum(square, axis=0, keepdims=True)
        piece += [down[:, :LANES], down[:, LANES:]]
        across.append(jnp.sum(square, axis=1, keepdims=True))
    across = column_to_row(across, total.shape[0])
    across = jnp.concatenate([across[0:1], across[1:2]], axis=1)
    olds = jnp.zeros((1, LANES), F32)
    for i, ref in enumerate((rows_1, rows_2)):
        olds = jnp.where(lane == i, jnp.sum(ref[...], axis=1, keepdims=True), olds)
    stat_ref[...] = jnp.concatenate([across] + piece + [olds, jnp.zeros((2, LANES), F32)], axis=0)


def tail_send_kernel(
    place, mine_ref, got_ref, vector_ref, sums_ref, stat_ref, stat_other_ref, send_ref
):
    tall = D // VDP
    low, high = sums_ref[0], sums_ref[1]
    vector = jnp.concatenate(
        [
            vector_ref[:8, :],
            jnp.concatenate([low[:2], high[:2]], axis=1),
            vector_ref[10:, :],
        ],
        axis=0,
    )
    stat = jnp.concatenate([stat_ref[0:1, :] + stat_other_ref[0:1, :], stat_ref[1:6, :]], axis=0)
    stat = two_terms(stat)
    rows = VEC // VDP
    for d in range(VDP):
        for c in range(VCHIP):
            at = d * VCHIP + c
            both = mine_ref[d, c].astype(F32) + got_ref[d, c].astype(F32)
            send_ref[at, :tall, :] = both.astype(BF16)
            part = vector[d * rows : (d + 1) * rows, c * 64 : (c + 1) * 64]
            part = jnp.concatenate([part, jnp.zeros((rows, LANES - 64), F32)], axis=1)
            send_ref[at, tall:, :] = jnp.concatenate([part, stat], axis=0).astype(BF16)


def tail_reduce_kernel(
    place,
    earlier_ref,
    got_ref,
    ffn_grad_ref,
    attn_ref,
    first_ref,
    second_ref,
    rows_0,
    rows_1,
    rows_2,
    cols_0,
    cols_1,
    cols_2,
    vector_ref,
    moment_ref,
    grad_ref,
    update_1,
    update_2,
    rows_out_1,
    rows_out_2,
    cols_out_1,
    cols_out_2,
    send_ref,
):
    decay = 1.0 - STEP ** (-0.8)
    chip = place[1]
    dp = place[0]
    tall = attn_ref.shape[0]
    rows, width = vector_ref.shape
    pieces = VDP * VCHIP
    lane = iota((1, LANES), 1)
    total = got_ref[0, :tall, :].astype(F32)
    part = got_ref[0, tall:, :].astype(F32)[:rows]
    for at in range(1, pieces):
        total = total + got_ref[at, :tall, :].astype(F32)
        part = part + got_ref[at, tall:, :].astype(F32)[:rows]
    grad_ref[...] = total
    low = total.astype(BF16)

    def stat_of(at):
        both = got_ref[pl.ds(at, 1), tall:, :][0].astype(F32)[rows:]
        return both[:6] + both[6:12]

    every = jnp.zeros((1, LANES), F32)
    olds = jnp.zeros((1, LANES), F32)
    mine = jnp.zeros((1, LANES), F32)
    down = jnp.zeros((6, LANES), F32)
    for d in range(VDP):
        down = down + stat_of(d * VCHIP + chip)
        for c in range(VCHIP):
            stat = stat_of(d * VCHIP + c)
            every = every + stat[0:1]
            if c == 0:
                olds = olds + stat[5:6]
    for c in range(VCHIP):
        mine = mine + stat_of(dp * VCHIP + c)[0:1]
    row_total = tall * VDP
    new_rows, means = [], []
    for i, ref in enumerate((rows_1, rows_2)):
        count = first_ref.shape[1] * 2 * VCHIP
        new_rows.append(decay * ref[...] + (1.0 - decay) * (mine[:, i * tall : (i + 1) * tall] / count))
        old = jnp.sum(jnp.where(lane == i, olds, 0.0), axis=1, keepdims=True)
        fresh = jnp.sum(every[:, i * tall : (i + 1) * tall], axis=1, keepdims=True)
        means.append((decay * old + (1.0 - decay) * (fresh / count)) / row_total)
    tile = jnp.concatenate(new_rows + [jnp.zeros((6, tall), F32)], axis=0)
    rows_out_1[...] = new_rows[0]
    rows_out_2[...] = new_rows[1]
    tile = jnp.concatenate([tile, jnp.zeros((8, LANES - tall), F32)], axis=1)
    turned = jnp.concatenate([tile, jnp.zeros((LANES - 8, LANES), F32)], axis=0).T
    scalars = jnp.zeros((1, LANES), F32)
    for i, (old_ref, out_ref, to) in enumerate(
        ((cols_1, cols_out_1, update_1), (cols_2, cols_out_2, update_2))
    ):
        sums = jnp.concatenate([down[1 + 2 * i : 2 + 2 * i], down[2 + 2 * i : 3 + 2 * i]], axis=1)
        cols = decay * old_ref[...] + (1.0 - decay) * (sums / row_total)
        out_ref[...] = cols
        grad = ffn_grad_ref[i]
        update = grad * lax.rsqrt(turned[:tall, i : i + 1] * cols / means[i])
        to[...] = update
        scalars = jnp.where(lane == 67 + i, total_of(update * update), scalars)
    for i, ref in enumerate((attn_ref, first_ref, second_ref)):
        weight = ref[...]
        scalars = jnp.where(lane == 64 + i, total_of(weight * weight), scalars)
    scalars = jnp.concatenate([rows_0[...], scalars[:, tall:]], axis=1)
    vector = vector_ref[...]
    power = jnp.sum(vector * vector, axis=1, keepdims=True)
    lines = jnp.concatenate(
        [part[:, :64], moment_ref[...], jnp.broadcast_to(power, (rows, LANES - 64 - width))], axis=1
    )
    piece = jnp.concatenate(
        [two_terms(lines), two_terms(jnp.concatenate([cols_0[...], scalars], axis=0))]
        + [jnp.zeros((4, LANES), F32)],
        axis=0,
    ).astype(BF16)
    for at in range(pieces):
        send_ref[at, :tall, :] = low
        send_ref[at, tall:, :] = piece


def tail_apply_kernel(
    place,
    mine_ref,
    other_ref,
    grad_ref,
    update_1,
    update_2,
    weight_0,
    weight_1,
    weight_2,
    rows_0,
    cols_0,
    vector_ref,
    moment_ref,
    new_0,
    new_1,
    new_2,
    rows_out,
    cols_out,
    vector_grad_ref,
    moment_out,
    vector_out,
    sums_s,
    rows_s,
):
    decay = 1.0 - STEP ** (-0.8)
    dp, chip, core = place[0], place[1], place[2]
    tall = weight_0.shape[0]
    rows, width = vector_ref.shape
    fsdp = 2 * VCHIP
    lane = iota((1, LANES), 1)
    refs = (mine_ref, other_ref)
    row_total = float(tall * VDP)
    col_total = float(LANES * fsdp)

    def lines_of(ref, at):
        both = ref[at, tall:, :].astype(F32)
        return both[0:4] + both[4:8], both[8:10] + both[10:12]

    scalars = jnp.zeros((1, LANES), F32)
    for ref in refs:
        for at in range(VDP * VCHIP):
            scalars = scalars + lines_of(ref, at)[1][1:2]
    scalar = lambda at: jnp.sum(jnp.where(lane == at, scalars, 0.0), axis=1, keepdims=True)

    tile, fresh = [], []
    for d in range(VDP):
        wide = jnp.zeros((tall, LANES), F32)
        for ref in refs:
            for c in range(VCHIP):
                block = ref[d * VCHIP + c, :tall, :].astype(F32)
                wide = wide + (block * block + EPS_ONE)
        fresh.append(jnp.sum(wide, axis=1, keepdims=True))
        tile.append(lines_of(mine_ref, d * VCHIP)[1][1:2])
    tile = jnp.concatenate(tile + [jnp.zeros((LANES - VDP, LANES), F32)], axis=0).T
    mean = jnp.zeros((1, 1), F32)
    new_rows = []
    for d in range(VDP):
        new = decay * tile[:tall, d : d + 1] + (1.0 - decay) * (fresh[d] / col_total)
        new_rows.append(1.0 / new)
        mean = mean + jnp.sum(new, axis=0, keepdims=True)
        sums_s[d] = jnp.broadcast_to(fresh[d], (tall, LANES))
    mean = mean / row_total
    mine = sums_s[pl.ds(dp, 1)][0]
    rows_s[...] = mine.T
    rows_new = decay * rows_0[...] + (1.0 - decay) * (rows_s[0:1, :tall] / col_total)
    rows_out[...] = rows_new
    power = jnp.zeros((1, 1), F32)
    for half, ref in enumerate(refs):
        for c in range(VCHIP):
            down = jnp.zeros((tall, LANES), F32)
            weighted = jnp.zeros((tall, LANES), F32)
            for d in range(VDP):
                block = ref[d * VCHIP + c, :tall, :].astype(F32)
                square = block * block
                down = down + (square + EPS_ONE)
                weighted = weighted + square * new_rows[d]
            down = jnp.sum(down, axis=0, keepdims=True)
            old = lines_of(ref, c)[1][0:1]
            cols = decay * old + (1.0 - decay) * (down / row_total)
            weighted = jnp.sum(weighted, axis=0, keepdims=True) / cols
            power = power + jnp.sum(weighted, axis=1, keepdims=True)
            if half == 0:
                sums_s[VDP + c] = jnp.broadcast_to(down, (tall, LANES))
    power = power * mean
    down = sums_s[pl.ds(VDP + chip, 1)][0][0:1, :]
    cols_new = decay * cols_0[...] + (1.0 - decay) * (down / row_total)
    cols_out[...] = cols_new
    column = jnp.concatenate(
        [
            jnp.concatenate([rows_new, jnp.zeros((1, LANES - tall), F32)], axis=1),
            jnp.zeros((LANES - 1, LANES), F32),
        ],
        axis=0,
    ).T[:tall, 0:1]
    update_0 = grad_ref[...] * lax.rsqrt(column * cols_new / mean)
    powers = (power, scalar(67), scalar(68))
    for i, (update, weight, new) in enumerate(
        (
            (update_0, weight_0, new_0),
            (update_1[...], weight_1, new_1),
            (update_2[...], weight_2, new_2),
        )
    ):
        entries = float(weight.shape[0] * weight.shape[1] * VDP * fsdp)
        clip = jnp.maximum(1.0, jnp.sqrt(powers[i] / entries) / CLIP_LIMIT)
        rate = STEP_RATE * jnp.maximum(EPS_TWO, jnp.sqrt(scalar(64 + i) / entries))
        new[...] = weight[...] - rate / clip * update
    powers, sizes = [], []
    for d in range(VDP):
        power = jnp.zeros((rows, 1), F32)
        size = jnp.zeros((rows, 1), F32)
        for c in range(VCHIP):
            at = d * VCHIP + c
            first, second = lines_of(mine_ref, at)[0], lines_of(other_ref, at)[0]
            both = first[:, :64] + second[:, :64]
            size = size + first[:, LANES - 1 :] + second[:, LANES - 1 :]
            near = jnp.where(core == 0, first[:, 64 : 64 + width], second[:, 64 : 64 + width])
            far = jnp.where(core == 0, second[:, 64 : 64 + width], first[:, 64 : 64 + width])
            moment = jnp.concatenate([near, far], axis=1)
            moment = decay * moment + (1.0 - decay) * (both * both + EPS_ONE)
            power = power + jnp.sum(both * both / moment, axis=1, keepdims=True)
            wide = jnp.concatenate([both, jnp.zeros((rows, LANES - 64), F32)], axis=1)
            sums_s[2 * VDP + at, :rows, :] = wide
        powers.append(power)
        sizes.append(size)
    both = sums_s[pl.ds(2 * VDP + dp * VCHIP + chip, 1), :rows, :][0]
    vector_grad = jnp.where(core == 0, both[:, :width], both[:, width : 2 * width])
    vector_grad_ref[...] = vector_grad
    moment = decay * moment_ref[...] + (1.0 - decay) * (vector_grad * vector_grad + EPS_ONE)
    moment_out[...] = moment
    step = vector_grad * lax.rsqrt(moment)
    bias = VDP // 2
    bias_power = sum(jnp.sum(power, axis=0, keepdims=True) for power in powers[:bias])
    bias_size = sum(jnp.sum(size, axis=0, keepdims=True) for size in sizes[:bias])
    power, size = powers[bias], sizes[bias]
    for d in range(bias + 1, VDP):
        power = jnp.where(dp == d, powers[d], power)
        size = jnp.where(dp == d, sizes[d], size)
    is_bias = dp < bias
    power = jnp.where(is_bias, bias_power, power)
    size = jnp.where(is_bias, bias_size, size)
    count = jnp.where(is_bias, float(FF), float(D))
    clip = jnp.maximum(1.0, jnp.sqrt(power / count) / CLIP_LIMIT)
    rate = STEP_RATE * jnp.maximum(EPS_TWO, jnp.sqrt(size / count))
    vector_out[...] = vector_ref[...] - rate / clip * step


def whole_call(kernel, name, place, outs, *operands, scratch=(), earlier=None):
    tied = () if earlier is None else (earlier,)
    return pl.pallas_call(
        kernel,
        out_shape=[jax.ShapeDtypeStruct(shape, kind) for shape, kind in outs],
        in_specs=[pl.BlockSpec(memory_space=pltpu.SMEM)]
        + [pl.BlockSpec(memory_space=pl.ANY)] * len(tied)
        + [vspec()] * len(operands),
        out_specs=[vspec()] * len(outs),
        scratch_shapes=list(scratch),
        compiler_params=params(16),
        name=name,
    )(place, *tied, *operands)


def core_swap(block):
    return lax.ppermute(block, "core", [(0, 1), (1, 0)])


def exchange(blocks, axes):
    return lax.all_to_all(blocks, axes, split_axis=0, concat_axis=0, tiled=True)


def after(value, *earlier, mib=8):
    return pl.pallas_call(
        lambda *refs: None,
        out_shape=jax.ShapeDtypeStruct(value.shape, value.dtype),
        in_specs=[pl.BlockSpec(memory_space=pltpu.HBM)] * (1 + len(earlier)),
        out_specs=pl.BlockSpec(memory_space=pltpu.HBM),
        input_output_aliases={0: 0},
        compiler_params=params(mib),
        name="after",
    )(value, *earlier)


def pair_kernel(mine_ref, got_ref, out_ref):
    out_ref[...] = (mine_ref[...].astype(F32) + got_ref[...].astype(F32)).astype(BF16)


def pair_sum(mine, got):
    return pl.pallas_call(
        pair_kernel,
        out_shape=jax.ShapeDtypeStruct(mine.shape, BF16),
        in_specs=[vspec(), vspec()],
        out_specs=vspec(),
        compiler_params=params(16),
        name="pair_sum",
    )(mine, got)


CHIPS = ("dp", "chip")
ALL = ("dp", "chip", "core")


def layer(place, weights, segment_ids, tokens, cotangent, ffn_weights, send_core, send_ffn):
    table = jnp.asarray(encode_table())
    qk, x, qk_t, x_t, marks = place_tokens(segment_ids, tokens, table)
    query_t, value, key_t, out_t, inverse, mixed, mixed_t, exps, weight, proj, vector = attend_forward(
        marks, place, x, qk, x_t, qk_t, *weights(marks)
    )
    ffn_mine, ffn_other = ffn_weights(marks, vector)
    block_out, resid, grad_t, ffn_mine, ffn_other, proj_g, vector_g = feed_forward(
        marks, place, x, cotangent, mixed, mixed_t, proj, ffn_mine, ffn_other, vector
    )
    ffn_got, grad_t = send_ffn(ffn_mine, ffn_other, grad_t)
    low, grads_own, grads_other, sums = attend_back(
        marks, place, grad_t, query_t, value, key_t, out_t, inverse, exps, qk_t, x_t, proj_g
    )
    attn_got = send_core(grads_other)
    pull = lambda earlier: input_pull(marks, low, weight, resid, block_out, earlier)
    return pull, grads_own, grads_other, attn_got, sums, vector_g, ffn_got


def body(
    tokens,
    cotangent,
    segment_ids,
    attn_weight,
    ffn_in,
    ffn_out,
    vectors,
    attn_rows,
    attn_cols,
    in_rows,
    in_cols,
    out_rows,
    out_cols,
    vector_moment,
):
    place = jnp.stack([lax.axis_index("dp"), lax.axis_index("chip"), lax.axis_index("core")])
    place = place.astype(jnp.int32)
    pieces = VDP * VCHIP
    tall, wide = attn_weight.shape
    rows_v, cols_v = vectors.shape
    split = lambda array: array.reshape((VDP, VCHIP) + array.shape[1:])
    attn_sent, ffn_low = pack_attn(place, attn_weight, ffn_in, ffn_out, vectors)
    attn_mine = exchange(attn_sent, CHIPS)

    parts = [
        lax.ppermute(ffn_low, "dp", [(i, i ^ step) for i in range(VDP)]) for step in range(1, VDP)
    ]
    ffn_sent = pack_ffn(place, ffn_low, parts)

    def attn_weights(marks):
        mine = split(after(attn_mine, marks, ffn_sent))
        return mine, core_swap(mine)

    def ffn_weights(marks, vector):
        got = exchange(after(ffn_sent, marks), "chip")
        ffn_mine = after(got, vector)
        return ffn_mine, core_swap(ffn_mine)

    def send_ffn(mine, other, grad_t):
        both = pair_sum(mine, core_swap(other))
        got = exchange(both.reshape((pieces,) + mine.shape[2:]), CHIPS)
        return got, after(grad_t, both, mib=56)

    (
        pull,
        grads_own,
        grads_other,
        attn_got,
        sums,
        vector_g,
        ffn_got,
    ) = layer(place, attn_weights, segment_ids, tokens, cotangent, ffn_weights, core_swap, send_ffn)
    lay = lambda stat: stat.reshape(1, -1)
    rows_old = (lay(attn_rows), lay(in_rows), lay(out_rows))
    cols_old = (lay(attn_cols), lay(in_cols), lay(out_cols))
    weights_old = (attn_weight, ffn_in, ffn_out)
    in_grad, out_grad, ffn_grad, stat = whole_call(
        tail_ffn_kernel,
        "tail_ffn",
        place,
        [(ffn_in.shape, F32), (ffn_out.shape, F32), ((2,) + ffn_in.shape, F32), ((8, LANES), F32)],
        ffn_got,
        *rows_old[1:],
        sums,
    )
    stat_other = core_swap(stat)
    (sent,) = whole_call(
        tail_send_kernel,
        "tail_send",
        place,
        [((pieces, tall + VROWS, LANES), BF16)],
        grads_own,
        attn_got,
        vector_g,
        sums,
        stat,
        stat_other,
    )
    block_out, input_grad, token = pull(sent)
    got = exchange(sent, CHIPS)
    attn_grad, update_1, update_2, rows_new_1, rows_new_2, cols_new_1, cols_new_2, sent = whole_call(
        tail_reduce_kernel,
        "tail_reduce",
        place,
        [
            (attn_weight.shape, F32),
            (ffn_in.shape, F32),
            (ffn_out.shape, F32),
            (rows_old[1].shape, F32),
            (rows_old[2].shape, F32),
            (cols_old[1].shape, F32),
            (cols_old[2].shape, F32),
            ((pieces, tall + VROWS, LANES), BF16),
        ],
        got,
        ffn_grad,
        *weights_old,
        *rows_old,
        *cols_old,
        vectors,
        vector_moment,
        earlier=token,
    )
    mine = exchange(sent, CHIPS)
    attn_new, in_new, out_new, rows_new_0, cols_new_0, vector_grad, moment_new, vectors_new = whole_call(
        tail_apply_kernel,
        "tail_apply",
        place,
        [
            (attn_weight.shape, F32),
            (ffn_in.shape, F32),
            (ffn_out.shape, F32),
            (rows_old[0].shape, F32),
            (cols_old[0].shape, F32),
            (vectors.shape, F32),
            (vectors.shape, F32),
            (vectors.shape, F32),
        ],
        mine,
        core_swap(mine),
        attn_grad,
        update_1,
        update_2,
        *weights_old,
        rows_old[0],
        cols_old[0],
        vectors,
        vector_moment,
        scratch=[
            pltpu.VMEM((2 * VDP + pieces, tall, LANES), F32),
            pltpu.VMEM((LANES, tall), F32),
        ],
    )
    return (
        block_out,
        input_grad,
        attn_grad,
        in_grad,
        out_grad,
        vector_grad,
        rows_new_0.reshape(-1),
        cols_new_0.reshape(-1),
        rows_new_1.reshape(-1),
        cols_new_1.reshape(-1),
        rows_new_2.reshape(-1),
        cols_new_2.reshape(-1),
        moment_new,
        attn_new,
        in_new,
        out_new,
        vectors_new,
    )


def gather_all(block):
    shape = (lax.axis_size("dp"), lax.axis_size("chip") * 2)
    count = shape[0] * shape[1]
    got = exchange(jnp.broadcast_to(block[None], (count,) + block.shape), ALL)
    return got.reshape(shape + block.shape)


def unblock(parts):
    dp_count, fsdp_count, rows, cols = parts.shape
    return parts.transpose(0, 2, 1, 3).reshape(dp_count * rows, fsdp_count * cols)


def scatter_sum(full):
    dp_count = lax.axis_size("dp")
    fsdp_count = lax.axis_size("chip") * 2
    rows, cols = full.shape
    by_col = full.astype(BF16).reshape(rows, fsdp_count, cols // fsdp_count).transpose(1, 0, 2)
    got = exchange(by_col, ("chip", "core"))
    part = jnp.sum(got.astype(F32), axis=0).astype(BF16)
    by_row = part.reshape(dp_count, rows // dp_count, cols // fsdp_count)
    return jnp.sum(exchange(by_row, "dp").astype(F32), axis=0)


def body_any(
    tokens,
    cotangent,
    segment_ids,
    attn_weight,
    ffn_in,
    ffn_out,
    vectors,
    attn_rows,
    attn_cols,
    in_rows,
    in_cols,
    out_rows,
    out_cols,
    vector_moment,
):
    dp_count = lax.axis_size("dp")
    fsdp_count = lax.axis_size("chip") * 2
    dp_place = lax.axis_index("dp")
    fsdp_place = lax.axis_index("chip") * 2 + lax.axis_index("core")
    rows_w = attn_weight.shape[0]
    rows_v = vectors.shape[0]
    place = jnp.zeros((3,), jnp.int32)
    full_attn = unblock(gather_all(attn_weight.astype(BF16)))
    full_vector = unblock(gather_all(vectors.astype(BF16)))
    full_ffn = jnp.stack(
        [unblock(gather_all(ffn_in.astype(BF16))), unblock(gather_all(ffn_out.astype(BF16)))]
    )
    tall = D // VDP
    cut = full_attn.reshape(VDP, tall, VCHIP, 2, LANES).transpose(3, 0, 2, 1, 4)
    lines = full_vector.reshape(VDP, VEC // VDP, 2, LANES).transpose(0, 2, 1, 3)
    lines = lines.reshape(VDP, 1, 2 * VEC // VDP, LANES)
    lines = jnp.pad(lines, ((0, 0), (0, VCHIP - 1), (0, VROWS - 2 * VEC // VDP), (0, 0)))
    weights = (
        jnp.concatenate([cut[0], lines], axis=2),
        jnp.concatenate([cut[1], jnp.zeros_like(lines)], axis=2),
    )
    ffn_cut = full_ffn.reshape(2, VDP, tall, VCHIP, 2, FF // (2 * VCHIP))
    ffn_cut = ffn_cut.transpose(4, 3, 1, 0, 2, 5)
    (
        pull,
        grads_own,
        grads_other,
        _,
        sums,
        vector_g,
        ffn_got,
    ) = layer(
        place,
        lambda marks: weights,
        segment_ids,
        tokens,
        cotangent,
        lambda marks, vector: (ffn_cut[0], ffn_cut[1]),
        lambda block: block,
        lambda mine, other, grad_t: (jnp.stack([mine, other]), grad_t),
    )
    block_out, input_grad, _ = pull(sums)
    attn_full = jnp.stack([grads_own, grads_other]).transpose(1, 3, 2, 0, 4).reshape(D, 4 * D)
    ffn_full = ffn_got.transpose(3, 1, 4, 2, 0, 5).reshape(2, D, FF)
    sums = jnp.concatenate([sums[0, :2], sums[1, :2]], axis=1)
    vector_full = jnp.concatenate([vector_g[:8], sums, vector_g[10:]], axis=0)
    attn_grad = scatter_sum(attn_full)
    in_grad = scatter_sum(ffn_full[0])
    out_grad = scatter_sum(ffn_full[1])
    vector_grad = scatter_sum(vector_full)

    decay = 1.0 - STEP ** (-0.8)
    gradients = (attn_grad, in_grad, out_grad)
    weights_old = (attn_weight, ffn_in, ffn_out)
    rows_old = (attn_rows, in_rows, out_rows)
    cols_old = (attn_cols, in_cols, out_cols)
    moment_new = decay * vector_moment + (1.0 - decay) * (vector_grad * vector_grad + EPS_ONE)
    vector_step = vector_grad * lax.rsqrt(moment_new)
    squares = [gradient * gradient + EPS_ONE for gradient in gradients]
    pieces = []
    for square in squares:
        pieces.append(jnp.sum(square, axis=1))
    for square in squares:
        pieces.append(jnp.sum(square, axis=0))
    pieces.append(jnp.sum(vector_step * vector_step, axis=1))
    pieces.append(jnp.sum(vectors * vectors, axis=1))
    pieces.append(jnp.stack([jnp.sum(weight * weight) for weight in weights_old]))
    pieces.append(jnp.stack([jnp.sum(old) for old in rows_old]))
    sizes = [piece.shape[0] for piece in pieces]
    flat = jnp.concatenate(pieces)
    flat = jnp.pad(flat, (0, -flat.shape[0] % 1024)).reshape(-1, LANES)
    got = gather_all(flat).reshape(dp_count, fsdp_count, -1)
    offsets = [0]
    for length in sizes:
        offsets.append(offsets[-1] + length)
    take = lambda i: got[:, :, offsets[i] : offsets[i + 1]]
    rows_new, cols_new, row_means, entries = [], [], [], []
    for i in range(3):
        count_rows = rows_w * dp_count
        count_cols = weights_old[i].shape[1] * fsdp_count
        entries.append(float(count_rows * count_cols))
        row_all = jnp.sum(take(i), axis=1)
        mine = lax.dynamic_index_in_dim(row_all, dp_place, 0, keepdims=False)
        rows_new.append(decay * rows_old[i] + (1.0 - decay) * mine / count_cols)
        col_all = jnp.sum(take(3 + i), axis=0)
        mine = lax.dynamic_index_in_dim(col_all, fsdp_place, 0, keepdims=False)
        cols_new.append(decay * cols_old[i] + (1.0 - decay) * mine / count_rows)
        old_total = jnp.sum(take(9)[:, 0, i])
        row_means.append(
            (decay * old_total + (1.0 - decay) * jnp.sum(row_all) / count_cols) / count_rows
        )
    step_rows = jnp.sum(take(6), axis=1).reshape(-1)
    weight_rows = jnp.sum(take(7), axis=1).reshape(-1)
    weight_totals = jnp.sum(take(8), axis=(0, 1))
    updates = []
    for i in range(3):
        second = rows_new[i][:, None] * cols_new[i][None, :] / row_means[i]
        updates.append(gradients[i] * lax.rsqrt(second))
    flat = jnp.stack([jnp.sum(update * update) for update in updates])
    flat = jnp.broadcast_to(jnp.pad(flat, (0, 5))[:, None], (8, LANES))
    totals = jnp.sum(gather_all(flat)[:, :, :, 0], axis=(0, 1))
    new_weights = []
    for i in range(3):
        clip_factor = jnp.maximum(1.0, jnp.sqrt(totals[i] / entries[i]) / CLIP_LIMIT)
        step_size = STEP_RATE * jnp.maximum(EPS_TWO, jnp.sqrt(weight_totals[i] / entries[i]))
        new_weights.append(weights_old[i] - step_size / clip_factor * updates[i])
    bias_rows = FF // D
    row_places = jnp.arange(VEC)
    counts = jnp.where(row_places < bias_rows, float(FF), float(D))
    grouped_updates = jnp.where(row_places < bias_rows, jnp.sum(step_rows[:bias_rows]), step_rows)
    grouped_weights = jnp.where(row_places < bias_rows, jnp.sum(weight_rows[:bias_rows]), weight_rows)
    clip_rows = jnp.maximum(1.0, jnp.sqrt(grouped_updates / counts) / CLIP_LIMIT)
    step_sizes = STEP_RATE * jnp.maximum(EPS_TWO, jnp.sqrt(grouped_weights / counts))
    factor_rows = lax.dynamic_slice_in_dim(step_sizes / clip_rows, dp_place * rows_v, rows_v)
    vectors_new = vectors - factor_rows[:, None] * vector_step
    return (
        block_out,
        input_grad,
        attn_grad,
        in_grad,
        out_grad,
        vector_grad,
        rows_new[0],
        cols_new[0],
        rows_new[1],
        cols_new[1],
        rows_new[2],
        cols_new[2],
        moment_new,
        new_weights[0],
        new_weights[1],
        new_weights[2],
        vectors_new,
    )


def solution(mesh):
    dp_count, fsdp_count = mesh.shape["dp"], mesh.shape["fsdp"]
    inner = jax.sharding.Mesh(mesh.devices.reshape(dp_count, fsdp_count // 2, 2), ALL)
    fsdp = ("chip", "core")
    split = P(ALL, None)
    block = P("dp", fsdp)
    stats = (P("dp"), P(fsdp)) * 3
    plain = dp_count == VDP and fsdp_count == 2 * VCHIP
    return jax.shard_map(
        body if plain else body_any,
        mesh=inner,
        in_specs=(split,) * 3 + (block,) * 4 + stats + (block,),
        out_specs=(split,) * 2 + (block,) * 4 + stats + (block,) * 5,
        check_vma=False,
    )
```

```python
import functools
import math

import jax
import jax.numpy as jnp
import numpy as np
from jax import lax
from jax.experimental import pallas as pl
from jax.experimental.pallas import tpu as pltpu
from jax.sharding import PartitionSpec as P

D = 256
FF = 2048
HEADS = 8
HEAD_DIM = 32
SEQ = 1024
HALF = 512
GROUP = 4
LANES = 128
QBLOCK = 512
WGRID = 32
STEP = 10
VEC = 16
TILE = 1024
CHUNK = 256
SUB = 512
LEAD = 5
STRIP = 64
VDP = 4
VCHIP = 4
VROWS = 16

EPS_NORM = 1e-05
EPS_ONE = 1e-30
EPS_TWO = 0.001
CLIP_LIMIT = 1.0
STEP_RATE = 0.3
FAR = 1e30
TAME = 40.0
LOG2_E = math.log2(math.e)
SCALE = HEAD_DIM ** (-0.5)
GELU_A = math.sqrt(2.0 / math.pi)
GELU_B = 0.044715
F32 = jnp.float32
BF16 = jnp.bfloat16
MIB = 1024 * 1024


def dot(left, right):
    return jnp.dot(left, right, preferred_element_type=F32)


def dot_nt(left, right):
    return lax.dot_general(left, right, (((1,), (1,)), ((), ())), preferred_element_type=F32)


def encode_table():
    half = D // 2
    feature = np.arange(half)
    freq = np.exp(
        (2 * (feature // 2)).astype(np.float32) * np.float32(-math.log(10000.0) / half)
    ).astype(np.float32)
    angles = np.arange(1, WGRID + 1, dtype=np.float32)[:, None] * freq[None, :]
    table = np.where(feature % 2 == 0, np.sin(angles), np.cos(angles)).astype(np.float32)
    low = jnp.bfloat16
    one = table.astype(low)
    rest = table - one.astype(np.float32)
    two = rest.astype(low)
    three = (rest - two.astype(np.float32)).astype(low)
    blank = np.zeros((LANES - 3 * WGRID, half), low)
    return np.concatenate([one, two, three, blank], axis=0)


def iota(shape, dim):
    return lax.broadcasted_iota(jnp.int32, shape, dim)


def norm_forward(rows):
    centered = rows - jnp.mean(rows, axis=-1, keepdims=True)
    inverse = lax.rsqrt(jnp.mean(centered * centered, axis=-1, keepdims=True) + EPS_NORM)
    return centered * inverse, inverse


def norm_backward(upstream, normed, inverse):
    return inverse * (
        upstream
        - jnp.mean(upstream, axis=-1, keepdims=True)
        - normed * jnp.mean(upstream * normed, axis=-1, keepdims=True)
    )

def vspec():
    return pl.BlockSpec(memory_space=pltpu.VMEM)


def params(mib=56, **more):
    return pltpu.CompilerParams(vmem_limit_bytes=mib * MIB, **more)


def pack_kernel(place, attn_ref, first_ref, second_ref, vector_ref, out_ref, ffn_ref):
    owner = place[1] * 2 + place[2]
    vector = vector_ref[...]
    rows = vector.shape[0]
    wide = jnp.concatenate([vector] * (LANES // vector.shape[1]), axis=1)
    slot = iota((rows, LANES), 1) // vector.shape[1]
    per = LANES // vector.shape[1]
    parts = [attn_ref[...]]
    for half in range(2):
        parts.append(jnp.where(slot + half * per == owner, wide, 0.0))
    parts.append(jnp.zeros((VROWS - 2 * rows, LANES), F32))
    piece = jnp.concatenate(parts, axis=0).astype(BF16)
    for at in range(VDP * VCHIP):
        out_ref[at] = piece
    ffn_ref[0] = first_ref[...].astype(BF16)
    ffn_ref[1] = second_ref[...].astype(BF16)


def pack_attn(place, attn_weight, ffn_in, ffn_out, vectors):
    return pl.pallas_call(
        pack_kernel,
        out_shape=(
            jax.ShapeDtypeStruct((VDP * VCHIP, attn_weight.shape[0] + VROWS, LANES), BF16),
            jax.ShapeDtypeStruct((2,) + ffn_in.shape, BF16),
        ),
        in_specs=[pl.BlockSpec(memory_space=pltpu.SMEM)] + [vspec()] * 4,
        out_specs=(vspec(), vspec()),
        compiler_params=params(),
        name="pack_attn",
    )(place, attn_weight, ffn_in, ffn_out, vectors)


def pack_ffn_kernel(place, own_ref, *refs):
    out_ref = refs[-1]
    for at in range(VCHIP):
        out_ref[at, pl.ds(place[0], 1)] = own_ref[...][None]
        for step in range(1, VDP):
            out_ref[at, pl.ds(place[0] ^ step, 1)] = refs[step - 1][...][None]


def pack_ffn(place, own, parts):
    return pl.pallas_call(
        pack_ffn_kernel,
        out_shape=jax.ShapeDtypeStruct((VCHIP, VDP) + own.shape, BF16),
        in_specs=[pl.BlockSpec(memory_space=pltpu.SMEM)] + [vspec()] * (1 + len(parts)),
        out_specs=vspec(),
        compiler_params=params(16),
        name="pack_ffn",
    )(place, own, *parts)


def place_kernel(
    segment_ref, tokens_ref, back_ref, table_ref, qk_ref, x_ref, qk_t_ref, x_t_ref, turned_ref, marks_ref
):
    row = pl.program_id(0)
    starts = []
    for number in range(1, 4):
        at = jnp.int32(0)
        for step in (512, 256, 128, 64, 32, 16, 8, 4, 2, 1, 1):
            probe = jnp.minimum(at + (step - 1), SEQ - 1)
            at = jnp.where(segment_ref[row, probe] < number, at + step, at)
        starts.append(at)
    edges = [jnp.int32(0)] + starts + [jnp.int32(SEQ)]
    begin = jnp.int32(0)
    for number in range(3, -1, -1):
        begin = jnp.where(edges[number + 1] - edges[number] == HALF, edges[number], begin)
    for number in range(3):
        marks_ref[row, number] = starts[number]
    marks_ref[row, 3] = begin
    one, two, three = starts
    x = pltpu.roll(tokens_ref[...].astype(F32), (SEQ - begin) & (SEQ - 1), 0)
    x_ref[...] = x.astype(BF16)
    x_t_ref[...] = x.T.astype(BF16)
    back = back_ref[...].astype(F32)
    turned_ref[...] = pltpu.roll(back, (SEQ - begin) & (SEQ - 1), 0).astype(BF16)
    at = (iota((SEQ, LANES), 0) + begin) & (SEQ - 1)
    lane = iota((SEQ, LANES), 1)
    start = jnp.where(at >= three, three, jnp.where(at >= two, two, jnp.where(at >= one, one, 0)))
    local = at - start
    kept = lane < 3 * WGRID
    slot = lane & (WGRID - 1)
    hot_r = jnp.where(((local >> 5) == slot) & kept, 1.0, 0.0).astype(BF16)
    hot_c = jnp.where(((local & (WGRID - 1)) == slot) & kept, 1.0, 0.0).astype(BF16)
    table = table_ref[...]
    places = jnp.concatenate([dot(hot_r, table), dot(hot_c, table)], axis=1)
    qk = x + places
    qk_ref[...] = qk.astype(BF16)
    qk_t_ref[...] = qk.T.astype(BF16)


def place_tokens(segment_ids, tokens, cotangent, table):
    rows = segment_ids.shape[0]
    by_row = lambda r: (r, 0)
    return pl.pallas_call(
        place_kernel,
        out_shape=(
            jax.ShapeDtypeStruct(tokens.shape, BF16),
            jax.ShapeDtypeStruct(tokens.shape, BF16),
            jax.ShapeDtypeStruct((D, tokens.shape[0]), BF16),
            jax.ShapeDtypeStruct((D, tokens.shape[0]), BF16),
            jax.ShapeDtypeStruct(tokens.shape, BF16),
            jax.ShapeDtypeStruct((rows, 4), jnp.int32),
        ),
        grid=(rows,),
        in_specs=[
            pl.BlockSpec(memory_space=pltpu.SMEM),
            pl.BlockSpec((SEQ, D), by_row),
            pl.BlockSpec((SEQ, D), by_row),
            pl.BlockSpec((LANES, LANES), lambda r: (0, 0)),
        ],
        out_specs=(
            pl.BlockSpec((SEQ, D), by_row),
            pl.BlockSpec((SEQ, D), by_row),
            pl.BlockSpec((D, SEQ), lambda r: (0, r)),
            pl.BlockSpec((D, SEQ), lambda r: (0, r)),
            pl.BlockSpec((SEQ, D), by_row),
            pl.BlockSpec(memory_space=pltpu.SMEM),
        ),
        compiler_params=params(dimension_semantics=("arbitrary",)),
        cost_estimate=pl.CostEstimate(flops=600_000_000, bytes_accessed=4_000_000, transcendentals=0),
        name="place_tokens",
    )(segment_ids, tokens, cotangent, table)


def attend_kernel(
    marks,
    place,
    x_ref,
    qk_ref,
    x_t_ref,
    qk_t_ref,
    mine_ref,
    other_ref,
    query_t_ref,
    value_ref,
    key_t_ref,
    out_t_ref,
    inverse_ref,
    mixed_ref,
    mixed_t_ref,
    exps_ref,
    weight_ref,
    proj_ref,
    vector_ref,
    key_s,
    value_s,
    mark_k,
    mark_q,
    first_s,
    second_s,
    weight_t_s,
    bias_s,
    tame_s,
    exps_s,
    exps_sem,
):
    row = pl.program_id(0)
    begin = marks[row, 3]
    core = place[2]

    def copy_of(group, half):
        return pltpu.make_async_copy(
            exps_s.at[group, half], exps_ref.at[row, group, half], exps_sem.at[group * 2 + half]
        )

    @pl.when(row == 0)
    def _():
        tall = D // VDP
        for d in range(VDP):
            rows = slice(d * tall, (d + 1) * tall)
            total = jnp.zeros((8, LANES), F32)
            for c in range(VCHIP):
                for ref, half in ((mine_ref, core), (other_ref, 1 - core)):
                    if c < 3:
                        to = pl.ds(pl.multiple_of(c * D + half * LANES, LANES), LANES)
                        weight_ref[rows, to] = ref[d, c, :tall, :]
                    else:
                        to = pl.ds(pl.multiple_of(half * LANES, LANES), LANES)
                        proj_ref[rows, to] = ref[d, c, :tall, :]
                    total += ref[d, c, tall:, :].astype(F32)[:8]
            vector_ref[d * 4 : (d + 1) * 4, :LANES] = total[:4]
            vector_ref[d * 4 : (d + 1) * 4, LANES:] = total[4:]
        weight_t_s[...] = weight_ref[...].astype(F32).T.astype(BF16)
        bias_s[...] = vector_ref[8:16, :].T

    qk_t = qk_t_ref[...]
    query_t = (dot(weight_t_s[:D, :], qk_t) + bias_s[:, 0:1]) * SCALE
    query_t = query_t.astype(BF16)
    query_t_ref[...] = query_t
    key_t = dot(weight_t_s[D : 2 * D, :], qk_t).astype(BF16)
    key_t_ref[...] = key_t

    def largest_norms(rows):
        rows = rows.astype(F32)
        rows = rows * rows
        sums = [
            jnp.sum(rows[head * HEAD_DIM : (head + 1) * HEAD_DIM], axis=0, keepdims=True)
            for head in range(HEADS)
        ]
        return jnp.max(jnp.concatenate(sums, axis=0), axis=1, keepdims=True)

    bound = jnp.max(largest_norms(query_t) * largest_norms(key_t))
    tame_s[0] = jnp.where(bound <= TAME * TAME, 1, 0)
    key_s[...] = dot(qk_ref[...], weight_ref[:, D : 2 * D]).astype(BF16)
    value = dot(x_ref[...], weight_ref[:, 2 * D : 3 * D]) + vector_ref[9:10, :]
    value_ref[...] = value.astype(BF16)
    value_t = dot(weight_t_s[2 * D :, :], x_t_ref[...]) + bias_s[:, 1:2]
    value_t = value_t.astype(BF16)
    for head in range(HEADS):
        value_s[head, :HEAD_DIM, :] = value_t[head * HEAD_DIM : (head + 1) * HEAD_DIM, :]
        value_s[head, HEAD_DIM:, :] = jnp.ones((16, SEQ), BF16)
    one, two, three = marks[row, 0], marks[row, 1], marks[row, 2]

    def number_of(shape, dim):
        here = (iota(shape, dim) + (HALF + begin)) & (SEQ - 1)
        return (
            jnp.where(here >= one, 1, 0)
            + jnp.where(here >= two, 1, 0)
            + jnp.where(here >= three, 1, 0)
        )

    lane = iota((HALF, LANES), 1)
    number = number_of((HALF, LANES), 0)
    mark_k[...] = jnp.where((number != lane) & (lane < 4), -FAR, 0.0).astype(BF16)
    number = number_of((LANES, HALF), 1)
    mark_q[...] = jnp.where(number == iota((LANES, HALF), 0), 1.0, 0.0).astype(BF16)

    head_of = iota((1, LANES), 1) // HEAD_DIM
    for group in range(2):
        keys_here = key_s[:, group * LANES : (group + 1) * LANES]
        for at_head in range(GROUP):
            mask = jnp.where(head_of == at_head, 1.0, 0.0).astype(BF16)
            rows = slice(at_head * HALF, (at_head + 1) * HALF)
            first_s[group, rows, :] = keys_here[:HALF] * mask
            second_s[group, rows, :LANES] = keys_here[HALF:] * mask
            second_s[group, rows, LANES:] = mark_k[...]

    @pl.when(row > 0)
    def _():
        for group in range(2):
            for half in range(2):
                copy_of(group, half).wait()

    def scores_of(group, half, rows):
        query = query_t_ref[group * LANES : (group + 1) * LANES, half * HALF : (half + 1) * HALF]
        if half == 0:
            return dot(first_s[group, rows, :], query)
        return dot(second_s[group, rows, :], jnp.concatenate([query, mark_q[...]], axis=0))

    def place_of(at_head):
        return slice(at_head * HALF, (at_head + 1) * HALF)

    def exps_plain(group, half):
        scores = scores_of(group, half, slice(0, GROUP * HALF))
        for at_head in range(GROUP):
            exps = jnp.exp2(scores[place_of(at_head), :] * LOG2_E)
            exps_s[group, half, :, place_of(at_head)] = exps.astype(BF16)

    def exps_shifted(group, half):
        for at_head in range(GROUP):
            rows = place_of(at_head)
            largest = jnp.max(scores_of(group, half, rows), axis=0, keepdims=True)
            exps = jnp.exp2((scores_of(group, half, rows) - largest) * LOG2_E)
            exps_s[group, half, :, rows] = exps.astype(BF16)

    def finish(group, half):
        rows = slice(half * HALF, (half + 1) * HALF)
        for at_head in range(GROUP):
            head = group * GROUP + at_head
            out = dot(value_s[head, :, rows], exps_s[group, half, :, place_of(at_head)])
            inverse = 1.0 / out[HEAD_DIM : HEAD_DIM + 1, :]
            inverse_ref[group, at_head : at_head + 1, rows] = inverse
            out_t_ref[head * HEAD_DIM : (head + 1) * HEAD_DIM, rows] = out[:HEAD_DIM, :] * inverse

    def run(exps_of):
        items = [(group, half) for group in range(2) for half in range(2)]
        for i in range(len(items) + 1):
            if i < len(items):
                exps_of(*items[i])
                copy_of(*items[i]).start()
            if i >= 1:
                finish(*items[i - 1])

    @pl.when(tame_s[0] == 1)
    def _():
        run(exps_plain)

    @pl.when(tame_s[0] == 0)
    def _():
        run(exps_shifted)

    out_t = out_t_ref[...]
    mixed_t_ref[...] = out_t.astype(BF16)
    mixed_ref[...] = out_t.T.astype(BF16)

    @pl.when(row == pl.num_programs(0) - 1)
    def _():
        for group in range(2):
            for half in range(2):
                copy_of(group, half).wait()


def attend_forward(marks, place, x, qk, x_t, qk_t, mine, other):
    total = x.shape[0]
    rows = total // SEQ
    by_row = lambda r, m, p: (r, 0)
    by_col = lambda r, m, p: (0, r)
    whole = lambda r, m, p: (0, 0)
    return pl.pallas_call(
        attend_kernel,
        out_shape=(
            jax.ShapeDtypeStruct((D, total), BF16),
            jax.ShapeDtypeStruct((total, D), BF16),
            jax.ShapeDtypeStruct((D, total), BF16),
            jax.ShapeDtypeStruct((D, total), F32),
            jax.ShapeDtypeStruct((2, 8, total), F32),
            jax.ShapeDtypeStruct((total, D), BF16),
            jax.ShapeDtypeStruct((D, total), BF16),
            jax.ShapeDtypeStruct((rows, 2, 2, HALF, GROUP * HALF), BF16),
            jax.ShapeDtypeStruct((D, 3 * D), BF16),
            jax.ShapeDtypeStruct((D, D), BF16),
            jax.ShapeDtypeStruct((VEC, D), F32),
        ),
        grid_spec=pltpu.PrefetchScalarGridSpec(
            num_scalar_prefetch=2,
            grid=(rows,),
            in_specs=[
                pl.BlockSpec((SEQ, D), by_row),
                pl.BlockSpec((SEQ, D), by_row),
                pl.BlockSpec((D, SEQ), by_col),
                pl.BlockSpec((D, SEQ), by_col),
                vspec(),
                vspec(),
            ],
            out_specs=[
                pl.BlockSpec((D, SEQ), by_col),
                pl.BlockSpec((SEQ, D), by_row),
                pl.BlockSpec((D, SEQ), by_col),
                pl.BlockSpec((D, SEQ), by_col),
                pl.BlockSpec((2, 8, SEQ), lambda r, m, p: (0, 0, r)),
                pl.BlockSpec((SEQ, D), by_row),
                pl.BlockSpec((D, SEQ), by_col),
                pl.BlockSpec(memory_space=pl.ANY),
                pl.BlockSpec((D, 3 * D), whole),
                pl.BlockSpec((D, D), whole),
                pl.BlockSpec((VEC, D), whole),
            ],
            scratch_shapes=[
                pltpu.VMEM((SEQ, D), BF16),
                pltpu.VMEM((HEADS, HEAD_DIM + 16, SEQ), BF16),
                pltpu.VMEM((HALF, LANES), BF16),
                pltpu.VMEM((LANES, HALF), BF16),
                pltpu.VMEM((2, GROUP * HALF, LANES), BF16),
                pltpu.VMEM((2, GROUP * HALF, 2 * LANES), BF16),
                pltpu.VMEM((3 * D, D), BF16),
                pltpu.VMEM((D, 8), F32),
                pltpu.SMEM((1,), jnp.int32),
                pltpu.VMEM((2, 2, HALF, GROUP * HALF), BF16),
                pltpu.SemaphoreType.DMA((4,)),
            ],
        ),
        compiler_params=params(dimension_semantics=("arbitrary",)),
        cost_estimate=pl.CostEstimate(
            flops=20_000_000_000, bytes_accessed=30_000_000, transcendentals=8_400_000
        ),
        name="attend_forward",
    )(marks, place, x, qk, x_t, qk_t, mine, other)


def feed_kernel(
    marks,
    place,
    x_ref,
    back_ref,
    mixed_ref,
    mixed_t_ref,
    proj_ref,
    mine_ref,
    other_ref,
    vector_ref,
    block_ref,
    resid_ref,
    mixed_grad_ref,
    mine_out,
    other_out,
    proj_out,
    vector_out,
    first_w,
    second_w,
    first_acc,
    second_acc,
    proj_acc,
    vector_acc,
    hidden_s,
    slope_s,
    pre_s,
    first_low_s,
    branch_low_s,
    attended_s,
    eye_s,
):
    step = pl.program_id(0)
    core = place[2]
    tall = D // VDP
    wide = FF // (2 * VCHIP)

    @pl.when(step == 0)
    def _():
        first_acc[...] = jnp.zeros_like(first_acc)
        second_acc[...] = jnp.zeros_like(second_acc)
        proj_acc[...] = jnp.zeros_like(proj_acc)
        vector_acc[...] = jnp.zeros_like(vector_acc)
        eye_s[...] = jnp.where(iota((D, D), 0) == iota((D, D), 1), 1.0, 0.0).astype(BF16)
        for d in range(VDP):
            rows = slice(d * tall, (d + 1) * tall)
            for c in range(VCHIP):
                for ref, half in ((mine_ref, core), (other_ref, 1 - core)):
                    to = pl.ds(pl.multiple_of((2 * c + half) * wide, wide), wide)
                    first_w[rows, to] = ref[c, d, 0]
                    second_w[rows, to] = ref[c, d, 1]

    bias_o, bias_2 = vector_ref[10:11, :], vector_ref[11:12, :]
    gain_1, shift_1 = vector_ref[12:13, :], vector_ref[13:14, :]
    gain_2, shift_2 = vector_ref[14:15, :], vector_ref[15:16, :]
    chunks = FF // CHUNK
    pair = 2

    def columns(at, count=1):
        return slice(at * CHUNK, (at + count) * CHUNK)

    def hidden_of(rows, at, pre):
        per = CHUNK // D
        bias = [vector_ref[at * per + i : at * per + i + 1, :] for i in range(per)]
        pre = (pre + jnp.concatenate(bias, axis=1)).astype(BF16)
        cube = BF16(GELU_A * GELU_B) * (pre * pre)
        gate = BF16(0.5) + BF16(0.5) * jnp.tanh(pre * (cube + BF16(GELU_A)))
        hidden_s[rows, columns(at)] = pre * gate
        slope_s[rows, columns(at)] = gate + (gate - gate * gate) * (
            pre * (BF16(6.0) * cube + BF16(2.0 * GELU_A))
        )

    def stages(sub):
        rows_at = sub * SUB
        rows = slice(rows_at, rows_at + SUB)
        attended = dot(mixed_ref[rows, :], proj_ref[...]) + bias_o
        norm_1, inverse_1 = norm_forward(x_ref[rows, :].astype(F32) + attended)
        first = norm_1 * gain_1 + shift_1
        first_low = first.astype(BF16)
        first_low_s[rows, :] = first_low
        yield
        branch = jnp.zeros((SUB, D), F32)
        for i in range(chunks + 1):
            if i < chunks:
                hidden_of(rows, i, dot(first_low, first_w[:, columns(i)]))
            if i >= pair and i % pair == 0:
                cols = columns(i - pair, pair)
                branch += dot_nt(hidden_s[rows, cols], second_w[:, cols])
            yield
        norm_2, inverse_2 = norm_forward(first + (branch + bias_2))
        block_ref[rows, :] = norm_2 * gain_2 + shift_2
        back = back_ref[rows, :].astype(F32)
        vector_acc[14:15, :] += jnp.sum(back * norm_2, axis=0, keepdims=True)
        vector_acc[15:16, :] += jnp.sum(back, axis=0, keepdims=True)
        resid_2 = norm_backward(back * gain_2, norm_2, inverse_2)
        branch_low = resid_2.astype(BF16)
        branch_low_s[rows, :] = branch_low
        vector_acc[11:12, :] += jnp.sum(branch_low.astype(F32), axis=0, keepdims=True)
        yield
        first_back = resid_2
        if sub == 1:
            branch_t = dot_nt(eye_s[...], branch_low_s[...]).astype(BF16)
            first_t = dot_nt(eye_s[...], first_low_s[...]).astype(BF16)
            first_t = jnp.concatenate([first_t, jnp.ones((16, TILE), BF16)], axis=0)
        for i in range(chunks + 1):
            if i < chunks:
                pull = dot(branch_low, second_w[:, columns(i)]).astype(BF16)
                pre_s[rows, columns(i)] = pull * slope_s[rows, columns(i)]
                if sub == 1:
                    second_acc[:, columns(i)] += dot(branch_t, hidden_s[:, columns(i)])
            if i >= 1 and sub == 1:
                cols = columns(i - 1)
                first_acc[:, cols] += dot(first_t, pre_s[:, cols])
            if i >= pair and i % pair == 0:
                cols = columns(i - pair, pair)
                first_back += dot_nt(pre_s[rows, cols], first_w[:, cols])
            yield
        vector_acc[12:13, :] += jnp.sum(first_back * norm_1, axis=0, keepdims=True)
        vector_acc[13:14, :] += jnp.sum(first_back, axis=0, keepdims=True)
        resid_1 = norm_backward(first_back * gain_1, norm_1, inverse_1)
        resid_ref[rows, :] = resid_1
        attended_low = resid_1.astype(BF16)
        attended_s[rows, :] = attended_low
        vector_acc[10:11, :] += jnp.sum(attended_low.astype(F32), axis=0, keepdims=True)
        mixed_grad_ref[:, rows] = dot_nt(proj_ref[...], attended_low).astype(BF16)
        yield

    ahead, behind = stages(0), stages(1)
    for _ in range(LEAD):
        next(ahead)
    running = [ahead, behind]
    while running:
        for program in list(running):
            if next(program, 0) == 0:
                running.remove(program)
    proj_acc[...] += dot(mixed_t_ref[...], attended_s[...])

    @pl.when(step == pl.num_programs(0) - 1)
    def _():
        for d in range(VDP):
            rows = slice(d * tall, (d + 1) * tall)
            for c in range(VCHIP):
                for ref, half in ((mine_out, core), (other_out, 1 - core)):
                    to = pl.ds(pl.multiple_of((2 * c + half) * wide, wide), wide)
                    ref[d, c, 0] = first_acc[rows, to].astype(BF16)
                    ref[d, c, 1] = second_acc[rows, to].astype(BF16)
        proj_out[...] = proj_acc[...]
        for at in range(FF // D):
            vector_out[at : at + 1, :] = first_acc[D : D + 1, at * D : (at + 1) * D]
        vector_out[FF // D :, :] = vector_acc[FF // D :, :]


def feed_forward(marks, place, x, back, mixed, mixed_t, proj, mine, other, vector):
    total = x.shape[0]
    tile = lambda i, m, p: (i, 0)
    by_col = lambda i, m, p: (0, i)
    whole = lambda i, m, p: (0, 0)
    whole5 = lambda i, m, p: (0, 0, 0, 0, 0)
    return pl.pallas_call(
        feed_kernel,
        out_shape=(
            jax.ShapeDtypeStruct((total, D), F32),
            jax.ShapeDtypeStruct((total, D), F32),
            jax.ShapeDtypeStruct((D, total), BF16),
            jax.ShapeDtypeStruct(mine.shape, BF16),
            jax.ShapeDtypeStruct(mine.shape, BF16),
            jax.ShapeDtypeStruct((D, D), F32),
            jax.ShapeDtypeStruct((VEC, D), F32),
        ),
        grid_spec=pltpu.PrefetchScalarGridSpec(
            num_scalar_prefetch=2,
            grid=(total // TILE,),
            in_specs=[
                pl.BlockSpec((TILE, D), tile),
                pl.BlockSpec((TILE, D), tile),
                pl.BlockSpec((TILE, D), tile),
                pl.BlockSpec((D, TILE), by_col),
                pl.BlockSpec((D, D), whole),
                vspec(),
                vspec(),
                pl.BlockSpec((VEC, D), whole),
            ],
            out_specs=[
                pl.BlockSpec((TILE, D), tile),
                pl.BlockSpec((TILE, D), tile),
                pl.BlockSpec((D, TILE), by_col),
                pl.BlockSpec(mine.shape, whole5),
                pl.BlockSpec(mine.shape, whole5),
                pl.BlockSpec((D, D), whole),
                pl.BlockSpec((VEC, D), whole),
            ],
            scratch_shapes=[
                pltpu.VMEM((D, FF), BF16),
                pltpu.VMEM((D, FF), BF16),
                pltpu.VMEM((D + 16, FF), F32),
                pltpu.VMEM((D, FF), F32),
                pltpu.VMEM((D, D), F32),
                pltpu.VMEM((VEC, D), F32),
                pltpu.VMEM((TILE, FF), BF16),
                pltpu.VMEM((TILE, FF), BF16),
                pltpu.VMEM((TILE, FF), BF16),
                pltpu.VMEM((TILE, D), BF16),
                pltpu.VMEM((TILE, D), BF16),
                pltpu.VMEM((TILE, D), BF16),
                pltpu.VMEM((D, D), BF16),
            ],
        ),
        compiler_params=params(dimension_semantics=("arbitrary",)),
        cost_estimate=pl.CostEstimate(
            flops=14_000_000_000, bytes_accessed=15_000_000, transcendentals=4_200_000
        ),
        name="feed_forward",
    )(marks, place, x, back, mixed, mixed_t, proj, mine, other, vector)


def pull_kernel(
    marks,
    place,
    grad_t_ref,
    query_t_ref,
    value_ref,
    key_t_ref,
    out_t_ref,
    inverse_ref,
    exps_ref,
    qk_t_ref,
    x_t_ref,
    proj_ref,
    low_ref,
    own_ref,
    other_ref,
    sums_ref,
    dot_s,
    query_g,
    key_g,
    value_g,
    acc,
    sum_acc,
    value_s,
    scaled_t_s,
    score_s,
):
    group = pl.program_id(0)
    row = pl.program_id(1)
    begin = marks[row, 3]

    @pl.when(row == 0)
    def _():
        acc[...] = jnp.zeros_like(acc)
        sum_acc[...] = jnp.zeros_like(sum_acc)

    grad_t = grad_t_ref[...].astype(F32)
    head_of = iota((1, LANES), 1) // HEAD_DIM
    for at_head in range(GROUP):
        heads = slice(at_head * HEAD_DIM, (at_head + 1) * HEAD_DIM)
        part = grad_t[heads, :] * inverse_ref[0, at_head : at_head + 1, :]
        dot_s[at_head : at_head + 1, :] = jnp.sum(part * out_t_ref[heads, :], axis=0, keepdims=True)
        part = part.astype(BF16)
        scaled_t_s[heads, :] = part
        mask = jnp.where(head_of == at_head, 1.0, 0.0).astype(BF16)
        for half in range(2):
            rows = slice(half * HALF, (half + 1) * HALF)
            to = slice(at_head * HALF, (at_head + 1) * HALF)
            value_s[half, to, :] = value_ref[rows, :] * mask

    def score_grads_of(half, block):
        at = half * HALF + block * QBLOCK
        pulls = dot(value_s[half], scaled_t_s[:, at : at + QBLOCK])
        for at_head in range(GROUP):
            cols = slice(at_head * HALF + block * QBLOCK, at_head * HALF + (block + 1) * QBLOCK)
            pull = pulls[at_head * HALF : (at_head + 1) * HALF, :]
            pull = (pull - dot_s[at_head : at_head + 1, at : at + QBLOCK]).astype(BF16)
            score_s[half, :, cols] = exps_ref[0, 0, half, :, cols] * pull

    def finish(half, at_head):
        cols = slice(at_head * HALF, (at_head + 1) * HALF)
        rows = slice(half * HALF, (half + 1) * HALF)
        heads = slice(at_head * HEAD_DIM, (at_head + 1) * HEAD_DIM)
        score_grad = score_s[half, :, cols]
        value_g[heads, rows] = dot_nt(scaled_t_s[heads, rows], exps_ref[0, 0, half, :, cols])
        query_g[heads, rows] = dot(key_t_ref[heads, rows], score_grad)
        key_g[heads, rows] = dot_nt(query_t_ref[heads, rows], score_grad)

    blocks = HALF // QBLOCK
    each = GROUP // blocks
    for block in range(blocks):
        score_grads_of(0, block)
    for block in range(blocks):
        score_grads_of(1, block)
        for at_head in range(each * block, each * (block + 1)):
            finish(0, at_head)
    for at_head in range(GROUP):
        finish(1, at_head)
    query_low = query_g[...].astype(BF16)
    both_low = jnp.concatenate([key_g[...].astype(BF16), value_g[...].astype(BF16)], axis=0)
    ones = jnp.ones((16, SEQ), BF16)
    sum_acc[0:1, :] += dot_nt(ones, query_low)[0:1, :] * SCALE
    sum_acc[1:2, :] += dot_nt(ones, both_low[LANES:, :])[0:1, :]
    qk_t = qk_t_ref[...]
    both = dot_nt(qk_t, jnp.concatenate([query_low, both_low[:LANES, :]], axis=0))
    acc[:, :LANES] += both[:, :LANES] * SCALE
    acc[:, LANES : 2 * LANES] += both[:, LANES:]
    acc[:, 2 * LANES :] += dot_nt(x_t_ref[...], both_low[LANES:, :])
    low_ref[0, :LANES, :] = query_low
    low_ref[0, LANES:, :] = both_low

    def write(ref):
        tall = D // VDP
        for d in range(VDP):
            rows = slice(d * tall, (d + 1) * tall)
            for c in range(3):
                ref[d, c] = acc[rows, c * LANES : (c + 1) * LANES].astype(BF16)
            ref[d, 3] = proj_ref[rows, :].astype(BF16)

    last = row == pl.num_programs(1) - 1

    @pl.when(last & (group == place[2]))
    def _():
        write(own_ref)

    @pl.when(last & (group != place[2]))
    def _():
        write(other_ref)

    @pl.when(last)
    def _():
        sums_ref[pl.ds(group, 1)] = sum_acc[...][None]


def attend_back(marks, place, grad_t, query_t, value, key_t, out_t, inverse, exps, qk_t, x_t, proj):
    total = value.shape[0]
    rows = total // SEQ
    by_both = lambda g, r, m, p: (g, r)
    by_col = lambda g, r, m, p: (0, r)
    grads = jax.ShapeDtypeStruct((VDP, VCHIP, D // VDP, LANES), BF16)
    grads_spec = pl.BlockSpec(grads.shape, lambda g, r, m, p: (0, 0, 0, 0))
    return pl.pallas_call(
        pull_kernel,
        out_shape=(
            jax.ShapeDtypeStruct((2, 3 * LANES, total), BF16),
            grads,
            grads,
            jax.ShapeDtypeStruct((2, 8, LANES), F32),
        ),
        grid_spec=pltpu.PrefetchScalarGridSpec(
            num_scalar_prefetch=2,
            grid=(2, rows),
            in_specs=[
                pl.BlockSpec((LANES, SEQ), by_both),
                pl.BlockSpec((LANES, SEQ), by_both),
                pl.BlockSpec((SEQ, LANES), lambda g, r, m, p: (r, g)),
                pl.BlockSpec((LANES, SEQ), by_both),
                pl.BlockSpec((LANES, SEQ), by_both),
                pl.BlockSpec((1, 8, SEQ), lambda g, r, m, p: (g, 0, r)),
                pl.BlockSpec((1, 1, 2, HALF, GROUP * HALF), lambda g, r, m, p: (r, g, 0, 0, 0)),
                pl.BlockSpec((D, SEQ), by_col),
                pl.BlockSpec((D, SEQ), by_col),
                pl.BlockSpec((D, LANES), lambda g, r, m, p: (0, g)),
            ],
            out_specs=[
                pl.BlockSpec((1, 3 * LANES, SEQ), lambda g, r, m, p: (g, 0, r)),
                grads_spec,
                grads_spec,
                pl.BlockSpec((2, 8, LANES), lambda g, r, m, p: (0, 0, 0)),
            ],
            scratch_shapes=[
                pltpu.VMEM((8, SEQ), F32),
                pltpu.VMEM((LANES, SEQ), F32),
                pltpu.VMEM((LANES, SEQ), F32),
                pltpu.VMEM((LANES, SEQ), F32),
                pltpu.VMEM((D, 3 * LANES), F32),
                pltpu.VMEM((8, LANES), F32),
                pltpu.VMEM((2, GROUP * HALF, LANES), BF16),
                pltpu.VMEM((LANES, SEQ), BF16),
                pltpu.VMEM((2, HALF, GROUP * HALF), BF16),
            ],
        ),
        compiler_params=params(dimension_semantics=("arbitrary", "arbitrary")),
        cost_estimate=pl.CostEstimate(
            flops=36_000_000_000, bytes_accessed=30_000_000, transcendentals=0
        ),
        name="attend_back",
    )(marks, place, grad_t, query_t, value, key_t, out_t, inverse, exps, qk_t, x_t, proj)


def input_kernel(
    marks, low_ref, weight_ref, resid_ref, turned_ref, block_ref, input_ref, token_ref
):
    token_ref[...] = jnp.zeros_like(token_ref)
    at = slice(0, LANES), slice(LANES, 2 * LANES), slice(2 * LANES, 3 * LANES)
    parts = [jnp.concatenate([low_ref[0, rows, :], low_ref[1, rows, :]], axis=0) for rows in at]
    pulled = dot(weight_ref[:, :D], parts[0]) * SCALE + (
        dot(weight_ref[:, D : 2 * D], parts[1]) + dot(weight_ref[:, 2 * D :], parts[2])
    )
    begin = marks[pl.program_id(0), 3]
    input_ref[...] = pltpu.roll(resid_ref[...] + pulled.T, begin, 0)
    block_ref[...] = pltpu.roll(turned_ref[...], begin, 0)


def input_pull(marks, low, weight, resid, turned):
    total = resid.shape[0]
    by_row = pl.BlockSpec((SEQ, D), lambda r, m: (r, 0))
    return pl.pallas_call(
        input_kernel,
        out_shape=(
            jax.ShapeDtypeStruct((total, D), F32),
            jax.ShapeDtypeStruct((total, D), F32),
            jax.ShapeDtypeStruct((8, LANES), F32),
        ),
        grid_spec=pltpu.PrefetchScalarGridSpec(
            num_scalar_prefetch=1,
            grid=(total // SEQ,),
            in_specs=[
                pl.BlockSpec((2, 3 * LANES, SEQ), lambda r, m: (0, 0, r)),
                pl.BlockSpec((D, 3 * D), lambda r, m: (0, 0)),
                by_row,
                by_row,
            ],
            out_specs=[by_row, by_row, pl.BlockSpec((8, LANES), lambda r, m: (0, 0))],
        ),
        compiler_params=params(dimension_semantics=("arbitrary",)),
        cost_estimate=pl.CostEstimate(
            flops=1_000_000_000, bytes_accessed=8_000_000, transcendentals=0
        ),
        name="input_pull",
    )(marks, low, weight, resid, turned)


def two_terms(rows):
    high = rows.astype(BF16)
    return jnp.concatenate([high.astype(F32), rows - high.astype(F32)], axis=0)


def column_to_row(columns, rows):
    lane = iota((rows, LANES), 1)
    wide = jnp.zeros((rows, LANES), F32)
    for i, column in enumerate(columns):
        wide = jnp.where(lane == i, column, wide)
    return wide.T[:8, :]


def total_of(array):
    return jnp.sum(jnp.sum(array, axis=0, keepdims=True), axis=1, keepdims=True)


def tail_ffn_kernel(place, ffn_ref, rows_1, rows_2, last_ref, grad_1, grad_2, grad_ref, stat_ref):
    lane = iota((1, LANES), 1)
    piece, across = [], []
    for kind in range(2):
        total = ffn_ref[0, kind].astype(F32)
        for at in range(1, VDP * VCHIP):
            total = total + ffn_ref[at, kind].astype(F32)
        (grad_1, grad_2)[kind][...] = total
        grad_ref[kind] = total
        square = total * total + EPS_ONE
        down = jnp.sum(square, axis=0, keepdims=True)
        piece += [down[:, :LANES], down[:, LANES:]]
        across.append(jnp.sum(square, axis=1, keepdims=True))
    across = column_to_row(across, total.shape[0])
    across = jnp.concatenate([across[0:1], across[1:2]], axis=1)
    olds = jnp.zeros((1, LANES), F32)
    for i, ref in enumerate((rows_1, rows_2)):
        olds = jnp.where(lane == i, jnp.sum(ref[...], axis=1, keepdims=True), olds)
    stat_ref[...] = jnp.concatenate([across] + piece + [olds, jnp.zeros((2, LANES), F32)], axis=0)


def tail_send_kernel(
    place, mine_ref, got_ref, vector_ref, sums_ref, stat_ref, stat_other_ref, send_ref
):
    tall = D // VDP
    low, high = sums_ref[0], sums_ref[1]
    vector = jnp.concatenate(
        [
            vector_ref[:8, :],
            jnp.concatenate([low[:2], high[:2]], axis=1),
            vector_ref[10:, :],
        ],
        axis=0,
    )
    stat = jnp.concatenate([stat_ref[0:1, :] + stat_other_ref[0:1, :], stat_ref[1:6, :]], axis=0)
    stat = two_terms(stat)
    rows = VEC // VDP
    for d in range(VDP):
        for c in range(VCHIP):
            at = d * VCHIP + c
            both = mine_ref[d, c].astype(F32) + got_ref[d, c].astype(F32)
            send_ref[at, :tall, :] = both.astype(BF16)
            part = vector[d * rows : (d + 1) * rows, c * 64 : (c + 1) * 64]
            part = jnp.concatenate([part, jnp.zeros((rows, LANES - 64), F32)], axis=1)
            send_ref[at, tall:, :] = jnp.concatenate([part, stat], axis=0).astype(BF16)


def tail_reduce_kernel(
    place,
    earlier_ref,
    got_ref,
    ffn_grad_ref,
    attn_ref,
    first_ref,
    second_ref,
    rows_0,
    rows_1,
    rows_2,
    cols_0,
    cols_1,
    cols_2,
    vector_ref,
    moment_ref,
    grad_ref,
    update_1,
    update_2,
    rows_out_1,
    rows_out_2,
    cols_out_1,
    cols_out_2,
    send_ref,
):
    decay = 1.0 - STEP ** (-0.8)
    chip = place[1]
    dp = place[0]
    tall = attn_ref.shape[0]
    rows, width = vector_ref.shape
    pieces = VDP * VCHIP
    lane = iota((1, LANES), 1)
    total = got_ref[0, :tall, :].astype(F32)
    part = got_ref[0, tall:, :].astype(F32)[:rows]
    for at in range(1, pieces):
        total = total + got_ref[at, :tall, :].astype(F32)
        part = part + got_ref[at, tall:, :].astype(F32)[:rows]
    grad_ref[...] = total
    low = total.astype(BF16)

    def stat_of(at):
        both = got_ref[pl.ds(at, 1), tall:, :][0].astype(F32)[rows:]
        return both[:6] + both[6:12]

    every = jnp.zeros((1, LANES), F32)
    olds = jnp.zeros((1, LANES), F32)
    mine = jnp.zeros((1, LANES), F32)
    down = jnp.zeros((6, LANES), F32)
    for d in range(VDP):
        down = down + stat_of(d * VCHIP + chip)
        for c in range(VCHIP):
            stat = stat_of(d * VCHIP + c)
            every = every + stat[0:1]
            if c == 0:
                olds = olds + stat[5:6]
    for c in range(VCHIP):
        mine = mine + stat_of(dp * VCHIP + c)[0:1]
    row_total = tall * VDP
    new_rows, means = [], []
    for i, ref in enumerate((rows_1, rows_2)):
        count = first_ref.shape[1] * 2 * VCHIP
        new_rows.append(decay * ref[...] + (1.0 - decay) * (mine[:, i * tall : (i + 1) * tall] / count))
        old = jnp.sum(jnp.where(lane == i, olds, 0.0), axis=1, keepdims=True)
        fresh = jnp.sum(every[:, i * tall : (i + 1) * tall], axis=1, keepdims=True)
        means.append((decay * old + (1.0 - decay) * (fresh / count)) / row_total)
    tile = jnp.concatenate(new_rows + [jnp.zeros((6, tall), F32)], axis=0)
    rows_out_1[...] = new_rows[0]
    rows_out_2[...] = new_rows[1]
    tile = jnp.concatenate([tile, jnp.zeros((8, LANES - tall), F32)], axis=1)
    turned = jnp.concatenate([tile, jnp.zeros((LANES - 8, LANES), F32)], axis=0).T
    scalars = jnp.zeros((1, LANES), F32)
    for i, (old_ref, out_ref, to) in enumerate(
        ((cols_1, cols_out_1, update_1), (cols_2, cols_out_2, update_2))
    ):
        sums = jnp.concatenate([down[1 + 2 * i : 2 + 2 * i], down[2 + 2 * i : 3 + 2 * i]], axis=1)
        cols = decay * old_ref[...] + (1.0 - decay) * (sums / row_total)
        out_ref[...] = cols
        grad = ffn_grad_ref[i]
        update = grad * lax.rsqrt(turned[:tall, i : i + 1] * cols / means[i])
        to[...] = update
        scalars = jnp.where(lane == 67 + i, total_of(update * update), scalars)
    for i, ref in enumerate((attn_ref, first_ref, second_ref)):
        weight = ref[...]
        scalars = jnp.where(lane == 64 + i, total_of(weight * weight), scalars)
    scalars = jnp.concatenate([rows_0[...], scalars[:, tall:]], axis=1)
    vector = vector_ref[...]
    power = jnp.sum(vector * vector, axis=1, keepdims=True)
    lines = jnp.concatenate(
        [part[:, :64], moment_ref[...], jnp.broadcast_to(power, (rows, LANES - 64 - width))], axis=1
    )
    piece = jnp.concatenate(
        [two_terms(lines), two_terms(jnp.concatenate([cols_0[...], scalars], axis=0))]
        + [jnp.zeros((4, LANES), F32)],
        axis=0,
    ).astype(BF16)
    for at in range(pieces):
        send_ref[at, :tall, :] = low
        send_ref[at, tall:, :] = piece


def tail_apply_kernel(
    place,
    mine_ref,
    other_ref,
    grad_ref,
    update_1,
    update_2,
    weight_0,
    weight_1,
    weight_2,
    rows_0,
    cols_0,
    vector_ref,
    moment_ref,
    new_0,
    new_1,
    new_2,
    rows_out,
    cols_out,
    vector_grad_ref,
    moment_out,
    vector_out,
    sums_s,
    rows_s,
):
    decay = 1.0 - STEP ** (-0.8)
    dp, chip, core = place[0], place[1], place[2]
    tall = weight_0.shape[0]
    rows, width = vector_ref.shape
    fsdp = 2 * VCHIP
    lane = iota((1, LANES), 1)
    refs = (mine_ref, other_ref)
    row_total = float(tall * VDP)
    col_total = float(LANES * fsdp)

    def lines_of(ref, at):
        both = ref[at, tall:, :].astype(F32)
        return both[0:4] + both[4:8], both[8:10] + both[10:12]

    scalars = jnp.zeros((1, LANES), F32)
    for ref in refs:
        for at in range(VDP * VCHIP):
            scalars = scalars + lines_of(ref, at)[1][1:2]
    scalar = lambda at: jnp.sum(jnp.where(lane == at, scalars, 0.0), axis=1, keepdims=True)

    tile, fresh = [], []
    for d in range(VDP):
        wide = jnp.zeros((tall, LANES), F32)
        for ref in refs:
            for c in range(VCHIP):
                block = ref[d * VCHIP + c, :tall, :].astype(F32)
                wide = wide + (block * block + EPS_ONE)
        fresh.append(jnp.sum(wide, axis=1, keepdims=True))
        tile.append(lines_of(mine_ref, d * VCHIP)[1][1:2])
    tile = jnp.concatenate(tile + [jnp.zeros((LANES - VDP, LANES), F32)], axis=0).T
    mean = jnp.zeros((1, 1), F32)
    new_rows = []
    for d in range(VDP):
        new = decay * tile[:tall, d : d + 1] + (1.0 - decay) * (fresh[d] / col_total)
        new_rows.append(1.0 / new)
        mean = mean + jnp.sum(new, axis=0, keepdims=True)
        sums_s[d] = jnp.broadcast_to(fresh[d], (tall, LANES))
    mean = mean / row_total
    mine = sums_s[pl.ds(dp, 1)][0]
    rows_s[...] = mine.T
    rows_new = decay * rows_0[...] + (1.0 - decay) * (rows_s[0:1, :tall] / col_total)
    rows_out[...] = rows_new
    power = jnp.zeros((1, 1), F32)
    for half, ref in enumerate(refs):
        for c in range(VCHIP):
            down = jnp.zeros((tall, LANES), F32)
            weighted = jnp.zeros((tall, LANES), F32)
            for d in range(VDP):
                block = ref[d * VCHIP + c, :tall, :].astype(F32)
                square = block * block
                down = down + (square + EPS_ONE)
                weighted = weighted + square * new_rows[d]
            down = jnp.sum(down, axis=0, keepdims=True)
            old = lines_of(ref, c)[1][0:1]
            cols = decay * old + (1.0 - decay) * (down / row_total)
            weighted = jnp.sum(weighted, axis=0, keepdims=True) / cols
            power = power + jnp.sum(weighted, axis=1, keepdims=True)
            if half == 0:
                sums_s[VDP + c] = jnp.broadcast_to(down, (tall, LANES))
    power = power * mean
    down = sums_s[pl.ds(VDP + chip, 1)][0][0:1, :]
    cols_new = decay * cols_0[...] + (1.0 - decay) * (down / row_total)
    cols_out[...] = cols_new
    column = jnp.concatenate(
        [
            jnp.concatenate([rows_new, jnp.zeros((1, LANES - tall), F32)], axis=1),
            jnp.zeros((LANES - 1, LANES), F32),
        ],
        axis=0,
    ).T[:tall, 0:1]
    update_0 = grad_ref[...] * lax.rsqrt(column * cols_new / mean)
    powers = (power, scalar(67), scalar(68))
    for i, (update, weight, new) in enumerate(
        (
            (update_0, weight_0, new_0),
            (update_1[...], weight_1, new_1),
            (update_2[...], weight_2, new_2),
        )
    ):
        entries = float(weight.shape[0] * weight.shape[1] * VDP * fsdp)
        clip = jnp.maximum(1.0, jnp.sqrt(powers[i] / entries) / CLIP_LIMIT)
        rate = STEP_RATE * jnp.maximum(EPS_TWO, jnp.sqrt(scalar(64 + i) / entries))
        new[...] = weight[...] - rate / clip * update
    powers, sizes = [], []
    for d in range(VDP):
        power = jnp.zeros((rows, 1), F32)
        size = jnp.zeros((rows, 1), F32)
        for c in range(VCHIP):
            at = d * VCHIP + c
            first, second = lines_of(mine_ref, at)[0], lines_of(other_ref, at)[0]
            both = first[:, :64] + second[:, :64]
            size = size + first[:, LANES - 1 :] + second[:, LANES - 1 :]
            near = jnp.where(core == 0, first[:, 64 : 64 + width], second[:, 64 : 64 + width])
            far = jnp.where(core == 0, second[:, 64 : 64 + width], first[:, 64 : 64 + width])
            moment = jnp.concatenate([near, far], axis=1)
            moment = decay * moment + (1.0 - decay) * (both * both + EPS_ONE)
            power = power + jnp.sum(both * both / moment, axis=1, keepdims=True)
            wide = jnp.concatenate([both, jnp.zeros((rows, LANES - 64), F32)], axis=1)
            sums_s[2 * VDP + at, :rows, :] = wide
        powers.append(power)
        sizes.append(size)
    both = sums_s[pl.ds(2 * VDP + dp * VCHIP + chip, 1), :rows, :][0]
    vector_grad = jnp.where(core == 0, both[:, :width], both[:, width : 2 * width])
    vector_grad_ref[...] = vector_grad
    moment = decay * moment_ref[...] + (1.0 - decay) * (vector_grad * vector_grad + EPS_ONE)
    moment_out[...] = moment
    step = vector_grad * lax.rsqrt(moment)
    bias = VDP // 2
    bias_power = sum(jnp.sum(power, axis=0, keepdims=True) for power in powers[:bias])
    bias_size = sum(jnp.sum(size, axis=0, keepdims=True) for size in sizes[:bias])
    power, size = powers[bias], sizes[bias]
    for d in range(bias + 1, VDP):
        power = jnp.where(dp == d, powers[d], power)
        size = jnp.where(dp == d, sizes[d], size)
    is_bias = dp < bias
    power = jnp.where(is_bias, bias_power, power)
    size = jnp.where(is_bias, bias_size, size)
    count = jnp.where(is_bias, float(FF), float(D))
    clip = jnp.maximum(1.0, jnp.sqrt(power / count) / CLIP_LIMIT)
    rate = STEP_RATE * jnp.maximum(EPS_TWO, jnp.sqrt(size / count))
    vector_out[...] = vector_ref[...] - rate / clip * step


def whole_call(kernel, name, place, outs, *operands, scratch=(), earlier=None):
    tied = () if earlier is None else (earlier,)
    return pl.pallas_call(
        kernel,
        out_shape=[jax.ShapeDtypeStruct(shape, kind) for shape, kind in outs],
        in_specs=[pl.BlockSpec(memory_space=pltpu.SMEM)]
        + [pl.BlockSpec(memory_space=pl.ANY)] * len(tied)
        + [vspec()] * len(operands),
        out_specs=[vspec()] * len(outs),
        scratch_shapes=list(scratch),
        compiler_params=params(16),
        name=name,
    )(place, *tied, *operands)


def core_swap(block):
    return lax.ppermute(block, "core", [(0, 1), (1, 0)])


def exchange(blocks, axes):
    return lax.all_to_all(blocks, axes, split_axis=0, concat_axis=0, tiled=True)


def after(value, *earlier, mib=8):
    return pl.pallas_call(
        lambda *refs: None,
        out_shape=jax.ShapeDtypeStruct(value.shape, value.dtype),
        in_specs=[pl.BlockSpec(memory_space=pltpu.HBM)] * (1 + len(earlier)),
        out_specs=pl.BlockSpec(memory_space=pltpu.HBM),
        input_output_aliases={0: 0},
        compiler_params=params(mib),
        name="after",
    )(value, *earlier)


def pair_kernel(mine_ref, got_ref, out_ref):
    out_ref[...] = (mine_ref[...].astype(F32) + got_ref[...].astype(F32)).astype(BF16)


def pair_sum(mine, got):
    return pl.pallas_call(
        pair_kernel,
        out_shape=jax.ShapeDtypeStruct(mine.shape, BF16),
        in_specs=[vspec(), vspec()],
        out_specs=vspec(),
        compiler_params=params(16),
        name="pair_sum",
    )(mine, got)


CHIPS = ("dp", "chip")
ALL = ("dp", "chip", "core")


def layer(place, weights, segment_ids, tokens, cotangent, ffn_weights, send_core, send_ffn):
    table = jnp.asarray(encode_table())
    qk, x, qk_t, x_t, back, marks = place_tokens(segment_ids, tokens, cotangent, table)
    query_t, value, key_t, out_t, inverse, mixed, mixed_t, exps, weight, proj, vector = attend_forward(
        marks, place, x, qk, x_t, qk_t, *weights(marks)
    )
    ffn_mine, ffn_other = ffn_weights(marks, vector)
    block_out, resid, grad_t, ffn_mine, ffn_other, proj_g, vector_g = feed_forward(
        marks, place, x, back, mixed, mixed_t, proj, ffn_mine, ffn_other, vector
    )
    ffn_got, grad_t = send_ffn(ffn_mine, ffn_other, grad_t)
    low, grads_own, grads_other, sums = attend_back(
        marks, place, grad_t, query_t, value, key_t, out_t, inverse, exps, qk_t, x_t, proj_g
    )
    attn_got = send_core(grads_other)
    pulled = input_pull(marks, low, weight, resid, block_out)
    return pulled, grads_own, grads_other, attn_got, sums, vector_g, ffn_got


def body(
    tokens,
    cotangent,
    segment_ids,
    attn_weight,
    ffn_in,
    ffn_out,
    vectors,
    attn_rows,
    attn_cols,
    in_rows,
    in_cols,
    out_rows,
    out_cols,
    vector_moment,
):
    place = jnp.stack([lax.axis_index("dp"), lax.axis_index("chip"), lax.axis_index("core")])
    place = place.astype(jnp.int32)
    pieces = VDP * VCHIP
    tall, wide = attn_weight.shape
    rows_v, cols_v = vectors.shape
    split = lambda array: array.reshape((VDP, VCHIP) + array.shape[1:])
    attn_sent, ffn_low = pack_attn(place, attn_weight, ffn_in, ffn_out, vectors)
    attn_mine = exchange(attn_sent, CHIPS)

    parts = [
        lax.ppermute(ffn_low, "dp", [(i, i ^ step) for i in range(VDP)]) for step in range(1, VDP)
    ]
    ffn_sent = pack_ffn(place, ffn_low, parts)

    def attn_weights(marks):
        mine = split(after(attn_mine, marks, *parts))
        return mine, core_swap(mine)

    def ffn_weights(marks, vector):
        got = exchange(after(ffn_sent, marks), "chip")
        ffn_mine = after(got, vector)
        return ffn_mine, core_swap(ffn_mine)

    def send_ffn(mine, other, grad_t):
        both = pair_sum(mine, core_swap(other))
        got = exchange(both.reshape((pieces,) + mine.shape[2:]), CHIPS)
        return got, after(grad_t, both, mib=56)

    (
        pulled,
        grads_own,
        grads_other,
        attn_got,
        sums,
        vector_g,
        ffn_got,
    ) = layer(place, attn_weights, segment_ids, tokens, cotangent, ffn_weights, core_swap, send_ffn)
    lay = lambda stat: stat.reshape(1, -1)
    rows_old = (lay(attn_rows), lay(in_rows), lay(out_rows))
    cols_old = (lay(attn_cols), lay(in_cols), lay(out_cols))
    weights_old = (attn_weight, ffn_in, ffn_out)
    in_grad, out_grad, ffn_grad, stat = whole_call(
        tail_ffn_kernel,
        "tail_ffn",
        place,
        [(ffn_in.shape, F32), (ffn_out.shape, F32), ((2,) + ffn_in.shape, F32), ((8, LANES), F32)],
        ffn_got,
        *rows_old[1:],
        sums,
    )
    stat_other = core_swap(stat)
    (sent,) = whole_call(
        tail_send_kernel,
        "tail_send",
        place,
        [((pieces, tall + VROWS, LANES), BF16)],
        grads_own,
        attn_got,
        vector_g,
        sums,
        stat,
        stat_other,
    )
    block_out, input_grad, token = pulled
    got = exchange(sent, CHIPS)
    attn_grad, update_1, update_2, rows_new_1, rows_new_2, cols_new_1, cols_new_2, sent = whole_call(
        tail_reduce_kernel,
        "tail_reduce",
        place,
        [
            (attn_weight.shape, F32),
            (ffn_in.shape, F32),
            (ffn_out.shape, F32),
            (rows_old[1].shape, F32),
            (rows_old[2].shape, F32),
            (cols_old[1].shape, F32),
            (cols_old[2].shape, F32),
            ((pieces, tall + VROWS, LANES), BF16),
        ],
        got,
        ffn_grad,
        *weights_old,
        *rows_old,
        *cols_old,
        vectors,
        vector_moment,
        earlier=token,
    )
    mine = exchange(sent, CHIPS)
    attn_new, in_new, out_new, rows_new_0, cols_new_0, vector_grad, moment_new, vectors_new = whole_call(
        tail_apply_kernel,
        "tail_apply",
        place,
        [
            (attn_weight.shape, F32),
            (ffn_in.shape, F32),
            (ffn_out.shape, F32),
            (rows_old[0].shape, F32),
            (cols_old[0].shape, F32),
            (vectors.shape, F32),
            (vectors.shape, F32),
            (vectors.shape, F32),
        ],
        mine,
        core_swap(mine),
        attn_grad,
        update_1,
        update_2,
        *weights_old,
        rows_old[0],
        cols_old[0],
        vectors,
        vector_moment,
        scratch=[
            pltpu.VMEM((2 * VDP + pieces, tall, LANES), F32),
            pltpu.VMEM((LANES, tall), F32),
        ],
    )
    return (
        block_out,
        input_grad,
        attn_grad,
        in_grad,
        out_grad,
        vector_grad,
        rows_new_0.reshape(-1),
        cols_new_0.reshape(-1),
        rows_new_1.reshape(-1),
        cols_new_1.reshape(-1),
        rows_new_2.reshape(-1),
        cols_new_2.reshape(-1),
        moment_new,
        attn_new,
        in_new,
        out_new,
        vectors_new,
    )


def gather_all(block):
    shape = (lax.axis_size("dp"), lax.axis_size("chip") * 2)
    count = shape[0] * shape[1]
    got = exchange(jnp.broadcast_to(block[None], (count,) + block.shape), ALL)
    return got.reshape(shape + block.shape)


def unblock(parts):
    dp_count, fsdp_count, rows, cols = parts.shape
    return parts.transpose(0, 2, 1, 3).reshape(dp_count * rows, fsdp_count * cols)


def scatter_sum(full):
    dp_count = lax.axis_size("dp")
    fsdp_count = lax.axis_size("chip") * 2
    rows, cols = full.shape
    by_col = full.astype(BF16).reshape(rows, fsdp_count, cols // fsdp_count).transpose(1, 0, 2)
    got = exchange(by_col, ("chip", "core"))
    part = jnp.sum(got.astype(F32), axis=0).astype(BF16)
    by_row = part.reshape(dp_count, rows // dp_count, cols // fsdp_count)
    return jnp.sum(exchange(by_row, "dp").astype(F32), axis=0)


def body_any(
    tokens,
    cotangent,
    segment_ids,
    attn_weight,
    ffn_in,
    ffn_out,
    vectors,
    attn_rows,
    attn_cols,
    in_rows,
    in_cols,
    out_rows,
    out_cols,
    vector_moment,
):
    dp_count = lax.axis_size("dp")
    fsdp_count = lax.axis_size("chip") * 2
    dp_place = lax.axis_index("dp")
    fsdp_place = lax.axis_index("chip") * 2 + lax.axis_index("core")
    rows_w = attn_weight.shape[0]
    rows_v = vectors.shape[0]
    place = jnp.zeros((3,), jnp.int32)
    full_attn = unblock(gather_all(attn_weight.astype(BF16)))
    full_vector = unblock(gather_all(vectors.astype(BF16)))
    full_ffn = jnp.stack(
        [unblock(gather_all(ffn_in.astype(BF16))), unblock(gather_all(ffn_out.astype(BF16)))]
    )
    tall = D // VDP
    cut = full_attn.reshape(VDP, tall, VCHIP, 2, LANES).transpose(3, 0, 2, 1, 4)
    lines = full_vector.reshape(VDP, VEC // VDP, 2, LANES).transpose(0, 2, 1, 3)
    lines = lines.reshape(VDP, 1, 2 * VEC // VDP, LANES)
    lines = jnp.pad(lines, ((0, 0), (0, VCHIP - 1), (0, VROWS - 2 * VEC // VDP), (0, 0)))
    weights = (
        jnp.concatenate([cut[0], lines], axis=2),
        jnp.concatenate([cut[1], jnp.zeros_like(lines)], axis=2),
    )
    ffn_cut = full_ffn.reshape(2, VDP, tall, VCHIP, 2, FF // (2 * VCHIP))
    ffn_cut = ffn_cut.transpose(4, 3, 1, 0, 2, 5)
    (
        pulled,
        grads_own,
        grads_other,
        _,
        sums,
        vector_g,
        ffn_got,
    ) = layer(
        place,
        lambda marks: weights,
        segment_ids,
        tokens,
        cotangent,
        lambda marks, vector: (ffn_cut[0], ffn_cut[1]),
        lambda block: block,
        lambda mine, other, grad_t: (jnp.stack([mine, other]), grad_t),
    )
    block_out, input_grad, _ = pulled
    attn_full = jnp.stack([grads_own, grads_other]).transpose(1, 3, 2, 0, 4).reshape(D, 4 * D)
    ffn_full = ffn_got.transpose(3, 1, 4, 2, 0, 5).reshape(2, D, FF)
    sums = jnp.concatenate([sums[0, :2], sums[1, :2]], axis=1)
    vector_full = jnp.concatenate([vector_g[:8], sums, vector_g[10:]], axis=0)
    attn_grad = scatter_sum(attn_full)
    in_grad = scatter_sum(ffn_full[0])
    out_grad = scatter_sum(ffn_full[1])
    vector_grad = scatter_sum(vector_full)

    decay = 1.0 - STEP ** (-0.8)
    gradients = (attn_grad, in_grad, out_grad)
    weights_old = (attn_weight, ffn_in, ffn_out)
    rows_old = (attn_rows, in_rows, out_rows)
    cols_old = (attn_cols, in_cols, out_cols)
    moment_new = decay * vector_moment + (1.0 - decay) * (vector_grad * vector_grad + EPS_ONE)
    vector_step = vector_grad * lax.rsqrt(moment_new)
    squares = [gradient * gradient + EPS_ONE for gradient in gradients]
    pieces = []
    for square in squares:
        pieces.append(jnp.sum(square, axis=1))
    for square in squares:
        pieces.append(jnp.sum(square, axis=0))
    pieces.append(jnp.sum(vector_step * vector_step, axis=1))
    pieces.append(jnp.sum(vectors * vectors, axis=1))
    pieces.append(jnp.stack([jnp.sum(weight * weight) for weight in weights_old]))
    pieces.append(jnp.stack([jnp.sum(old) for old in rows_old]))
    sizes = [piece.shape[0] for piece in pieces]
    flat = jnp.concatenate(pieces)
    flat = jnp.pad(flat, (0, -flat.shape[0] % 1024)).reshape(-1, LANES)
    got = gather_all(flat).reshape(dp_count, fsdp_count, -1)
    offsets = [0]
    for length in sizes:
        offsets.append(offsets[-1] + length)
    take = lambda i: got[:, :, offsets[i] : offsets[i + 1]]
    rows_new, cols_new, row_means, entries = [], [], [], []
    for i in range(3):
        count_rows = rows_w * dp_count
        count_cols = weights_old[i].shape[1] * fsdp_count
        entries.append(float(count_rows * count_cols))
        row_all = jnp.sum(take(i), axis=1)
        mine = lax.dynamic_index_in_dim(row_all, dp_place, 0, keepdims=False)
        rows_new.append(decay * rows_old[i] + (1.0 - decay) * mine / count_cols)
        col_all = jnp.sum(take(3 + i), axis=0)
        mine = lax.dynamic_index_in_dim(col_all, fsdp_place, 0, keepdims=False)
        cols_new.append(decay * cols_old[i] + (1.0 - decay) * mine / count_rows)
        old_total = jnp.sum(take(9)[:, 0, i])
        row_means.append(
            (decay * old_total + (1.0 - decay) * jnp.sum(row_all) / count_cols) / count_rows
        )
    step_rows = jnp.sum(take(6), axis=1).reshape(-1)
    weight_rows = jnp.sum(take(7), axis=1).reshape(-1)
    weight_totals = jnp.sum(take(8), axis=(0, 1))
    updates = []
    for i in range(3):
        second = rows_new[i][:, None] * cols_new[i][None, :] / row_means[i]
        updates.append(gradients[i] * lax.rsqrt(second))
    flat = jnp.stack([jnp.sum(update * update) for update in updates])
    flat = jnp.broadcast_to(jnp.pad(flat, (0, 5))[:, None], (8, LANES))
    totals = jnp.sum(gather_all(flat)[:, :, :, 0], axis=(0, 1))
    new_weights = []
    for i in range(3):
        clip_factor = jnp.maximum(1.0, jnp.sqrt(totals[i] / entries[i]) / CLIP_LIMIT)
        step_size = STEP_RATE * jnp.maximum(EPS_TWO, jnp.sqrt(weight_totals[i] / entries[i]))
        new_weights.append(weights_old[i] - step_size / clip_factor * updates[i])
    bias_rows = FF // D
    row_places = jnp.arange(VEC)
    counts = jnp.where(row_places < bias_rows, float(FF), float(D))
    grouped_updates = jnp.where(row_places < bias_rows, jnp.sum(step_rows[:bias_rows]), step_rows)
    grouped_weights = jnp.where(row_places < bias_rows, jnp.sum(weight_rows[:bias_rows]), weight_rows)
    clip_rows = jnp.maximum(1.0, jnp.sqrt(grouped_updates / counts) / CLIP_LIMIT)
    step_sizes = STEP_RATE * jnp.maximum(EPS_TWO, jnp.sqrt(grouped_weights / counts))
    factor_rows = lax.dynamic_slice_in_dim(step_sizes / clip_rows, dp_place * rows_v, rows_v)
    vectors_new = vectors - factor_rows[:, None] * vector_step
    return (
        block_out,
        input_grad,
        attn_grad,
        in_grad,
        out_grad,
        vector_grad,
        rows_new[0],
        cols_new[0],
        rows_new[1],
        cols_new[1],
        rows_new[2],
        cols_new[2],
        moment_new,
        new_weights[0],
        new_weights[1],
        new_weights[2],
        vectors_new,
    )


def solution(mesh):
    dp_count, fsdp_count = mesh.shape["dp"], mesh.shape["fsdp"]
    inner = jax.sharding.Mesh(mesh.devices.reshape(dp_count, fsdp_count // 2, 2), ALL)
    fsdp = ("chip", "core")
    split = P(ALL, None)
    block = P("dp", fsdp)
    stats = (P("dp"), P(fsdp)) * 3
    plain = dp_count == VDP and fsdp_count == 2 * VCHIP
    return jax.shard_map(
        body if plain else body_any,
        mesh=inner,
        in_specs=(split,) * 3 + (block,) * 4 + stats + (block,),
        out_specs=(split,) * 2 + (block,) * 4 + stats + (block,) * 5,
        check_vma=False,
    )
```

```python
import functools
import math

import jax
import jax.numpy as jnp
import numpy as np
from jax import lax
from jax.experimental import pallas as pl
from jax.experimental.pallas import tpu as pltpu
from jax.sharding import PartitionSpec as P

D = 256
FF = 2048
HEADS = 8
HEAD_DIM = 32
SEQ = 1024
HALF = 512
GROUP = 4
LANES = 128
QBLOCK = 512
WGRID = 32
STEP = 10
VEC = 16
TILE = 1024
CHUNK = 256
SUB = 512
LEAD = 5
STRIP = 64
VDP = 4
VCHIP = 4
VROWS = 16

EPS_NORM = 1e-05
EPS_ONE = 1e-30
EPS_TWO = 0.001
CLIP_LIMIT = 1.0
STEP_RATE = 0.3
FAR = 1e30
TAME = 40.0
LOG2_E = math.log2(math.e)
SCALE = HEAD_DIM ** (-0.5)
GELU_A = math.sqrt(2.0 / math.pi)
GELU_B = 0.044715
F32 = jnp.float32
BF16 = jnp.bfloat16
MIB = 1024 * 1024


def dot(left, right):
    return jnp.dot(left, right, preferred_element_type=F32)


def dot_nt(left, right):
    return lax.dot_general(left, right, (((1,), (1,)), ((), ())), preferred_element_type=F32)


def encode_table():
    half = D // 2
    feature = np.arange(half)
    freq = np.exp(
        (2 * (feature // 2)).astype(np.float32) * np.float32(-math.log(10000.0) / half)
    ).astype(np.float32)
    angles = np.arange(1, WGRID + 1, dtype=np.float32)[:, None] * freq[None, :]
    table = np.where(feature % 2 == 0, np.sin(angles), np.cos(angles)).astype(np.float32)
    low = jnp.bfloat16
    one = table.astype(low)
    rest = table - one.astype(np.float32)
    two = rest.astype(low)
    three = (rest - two.astype(np.float32)).astype(low)
    blank = np.zeros((LANES - 3 * WGRID, half), low)
    return np.concatenate([one, two, three, blank], axis=0)


def iota(shape, dim):
    return lax.broadcasted_iota(jnp.int32, shape, dim)


def norm_forward(rows):
    centered = rows - jnp.mean(rows, axis=-1, keepdims=True)
    inverse = lax.rsqrt(jnp.mean(centered * centered, axis=-1, keepdims=True) + EPS_NORM)
    return centered * inverse, inverse


def norm_backward(upstream, normed, inverse):
    return inverse * (
        upstream
        - jnp.mean(upstream, axis=-1, keepdims=True)
        - normed * jnp.mean(upstream * normed, axis=-1, keepdims=True)
    )

def vspec():
    return pl.BlockSpec(memory_space=pltpu.VMEM)


def params(mib=56, **more):
    return pltpu.CompilerParams(vmem_limit_bytes=mib * MIB, **more)


def pack_kernel(place, attn_ref, first_ref, second_ref, vector_ref, out_ref, ffn_ref):
    owner = place[1] * 2 + place[2]
    vector = vector_ref[...]
    rows = vector.shape[0]
    wide = jnp.concatenate([vector] * (LANES // vector.shape[1]), axis=1)
    slot = iota((rows, LANES), 1) // vector.shape[1]
    per = LANES // vector.shape[1]
    parts = [attn_ref[...]]
    for half in range(2):
        parts.append(jnp.where(slot + half * per == owner, wide, 0.0))
    parts.append(jnp.zeros((VROWS - 2 * rows, LANES), F32))
    piece = jnp.concatenate(parts, axis=0).astype(BF16)
    for at in range(VDP * VCHIP):
        out_ref[at] = piece
    ffn_ref[0] = first_ref[...].astype(BF16)
    ffn_ref[1] = second_ref[...].astype(BF16)


def pack_attn(place, attn_weight, ffn_in, ffn_out, vectors):
    return pl.pallas_call(
        pack_kernel,
        out_shape=(
            jax.ShapeDtypeStruct((VDP * VCHIP, attn_weight.shape[0] + VROWS, LANES), BF16),
            jax.ShapeDtypeStruct((2,) + ffn_in.shape, BF16),
        ),
        in_specs=[pl.BlockSpec(memory_space=pltpu.SMEM)] + [vspec()] * 4,
        out_specs=(vspec(), vspec()),
        compiler_params=params(),
        name="pack_attn",
    )(place, attn_weight, ffn_in, ffn_out, vectors)


def pack_ffn_kernel(place, own_ref, *refs):
    out_ref = refs[-1]
    for at in range(VCHIP):
        out_ref[at, pl.ds(place[0], 1)] = own_ref[...][None]
        for step in range(1, VDP):
            out_ref[at, pl.ds(place[0] ^ step, 1)] = refs[step - 1][...][None]


def pack_ffn(place, own, parts):
    return pl.pallas_call(
        pack_ffn_kernel,
        out_shape=jax.ShapeDtypeStruct((VCHIP, VDP) + own.shape, BF16),
        in_specs=[pl.BlockSpec(memory_space=pltpu.SMEM)] + [vspec()] * (1 + len(parts)),
        out_specs=vspec(),
        compiler_params=params(16),
        name="pack_ffn",
    )(place, own, *parts)


def place_kernel(
    segment_ref, tokens_ref, back_ref, table_ref, qk_ref, x_ref, qk_t_ref, x_t_ref, turned_ref, marks_ref
):
    row = pl.program_id(0)
    starts = []
    for number in range(1, 4):
        at = jnp.int32(0)
        for step in (512, 256, 128, 64, 32, 16, 8, 4, 2, 1, 1):
            probe = jnp.minimum(at + (step - 1), SEQ - 1)
            at = jnp.where(segment_ref[row, probe] < number, at + step, at)
        starts.append(at)
    edges = [jnp.int32(0)] + starts + [jnp.int32(SEQ)]
    begin = jnp.int32(0)
    for number in range(3, -1, -1):
        begin = jnp.where(edges[number + 1] - edges[number] == HALF, edges[number], begin)
    for number in range(3):
        marks_ref[row, number] = starts[number]
    marks_ref[row, 3] = begin
    one, two, three = starts
    x = pltpu.roll(tokens_ref[...].astype(F32), (SEQ - begin) & (SEQ - 1), 0)
    x_ref[...] = x.astype(BF16)
    x_t_ref[...] = x.T.astype(BF16)
    back = back_ref[...].astype(F32)
    turned_ref[...] = pltpu.roll(back, (SEQ - begin) & (SEQ - 1), 0).astype(BF16)
    at = (iota((SEQ, LANES), 0) + begin) & (SEQ - 1)
    lane = iota((SEQ, LANES), 1)
    start = jnp.where(at >= three, three, jnp.where(at >= two, two, jnp.where(at >= one, one, 0)))
    local = at - start
    kept = lane < 3 * WGRID
    slot = lane & (WGRID - 1)
    hot_r = jnp.where(((local >> 5) == slot) & kept, 1.0, 0.0).astype(BF16)
    hot_c = jnp.where(((local & (WGRID - 1)) == slot) & kept, 1.0, 0.0).astype(BF16)
    table = table_ref[...]
    places = jnp.concatenate([dot(hot_r, table), dot(hot_c, table)], axis=1)
    qk = x + places
    qk_ref[...] = qk.astype(BF16)
    qk_t_ref[...] = qk.T.astype(BF16)


def place_tokens(segment_ids, tokens, cotangent, table):
    rows = segment_ids.shape[0]
    by_row = lambda r: (r, 0)
    return pl.pallas_call(
        place_kernel,
        out_shape=(
            jax.ShapeDtypeStruct(tokens.shape, BF16),
            jax.ShapeDtypeStruct(tokens.shape, BF16),
            jax.ShapeDtypeStruct((D, tokens.shape[0]), BF16),
            jax.ShapeDtypeStruct((D, tokens.shape[0]), BF16),
            jax.ShapeDtypeStruct(tokens.shape, BF16),
            jax.ShapeDtypeStruct((rows, 4), jnp.int32),
        ),
        grid=(rows,),
        in_specs=[
            pl.BlockSpec(memory_space=pltpu.SMEM),
            pl.BlockSpec((SEQ, D), by_row),
            pl.BlockSpec((SEQ, D), by_row),
            pl.BlockSpec((LANES, LANES), lambda r: (0, 0)),
        ],
        out_specs=(
            pl.BlockSpec((SEQ, D), by_row),
            pl.BlockSpec((SEQ, D), by_row),
            pl.BlockSpec((D, SEQ), lambda r: (0, r)),
            pl.BlockSpec((D, SEQ), lambda r: (0, r)),
            pl.BlockSpec((SEQ, D), by_row),
            pl.BlockSpec(memory_space=pltpu.SMEM),
        ),
        compiler_params=params(dimension_semantics=("arbitrary",)),
        cost_estimate=pl.CostEstimate(flops=600_000_000, bytes_accessed=4_000_000, transcendentals=0),
        name="place_tokens",
    )(segment_ids, tokens, cotangent, table)


def attend_kernel(
    marks,
    place,
    x_ref,
    qk_ref,
    x_t_ref,
    qk_t_ref,
    mine_ref,
    other_ref,
    query_t_ref,
    value_ref,
    key_t_ref,
    out_t_ref,
    inverse_ref,
    mixed_ref,
    mixed_t_ref,
    exps_ref,
    weight_ref,
    proj_ref,
    vector_ref,
    key_s,
    value_s,
    mark_k,
    mark_q,
    first_s,
    second_s,
    weight_t_s,
    bias_s,
    tame_s,
    exps_s,
    exps_sem,
):
    row = pl.program_id(0)
    begin = marks[row, 3]
    core = place[2]

    def copy_of(group, half):
        return pltpu.make_async_copy(
            exps_s.at[group, half], exps_ref.at[row, group, half], exps_sem.at[group * 2 + half]
        )

    @pl.when(row == 0)
    def _():
        tall = D // VDP
        for d in range(VDP):
            rows = slice(d * tall, (d + 1) * tall)
            total = jnp.zeros((8, LANES), F32)
            for c in range(VCHIP):
                for ref, half in ((mine_ref, core), (other_ref, 1 - core)):
                    if c < 3:
                        to = pl.ds(pl.multiple_of(c * D + half * LANES, LANES), LANES)
                        weight_ref[rows, to] = ref[d, c, :tall, :]
                    else:
                        to = pl.ds(pl.multiple_of(half * LANES, LANES), LANES)
                        proj_ref[rows, to] = ref[d, c, :tall, :]
                    total += ref[d, c, tall:, :].astype(F32)[:8]
            vector_ref[d * 4 : (d + 1) * 4, :LANES] = total[:4]
            vector_ref[d * 4 : (d + 1) * 4, LANES:] = total[4:]
        weight_t_s[...] = weight_ref[...].astype(F32).T.astype(BF16)
        bias_s[...] = vector_ref[8:16, :].T

    qk_t = qk_t_ref[...]
    query_t = (dot(weight_t_s[:D, :], qk_t) + bias_s[:, 0:1]) * SCALE
    query_t = query_t.astype(BF16)
    query_t_ref[...] = query_t
    key_t = dot(weight_t_s[D : 2 * D, :], qk_t).astype(BF16)
    key_t_ref[...] = key_t

    def largest_norms(rows):
        rows = rows.astype(F32)
        rows = rows * rows
        sums = [
            jnp.sum(rows[head * HEAD_DIM : (head + 1) * HEAD_DIM], axis=0, keepdims=True)
            for head in range(HEADS)
        ]
        return jnp.max(jnp.concatenate(sums, axis=0), axis=1, keepdims=True)

    bound = jnp.max(largest_norms(query_t) * largest_norms(key_t))
    tame_s[0] = jnp.where(bound <= TAME * TAME, 1, 0)
    key_s[...] = dot(qk_ref[...], weight_ref[:, D : 2 * D]).astype(BF16)
    value = dot(x_ref[...], weight_ref[:, 2 * D : 3 * D]) + vector_ref[9:10, :]
    value_ref[...] = value.astype(BF16)
    value_t = dot(weight_t_s[2 * D :, :], x_t_ref[...]) + bias_s[:, 1:2]
    value_t = value_t.astype(BF16)
    for head in range(HEADS):
        value_s[head, :HEAD_DIM, :] = value_t[head * HEAD_DIM : (head + 1) * HEAD_DIM, :]
        value_s[head, HEAD_DIM:, :] = jnp.ones((16, SEQ), BF16)
    one, two, three = marks[row, 0], marks[row, 1], marks[row, 2]

    def number_of(shape, dim):
        here = (iota(shape, dim) + (HALF + begin)) & (SEQ - 1)
        return (
            jnp.where(here >= one, 1, 0)
            + jnp.where(here >= two, 1, 0)
            + jnp.where(here >= three, 1, 0)
        )

    lane = iota((HALF, LANES), 1)
    number = number_of((HALF, LANES), 0)
    mark_k[...] = jnp.where((number != lane) & (lane < 4), -FAR, 0.0).astype(BF16)
    number = number_of((LANES, HALF), 1)
    mark_q[...] = jnp.where(number == iota((LANES, HALF), 0), 1.0, 0.0).astype(BF16)

    head_of = iota((1, LANES), 1) // HEAD_DIM
    for group in range(2):
        keys_here = key_s[:, group * LANES : (group + 1) * LANES]
        for at_head in range(GROUP):
            mask = jnp.where(head_of == at_head, 1.0, 0.0).astype(BF16)
            rows = slice(at_head * HALF, (at_head + 1) * HALF)
            first_s[group, rows, :] = keys_here[:HALF] * mask
            second_s[group, rows, :LANES] = keys_here[HALF:] * mask
            second_s[group, rows, LANES:] = mark_k[...]

    @pl.when(row > 0)
    def _():
        for group in range(2):
            for half in range(2):
                copy_of(group, half).wait()

    def scores_of(group, half, rows):
        query = query_t_ref[group * LANES : (group + 1) * LANES, half * HALF : (half + 1) * HALF]
        if half == 0:
            return dot(first_s[group, rows, :], query)
        return dot(second_s[group, rows, :], jnp.concatenate([query, mark_q[...]], axis=0))

    def place_of(at_head):
        return slice(at_head * HALF, (at_head + 1) * HALF)

    def exps_plain(group, half):
        scores = scores_of(group, half, slice(0, GROUP * HALF))
        for at_head in range(GROUP):
            exps = jnp.exp2(scores[place_of(at_head), :] * LOG2_E)
            exps_s[group, half, :, place_of(at_head)] = exps.astype(BF16)

    def exps_shifted(group, half):
        for at_head in range(GROUP):
            rows = place_of(at_head)
            largest = jnp.max(scores_of(group, half, rows), axis=0, keepdims=True)
            exps = jnp.exp2((scores_of(group, half, rows) - largest) * LOG2_E)
            exps_s[group, half, :, rows] = exps.astype(BF16)

    def finish(group, half):
        rows = slice(half * HALF, (half + 1) * HALF)
        for at_head in range(GROUP):
            head = group * GROUP + at_head
            out = dot(value_s[head, :, rows], exps_s[group, half, :, place_of(at_head)])
            inverse = 1.0 / out[HEAD_DIM : HEAD_DIM + 1, :]
            inverse_ref[group, at_head : at_head + 1, rows] = inverse
            out_t_ref[head * HEAD_DIM : (head + 1) * HEAD_DIM, rows] = out[:HEAD_DIM, :] * inverse

    def run(exps_of):
        items = [(group, half) for group in range(2) for half in range(2)]
        for i in range(len(items) + 1):
            if i < len(items):
                exps_of(*items[i])
                copy_of(*items[i]).start()
            if i >= 1:
                finish(*items[i - 1])

    @pl.when(tame_s[0] == 1)
    def _():
        run(exps_plain)

    @pl.when(tame_s[0] == 0)
    def _():
        run(exps_shifted)

    out_t = out_t_ref[...]
    mixed_t_ref[...] = out_t.astype(BF16)
    mixed_ref[...] = out_t.T.astype(BF16)

    @pl.when(row == pl.num_programs(0) - 1)
    def _():
        for group in range(2):
            for half in range(2):
                copy_of(group, half).wait()


def attend_forward(marks, place, x, qk, x_t, qk_t, mine, other):
    total = x.shape[0]
    rows = total // SEQ
    by_row = lambda r, m, p: (r, 0)
    by_col = lambda r, m, p: (0, r)
    whole = lambda r, m, p: (0, 0)
    return pl.pallas_call(
        attend_kernel,
        out_shape=(
            jax.ShapeDtypeStruct((D, total), BF16),
            jax.ShapeDtypeStruct((total, D), BF16),
            jax.ShapeDtypeStruct((D, total), BF16),
            jax.ShapeDtypeStruct((D, total), F32),
            jax.ShapeDtypeStruct((2, 8, total), F32),
            jax.ShapeDtypeStruct((total, D), BF16),
            jax.ShapeDtypeStruct((D, total), BF16),
            jax.ShapeDtypeStruct((rows, 2, 2, HALF, GROUP * HALF), BF16),
            jax.ShapeDtypeStruct((D, 3 * D), BF16),
            jax.ShapeDtypeStruct((D, D), BF16),
            jax.ShapeDtypeStruct((VEC, D), F32),
        ),
        grid_spec=pltpu.PrefetchScalarGridSpec(
            num_scalar_prefetch=2,
            grid=(rows,),
            in_specs=[
                pl.BlockSpec((SEQ, D), by_row),
                pl.BlockSpec((SEQ, D), by_row),
                pl.BlockSpec((D, SEQ), by_col),
                pl.BlockSpec((D, SEQ), by_col),
                vspec(),
                vspec(),
            ],
            out_specs=[
                pl.BlockSpec((D, SEQ), by_col),
                pl.BlockSpec((SEQ, D), by_row),
                pl.BlockSpec((D, SEQ), by_col),
                pl.BlockSpec((D, SEQ), by_col),
                pl.BlockSpec((2, 8, SEQ), lambda r, m, p: (0, 0, r)),
                pl.BlockSpec((SEQ, D), by_row),
                pl.BlockSpec((D, SEQ), by_col),
                pl.BlockSpec(memory_space=pl.ANY),
                pl.BlockSpec((D, 3 * D), whole),
                pl.BlockSpec((D, D), whole),
                pl.BlockSpec((VEC, D), whole),
            ],
            scratch_shapes=[
                pltpu.VMEM((SEQ, D), BF16),
                pltpu.VMEM((HEADS, HEAD_DIM + 16, SEQ), BF16),
                pltpu.VMEM((HALF, LANES), BF16),
                pltpu.VMEM((LANES, HALF), BF16),
                pltpu.VMEM((2, GROUP * HALF, LANES), BF16),
                pltpu.VMEM((2, GROUP * HALF, 2 * LANES), BF16),
                pltpu.VMEM((3 * D, D), BF16),
                pltpu.VMEM((D, 8), F32),
                pltpu.SMEM((1,), jnp.int32),
                pltpu.VMEM((2, 2, HALF, GROUP * HALF), BF16),
                pltpu.SemaphoreType.DMA((4,)),
            ],
        ),
        compiler_params=params(dimension_semantics=("arbitrary",)),
        cost_estimate=pl.CostEstimate(
            flops=20_000_000_000, bytes_accessed=30_000_000, transcendentals=8_400_000
        ),
        name="attend_forward",
    )(marks, place, x, qk, x_t, qk_t, mine, other)


def feed_kernel(
    marks,
    place,
    x_ref,
    back_ref,
    mixed_ref,
    mixed_t_ref,
    proj_ref,
    mine_ref,
    other_ref,
    vector_ref,
    block_ref,
    resid_ref,
    mixed_grad_ref,
    mine_out,
    other_out,
    proj_out,
    vector_out,
    first_w,
    second_w,
    first_acc,
    second_acc,
    proj_acc,
    vector_acc,
    hidden_s,
    slope_s,
    pre_s,
    first_low_s,
    branch_low_s,
    attended_s,
    eye_s,
):
    step = pl.program_id(0)
    core = place[2]
    tall = D // VDP
    wide = FF // (2 * VCHIP)

    @pl.when(step == 0)
    def _():
        first_acc[...] = jnp.zeros_like(first_acc)
        second_acc[...] = jnp.zeros_like(second_acc)
        proj_acc[...] = jnp.zeros_like(proj_acc)
        vector_acc[...] = jnp.zeros_like(vector_acc)
        eye_s[...] = jnp.where(iota((D, D), 0) == iota((D, D), 1), 1.0, 0.0).astype(BF16)
        for d in range(VDP):
            rows = slice(d * tall, (d + 1) * tall)
            for c in range(VCHIP):
                for ref, half in ((mine_ref, core), (other_ref, 1 - core)):
                    to = pl.ds(pl.multiple_of((2 * c + half) * wide, wide), wide)
                    first_w[rows, to] = ref[c, d, 0]
                    second_w[rows, to] = ref[c, d, 1]

    bias_o, bias_2 = vector_ref[10:11, :], vector_ref[11:12, :]
    gain_1, shift_1 = vector_ref[12:13, :], vector_ref[13:14, :]
    gain_2, shift_2 = vector_ref[14:15, :], vector_ref[15:16, :]
    chunks = FF // CHUNK
    pair = 2

    def columns(at, count=1):
        return slice(at * CHUNK, (at + count) * CHUNK)

    def hidden_of(rows, at, pre):
        per = CHUNK // D
        bias = [vector_ref[at * per + i : at * per + i + 1, :] for i in range(per)]
        pre = (pre + jnp.concatenate(bias, axis=1)).astype(BF16)
        cube = BF16(GELU_A * GELU_B) * (pre * pre)
        gate = BF16(0.5) + BF16(0.5) * jnp.tanh(pre * (cube + BF16(GELU_A)))
        hidden_s[rows, columns(at)] = pre * gate
        slope_s[rows, columns(at)] = gate + (gate - gate * gate) * (
            pre * (BF16(6.0) * cube + BF16(2.0 * GELU_A))
        )

    def stages(sub):
        rows_at = sub * SUB
        rows = slice(rows_at, rows_at + SUB)
        attended = dot(mixed_ref[rows, :], proj_ref[...]) + bias_o
        norm_1, inverse_1 = norm_forward(x_ref[rows, :].astype(F32) + attended)
        first = norm_1 * gain_1 + shift_1
        first_low = first.astype(BF16)
        first_low_s[rows, :] = first_low
        yield
        branch = jnp.zeros((SUB, D), F32)
        for i in range(chunks + 1):
            if i < chunks:
                hidden_of(rows, i, dot(first_low, first_w[:, columns(i)]))
            if i >= pair and i % pair == 0:
                cols = columns(i - pair, pair)
                branch += dot_nt(hidden_s[rows, cols], second_w[:, cols])
            yield
        norm_2, inverse_2 = norm_forward(first + (branch + bias_2))
        block_ref[rows, :] = norm_2 * gain_2 + shift_2
        back = back_ref[rows, :].astype(F32)
        vector_acc[14:15, :] += jnp.sum(back * norm_2, axis=0, keepdims=True)
        vector_acc[15:16, :] += jnp.sum(back, axis=0, keepdims=True)
        resid_2 = norm_backward(back * gain_2, norm_2, inverse_2)
        branch_low = resid_2.astype(BF16)
        branch_low_s[rows, :] = branch_low
        vector_acc[11:12, :] += jnp.sum(branch_low.astype(F32), axis=0, keepdims=True)
        yield
        first_back = resid_2
        if sub == 1:
            branch_t = dot_nt(eye_s[...], branch_low_s[...]).astype(BF16)
            first_t = dot_nt(eye_s[...], first_low_s[...]).astype(BF16)
            first_t = jnp.concatenate([first_t, jnp.ones((16, TILE), BF16)], axis=0)
        for i in range(chunks + 1):
            if i < chunks:
                pull = dot(branch_low, second_w[:, columns(i)]).astype(BF16)
                pre_s[rows, columns(i)] = pull * slope_s[rows, columns(i)]
                if sub == 1:
                    second_acc[:, columns(i)] += dot(branch_t, hidden_s[:, columns(i)])
            if i >= 1 and sub == 1:
                cols = columns(i - 1)
                first_acc[:, cols] += dot(first_t, pre_s[:, cols])
            if i >= pair and i % pair == 0:
                cols = columns(i - pair, pair)
                first_back += dot_nt(pre_s[rows, cols], first_w[:, cols])
            yield
        vector_acc[12:13, :] += jnp.sum(first_back * norm_1, axis=0, keepdims=True)
        vector_acc[13:14, :] += jnp.sum(first_back, axis=0, keepdims=True)
        resid_1 = norm_backward(first_back * gain_1, norm_1, inverse_1)
        resid_ref[rows, :] = resid_1
        attended_low = resid_1.astype(BF16)
        attended_s[rows, :] = attended_low
        vector_acc[10:11, :] += jnp.sum(attended_low.astype(F32), axis=0, keepdims=True)
        mixed_grad_ref[:, rows] = dot_nt(proj_ref[...], attended_low).astype(BF16)
        yield

    ahead, behind = stages(0), stages(1)
    for _ in range(LEAD):
        next(ahead)
    running = [ahead, behind]
    while running:
        for program in list(running):
            if next(program, 0) == 0:
                running.remove(program)
    proj_acc[...] += dot(mixed_t_ref[...], attended_s[...])

    @pl.when(step == pl.num_programs(0) - 1)
    def _():
        for d in range(VDP):
            rows = slice(d * tall, (d + 1) * tall)
            for c in range(VCHIP):
                for ref, half in ((mine_out, core), (other_out, 1 - core)):
                    to = pl.ds(pl.multiple_of((2 * c + half) * wide, wide), wide)
                    ref[d, c, 0] = first_acc[rows, to].astype(BF16)
                    ref[d, c, 1] = second_acc[rows, to].astype(BF16)
        proj_out[...] = proj_acc[...]
        for at in range(FF // D):
            vector_out[at : at + 1, :] = first_acc[D : D + 1, at * D : (at + 1) * D]
        vector_out[FF // D :, :] = vector_acc[FF // D :, :]


def feed_forward(marks, place, x, back, mixed, mixed_t, proj, mine, other, vector):
    total = x.shape[0]
    tile = lambda i, m, p: (i, 0)
    by_col = lambda i, m, p: (0, i)
    whole = lambda i, m, p: (0, 0)
    whole5 = lambda i, m, p: (0, 0, 0, 0, 0)
    return pl.pallas_call(
        feed_kernel,
        out_shape=(
            jax.ShapeDtypeStruct((total, D), F32),
            jax.ShapeDtypeStruct((total, D), F32),
            jax.ShapeDtypeStruct((D, total), BF16),
            jax.ShapeDtypeStruct(mine.shape, BF16),
            jax.ShapeDtypeStruct(mine.shape, BF16),
            jax.ShapeDtypeStruct((D, D), F32),
            jax.ShapeDtypeStruct((VEC, D), F32),
        ),
        grid_spec=pltpu.PrefetchScalarGridSpec(
            num_scalar_prefetch=2,
            grid=(total // TILE,),
            in_specs=[
                pl.BlockSpec((TILE, D), tile),
                pl.BlockSpec((TILE, D), tile),
                pl.BlockSpec((TILE, D), tile),
                pl.BlockSpec((D, TILE), by_col),
                pl.BlockSpec((D, D), whole),
                vspec(),
                vspec(),
                pl.BlockSpec((VEC, D), whole),
            ],
            out_specs=[
                pl.BlockSpec((TILE, D), tile),
                pl.BlockSpec((TILE, D), tile),
                pl.BlockSpec((D, TILE), by_col),
                pl.BlockSpec(mine.shape, whole5),
                pl.BlockSpec(mine.shape, whole5),
                pl.BlockSpec((D, D), whole),
                pl.BlockSpec((VEC, D), whole),
            ],
            scratch_shapes=[
                pltpu.VMEM((D, FF), BF16),
                pltpu.VMEM((D, FF), BF16),
                pltpu.VMEM((D + 16, FF), F32),
                pltpu.VMEM((D, FF), F32),
                pltpu.VMEM((D, D), F32),
                pltpu.VMEM((VEC, D), F32),
                pltpu.VMEM((TILE, FF), BF16),
                pltpu.VMEM((TILE, FF), BF16),
                pltpu.VMEM((TILE, FF), BF16),
                pltpu.VMEM((TILE, D), BF16),
                pltpu.VMEM((TILE, D), BF16),
                pltpu.VMEM((TILE, D), BF16),
                pltpu.VMEM((D, D), BF16),
            ],
        ),
        compiler_params=params(dimension_semantics=("arbitrary",)),
        cost_estimate=pl.CostEstimate(
            flops=14_000_000_000, bytes_accessed=15_000_000, transcendentals=4_200_000
        ),
        name="feed_forward",
    )(marks, place, x, back, mixed, mixed_t, proj, mine, other, vector)


def pull_kernel(
    marks,
    place,
    grad_t_ref,
    query_t_ref,
    value_ref,
    key_t_ref,
    out_t_ref,
    inverse_ref,
    exps_ref,
    qk_t_ref,
    x_t_ref,
    proj_ref,
    low_ref,
    own_ref,
    other_ref,
    sums_ref,
    dot_s,
    query_g,
    key_g,
    value_g,
    acc,
    sum_acc,
    value_s,
    scaled_t_s,
    score_s,
):
    group = pl.program_id(0)
    row = pl.program_id(1)
    begin = marks[row, 3]

    @pl.when(row == 0)
    def _():
        acc[...] = jnp.zeros_like(acc)
        sum_acc[...] = jnp.zeros_like(sum_acc)

    grad_t = grad_t_ref[...].astype(F32)
    head_of = iota((1, LANES), 1) // HEAD_DIM
    for at_head in range(GROUP):
        heads = slice(at_head * HEAD_DIM, (at_head + 1) * HEAD_DIM)
        part = grad_t[heads, :] * inverse_ref[0, at_head : at_head + 1, :]
        dot_s[at_head : at_head + 1, :] = jnp.sum(part * out_t_ref[heads, :], axis=0, keepdims=True)
        part = part.astype(BF16)
        scaled_t_s[heads, :] = part
        mask = jnp.where(head_of == at_head, 1.0, 0.0).astype(BF16)
        for half in range(2):
            rows = slice(half * HALF, (half + 1) * HALF)
            to = slice(at_head * HALF, (at_head + 1) * HALF)
            value_s[half, to, :] = value_ref[rows, :] * mask

    def score_grads_of(half, block):
        at = half * HALF + block * QBLOCK
        pulls = dot(value_s[half], scaled_t_s[:, at : at + QBLOCK])
        for at_head in range(GROUP):
            cols = slice(at_head * HALF + block * QBLOCK, at_head * HALF + (block + 1) * QBLOCK)
            pull = pulls[at_head * HALF : (at_head + 1) * HALF, :]
            pull = (pull - dot_s[at_head : at_head + 1, at : at + QBLOCK]).astype(BF16)
            score_s[half, :, cols] = exps_ref[0, 0, half, :, cols] * pull

    def finish(half, at_head):
        cols = slice(at_head * HALF, (at_head + 1) * HALF)
        rows = slice(half * HALF, (half + 1) * HALF)
        heads = slice(at_head * HEAD_DIM, (at_head + 1) * HEAD_DIM)
        score_grad = score_s[half, :, cols]
        value_g[heads, rows] = dot_nt(scaled_t_s[heads, rows], exps_ref[0, 0, half, :, cols])
        query_g[heads, rows] = dot(key_t_ref[heads, rows], score_grad)
        key_g[heads, rows] = dot_nt(query_t_ref[heads, rows], score_grad)

    blocks = HALF // QBLOCK
    each = GROUP // blocks
    for block in range(blocks):
        score_grads_of(0, block)
    for block in range(blocks):
        score_grads_of(1, block)
        for at_head in range(each * block, each * (block + 1)):
            finish(0, at_head)
    for at_head in range(GROUP):
        finish(1, at_head)
    query_low = query_g[...].astype(BF16)
    both_low = jnp.concatenate([key_g[...].astype(BF16), value_g[...].astype(BF16)], axis=0)
    ones = jnp.ones((16, SEQ), BF16)
    sum_acc[0:1, :] += dot_nt(ones, query_low)[0:1, :] * SCALE
    sum_acc[1:2, :] += dot_nt(ones, both_low[LANES:, :])[0:1, :]
    qk_t = qk_t_ref[...]
    both = dot_nt(qk_t, jnp.concatenate([query_low, both_low[:LANES, :]], axis=0))
    acc[:, :LANES] += both[:, :LANES] * SCALE
    acc[:, LANES : 2 * LANES] += both[:, LANES:]
    acc[:, 2 * LANES :] += dot_nt(x_t_ref[...], both_low[LANES:, :])
    low_ref[0, :LANES, :] = query_low
    low_ref[0, LANES:, :] = both_low

    def write(ref):
        tall = D // VDP
        for d in range(VDP):
            rows = slice(d * tall, (d + 1) * tall)
            for c in range(3):
                ref[d, c] = acc[rows, c * LANES : (c + 1) * LANES].astype(BF16)
            ref[d, 3] = proj_ref[rows, :].astype(BF16)

    last = row == pl.num_programs(1) - 1

    @pl.when(last & (group == place[2]))
    def _():
        write(own_ref)

    @pl.when(last & (group != place[2]))
    def _():
        write(other_ref)

    @pl.when(last)
    def _():
        sums_ref[pl.ds(group, 1)] = sum_acc[...][None]


def attend_back(marks, place, grad_t, query_t, value, key_t, out_t, inverse, exps, qk_t, x_t, proj):
    total = value.shape[0]
    rows = total // SEQ
    by_both = lambda g, r, m, p: (g, r)
    by_col = lambda g, r, m, p: (0, r)
    grads = jax.ShapeDtypeStruct((VDP, VCHIP, D // VDP, LANES), BF16)
    grads_spec = pl.BlockSpec(grads.shape, lambda g, r, m, p: (0, 0, 0, 0))
    return pl.pallas_call(
        pull_kernel,
        out_shape=(
            jax.ShapeDtypeStruct((2, 3 * LANES, total), BF16),
            grads,
            grads,
            jax.ShapeDtypeStruct((2, 8, LANES), F32),
        ),
        grid_spec=pltpu.PrefetchScalarGridSpec(
            num_scalar_prefetch=2,
            grid=(2, rows),
            in_specs=[
                pl.BlockSpec((LANES, SEQ), by_both),
                pl.BlockSpec((LANES, SEQ), by_both),
                pl.BlockSpec((SEQ, LANES), lambda g, r, m, p: (r, g)),
                pl.BlockSpec((LANES, SEQ), by_both),
                pl.BlockSpec((LANES, SEQ), by_both),
                pl.BlockSpec((1, 8, SEQ), lambda g, r, m, p: (g, 0, r)),
                pl.BlockSpec((1, 1, 2, HALF, GROUP * HALF), lambda g, r, m, p: (r, g, 0, 0, 0)),
                pl.BlockSpec((D, SEQ), by_col),
                pl.BlockSpec((D, SEQ), by_col),
                pl.BlockSpec((D, LANES), lambda g, r, m, p: (0, g)),
            ],
            out_specs=[
                pl.BlockSpec((1, 3 * LANES, SEQ), lambda g, r, m, p: (g, 0, r)),
                grads_spec,
                grads_spec,
                pl.BlockSpec((2, 8, LANES), lambda g, r, m, p: (0, 0, 0)),
            ],
            scratch_shapes=[
                pltpu.VMEM((8, SEQ), F32),
                pltpu.VMEM((LANES, SEQ), F32),
                pltpu.VMEM((LANES, SEQ), F32),
                pltpu.VMEM((LANES, SEQ), F32),
                pltpu.VMEM((D, 3 * LANES), F32),
                pltpu.VMEM((8, LANES), F32),
                pltpu.VMEM((2, GROUP * HALF, LANES), BF16),
                pltpu.VMEM((LANES, SEQ), BF16),
                pltpu.VMEM((2, HALF, GROUP * HALF), BF16),
            ],
        ),
        compiler_params=params(dimension_semantics=("arbitrary", "arbitrary")),
        cost_estimate=pl.CostEstimate(
            flops=36_000_000_000, bytes_accessed=30_000_000, transcendentals=0
        ),
        name="attend_back",
    )(marks, place, grad_t, query_t, value, key_t, out_t, inverse, exps, qk_t, x_t, proj)


def input_kernel(
    marks, low_ref, weight_ref, resid_ref, turned_ref, block_ref, input_ref, token_ref
):
    token_ref[...] = jnp.zeros_like(token_ref)
    at = slice(0, LANES), slice(LANES, 2 * LANES), slice(2 * LANES, 3 * LANES)
    parts = [jnp.concatenate([low_ref[0, rows, :], low_ref[1, rows, :]], axis=0) for rows in at]
    pulled = dot(weight_ref[:, :D], parts[0]) * SCALE + (
        dot(weight_ref[:, D : 2 * D], parts[1]) + dot(weight_ref[:, 2 * D :], parts[2])
    )
    begin = marks[pl.program_id(0), 3]
    input_ref[...] = pltpu.roll(resid_ref[...] + pulled.T, begin, 0)
    block_ref[...] = pltpu.roll(turned_ref[...], begin, 0)


def input_pull(marks, low, weight, resid, turned):
    total = resid.shape[0]
    by_row = pl.BlockSpec((SEQ, D), lambda r, m: (r, 0))
    return pl.pallas_call(
        input_kernel,
        out_shape=(
            jax.ShapeDtypeStruct((total, D), F32),
            jax.ShapeDtypeStruct((total, D), F32),
            jax.ShapeDtypeStruct((8, LANES), F32),
        ),
        grid_spec=pltpu.PrefetchScalarGridSpec(
            num_scalar_prefetch=1,
            grid=(total // SEQ,),
            in_specs=[
                pl.BlockSpec((2, 3 * LANES, SEQ), lambda r, m: (0, 0, r)),
                pl.BlockSpec((D, 3 * D), lambda r, m: (0, 0)),
                by_row,
                by_row,
            ],
            out_specs=[by_row, by_row, pl.BlockSpec((8, LANES), lambda r, m: (0, 0))],
        ),
        compiler_params=params(dimension_semantics=("arbitrary",)),
        cost_estimate=pl.CostEstimate(
            flops=1_000_000_000, bytes_accessed=8_000_000, transcendentals=0
        ),
        name="input_pull",
    )(marks, low, weight, resid, turned)


def two_terms(rows):
    high = rows.astype(BF16)
    return jnp.concatenate([high.astype(F32), rows - high.astype(F32)], axis=0)


def column_to_row(columns, rows):
    lane = iota((rows, LANES), 1)
    wide = jnp.zeros((rows, LANES), F32)
    for i, column in enumerate(columns):
        wide = jnp.where(lane == i, column, wide)
    return wide.T[:8, :]


def total_of(array):
    return jnp.sum(jnp.sum(array, axis=0, keepdims=True), axis=1, keepdims=True)


def tail_send_kernel(
    place,
    mine_ref,
    got_ref,
    vector_ref,
    sums_ref,
    ffn_ref,
    send_ref,
    grad_1,
    grad_2,
    grad_ref,
):
    tall = D // VDP
    low, high = sums_ref[0], sums_ref[1]
    vector = jnp.concatenate(
        [
            vector_ref[:8, :],
            jnp.concatenate([low[:2], high[:2]], axis=1),
            vector_ref[10:, :],
        ],
        axis=0,
    )
    piece, across = [], []
    for kind in range(2):
        total = ffn_ref[0, kind].astype(F32)
        for at in range(1, VDP * VCHIP):
            total = total + ffn_ref[at, kind].astype(F32)
        (grad_1, grad_2)[kind][...] = total
        grad_ref[kind] = total
        square = total * total + EPS_ONE
        down = jnp.sum(square, axis=0, keepdims=True)
        piece += [down[:, :LANES], down[:, LANES:]]
        across.append(jnp.sum(square, axis=1, keepdims=True))
    across = column_to_row(across, tall)
    across = jnp.concatenate([across[0:1], across[1:2]], axis=1)
    stat = two_terms(jnp.concatenate([across] + piece + [jnp.zeros((1, LANES), F32)], axis=0))
    rows = VEC // VDP
    for d in range(VDP):
        for c in range(VCHIP):
            at = d * VCHIP + c
            both = mine_ref[d, c].astype(F32) + got_ref[d, c].astype(F32)
            send_ref[at, :tall, :] = both.astype(BF16)
            part = vector[d * rows : (d + 1) * rows, c * 64 : (c + 1) * 64]
            part = jnp.concatenate([part, jnp.zeros((rows, LANES - 64), F32)], axis=1)
            send_ref[at, tall:, :] = jnp.concatenate([part, stat], axis=0).astype(BF16)


def tail_reduce_kernel(
    place,
    earlier_ref,
    got_ref,
    ffn_grad_ref,
    attn_ref,
    first_ref,
    second_ref,
    rows_0,
    rows_1,
    rows_2,
    cols_0,
    cols_1,
    cols_2,
    vector_ref,
    moment_ref,
    grad_ref,
    cols_out_1,
    cols_out_2,
    send_ref,
):
    decay = 1.0 - STEP ** (-0.8)
    chip = place[1]
    dp = place[0]
    tall = attn_ref.shape[0]
    rows, width = vector_ref.shape
    pieces = VDP * VCHIP
    lane = iota((1, LANES), 1)
    total = got_ref[0, :tall, :].astype(F32)
    part = got_ref[0, tall:, :].astype(F32)[:rows]
    for at in range(1, pieces):
        total = total + got_ref[at, :tall, :].astype(F32)
        part = part + got_ref[at, tall:, :].astype(F32)[:rows]
    grad_ref[...] = total
    low = total.astype(BF16)

    def stat_of(at):
        both = got_ref[pl.ds(at, 1), tall:, :][0].astype(F32)[rows:]
        return both[:6] + both[6:12]

    down = jnp.zeros((6, LANES), F32)
    for d in range(VDP):
        down = down + stat_of(d * VCHIP + chip)
    mine = jnp.zeros((1, LANES), F32)
    for c in range(VCHIP):
        mine = mine + stat_of(dp * VCHIP + c)[0:1]
    row_total = tall * VDP
    count = first_ref.shape[1] * 2 * VCHIP
    share = (0.5 * decay) * jnp.concatenate([rows_1[...], rows_2[...]], axis=1) + (1.0 - decay) * (
        mine / count
    )
    scalars = jnp.zeros((1, LANES), F32)
    weighted = []
    for i, (old_ref, out_ref) in enumerate(((cols_1, cols_out_1), (cols_2, cols_out_2))):
        sums = jnp.concatenate([down[1 + 2 * i : 2 + 2 * i], down[2 + 2 * i : 3 + 2 * i]], axis=1)
        cols = decay * old_ref[...] + (1.0 - decay) * (sums / row_total)
        out_ref[...] = cols
        grad = ffn_grad_ref[i]
        weighted.append(jnp.sum(grad * grad / cols, axis=1, keepdims=True))
    weighted = column_to_row(weighted, tall)
    weighted = jnp.concatenate([weighted[0:1], weighted[1:2]], axis=1)
    for i, ref in enumerate((attn_ref, first_ref, second_ref)):
        weight = ref[...]
        scalars = jnp.where(lane == 64 + i, total_of(weight * weight), scalars)
    scalars = jnp.concatenate([rows_0[...], scalars[:, tall:]], axis=1)
    vector = vector_ref[...]
    power = jnp.sum(vector * vector, axis=1, keepdims=True)
    lines = jnp.concatenate(
        [part[:, :64], moment_ref[...], jnp.broadcast_to(power, (rows, LANES - 64 - width))], axis=1
    )
    piece = jnp.concatenate(
        [
            two_terms(lines),
            two_terms(jnp.concatenate([cols_0[...], scalars], axis=0)),
            two_terms(jnp.concatenate([share, weighted], axis=0)),
        ],
        axis=0,
    ).astype(BF16)
    for at in range(pieces):
        send_ref[at, :tall, :] = low
        send_ref[at, tall:, :] = piece


def tail_apply_kernel(
    place,
    mine_ref,
    other_ref,
    grad_ref,
    ffn_grad_ref,
    cols_new_1,
    cols_new_2,
    weight_0,
    weight_1,
    weight_2,
    rows_0,
    cols_0,
    vector_ref,
    moment_ref,
    new_0,
    new_1,
    new_2,
    rows_out,
    rows_out_1,
    rows_out_2,
    cols_out,
    vector_grad_ref,
    moment_out,
    vector_out,
    sums_s,
    rows_s,
):
    decay = 1.0 - STEP ** (-0.8)
    dp, chip, core = place[0], place[1], place[2]
    tall = weight_0.shape[0]
    rows, width = vector_ref.shape
    fsdp = 2 * VCHIP
    lane = iota((1, LANES), 1)
    refs = (mine_ref, other_ref)
    row_total = float(tall * VDP)
    col_total = float(LANES * fsdp)

    def lines_of(ref, at):
        both = ref[at, tall:, :].astype(F32)
        return both[0:4] + both[4:8], both[8:10] + both[10:12], both[12:14] + both[14:16]

    scalars = jnp.zeros((1, LANES), F32)
    for ref in refs:
        for at in range(VDP * VCHIP):
            scalars = scalars + lines_of(ref, at)[1][1:2]
    scalar = lambda at: jnp.sum(jnp.where(lane == at, scalars, 0.0), axis=1, keepdims=True)

    tile, fresh = [], []
    for d in range(VDP):
        wide = jnp.zeros((tall, LANES), F32)
        for ref in refs:
            for c in range(VCHIP):
                block = ref[d * VCHIP + c, :tall, :].astype(F32)
                wide = wide + (block * block + EPS_ONE)
        fresh.append(jnp.sum(wide, axis=1, keepdims=True))
        tile.append(lines_of(mine_ref, d * VCHIP)[1][1:2])
    tile = jnp.concatenate(tile + [jnp.zeros((LANES - VDP, LANES), F32)], axis=0).T
    mean = jnp.zeros((1, 1), F32)
    new_rows = []
    for d in range(VDP):
        new = decay * tile[:tall, d : d + 1] + (1.0 - decay) * (fresh[d] / col_total)
        new_rows.append(1.0 / new)
        mean = mean + jnp.sum(new, axis=0, keepdims=True)
        sums_s[d] = jnp.broadcast_to(fresh[d], (tall, LANES))
    mean = mean / row_total
    mine = sums_s[pl.ds(dp, 1)][0]
    rows_s[...] = mine.T
    rows_new = decay * rows_0[...] + (1.0 - decay) * (rows_s[0:1, :tall] / col_total)
    rows_out[...] = rows_new
    power = jnp.zeros((1, 1), F32)
    for half, ref in enumerate(refs):
        for c in range(VCHIP):
            down = jnp.zeros((tall, LANES), F32)
            weighted = jnp.zeros((tall, LANES), F32)
            for d in range(VDP):
                block = ref[d * VCHIP + c, :tall, :].astype(F32)
                square = block * block
                down = down + (square + EPS_ONE)
                weighted = weighted + square * new_rows[d]
            down = jnp.sum(down, axis=0, keepdims=True)
            old = lines_of(ref, c)[1][0:1]
            cols = decay * old + (1.0 - decay) * (down / row_total)
            weighted = jnp.sum(weighted, axis=0, keepdims=True) / cols
            power = power + jnp.sum(weighted, axis=1, keepdims=True)
            if half == 0:
                sums_s[VDP + c] = jnp.broadcast_to(down, (tall, LANES))
    power = power * mean
    down = sums_s[pl.ds(VDP + chip, 1)][0][0:1, :]
    cols_new = decay * cols_0[...] + (1.0 - decay) * (down / row_total)
    cols_out[...] = cols_new
    ffn_rows = jnp.zeros((1, LANES), F32)
    ffn_means = jnp.zeros((1, LANES), F32)
    ffn_powers = jnp.zeros((1, LANES), F32)
    for d in range(VDP):
        fresh = lines_of(mine_ref, d * VCHIP)[2][0:1] + lines_of(other_ref, d * VCHIP)[2][0:1]
        weighted = jnp.zeros((1, LANES), F32)
        for ref in refs:
            for c in range(VCHIP):
                weighted = weighted + lines_of(ref, d * VCHIP + c)[2][1:2]
        ffn_rows = jnp.where(dp == d, fresh, ffn_rows)
        ffn_means = ffn_means + fresh
        ffn_powers = ffn_powers + weighted / fresh
    parts = (slice(0, tall), slice(tall, 2 * tall))
    ffn_means = [jnp.sum(ffn_means[:, part], axis=1, keepdims=True) / row_total for part in parts]
    ffn_powers = [
        jnp.sum(ffn_powers[:, part], axis=1, keepdims=True) * ffn_mean
        for part, ffn_mean in zip(parts, ffn_means)
    ]
    ffn_rows = [ffn_rows[:, part] for part in parts]
    rows_out_1[...] = ffn_rows[0]
    rows_out_2[...] = ffn_rows[1]
    stacked = jnp.concatenate([rows_new] + ffn_rows + [jnp.zeros((5, tall), F32)], axis=0)
    stacked = jnp.concatenate([stacked, jnp.zeros((8, LANES - tall), F32)], axis=1)
    stacked = jnp.concatenate([stacked, jnp.zeros((LANES - 8, LANES), F32)], axis=0).T
    update_0 = grad_ref[...] * lax.rsqrt(stacked[:tall, 0:1] * cols_new / mean)
    ffn_updates = [
        ffn_grad_ref[i] * lax.rsqrt(stacked[:tall, i + 1 : i + 2] * ref[...] / ffn_means[i])
        for i, ref in enumerate((cols_new_1, cols_new_2))
    ]
    powers = (power, ffn_powers[0], ffn_powers[1])
    for i, (update, weight, new) in enumerate(
        (
            (update_0, weight_0, new_0),
            (ffn_updates[0], weight_1, new_1),
            (ffn_updates[1], weight_2, new_2),
        )
    ):
        entries = float(weight.shape[0] * weight.shape[1] * VDP * fsdp)
        clip = jnp.maximum(1.0, jnp.sqrt(powers[i] / entries) / CLIP_LIMIT)
        rate = STEP_RATE * jnp.maximum(EPS_TWO, jnp.sqrt(scalar(64 + i) / entries))
        new[...] = weight[...] - rate / clip * update
    powers, sizes = [], []
    for d in range(VDP):
        power = jnp.zeros((rows, 1), F32)
        size = jnp.zeros((rows, 1), F32)
        for c in range(VCHIP):
            at = d * VCHIP + c
            first, second = lines_of(mine_ref, at)[0], lines_of(other_ref, at)[0]
            both = first[:, :64] + second[:, :64]
            size = size + first[:, LANES - 1 :] + second[:, LANES - 1 :]
            near = jnp.where(core == 0, first[:, 64 : 64 + width], second[:, 64 : 64 + width])
            far = jnp.where(core == 0, second[:, 64 : 64 + width], first[:, 64 : 64 + width])
            moment = jnp.concatenate([near, far], axis=1)
            moment = decay * moment + (1.0 - decay) * (both * both + EPS_ONE)
            power = power + jnp.sum(both * both / moment, axis=1, keepdims=True)
            wide = jnp.concatenate([both, jnp.zeros((rows, LANES - 64), F32)], axis=1)
            sums_s[2 * VDP + at, :rows, :] = wide
        powers.append(power)
        sizes.append(size)
    both = sums_s[pl.ds(2 * VDP + dp * VCHIP + chip, 1), :rows, :][0]
    vector_grad = jnp.where(core == 0, both[:, :width], both[:, width : 2 * width])
    vector_grad_ref[...] = vector_grad
    moment = decay * moment_ref[...] + (1.0 - decay) * (vector_grad * vector_grad + EPS_ONE)
    moment_out[...] = moment
    step = vector_grad * lax.rsqrt(moment)
    bias = VDP // 2
    bias_power = sum(jnp.sum(power, axis=0, keepdims=True) for power in powers[:bias])
    bias_size = sum(jnp.sum(size, axis=0, keepdims=True) for size in sizes[:bias])
    power, size = powers[bias], sizes[bias]
    for d in range(bias + 1, VDP):
        power = jnp.where(dp == d, powers[d], power)
        size = jnp.where(dp == d, sizes[d], size)
    is_bias = dp < bias
    power = jnp.where(is_bias, bias_power, power)
    size = jnp.where(is_bias, bias_size, size)
    count = jnp.where(is_bias, float(FF), float(D))
    clip = jnp.maximum(1.0, jnp.sqrt(power / count) / CLIP_LIMIT)
    rate = STEP_RATE * jnp.maximum(EPS_TWO, jnp.sqrt(size / count))
    vector_out[...] = vector_ref[...] - rate / clip * step


def whole_call(kernel, name, place, outs, *operands, scratch=(), earlier=None):
    tied = () if earlier is None else (earlier,)
    return pl.pallas_call(
        kernel,
        out_shape=[jax.ShapeDtypeStruct(shape, kind) for shape, kind in outs],
        in_specs=[pl.BlockSpec(memory_space=pltpu.SMEM)]
        + [pl.BlockSpec(memory_space=pl.ANY)] * len(tied)
        + [vspec()] * len(operands),
        out_specs=[vspec()] * len(outs),
        scratch_shapes=list(scratch),
        compiler_params=params(16),
        name=name,
    )(place, *tied, *operands)


def core_swap(block):
    return lax.ppermute(block, "core", [(0, 1), (1, 0)])


def exchange(blocks, axes):
    return lax.all_to_all(blocks, axes, split_axis=0, concat_axis=0, tiled=True)


def after(value, *earlier, mib=8):
    return pl.pallas_call(
        lambda *refs: None,
        out_shape=jax.ShapeDtypeStruct(value.shape, value.dtype),
        in_specs=[pl.BlockSpec(memory_space=pltpu.HBM)] * (1 + len(earlier)),
        out_specs=pl.BlockSpec(memory_space=pltpu.HBM),
        input_output_aliases={0: 0},
        compiler_params=params(mib),
        name="after",
    )(value, *earlier)


def pair_kernel(mine_ref, got_ref, out_ref):
    out_ref[...] = (mine_ref[...].astype(F32) + got_ref[...].astype(F32)).astype(BF16)


def pair_sum(mine, got):
    return pl.pallas_call(
        pair_kernel,
        out_shape=jax.ShapeDtypeStruct(mine.shape, BF16),
        in_specs=[vspec(), vspec()],
        out_specs=vspec(),
        compiler_params=params(16),
        name="pair_sum",
    )(mine, got)


CHIPS = ("dp", "chip")
ALL = ("dp", "chip", "core")


def layer(place, weights, segment_ids, tokens, cotangent, ffn_weights, send_core, send_ffn):
    table = jnp.asarray(encode_table())
    qk, x, qk_t, x_t, back, marks = place_tokens(segment_ids, tokens, cotangent, table)
    query_t, value, key_t, out_t, inverse, mixed, mixed_t, exps, weight, proj, vector = attend_forward(
        marks, place, x, qk, x_t, qk_t, *weights(marks)
    )
    ffn_mine, ffn_other = ffn_weights(marks, vector)
    block_out, resid, grad_t, ffn_mine, ffn_other, proj_g, vector_g = feed_forward(
        marks, place, x, back, mixed, mixed_t, proj, ffn_mine, ffn_other, vector
    )
    ffn_got, grad_t = send_ffn(ffn_mine, ffn_other, grad_t)
    low, grads_own, grads_other, sums = attend_back(
        marks, place, grad_t, query_t, value, key_t, out_t, inverse, exps, qk_t, x_t, proj_g
    )
    attn_got = send_core(grads_other)
    pulled = input_pull(marks, low, weight, resid, block_out)
    return pulled, grads_own, grads_other, attn_got, sums, vector_g, ffn_got


def body(
    tokens,
    cotangent,
    segment_ids,
    attn_weight,
    ffn_in,
    ffn_out,
    vectors,
    attn_rows,
    attn_cols,
    in_rows,
    in_cols,
    out_rows,
    out_cols,
    vector_moment,
):
    place = jnp.stack([lax.axis_index("dp"), lax.axis_index("chip"), lax.axis_index("core")])
    place = place.astype(jnp.int32)
    pieces = VDP * VCHIP
    tall, wide = attn_weight.shape
    rows_v, cols_v = vectors.shape
    split = lambda array: array.reshape((VDP, VCHIP) + array.shape[1:])
    attn_sent, ffn_low = pack_attn(place, attn_weight, ffn_in, ffn_out, vectors)
    attn_mine = exchange(attn_sent, CHIPS)

    parts = [
        lax.ppermute(ffn_low, "dp", [(i, i ^ step) for i in range(VDP)]) for step in range(1, VDP)
    ]
    ffn_sent = pack_ffn(place, ffn_low, parts)

    def attn_weights(marks):
        mine = split(after(attn_mine, marks, *parts))
        return mine, core_swap(mine)

    def ffn_weights(marks, vector):
        got = exchange(after(ffn_sent, marks), "chip")
        ffn_mine = after(got, vector)
        return ffn_mine, core_swap(ffn_mine)

    def send_ffn(mine, other, grad_t):
        both = pair_sum(mine, core_swap(other))
        got = exchange(both.reshape((pieces,) + mine.shape[2:]), CHIPS)
        return got, after(grad_t, both, mib=56)

    (
        pulled,
        grads_own,
        grads_other,
        attn_got,
        sums,
        vector_g,
        ffn_got,
    ) = layer(place, attn_weights, segment_ids, tokens, cotangent, ffn_weights, core_swap, send_ffn)
    lay = lambda stat: stat.reshape(1, -1)
    rows_old = (lay(attn_rows), lay(in_rows), lay(out_rows))
    cols_old = (lay(attn_cols), lay(in_cols), lay(out_cols))
    weights_old = (attn_weight, ffn_in, ffn_out)
    sent, in_grad, out_grad, ffn_grad = whole_call(
        tail_send_kernel,
        "tail_send",
        place,
        [
            ((pieces, tall + VROWS, LANES), BF16),
            (ffn_in.shape, F32),
            (ffn_out.shape, F32),
            ((2,) + ffn_in.shape, F32),
        ],
        grads_own,
        attn_got,
        vector_g,
        sums,
        ffn_got,
    )
    block_out, input_grad, token = pulled
    got = exchange(sent, CHIPS)
    attn_grad, cols_new_1, cols_new_2, sent = whole_call(
        tail_reduce_kernel,
        "tail_reduce",
        place,
        [
            (attn_weight.shape, F32),
            (cols_old[1].shape, F32),
            (cols_old[2].shape, F32),
            ((pieces, tall + VROWS, LANES), BF16),
        ],
        got,
        ffn_grad,
        *weights_old,
        *rows_old,
        *cols_old,
        vectors,
        vector_moment,
        earlier=token,
    )
    mine = exchange(sent, CHIPS)
    attn_new, in_new, out_new, rows_new_0, rows_new_1, rows_new_2, cols_new_0, vector_grad, moment_new, vectors_new = whole_call(
        tail_apply_kernel,
        "tail_apply",
        place,
        [
            (attn_weight.shape, F32),
            (ffn_in.shape, F32),
            (ffn_out.shape, F32),
            (rows_old[0].shape, F32),
            (rows_old[1].shape, F32),
            (rows_old[2].shape, F32),
            (cols_old[0].shape, F32),
            (vectors.shape, F32),
            (vectors.shape, F32),
            (vectors.shape, F32),
        ],
        mine,
        core_swap(mine),
        attn_grad,
        ffn_grad,
        cols_new_1,
        cols_new_2,
        *weights_old,
        rows_old[0],
        cols_old[0],
        vectors,
        vector_moment,
        scratch=[
            pltpu.VMEM((2 * VDP + pieces, tall, LANES), F32),
            pltpu.VMEM((LANES, tall), F32),
        ],
    )
    return (
        block_out,
        input_grad,
        attn_grad,
        in_grad,
        out_grad,
        vector_grad,
        rows_new_0.reshape(-1),
        cols_new_0.reshape(-1),
        rows_new_1.reshape(-1),
        cols_new_1.reshape(-1),
        rows_new_2.reshape(-1),
        cols_new_2.reshape(-1),
        moment_new,
        attn_new,
        in_new,
        out_new,
        vectors_new,
    )


def gather_all(block):
    shape = (lax.axis_size("dp"), lax.axis_size("chip") * 2)
    count = shape[0] * shape[1]
    got = exchange(jnp.broadcast_to(block[None], (count,) + block.shape), ALL)
    return got.reshape(shape + block.shape)


def unblock(parts):
    dp_count, fsdp_count, rows, cols = parts.shape
    return parts.transpose(0, 2, 1, 3).reshape(dp_count * rows, fsdp_count * cols)


def scatter_sum(full):
    dp_count = lax.axis_size("dp")
    fsdp_count = lax.axis_size("chip") * 2
    rows, cols = full.shape
    by_col = full.astype(BF16).reshape(rows, fsdp_count, cols // fsdp_count).transpose(1, 0, 2)
    got = exchange(by_col, ("chip", "core"))
    part = jnp.sum(got.astype(F32), axis=0).astype(BF16)
    by_row = part.reshape(dp_count, rows // dp_count, cols // fsdp_count)
    return jnp.sum(exchange(by_row, "dp").astype(F32), axis=0)


def body_any(
    tokens,
    cotangent,
    segment_ids,
    attn_weight,
    ffn_in,
    ffn_out,
    vectors,
    attn_rows,
    attn_cols,
    in_rows,
    in_cols,
    out_rows,
    out_cols,
    vector_moment,
):
    dp_count = lax.axis_size("dp")
    fsdp_count = lax.axis_size("chip") * 2
    dp_place = lax.axis_index("dp")
    fsdp_place = lax.axis_index("chip") * 2 + lax.axis_index("core")
    rows_w = attn_weight.shape[0]
    rows_v = vectors.shape[0]
    place = jnp.zeros((3,), jnp.int32)
    full_attn = unblock(gather_all(attn_weight.astype(BF16)))
    full_vector = unblock(gather_all(vectors.astype(BF16)))
    full_ffn = jnp.stack(
        [unblock(gather_all(ffn_in.astype(BF16))), unblock(gather_all(ffn_out.astype(BF16)))]
    )
    tall = D // VDP
    cut = full_attn.reshape(VDP, tall, VCHIP, 2, LANES).transpose(3, 0, 2, 1, 4)
    lines = full_vector.reshape(VDP, VEC // VDP, 2, LANES).transpose(0, 2, 1, 3)
    lines = lines.reshape(VDP, 1, 2 * VEC // VDP, LANES)
    lines = jnp.pad(lines, ((0, 0), (0, VCHIP - 1), (0, VROWS - 2 * VEC // VDP), (0, 0)))
    weights = (
        jnp.concatenate([cut[0], lines], axis=2),
        jnp.concatenate([cut[1], jnp.zeros_like(lines)], axis=2),
    )
    ffn_cut = full_ffn.reshape(2, VDP, tall, VCHIP, 2, FF // (2 * VCHIP))
    ffn_cut = ffn_cut.transpose(4, 3, 1, 0, 2, 5)
    (
        pulled,
        grads_own,
        grads_other,
        _,
        sums,
        vector_g,
        ffn_got,
    ) = layer(
        place,
        lambda marks: weights,
        segment_ids,
        tokens,
        cotangent,
        lambda marks, vector: (ffn_cut[0], ffn_cut[1]),
        lambda block: block,
        lambda mine, other, grad_t: (jnp.stack([mine, other]), grad_t),
    )
    block_out, input_grad, _ = pulled
    attn_full = jnp.stack([grads_own, grads_other]).transpose(1, 3, 2, 0, 4).reshape(D, 4 * D)
    ffn_full = ffn_got.transpose(3, 1, 4, 2, 0, 5).reshape(2, D, FF)
    sums = jnp.concatenate([sums[0, :2], sums[1, :2]], axis=1)
    vector_full = jnp.concatenate([vector_g[:8], sums, vector_g[10:]], axis=0)
    attn_grad = scatter_sum(attn_full)
    in_grad = scatter_sum(ffn_full[0])
    out_grad = scatter_sum(ffn_full[1])
    vector_grad = scatter_sum(vector_full)

    decay = 1.0 - STEP ** (-0.8)
    gradients = (attn_grad, in_grad, out_grad)
    weights_old = (attn_weight, ffn_in, ffn_out)
    rows_old = (attn_rows, in_rows, out_rows)
    cols_old = (attn_cols, in_cols, out_cols)
    moment_new = decay * vector_moment + (1.0 - decay) * (vector_grad * vector_grad + EPS_ONE)
    vector_step = vector_grad * lax.rsqrt(moment_new)
    squares = [gradient * gradient + EPS_ONE for gradient in gradients]
    pieces = []
    for square in squares:
        pieces.append(jnp.sum(square, axis=1))
    for square in squares:
        pieces.append(jnp.sum(square, axis=0))
    pieces.append(jnp.sum(vector_step * vector_step, axis=1))
    pieces.append(jnp.sum(vectors * vectors, axis=1))
    pieces.append(jnp.stack([jnp.sum(weight * weight) for weight in weights_old]))
    pieces.append(jnp.stack([jnp.sum(old) for old in rows_old]))
    sizes = [piece.shape[0] for piece in pieces]
    flat = jnp.concatenate(pieces)
    flat = jnp.pad(flat, (0, -flat.shape[0] % 1024)).reshape(-1, LANES)
    got = gather_all(flat).reshape(dp_count, fsdp_count, -1)
    offsets = [0]
    for length in sizes:
        offsets.append(offsets[-1] + length)
    take = lambda i: got[:, :, offsets[i] : offsets[i + 1]]
    rows_new, cols_new, row_means, entries = [], [], [], []
    for i in range(3):
        count_rows = rows_w * dp_count
        count_cols = weights_old[i].shape[1] * fsdp_count
        entries.append(float(count_rows * count_cols))
        row_all = jnp.sum(take(i), axis=1)
        mine = lax.dynamic_index_in_dim(row_all, dp_place, 0, keepdims=False)
        rows_new.append(decay * rows_old[i] + (1.0 - decay) * mine / count_cols)
        col_all = jnp.sum(take(3 + i), axis=0)
        mine = lax.dynamic_index_in_dim(col_all, fsdp_place, 0, keepdims=False)
        cols_new.append(decay * cols_old[i] + (1.0 - decay) * mine / count_rows)
        old_total = jnp.sum(take(9)[:, 0, i])
        row_means.append(
            (decay * old_total + (1.0 - decay) * jnp.sum(row_all) / count_cols) / count_rows
        )
    step_rows = jnp.sum(take(6), axis=1).reshape(-1)
    weight_rows = jnp.sum(take(7), axis=1).reshape(-1)
    weight_totals = jnp.sum(take(8), axis=(0, 1))
    updates = []
    for i in range(3):
        second = rows_new[i][:, None] * cols_new[i][None, :] / row_means[i]
        updates.append(gradients[i] * lax.rsqrt(second))
    flat = jnp.stack([jnp.sum(update * update) for update in updates])
    flat = jnp.broadcast_to(jnp.pad(flat, (0, 5))[:, None], (8, LANES))
    totals = jnp.sum(gather_all(flat)[:, :, :, 0], axis=(0, 1))
    new_weights = []
    for i in range(3):
        clip_factor = jnp.maximum(1.0, jnp.sqrt(totals[i] / entries[i]) / CLIP_LIMIT)
        step_size = STEP_RATE * jnp.maximum(EPS_TWO, jnp.sqrt(weight_totals[i] / entries[i]))
        new_weights.append(weights_old[i] - step_size / clip_factor * updates[i])
    bias_rows = FF // D
    row_places = jnp.arange(VEC)
    counts = jnp.where(row_places < bias_rows, float(FF), float(D))
    grouped_updates = jnp.where(row_places < bias_rows, jnp.sum(step_rows[:bias_rows]), step_rows)
    grouped_weights = jnp.where(row_places < bias_rows, jnp.sum(weight_rows[:bias_rows]), weight_rows)
    clip_rows = jnp.maximum(1.0, jnp.sqrt(grouped_updates / counts) / CLIP_LIMIT)
    step_sizes = STEP_RATE * jnp.maximum(EPS_TWO, jnp.sqrt(grouped_weights / counts))
    factor_rows = lax.dynamic_slice_in_dim(step_sizes / clip_rows, dp_place * rows_v, rows_v)
    vectors_new = vectors - factor_rows[:, None] * vector_step
    return (
        block_out,
        input_grad,
        attn_grad,
        in_grad,
        out_grad,
        vector_grad,
        rows_new[0],
        cols_new[0],
        rows_new[1],
        cols_new[1],
        rows_new[2],
        cols_new[2],
        moment_new,
        new_weights[0],
        new_weights[1],
        new_weights[2],
        vectors_new,
    )


def solution(mesh):
    dp_count, fsdp_count = mesh.shape["dp"], mesh.shape["fsdp"]
    inner = jax.sharding.Mesh(mesh.devices.reshape(dp_count, fsdp_count // 2, 2), ALL)
    fsdp = ("chip", "core")
    split = P(ALL, None)
    block = P("dp", fsdp)
    stats = (P("dp"), P(fsdp)) * 3
    plain = dp_count == VDP and fsdp_count == 2 * VCHIP
    return jax.shard_map(
        body if plain else body_any,
        mesh=inner,
        in_specs=(split,) * 3 + (block,) * 4 + stats + (block,),
        out_specs=(split,) * 2 + (block,) * 4 + stats + (block,) * 5,
        check_vma=False,
    )
```

```python
import functools
import math

import jax
import jax.numpy as jnp
import numpy as np
from jax import lax
from jax.experimental import pallas as pl
from jax.experimental.pallas import tpu as pltpu
from jax.sharding import PartitionSpec as P

D = 256
FF = 2048
HEADS = 8
HEAD_DIM = 32
SEQ = 1024
HALF = 512
GROUP = 4
LANES = 128
QBLOCK = 512
WGRID = 32
STEP = 10
VEC = 16
TILE = 1024
CHUNK = 256
SUB = 512
LEAD = 5
STRIP = 64
VDP = 4
VCHIP = 4
VROWS = 16

EPS_NORM = 1e-05
EPS_ONE = 1e-30
EPS_TWO = 0.001
CLIP_LIMIT = 1.0
STEP_RATE = 0.3
FAR = 1e30
TAME = 40.0
LOG2_E = math.log2(math.e)
SCALE = HEAD_DIM ** (-0.5)
GELU_A = math.sqrt(2.0 / math.pi)
GELU_B = 0.044715
F32 = jnp.float32
BF16 = jnp.bfloat16
MIB = 1024 * 1024


def dot(left, right):
    return jnp.dot(left, right, preferred_element_type=F32)


def dot_nt(left, right):
    return lax.dot_general(left, right, (((1,), (1,)), ((), ())), preferred_element_type=F32)


def encode_table():
    half = D // 2
    feature = np.arange(half)
    freq = np.exp(
        (2 * (feature // 2)).astype(np.float32) * np.float32(-math.log(10000.0) / half)
    ).astype(np.float32)
    angles = np.arange(1, WGRID + 1, dtype=np.float32)[:, None] * freq[None, :]
    table = np.where(feature % 2 == 0, np.sin(angles), np.cos(angles)).astype(np.float32)
    low = jnp.bfloat16
    one = table.astype(low)
    rest = table - one.astype(np.float32)
    two = rest.astype(low)
    three = (rest - two.astype(np.float32)).astype(low)
    blank = np.zeros((LANES - 3 * WGRID, half), low)
    return np.concatenate([one, two, three, blank], axis=0)


def iota(shape, dim):
    return lax.broadcasted_iota(jnp.int32, shape, dim)


def norm_forward(rows):
    centered = rows - jnp.mean(rows, axis=-1, keepdims=True)
    inverse = lax.rsqrt(jnp.mean(centered * centered, axis=-1, keepdims=True) + EPS_NORM)
    return centered * inverse, inverse


def norm_backward(upstream, normed, inverse):
    return inverse * (
        upstream
        - jnp.mean(upstream, axis=-1, keepdims=True)
        - normed * jnp.mean(upstream * normed, axis=-1, keepdims=True)
    )

def vspec():
    return pl.BlockSpec(memory_space=pltpu.VMEM)


def params(mib=56, **more):
    return pltpu.CompilerParams(vmem_limit_bytes=mib * MIB, **more)


def pack_kernel(place, attn_ref, first_ref, second_ref, vector_ref, out_ref, ffn_ref):
    owner = place[1] * 2 + place[2]
    vector = vector_ref[...]
    rows = vector.shape[0]
    wide = jnp.concatenate([vector] * (LANES // vector.shape[1]), axis=1)
    slot = iota((rows, LANES), 1) // vector.shape[1]
    per = LANES // vector.shape[1]
    parts = [attn_ref[...]]
    for half in range(2):
        parts.append(jnp.where(slot + half * per == owner, wide, 0.0))
    parts.append(jnp.zeros((VROWS - 2 * rows, LANES), F32))
    piece = jnp.concatenate(parts, axis=0).astype(BF16)
    for at in range(VDP * VCHIP):
        out_ref[at] = piece
    ffn_ref[0] = first_ref[...].astype(BF16)
    ffn_ref[1] = second_ref[...].astype(BF16)


def pack_attn(place, attn_weight, ffn_in, ffn_out, vectors):
    return pl.pallas_call(
        pack_kernel,
        out_shape=(
            jax.ShapeDtypeStruct((VDP * VCHIP, attn_weight.shape[0] + VROWS, LANES), BF16),
            jax.ShapeDtypeStruct((2,) + ffn_in.shape, BF16),
        ),
        in_specs=[pl.BlockSpec(memory_space=pltpu.SMEM)] + [vspec()] * 4,
        out_specs=(vspec(), vspec()),
        compiler_params=params(),
        name="pack_attn",
    )(place, attn_weight, ffn_in, ffn_out, vectors)


def pack_ffn_kernel(place, own_ref, *refs):
    out_ref = refs[-1]
    for at in range(VCHIP):
        out_ref[at, pl.ds(place[0], 1)] = own_ref[...][None]
        for step in range(1, VDP):
            out_ref[at, pl.ds(place[0] ^ step, 1)] = refs[step - 1][...][None]


def pack_ffn(place, own, parts):
    return pl.pallas_call(
        pack_ffn_kernel,
        out_shape=jax.ShapeDtypeStruct((VCHIP, VDP) + own.shape, BF16),
        in_specs=[pl.BlockSpec(memory_space=pltpu.SMEM)] + [vspec()] * (1 + len(parts)),
        out_specs=vspec(),
        compiler_params=params(16),
        name="pack_ffn",
    )(place, own, *parts)


def place_kernel(
    segment_ref, tokens_ref, back_ref, table_ref, qk_ref, x_ref, qk_t_ref, x_t_ref, turned_ref, marks_ref
):
    row = pl.program_id(0)
    starts = []
    for number in range(1, 4):
        at = jnp.int32(0)
        for step in (512, 256, 128, 64, 32, 16, 8, 4, 2, 1, 1):
            probe = jnp.minimum(at + (step - 1), SEQ - 1)
            at = jnp.where(segment_ref[row, probe] < number, at + step, at)
        starts.append(at)
    edges = [jnp.int32(0)] + starts + [jnp.int32(SEQ)]
    begin = jnp.int32(0)
    for number in range(3, -1, -1):
        begin = jnp.where(edges[number + 1] - edges[number] == HALF, edges[number], begin)
    for number in range(3):
        marks_ref[row, number] = starts[number]
    marks_ref[row, 3] = begin
    one, two, three = starts
    x = pltpu.roll(tokens_ref[...].astype(F32), (SEQ - begin) & (SEQ - 1), 0)
    x_ref[...] = x.astype(BF16)
    x_t_ref[...] = x.T.astype(BF16)
    back = back_ref[...].astype(F32)
    turned_ref[...] = pltpu.roll(back, (SEQ - begin) & (SEQ - 1), 0).astype(BF16)
    at = (iota((SEQ, LANES), 0) + begin) & (SEQ - 1)
    lane = iota((SEQ, LANES), 1)
    start = jnp.where(at >= three, three, jnp.where(at >= two, two, jnp.where(at >= one, one, 0)))
    local = at - start
    kept = lane < 3 * WGRID
    slot = lane & (WGRID - 1)
    hot_r = jnp.where(((local >> 5) == slot) & kept, 1.0, 0.0).astype(BF16)
    hot_c = jnp.where(((local & (WGRID - 1)) == slot) & kept, 1.0, 0.0).astype(BF16)
    table = table_ref[...]
    places = jnp.concatenate([dot(hot_r, table), dot(hot_c, table)], axis=1)
    qk = x + places
    qk_ref[...] = qk.astype(BF16)
    qk_t_ref[...] = qk.T.astype(BF16)


def place_tokens(segment_ids, tokens, cotangent, table):
    rows = segment_ids.shape[0]
    by_row = lambda r: (r, 0)
    return pl.pallas_call(
        place_kernel,
        out_shape=(
            jax.ShapeDtypeStruct(tokens.shape, BF16),
            jax.ShapeDtypeStruct(tokens.shape, BF16),
            jax.ShapeDtypeStruct((D, tokens.shape[0]), BF16),
            jax.ShapeDtypeStruct((D, tokens.shape[0]), BF16),
            jax.ShapeDtypeStruct(tokens.shape, BF16),
            jax.ShapeDtypeStruct((rows, 4), jnp.int32),
        ),
        grid=(rows,),
        in_specs=[
            pl.BlockSpec(memory_space=pltpu.SMEM),
            pl.BlockSpec((SEQ, D), by_row),
            pl.BlockSpec((SEQ, D), by_row),
            pl.BlockSpec((LANES, LANES), lambda r: (0, 0)),
        ],
        out_specs=(
            pl.BlockSpec((SEQ, D), by_row),
            pl.BlockSpec((SEQ, D), by_row),
            pl.BlockSpec((D, SEQ), lambda r: (0, r)),
            pl.BlockSpec((D, SEQ), lambda r: (0, r)),
            pl.BlockSpec((SEQ, D), by_row),
            pl.BlockSpec(memory_space=pltpu.SMEM),
        ),
        compiler_params=params(dimension_semantics=("arbitrary",)),
        cost_estimate=pl.CostEstimate(flops=600_000_000, bytes_accessed=4_000_000, transcendentals=0),
        name="place_tokens",
    )(segment_ids, tokens, cotangent, table)


def attend_kernel(
    marks,
    place,
    x_ref,
    qk_ref,
    x_t_ref,
    qk_t_ref,
    mine_ref,
    other_ref,
    query_t_ref,
    value_ref,
    key_t_ref,
    out_t_ref,
    inverse_ref,
    mixed_ref,
    mixed_t_ref,
    exps_ref,
    weight_ref,
    proj_ref,
    vector_ref,
    key_s,
    value_s,
    mark_k,
    mark_q,
    first_s,
    second_s,
    weight_t_s,
    bias_s,
    tame_s,
    exps_s,
    exps_sem,
):
    row = pl.program_id(0)
    begin = marks[row, 3]
    core = place[2]

    def copy_of(group, half):
        return pltpu.make_async_copy(
            exps_s.at[group, half], exps_ref.at[row, group, half], exps_sem.at[group * 2 + half]
        )

    @pl.when(row == 0)
    def _():
        tall = D // VDP
        for d in range(VDP):
            rows = slice(d * tall, (d + 1) * tall)
            total = jnp.zeros((8, LANES), F32)
            for c in range(VCHIP):
                for ref, half in ((mine_ref, core), (other_ref, 1 - core)):
                    if c < 3:
                        to = pl.ds(pl.multiple_of(c * D + half * LANES, LANES), LANES)
                        weight_ref[rows, to] = ref[d, c, :tall, :]
                    else:
                        to = pl.ds(pl.multiple_of(half * LANES, LANES), LANES)
                        proj_ref[rows, to] = ref[d, c, :tall, :]
                    total += ref[d, c, tall:, :].astype(F32)[:8]
            vector_ref[d * 4 : (d + 1) * 4, :LANES] = total[:4]
            vector_ref[d * 4 : (d + 1) * 4, LANES:] = total[4:]
        weight_t_s[...] = weight_ref[...].astype(F32).T.astype(BF16)
        bias_s[...] = vector_ref[8:16, :].T

    qk_t = qk_t_ref[...]
    query_t = (dot(weight_t_s[:D, :], qk_t) + bias_s[:, 0:1]) * SCALE
    query_t = query_t.astype(BF16)
    query_t_ref[...] = query_t
    key_t = dot(weight_t_s[D : 2 * D, :], qk_t).astype(BF16)
    key_t_ref[...] = key_t

    def largest_norms(rows):
        rows = rows.astype(F32)
        rows = rows * rows
        sums = [
            jnp.sum(rows[head * HEAD_DIM : (head + 1) * HEAD_DIM], axis=0, keepdims=True)
            for head in range(HEADS)
        ]
        return jnp.max(jnp.concatenate(sums, axis=0), axis=1, keepdims=True)

    bound = jnp.max(largest_norms(query_t) * largest_norms(key_t))
    tame_s[0] = jnp.where(bound <= TAME * TAME, 1, 0)
    key_s[...] = dot(qk_ref[...], weight_ref[:, D : 2 * D]).astype(BF16)
    value = dot(x_ref[...], weight_ref[:, 2 * D : 3 * D]) + vector_ref[9:10, :]
    value_ref[...] = value.astype(BF16)
    value_t = dot(weight_t_s[2 * D :, :], x_t_ref[...]) + bias_s[:, 1:2]
    value_t = value_t.astype(BF16)
    for head in range(HEADS):
        value_s[head, :HEAD_DIM, :] = value_t[head * HEAD_DIM : (head + 1) * HEAD_DIM, :]
        value_s[head, HEAD_DIM:, :] = jnp.ones((16, SEQ), BF16)
    one, two, three = marks[row, 0], marks[row, 1], marks[row, 2]

    def number_of(shape, dim):
        here = (iota(shape, dim) + (HALF + begin)) & (SEQ - 1)
        return (
            jnp.where(here >= one, 1, 0)
            + jnp.where(here >= two, 1, 0)
            + jnp.where(here >= three, 1, 0)
        )

    lane = iota((HALF, LANES), 1)
    number = number_of((HALF, LANES), 0)
    mark_k[...] = jnp.where((number != lane) & (lane < 4), -FAR, 0.0).astype(BF16)
    number = number_of((LANES, HALF), 1)
    mark_q[...] = jnp.where(number == iota((LANES, HALF), 0), 1.0, 0.0).astype(BF16)

    head_of = iota((1, LANES), 1) // HEAD_DIM
    for group in range(2):
        keys_here = key_s[:, group * LANES : (group + 1) * LANES]
        for at_head in range(GROUP):
            mask = jnp.where(head_of == at_head, 1.0, 0.0).astype(BF16)
            rows = slice(at_head * HALF, (at_head + 1) * HALF)
            first_s[group, rows, :] = keys_here[:HALF] * mask
            second_s[group, rows, :LANES] = keys_here[HALF:] * mask
            second_s[group, rows, LANES:] = mark_k[...]

    @pl.when(row > 0)
    def _():
        for group in range(2):
            for half in range(2):
                copy_of(group, half).wait()

    def scores_of(group, half, rows):
        query = query_t_ref[group * LANES : (group + 1) * LANES, half * HALF : (half + 1) * HALF]
        if half == 0:
            return dot(first_s[group, rows, :], query)
        return dot(second_s[group, rows, :], jnp.concatenate([query, mark_q[...]], axis=0))

    def place_of(at_head):
        return slice(at_head * HALF, (at_head + 1) * HALF)

    def exps_plain(group, half):
        scores = scores_of(group, half, slice(0, GROUP * HALF))
        for at_head in range(GROUP):
            exps = jnp.exp2(scores[place_of(at_head), :] * LOG2_E)
            exps_s[group, half, :, place_of(at_head)] = exps.astype(BF16)

    def exps_shifted(group, half):
        for at_head in range(GROUP):
            rows = place_of(at_head)
            largest = jnp.max(scores_of(group, half, rows), axis=0, keepdims=True)
            exps = jnp.exp2((scores_of(group, half, rows) - largest) * LOG2_E)
            exps_s[group, half, :, rows] = exps.astype(BF16)

    def finish(group, half):
        rows = slice(half * HALF, (half + 1) * HALF)
        for at_head in range(GROUP):
            head = group * GROUP + at_head
            out = dot(value_s[head, :, rows], exps_s[group, half, :, place_of(at_head)])
            inverse = 1.0 / out[HEAD_DIM : HEAD_DIM + 1, :]
            inverse_ref[group, at_head : at_head + 1, rows] = inverse
            out_t_ref[head * HEAD_DIM : (head + 1) * HEAD_DIM, rows] = out[:HEAD_DIM, :] * inverse

    def run(exps_of):
        items = [(group, half) for group in range(2) for half in range(2)]
        for i in range(len(items) + 1):
            if i < len(items):
                exps_of(*items[i])
                copy_of(*items[i]).start()
            if i >= 1:
                finish(*items[i - 1])

    @pl.when(tame_s[0] == 1)
    def _():
        run(exps_plain)

    @pl.when(tame_s[0] == 0)
    def _():
        run(exps_shifted)

    out_t = out_t_ref[...]
    mixed_t_ref[...] = out_t.astype(BF16)
    mixed_ref[...] = out_t.T.astype(BF16)

    @pl.when(row == pl.num_programs(0) - 1)
    def _():
        for group in range(2):
            for half in range(2):
                copy_of(group, half).wait()


def attend_forward(marks, place, x, qk, x_t, qk_t, mine, other):
    total = x.shape[0]
    rows = total // SEQ
    by_row = lambda r, m, p: (r, 0)
    by_col = lambda r, m, p: (0, r)
    whole = lambda r, m, p: (0, 0)
    return pl.pallas_call(
        attend_kernel,
        out_shape=(
            jax.ShapeDtypeStruct((D, total), BF16),
            jax.ShapeDtypeStruct((total, D), BF16),
            jax.ShapeDtypeStruct((D, total), BF16),
            jax.ShapeDtypeStruct((D, total), F32),
            jax.ShapeDtypeStruct((2, 8, total), F32),
            jax.ShapeDtypeStruct((total, D), BF16),
            jax.ShapeDtypeStruct((D, total), BF16),
            jax.ShapeDtypeStruct((rows, 2, 2, HALF, GROUP * HALF), BF16),
            jax.ShapeDtypeStruct((D, 3 * D), BF16),
            jax.ShapeDtypeStruct((D, D), BF16),
            jax.ShapeDtypeStruct((VEC, D), F32),
        ),
        grid_spec=pltpu.PrefetchScalarGridSpec(
            num_scalar_prefetch=2,
            grid=(rows,),
            in_specs=[
                pl.BlockSpec((SEQ, D), by_row),
                pl.BlockSpec((SEQ, D), by_row),
                pl.BlockSpec((D, SEQ), by_col),
                pl.BlockSpec((D, SEQ), by_col),
                vspec(),
                vspec(),
            ],
            out_specs=[
                pl.BlockSpec((D, SEQ), by_col),
                pl.BlockSpec((SEQ, D), by_row),
                pl.BlockSpec((D, SEQ), by_col),
                pl.BlockSpec((D, SEQ), by_col),
                pl.BlockSpec((2, 8, SEQ), lambda r, m, p: (0, 0, r)),
                pl.BlockSpec((SEQ, D), by_row),
                pl.BlockSpec((D, SEQ), by_col),
                pl.BlockSpec(memory_space=pl.ANY),
                pl.BlockSpec((D, 3 * D), whole),
                pl.BlockSpec((D, D), whole),
                pl.BlockSpec((VEC, D), whole),
            ],
            scratch_shapes=[
                pltpu.VMEM((SEQ, D), BF16),
                pltpu.VMEM((HEADS, HEAD_DIM + 16, SEQ), BF16),
                pltpu.VMEM((HALF, LANES), BF16),
                pltpu.VMEM((LANES, HALF), BF16),
                pltpu.VMEM((2, GROUP * HALF, LANES), BF16),
                pltpu.VMEM((2, GROUP * HALF, 2 * LANES), BF16),
                pltpu.VMEM((3 * D, D), BF16),
                pltpu.VMEM((D, 8), F32),
                pltpu.SMEM((1,), jnp.int32),
                pltpu.VMEM((2, 2, HALF, GROUP * HALF), BF16),
                pltpu.SemaphoreType.DMA((4,)),
            ],
        ),
        compiler_params=params(dimension_semantics=("arbitrary",)),
        cost_estimate=pl.CostEstimate(
            flops=20_000_000_000, bytes_accessed=30_000_000, transcendentals=8_400_000
        ),
        name="attend_forward",
    )(marks, place, x, qk, x_t, qk_t, mine, other)


def feed_kernel(
    marks,
    place,
    x_ref,
    back_ref,
    mixed_ref,
    mixed_t_ref,
    proj_ref,
    mine_ref,
    other_ref,
    vector_ref,
    block_ref,
    resid_ref,
    mixed_grad_ref,
    mine_out,
    other_out,
    proj_out,
    vector_out,
    first_w,
    second_w,
    first_acc,
    second_acc,
    proj_acc,
    vector_acc,
    hidden_s,
    slope_s,
    pre_s,
    first_low_s,
    branch_low_s,
    attended_s,
    eye_s,
):
    step = pl.program_id(0)
    core = place[2]
    tall = D // VDP
    wide = FF // (2 * VCHIP)

    @pl.when(step == 0)
    def _():
        first_acc[...] = jnp.zeros_like(first_acc)
        second_acc[...] = jnp.zeros_like(second_acc)
        proj_acc[...] = jnp.zeros_like(proj_acc)
        vector_acc[...] = jnp.zeros_like(vector_acc)
        eye_s[...] = jnp.where(iota((D, D), 0) == iota((D, D), 1), 1.0, 0.0).astype(BF16)
        for d in range(VDP):
            rows = slice(d * tall, (d + 1) * tall)
            for c in range(VCHIP):
                for ref, half in ((mine_ref, core), (other_ref, 1 - core)):
                    to = pl.ds(pl.multiple_of((2 * c + half) * wide, wide), wide)
                    first_w[rows, to] = ref[c, d, 0]
                    second_w[rows, to] = ref[c, d, 1]

    bias_o, bias_2 = vector_ref[10:11, :], vector_ref[11:12, :]
    gain_1, shift_1 = vector_ref[12:13, :], vector_ref[13:14, :]
    gain_2, shift_2 = vector_ref[14:15, :], vector_ref[15:16, :]
    chunks = FF // CHUNK
    pair = 2

    def columns(at, count=1):
        return slice(at * CHUNK, (at + count) * CHUNK)

    def hidden_of(rows, at, pre):
        per = CHUNK // D
        bias = [vector_ref[at * per + i : at * per + i + 1, :] for i in range(per)]
        pre = (pre + jnp.concatenate(bias, axis=1)).astype(BF16)
        cube = BF16(GELU_A * GELU_B) * (pre * pre)
        gate = BF16(0.5) + BF16(0.5) * jnp.tanh(pre * (cube + BF16(GELU_A)))
        hidden_s[rows, columns(at)] = pre * gate
        slope_s[rows, columns(at)] = gate + (gate - gate * gate) * (
            pre * (BF16(6.0) * cube + BF16(2.0 * GELU_A))
        )

    def stages(sub):
        rows_at = sub * SUB
        rows = slice(rows_at, rows_at + SUB)
        attended = dot(mixed_ref[rows, :], proj_ref[...]) + bias_o
        norm_1, inverse_1 = norm_forward(x_ref[rows, :].astype(F32) + attended)
        first = norm_1 * gain_1 + shift_1
        first_low = first.astype(BF16)
        first_low_s[rows, :] = first_low
        yield
        branch = jnp.zeros((SUB, D), F32)
        for i in range(chunks + 1):
            if i < chunks:
                hidden_of(rows, i, dot(first_low, first_w[:, columns(i)]))
            if i >= pair and i % pair == 0:
                cols = columns(i - pair, pair)
                branch += dot_nt(hidden_s[rows, cols], second_w[:, cols])
            yield
        norm_2, inverse_2 = norm_forward(first + (branch + bias_2))
        block_ref[rows, :] = norm_2 * gain_2 + shift_2
        back = back_ref[rows, :].astype(F32)
        vector_acc[14:15, :] += jnp.sum(back * norm_2, axis=0, keepdims=True)
        vector_acc[15:16, :] += jnp.sum(back, axis=0, keepdims=True)
        resid_2 = norm_backward(back * gain_2, norm_2, inverse_2)
        branch_low = resid_2.astype(BF16)
        branch_low_s[rows, :] = branch_low
        vector_acc[11:12, :] += jnp.sum(branch_low.astype(F32), axis=0, keepdims=True)
        yield
        first_back = resid_2
        if sub == 1:
            branch_t = dot_nt(eye_s[...], branch_low_s[...]).astype(BF16)
            first_t = dot_nt(eye_s[...], first_low_s[...]).astype(BF16)
            first_t = jnp.concatenate([first_t, jnp.ones((16, TILE), BF16)], axis=0)
        for i in range(chunks + 1):
            if i < chunks:
                pull = dot(branch_low, second_w[:, columns(i)]).astype(BF16)
                pre_s[rows, columns(i)] = pull * slope_s[rows, columns(i)]
                if sub == 1:
                    second_acc[:, columns(i)] += dot(branch_t, hidden_s[:, columns(i)])
            if i >= 1 and sub == 1:
                cols = columns(i - 1)
                first_acc[:, cols] += dot(first_t, pre_s[:, cols])
            if i >= pair and i % pair == 0:
                cols = columns(i - pair, pair)
                first_back += dot_nt(pre_s[rows, cols], first_w[:, cols])
            yield
        vector_acc[12:13, :] += jnp.sum(first_back * norm_1, axis=0, keepdims=True)
        vector_acc[13:14, :] += jnp.sum(first_back, axis=0, keepdims=True)
        resid_1 = norm_backward(first_back * gain_1, norm_1, inverse_1)
        resid_ref[rows, :] = resid_1
        attended_low = resid_1.astype(BF16)
        attended_s[rows, :] = attended_low
        vector_acc[10:11, :] += jnp.sum(attended_low.astype(F32), axis=0, keepdims=True)
        mixed_grad_ref[:, rows] = dot_nt(proj_ref[...], attended_low).astype(BF16)
        yield

    ahead, behind = stages(0), stages(1)
    for _ in range(LEAD):
        next(ahead)
    running = [ahead, behind]
    while running:
        for program in list(running):
            if next(program, 0) == 0:
                running.remove(program)
    proj_acc[...] += dot(mixed_t_ref[...], attended_s[...])

    @pl.when(step == pl.num_programs(0) - 1)
    def _():
        for d in range(VDP):
            rows = slice(d * tall, (d + 1) * tall)
            for c in range(VCHIP):
                for ref, half in ((mine_out, core), (other_out, 1 - core)):
                    to = pl.ds(pl.multiple_of((2 * c + half) * wide, wide), wide)
                    ref[d, c, 0] = first_acc[rows, to].astype(BF16)
                    ref[d, c, 1] = second_acc[rows, to].astype(BF16)
        proj_out[...] = proj_acc[...]
        for at in range(FF // D):
            vector_out[at : at + 1, :] = first_acc[D : D + 1, at * D : (at + 1) * D]
        vector_out[FF // D :, :] = vector_acc[FF // D :, :]


def feed_forward(marks, place, x, back, mixed, mixed_t, proj, mine, other, vector):
    total = x.shape[0]
    tile = lambda i, m, p: (i, 0)
    by_col = lambda i, m, p: (0, i)
    whole = lambda i, m, p: (0, 0)
    whole5 = lambda i, m, p: (0, 0, 0, 0, 0)
    return pl.pallas_call(
        feed_kernel,
        out_shape=(
            jax.ShapeDtypeStruct((total, D), F32),
            jax.ShapeDtypeStruct((total, D), F32),
            jax.ShapeDtypeStruct((D, total), BF16),
            jax.ShapeDtypeStruct(mine.shape, BF16),
            jax.ShapeDtypeStruct(mine.shape, BF16),
            jax.ShapeDtypeStruct((D, D), F32),
            jax.ShapeDtypeStruct((VEC, D), F32),
        ),
        grid_spec=pltpu.PrefetchScalarGridSpec(
            num_scalar_prefetch=2,
            grid=(total // TILE,),
            in_specs=[
                pl.BlockSpec((TILE, D), tile),
                pl.BlockSpec((TILE, D), tile),
                pl.BlockSpec((TILE, D), tile),
                pl.BlockSpec((D, TILE), by_col),
                pl.BlockSpec((D, D), whole),
                vspec(),
                vspec(),
                pl.BlockSpec((VEC, D), whole),
            ],
            out_specs=[
                pl.BlockSpec((TILE, D), tile),
                pl.BlockSpec((TILE, D), tile),
                pl.BlockSpec((D, TILE), by_col),
                pl.BlockSpec(mine.shape, whole5),
                pl.BlockSpec(mine.shape, whole5),
                pl.BlockSpec((D, D), whole),
                pl.BlockSpec((VEC, D), whole),
            ],
            scratch_shapes=[
                pltpu.VMEM((D, FF), BF16),
                pltpu.VMEM((D, FF), BF16),
                pltpu.VMEM((D + 16, FF), F32),
                pltpu.VMEM((D, FF), F32),
                pltpu.VMEM((D, D), F32),
                pltpu.VMEM((VEC, D), F32),
                pltpu.VMEM((TILE, FF), BF16),
                pltpu.VMEM((TILE, FF), BF16),
                pltpu.VMEM((TILE, FF), BF16),
                pltpu.VMEM((TILE, D), BF16),
                pltpu.VMEM((TILE, D), BF16),
                pltpu.VMEM((TILE, D), BF16),
                pltpu.VMEM((D, D), BF16),
            ],
        ),
        compiler_params=params(dimension_semantics=("arbitrary",)),
        cost_estimate=pl.CostEstimate(
            flops=14_000_000_000, bytes_accessed=15_000_000, transcendentals=4_200_000
        ),
        name="feed_forward",
    )(marks, place, x, back, mixed, mixed_t, proj, mine, other, vector)


def pull_kernel(
    marks,
    place,
    grad_t_ref,
    query_t_ref,
    value_ref,
    key_t_ref,
    out_t_ref,
    inverse_ref,
    exps_ref,
    qk_t_ref,
    x_t_ref,
    proj_ref,
    low_ref,
    own_ref,
    other_ref,
    sums_ref,
    dot_s,
    query_g,
    key_g,
    value_g,
    acc,
    sum_acc,
    value_s,
    scaled_t_s,
    score_s,
):
    group = pl.program_id(0)
    row = pl.program_id(1)
    begin = marks[row, 3]

    @pl.when(row == 0)
    def _():
        acc[...] = jnp.zeros_like(acc)
        sum_acc[...] = jnp.zeros_like(sum_acc)

    grad_t = grad_t_ref[...].astype(F32)
    head_of = iota((1, LANES), 1) // HEAD_DIM
    for at_head in range(GROUP):
        heads = slice(at_head * HEAD_DIM, (at_head + 1) * HEAD_DIM)
        part = grad_t[heads, :] * inverse_ref[0, at_head : at_head + 1, :]
        dot_s[at_head : at_head + 1, :] = jnp.sum(part * out_t_ref[heads, :], axis=0, keepdims=True)
        part = part.astype(BF16)
        scaled_t_s[heads, :] = part
        mask = jnp.where(head_of == at_head, 1.0, 0.0).astype(BF16)
        for half in range(2):
            rows = slice(half * HALF, (half + 1) * HALF)
            to = slice(at_head * HALF, (at_head + 1) * HALF)
            value_s[half, to, :] = value_ref[rows, :] * mask

    def score_grads_of(half, block):
        at = half * HALF + block * QBLOCK
        pulls = dot(value_s[half], scaled_t_s[:, at : at + QBLOCK])
        for at_head in range(GROUP):
            cols = slice(at_head * HALF + block * QBLOCK, at_head * HALF + (block + 1) * QBLOCK)
            pull = pulls[at_head * HALF : (at_head + 1) * HALF, :]
            pull = (pull - dot_s[at_head : at_head + 1, at : at + QBLOCK]).astype(BF16)
            score_s[half, :, cols] = exps_ref[0, 0, half, :, cols] * pull

    def finish(half, at_head):
        cols = slice(at_head * HALF, (at_head + 1) * HALF)
        rows = slice(half * HALF, (half + 1) * HALF)
        heads = slice(at_head * HEAD_DIM, (at_head + 1) * HEAD_DIM)
        score_grad = score_s[half, :, cols]
        value_g[heads, rows] = dot_nt(scaled_t_s[heads, rows], exps_ref[0, 0, half, :, cols])
        query_g[heads, rows] = dot(key_t_ref[heads, rows], score_grad)
        key_g[heads, rows] = dot_nt(query_t_ref[heads, rows], score_grad)

    blocks = HALF // QBLOCK
    each = GROUP // blocks
    for block in range(blocks):
        score_grads_of(0, block)
    for block in range(blocks):
        score_grads_of(1, block)
        for at_head in range(each * block, each * (block + 1)):
            finish(0, at_head)
    for at_head in range(GROUP):
        finish(1, at_head)
    query_low = query_g[...].astype(BF16)
    both_low = jnp.concatenate([key_g[...].astype(BF16), value_g[...].astype(BF16)], axis=0)
    ones = jnp.ones((16, SEQ), BF16)
    sum_acc[0:1, :] += dot_nt(ones, query_low)[0:1, :] * SCALE
    sum_acc[1:2, :] += dot_nt(ones, both_low[LANES:, :])[0:1, :]
    qk_t = qk_t_ref[...]
    both = dot_nt(qk_t, jnp.concatenate([query_low, both_low[:LANES, :]], axis=0))
    acc[:, :LANES] += both[:, :LANES] * SCALE
    acc[:, LANES : 2 * LANES] += both[:, LANES:]
    acc[:, 2 * LANES :] += dot_nt(x_t_ref[...], both_low[LANES:, :])
    low_ref[0, :LANES, :] = query_low
    low_ref[0, LANES:, :] = both_low

    def write(ref):
        tall = D // VDP
        for d in range(VDP):
            rows = slice(d * tall, (d + 1) * tall)
            for c in range(3):
                ref[d, c] = acc[rows, c * LANES : (c + 1) * LANES].astype(BF16)
            ref[d, 3] = proj_ref[rows, :].astype(BF16)

    last = row == pl.num_programs(1) - 1

    @pl.when(last & (group == place[2]))
    def _():
        write(own_ref)

    @pl.when(last & (group != place[2]))
    def _():
        write(other_ref)

    @pl.when(last)
    def _():
        sums_ref[pl.ds(group, 1)] = sum_acc[...][None]


def attend_back(marks, place, grad_t, query_t, value, key_t, out_t, inverse, exps, qk_t, x_t, proj):
    total = value.shape[0]
    rows = total // SEQ
    by_both = lambda g, r, m, p: (g, r)
    by_col = lambda g, r, m, p: (0, r)
    grads = jax.ShapeDtypeStruct((VDP, VCHIP, D // VDP, LANES), BF16)
    grads_spec = pl.BlockSpec(grads.shape, lambda g, r, m, p: (0, 0, 0, 0))
    return pl.pallas_call(
        pull_kernel,
        out_shape=(
            jax.ShapeDtypeStruct((2, 3 * LANES, total), BF16),
            grads,
            grads,
            jax.ShapeDtypeStruct((2, 8, LANES), F32),
        ),
        grid_spec=pltpu.PrefetchScalarGridSpec(
            num_scalar_prefetch=2,
            grid=(2, rows),
            in_specs=[
                pl.BlockSpec((LANES, SEQ), by_both),
                pl.BlockSpec((LANES, SEQ), by_both),
                pl.BlockSpec((SEQ, LANES), lambda g, r, m, p: (r, g)),
                pl.BlockSpec((LANES, SEQ), by_both),
                pl.BlockSpec((LANES, SEQ), by_both),
                pl.BlockSpec((1, 8, SEQ), lambda g, r, m, p: (g, 0, r)),
                pl.BlockSpec((1, 1, 2, HALF, GROUP * HALF), lambda g, r, m, p: (r, g, 0, 0, 0)),
                pl.BlockSpec((D, SEQ), by_col),
                pl.BlockSpec((D, SEQ), by_col),
                pl.BlockSpec((D, LANES), lambda g, r, m, p: (0, g)),
            ],
            out_specs=[
                pl.BlockSpec((1, 3 * LANES, SEQ), lambda g, r, m, p: (g, 0, r)),
                grads_spec,
                grads_spec,
                pl.BlockSpec((2, 8, LANES), lambda g, r, m, p: (0, 0, 0)),
            ],
            scratch_shapes=[
                pltpu.VMEM((8, SEQ), F32),
                pltpu.VMEM((LANES, SEQ), F32),
                pltpu.VMEM((LANES, SEQ), F32),
                pltpu.VMEM((LANES, SEQ), F32),
                pltpu.VMEM((D, 3 * LANES), F32),
                pltpu.VMEM((8, LANES), F32),
                pltpu.VMEM((2, GROUP * HALF, LANES), BF16),
                pltpu.VMEM((LANES, SEQ), BF16),
                pltpu.VMEM((2, HALF, GROUP * HALF), BF16),
            ],
        ),
        compiler_params=params(dimension_semantics=("arbitrary", "arbitrary")),
        cost_estimate=pl.CostEstimate(
            flops=36_000_000_000, bytes_accessed=30_000_000, transcendentals=0
        ),
        name="attend_back",
    )(marks, place, grad_t, query_t, value, key_t, out_t, inverse, exps, qk_t, x_t, proj)


def input_kernel(
    marks, low_ref, weight_ref, resid_ref, turned_ref, block_ref, input_ref, token_ref
):
    token_ref[...] = jnp.zeros_like(token_ref)
    at = slice(0, LANES), slice(LANES, 2 * LANES), slice(2 * LANES, 3 * LANES)
    parts = [jnp.concatenate([low_ref[0, rows, :], low_ref[1, rows, :]], axis=0) for rows in at]
    pulled = dot(weight_ref[:, :D], parts[0]) * SCALE + (
        dot(weight_ref[:, D : 2 * D], parts[1]) + dot(weight_ref[:, 2 * D :], parts[2])
    )
    begin = marks[pl.program_id(0), 3]
    input_ref[...] = pltpu.roll(resid_ref[...] + pulled.T, begin, 0)
    block_ref[...] = pltpu.roll(turned_ref[...], begin, 0)


def input_pull(marks, low, weight, resid, turned):
    total = resid.shape[0]
    by_row = pl.BlockSpec((SEQ, D), lambda r, m: (r, 0))
    return pl.pallas_call(
        input_kernel,
        out_shape=(
            jax.ShapeDtypeStruct((total, D), F32),
            jax.ShapeDtypeStruct((total, D), F32),
            jax.ShapeDtypeStruct((8, LANES), F32),
        ),
        grid_spec=pltpu.PrefetchScalarGridSpec(
            num_scalar_prefetch=1,
            grid=(total // SEQ,),
            in_specs=[
                pl.BlockSpec((2, 3 * LANES, SEQ), lambda r, m: (0, 0, r)),
                pl.BlockSpec((D, 3 * D), lambda r, m: (0, 0)),
                by_row,
                by_row,
            ],
            out_specs=[by_row, by_row, pl.BlockSpec((8, LANES), lambda r, m: (0, 0))],
        ),
        compiler_params=params(dimension_semantics=("arbitrary",)),
        cost_estimate=pl.CostEstimate(
            flops=1_000_000_000, bytes_accessed=8_000_000, transcendentals=0
        ),
        name="input_pull",
    )(marks, low, weight, resid, turned)


def two_terms(rows):
    high = rows.astype(BF16)
    return jnp.concatenate([high.astype(F32), rows - high.astype(F32)], axis=0)


def column_to_row(columns, rows):
    lane = iota((rows, LANES), 1)
    wide = jnp.zeros((rows, LANES), F32)
    for i, column in enumerate(columns):
        wide = jnp.where(lane == i, column, wide)
    return wide.T[:8, :]


def total_of(array):
    return jnp.sum(jnp.sum(array, axis=0, keepdims=True), axis=1, keepdims=True)


def tail_send_kernel(
    place,
    mine_ref,
    got_ref,
    vector_ref,
    sums_ref,
    ffn_ref,
    send_ref,
    grad_1,
    grad_2,
    grad_ref,
):
    tall = D // VDP
    low, high = sums_ref[0], sums_ref[1]
    vector = jnp.concatenate(
        [
            vector_ref[:8, :],
            jnp.concatenate([low[:2], high[:2]], axis=1),
            vector_ref[10:, :],
        ],
        axis=0,
    )
    piece, across = [], []
    for kind in range(2):
        total = ffn_ref[0, kind].astype(F32)
        for at in range(1, VDP * VCHIP):
            total = total + ffn_ref[at, kind].astype(F32)
        (grad_1, grad_2)[kind][...] = total
        grad_ref[kind] = total
        square = total * total + EPS_ONE
        down = jnp.sum(square, axis=0, keepdims=True)
        piece += [down[:, :LANES], down[:, LANES:]]
        across.append(jnp.sum(square, axis=1, keepdims=True))
    across = column_to_row(across, tall)
    across = jnp.concatenate([across[0:1], across[1:2]], axis=1)
    stat = two_terms(jnp.concatenate([across] + piece + [jnp.zeros((1, LANES), F32)], axis=0))
    rows = VEC // VDP
    for d in range(VDP):
        for c in range(VCHIP):
            at = d * VCHIP + c
            both = mine_ref[d, c].astype(F32) + got_ref[d, c].astype(F32)
            send_ref[at, :tall, :] = both.astype(BF16)
            part = vector[d * rows : (d + 1) * rows, c * 64 : (c + 1) * 64]
            part = jnp.concatenate([part, jnp.zeros((rows, LANES - 64), F32)], axis=1)
            send_ref[at, tall:, :] = jnp.concatenate([part, stat], axis=0).astype(BF16)


def tail_reduce_kernel(
    place,
    earlier_ref,
    got_ref,
    ffn_grad_ref,
    attn_ref,
    first_ref,
    second_ref,
    rows_0,
    rows_1,
    rows_2,
    cols_0,
    cols_1,
    cols_2,
    vector_ref,
    moment_ref,
    grad_ref,
    grad_kept,
    cols_out_1,
    cols_out_2,
    cols_kept,
    send_ref,
):
    decay = 1.0 - STEP ** (-0.8)
    chip = place[1]
    dp = place[0]
    tall = attn_ref.shape[0]
    rows, width = vector_ref.shape
    pieces = VDP * VCHIP
    lane = iota((1, LANES), 1)
    total = got_ref[0, :tall, :].astype(F32)
    part = got_ref[0, tall:, :].astype(F32)[:rows]
    for at in range(1, pieces):
        total = total + got_ref[at, :tall, :].astype(F32)
        part = part + got_ref[at, tall:, :].astype(F32)[:rows]
    grad_ref[...] = total
    grad_kept[...] = total
    low = total.astype(BF16)

    def stat_of(at):
        both = got_ref[pl.ds(at, 1), tall:, :][0].astype(F32)[rows:]
        return both[:6] + both[6:12]

    down = jnp.zeros((6, LANES), F32)
    for d in range(VDP):
        down = down + stat_of(d * VCHIP + chip)
    mine = jnp.zeros((1, LANES), F32)
    for c in range(VCHIP):
        mine = mine + stat_of(dp * VCHIP + c)[0:1]
    row_total = tall * VDP
    count = first_ref.shape[1] * 2 * VCHIP
    share = (0.5 * decay) * jnp.concatenate([rows_1[...], rows_2[...]], axis=1) + (1.0 - decay) * (
        mine / count
    )
    scalars = jnp.zeros((1, LANES), F32)
    weighted = []
    for i, (old_ref, out_ref) in enumerate(((cols_1, cols_out_1), (cols_2, cols_out_2))):
        sums = jnp.concatenate([down[1 + 2 * i : 2 + 2 * i], down[2 + 2 * i : 3 + 2 * i]], axis=1)
        cols = decay * old_ref[...] + (1.0 - decay) * (sums / row_total)
        out_ref[...] = cols
        cols_kept[i : i + 1, :] = cols
        grad = ffn_grad_ref[i]
        weighted.append(jnp.sum(grad * grad / cols, axis=1, keepdims=True))
    weighted = column_to_row(weighted, tall)
    weighted = jnp.concatenate([weighted[0:1], weighted[1:2]], axis=1)
    for i, ref in enumerate((attn_ref, first_ref, second_ref)):
        weight = ref[...]
        scalars = jnp.where(lane == 64 + i, total_of(weight * weight), scalars)
    scalars = jnp.concatenate([rows_0[...], scalars[:, tall:]], axis=1)
    vector = vector_ref[...]
    power = jnp.sum(vector * vector, axis=1, keepdims=True)
    lines = jnp.concatenate(
        [part[:, :64], moment_ref[...], jnp.broadcast_to(power, (rows, LANES - 64 - width))], axis=1
    )
    piece = jnp.concatenate(
        [
            two_terms(lines),
            two_terms(jnp.concatenate([cols_0[...], scalars], axis=0)),
            two_terms(jnp.concatenate([share, weighted], axis=0)),
        ],
        axis=0,
    ).astype(BF16)
    for at in range(pieces):
        send_ref[at, :tall, :] = low
        send_ref[at, tall:, :] = piece


def tail_apply_kernel(
    place,
    mine_ref,
    other_ref,
    grad_ref,
    ffn_grad_ref,
    cols_kept,
    weight_0,
    weight_1,
    weight_2,
    rows_0,
    cols_0,
    vector_ref,
    moment_ref,
    new_0,
    new_1,
    new_2,
    rows_out,
    rows_out_1,
    rows_out_2,
    cols_out,
    vector_grad_ref,
    moment_out,
    vector_out,
    sums_s,
    rows_s,
):
    decay = 1.0 - STEP ** (-0.8)
    dp, chip, core = place[0], place[1], place[2]
    tall = weight_0.shape[0]
    rows, width = vector_ref.shape
    fsdp = 2 * VCHIP
    lane = iota((1, LANES), 1)
    refs = (mine_ref, other_ref)
    row_total = float(tall * VDP)
    col_total = float(LANES * fsdp)

    def lines_of(ref, at):
        both = ref[at, tall:, :].astype(F32)
        return both[0:4] + both[4:8], both[8:10] + both[10:12], both[12:14] + both[14:16]

    scalars = jnp.zeros((1, LANES), F32)
    for ref in refs:
        for at in range(VDP * VCHIP):
            scalars = scalars + lines_of(ref, at)[1][1:2]
    scalar = lambda at: jnp.sum(jnp.where(lane == at, scalars, 0.0), axis=1, keepdims=True)

    tile, fresh = [], []
    for d in range(VDP):
        wide = jnp.zeros((tall, LANES), F32)
        for ref in refs:
            for c in range(VCHIP):
                block = ref[d * VCHIP + c, :tall, :].astype(F32)
                wide = wide + (block * block + EPS_ONE)
        fresh.append(jnp.sum(wide, axis=1, keepdims=True))
        tile.append(lines_of(mine_ref, d * VCHIP)[1][1:2])
    tile = jnp.concatenate(tile + [jnp.zeros((LANES - VDP, LANES), F32)], axis=0).T
    mean = jnp.zeros((1, 1), F32)
    new_rows = []
    for d in range(VDP):
        new = decay * tile[:tall, d : d + 1] + (1.0 - decay) * (fresh[d] / col_total)
        new_rows.append(1.0 / new)
        mean = mean + jnp.sum(new, axis=0, keepdims=True)
        sums_s[d] = jnp.broadcast_to(fresh[d], (tall, LANES))
    mean = mean / row_total
    mine = sums_s[pl.ds(dp, 1)][0]
    rows_s[...] = mine.T
    rows_new = decay * rows_0[...] + (1.0 - decay) * (rows_s[0:1, :tall] / col_total)
    rows_out[...] = rows_new
    power = jnp.zeros((1, 1), F32)
    for half, ref in enumerate(refs):
        for c in range(VCHIP):
            down = jnp.zeros((tall, LANES), F32)
            weighted = jnp.zeros((tall, LANES), F32)
            for d in range(VDP):
                block = ref[d * VCHIP + c, :tall, :].astype(F32)
                square = block * block
                down = down + (square + EPS_ONE)
                weighted = weighted + square * new_rows[d]
            down = jnp.sum(down, axis=0, keepdims=True)
            old = lines_of(ref, c)[1][0:1]
            cols = decay * old + (1.0 - decay) * (down / row_total)
            weighted = jnp.sum(weighted, axis=0, keepdims=True) / cols
            power = power + jnp.sum(weighted, axis=1, keepdims=True)
            if half == 0:
                sums_s[VDP + c] = jnp.broadcast_to(down, (tall, LANES))
    power = power * mean
    down = sums_s[pl.ds(VDP + chip, 1)][0][0:1, :]
    cols_new = decay * cols_0[...] + (1.0 - decay) * (down / row_total)
    cols_out[...] = cols_new
    ffn_rows = jnp.zeros((1, LANES), F32)
    ffn_means = jnp.zeros((1, LANES), F32)
    ffn_powers = jnp.zeros((1, LANES), F32)
    for d in range(VDP):
        fresh = lines_of(mine_ref, d * VCHIP)[2][0:1] + lines_of(other_ref, d * VCHIP)[2][0:1]
        weighted = jnp.zeros((1, LANES), F32)
        for ref in refs:
            for c in range(VCHIP):
                weighted = weighted + lines_of(ref, d * VCHIP + c)[2][1:2]
        ffn_rows = jnp.where(dp == d, fresh, ffn_rows)
        ffn_means = ffn_means + fresh
        ffn_powers = ffn_powers + weighted / fresh
    parts = (slice(0, tall), slice(tall, 2 * tall))
    ffn_means = [jnp.sum(ffn_means[:, part], axis=1, keepdims=True) / row_total for part in parts]
    ffn_powers = [
        jnp.sum(ffn_powers[:, part], axis=1, keepdims=True) * ffn_mean
        for part, ffn_mean in zip(parts, ffn_means)
    ]
    ffn_rows = [ffn_rows[:, part] for part in parts]
    rows_out_1[...] = ffn_rows[0]
    rows_out_2[...] = ffn_rows[1]
    stacked = jnp.concatenate([rows_new] + ffn_rows + [jnp.zeros((5, tall), F32)], axis=0)
    stacked = jnp.concatenate([stacked, jnp.zeros((8, LANES - tall), F32)], axis=1)
    stacked = jnp.concatenate([stacked, jnp.zeros((LANES - 8, LANES), F32)], axis=0).T
    update_0 = grad_ref[...] * lax.rsqrt(stacked[:tall, 0:1] * cols_new / mean)
    ffn_updates = [
        ffn_grad_ref[i]
        * lax.rsqrt(stacked[:tall, i + 1 : i + 2] * cols_kept[i : i + 1, :] / ffn_means[i])
        for i in range(2)
    ]
    powers = (power, ffn_powers[0], ffn_powers[1])
    for i, (update, weight, new) in enumerate(
        (
            (update_0, weight_0, new_0),
            (ffn_updates[0], weight_1, new_1),
            (ffn_updates[1], weight_2, new_2),
        )
    ):
        entries = float(weight.shape[0] * weight.shape[1] * VDP * fsdp)
        clip = jnp.maximum(1.0, jnp.sqrt(powers[i] / entries) / CLIP_LIMIT)
        rate = STEP_RATE * jnp.maximum(EPS_TWO, jnp.sqrt(scalar(64 + i) / entries))
        new[...] = weight[...] - rate / clip * update
    powers, sizes = [], []
    for d in range(VDP):
        power = jnp.zeros((rows, 1), F32)
        size = jnp.zeros((rows, 1), F32)
        for c in range(VCHIP):
            at = d * VCHIP + c
            first, second = lines_of(mine_ref, at)[0], lines_of(other_ref, at)[0]
            both = first[:, :64] + second[:, :64]
            size = size + first[:, LANES - 1 :] + second[:, LANES - 1 :]
            near = jnp.where(core == 0, first[:, 64 : 64 + width], second[:, 64 : 64 + width])
            far = jnp.where(core == 0, second[:, 64 : 64 + width], first[:, 64 : 64 + width])
            moment = jnp.concatenate([near, far], axis=1)
            moment = decay * moment + (1.0 - decay) * (both * both + EPS_ONE)
            power = power + jnp.sum(both * both / moment, axis=1, keepdims=True)
            wide = jnp.concatenate([both, jnp.zeros((rows, LANES - 64), F32)], axis=1)
            sums_s[2 * VDP + at, :rows, :] = wide
        powers.append(power)
        sizes.append(size)
    both = sums_s[pl.ds(2 * VDP + dp * VCHIP + chip, 1), :rows, :][0]
    vector_grad = jnp.where(core == 0, both[:, :width], both[:, width : 2 * width])
    vector_grad_ref[...] = vector_grad
    moment = decay * moment_ref[...] + (1.0 - decay) * (vector_grad * vector_grad + EPS_ONE)
    moment_out[...] = moment
    step = vector_grad * lax.rsqrt(moment)
    bias = VDP // 2
    bias_power = sum(jnp.sum(power, axis=0, keepdims=True) for power in powers[:bias])
    bias_size = sum(jnp.sum(size, axis=0, keepdims=True) for size in sizes[:bias])
    power, size = powers[bias], sizes[bias]
    for d in range(bias + 1, VDP):
        power = jnp.where(dp == d, powers[d], power)
        size = jnp.where(dp == d, sizes[d], size)
    is_bias = dp < bias
    power = jnp.where(is_bias, bias_power, power)
    size = jnp.where(is_bias, bias_size, size)
    count = jnp.where(is_bias, float(FF), float(D))
    clip = jnp.maximum(1.0, jnp.sqrt(power / count) / CLIP_LIMIT)
    rate = STEP_RATE * jnp.maximum(EPS_TWO, jnp.sqrt(size / count))
    vector_out[...] = vector_ref[...] - rate / clip * step


def whole_call(kernel, name, place, outs, *operands, scratch=(), earlier=None):
    tied = () if earlier is None else (earlier,)
    return pl.pallas_call(
        kernel,
        out_shape=[jax.ShapeDtypeStruct(shape, kind) for shape, kind in outs],
        in_specs=[pl.BlockSpec(memory_space=pltpu.SMEM)]
        + [pl.BlockSpec(memory_space=pl.ANY)] * len(tied)
        + [vspec()] * len(operands),
        out_specs=[vspec()] * len(outs),
        scratch_shapes=list(scratch),
        compiler_params=params(16),
        name=name,
    )(place, *tied, *operands)


def core_swap(block):
    return lax.ppermute(block, "core", [(0, 1), (1, 0)])


def exchange(blocks, axes):
    return lax.all_to_all(blocks, axes, split_axis=0, concat_axis=0, tiled=True)


def after(value, *earlier, mib=8):
    return pl.pallas_call(
        lambda *refs: None,
        out_shape=jax.ShapeDtypeStruct(value.shape, value.dtype),
        in_specs=[pl.BlockSpec(memory_space=pltpu.HBM)] * (1 + len(earlier)),
        out_specs=pl.BlockSpec(memory_space=pltpu.HBM),
        input_output_aliases={0: 0},
        compiler_params=params(mib),
        name="after",
    )(value, *earlier)


def pair_kernel(mine_ref, got_ref, out_ref):
    out_ref[...] = (mine_ref[...].astype(F32) + got_ref[...].astype(F32)).astype(BF16)


def pair_sum(mine, got):
    return pl.pallas_call(
        pair_kernel,
        out_shape=jax.ShapeDtypeStruct(mine.shape, BF16),
        in_specs=[vspec(), vspec()],
        out_specs=vspec(),
        compiler_params=params(16),
        name="pair_sum",
    )(mine, got)


CHIPS = ("dp", "chip")
ALL = ("dp", "chip", "core")


def layer(place, weights, segment_ids, tokens, cotangent, ffn_weights, send_core, send_ffn):
    table = jnp.asarray(encode_table())
    qk, x, qk_t, x_t, back, marks = place_tokens(segment_ids, tokens, cotangent, table)
    query_t, value, key_t, out_t, inverse, mixed, mixed_t, exps, weight, proj, vector = attend_forward(
        marks, place, x, qk, x_t, qk_t, *weights(marks)
    )
    ffn_mine, ffn_other = ffn_weights(marks, vector)
    block_out, resid, grad_t, ffn_mine, ffn_other, proj_g, vector_g = feed_forward(
        marks, place, x, back, mixed, mixed_t, proj, ffn_mine, ffn_other, vector
    )
    ffn_got, grad_t = send_ffn(ffn_mine, ffn_other, grad_t)
    low, grads_own, grads_other, sums = attend_back(
        marks, place, grad_t, query_t, value, key_t, out_t, inverse, exps, qk_t, x_t, proj_g
    )
    attn_got = send_core(grads_other)
    pulled = input_pull(marks, low, weight, resid, block_out)
    return pulled, grads_own, grads_other, attn_got, sums, vector_g, ffn_got


def body(
    tokens,
    cotangent,
    segment_ids,
    attn_weight,
    ffn_in,
    ffn_out,
    vectors,
    attn_rows,
    attn_cols,
    in_rows,
    in_cols,
    out_rows,
    out_cols,
    vector_moment,
):
    place = jnp.stack([lax.axis_index("dp"), lax.axis_index("chip"), lax.axis_index("core")])
    place = place.astype(jnp.int32)
    pieces = VDP * VCHIP
    tall, wide = attn_weight.shape
    rows_v, cols_v = vectors.shape
    split = lambda array: array.reshape((VDP, VCHIP) + array.shape[1:])
    attn_sent, ffn_low = pack_attn(place, attn_weight, ffn_in, ffn_out, vectors)
    attn_mine = exchange(attn_sent, CHIPS)

    parts = [
        lax.ppermute(ffn_low, "dp", [(i, i ^ step) for i in range(VDP)]) for step in range(1, VDP)
    ]
    ffn_sent = pack_ffn(place, ffn_low, parts)

    def attn_weights(marks):
        mine = split(after(attn_mine, marks, *parts))
        return mine, core_swap(mine)

    def ffn_weights(marks, vector):
        got = exchange(after(ffn_sent, marks), "chip")
        ffn_mine = after(got, vector)
        return ffn_mine, core_swap(ffn_mine)

    def send_ffn(mine, other, grad_t):
        both = pair_sum(mine, core_swap(other))
        got = exchange(both.reshape((pieces,) + mine.shape[2:]), CHIPS)
        return got, after(grad_t, both, mib=56)

    (
        pulled,
        grads_own,
        grads_other,
        attn_got,
        sums,
        vector_g,
        ffn_got,
    ) = layer(place, attn_weights, segment_ids, tokens, cotangent, ffn_weights, core_swap, send_ffn)
    lay = lambda stat: stat.reshape(1, -1)
    rows_old = (lay(attn_rows), lay(in_rows), lay(out_rows))
    cols_old = (lay(attn_cols), lay(in_cols), lay(out_cols))
    weights_old = (attn_weight, ffn_in, ffn_out)
    sent, in_grad, out_grad, ffn_grad = whole_call(
        tail_send_kernel,
        "tail_send",
        place,
        [
            ((pieces, tall + VROWS, LANES), BF16),
            (ffn_in.shape, F32),
            (ffn_out.shape, F32),
            ((2,) + ffn_in.shape, F32),
        ],
        grads_own,
        attn_got,
        vector_g,
        sums,
        ffn_got,
    )
    block_out, input_grad, token = pulled
    got = exchange(sent, CHIPS)
    attn_grad, attn_kept, cols_new_1, cols_new_2, cols_kept, sent = whole_call(
        tail_reduce_kernel,
        "tail_reduce",
        place,
        [
            (attn_weight.shape, F32),
            (attn_weight.shape, F32),
            (cols_old[1].shape, F32),
            (cols_old[2].shape, F32),
            ((2, ffn_in.shape[1]), F32),
            ((pieces, tall + VROWS, LANES), BF16),
        ],
        got,
        ffn_grad,
        *weights_old,
        *rows_old,
        *cols_old,
        vectors,
        vector_moment,
        earlier=token,
    )
    mine = exchange(sent, CHIPS)
    attn_new, in_new, out_new, rows_new_0, rows_new_1, rows_new_2, cols_new_0, vector_grad, moment_new, vectors_new = whole_call(
        tail_apply_kernel,
        "tail_apply",
        place,
        [
            (attn_weight.shape, F32),
            (ffn_in.shape, F32),
            (ffn_out.shape, F32),
            (rows_old[0].shape, F32),
            (rows_old[1].shape, F32),
            (rows_old[2].shape, F32),
            (cols_old[0].shape, F32),
            (vectors.shape, F32),
            (vectors.shape, F32),
            (vectors.shape, F32),
        ],
        mine,
        core_swap(mine),
        attn_kept,
        ffn_grad,
        cols_kept,
        *weights_old,
        rows_old[0],
        cols_old[0],
        vectors,
        vector_moment,
        scratch=[
            pltpu.VMEM((2 * VDP + pieces, tall, LANES), F32),
            pltpu.VMEM((LANES, tall), F32),
        ],
    )
    return (
        block_out,
        input_grad,
        attn_grad,
        in_grad,
        out_grad,
        vector_grad,
        rows_new_0.reshape(-1),
        cols_new_0.reshape(-1),
        rows_new_1.reshape(-1),
        cols_new_1.reshape(-1),
        rows_new_2.reshape(-1),
        cols_new_2.reshape(-1),
        moment_new,
        attn_new,
        in_new,
        out_new,
        vectors_new,
    )


def gather_all(block):
    shape = (lax.axis_size("dp"), lax.axis_size("chip") * 2)
    count = shape[0] * shape[1]
    got = exchange(jnp.broadcast_to(block[None], (count,) + block.shape), ALL)
    return got.reshape(shape + block.shape)


def unblock(parts):
    dp_count, fsdp_count, rows, cols = parts.shape
    return parts.transpose(0, 2, 1, 3).reshape(dp_count * rows, fsdp_count * cols)


def scatter_sum(full):
    dp_count = lax.axis_size("dp")
    fsdp_count = lax.axis_size("chip") * 2
    rows, cols = full.shape
    by_col = full.astype(BF16).reshape(rows, fsdp_count, cols // fsdp_count).transpose(1, 0, 2)
    got = exchange(by_col, ("chip", "core"))
    part = jnp.sum(got.astype(F32), axis=0).astype(BF16)
    by_row = part.reshape(dp_count, rows // dp_count, cols // fsdp_count)
    return jnp.sum(exchange(by_row, "dp").astype(F32), axis=0)


def body_any(
    tokens,
    cotangent,
    segment_ids,
    attn_weight,
    ffn_in,
    ffn_out,
    vectors,
    attn_rows,
    attn_cols,
    in_rows,
    in_cols,
    out_rows,
    out_cols,
    vector_moment,
):
    dp_count = lax.axis_size("dp")
    fsdp_count = lax.axis_size("chip") * 2
    dp_place = lax.axis_index("dp")
    fsdp_place = lax.axis_index("chip") * 2 + lax.axis_index("core")
    rows_w = attn_weight.shape[0]
    rows_v = vectors.shape[0]
    place = jnp.zeros((3,), jnp.int32)
    full_attn = unblock(gather_all(attn_weight.astype(BF16)))
    full_vector = unblock(gather_all(vectors.astype(BF16)))
    full_ffn = jnp.stack(
        [unblock(gather_all(ffn_in.astype(BF16))), unblock(gather_all(ffn_out.astype(BF16)))]
    )
    tall = D // VDP
    cut = full_attn.reshape(VDP, tall, VCHIP, 2, LANES).transpose(3, 0, 2, 1, 4)
    lines = full_vector.reshape(VDP, VEC // VDP, 2, LANES).transpose(0, 2, 1, 3)
    lines = lines.reshape(VDP, 1, 2 * VEC // VDP, LANES)
    lines = jnp.pad(lines, ((0, 0), (0, VCHIP - 1), (0, VROWS - 2 * VEC // VDP), (0, 0)))
    weights = (
        jnp.concatenate([cut[0], lines], axis=2),
        jnp.concatenate([cut[1], jnp.zeros_like(lines)], axis=2),
    )
    ffn_cut = full_ffn.reshape(2, VDP, tall, VCHIP, 2, FF // (2 * VCHIP))
    ffn_cut = ffn_cut.transpose(4, 3, 1, 0, 2, 5)
    (
        pulled,
        grads_own,
        grads_other,
        _,
        sums,
        vector_g,
        ffn_got,
    ) = layer(
        place,
        lambda marks: weights,
        segment_ids,
        tokens,
        cotangent,
        lambda marks, vector: (ffn_cut[0], ffn_cut[1]),
        lambda block: block,
        lambda mine, other, grad_t: (jnp.stack([mine, other]), grad_t),
    )
    block_out, input_grad, _ = pulled
    attn_full = jnp.stack([grads_own, grads_other]).transpose(1, 3, 2, 0, 4).reshape(D, 4 * D)
    ffn_full = ffn_got.transpose(3, 1, 4, 2, 0, 5).reshape(2, D, FF)
    sums = jnp.concatenate([sums[0, :2], sums[1, :2]], axis=1)
    vector_full = jnp.concatenate([vector_g[:8], sums, vector_g[10:]], axis=0)
    attn_grad = scatter_sum(attn_full)
    in_grad = scatter_sum(ffn_full[0])
    out_grad = scatter_sum(ffn_full[1])
    vector_grad = scatter_sum(vector_full)

    decay = 1.0 - STEP ** (-0.8)
    gradients = (attn_grad, in_grad, out_grad)
    weights_old = (attn_weight, ffn_in, ffn_out)
    rows_old = (attn_rows, in_rows, out_rows)
    cols_old = (attn_cols, in_cols, out_cols)
    moment_new = decay * vector_moment + (1.0 - decay) * (vector_grad * vector_grad + EPS_ONE)
    vector_step = vector_grad * lax.rsqrt(moment_new)
    squares = [gradient * gradient + EPS_ONE for gradient in gradients]
    pieces = []
    for square in squares:
        pieces.append(jnp.sum(square, axis=1))
    for square in squares:
        pieces.append(jnp.sum(square, axis=0))
    pieces.append(jnp.sum(vector_step * vector_step, axis=1))
    pieces.append(jnp.sum(vectors * vectors, axis=1))
    pieces.append(jnp.stack([jnp.sum(weight * weight) for weight in weights_old]))
    pieces.append(jnp.stack([jnp.sum(old) for old in rows_old]))
    sizes = [piece.shape[0] for piece in pieces]
    flat = jnp.concatenate(pieces)
    flat = jnp.pad(flat, (0, -flat.shape[0] % 1024)).reshape(-1, LANES)
    got = gather_all(flat).reshape(dp_count, fsdp_count, -1)
    offsets = [0]
    for length in sizes:
        offsets.append(offsets[-1] + length)
    take = lambda i: got[:, :, offsets[i] : offsets[i + 1]]
    rows_new, cols_new, row_means, entries = [], [], [], []
    for i in range(3):
        count_rows = rows_w * dp_count
        count_cols = weights_old[i].shape[1] * fsdp_count
        entries.append(float(count_rows * count_cols))
        row_all = jnp.sum(take(i), axis=1)
        mine = lax.dynamic_index_in_dim(row_all, dp_place, 0, keepdims=False)
        rows_new.append(decay * rows_old[i] + (1.0 - decay) * mine / count_cols)
        col_all = jnp.sum(take(3 + i), axis=0)
        mine = lax.dynamic_index_in_dim(col_all, fsdp_place, 0, keepdims=False)
        cols_new.append(decay * cols_old[i] + (1.0 - decay) * mine / count_rows)
        old_total = jnp.sum(take(9)[:, 0, i])
        row_means.append(
            (decay * old_total + (1.0 - decay) * jnp.sum(row_all) / count_cols) / count_rows
        )
    step_rows = jnp.sum(take(6), axis=1).reshape(-1)
    weight_rows = jnp.sum(take(7), axis=1).reshape(-1)
    weight_totals = jnp.sum(take(8), axis=(0, 1))
    updates = []
    for i in range(3):
        second = rows_new[i][:, None] * cols_new[i][None, :] / row_means[i]
        updates.append(gradients[i] * lax.rsqrt(second))
    flat = jnp.stack([jnp.sum(update * update) for update in updates])
    flat = jnp.broadcast_to(jnp.pad(flat, (0, 5))[:, None], (8, LANES))
    totals = jnp.sum(gather_all(flat)[:, :, :, 0], axis=(0, 1))
    new_weights = []
    for i in range(3):
        clip_factor = jnp.maximum(1.0, jnp.sqrt(totals[i] / entries[i]) / CLIP_LIMIT)
        step_size = STEP_RATE * jnp.maximum(EPS_TWO, jnp.sqrt(weight_totals[i] / entries[i]))
        new_weights.append(weights_old[i] - step_size / clip_factor * updates[i])
    bias_rows = FF // D
    row_places = jnp.arange(VEC)
    counts = jnp.where(row_places < bias_rows, float(FF), float(D))
    grouped_updates = jnp.where(row_places < bias_rows, jnp.sum(step_rows[:bias_rows]), step_rows)
    grouped_weights = jnp.where(row_places < bias_rows, jnp.sum(weight_rows[:bias_rows]), weight_rows)
    clip_rows = jnp.maximum(1.0, jnp.sqrt(grouped_updates / counts) / CLIP_LIMIT)
    step_sizes = STEP_RATE * jnp.maximum(EPS_TWO, jnp.sqrt(grouped_weights / counts))
    factor_rows = lax.dynamic_slice_in_dim(step_sizes / clip_rows, dp_place * rows_v, rows_v)
    vectors_new = vectors - factor_rows[:, None] * vector_step
    return (
        block_out,
        input_grad,
        attn_grad,
        in_grad,
        out_grad,
        vector_grad,
        rows_new[0],
        cols_new[0],
        rows_new[1],
        cols_new[1],
        rows_new[2],
        cols_new[2],
        moment_new,
        new_weights[0],
        new_weights[1],
        new_weights[2],
        vectors_new,
    )


def solution(mesh):
    dp_count, fsdp_count = mesh.shape["dp"], mesh.shape["fsdp"]
    inner = jax.sharding.Mesh(mesh.devices.reshape(dp_count, fsdp_count // 2, 2), ALL)
    fsdp = ("chip", "core")
    split = P(ALL, None)
    block = P("dp", fsdp)
    stats = (P("dp"), P(fsdp)) * 3
    plain = dp_count == VDP and fsdp_count == 2 * VCHIP
    return jax.shard_map(
        body if plain else body_any,
        mesh=inner,
        in_specs=(split,) * 3 + (block,) * 4 + stats + (block,),
        out_specs=(split,) * 2 + (block,) * 4 + stats + (block,) * 5,
        check_vma=False,
    )
```
